32 devices in a mesh: section: 2 (over core), dp: 16 (over z, y, x).
Axes of the slice: x: 2, y: 2, z: 4, core: 2. Of those that a mesh axis runs over, the one named last changes fastest.
Arguments:
- padded_segments: float32 [49152, 126], P('dp'), may hold values from -6 to 6
- history_extents: int32 [49152], P('dp'), may hold values from 36 to 126
- loss_prediction_adjoint: float32 [49152, 18], P('dp'), may hold values from -6 to 6
- first_layer: float32 [2, 126, 512], P('section', None, 'dp'), may hold values from -1 to 1
- square_layers: float32 [2, 5, 512, 512], P('section', None, 'dp'), may hold values from -0.25 to 0.25
- head_layer: float32 [2, 512, 144], P('section', 'dp'), may hold values from -0.25 to 0.25
- biases: float32 [2, 4, 512], P('section', None, 'dp'), may hold values from -0.875 to 0.875
- first_momentum: float32 [2, 126, 512], P('section', None, 'dp'), may hold values from -0.00036621094 to 0.00036621094
- square_momentum: float32 [2, 5, 512, 512], P('section', None, 'dp'), may hold values from -0.00036621094 to 0.00036621094
- head_momentum: float32 [2, 512, 144], P('section', 'dp'), may hold values from -0.00036621094 to 0.00036621094
- biases_momentum: float32 [2, 4, 512], P('section', None, 'dp'), may hold values from -0.00036621094 to 0.00036621094
- first_variance: float32 [2, 126, 512], P('section', None, 'dp'), may hold values from 3.4458802e-10 to 1.3783521e-09
- square_variance: float32 [2, 5, 512, 512], P('section', None, 'dp'), may hold values from 3.4458802e-10 to 1.3783521e-09
- head_variance: float32 [2, 512, 144], P('section', 'dp'), may hold values from 3.4458802e-10 to 1.3783521e-09
- biases_variance: float32 [2, 4, 512], P('section', None, 'dp'), may hold values from 3.4458802e-10 to 1.3783521e-09
Outputs:
- prediction_series: float32 [2, 49152, 18], P('section', 'dp')
- unit_entry_sensitivity: float32 [2, 49152, 126], P('section', 'dp')
- overall_slope_magnitude: float32 [], replicated
- first_grad: float32 [2, 126, 512], P('section', None, 'dp')
- square_grad: float32 [2, 5, 512, 512], P('section', None, 'dp')
- head_grad: float32 [2, 512, 144], P('section', 'dp')
- biases_grad: float32 [2, 4, 512], P('section', None, 'dp')
- first_layer_new: float32 [2, 126, 512], P('section', None, 'dp')
- square_layers_new: float32 [2, 5, 512, 512], P('section', None, 'dp')
- head_layer_new: float32 [2, 512, 144], P('section', 'dp')
- biases_new: float32 [2, 4, 512], P('section', None, 'dp')
- first_momentum_new: float32 [2, 126, 512], P('section', None, 'dp')
- square_momentum_new: float32 [2, 5, 512, 512], P('section', None, 'dp')
- head_momentum_new: float32 [2, 512, 144], P('section', 'dp')
- biases_momentum_new: float32 [2, 4, 512], P('section', None, 'dp')
- first_variance_new: float32 [2, 126, 512], P('section', None, 'dp')
- square_variance_new: float32 [2, 5, 512, 512], P('section', None, 'dp')
- head_variance_new: float32 [2, 512, 144], P('section', 'dp')
- biases_variance_new: float32 [2, 4, 512], P('section', None, 'dp')
The draws below stay inside these ranges and needn't reach their ends.
Inputs may be any that keep to these rules, and one draw needn't show every extreme that they name: `history_extents`: a window's data are its last lengths positions, the earlier ones are padding.
All inputs are finite; a program needn't handle non-finite values.
Results may differ from the reference program's by a relative error of at most 0.013.
The reference program's roundings to bfloat16 on the way count: a program that leaves them out, or rounds other values in their place, can miss the bound.
Values may be sent and summed in bfloat16 or wider, within the bound.
A program may use at most 128 MiB of HBM per device.

```python
import math
import jax
import jax.numpy as jnp
from jax import lax

PAST_STEPS = 126
FUTURE_STEPS = 18
H = 512
SLICES_EACH_RANK = 3072
STEP = 10
SLICE_COUNT = 49152
PARAMS = 2902016
N_DP = 16


def draw_first_layer(key, part):
    key = jax.random.fold_in(key, 7)
    column = jnp.arange(H, dtype=jnp.float32) / (H - 1)
    base = jax.random.normal(key, (2, PAST_STEPS, H), jnp.float32)
    rising = jnp.exp(column * math.log(3.0))
    return jnp.clip(base * rising / math.sqrt(PAST_STEPS), -1.0, 1.0)


def place_ends(array, own_key, smallest, high):
    longest = array.shape.index(max(array.shape))
    spots = []
    for shift in (0, 1):
        where = [jax.random.randint(jax.random.fold_in(own_key, axis), (), 0, length) for axis, length in enumerate(array.shape)]
        where[longest] = (where[longest] + shift) % array.shape[longest]
        spots.append(tuple(where))
    return array.at[spots[0]].set(smallest).at[spots[1]].set(high)


def block_scale(key, dims, cuts, low, top_value):
    def one(position, parts):
        steps = jax.random.uniform(jax.random.fold_in(jax.random.fold_in(key, 6), position), (parts,), jnp.float32, low / len(cuts), top_value / len(cuts))
        return jnp.repeat(jnp.exp(steps), dims[position] // parts).reshape((-1,) + (1,) * (len(dims) - position - 1))

    factor_of = one(*cuts[0])
    for cut in cuts[1:]:
        factor_of = factor_of * one(*cut)
    return factor_of


def normal_values(stream_key, dims, scale, most, split=(), kind=jnp.bfloat16):
    array = jax.random.normal(stream_key, dims, jnp.float32) * scale
    if len(split) > 0:
        array = block_scale(stream_key, dims, split, -0.22, 0.18) * array
    return jnp.clip(array, min=-most, max=most).astype(kind)


def setup_inputs(seed: int = 0) -> dict:
    splits = jax.random.split(jax.random.key(seed), 16)
    padded_segments = normal_values(splits[0], (SLICE_COUNT, PAST_STEPS), 1.0, 6.0, ((0, 16),), jnp.float32)
    history_extents = place_ends(jax.random.randint(splits[1], (SLICE_COUNT,), (2 * PAST_STEPS) // 7, PAST_STEPS + 1), jax.random.fold_in(splits[1], 1), (2 * PAST_STEPS) // 7, PAST_STEPS).astype(jnp.int32)
    loss_prediction_adjoint = normal_values(splits[2], (SLICE_COUNT, FUTURE_STEPS), 1.0, 6.0, ((0, 16),), jnp.float32)
    first_layer = draw_first_layer(jax.random.fold_in(splits[15], 71), 0)
    square_layers = normal_values(splits[4], (2, 5, H, H), H ** -0.5, 0.25, ((0, 2), (2, 16)), jnp.float32)
    head_layer = normal_values(splits[5], (2, H, PAST_STEPS + FUTURE_STEPS), H ** -0.5, 0.25, ((0, 2), (1, 16)), jnp.float32)
    biases = normal_values(splits[6], (2, 4, H), 0.15, 0.875, ((0, 2), (2, 16)), jnp.float32)
    first_momentum = normal_values(splits[7], (2, PAST_STEPS, H), (0.11 / PARAMS ** 0.5), 0.00036621094, ((0, 2), (2, 16)), jnp.float32)
    square_momentum = normal_values(splits[8], (2, 5, H, H), (0.11 / PARAMS ** 0.5), 0.00036621094, ((0, 2), (2, 16)), jnp.float32)
    head_momentum = normal_values(splits[9], (2, H, PAST_STEPS + FUTURE_STEPS), (0.11 / PARAMS ** 0.5), 0.00036621094, ((0, 2), (1, 16)), jnp.float32)
    biases_momentum = normal_values(splits[10], (2, 4, H), (0.11 / PARAMS ** 0.5), 0.00036621094, ((0, 2), (2, 16)), jnp.float32)
    first_variance = jnp.clip(jnp.exp(math.log(1.3783520991239584e-09) - 1.3862944 * jax.random.uniform(splits[11], (2, PAST_STEPS, H), jnp.float32) ** block_scale(splits[11], (2, PAST_STEPS, H), ((0, 2), (2, 16)), -0.2, 0.2)), 3.445880247809896e-10, 1.3783520991239584e-09)
    square_variance = jnp.clip(jnp.exp(math.log(1.3783520991239584e-09) - 1.3862944 * jax.random.uniform(splits[12], (2, 5, H, H), jnp.float32) ** block_scale(splits[12], (2, 5, H, H), ((0, 2), (2, 16)), -0.2, 0.2)), 3.445880247809896e-10, 1.3783520991239584e-09)
    head_variance = jnp.clip(jnp.exp(math.log(1.3783520991239584e-09) - 1.3862944 * jax.random.uniform(splits[13], (2, H, PAST_STEPS + FUTURE_STEPS), jnp.float32) ** block_scale(splits[13], (2, H, PAST_STEPS + FUTURE_STEPS), ((0, 2), (1, 16)), -0.2, 0.2)), 3.445880247809896e-10, 1.3783520991239584e-09)
    biases_variance = jnp.clip(jnp.exp(math.log(1.3783520991239584e-09) - 1.3862944 * jax.random.uniform(splits[14], (2, 4, H), jnp.float32) ** block_scale(splits[14], (2, 4, H), ((0, 2), (2, 16)), -0.2, 0.2)), 3.445880247809896e-10, 1.3783520991239584e-09)
    return dict(padded_segments=padded_segments, history_extents=history_extents, loss_prediction_adjoint=loss_prediction_adjoint, first_layer=first_layer, square_layers=square_layers, head_layer=head_layer, biases=biases, first_momentum=first_momentum, square_momentum=square_momentum, head_momentum=head_momentum, biases_momentum=biases_momentum, first_variance=first_variance, square_variance=square_variance, head_variance=head_variance, biases_variance=biases_variance)


@jax.custom_vjp
def reduced_precision(v):
    return lax.optimization_barrier(v.astype(jnp.bfloat16)).astype(jnp.float32)

@jax.custom_vjp
def reduced_reverse(v):
    return v

def low_keep(v):
    return (reduced_precision(v), None)

def low_pass(kept, grad):
    return (grad,)

def back_keep(v):
    return (v, None)

def back_low(kept, grad):
    return (reduced_precision(grad),)
reduced_precision.defvjp(low_keep, low_pass)
reduced_reverse.defvjp(back_keep, back_low)

def product_of_arrays(former, latter):
    return jnp.dot(former, latter, precision=lax.Precision.HIGHEST)

def block(coefficient_arrays, remainder_signal, window_mask):
    first_w, inner_square_matrix, readout_matrix, bias_w = coefficient_arrays
    present_state = reduced_precision(remainder_signal)
    for number in range(4):
        matrix = first_w if number == 0 else inner_square_matrix[number - 1]
        preact = reduced_reverse(product_of_arrays(present_state, matrix) + bias_w[number])
        present_state = reduced_precision(jax.nn.silu(preact))
    backcast_theta = reduced_precision(reduced_reverse(product_of_arrays(present_state, inner_square_matrix[3])))
    prediction_coefficients = reduced_precision(reduced_reverse(product_of_arrays(present_state, inner_square_matrix[4])))
    backcast = reduced_reverse(product_of_arrays(backcast_theta, readout_matrix[:, :PAST_STEPS]))
    prediction_share = reduced_reverse(product_of_arrays(prediction_coefficients, readout_matrix[:, PAST_STEPS:]))
    return ((remainder_signal - backcast) * window_mask, prediction_share)

def network(inputs, probe, masters, window_mask):
    early = tuple((reduced_precision(master[0]) for master in masters))
    later = tuple((reduced_precision(master[1]) for master in masters))
    resid_one, fore_one = block(early, inputs * window_mask, window_mask)
    handed = reduced_precision(reduced_reverse(resid_one)) + probe
    resid_two, fore_two = block(later, handed, window_mask)
    return (reduced_precision(fore_one) + fore_two, fore_one)

def reference(padded_segments, history_extents, loss_prediction_adjoint, first_layer, square_layers, head_layer, biases, first_momentum, square_momentum, head_momentum, biases_momentum, first_variance, square_variance, head_variance, biases_variance):
    masters = (first_layer, square_layers, head_layer, biases)
    positions = jnp.arange(PAST_STEPS, dtype=jnp.int32)

    def lone_learnable_bundle(totals, fragment_list):
        inputs, group_lengths, group_cot = fragment_list
        window_mask = (positions[None, :] >= PAST_STEPS - group_lengths[:, None]).astype(jnp.float32)
        probe = jnp.zeros_like(inputs)

        def forward(inputs_in, probe_in, masters_in):
            return network(inputs_in, probe_in, masters_in, window_mask)
        final, pull, first_part = jax.vjp(forward, inputs, probe, masters, has_aux=True)
        grad_inputs, grad_probe, grad_masters = pull(group_cot)
        totals = jax.tree.map(jnp.add, totals, grad_masters)
        return (totals, (jnp.stack([first_part, final]), jnp.stack([grad_inputs, grad_probe])))
    segment_beginning = jax.tree.map(jnp.zeros_like, masters)
    learnable_sensitivities, (prediction_results, arriving_sensitivities) = lax.scan(lone_learnable_bundle, segment_beginning, (padded_segments.reshape(N_DP, SLICES_EACH_RANK, PAST_STEPS), history_extents.reshape(N_DP, SLICES_EACH_RANK), loss_prediction_adjoint.reshape(N_DP, SLICES_EACH_RANK, FUTURE_STEPS)))
    prediction_series = prediction_results.transpose(1, 0, 2, 3).reshape(2, SLICE_COUNT, FUTURE_STEPS)
    unit_entry_sensitivity = arriving_sensitivities.transpose(1, 0, 2, 3).reshape(2, SLICE_COUNT, PAST_STEPS)
    squares = jnp.float32(0.0)
    for gradient in learnable_sensitivities:
        squares = squares + jnp.sum(gradient * gradient)
    overall_slope_magnitude = jnp.sqrt(squares)
    factor = 1.0 / jnp.maximum(overall_slope_magnitude, 1.0)
    refreshed_entries, mean_estimates, variance_estimates = ([], [], [])
    for master, gradient, momentum, variance in zip(masters, learnable_sensitivities, (first_momentum, square_momentum, head_momentum, biases_momentum), (first_variance, square_variance, head_variance, biases_variance)):
        clipped = gradient * factor
        moment_new = 0.9 * momentum + 0.1 * clipped
        variance_new = 0.999 * variance + 0.001 * clipped * clipped
        ratio = moment_new / (1.0 - 0.9 ** STEP) / (jnp.sqrt(variance_new / (1.0 - 0.999 ** STEP)) + 1e-08)
        refreshed_entries.append(master - 0.05 * (ratio + 0.01 * master))
        mean_estimates.append(moment_new)
        variance_estimates.append(variance_new)
    return (prediction_series, unit_entry_sensitivity, overall_slope_magnitude, learnable_sensitivities[0], learnable_sensitivities[1], learnable_sensitivities[2], learnable_sensitivities[3], refreshed_entries[0], refreshed_entries[1], refreshed_entries[2], refreshed_entries[3], mean_estimates[0], mean_estimates[1], mean_estimates[2], mean_estimates[3], variance_estimates[0], variance_estimates[1], variance_estimates[2], variance_estimates[3])
```

```python
import jax
import jax.numpy as jnp
from jax import lax
from jax.sharding import PartitionSpec as P

STEP = 10


def dot_nn(a, b):
    return jnp.dot(a, b, preferred_element_type=jnp.float32)


def dot_tn(a, b):
    return lax.dot_general(a, b, (((0,), (0,)), ((), ())), preferred_element_type=jnp.float32)


def dot_nt(a, b):
    return lax.dot_general(a, b, (((1,), (1,)), ((), ())), preferred_element_type=jnp.float32)


def unit_rows(first, square, head, biases):
    units = first.shape[1]
    return jnp.concatenate(
        [square.transpose(1, 0, 2).reshape(units, -1), first.T, head, biases.T], axis=1
    )


def from_unit_rows(rows, past, hidden, out):
    wide = 5 * hidden
    square = rows[:, :wide].reshape(-1, 5, hidden).transpose(1, 0, 2)
    first = rows[:, wide : wide + past].T
    head = rows[:, wide + past : wide + past + out]
    biases = rows[:, wide + past + out :].T
    return first, square, head, biases


def plain_forward(weights, resid):
    first, square, head, biases = weights
    past = resid.shape[1]
    acts, slopes = [resid.astype(jnp.bfloat16)], []
    for k in range(4):
        z = dot_nn(acts[-1], first if k == 0 else square[k - 1]) + biases[k].astype(jnp.float32)
        sig = jax.nn.sigmoid(z)
        acts.append((z * sig).astype(jnp.bfloat16))
        slopes.append(sig * (1.0 + z * (1.0 - sig)))
    theta_b = dot_nn(acts[4], square[3]).astype(jnp.bfloat16)
    theta_f = dot_nn(acts[4], square[4]).astype(jnp.bfloat16)
    backcast = dot_nn(theta_b, head[:, :past])
    part = dot_nn(theta_f, head[:, past:])
    return backcast, part, (acts, slopes, theta_b, theta_f)


def plain_backward(weights, saved, e, f):
    first, square, head, biases = weights
    acts, slopes, theta_b, theta_f = saved
    past = e.shape[1]
    head_grad = jnp.concatenate([dot_tn(theta_b, e), dot_tn(theta_f, f)], axis=1)
    u_b = dot_nt(e, head[:, :past]).astype(jnp.bfloat16)
    u_f = dot_nt(f, head[:, past:]).astype(jnp.bfloat16)
    squares = [None, None, None, dot_tn(acts[4], u_b), dot_tn(acts[4], u_f)]
    da = dot_nt(u_b, square[3]) + dot_nt(u_f, square[4])
    bias_grads = [None] * 4
    first_grad = None
    for k in (3, 2, 1, 0):
        dz = (da * slopes[k]).astype(jnp.bfloat16)
        bias_grads[k] = jnp.sum(dz, axis=0, dtype=jnp.float32)
        grad = dot_tn(acts[k], dz)
        if k == 0:
            first_grad = grad
        else:
            squares[k - 1] = grad
        da = dot_nt(dz, first if k == 0 else square[k - 1])
    return da, (first_grad, jnp.stack(squares), head_grad, jnp.stack(bias_grads))


def adamw(master, gradient, momentum, variance, factor):
    clipped = gradient * factor
    moment_new = 0.9 * momentum + 0.1 * clipped
    variance_new = 0.999 * variance + 0.001 * clipped * clipped
    ratio = moment_new / (1.0 - 0.9**STEP) / (jnp.sqrt(variance_new / (1.0 - 0.999**STEP)) + 1e-08)
    return master - 0.05 * (ratio + 0.01 * master), moment_new, variance_new


def plain_shards(segments, extents, adjoint, *state):
    masters, momenta, variances = state[:4], state[4:8], state[8:]
    core = lax.axis_index("section")
    past, span = segments.shape[1], adjoint.shape[1]
    windows = segments.shape[0] // 2
    hidden = masters[1].shape[3]
    mine = [
        lax.dynamic_slice_in_dim(v, core * windows, windows, 0) for v in (segments, extents, adjoint)
    ]
    seg, ext, adj = mine
    rows = unit_rows(*(m[0].astype(jnp.bfloat16) for m in masters))
    rows = lax.all_gather(rows, "dp", axis=0, tiled=True)
    rows = lax.all_gather(rows, "section", axis=0)
    blocks = [from_unit_rows(rows[b], past, hidden, past + span) for b in range(2)]
    mask = (
        lax.broadcasted_iota(jnp.int32, (windows, past), 1) >= past - ext[:, None]
    ).astype(jnp.float32)
    r0 = seg * mask
    backcast, part0, saved0 = plain_forward(blocks[0], r0)
    r1 = (r0 - backcast) * mask
    _, part1, saved1 = plain_forward(blocks[1], r1)
    forecast = part0.astype(jnp.bfloat16).astype(jnp.float32) + part1
    f = adj.astype(jnp.bfloat16)
    zero = jnp.zeros_like(r0)
    da1, grads1 = plain_backward(blocks[1], saved1, (-(zero * mask)).astype(jnp.bfloat16), f)
    dr1 = zero * mask + da1
    t = dr1.astype(jnp.bfloat16).astype(jnp.float32)
    da0, grads0 = plain_backward(blocks[0], saved0, (-(t * mask)).astype(jnp.bfloat16), f)
    dr0 = (t * mask + da0) * mask

    def by_section(first_block, second_block):
        mine, other = (
            jnp.where(core == 0, first_block, second_block),
            jnp.where(core == 0, second_block, first_block),
        )
        got = lax.ppermute(other, "section", [(0, 1), (1, 0)])
        return jnp.where(
            core == 0, jnp.concatenate([mine, got]), jnp.concatenate([got, mine])
        )[None]

    prediction = by_section(part0, forecast)
    sensitivity = by_section(dr0, dr1)
    packed = jnp.stack([unit_rows(*grads0), unit_rows(*grads1)])
    packed = lax.psum_scatter(packed, "section", scatter_dimension=0, tiled=False)
    packed = lax.psum_scatter(packed, "dp", scatter_dimension=0, tiled=True)
    norm = jnp.sqrt(lax.psum(jnp.sum(packed * packed), ("section", "dp")))
    factor = 1.0 / jnp.maximum(norm, 1.0)
    summed = [g[None] for g in from_unit_rows(packed, past, hidden, past + span)]
    updated = [adamw(*four, factor) for four in zip(masters, summed, momenta, variances)]
    return (
        prediction,
        sensitivity,
        norm,
        *summed,
        *(u[0] for u in updated),
        *(u[1] for u in updated),
        *(u[2] for u in updated),
    )


STATE_SPECS = (
    P("section", None, "dp"),
    P("section", None, "dp", None),
    P("section", "dp", None),
    P("section", None, "dp"),
)


def solution(mesh):
    in_specs = (P("dp", None), P("dp"), P("dp", None)) + 3 * STATE_SPECS
    out_specs = (P("section", "dp", None), P("section", "dp", None), P()) + 4 * STATE_SPECS
    return jax.shard_map(
        plain_shards, mesh=mesh, in_specs=in_specs, out_specs=out_specs, check_vma=False
    )
```

```python
import functools

import jax
import jax.numpy as jnp
from jax import lax
from jax.experimental import pallas as pl
from jax.experimental.pallas import tpu as pltpu
from jax.sharding import PartitionSpec as P

STEP = 10


def dot_nn(a, b):
    return jnp.dot(a, b, preferred_element_type=jnp.float32)


def dot_tn(a, b):
    return lax.dot_general(a, b, (((0,), (0,)), ((), ())), preferred_element_type=jnp.float32)


def dot_nt(a, b):
    return lax.dot_general(a, b, (((1,), (1,)), ((), ())), preferred_element_type=jnp.float32)


def unit_rows(first, square, head, biases):
    units = first.shape[1]
    return jnp.concatenate(
        [square.transpose(1, 0, 2).reshape(units, -1), first.T, head, biases.T], axis=1
    )


def from_unit_rows(rows, past, hidden, out):
    wide = 5 * hidden
    square = rows[:, :wide].reshape(-1, 5, hidden).transpose(1, 0, 2)
    first = rows[:, wide : wide + past].T
    head = rows[:, wide + past : wide + past + out]
    biases = rows[:, wide + past + out :].T
    return first, square, head, biases


def plain_forward(weights, resid):
    first, square, head, biases = weights
    past = resid.shape[1]
    acts, slopes = [resid.astype(jnp.bfloat16)], []
    for k in range(4):
        z = dot_nn(acts[-1], first if k == 0 else square[k - 1]) + biases[k].astype(jnp.float32)
        sig = jax.nn.sigmoid(z)
        acts.append((z * sig).astype(jnp.bfloat16))
        slopes.append(sig * (1.0 + z * (1.0 - sig)))
    theta_b = dot_nn(acts[4], square[3]).astype(jnp.bfloat16)
    theta_f = dot_nn(acts[4], square[4]).astype(jnp.bfloat16)
    backcast = dot_nn(theta_b, head[:, :past])
    part = dot_nn(theta_f, head[:, past:])
    return backcast, part, (acts, slopes, theta_b, theta_f)


def plain_backward(weights, saved, e, f):
    first, square, head, biases = weights
    acts, slopes, theta_b, theta_f = saved
    past = e.shape[1]
    head_grad = jnp.concatenate([dot_tn(theta_b, e), dot_tn(theta_f, f)], axis=1)
    u_b = dot_nt(e, head[:, :past]).astype(jnp.bfloat16)
    u_f = dot_nt(f, head[:, past:]).astype(jnp.bfloat16)
    squares = [None, None, None, dot_tn(acts[4], u_b), dot_tn(acts[4], u_f)]
    da = dot_nt(u_b, square[3]) + dot_nt(u_f, square[4])
    bias_grads = [None] * 4
    first_grad = None
    for k in (3, 2, 1, 0):
        dz = (da * slopes[k]).astype(jnp.bfloat16)
        bias_grads[k] = jnp.sum(dz, axis=0, dtype=jnp.float32)
        grad = dot_tn(acts[k], dz)
        if k == 0:
            first_grad = grad
        else:
            squares[k - 1] = grad
        da = dot_nt(dz, first if k == 0 else square[k - 1])
    return da, (first_grad, jnp.stack(squares), head_grad, jnp.stack(bias_grads))


def adamw(master, gradient, momentum, variance, factor):
    clipped = gradient * factor
    moment_new = 0.9 * momentum + 0.1 * clipped
    variance_new = 0.999 * variance + 0.001 * clipped * clipped
    ratio = moment_new / (1.0 - 0.9**STEP) / (jnp.sqrt(variance_new / (1.0 - 0.999**STEP)) + 1e-08)
    return master - 0.05 * (ratio + 0.01 * master), moment_new, variance_new


def plain_shards(segments, extents, adjoint, *state):
    masters, momenta, variances = state[:4], state[4:8], state[8:]
    core = lax.axis_index("section")
    past, span = segments.shape[1], adjoint.shape[1]
    windows = segments.shape[0] // 2
    hidden = masters[1].shape[3]
    mine = [
        lax.dynamic_slice_in_dim(v, core * windows, windows, 0) for v in (segments, extents, adjoint)
    ]
    seg, ext, adj = mine
    rows = unit_rows(*(m[0].astype(jnp.bfloat16) for m in masters))
    rows = lax.all_gather(rows, "dp", axis=0, tiled=True)
    rows = lax.all_gather(rows, "section", axis=0)
    blocks = [from_unit_rows(rows[b], past, hidden, past + span) for b in range(2)]
    mask = (
        lax.broadcasted_iota(jnp.int32, (windows, past), 1) >= past - ext[:, None]
    ).astype(jnp.float32)
    r0 = seg * mask
    backcast, part0, saved0 = plain_forward(blocks[0], r0)
    r1 = (r0 - backcast) * mask
    _, part1, saved1 = plain_forward(blocks[1], r1)
    forecast = part0.astype(jnp.bfloat16).astype(jnp.float32) + part1
    f = adj.astype(jnp.bfloat16)
    zero = jnp.zeros_like(r0)
    da1, grads1 = plain_backward(blocks[1], saved1, (-(zero * mask)).astype(jnp.bfloat16), f)
    dr1 = zero * mask + da1
    t = dr1.astype(jnp.bfloat16).astype(jnp.float32)
    da0, grads0 = plain_backward(blocks[0], saved0, (-(t * mask)).astype(jnp.bfloat16), f)
    dr0 = (t * mask + da0) * mask

    def by_section(first_block, second_block):
        mine, other = (
            jnp.where(core == 0, first_block, second_block),
            jnp.where(core == 0, second_block, first_block),
        )
        got = lax.ppermute(other, "section", [(0, 1), (1, 0)])
        return jnp.where(
            core == 0, jnp.concatenate([mine, got]), jnp.concatenate([got, mine])
        )[None]

    prediction = by_section(part0, forecast)
    sensitivity = by_section(dr0, dr1)
    packed = jnp.stack([unit_rows(*grads0), unit_rows(*grads1)])
    packed = lax.psum_scatter(packed, "section", scatter_dimension=0, tiled=False)
    packed = lax.psum_scatter(packed, "dp", scatter_dimension=0, tiled=True)
    norm = jnp.sqrt(lax.psum(jnp.sum(packed * packed), ("section", "dp")))
    factor = 1.0 / jnp.maximum(norm, 1.0)
    summed = [g[None] for g in from_unit_rows(packed, past, hidden, past + span)]
    updated = [adamw(*four, factor) for four in zip(masters, summed, momenta, variances)]
    return (
        prediction,
        sensitivity,
        norm,
        *summed,
        *(u[0] for u in updated),
        *(u[1] for u in updated),
        *(u[2] for u in updated),
    )


PLANES = {16: (4, 2, 2)}
MESH = pl.DeviceIdType.MESH
MATS = 6
BF, F32 = jnp.bfloat16, jnp.float32


def remote(src, dst, send_sem, recv_sem, device):
    return pltpu.make_async_remote_copy(
        src_ref=src, dst_ref=dst, send_sem=send_sem, recv_sem=recv_sem, device_id=device, device_id_type=MESH
    )


def train_kernel(
    sizes,
    seg_hbm, adj_hbm, ext, first, square, head, biases,
    pred_out, sens_out, grad_out, norm_out,
    wg, handed, gp, from_core, from_diag, from_plain, from_pair, from_z, total,
    act_t, in_t, theta_t, slope, work, resid, mask, f_ref, e_ref, t_ref, bias_t, bias_sum, pad,
    seg, adj, pred, sens, squares, norm_buf,
    own_send, own_recv, ag_send, ag_recv, rs_send, rs_recv, out_send, out_recv, local_sem, norm_send, norm_recv,
):
    ZN, YN, XN, windows, tile, past, span, hidden = sizes
    units = ZN * YN * XN
    core, dp = lax.axis_index("section"), lax.axis_index("dp")
    x, y, z = lax.rem(dp, XN), lax.rem(lax.div(dp, XN), YN), lax.div(dp, XN * YN)
    other, xo, yo = 1 - core, 1 - x, 1 - y
    near_y, near_x = y + core * (yo - y), xo + core * (x - xo)
    far_y, far_x = yo + core * (y - yo), x + core * (xo - x)

    def chip(zi, yi, xi):
        return (core, (zi * YN + yi) * XN + xi)

    sibling = (other, dp)
    z_peers = [lax.rem(z + step, ZN) for step in range(1, ZN)]

    row0 = core * windows
    loads = [
        pltpu.make_async_copy(seg_hbm.at[pl.ds(row0, windows), :], seg, local_sem.at[0]),
        pltpu.make_async_copy(adj_hbm.at[pl.ds(row0, windows), :], adj, local_sem.at[1]),
    ]
    for load in loads:
        load.start()

    barrier = pltpu.get_barrier_semaphore()
    peers = [sibling, chip(z, y, xo), chip(z, yo, x)] + [chip(zi, y, x) for zi in z_peers]
    for peer in peers:
        pl.semaphore_signal(barrier, inc=1, device_id=peer, device_id_type=MESH)

    rows = hidden // units
    half_rows = rows // 2

    def put_own(m, value, lanes):
        halves = value.astype(BF).reshape(2, half_rows, -1)
        for h in range(2):
            pl.when(core == h)(functools.partial(put_half, m, halves[h], halves[1 - h], lanes))

    def put_half(m, kept, given, lanes):
        wg[core, m, z, y, x, core, :, lanes] = kept
        handed[m, :, lanes] = given

    pad[...] = jnp.zeros_like(pad)
    pad[0:past, 0:rows] = first[0] * 0.5
    put_own(0, pad[...].T[0:rows], slice(0, 128))
    pad[...] = jnp.zeros_like(pad)
    pad[span : span + 4, 0:rows] = biases[0] * 0.5
    bias_cols = pad[...].T[0:rows]
    pad[...] = jnp.zeros_like(pad)
    pad[0:rows, 0:span] = head[0, :, past : past + span]
    put_own(0, pad[0:rows, :] + bias_cols, slice(128, 256))
    pad[...] = jnp.zeros_like(pad)
    pad[0:rows, 0:past] = head[0, :, 0:past]
    put_own(0, pad[0:rows, :], slice(256, 384))
    put_own(0, jnp.zeros((rows, 128), F32), slice(384, 512))
    for m in range(5):
        put_own(m + 1, square[0, m] * 0.5 if m < 3 else square[0, m], slice(0, hidden))
    pl.semaphore_wait(barrier, len(peers))

    own = remote(handed, wg.at[core, :, z, y, x, other], own_send.at[0], own_recv.at[0], sibling)
    own.start()

    def of(i):
        return lax.div(i, MATS), lax.rem(i, MATS)

    def z_copies(i):
        b, m = of(i)
        part = wg.at[b, m, z, y, x, core]
        return [
            remote(part, part, ag_send.at[i, s], ag_recv.at[i, s], chip(zi, y, x)) for s, zi in enumerate(z_peers)
        ]

    def column_copies(i):
        b, m = of(i)
        part = wg.at[b, m, :, y, x, core]
        return [
            remote(part, part, ag_send.at[i, 3], ag_recv.at[i, 3], chip(z, near_y, near_x)),
            remote(part, part, ag_send.at[i, 4], ag_recv.at[i, 4], chip(z, far_y, far_x)),
        ]

    def corner_copy(i):
        b, m = of(i)
        part = wg.at[b, m, :, near_y, near_x, core]
        return remote(part, part, ag_send.at[i, 5], ag_recv.at[i, 5], chip(z, far_y, far_x))

    def core_copy(i):
        b, m = of(i)
        part = wg.at[b, m, :, :, :, core]
        return remote(part, part, ag_send.at[i, 6], ag_recv.at[i, 6], sibling)

    def start_all(copies):
        for copy in copies:
            copy.start()

    for load in loads:
        load.wait()
    zeros_tile = jnp.zeros((tile, 128), F32)

    def prepare(t, carry):
        at = pl.ds(t * tile, tile)
        resid[at, :] = zeros_tile
        resid[at, 0:span] = adj[at, :]
        f_ref[at, :] = resid[at, :].astype(BF)
        resid[at, :] = zeros_tile
        resid[at, 0:past] = seg[at, :]
        return carry

    def prepare_mask(g, carry):
        lengths = ext[pl.ds(core * (windows // 128) + g, 1), :]
        position = lax.broadcasted_iota(jnp.int32, (128, 128), 0)
        keep = jnp.where(position >= past - lengths, 1.0, 0.0).astype(F32).T
        at = pl.ds(pl.multiple_of(g * 128, 128), 128)
        mask[at, :] = keep
        resid[at, :] = resid[at, :] * keep
        return carry

    tiles = windows // tile

    def matrix(b, m):
        return wg[b, m].reshape(hidden, hidden)

    def small(b, lane):
        return wg[b, 0, :, :, :, :, :, lane : lane + 128].reshape(hidden, 128)

    def store_layer(b, k, at, v, scale):
        p = 1.0 + jnp.tanh(v)
        a = v * p
        rate = p + a * (2.0 - p)
        slope[b, k, at, :] = (rate if scale is None else rate * scale).astype(BF)
        low = a.astype(BF)
        act_t[b, k, :, at] = low.T
        return low

    def layer_zero(b):
        bias_t[...] = small(b, 128).astype(F32).T

        def body(t, carry):
            at = pl.ds(pl.multiple_of(t * tile, tile), tile)
            a = resid[at, :].astype(BF)
            in_t[b, :, at] = a.T
            v = dot_nt(a, small(b, 0)) + bias_t[span : span + 1, :]
            work[0, at, :] = store_layer(b, 0, at, v, None)
            return carry

        lax.fori_loop(0, tiles, body, 0)

    def layer_next(b, k):
        source, target = lax.rem(k + 1, 2), lax.rem(k, 2)
        bias = bias_t[pl.ds(span + k, 1), :]
        scale = jnp.where(k == 3, 0.5, 1.0)

        def body(t, carry):
            at = pl.ds(pl.multiple_of(t * tile, tile), tile)
            v = dot_nn(work[source, at, :], matrix(b, k)) + bias
            work[target, at, :] = store_layer(b, k, at, v, scale)
            return carry

        lax.fori_loop(0, tiles, body, 0)

    def backcast_step(b):
        def body(t, carry):
            at = pl.ds(pl.multiple_of(t * tile, tile), tile)
            theta = dot_nn(work[1, at, :], matrix(b, 4)).astype(BF)
            theta_t[b, 0, :, at] = theta.T

            @pl.when(b == 0)
            def _():
                backcast = dot_nn(theta, small(b, 256))
                resid[at, :] = (resid[at, :] - backcast) * mask[at, :]

            return carry

        lax.fori_loop(0, tiles, body, 0)

    def forecast_step(b):
        def body(t, carry):
            at = pl.ds(pl.multiple_of(t * tile, tile), tile)
            theta = dot_nn(work[1, at, :], matrix(b, 5)).astype(BF)
            theta_t[b, 1, :, at] = theta.T
            part = dot_nn(theta, small(b, 128))[:, 0:span]

            @pl.when(b == 0)
            def _():
                pred[0, at, :] = part

            @pl.when(b == 1)
            def _():
                pred[1, at, :] = pred[0, at, :].astype(BF).astype(F32) + part

            return carry

        lax.fori_loop(0, tiles, body, 0)

    own.wait_recv()
    for i in range(3):
        start_all(z_copies(i))
    lax.fori_loop(0, tiles, prepare, 0)
    lax.fori_loop(0, windows // 128, prepare_mask, 0)

    count = 2 * MATS

    def gather_step(i, carry):
        @pl.when(i + 3 < count)
        def _():
            start_all(z_copies(i + 3))

        @pl.when(i < count)
        def _():
            for copy in z_copies(i):
                copy.wait_recv()
            start_all(column_copies(i))

        @pl.when(jnp.logical_and(i >= 1, i < count + 1))
        def _():
            column_copies(i - 1)[0].wait_recv()
            corner_copy(i - 1).start()

        @pl.when(jnp.logical_and(i >= 2, i < count + 2))
        def _():
            column_copies(i - 2)[1].wait_recv()
            corner_copy(i - 2).wait_recv()
            core_copy(i - 2).start()

        @pl.when(i >= 3)
        def _():
            core_copy(i - 3).wait_recv()
            b, m = of(i - 3)
            pl.when(m == 0)(lambda: layer_zero(b))
            pl.when(jnp.logical_and(m >= 1, m <= 3))(lambda: layer_next(b, m))
            pl.when(m == 4)(lambda: backcast_step(b))
            pl.when(m == 5)(lambda: forecast_step(b))

        return carry

    lax.fori_loop(0, count + 3, gather_step, 0)

    def out_copies(buf, out, s):
        at = pl.ds(row0, windows)
        return [
            pltpu.make_async_copy(buf.at[core], out.at[0, at, :], local_sem.at[2 + s]),
            remote(buf.at[other], out.at[0, at, :], out_send.at[s], out_recv.at[s], sibling),
        ]

    start_all(out_copies(pred, pred_out, 0))

    def back_of(j):
        s = lax.rem(j, MATS)
        return 1 - lax.div(j, MATS), jnp.where(s == 0, 4, jnp.where(s == 1, 5, 5 - s))

    def to_core(j):
        b, m = back_of(j)
        return remote(
            gp.at[b, m, :, :, :, other], from_core.at[b, m], rs_send.at[j, 0], rs_recv.at[j, 0], sibling
        )

    def to_far(j):
        b, m = back_of(j)
        device = chip(z, far_y, far_x)
        return [
            remote(gp.at[b, m, :, yo, xo, core], from_diag.at[b, m], rs_send.at[j, 1], rs_recv.at[j, 1], device),
            remote(gp.at[b, m, :, far_y, far_x, core], from_plain.at[b, m], rs_send.at[j, 2], rs_recv.at[j, 2], device),
        ]

    def to_near(j):
        b, m = back_of(j)
        return remote(
            gp.at[b, m, :, near_y, near_x, core], from_pair.at[b, m], rs_send.at[j, 3], rs_recv.at[j, 3],
            chip(z, near_y, near_x),
        )

    def to_z(j):
        b, m = back_of(j)
        return [
            remote(gp.at[b, m, zi, y, x, core], from_z.at[b, m, s], rs_send.at[j, 4 + s], rs_recv.at[j, 4 + s], chip(zi, y, x))
            for s, zi in enumerate(z_peers)
        ]

    def scatter_core(j):
        b, m = back_of(j)
        to_core(j).wait_recv()
        gp[b, m, :, :, :, core] = gp[b, m, :, :, :, core] + from_core[b, m]
        start_all(to_far(j))

    def scatter_diag(j):
        b, m = back_of(j)
        to_far(j)[0].wait_recv()
        gp[b, m, :, near_y, near_x, core] = gp[b, m, :, near_y, near_x, core] + from_diag[b, m]
        to_near(j).start()

    def scatter_plane(j):
        b, m = back_of(j)
        to_far(j)[1].wait_recv()
        to_near(j).wait_recv()
        value = gp[b, m, :, y, x, core].astype(F32) + from_plain[b, m].astype(F32) + from_pair[b, m].astype(F32)
        gp[b, m, :, y, x, core] = value.astype(BF)
        start_all(to_z(j))

    def scatter_z(j):
        b, m = back_of(j)
        for copy in to_z(j):
            copy.wait_recv()
        value = gp[b, m, z, y, x, core].astype(F32)
        for s in range(ZN - 1):
            value = value + from_z[b, m, s].astype(F32)
        total[b, m] = value
        squares[...] = squares[...] + value * value

    def guarded(low, j, step):
        pl.when(jnp.logical_and(j >= low, j < count + low))(lambda: step(j - low))

    def dz_slot(k):
        return lax.rem(5 - k, 3)

    def add_rows(value):
        return jnp.sum(value.reshape(-1, 8, hidden), axis=0)

    def put_bias(k, acc):
        bias_sum[pl.ds(span + k, 1), :] = jnp.sum(acc, axis=0, keepdims=True)

    def head_step(b):
        def body(t, carry):
            at = pl.ds(pl.multiple_of(t * tile, tile), tile)

            @pl.when(b == 1)
            def _():
                resid[at, :] = jnp.zeros((tile, 128), F32)

            e = (-(resid[at, :] * mask[at, :])).astype(BF)
            e_ref[at, :] = e
            work[0, at, :] = dot_nt(e, small(b, 256)).astype(BF)
            work[1, at, :] = dot_nt(f_ref[at, :], small(b, 128)).astype(BF)
            return carry

        lax.fori_loop(0, tiles, body, 0)

    def theta_step(b):
        def body(t, acc):
            at = pl.ds(pl.multiple_of(t * tile, tile), tile)
            da = dot_nt(work[0, at, :], matrix(b, 4)) + dot_nt(work[1, at, :], matrix(b, 5))
            dz = da * slope[b, 3, at, :].astype(F32)
            work[2, at, :] = dz.astype(BF)
            return acc + add_rows(dz)

        put_bias(3, lax.fori_loop(0, tiles, body, jnp.zeros((8, hidden), F32)))

    def layer_back(b, k):
        source, target = dz_slot(k + 1), dz_slot(k)

        def body(t, acc):
            at = pl.ds(pl.multiple_of(t * tile, tile), tile)
            dz = dot_nt(work[source, at, :], matrix(b, k + 1)) * slope[b, k, at, :].astype(F32)
            work[target, at, :] = dz.astype(BF)
            return acc + add_rows(dz)

        put_bias(k, lax.fori_loop(0, tiles, body, jnp.zeros((8, hidden), F32)))

    def grid(value):
        return value.astype(BF).reshape(ZN, YN, XN, 2, half_rows, -1)

    def weight_grad(b, j):
        s = lax.rem(j, MATS)
        layer = jnp.where(s <= 1, 3, 4 - s)
        slot = jnp.where(s <= 1, s, dz_slot(5 - s))
        _, m = back_of(j)
        gp[b, m] = grid(dot_nn(act_t[b, layer], work[slot]))

    def small_grads(b):
        gp[b, 0, :, :, :, :, :, 0:128] = grid(dot_nn(in_t[b], work[2]).T)
        forecast = dot_nn(theta_t[b, 1], f_ref[...]) + bias_sum[...].T
        gp[b, 0, :, :, :, :, :, 128:256] = grid(forecast)
        gp[b, 0, :, :, :, :, :, 256:384] = grid(dot_nn(theta_t[b, 0], e_ref[...]))
        gp[b, 0, :, :, :, :, :, 384:512] = jnp.zeros((ZN, YN, XN, 2, half_rows, 128), BF)

    def input_grad(b):
        def body(t, carry):
            at = pl.ds(pl.multiple_of(t * tile, tile), tile)
            keep = mask[at, :]
            dr = resid[at, :] * keep + 2.0 * dot_nn(work[2, at, :], small(b, 0))

            @pl.when(b == 1)
            def _():
                sens[1, at, :] = dr[:, 0:past]
                resid[at, :] = dr.astype(BF).astype(F32)

            @pl.when(b == 0)
            def _():
                sens[0, at, :] = (dr * keep)[:, 0:past]

            return carry

        lax.fori_loop(0, tiles, body, 0)

    bias_sum[...] = jnp.zeros_like(bias_sum)
    squares[...] = jnp.zeros_like(squares)

    def back_step(j, carry):
        s = lax.rem(j, MATS)
        b, _ = back_of(j)
        live = j < count

        def on(test, step):
            pl.when(jnp.logical_and(live, test))(step)

        on(s == 0, lambda: head_step(b))
        on(s == 2, lambda: theta_step(b))
        on(s >= 3, lambda: layer_back(b, 5 - s))
        guarded(4, j, scatter_z)
        guarded(3, j, scatter_plane)
        guarded(2, j, scatter_diag)
        guarded(1, j, scatter_core)
        on(s <= 4, lambda: weight_grad(b, j))
        on(s == 5, lambda: small_grads(b))
        pl.when(live)(lambda: to_core(j).start())
        on(s == 5, lambda: input_grad(b))
        pl.when(j == count - 1)(lambda: start_all(out_copies(sens, sens_out, 1)))
        return carry

    lax.fori_loop(0, count + 4, back_step, 0)

    grad_copy = remote(total.at[other], grad_out.at[:, core], out_send.at[2], out_recv.at[2], sibling)
    grad_copy.start()
    grad_out[:, core] = total[core]
    sq = squares[:, 0:128] + squares[:, 128:256] + squares[:, 256:384] + squares[:, 384:512]
    norm_buf[0] = sq[0:8] + sq[8:16]
    for step, device in enumerate([sibling, chip(z, y, xo), chip(z, yo, x)]):
        copy = remote(norm_buf.at[2 * step], norm_buf.at[2 * step + 1], norm_send.at[step], norm_recv.at[step], device)
        copy.start()
        copy.wait()
        norm_buf[2 * step + 2] = norm_buf[2 * step] + norm_buf[2 * step + 1]
    norm_buf[7 + z] = norm_buf[6]
    spread = [
        remote(norm_buf.at[6], norm_buf.at[7 + z], norm_send.at[3 + s], norm_recv.at[3 + s], chip(zi, y, x))
        for s, zi in enumerate(z_peers)
    ]
    start_all(spread)
    for copy in spread:
        copy.wait()
    everything = norm_buf[7]
    for zi in range(1, ZN):
        everything = everything + norm_buf[7 + zi]
    norm_out[...] = jnp.broadcast_to(jnp.sqrt(jnp.sum(everything, keepdims=True)), norm_out.shape)

    grad_copy.wait()
    for buf, out, s in ((pred, pred_out, 0), (sens, sens_out, 1)):
        for copy in out_copies(buf, out, s):
            copy.wait()
    own.wait_send()

    def drain(i, carry):
        for copy in z_copies(i) + column_copies(i) + [corner_copy(i), core_copy(i)]:
            copy.wait_send()
        for copy in [to_core(i), *to_far(i), to_near(i), *to_z(i)]:
            copy.wait_send()
        return carry

    lax.fori_loop(0, count, drain, 0)


def train_call(plane, segments, extents, adjoint, first, square, head, biases):
    ZN, YN, XN = plane
    past, span, hidden = segments.shape[1], adjoint.shape[1], square.shape[3]
    windows = segments.shape[0] // 2
    tile = 512
    half = hidden // (ZN * YN * XN) // 2
    sizes = (ZN, YN, XN, windows, tile, past, span, hidden)
    DMA = pltpu.SemaphoreType.DMA
    vmem = pl.BlockSpec(memory_space=pltpu.VMEM)
    hbm = pl.BlockSpec(memory_space=pl.ANY)
    count = 2 * MATS
    flops = 2 * 2 * 3 * windows * hidden * (6 * hidden + 2 * 128)
    return pl.pallas_call(
        functools.partial(train_kernel, sizes),
        out_shape=(
            jax.ShapeDtypeStruct((1, 2 * windows, span), F32),
            jax.ShapeDtypeStruct((1, 2 * windows, past), F32),
            jax.ShapeDtypeStruct((MATS, 2, half, hidden), F32),
            jax.ShapeDtypeStruct((8, 128), F32),
        ),
        in_specs=[hbm, hbm] + [vmem] * 5,
        out_specs=(hbm, hbm, vmem, vmem),
        scratch_shapes=[
            pltpu.VMEM((2, MATS, ZN, YN, XN, 2, half, hidden), BF),
            pltpu.VMEM((MATS, half, hidden), BF),
            pltpu.VMEM((2, MATS, ZN, YN, XN, 2, half, hidden), BF),
            pltpu.VMEM((2, MATS, ZN, YN, XN, half, hidden), BF),
            pltpu.VMEM((2, MATS, ZN, half, hidden), BF),
            pltpu.VMEM((2, MATS, ZN, half, hidden), BF),
            pltpu.VMEM((2, MATS, ZN, half, hidden), BF),
            pltpu.VMEM((2, MATS, ZN - 1, half, hidden), BF),
            pltpu.VMEM((2, MATS, half, hidden), F32),
            pltpu.VMEM((2, 4, hidden, windows), BF),
            pltpu.VMEM((2, 128, windows), BF),
            pltpu.VMEM((2, 2, hidden, windows), BF),
            pltpu.VMEM((2, 4, windows, hidden), BF),
            pltpu.VMEM((3, windows, hidden), BF),
            pltpu.VMEM((windows, 128), F32),
            pltpu.VMEM((windows, 128), F32),
            pltpu.VMEM((windows, 128), BF),
            pltpu.VMEM((windows, 128), BF),
            pltpu.VMEM((8, 128), F32),
            pltpu.VMEM((128, hidden), F32),
            pltpu.VMEM((128, hidden), F32),
            pltpu.VMEM((128, 128), F32),
            pltpu.VMEM((windows, past), F32),
            pltpu.VMEM((windows, span), F32),
            pltpu.VMEM((2, windows, span), F32),
            pltpu.VMEM((2, windows, past), F32),
            pltpu.VMEM((half, hidden), F32),
            pltpu.VMEM((7 + ZN, 8, 128), F32),
            DMA((1,)),
            DMA((1,)),
            DMA((count, 7)),
            DMA((count, 7)),
            DMA((count, 4 + ZN - 1)),
            DMA((count, 4 + ZN - 1)),
            DMA((3,)),
            DMA((3,)),
            DMA((4,)),
            DMA((3 + ZN - 1,)),
            DMA((3 + ZN - 1,)),
        ],
        compiler_params=pltpu.CompilerParams(
            collective_id=0, has_side_effects=True, vmem_limit_bytes=64 * 1024 * 1024
        ),
        cost_estimate=pl.CostEstimate(flops=flops, bytes_accessed=8_000_000, transcendentals=8 * windows * hidden),
        name="train",
    )(segments, adjoint, extents.reshape(-1, 128), first, square, head, biases)


def update_kernel(past, span, grads, norm, *refs):
    masters, momenta, variances, outs, pad = refs[0:4], refs[4:8], refs[8:12], refs[12:-1], refs[-1]
    factor = 1.0 / jnp.maximum(norm[0:1, 0:1], 1.0)
    units = masters[3].shape[2]

    def rows(m, lane, width):
        return grads[m, :, :, lane : lane + width].reshape(units, width)

    forecast = rows(0, 128, 128)
    pad[...] = jnp.zeros_like(pad)
    pad[0:units, :] = rows(0, 0, 128)
    outs[0][0] = pad[...].T[0:past, 0:units]
    pad[0:units, :] = forecast
    outs[3][0] = pad[...].T[span : span + 4, 0:units]
    for m in range(5):
        outs[1][0, m] = rows(m + 1, 0, grads.shape[3])
    outs[2][0, :, 0:past] = rows(0, 256, 128)[:, 0:past]
    outs[2][0, :, past : past + span] = forecast[:, 0:span]
    for n in range(4):
        master, gradient = masters[n][...], outs[n][...]
        new, moment, spread = adamw(master, gradient, momenta[n][...], variances[n][...], factor[None])
        outs[4 + n][...], outs[8 + n][...], outs[12 + n][...] = new, moment, spread


def update_call(past, span, grads, norm, state):
    vmem = pl.BlockSpec(memory_space=pltpu.VMEM)
    shapes = tuple(jax.ShapeDtypeStruct(a.shape, F32) for a in state[:4])
    return pl.pallas_call(
        functools.partial(update_kernel, past, span),
        out_shape=4 * shapes,
        in_specs=[vmem] * (2 + len(state)),
        out_specs=tuple([vmem] * 16),
        scratch_shapes=[pltpu.VMEM((128, 128), F32)],
        name="update",
    )(grads, norm, *state)


def kernel_shards(plane, segments, extents, adjoint, *state):
    prediction, sensitivity, grads, norm = train_call(plane, segments, extents, adjoint, *state[:4])
    updated = update_call(segments.shape[1], adjoint.shape[1], grads, norm, state)
    return (prediction, sensitivity, norm[0, 0], *updated)


STATE_SPECS = (
    P("section", None, "dp"),
    P("section", None, "dp", None),
    P("section", "dp", None),
    P("section", None, "dp"),
)


def solution(mesh):
    in_specs = (P("dp", None), P("dp"), P("dp", None)) + 3 * STATE_SPECS
    out_specs = (P("section", "dp", None), P("section", "dp", None), P()) + 4 * STATE_SPECS
    plane = PLANES.get(mesh.shape["dp"])
    shards = plain_shards if plane is None else functools.partial(kernel_shards, plane)
    return jax.shard_map(shards, mesh=mesh, in_specs=in_specs, out_specs=out_specs, check_vma=False)
```

```python
import functools

import jax
import jax.numpy as jnp
from jax import lax
from jax.experimental import pallas as pl
from jax.experimental.pallas import tpu as pltpu
from jax.sharding import PartitionSpec as P

STEP = 10


def dot_nn(a, b):
    return jnp.dot(a, b, preferred_element_type=jnp.float32)


def dot_tn(a, b):
    return lax.dot_general(a, b, (((0,), (0,)), ((), ())), preferred_element_type=jnp.float32)


def dot_nt(a, b):
    return lax.dot_general(a, b, (((1,), (1,)), ((), ())), preferred_element_type=jnp.float32)


def unit_rows(first, square, head, biases):
    units = first.shape[1]
    return jnp.concatenate(
        [square.transpose(1, 0, 2).reshape(units, -1), first.T, head, biases.T], axis=1
    )


def from_unit_rows(rows, past, hidden, out):
    wide = 5 * hidden
    square = rows[:, :wide].reshape(-1, 5, hidden).transpose(1, 0, 2)
    first = rows[:, wide : wide + past].T
    head = rows[:, wide + past : wide + past + out]
    biases = rows[:, wide + past + out :].T
    return first, square, head, biases


def plain_forward(weights, resid):
    first, square, head, biases = weights
    past = resid.shape[1]
    acts, slopes = [resid.astype(jnp.bfloat16)], []
    for k in range(4):
        z = dot_nn(acts[-1], first if k == 0 else square[k - 1]) + biases[k].astype(jnp.float32)
        sig = jax.nn.sigmoid(z)
        acts.append((z * sig).astype(jnp.bfloat16))
        slopes.append(sig * (1.0 + z * (1.0 - sig)))
    theta_b = dot_nn(acts[4], square[3]).astype(jnp.bfloat16)
    theta_f = dot_nn(acts[4], square[4]).astype(jnp.bfloat16)
    backcast = dot_nn(theta_b, head[:, :past])
    part = dot_nn(theta_f, head[:, past:])
    return backcast, part, (acts, slopes, theta_b, theta_f)


def plain_backward(weights, saved, e, f):
    first, square, head, biases = weights
    acts, slopes, theta_b, theta_f = saved
    past = e.shape[1]
    head_grad = jnp.concatenate([dot_tn(theta_b, e), dot_tn(theta_f, f)], axis=1)
    u_b = dot_nt(e, head[:, :past]).astype(jnp.bfloat16)
    u_f = dot_nt(f, head[:, past:]).astype(jnp.bfloat16)
    squares = [None, None, None, dot_tn(acts[4], u_b), dot_tn(acts[4], u_f)]
    da = dot_nt(u_b, square[3]) + dot_nt(u_f, square[4])
    bias_grads = [None] * 4
    first_grad = None
    for k in (3, 2, 1, 0):
        dz = (da * slopes[k]).astype(jnp.bfloat16)
        bias_grads[k] = jnp.sum(dz, axis=0, dtype=jnp.float32)
        grad = dot_tn(acts[k], dz)
        if k == 0:
            first_grad = grad
        else:
            squares[k - 1] = grad
        da = dot_nt(dz, first if k == 0 else square[k - 1])
    return da, (first_grad, jnp.stack(squares), head_grad, jnp.stack(bias_grads))


def adamw(master, gradient, momentum, variance, factor):
    clipped = gradient * factor
    moment_new = 0.9 * momentum + 0.1 * clipped
    variance_new = 0.999 * variance + 0.001 * clipped * clipped
    ratio = moment_new / (1.0 - 0.9**STEP) / (jnp.sqrt(variance_new / (1.0 - 0.999**STEP)) + 1e-08)
    return master - 0.05 * (ratio + 0.01 * master), moment_new, variance_new


def plain_shards(segments, extents, adjoint, *state):
    masters, momenta, variances = state[:4], state[4:8], state[8:]
    core = lax.axis_index("section")
    past, span = segments.shape[1], adjoint.shape[1]
    windows = segments.shape[0] // 2
    hidden = masters[1].shape[3]
    mine = [
        lax.dynamic_slice_in_dim(v, core * windows, windows, 0) for v in (segments, extents, adjoint)
    ]
    seg, ext, adj = mine
    rows = unit_rows(*(m[0].astype(jnp.bfloat16) for m in masters))
    rows = lax.all_gather(rows, "dp", axis=0, tiled=True)
    rows = lax.all_gather(rows, "section", axis=0)
    blocks = [from_unit_rows(rows[b], past, hidden, past + span) for b in range(2)]
    mask = (
        lax.broadcasted_iota(jnp.int32, (windows, past), 1) >= past - ext[:, None]
    ).astype(jnp.float32)
    r0 = seg * mask
    backcast, part0, saved0 = plain_forward(blocks[0], r0)
    r1 = (r0 - backcast) * mask
    _, part1, saved1 = plain_forward(blocks[1], r1)
    forecast = part0.astype(jnp.bfloat16).astype(jnp.float32) + part1
    f = adj.astype(jnp.bfloat16)
    zero = jnp.zeros_like(r0)
    da1, grads1 = plain_backward(blocks[1], saved1, (-(zero * mask)).astype(jnp.bfloat16), f)
    dr1 = zero * mask + da1
    t = dr1.astype(jnp.bfloat16).astype(jnp.float32)
    da0, grads0 = plain_backward(blocks[0], saved0, (-(t * mask)).astype(jnp.bfloat16), f)
    dr0 = (t * mask + da0) * mask

    def by_section(first_block, second_block):
        mine, other = (
            jnp.where(core == 0, first_block, second_block),
            jnp.where(core == 0, second_block, first_block),
        )
        got = lax.ppermute(other, "section", [(0, 1), (1, 0)])
        return jnp.where(
            core == 0, jnp.concatenate([mine, got]), jnp.concatenate([got, mine])
        )[None]

    prediction = by_section(part0, forecast)
    sensitivity = by_section(dr0, dr1)
    packed = jnp.stack([unit_rows(*grads0), unit_rows(*grads1)])
    packed = lax.psum_scatter(packed, "section", scatter_dimension=0, tiled=False)
    packed = lax.psum_scatter(packed, "dp", scatter_dimension=0, tiled=True)
    norm = jnp.sqrt(lax.psum(jnp.sum(packed * packed), ("section", "dp")))
    factor = 1.0 / jnp.maximum(norm, 1.0)
    summed = [g[None] for g in from_unit_rows(packed, past, hidden, past + span)]
    updated = [adamw(*four, factor) for four in zip(masters, summed, momenta, variances)]
    return (
        prediction,
        sensitivity,
        norm,
        *summed,
        *(u[0] for u in updated),
        *(u[1] for u in updated),
        *(u[2] for u in updated),
    )


PLANES = {16: (4, 2, 2)}
MESH = pl.DeviceIdType.MESH
MATS = 6
BF, F32 = jnp.bfloat16, jnp.float32


def remote(src, dst, send_sem, recv_sem, device):
    return pltpu.make_async_remote_copy(
        src_ref=src, dst_ref=dst, send_sem=send_sem, recv_sem=recv_sem, device_id=device, device_id_type=MESH
    )


def train_kernel(
    sizes,
    seg_hbm, adj_hbm, ext, first, square, head, biases,
    pred_out, sens_out, grad_out, norm_out,
    wg, handed, gp, from_core, from_diag, from_plain, from_pair, from_z, total,
    act_t, in_t, theta_t, forecast_grad, slope, work, resid, mask, f_ref, e_ref, t_ref, bias_t, bias_sum, pad,
    seg, adj, pred, sens, squares, norm_buf,
    own_send, own_recv, ag_send, ag_recv, rs_send, rs_recv, out_send, out_recv, local_sem, norm_send, norm_recv,
):
    ZN, YN, XN, windows, tile, past, span, hidden = sizes
    units = ZN * YN * XN
    core, dp = lax.axis_index("section"), lax.axis_index("dp")
    x, y, z = lax.rem(dp, XN), lax.rem(lax.div(dp, XN), YN), lax.div(dp, XN * YN)
    other, xo, yo = 1 - core, 1 - x, 1 - y
    near_y, near_x = y + core * (yo - y), xo + core * (x - xo)
    far_y, far_x = yo + core * (y - yo), x + core * (xo - x)

    def chip(zi, yi, xi):
        return (core, (zi * YN + yi) * XN + xi)

    sibling = (other, dp)
    z_peers = [lax.rem(z + step, ZN) for step in range(1, ZN)]

    row0 = core * windows
    loads = [
        pltpu.make_async_copy(seg_hbm.at[pl.ds(row0, windows), :], seg, local_sem.at[0]),
        pltpu.make_async_copy(adj_hbm.at[:, pl.ds(row0, windows)], adj, local_sem.at[1]),
    ]
    for load in loads:
        load.start()

    barrier = pltpu.get_barrier_semaphore()
    peers = [sibling, chip(z, y, xo), chip(z, yo, x)] + [chip(zi, y, x) for zi in z_peers]
    for peer in peers:
        pl.semaphore_signal(barrier, inc=1, device_id=peer, device_id_type=MESH)

    rows = hidden // units
    half_rows = rows // 2

    def put_own(m, value, lanes):
        halves = value.astype(BF).reshape(2, half_rows, -1)
        for h in range(2):
            pl.when(core == h)(functools.partial(put_half, m, halves[h], halves[1 - h], lanes))

    def put_half(m, kept, given, lanes):
        wg[core, m, z, y, x, core, :, lanes] = kept
        handed[m, :, lanes] = given

    pad[...] = jnp.zeros_like(pad)
    pad[0:rows, 0:past] = first[0] * 0.5
    put_own(0, pad[0:rows, :], slice(0, 128))
    pad[...] = jnp.zeros_like(pad)
    pad[span : span + 4, 0:rows] = biases[0] * 0.5
    bias_cols = pad[...].T[0:rows]
    pad[...] = jnp.zeros_like(pad)
    pad[0:rows, 0:span] = head[0, :, past : past + span]
    put_own(0, pad[0:rows, :] + bias_cols, slice(128, 256))
    pad[...] = jnp.zeros_like(pad)
    pad[0:rows, 0:past] = head[0, :, 0:past]
    put_own(0, pad[0:rows, :], slice(256, 384))
    put_own(0, jnp.zeros((rows, 128), F32), slice(384, 512))
    for m in range(5):
        put_own(m + 1, square[0, m] * 0.5 if m < 3 else square[0, m], slice(0, hidden))
    pl.semaphore_wait(barrier, len(peers))

    own = remote(handed, wg.at[core, :, z, y, x, other], own_send.at[0], own_recv.at[0], sibling)
    own.start()

    def of(i):
        return lax.div(i, MATS), lax.rem(i, MATS)

    def z_copies(i):
        b, m = of(i)
        part = wg.at[b, m, z, y, x, core]
        return [
            remote(part, part, ag_send.at[i, s], ag_recv.at[i, s], chip(zi, y, x)) for s, zi in enumerate(z_peers)
        ]

    def column_copies(i):
        b, m = of(i)
        part = wg.at[b, m, :, y, x, core]
        return [
            remote(part, part, ag_send.at[i, 3], ag_recv.at[i, 3], chip(z, near_y, near_x)),
            remote(part, part, ag_send.at[i, 4], ag_recv.at[i, 4], chip(z, far_y, far_x)),
        ]

    def corner_copy(i):
        b, m = of(i)
        part = wg.at[b, m, :, near_y, near_x, core]
        return remote(part, part, ag_send.at[i, 5], ag_recv.at[i, 5], chip(z, far_y, far_x))

    def core_copy(i):
        b, m = of(i)
        part = wg.at[b, m, :, :, :, core]
        return remote(part, part, ag_send.at[i, 6], ag_recv.at[i, 6], sibling)

    def start_all(copies):
        for copy in copies:
            copy.start()

    for load in loads:
        load.wait()
    zeros_tile = jnp.zeros((tile, 128), F32)

    def prepare(t, carry):
        at = pl.ds(t * tile, tile)
        resid[at, :] = zeros_tile
        resid[at, 0:past] = seg[at, :]
        return carry

    def prepare_mask(g, carry):
        lengths = ext[pl.ds(core * (windows // 128) + g, 1), :]
        position = lax.broadcasted_iota(jnp.int32, (128, 128), 0)
        keep = jnp.where(position >= past - lengths, 1.0, 0.0).astype(F32).T
        at = pl.ds(pl.multiple_of(g * 128, 128), 128)
        pad[0:span, :] = adj[:, at]
        f_ref[at, :] = pad[...].T.astype(BF)
        mask[at, :] = keep
        resid[at, :] = resid[at, :] * keep
        return carry

    tiles = windows // tile

    def matrix(b, m):
        return wg[b, m].reshape(hidden, hidden)

    def small(b, lane):
        return wg[b, 0, :, :, :, :, :, lane : lane + 128].reshape(hidden, 128)

    def store_layer(b, k, at, v, scale):
        p = 1.0 + jnp.tanh(v)
        a = v * p
        rate = p + a * (2.0 - p)
        slope[b, k, at, :] = (rate if scale is None else rate * scale).astype(BF)
        low = a.astype(BF)
        act_t[b, k, :, at] = low.T
        return low

    def layer_zero(b):
        bias_t[...] = small(b, 128).astype(F32).T

        def body(t, carry):
            at = pl.ds(pl.multiple_of(t * tile, tile), tile)
            a = resid[at, :].astype(BF)
            in_t[b, :, at] = a.T
            v = dot_nt(a, small(b, 0)) + bias_t[span : span + 1, :]
            work[0, at, :] = store_layer(b, 0, at, v, None)
            return carry

        lax.fori_loop(0, tiles, body, 0)

    def layer_next(b, k):
        source, target = lax.rem(k + 1, 2), lax.rem(k, 2)
        bias = bias_t[pl.ds(span + k, 1), :]
        scale = jnp.where(k == 3, 0.5, 1.0)

        def body(t, carry):
            at = pl.ds(pl.multiple_of(t * tile, tile), tile)
            v = dot_nn(work[source, at, :], matrix(b, k)) + bias
            work[target, at, :] = store_layer(b, k, at, v, scale)
            return carry

        lax.fori_loop(0, tiles, body, 0)

    def grid(value):
        return value.astype(BF).reshape(ZN, YN, XN, 2, half_rows, -1)

    def backcast_grad(b):
        gp[b, 0, :, :, :, :, :, 256:384] = grid(dot_nn(theta_t[b], e_ref[...]))

    def backcast_step(b):
        def body(t, carry):
            at = pl.ds(pl.multiple_of(t * tile, tile), tile)
            theta = dot_nn(work[1, at, :], matrix(b, 4)).astype(BF)
            theta_t[b, :, at] = theta.T

            @pl.when(b == 0)
            def _():
                backcast = dot_nn(theta, small(b, 256))
                resid[at, :] = (resid[at, :] - backcast) * mask[at, :]

            @pl.when(b == 1)
            def _():
                e_ref[at, :] = (-(jnp.zeros((tile, 128), F32) * mask[at, :])).astype(BF)

            return carry

        lax.fori_loop(0, tiles, body, 0)
        pl.when(b == 1)(lambda: backcast_grad(b))

    def forecast_step(b):
        def body(t, carry):
            at = pl.ds(pl.multiple_of(t * tile, tile), tile)
            theta = dot_nn(work[1, at, :], matrix(b, 5)).astype(BF)
            theta_t[1, :, at] = theta.T
            part = dot_nn(theta, small(b, 128)).T[0:span]

            @pl.when(b == 0)
            def _():
                pred[0, :, at] = part

            @pl.when(b == 1)
            def _():
                pred[1, :, at] = pred[0, :, at].astype(BF).astype(F32) + part

            return carry

        lax.fori_loop(0, tiles, body, 0)
        forecast_grad[b] = dot_nn(theta_t[1], f_ref[...])

    own.wait_recv()
    for i in range(3):
        start_all(z_copies(i))
    lax.fori_loop(0, tiles, prepare, 0)
    pad[...] = jnp.zeros_like(pad)
    lax.fori_loop(0, windows // 128, prepare_mask, 0)

    count = 2 * MATS

    def gather_step(i, carry):
        @pl.when(i + 3 < count)
        def _():
            start_all(z_copies(i + 3))

        @pl.when(i < count)
        def _():
            for copy in z_copies(i):
                copy.wait_recv()
            start_all(column_copies(i))

        @pl.when(jnp.logical_and(i >= 1, i < count + 1))
        def _():
            column_copies(i - 1)[0].wait_recv()
            corner_copy(i - 1).start()

        @pl.when(jnp.logical_and(i >= 2, i < count + 2))
        def _():
            column_copies(i - 2)[1].wait_recv()
            corner_copy(i - 2).wait_recv()
            core_copy(i - 2).start()

        @pl.when(i >= 3)
        def _():
            core_copy(i - 3).wait_recv()
            b, m = of(i - 3)
            pl.when(m == 0)(lambda: layer_zero(b))
            pl.when(jnp.logical_and(m >= 1, m <= 3))(lambda: layer_next(b, m))
            pl.when(m == 4)(lambda: backcast_step(b))
            pl.when(m == 5)(lambda: forecast_step(b))

        return carry

    lax.fori_loop(0, count + 3, gather_step, 0)

    def out_copies(buf, out, s):
        at = pl.ds(row0, windows)
        return [
            pltpu.make_async_copy(buf.at[core], out.at[:, 0, at], local_sem.at[2 + s]),
            remote(buf.at[other], out.at[:, 0, at], out_send.at[s], out_recv.at[s], sibling),
        ]

    start_all(out_copies(pred, pred_out, 0))

    def back_of(j):
        s = lax.rem(j, MATS)
        return 1 - lax.div(j, MATS), jnp.where(s == 0, 4, jnp.where(s == 1, 5, 5 - s))

    def to_core(j):
        b, m = back_of(j)
        return remote(
            gp.at[b, m, :, :, :, other], from_core.at[lax.rem(j, 2)], rs_send.at[j, 0], rs_recv.at[j, 0], sibling
        )

    def to_far(j):
        b, m = back_of(j)
        device = chip(z, far_y, far_x)
        return [
            remote(gp.at[b, m, :, yo, xo, core], from_diag.at[b, m], rs_send.at[j, 1], rs_recv.at[j, 1], device),
            remote(gp.at[b, m, :, far_y, far_x, core], from_plain.at[b, m], rs_send.at[j, 2], rs_recv.at[j, 2], device),
        ]

    def to_near(j):
        b, m = back_of(j)
        return remote(
            gp.at[b, m, :, near_y, near_x, core], from_pair.at[b, m], rs_send.at[j, 3], rs_recv.at[j, 3],
            chip(z, near_y, near_x),
        )

    def to_z(j):
        b, m = back_of(j)
        return [
            remote(gp.at[b, m, zi, y, x, core], from_z.at[b, m, s], rs_send.at[j, 4 + s], rs_recv.at[j, 4 + s], chip(zi, y, x))
            for s, zi in enumerate(z_peers)
        ]

    def scatter_core(j):
        b, m = back_of(j)
        to_core(j).wait_recv()
        gp[b, m, :, :, :, core] = gp[b, m, :, :, :, core] + from_core[lax.rem(j, 2)]
        start_all(to_far(j))

    def scatter_diag(j):
        b, m = back_of(j)
        to_far(j)[0].wait_recv()
        gp[b, m, :, near_y, near_x, core] = gp[b, m, :, near_y, near_x, core] + from_diag[b, m]
        to_near(j).start()

    def scatter_plane(j):
        b, m = back_of(j)
        to_far(j)[1].wait_recv()
        to_near(j).wait_recv()
        value = gp[b, m, :, y, x, core].astype(F32) + from_plain[b, m].astype(F32) + from_pair[b, m].astype(F32)
        gp[b, m, :, y, x, core] = value.astype(BF)
        start_all(to_z(j))

    def scatter_z(j):
        b, m = back_of(j)
        for copy in to_z(j):
            copy.wait_recv()
        value = gp[b, m, z, y, x, core].astype(F32)
        for s in range(ZN - 1):
            value = value + from_z[b, m, s].astype(F32)
        total[b, m] = value
        squares[...] = squares[...] + value * value

    def guarded(low, j, step):
        pl.when(jnp.logical_and(j >= low, j < count + low))(lambda: step(j - low))

    def dz_slot(k):
        return lax.rem(5 - k, 3)

    def add_rows(value):
        return jnp.sum(value.reshape(-1, 8, hidden), axis=0)

    def put_bias(k, acc):
        bias_sum[pl.ds(span + k, 1), :] = jnp.sum(acc, axis=0, keepdims=True)

    def head_step(b):
        def body(t, carry):
            at = pl.ds(pl.multiple_of(t * tile, tile), tile)

            @pl.when(b == 1)
            def _():
                resid[at, :] = jnp.zeros((tile, 128), F32)

            e = (-(resid[at, :] * mask[at, :])).astype(BF)
            e_ref[at, :] = e
            work[0, at, :] = dot_nt(e, small(b, 256)).astype(BF)
            work[1, at, :] = dot_nt(f_ref[at, :], small(b, 128)).astype(BF)
            return carry

        lax.fori_loop(0, tiles, body, 0)

    def theta_step(b):
        def body(t, acc):
            at = pl.ds(pl.multiple_of(t * tile, tile), tile)
            da = dot_nt(work[0, at, :], matrix(b, 4)) + dot_nt(work[1, at, :], matrix(b, 5))
            dz = da * slope[b, 3, at, :].astype(F32)
            work[2, at, :] = dz.astype(BF)
            return acc + add_rows(dz)

        put_bias(3, lax.fori_loop(0, tiles, body, jnp.zeros((8, hidden), F32)))

    def layer_back(b, k):
        source, target = dz_slot(k + 1), dz_slot(k)

        def body(t, acc):
            at = pl.ds(pl.multiple_of(t * tile, tile), tile)
            dz = dot_nt(work[source, at, :], matrix(b, k + 1)) * slope[b, k, at, :].astype(F32)
            work[target, at, :] = dz.astype(BF)
            return acc + add_rows(dz)

        put_bias(k, lax.fori_loop(0, tiles, body, jnp.zeros((8, hidden), F32)))

    def weight_grad(b, j):
        s = lax.rem(j, MATS)
        layer = jnp.where(s <= 1, 3, 4 - s)
        slot = jnp.where(s <= 1, s, dz_slot(5 - s))
        _, m = back_of(j)
        gp[b, m] = grid(dot_nn(act_t[b, layer], work[slot]))

    def small_grads(b):
        gp[b, 0, :, :, :, :, :, 0:128] = grid(dot_nn(in_t[b], work[2]).T)
        forecast = forecast_grad[b] + bias_sum[...].T
        gp[b, 0, :, :, :, :, :, 128:256] = grid(forecast)
        pl.when(b == 0)(lambda: backcast_grad(b))
        gp[b, 0, :, :, :, :, :, 384:512] = jnp.zeros((ZN, YN, XN, 2, half_rows, 128), BF)

    def input_grad(b):
        def body(t, carry):
            at = pl.ds(pl.multiple_of(t * tile, tile), tile)
            keep = mask[at, :]
            dr = resid[at, :] * keep + 2.0 * dot_nn(work[2, at, :], small(b, 0))

            @pl.when(b == 1)
            def _():
                sens[1, :, at] = dr.T[0:past]
                resid[at, :] = dr.astype(BF).astype(F32)

            @pl.when(b == 0)
            def _():
                sens[0, :, at] = (dr * keep).T[0:past]

            return carry

        lax.fori_loop(0, tiles, body, 0)

    bias_sum[...] = jnp.zeros_like(bias_sum)
    squares[...] = jnp.zeros_like(squares)

    def back_step(j, carry):
        s = lax.rem(j, MATS)
        b, _ = back_of(j)
        live = j < count

        def on(test, step):
            pl.when(jnp.logical_and(live, test))(step)

        on(s == 0, lambda: head_step(b))
        on(s == 2, lambda: theta_step(b))
        on(s >= 3, lambda: layer_back(b, 5 - s))
        guarded(4, j, scatter_z)
        guarded(3, j, scatter_plane)
        guarded(2, j, scatter_diag)
        guarded(1, j, scatter_core)
        on(s <= 4, lambda: weight_grad(b, j))
        on(s == 5, lambda: small_grads(b))
        pl.when(live)(lambda: to_core(j).start())
        on(s == 5, lambda: input_grad(b))
        pl.when(j == count - 1)(lambda: start_all(out_copies(sens, sens_out, 1)))
        return carry

    lax.fori_loop(0, count + 4, back_step, 0)

    grad_copy = remote(total.at[other], grad_out.at[:, core], out_send.at[2], out_recv.at[2], sibling)
    grad_copy.start()
    grad_out[:, core] = total[core]
    sq = squares[:, 0:128] + squares[:, 128:256] + squares[:, 256:384] + squares[:, 384:512]
    norm_buf[0] = sq[0:8] + sq[8:16]
    for step, device in enumerate([sibling, chip(z, y, xo), chip(z, yo, x)]):
        copy = remote(norm_buf.at[2 * step], norm_buf.at[2 * step + 1], norm_send.at[step], norm_recv.at[step], device)
        copy.start()
        copy.wait()
        norm_buf[2 * step + 2] = norm_buf[2 * step] + norm_buf[2 * step + 1]
    norm_buf[7 + z] = norm_buf[6]
    spread = [
        remote(norm_buf.at[6], norm_buf.at[7 + z], norm_send.at[3 + s], norm_recv.at[3 + s], chip(zi, y, x))
        for s, zi in enumerate(z_peers)
    ]
    start_all(spread)
    for copy in spread:
        copy.wait()
    everything = norm_buf[7]
    for zi in range(1, ZN):
        everything = everything + norm_buf[7 + zi]
    norm_out[...] = jnp.broadcast_to(jnp.sqrt(jnp.sum(everything, keepdims=True)), norm_out.shape)

    grad_copy.wait()
    for buf, out, s in ((pred, pred_out, 0), (sens, sens_out, 1)):
        for copy in out_copies(buf, out, s):
            copy.wait()
    own.wait_send()

    def drain(i, carry):
        for copy in z_copies(i) + column_copies(i) + [corner_copy(i), core_copy(i)]:
            copy.wait_send()
        for copy in [to_core(i), *to_far(i), to_near(i), *to_z(i)]:
            copy.wait_send()
        return carry

    lax.fori_loop(0, count, drain, 0)


def train_call(plane, segments, extents, adjoint, first, square, head, biases):
    ZN, YN, XN = plane
    past, span, hidden = segments.shape[1], adjoint.shape[0], square.shape[3]
    windows = segments.shape[0] // 2
    tile = windows
    half = hidden // (ZN * YN * XN) // 2
    sizes = (ZN, YN, XN, windows, tile, past, span, hidden)
    DMA = pltpu.SemaphoreType.DMA
    vmem = pl.BlockSpec(memory_space=pltpu.VMEM)
    hbm = pl.BlockSpec(memory_space=pl.ANY)
    count = 2 * MATS
    flops = 2 * 2 * 3 * windows * hidden * (6 * hidden + 2 * 128)
    return pl.pallas_call(
        functools.partial(train_kernel, sizes),
        out_shape=(
            jax.ShapeDtypeStruct((span, 1, 2 * windows), F32),
            jax.ShapeDtypeStruct((past, 1, 2 * windows), F32),
            jax.ShapeDtypeStruct((MATS, 2, half, hidden), F32),
            jax.ShapeDtypeStruct((8, 128), F32),
        ),
        in_specs=[hbm, hbm] + [vmem] * 5,
        out_specs=(hbm, hbm, vmem, vmem),
        scratch_shapes=[
            pltpu.VMEM((2, MATS, ZN, YN, XN, 2, half, hidden), BF),
            pltpu.VMEM((MATS, half, hidden), BF),
            pltpu.VMEM((2, MATS, ZN, YN, XN, 2, half, hidden), BF),
            pltpu.VMEM((2, ZN, YN, XN, half, hidden), BF),
            pltpu.VMEM((2, MATS, ZN, half, hidden), BF),
            pltpu.VMEM((2, MATS, ZN, half, hidden), BF),
            pltpu.VMEM((2, MATS, ZN, half, hidden), BF),
            pltpu.VMEM((2, MATS, ZN - 1, half, hidden), BF),
            pltpu.VMEM((2, MATS, half, hidden), F32),
            pltpu.VMEM((2, 4, hidden, windows), BF),
            pltpu.VMEM((2, 128, windows), BF),
            pltpu.VMEM((2, hidden, windows), BF),
            pltpu.VMEM((2, hidden, 128), F32),
            pltpu.VMEM((2, 4, windows, hidden), BF),
            pltpu.VMEM((3, windows, hidden), BF),
            pltpu.VMEM((windows, 128), F32),
            pltpu.VMEM((windows, 128), F32),
            pltpu.VMEM((windows, 128), BF),
            pltpu.VMEM((windows, 128), BF),
            pltpu.VMEM((8, 128), F32),
            pltpu.VMEM((128, hidden), F32),
            pltpu.VMEM((128, hidden), F32),
            pltpu.VMEM((128, 128), F32),
            pltpu.VMEM((windows, past), F32),
            pltpu.VMEM((span, windows), F32),
            pltpu.VMEM((2, span, windows), F32),
            pltpu.VMEM((2, past, windows), F32),
            pltpu.VMEM((half, hidden), F32),
            pltpu.VMEM((7 + ZN, 8, 128), F32),
            DMA((1,)),
            DMA((1,)),
            DMA((count, 7)),
            DMA((count, 7)),
            DMA((count, 4 + ZN - 1)),
            DMA((count, 4 + ZN - 1)),
            DMA((3,)),
            DMA((3,)),
            DMA((4,)),
            DMA((3 + ZN - 1,)),
            DMA((3 + ZN - 1,)),
        ],
        compiler_params=pltpu.CompilerParams(
            collective_id=0, has_side_effects=True, vmem_limit_bytes=64 * 1024 * 1024
        ),
        cost_estimate=pl.CostEstimate(flops=flops, bytes_accessed=8_000_000, transcendentals=8 * windows * hidden),
        name="train",
    )(segments, adjoint, extents.reshape(-1, 128), first, square, head, biases)


def update_kernel(past, span, prediction, sensitivity, grads, norm, *refs):
    masters, momenta, variances, outs = refs[0:4], refs[4:8], refs[8:12], refs[12:28]
    norm_out, prediction_out, sensitivity_out, pad, sems = refs[28:]
    passed = [
        pltpu.make_async_copy(prediction, prediction_out, sems.at[0]),
        pltpu.make_async_copy(sensitivity, sensitivity_out, sems.at[1]),
    ]
    for copy in passed:
        copy.start()
    norm_out[...] = norm[0:1, 0:1]
    factor = 1.0 / jnp.maximum(norm[0:1, 0:1], 1.0)
    units = masters[3].shape[2]

    def rows(m, lane, width):
        return grads[m, :, :, lane : lane + width].reshape(units, width)

    forecast = rows(0, 128, 128)
    pad[...] = jnp.zeros_like(pad)
    outs[0][0] = rows(0, 0, 128)[:, 0:past]
    pad[0:units, :] = forecast
    outs[3][0] = pad[...].T[span : span + 4, 0:units]
    for m in range(5):
        outs[1][0, m] = rows(m + 1, 0, grads.shape[3])
    outs[2][0, :, 0:past] = rows(0, 256, 128)[:, 0:past]
    outs[2][0, :, past : past + span] = forecast[:, 0:span]
    for n in range(4):
        master, gradient = masters[n][...], outs[n][...]
        new, moment, spread = adamw(master, gradient, momenta[n][...], variances[n][...], factor[None])
        outs[4 + n][...], outs[8 + n][...], outs[12 + n][...] = new, moment, spread
    for copy in passed:
        copy.wait()


def update_call(prediction, sensitivity, grads, norm, state):
    vmem, hbm = pl.BlockSpec(memory_space=pltpu.VMEM), pl.BlockSpec(memory_space=pl.ANY)
    shapes = tuple(jax.ShapeDtypeStruct(a.shape, F32) for a in state[:4])
    passed = tuple(jax.ShapeDtypeStruct(a.shape, F32) for a in (prediction, sensitivity))
    return pl.pallas_call(
        functools.partial(update_kernel, sensitivity.shape[0], prediction.shape[0]),
        out_shape=4 * shapes + (jax.ShapeDtypeStruct((1, 1), F32),) + passed,
        in_specs=[hbm, hbm] + [vmem] * (2 + len(state)),
        out_specs=tuple([vmem] * 17 + [hbm, hbm]),
        scratch_shapes=[pltpu.VMEM((128, 128), F32), pltpu.SemaphoreType.DMA((2,))],
        name="update",
    )(prediction, sensitivity, grads, norm, *state)


def turned(arrays):
    return [a.transpose(0, 2, 1) if n % 4 == 0 else a for n, a in enumerate(arrays)]


def kernel_shards(plane, segments, extents, adjoint, *state):
    state = turned(state)
    results = train_call(plane, segments, extents, adjoint.T, *state[:4])
    *updated, norm, prediction, sensitivity = update_call(*results, state)
    by_window = (prediction.transpose(1, 2, 0), sensitivity.transpose(1, 2, 0))
    return (*by_window, norm.reshape(()), *turned(updated))


STATE_SPECS = (
    P("section", None, "dp"),
    P("section", None, "dp", None),
    P("section", "dp", None),
    P("section", None, "dp"),
)


def solution(mesh):
    in_specs = (P("dp", None), P("dp"), P("dp", None)) + 3 * STATE_SPECS
    out_specs = (P("section", "dp", None), P("section", "dp", None), P()) + 4 * STATE_SPECS
    plane = PLANES.get(mesh.shape["dp"])
    shards = plain_shards if plane is None else functools.partial(kernel_shards, plane)
    return jax.shard_map(shards, mesh=mesh, in_specs=in_specs, out_specs=out_specs, check_vma=False)
```

```python
import functools

import jax
import jax.numpy as jnp
from jax import lax
from jax.experimental import pallas as pl
from jax.experimental.pallas import tpu as pltpu
from jax.sharding import PartitionSpec as P

STEP = 10


def dot_nn(a, b):
    return jnp.dot(a, b, preferred_element_type=jnp.float32)


def dot_tn(a, b):
    return lax.dot_general(a, b, (((0,), (0,)), ((), ())), preferred_element_type=jnp.float32)


def dot_nt(a, b):
    return lax.dot_general(a, b, (((1,), (1,)), ((), ())), preferred_element_type=jnp.float32)


def unit_rows(first, square, head, biases):
    units = first.shape[1]
    return jnp.concatenate(
        [square.transpose(1, 0, 2).reshape(units, -1), first.T, head, biases.T], axis=1
    )


def from_unit_rows(rows, past, hidden, out):
    wide = 5 * hidden
    square = rows[:, :wide].reshape(-1, 5, hidden).transpose(1, 0, 2)
    first = rows[:, wide : wide + past].T
    head = rows[:, wide + past : wide + past + out]
    biases = rows[:, wide + past + out :].T
    return first, square, head, biases


def plain_forward(weights, resid):
    first, square, head, biases = weights
    past = resid.shape[1]
    acts, slopes = [resid.astype(jnp.bfloat16)], []
    for k in range(4):
        z = dot_nn(acts[-1], first if k == 0 else square[k - 1]) + biases[k].astype(jnp.float32)
        sig = jax.nn.sigmoid(z)
        acts.append((z * sig).astype(jnp.bfloat16))
        slopes.append(sig * (1.0 + z * (1.0 - sig)))
    theta_b = dot_nn(acts[4], square[3]).astype(jnp.bfloat16)
    theta_f = dot_nn(acts[4], square[4]).astype(jnp.bfloat16)
    backcast = dot_nn(theta_b, head[:, :past])
    part = dot_nn(theta_f, head[:, past:])
    return backcast, part, (acts, slopes, theta_b, theta_f)


def plain_backward(weights, saved, e, f):
    first, square, head, biases = weights
    acts, slopes, theta_b, theta_f = saved
    past = e.shape[1]
    head_grad = jnp.concatenate([dot_tn(theta_b, e), dot_tn(theta_f, f)], axis=1)
    u_b = dot_nt(e, head[:, :past]).astype(jnp.bfloat16)
    u_f = dot_nt(f, head[:, past:]).astype(jnp.bfloat16)
    squares = [None, None, None, dot_tn(acts[4], u_b), dot_tn(acts[4], u_f)]
    da = dot_nt(u_b, square[3]) + dot_nt(u_f, square[4])
    bias_grads = [None] * 4
    first_grad = None
    for k in (3, 2, 1, 0):
        dz = (da * slopes[k]).astype(jnp.bfloat16)
        bias_grads[k] = jnp.sum(dz, axis=0, dtype=jnp.float32)
        grad = dot_tn(acts[k], dz)
        if k == 0:
            first_grad = grad
        else:
            squares[k - 1] = grad
        da = dot_nt(dz, first if k == 0 else square[k - 1])
    return da, (first_grad, jnp.stack(squares), head_grad, jnp.stack(bias_grads))


def adamw(master, gradient, momentum, variance, factor):
    clipped = gradient * factor
    moment_new = 0.9 * momentum + 0.1 * clipped
    variance_new = 0.999 * variance + 0.001 * clipped * clipped
    ratio = moment_new / (1.0 - 0.9**STEP) / (jnp.sqrt(variance_new / (1.0 - 0.999**STEP)) + 1e-08)
    return master - 0.05 * (ratio + 0.01 * master), moment_new, variance_new


def plain_shards(segments, extents, adjoint, *state):
    masters, momenta, variances = state[:4], state[4:8], state[8:]
    core = lax.axis_index("section")
    past, span = segments.shape[1], adjoint.shape[1]
    windows = segments.shape[0] // 2
    hidden = masters[1].shape[3]
    mine = [
        lax.dynamic_slice_in_dim(v, core * windows, windows, 0) for v in (segments, extents, adjoint)
    ]
    seg, ext, adj = mine
    rows = unit_rows(*(m[0].astype(jnp.bfloat16) for m in masters))
    rows = lax.all_gather(rows, "dp", axis=0, tiled=True)
    rows = lax.all_gather(rows, "section", axis=0)
    blocks = [from_unit_rows(rows[b], past, hidden, past + span) for b in range(2)]
    mask = (
        lax.broadcasted_iota(jnp.int32, (windows, past), 1) >= past - ext[:, None]
    ).astype(jnp.float32)
    r0 = seg * mask
    backcast, part0, saved0 = plain_forward(blocks[0], r0)
    r1 = (r0 - backcast) * mask
    _, part1, saved1 = plain_forward(blocks[1], r1)
    forecast = part0.astype(jnp.bfloat16).astype(jnp.float32) + part1
    f = adj.astype(jnp.bfloat16)
    zero = jnp.zeros_like(r0)
    da1, grads1 = plain_backward(blocks[1], saved1, (-(zero * mask)).astype(jnp.bfloat16), f)
    dr1 = zero * mask + da1
    t = dr1.astype(jnp.bfloat16).astype(jnp.float32)
    da0, grads0 = plain_backward(blocks[0], saved0, (-(t * mask)).astype(jnp.bfloat16), f)
    dr0 = (t * mask + da0) * mask

    def by_section(first_block, second_block):
        mine, other = (
            jnp.where(core == 0, first_block, second_block),
            jnp.where(core == 0, second_block, first_block),
        )
        got = lax.ppermute(other, "section", [(0, 1), (1, 0)])
        return jnp.where(
            core == 0, jnp.concatenate([mine, got]), jnp.concatenate([got, mine])
        )[None]

    prediction = by_section(part0, forecast)
    sensitivity = by_section(dr0, dr1)
    packed = jnp.stack([unit_rows(*grads0), unit_rows(*grads1)])
    packed = lax.psum_scatter(packed, "section", scatter_dimension=0, tiled=False)
    packed = lax.psum_scatter(packed, "dp", scatter_dimension=0, tiled=True)
    norm = jnp.sqrt(lax.psum(jnp.sum(packed * packed), ("section", "dp")))
    factor = 1.0 / jnp.maximum(norm, 1.0)
    summed = [g[None] for g in from_unit_rows(packed, past, hidden, past + span)]
    updated = [adamw(*four, factor) for four in zip(masters, summed, momenta, variances)]
    return (
        prediction,
        sensitivity,
        norm,
        *summed,
        *(u[0] for u in updated),
        *(u[1] for u in updated),
        *(u[2] for u in updated),
    )


PLANES = {16: (4, 2, 2)}
MESH = pl.DeviceIdType.MESH
MATS = 6
BF, F32 = jnp.bfloat16, jnp.float32


def remote(src, dst, send_sem, recv_sem, device):
    return pltpu.make_async_remote_copy(
        src_ref=src, dst_ref=dst, send_sem=send_sem, recv_sem=recv_sem, device_id=device, device_id_type=MESH
    )


def train_kernel(
    sizes,
    seg_hbm, adj_hbm, ext, first, square, head, biases,
    pred_out, sens_out, grad_out, norm_out,
    wg, handed, gp, from_core, from_diag, from_plain, from_pair, from_z, total,
    act_t, in_t, theta_t, forecast_grad, slope, work, resid, mask, f_ref, e_ref, t_ref, bias_t, bias_sum, pad,
    seg, adj, first_part, pred, sens, squares, norm_buf,
    own_send, own_recv, ag_send, ag_recv, rs_send, rs_recv, out_send, out_recv, local_sem, norm_send, norm_recv,
):
    ZN, YN, XN, windows, tile, past, span, hidden = sizes
    units = ZN * YN * XN
    core, dp = lax.axis_index("section"), lax.axis_index("dp")
    x, y, z = lax.rem(dp, XN), lax.rem(lax.div(dp, XN), YN), lax.div(dp, XN * YN)
    other, xo, yo = 1 - core, 1 - x, 1 - y
    near_y, near_x = y + core * (yo - y), xo + core * (x - xo)
    far_y, far_x = yo + core * (y - yo), x + core * (xo - x)

    def chip(zi, yi, xi):
        return (core, (zi * YN + yi) * XN + xi)

    sibling = (other, dp)
    z_peers = [lax.rem(z + step, ZN) for step in range(1, ZN)]

    row0 = core * windows
    loads = [
        pltpu.make_async_copy(seg_hbm.at[pl.ds(row0, windows), :], seg, local_sem.at[0]),
        pltpu.make_async_copy(adj_hbm.at[:, pl.ds(row0, windows)], adj, local_sem.at[1]),
    ]
    for load in loads:
        load.start()

    barrier = pltpu.get_barrier_semaphore()
    peers = [sibling, chip(z, y, xo), chip(z, yo, x)] + [chip(zi, y, x) for zi in z_peers]
    for peer in peers:
        pl.semaphore_signal(barrier, inc=1, device_id=peer, device_id_type=MESH)

    rows = hidden // units
    half_rows = rows // 2

    def put_own(m, value, lanes):
        halves = value.astype(BF).reshape(2, half_rows, -1)
        for h in range(2):
            pl.when(core == h)(functools.partial(put_half, m, halves[h], halves[1 - h], lanes))

    def put_half(m, kept, given, lanes):
        wg[core, m, z, y, x, core, :, lanes] = kept
        handed[m, :, lanes] = given

    pad[...] = jnp.zeros_like(pad)
    pad[0:rows, 0:past] = first[0] * 0.5
    put_own(0, pad[0:rows, :], slice(0, 128))
    pad[...] = jnp.zeros_like(pad)
    pad[span : span + 4, 0:rows] = biases[0] * 0.5
    bias_cols = pad[...].T[0:rows]
    pad[...] = jnp.zeros_like(pad)
    pad[0:rows, 0:span] = head[0, :, past : past + span]
    put_own(0, pad[0:rows, :] + bias_cols, slice(128, 256))
    pad[...] = jnp.zeros_like(pad)
    pad[0:rows, 0:past] = head[0, :, 0:past]
    put_own(0, pad[0:rows, :], slice(256, 384))
    put_own(0, jnp.zeros((rows, 128), F32), slice(384, 512))
    for m in range(5):
        put_own(m + 1, square[0, m] * 0.5 if m < 3 else square[0, m], slice(0, hidden))
    pl.semaphore_wait(barrier, len(peers))

    own = remote(handed, wg.at[core, :, z, y, x, other], own_send.at[0], own_recv.at[0], sibling)
    own.start()

    def of(i):
        return lax.div(i, MATS), lax.rem(i, MATS)

    def z_copies(i):
        b, m = of(i)
        part = wg.at[b, m, z, y, x, core]
        return [
            remote(part, part, ag_send.at[i, s], ag_recv.at[i, s], chip(zi, y, x)) for s, zi in enumerate(z_peers)
        ]

    def column_copies(i):
        b, m = of(i)
        part = wg.at[b, m, :, y, x, core]
        return [
            remote(part, part, ag_send.at[i, 3], ag_recv.at[i, 3], chip(z, near_y, near_x)),
            remote(part, part, ag_send.at[i, 4], ag_recv.at[i, 4], chip(z, far_y, far_x)),
        ]

    def corner_copy(i):
        b, m = of(i)
        part = wg.at[b, m, :, near_y, near_x, core]
        return remote(part, part, ag_send.at[i, 5], ag_recv.at[i, 5], chip(z, far_y, far_x))

    def core_copy(i):
        b, m = of(i)
        part = wg.at[b, m, :, :, :, core]
        return remote(part, part, ag_send.at[i, 6], ag_recv.at[i, 6], sibling)

    def start_all(copies):
        for copy in copies:
            copy.start()

    for load in loads:
        load.wait()
    zeros_tile = jnp.zeros((tile, 128), F32)

    def prepare(t, carry):
        at = pl.ds(t * tile, tile)
        resid[at, :] = zeros_tile
        resid[at, 0:past] = seg[at, :]
        return carry

    def prepare_mask(g, carry):
        lengths = ext[pl.ds(core * (windows // 128) + g, 1), :]
        position = lax.broadcasted_iota(jnp.int32, (128, 128), 0)
        keep = jnp.where(position >= past - lengths, 1.0, 0.0).astype(F32).T
        at = pl.ds(pl.multiple_of(g * 128, 128), 128)
        pad[0:span, :] = adj[:, at]
        f_ref[at, :] = pad[...].T.astype(BF)
        mask[at, :] = keep
        resid[at, :] = resid[at, :] * keep
        return carry

    tiles = windows // tile

    def matrix(b, m):
        return wg[b, m].reshape(hidden, hidden)

    def small(b, lane):
        return wg[b, 0, :, :, :, :, :, lane : lane + 128].reshape(hidden, 128)

    def store_layer(b, k, at, v, scale):
        p = 1.0 + jnp.tanh(v)
        a = v * p
        rate = p + a * (2.0 - p)
        slope[b, k, at, :] = (rate if scale is None else rate * scale).astype(BF)
        low = a.astype(BF)
        act_t[b, k, :, at] = low.T
        return low

    def layer_zero(b):
        bias_t[...] = small(b, 128).astype(F32).T

        def body(t, carry):
            at = pl.ds(pl.multiple_of(t * tile, tile), tile)
            a = resid[at, :].astype(BF)
            in_t[b, :, at] = a.T
            v = dot_nt(a, small(b, 0)) + bias_t[span : span + 1, :]
            work[0, at, :] = store_layer(b, 0, at, v, None)
            return carry

        lax.fori_loop(0, tiles, body, 0)

    def layer_next(b, k):
        source, target = lax.rem(k + 1, 2), lax.rem(k, 2)
        bias = bias_t[pl.ds(span + k, 1), :]
        scale = jnp.where(k == 3, 0.5, 1.0)

        def body(t, carry):
            at = pl.ds(pl.multiple_of(t * tile, tile), tile)
            v = dot_nn(work[source, at, :], matrix(b, k)) + bias
            work[target, at, :] = store_layer(b, k, at, v, scale)
            return carry

        lax.fori_loop(0, tiles, body, 0)

    def grid(value):
        return value.astype(BF).reshape(ZN, YN, XN, 2, half_rows, -1)

    def backcast_grad(b):
        gp[b, 0, :, :, :, :, :, 256:384] = grid(dot_nn(theta_t[b], e_ref[...]))

    def backcast_step(b):
        def body(t, carry):
            at = pl.ds(pl.multiple_of(t * tile, tile), tile)
            theta = dot_nn(work[1, at, :], matrix(b, 4)).astype(BF)
            theta_t[b, :, at] = theta.T

            @pl.when(b == 0)
            def _():
                backcast = dot_nn(theta, small(b, 256))
                resid[at, :] = (resid[at, :] - backcast) * mask[at, :]

            @pl.when(b == 1)
            def _():
                e_ref[at, :] = (-(jnp.zeros((tile, 128), F32) * mask[at, :])).astype(BF)

            return carry

        lax.fori_loop(0, tiles, body, 0)
        pl.when(b == 1)(lambda: backcast_grad(b))

    def put_rows(buf, b, at, value):
        for row in range(value.shape[0]):
            buf[b, row, :, at] = value[row : row + 1]

    def forecast_step(b):
        def body(t, carry):
            at = pl.ds(pl.multiple_of(t * tile, tile), tile)
            theta = dot_nn(work[1, at, :], matrix(b, 5)).astype(BF)
            theta_t[1, :, at] = theta.T
            part = dot_nn(theta, small(b, 128)).T[0:span]

            @pl.when(b == 0)
            def _():
                first_part[:, at] = part
                put_rows(pred, 0, at, part)

            @pl.when(b == 1)
            def _():
                put_rows(pred, 1, at, first_part[:, at].astype(BF).astype(F32) + part)

            return carry

        lax.fori_loop(0, tiles, body, 0)
        forecast_grad[b] = dot_nn(theta_t[1], f_ref[...])

    own.wait_recv()
    for i in range(3):
        start_all(z_copies(i))
    lax.fori_loop(0, tiles, prepare, 0)
    pad[...] = jnp.zeros_like(pad)
    lax.fori_loop(0, windows // 128, prepare_mask, 0)

    count = 2 * MATS

    def gather_step(i, carry):
        @pl.when(i + 3 < count)
        def _():
            start_all(z_copies(i + 3))

        @pl.when(i < count)
        def _():
            for copy in z_copies(i):
                copy.wait_recv()
            start_all(column_copies(i))

        @pl.when(jnp.logical_and(i >= 1, i < count + 1))
        def _():
            column_copies(i - 1)[0].wait_recv()
            corner_copy(i - 1).start()

        @pl.when(jnp.logical_and(i >= 2, i < count + 2))
        def _():
            column_copies(i - 2)[1].wait_recv()
            corner_copy(i - 2).wait_recv()
            core_copy(i - 2).start()

        @pl.when(i >= 3)
        def _():
            core_copy(i - 3).wait_recv()
            b, m = of(i - 3)
            pl.when(m == 0)(lambda: layer_zero(b))
            pl.when(jnp.logical_and(m >= 1, m <= 3))(lambda: layer_next(b, m))
            pl.when(m == 4)(lambda: backcast_step(b))
            pl.when(m == 5)(lambda: forecast_step(b))

        return carry

    lax.fori_loop(0, count + 3, gather_step, 0)

    def out_copies(buf, out, s):
        at = pl.ds(row0, windows)
        return [
            pltpu.make_async_copy(buf.at[core], out.at[:, :, at], local_sem.at[2 + s]),
            remote(buf.at[other], out.at[:, :, at], out_send.at[s], out_recv.at[s], sibling),
        ]

    start_all(out_copies(pred, pred_out, 0))

    def back_of(j):
        s = lax.rem(j, MATS)
        return 1 - lax.div(j, MATS), jnp.where(s == 0, 4, jnp.where(s == 1, 5, 5 - s))

    def to_core(j):
        b, m = back_of(j)
        return remote(
            gp.at[b, m, :, :, :, other], from_core.at[lax.rem(j, 2)], rs_send.at[j, 0], rs_recv.at[j, 0], sibling
        )

    def to_far(j):
        b, m = back_of(j)
        device = chip(z, far_y, far_x)
        return [
            remote(gp.at[b, m, :, yo, xo, core], from_diag.at[b, m], rs_send.at[j, 1], rs_recv.at[j, 1], device),
            remote(gp.at[b, m, :, far_y, far_x, core], from_plain.at[b, m], rs_send.at[j, 2], rs_recv.at[j, 2], device),
        ]

    def to_near(j):
        b, m = back_of(j)
        return remote(
            gp.at[b, m, :, near_y, near_x, core], from_pair.at[b, m], rs_send.at[j, 3], rs_recv.at[j, 3],
            chip(z, near_y, near_x),
        )

    def to_z(j):
        b, m = back_of(j)
        return [
            remote(gp.at[b, m, zi, y, x, core], from_z.at[b, m, s], rs_send.at[j, 4 + s], rs_recv.at[j, 4 + s], chip(zi, y, x))
            for s, zi in enumerate(z_peers)
        ]

    def scatter_core(j):
        b, m = back_of(j)
        to_core(j).wait_recv()
        gp[b, m, :, :, :, core] = gp[b, m, :, :, :, core] + from_core[lax.rem(j, 2)]
        start_all(to_far(j))

    def scatter_diag(j):
        b, m = back_of(j)
        to_far(j)[0].wait_recv()
        gp[b, m, :, near_y, near_x, core] = gp[b, m, :, near_y, near_x, core] + from_diag[b, m]
        to_near(j).start()

    def scatter_plane(j):
        b, m = back_of(j)
        to_far(j)[1].wait_recv()
        to_near(j).wait_recv()
        value = gp[b, m, :, y, x, core].astype(F32) + from_plain[b, m].astype(F32) + from_pair[b, m].astype(F32)
        gp[b, m, :, y, x, core] = value.astype(BF)
        start_all(to_z(j))

    def scatter_z(j):
        b, m = back_of(j)
        for copy in to_z(j):
            copy.wait_recv()
        value = gp[b, m, z, y, x, core].astype(F32)
        for s in range(ZN - 1):
            value = value + from_z[b, m, s].astype(F32)
        total[b, m] = value
        squares[...] = squares[...] + value * value

    def guarded(low, j, step):
        pl.when(jnp.logical_and(j >= low, j < count + low))(lambda: step(j - low))

    def dz_slot(k):
        return lax.rem(5 - k, 3)

    def add_rows(value):
        return jnp.sum(value.reshape(-1, 8, hidden), axis=0)

    def put_bias(k, acc):
        bias_sum[pl.ds(span + k, 1), :] = jnp.sum(acc, axis=0, keepdims=True)

    def head_step(b):
        def body(t, carry):
            at = pl.ds(pl.multiple_of(t * tile, tile), tile)

            @pl.when(b == 1)
            def _():
                resid[at, :] = jnp.zeros((tile, 128), F32)

            e = (-(resid[at, :] * mask[at, :])).astype(BF)
            e_ref[at, :] = e
            work[0, at, :] = dot_nt(e, small(b, 256)).astype(BF)
            work[1, at, :] = dot_nt(f_ref[at, :], small(b, 128)).astype(BF)
            return carry

        lax.fori_loop(0, tiles, body, 0)

    def theta_step(b):
        def body(t, acc):
            at = pl.ds(pl.multiple_of(t * tile, tile), tile)
            da = dot_nt(work[0, at, :], matrix(b, 4)) + dot_nt(work[1, at, :], matrix(b, 5))
            dz = da * slope[b, 3, at, :].astype(F32)
            work[2, at, :] = dz.astype(BF)
            return acc + add_rows(dz)

        put_bias(3, lax.fori_loop(0, tiles, body, jnp.zeros((8, hidden), F32)))

    def layer_back(b, k):
        source, target = dz_slot(k + 1), dz_slot(k)

        def body(t, acc):
            at = pl.ds(pl.multiple_of(t * tile, tile), tile)
            dz = dot_nt(work[source, at, :], matrix(b, k + 1)) * slope[b, k, at, :].astype(F32)
            work[target, at, :] = dz.astype(BF)
            return acc + add_rows(dz)

        put_bias(k, lax.fori_loop(0, tiles, body, jnp.zeros((8, hidden), F32)))

    def weight_grad(b, j):
        s = lax.rem(j, MATS)
        layer = jnp.where(s <= 1, 3, 4 - s)
        slot = jnp.where(s <= 1, s, dz_slot(5 - s))
        _, m = back_of(j)
        gp[b, m] = grid(dot_nn(act_t[b, layer], work[slot]))

    def small_grads(b):
        gp[b, 0, :, :, :, :, :, 0:128] = grid(dot_nn(in_t[b], work[2]).T)
        forecast = forecast_grad[b] + bias_sum[...].T
        gp[b, 0, :, :, :, :, :, 128:256] = grid(forecast)
        pl.when(b == 0)(lambda: backcast_grad(b))
        gp[b, 0, :, :, :, :, :, 384:512] = jnp.zeros((ZN, YN, XN, 2, half_rows, 128), BF)

    def input_grad(b):
        def body(t, carry):
            at = pl.ds(pl.multiple_of(t * tile, tile), tile)
            keep = mask[at, :]
            dr = resid[at, :] * keep + 2.0 * dot_nn(work[2, at, :], small(b, 0))

            @pl.when(b == 1)
            def _():
                put_rows(sens, 1, at, dr.T[0:past])
                resid[at, :] = dr.astype(BF).astype(F32)

            @pl.when(b == 0)
            def _():
                put_rows(sens, 0, at, (dr * keep).T[0:past])

            return carry

        lax.fori_loop(0, tiles, body, 0)

    bias_sum[...] = jnp.zeros_like(bias_sum)
    squares[...] = jnp.zeros_like(squares)

    def back_step(j, carry):
        s = lax.rem(j, MATS)
        b, _ = back_of(j)
        live = j < count

        def on(test, step):
            pl.when(jnp.logical_and(live, test))(step)

        on(s == 0, lambda: head_step(b))
        on(s == 2, lambda: theta_step(b))
        on(s >= 3, lambda: layer_back(b, 5 - s))
        guarded(4, j, scatter_z)
        guarded(3, j, scatter_plane)
        guarded(2, j, scatter_diag)
        guarded(1, j, scatter_core)
        on(s <= 4, lambda: weight_grad(b, j))
        on(s == 5, lambda: small_grads(b))
        pl.when(live)(lambda: to_core(j).start())
        on(s == 5, lambda: input_grad(b))
        pl.when(j == count - 1)(lambda: start_all(out_copies(sens, sens_out, 1)))
        return carry

    lax.fori_loop(0, count + 4, back_step, 0)

    grad_copy = remote(total.at[other], grad_out.at[:, core], out_send.at[2], out_recv.at[2], sibling)
    grad_copy.start()
    grad_out[:, core] = total[core]
    sq = squares[:, 0:128] + squares[:, 128:256] + squares[:, 256:384] + squares[:, 384:512]
    norm_buf[0] = sq[0:8] + sq[8:16]
    for step, device in enumerate([sibling, chip(z, y, xo), chip(z, yo, x)]):
        copy = remote(norm_buf.at[2 * step], norm_buf.at[2 * step + 1], norm_send.at[step], norm_recv.at[step], device)
        copy.start()
        copy.wait()
        norm_buf[2 * step + 2] = norm_buf[2 * step] + norm_buf[2 * step + 1]
    norm_buf[7 + z] = norm_buf[6]
    spread = [
        remote(norm_buf.at[6], norm_buf.at[7 + z], norm_send.at[3 + s], norm_recv.at[3 + s], chip(zi, y, x))
        for s, zi in enumerate(z_peers)
    ]
    start_all(spread)
    for copy in spread:
        copy.wait()
    everything = norm_buf[7]
    for zi in range(1, ZN):
        everything = everything + norm_buf[7 + zi]
    norm_out[...] = jnp.broadcast_to(jnp.sqrt(jnp.sum(everything, keepdims=True)), norm_out.shape)

    grad_copy.wait()
    for buf, out, s in ((pred, pred_out, 0), (sens, sens_out, 1)):
        for copy in out_copies(buf, out, s):
            copy.wait()
    own.wait_send()

    def drain(i, carry):
        for copy in z_copies(i) + column_copies(i) + [corner_copy(i), core_copy(i)]:
            copy.wait_send()
        for copy in [to_core(i), *to_far(i), to_near(i), *to_z(i)]:
            copy.wait_send()
        return carry

    lax.fori_loop(0, count, drain, 0)


def train_call(plane, segments, extents, adjoint, first, square, head, biases):
    ZN, YN, XN = plane
    past, span, hidden = segments.shape[1], adjoint.shape[0], square.shape[3]
    windows = segments.shape[0] // 2
    tile = windows
    half = hidden // (ZN * YN * XN) // 2
    sizes = (ZN, YN, XN, windows, tile, past, span, hidden)
    DMA = pltpu.SemaphoreType.DMA
    vmem = pl.BlockSpec(memory_space=pltpu.VMEM)
    hbm = pl.BlockSpec(memory_space=pl.ANY)
    count = 2 * MATS
    flops = 2 * 2 * 3 * windows * hidden * (6 * hidden + 2 * 128)
    return pl.pallas_call(
        functools.partial(train_kernel, sizes),
        out_shape=(
            jax.ShapeDtypeStruct((span, 1, 2 * windows), F32),
            jax.ShapeDtypeStruct((past, 1, 2 * windows), F32),
            jax.ShapeDtypeStruct((MATS, 2, half, hidden), F32),
            jax.ShapeDtypeStruct((8, 128), F32),
        ),
        in_specs=[hbm, hbm] + [vmem] * 5,
        out_specs=(hbm, hbm, vmem, vmem),
        scratch_shapes=[
            pltpu.VMEM((2, MATS, ZN, YN, XN, 2, half, hidden), BF),
            pltpu.VMEM((MATS, half, hidden), BF),
            pltpu.VMEM((2, MATS, ZN, YN, XN, 2, half, hidden), BF),
            pltpu.VMEM((2, ZN, YN, XN, half, hidden), BF),
            pltpu.VMEM((2, MATS, ZN, half, hidden), BF),
            pltpu.VMEM((2, MATS, ZN, half, hidden), BF),
            pltpu.VMEM((2, MATS, ZN, half, hidden), BF),
            pltpu.VMEM((2, MATS, ZN - 1, half, hidden), BF),
            pltpu.VMEM((2, MATS, half, hidden), F32),
            pltpu.VMEM((2, 4, hidden, windows), BF),
            pltpu.VMEM((2, 128, windows), BF),
            pltpu.VMEM((2, hidden, windows), BF),
            pltpu.VMEM((2, hidden, 128), F32),
            pltpu.VMEM((2, 4, windows, hidden), BF),
            pltpu.VMEM((3, windows, hidden), BF),
            pltpu.VMEM((windows, 128), F32),
            pltpu.VMEM((windows, 128), F32),
            pltpu.VMEM((windows, 128), BF),
            pltpu.VMEM((windows, 128), BF),
            pltpu.VMEM((8, 128), F32),
            pltpu.VMEM((128, hidden), F32),
            pltpu.VMEM((128, hidden), F32),
            pltpu.VMEM((128, 128), F32),
            pltpu.VMEM((windows, past), F32),
            pltpu.VMEM((span, windows), F32),
            pltpu.VMEM((span, windows), F32),
            pltpu.VMEM((2, span, 1, windows), F32),
            pltpu.VMEM((2, past, 1, windows), F32),
            pltpu.VMEM((half, hidden), F32),
            pltpu.VMEM((7 + ZN, 8, 128), F32),
            DMA((1,)),
            DMA((1,)),
            DMA((count, 7)),
            DMA((count, 7)),
            DMA((count, 4 + ZN - 1)),
            DMA((count, 4 + ZN - 1)),
            DMA((3,)),
            DMA((3,)),
            DMA((4,)),
            DMA((3 + ZN - 1,)),
            DMA((3 + ZN - 1,)),
        ],
        compiler_params=pltpu.CompilerParams(
            collective_id=0, has_side_effects=True, vmem_limit_bytes=64 * 1024 * 1024
        ),
        cost_estimate=pl.CostEstimate(flops=flops, bytes_accessed=8_000_000, transcendentals=8 * windows * hidden),
        name="train",
    )(segments, adjoint, extents.reshape(-1, 128), first, square, head, biases)


def update_kernel(past, span, prediction, sensitivity, grads, norm, *refs):
    masters, momenta, variances, outs = refs[0:4], refs[4:8], refs[8:12], refs[12:28]
    norm_out, prediction_out, sensitivity_out, pad, prediction_held, sensitivity_held, sems = refs[28:]
    arriving = [
        pltpu.make_async_copy(sensitivity, sensitivity_held, sems.at[0]),
        pltpu.make_async_copy(prediction, prediction_held, sems.at[1]),
    ]
    leaving = [
        pltpu.make_async_copy(sensitivity_held, sensitivity_out, sems.at[2]),
        pltpu.make_async_copy(prediction_held, prediction_out, sems.at[3]),
    ]
    for copy in arriving:
        copy.start()
    norm_out[...] = norm[0:1, 0:1]
    factor = 1.0 / jnp.maximum(norm[0:1, 0:1], 1.0)
    units = masters[3].shape[2]

    def rows(m, lane, width):
        return grads[m, :, :, lane : lane + width].reshape(units, width)

    forecast = rows(0, 128, 128)
    pad[...] = jnp.zeros_like(pad)
    outs[0][0] = rows(0, 0, 128)[:, 0:past]
    pad[0:units, :] = forecast
    outs[3][0] = pad[...].T[span : span + 4, 0:units]
    for m in range(5):
        outs[1][0, m] = rows(m + 1, 0, grads.shape[3])
    outs[2][0, :, 0:past] = rows(0, 256, 128)[:, 0:past]
    outs[2][0, :, past : past + span] = forecast[:, 0:span]
    for before, after in zip(arriving, leaving):
        before.wait()
        after.start()
    for n in range(4):
        master, gradient = masters[n][...], outs[n][...]
        new, moment, spread = adamw(master, gradient, momenta[n][...], variances[n][...], factor[None])
        outs[4 + n][...], outs[8 + n][...], outs[12 + n][...] = new, moment, spread
    for copy in leaving:
        copy.wait()


def update_call(prediction, sensitivity, grads, norm, state):
    vmem, hbm = pl.BlockSpec(memory_space=pltpu.VMEM), pl.BlockSpec(memory_space=pl.ANY)
    shapes = tuple(jax.ShapeDtypeStruct(a.shape, F32) for a in state[:4])
    passed = tuple(jax.ShapeDtypeStruct(a.shape, F32) for a in (prediction, sensitivity))
    return pl.pallas_call(
        functools.partial(update_kernel, sensitivity.shape[0], prediction.shape[0]),
        out_shape=4 * shapes + (jax.ShapeDtypeStruct((1, 1), F32),) + passed,
        in_specs=[hbm, hbm] + [vmem] * (2 + len(state)),
        out_specs=tuple([vmem] * 17 + [hbm, hbm]),
        scratch_shapes=[
            pltpu.VMEM((128, 128), F32),
            pltpu.VMEM(prediction.shape, F32),
            pltpu.VMEM(sensitivity.shape, F32),
            pltpu.SemaphoreType.DMA((4,)),
        ],
        name="update",
    )(prediction, sensitivity, grads, norm, *state)


def turned(arrays):
    return [a.transpose(0, 2, 1) if n % 4 == 0 else a for n, a in enumerate(arrays)]


def kernel_shards(plane, segments, extents, adjoint, *state):
    state = turned(state)
    results = train_call(plane, segments, extents, adjoint.T, *state[:4])
    *updated, norm, prediction, sensitivity = update_call(*results, state)
    by_window = (prediction.transpose(1, 2, 0), sensitivity.transpose(1, 2, 0))
    return (*by_window, norm.reshape(()), *turned(updated))


STATE_SPECS = (
    P("section", None, "dp"),
    P("section", None, "dp", None),
    P("section", "dp", None),
    P("section", None, "dp"),
)


def solution(mesh):
    in_specs = (P("dp", None), P("dp"), P("dp", None)) + 3 * STATE_SPECS
    out_specs = (P("section", "dp", None), P("section", "dp", None), P()) + 4 * STATE_SPECS
    plane = PLANES.get(mesh.shape["dp"])
    shards = plain_shards if plane is None else functools.partial(kernel_shards, plane)
    return jax.shard_map(shards, mesh=mesh, in_specs=in_specs, out_specs=out_specs, check_vma=False)
```

```python
import functools

import jax
import jax.numpy as jnp
from jax import lax
from jax.experimental import pallas as pl
from jax.experimental.pallas import tpu as pltpu
from jax.sharding import PartitionSpec as P

STEP = 10


def dot_nn(a, b):
    return jnp.dot(a, b, preferred_element_type=jnp.float32)


def dot_tn(a, b):
    return lax.dot_general(a, b, (((0,), (0,)), ((), ())), preferred_element_type=jnp.float32)


def dot_nt(a, b):
    return lax.dot_general(a, b, (((1,), (1,)), ((), ())), preferred_element_type=jnp.float32)


def unit_rows(first, square, head, biases):
    units = first.shape[1]
    return jnp.concatenate(
        [square.transpose(1, 0, 2).reshape(units, -1), first.T, head, biases.T], axis=1
    )


def from_unit_rows(rows, past, hidden, out):
    wide = 5 * hidden
    square = rows[:, :wide].reshape(-1, 5, hidden).transpose(1, 0, 2)
    first = rows[:, wide : wide + past].T
    head = rows[:, wide + past : wide + past + out]
    biases = rows[:, wide + past + out :].T
    return first, square, head, biases


def plain_forward(weights, resid):
    first, square, head, biases = weights
    past = resid.shape[1]
    acts, slopes = [resid.astype(jnp.bfloat16)], []
    for k in range(4):
        z = dot_nn(acts[-1], first if k == 0 else square[k - 1]) + biases[k].astype(jnp.float32)
        sig = jax.nn.sigmoid(z)
        acts.append((z * sig).astype(jnp.bfloat16))
        slopes.append(sig * (1.0 + z * (1.0 - sig)))
    theta_b = dot_nn(acts[4], square[3]).astype(jnp.bfloat16)
    theta_f = dot_nn(acts[4], square[4]).astype(jnp.bfloat16)
    backcast = dot_nn(theta_b, head[:, :past])
    part = dot_nn(theta_f, head[:, past:])
    return backcast, part, (acts, slopes, theta_b, theta_f)


def plain_backward(weights, saved, e, f):
    first, square, head, biases = weights
    acts, slopes, theta_b, theta_f = saved
    past = e.shape[1]
    head_grad = jnp.concatenate([dot_tn(theta_b, e), dot_tn(theta_f, f)], axis=1)
    u_b = dot_nt(e, head[:, :past]).astype(jnp.bfloat16)
    u_f = dot_nt(f, head[:, past:]).astype(jnp.bfloat16)
    squares = [None, None, None, dot_tn(acts[4], u_b), dot_tn(acts[4], u_f)]
    da = dot_nt(u_b, square[3]) + dot_nt(u_f, square[4])
    bias_grads = [None] * 4
    first_grad = None
    for k in (3, 2, 1, 0):
        dz = (da * slopes[k]).astype(jnp.bfloat16)
        bias_grads[k] = jnp.sum(dz, axis=0, dtype=jnp.float32)
        grad = dot_tn(acts[k], dz)
        if k == 0:
            first_grad = grad
        else:
            squares[k - 1] = grad
        da = dot_nt(dz, first if k == 0 else square[k - 1])
    return da, (first_grad, jnp.stack(squares), head_grad, jnp.stack(bias_grads))


def adamw(master, gradient, momentum, variance, factor):
    clipped = gradient * factor
    moment_new = 0.9 * momentum + 0.1 * clipped
    variance_new = 0.999 * variance + 0.001 * clipped * clipped
    ratio = moment_new / (1.0 - 0.9**STEP) / (jnp.sqrt(variance_new / (1.0 - 0.999**STEP)) + 1e-08)
    return master - 0.05 * (ratio + 0.01 * master), moment_new, variance_new


def plain_shards(segments, extents, adjoint, *state):
    masters, momenta, variances = state[:4], state[4:8], state[8:]
    core = lax.axis_index("section")
    past, span = segments.shape[1], adjoint.shape[1]
    windows = segments.shape[0] // 2
    hidden = masters[1].shape[3]
    mine = [
        lax.dynamic_slice_in_dim(v, core * windows, windows, 0) for v in (segments, extents, adjoint)
    ]
    seg, ext, adj = mine
    rows = unit_rows(*(m[0].astype(jnp.bfloat16) for m in masters))
    rows = lax.all_gather(rows, "dp", axis=0, tiled=True)
    rows = lax.all_gather(rows, "section", axis=0)
    blocks = [from_unit_rows(rows[b], past, hidden, past + span) for b in range(2)]
    mask = (
        lax.broadcasted_iota(jnp.int32, (windows, past), 1) >= past - ext[:, None]
    ).astype(jnp.float32)
    r0 = seg * mask
    backcast, part0, saved0 = plain_forward(blocks[0], r0)
    r1 = (r0 - backcast) * mask
    _, part1, saved1 = plain_forward(blocks[1], r1)
    forecast = part0.astype(jnp.bfloat16).astype(jnp.float32) + part1
    f = adj.astype(jnp.bfloat16)
    zero = jnp.zeros_like(r0)
    da1, grads1 = plain_backward(blocks[1], saved1, (-(zero * mask)).astype(jnp.bfloat16), f)
    dr1 = zero * mask + da1
    t = dr1.astype(jnp.bfloat16).astype(jnp.float32)
    da0, grads0 = plain_backward(blocks[0], saved0, (-(t * mask)).astype(jnp.bfloat16), f)
    dr0 = (t * mask + da0) * mask

    def by_section(first_block, second_block):
        mine, other = (
            jnp.where(core == 0, first_block, second_block),
            jnp.where(core == 0, second_block, first_block),
        )
        got = lax.ppermute(other, "section", [(0, 1), (1, 0)])
        return jnp.where(
            core == 0, jnp.concatenate([mine, got]), jnp.concatenate([got, mine])
        )[None]

    prediction = by_section(part0, forecast)
    sensitivity = by_section(dr0, dr1)
    packed = jnp.stack([unit_rows(*grads0), unit_rows(*grads1)])
    packed = lax.psum_scatter(packed, "section", scatter_dimension=0, tiled=False)
    packed = lax.psum_scatter(packed, "dp", scatter_dimension=0, tiled=True)
    norm = jnp.sqrt(lax.psum(jnp.sum(packed * packed), ("section", "dp")))
    factor = 1.0 / jnp.maximum(norm, 1.0)
    summed = [g[None] for g in from_unit_rows(packed, past, hidden, past + span)]
    updated = [adamw(*four, factor) for four in zip(masters, summed, momenta, variances)]
    return (
        prediction,
        sensitivity,
        norm,
        *summed,
        *(u[0] for u in updated),
        *(u[1] for u in updated),
        *(u[2] for u in updated),
    )


PLANES = {16: (4, 2, 2)}
MESH = pl.DeviceIdType.MESH
MATS = 6
CORE_SLOTS = 4
BF, F32 = jnp.bfloat16, jnp.float32


def remote(src, dst, send_sem, recv_sem, device):
    return pltpu.make_async_remote_copy(
        src_ref=src, dst_ref=dst, send_sem=send_sem, recv_sem=recv_sem, device_id=device, device_id_type=MESH
    )


def train_kernel(
    sizes,
    seg_hbm, adj_hbm, ext, first, square, head, biases,
    pred_out, sens_out, grad_out, norm_out,
    wg, handed, gp, from_core, from_diag, from_plain, from_pair, from_z, total,
    act_t, in_t, theta_t, forecast_grad, slope, work, resid, mask, f_ref, e_ref, t_ref, bias_t, bias_sum, pad,
    seg, adj, first_part, pred, sens, squares, norm_buf,
    own_send, own_recv, ag_send, ag_recv, rs_send, rs_recv, out_send, out_recv, local_sem, norm_send, norm_recv,
):
    ZN, YN, XN, windows, tile, past, span, hidden = sizes
    units = ZN * YN * XN
    core, dp = lax.axis_index("section"), lax.axis_index("dp")
    x, y, z = lax.rem(dp, XN), lax.rem(lax.div(dp, XN), YN), lax.div(dp, XN * YN)
    other, xo, yo = 1 - core, 1 - x, 1 - y
    near_y, near_x = y + core * (yo - y), xo + core * (x - xo)
    far_y, far_x = yo + core * (y - yo), x + core * (xo - x)

    def chip(zi, yi, xi):
        return (core, (zi * YN + yi) * XN + xi)

    sibling = (other, dp)
    z_peers = [lax.rem(z + step, ZN) for step in range(1, ZN)]

    row0 = core * windows
    loads = [
        pltpu.make_async_copy(seg_hbm.at[pl.ds(row0, windows), :], seg, local_sem.at[0]),
        pltpu.make_async_copy(adj_hbm.at[:, pl.ds(row0, windows)], adj, local_sem.at[1]),
    ]
    for load in loads:
        load.start()

    barrier = pltpu.get_barrier_semaphore()
    peers = [sibling, chip(z, y, xo), chip(z, yo, x)] + [chip(zi, y, x) for zi in z_peers]
    for peer in peers:
        pl.semaphore_signal(barrier, inc=1, device_id=peer, device_id_type=MESH)

    rows = hidden // units
    half_rows = rows // 2

    def put_own(m, value, lanes):
        halves = value.astype(BF).reshape(2, half_rows, -1)
        for h in range(2):
            pl.when(core == h)(functools.partial(put_half, m, halves[h], halves[1 - h], lanes))

    def put_half(m, kept, given, lanes):
        wg[core, m, z, y, x, core, :, lanes] = kept
        handed[m, :, lanes] = given

    pad[...] = jnp.zeros_like(pad)
    pad[0:rows, 0:past] = first[0] * 0.5
    put_own(0, pad[0:rows, :], slice(0, 128))
    pad[...] = jnp.zeros_like(pad)
    pad[span : span + 4, 0:rows] = biases[0] * 0.5
    bias_cols = pad[...].T[0:rows]
    pad[...] = jnp.zeros_like(pad)
    pad[0:rows, 0:span] = head[0, :, past : past + span]
    put_own(0, pad[0:rows, :] + bias_cols, slice(128, 256))
    pad[...] = jnp.zeros_like(pad)
    pad[0:rows, 0:past] = head[0, :, 0:past]
    put_own(0, pad[0:rows, :], slice(256, 384))
    put_own(0, jnp.zeros((rows, 128), F32), slice(384, 512))
    for m in range(5):
        put_own(m + 1, square[0, m] * 0.5 if m < 3 else square[0, m], slice(0, hidden))
    pl.semaphore_wait(barrier, len(peers))

    own = remote(handed, wg.at[core, :, z, y, x, other], own_send.at[0], own_recv.at[0], sibling)
    own.start()

    def of(i):
        return lax.div(i, MATS), lax.rem(i, MATS)

    def z_copies(i):
        b, m = of(i)
        part = wg.at[b, m, z, y, x, core]
        return [
            remote(part, part, ag_send.at[i, s], ag_recv.at[i, s], chip(zi, y, x)) for s, zi in enumerate(z_peers)
        ]

    def column_copies(i):
        b, m = of(i)
        part = wg.at[b, m, :, y, x, core]
        return [
            remote(part, part, ag_send.at[i, 3], ag_recv.at[i, 3], chip(z, near_y, near_x)),
            remote(part, part, ag_send.at[i, 4], ag_recv.at[i, 4], chip(z, far_y, far_x)),
        ]

    def corner_copy(i):
        b, m = of(i)
        part = wg.at[b, m, :, near_y, near_x, core]
        return remote(part, part, ag_send.at[i, 5], ag_recv.at[i, 5], chip(z, far_y, far_x))

    def core_copy(i):
        b, m = of(i)
        part = wg.at[b, m, :, :, :, core]
        return remote(part, part, ag_send.at[i, 6], ag_recv.at[i, 6], sibling)

    def start_all(copies):
        for copy in copies:
            copy.start()

    for load in loads:
        load.wait()
    zeros_tile = jnp.zeros((tile, 128), F32)

    def prepare(t, carry):
        at = pl.ds(t * tile, tile)
        resid[at, :] = zeros_tile
        resid[at, 0:past] = seg[at, :]
        return carry

    def prepare_mask(g, carry):
        lengths = ext[pl.ds(core * (windows // 128) + g, 1), :]
        position = lax.broadcasted_iota(jnp.int32, (128, 128), 0)
        keep = jnp.where(position >= past - lengths, 1.0, 0.0).astype(F32).T
        at = pl.ds(pl.multiple_of(g * 128, 128), 128)
        pad[0:span, :] = adj[:, at]
        f_ref[at, :] = pad[...].T.astype(BF)
        mask[at, :] = keep
        resid[at, :] = resid[at, :] * keep
        return carry

    tiles = windows // tile

    def matrix(b, m):
        return wg[b, m].reshape(hidden, hidden)

    def small(b, lane):
        return wg[b, 0, :, :, :, :, :, lane : lane + 128].reshape(hidden, 128)

    def store_layer(b, k, at, v, scale):
        p = 1.0 + jnp.tanh(v)
        a = v * p
        rate = p + a * (2.0 - p)
        slope[b, k, at, :] = (rate if scale is None else rate * scale).astype(BF)
        low = a.astype(BF)
        act_t[b, k, :, at] = low.T
        return low

    def layer_zero(b):
        bias_t[...] = small(b, 128).astype(F32).T

        def body(t, carry):
            at = pl.ds(pl.multiple_of(t * tile, tile), tile)
            a = resid[at, :].astype(BF)
            in_t[b, :, at] = a.T
            v = dot_nt(a, small(b, 0)) + bias_t[span : span + 1, :]
            work[0, at, :] = store_layer(b, 0, at, v, None)
            return carry

        lax.fori_loop(0, tiles, body, 0)

    def layer_next(b, k):
        source, target = lax.rem(k + 1, 2), lax.rem(k, 2)
        bias = bias_t[pl.ds(span + k, 1), :]
        scale = jnp.where(k == 3, 0.5, 1.0)

        def body(t, carry):
            at = pl.ds(pl.multiple_of(t * tile, tile), tile)
            v = dot_nn(work[source, at, :], matrix(b, k)) + bias
            work[target, at, :] = store_layer(b, k, at, v, scale)
            return carry

        lax.fori_loop(0, tiles, body, 0)

    def grid(value):
        return value.astype(BF).reshape(ZN, YN, XN, 2, half_rows, -1)

    def backcast_grad(b):
        gp[b, 0, :, :, :, :, :, 256:384] = grid(dot_nn(theta_t[b], e_ref[...]))

    def backcast_step(b):
        def body(t, carry):
            at = pl.ds(pl.multiple_of(t * tile, tile), tile)
            theta = dot_nn(work[1, at, :], matrix(b, 4)).astype(BF)
            theta_t[b, :, at] = theta.T

            @pl.when(b == 0)
            def _():
                backcast = dot_nn(theta, small(b, 256))
                resid[at, :] = (resid[at, :] - backcast) * mask[at, :]

            @pl.when(b == 1)
            def _():
                e_ref[at, :] = (-(jnp.zeros((tile, 128), F32) * mask[at, :])).astype(BF)

            return carry

        lax.fori_loop(0, tiles, body, 0)
        pl.when(b == 1)(lambda: backcast_grad(b))

    def put_rows(buf, b, at, value):
        for row in range(value.shape[0]):
            buf[b, row, :, at] = value[row : row + 1]

    def forecast_step(b):
        def body(t, carry):
            at = pl.ds(pl.multiple_of(t * tile, tile), tile)
            theta = dot_nn(work[1, at, :], matrix(b, 5)).astype(BF)
            theta_t[1, :, at] = theta.T
            part = dot_nn(theta, small(b, 128)).T[0:span]

            @pl.when(b == 0)
            def _():
                first_part[:, at] = part
                put_rows(pred, 0, at, part)

            @pl.when(b == 1)
            def _():
                put_rows(pred, 1, at, first_part[:, at].astype(BF).astype(F32) + part)

            return carry

        lax.fori_loop(0, tiles, body, 0)
        forecast_grad[b] = dot_nn(theta_t[1], f_ref[...])

    def delayed(lag, t, step):
        pl.when(jnp.logical_and(t >= lag, t < count + lag))(lambda: step(t - lag))

    def gather_line(i):
        start_all(z_copies(i))

    def gather_columns(i):
        for copy in z_copies(i):
            copy.wait_recv()
        start_all(column_copies(i))

    def gather_corner(i):
        column_copies(i)[0].wait_recv()
        corner_copy(i).start()

    def gather_core(i):
        column_copies(i)[1].wait_recv()
        corner_copy(i).wait_recv()
        core_copy(i).start()

    def forward_unit(i):
        core_copy(i).wait_recv()
        b, m = of(i)
        pl.when(m == 0)(lambda: layer_zero(b))
        pl.when(jnp.logical_and(m >= 1, m <= 3))(lambda: layer_next(b, m))
        pl.when(m == 4)(lambda: backcast_step(b))
        pl.when(m == 5)(lambda: forecast_step(b))

    def gather_step(t, carry):
        delayed(4, t, gather_core)
        delayed(2, t, gather_corner)
        delayed(0, t, gather_columns)
        pl.when(t + 4 < count)(lambda: gather_line(t + 4))
        delayed(5, t, forward_unit)
        return carry

    count = 2 * MATS
    own.wait_recv()
    for i in range(4):
        gather_line(i)
    lax.fori_loop(0, tiles, prepare, 0)
    pad[...] = jnp.zeros_like(pad)
    lax.fori_loop(0, windows // 128, prepare_mask, 0)
    lax.fori_loop(0, count + 5, gather_step, 0)

    def out_copies(buf, out, s):
        at = pl.ds(row0, windows)
        return [
            pltpu.make_async_copy(buf.at[core], out.at[:, :, at], local_sem.at[2 + s]),
            remote(buf.at[other], out.at[:, :, at], out_send.at[s], out_recv.at[s], sibling),
        ]

    start_all(out_copies(pred, pred_out, 0))

    def back_of(j):
        s = lax.rem(j, MATS)
        return 1 - lax.div(j, MATS), jnp.where(s == 0, 4, jnp.where(s == 1, 5, 5 - s))

    def to_core(j):
        b, m = back_of(j)
        return remote(
            gp.at[b, m, :, :, :, other], from_core.at[lax.rem(j, CORE_SLOTS)], rs_send.at[j, 0], rs_recv.at[j, 0], sibling
        )

    def to_far(j):
        b, m = back_of(j)
        device = chip(z, far_y, far_x)
        return [
            remote(gp.at[b, m, :, yo, xo, core], from_diag.at[b, m], rs_send.at[j, 1], rs_recv.at[j, 1], device),
            remote(gp.at[b, m, :, far_y, far_x, core], from_plain.at[b, m], rs_send.at[j, 2], rs_recv.at[j, 2], device),
        ]

    def to_near(j):
        b, m = back_of(j)
        return remote(
            gp.at[b, m, :, near_y, near_x, core], from_pair.at[b, m], rs_send.at[j, 3], rs_recv.at[j, 3],
            chip(z, near_y, near_x),
        )

    def to_z(j):
        b, m = back_of(j)
        return [
            remote(gp.at[b, m, zi, y, x, core], from_z.at[b, m, s], rs_send.at[j, 4 + s], rs_recv.at[j, 4 + s], chip(zi, y, x))
            for s, zi in enumerate(z_peers)
        ]

    def scatter_core(j):
        b, m = back_of(j)
        to_core(j).wait_recv()
        gp[b, m, :, :, :, core] = gp[b, m, :, :, :, core] + from_core[lax.rem(j, CORE_SLOTS)]
        start_all(to_far(j))

    def scatter_diag(j):
        b, m = back_of(j)
        to_far(j)[0].wait_recv()
        gp[b, m, :, near_y, near_x, core] = gp[b, m, :, near_y, near_x, core] + from_diag[b, m]
        to_near(j).start()

    def scatter_plane(j):
        b, m = back_of(j)
        to_far(j)[1].wait_recv()
        to_near(j).wait_recv()
        value = gp[b, m, :, y, x, core].astype(F32) + from_plain[b, m].astype(F32) + from_pair[b, m].astype(F32)
        gp[b, m, :, y, x, core] = value.astype(BF)
        start_all(to_z(j))

    def scatter_z(j):
        b, m = back_of(j)
        for copy in to_z(j):
            copy.wait_recv()
        value = gp[b, m, z, y, x, core].astype(F32)
        for s in range(ZN - 1):
            value = value + from_z[b, m, s].astype(F32)
        total[b, m] = value
        squares[...] = squares[...] + value * value

    def dz_slot(k):
        return lax.rem(5 - k, 3)

    def add_rows(value):
        return jnp.sum(value.reshape(-1, 8, hidden), axis=0)

    def put_bias(k, acc):
        bias_sum[pl.ds(span + k, 1), :] = jnp.sum(acc, axis=0, keepdims=True)

    def head_step(b):
        def body(t, carry):
            at = pl.ds(pl.multiple_of(t * tile, tile), tile)

            @pl.when(b == 1)
            def _():
                resid[at, :] = jnp.zeros((tile, 128), F32)

            e = (-(resid[at, :] * mask[at, :])).astype(BF)
            e_ref[at, :] = e
            work[0, at, :] = dot_nt(e, small(b, 256)).astype(BF)
            work[1, at, :] = dot_nt(f_ref[at, :], small(b, 128)).astype(BF)
            return carry

        lax.fori_loop(0, tiles, body, 0)

    def theta_step(b):
        def body(t, acc):
            at = pl.ds(pl.multiple_of(t * tile, tile), tile)
            da = dot_nt(work[0, at, :], matrix(b, 4)) + dot_nt(work[1, at, :], matrix(b, 5))
            dz = da * slope[b, 3, at, :].astype(F32)
            work[2, at, :] = dz.astype(BF)
            return acc + add_rows(dz)

        put_bias(3, lax.fori_loop(0, tiles, body, jnp.zeros((8, hidden), F32)))

    def layer_back(b, k):
        source, target = dz_slot(k + 1), dz_slot(k)

        def body(t, acc):
            at = pl.ds(pl.multiple_of(t * tile, tile), tile)
            dz = dot_nt(work[source, at, :], matrix(b, k + 1)) * slope[b, k, at, :].astype(F32)
            work[target, at, :] = dz.astype(BF)
            return acc + add_rows(dz)

        put_bias(k, lax.fori_loop(0, tiles, body, jnp.zeros((8, hidden), F32)))

    def weight_grad(b, j):
        s = lax.rem(j, MATS)
        layer = jnp.where(s <= 1, 3, 4 - s)
        slot = jnp.where(s <= 1, s, dz_slot(5 - s))
        _, m = back_of(j)
        gp[b, m] = grid(dot_nn(act_t[b, layer], work[slot]))

    def small_grads(b):
        gp[b, 0, :, :, :, :, :, 0:128] = grid(dot_nn(in_t[b], work[2]).T)
        forecast = forecast_grad[b] + bias_sum[...].T
        gp[b, 0, :, :, :, :, :, 128:256] = grid(forecast)
        pl.when(b == 0)(lambda: backcast_grad(b))
        gp[b, 0, :, :, :, :, :, 384:512] = jnp.zeros((ZN, YN, XN, 2, half_rows, 128), BF)

    def input_grad(b):
        def body(t, carry):
            at = pl.ds(pl.multiple_of(t * tile, tile), tile)
            keep = mask[at, :]
            dr = resid[at, :] * keep + 2.0 * dot_nn(work[2, at, :], small(b, 0))

            @pl.when(b == 1)
            def _():
                put_rows(sens, 1, at, dr.T[0:past])
                resid[at, :] = dr.astype(BF).astype(F32)

            @pl.when(b == 0)
            def _():
                put_rows(sens, 0, at, (dr * keep).T[0:past])

            return carry

        lax.fori_loop(0, tiles, body, 0)

    bias_sum[...] = jnp.zeros_like(bias_sum)
    squares[...] = jnp.zeros_like(squares)

    def back_step(j, carry):
        s = lax.rem(j, MATS)
        b, _ = back_of(j)
        live = j < count

        def on(test, step):
            pl.when(jnp.logical_and(live, test))(step)

        on(s == 0, lambda: head_step(b))
        on(s == 2, lambda: theta_step(b))
        on(s >= 3, lambda: layer_back(b, 5 - s))
        delayed(8, j, scatter_z)
        delayed(6, j, scatter_plane)
        delayed(4, j, scatter_diag)
        delayed(2, j, scatter_core)
        on(s <= 4, lambda: weight_grad(b, j))
        on(s == 5, lambda: small_grads(b))
        pl.when(live)(lambda: to_core(j).start())
        on(s == 5, lambda: input_grad(b))
        pl.when(j == count - 1)(lambda: start_all(out_copies(sens, sens_out, 1)))
        return carry

    lax.fori_loop(0, count + 8, back_step, 0)

    grad_copy = remote(total.at[other], grad_out.at[:, core], out_send.at[2], out_recv.at[2], sibling)
    grad_copy.start()
    grad_out[:, core] = total[core]
    sq = squares[:, 0:128] + squares[:, 128:256] + squares[:, 256:384] + squares[:, 384:512]
    norm_buf[0] = sq[0:8] + sq[8:16]
    for step, device in enumerate([sibling, chip(z, y, xo), chip(z, yo, x)]):
        copy = remote(norm_buf.at[2 * step], norm_buf.at[2 * step + 1], norm_send.at[step], norm_recv.at[step], device)
        copy.start()
        copy.wait()
        norm_buf[2 * step + 2] = norm_buf[2 * step] + norm_buf[2 * step + 1]
    norm_buf[7 + z] = norm_buf[6]
    spread = [
        remote(norm_buf.at[6], norm_buf.at[7 + z], norm_send.at[3 + s], norm_recv.at[3 + s], chip(zi, y, x))
        for s, zi in enumerate(z_peers)
    ]
    start_all(spread)
    for copy in spread:
        copy.wait()
    everything = norm_buf[7]
    for zi in range(1, ZN):
        everything = everything + norm_buf[7 + zi]
    norm_out[...] = jnp.broadcast_to(jnp.sqrt(jnp.sum(everything, keepdims=True)), norm_out.shape)

    grad_copy.wait()
    for buf, out, s in ((pred, pred_out, 0), (sens, sens_out, 1)):
        for copy in out_copies(buf, out, s):
            copy.wait()
    own.wait_send()

    def drain(i, carry):
        for copy in z_copies(i) + column_copies(i) + [corner_copy(i), core_copy(i)]:
            copy.wait_send()
        for copy in [to_core(i), *to_far(i), to_near(i), *to_z(i)]:
            copy.wait_send()
        return carry

    lax.fori_loop(0, count, drain, 0)


def train_call(plane, segments, extents, adjoint, first, square, head, biases):
    ZN, YN, XN = plane
    past, span, hidden = segments.shape[1], adjoint.shape[0], square.shape[3]
    windows = segments.shape[0] // 2
    tile = windows
    half = hidden // (ZN * YN * XN) // 2
    sizes = (ZN, YN, XN, windows, tile, past, span, hidden)
    DMA = pltpu.SemaphoreType.DMA
    vmem = pl.BlockSpec(memory_space=pltpu.VMEM)
    hbm = pl.BlockSpec(memory_space=pl.ANY)
    count = 2 * MATS
    flops = 2 * 2 * 3 * windows * hidden * (6 * hidden + 2 * 128)
    return pl.pallas_call(
        functools.partial(train_kernel, sizes),
        out_shape=(
            jax.ShapeDtypeStruct((span, 1, 2 * windows), F32),
            jax.ShapeDtypeStruct((past, 1, 2 * windows), F32),
            jax.ShapeDtypeStruct((MATS, 2, half, hidden), F32),
            jax.ShapeDtypeStruct((8, 128), F32),
        ),
        in_specs=[hbm, hbm] + [vmem] * 5,
        out_specs=(hbm, hbm, vmem, vmem),
        scratch_shapes=[
            pltpu.VMEM((2, MATS, ZN, YN, XN, 2, half, hidden), BF),
            pltpu.VMEM((MATS, half, hidden), BF),
            pltpu.VMEM((2, MATS, ZN, YN, XN, 2, half, hidden), BF),
            pltpu.VMEM((CORE_SLOTS, ZN, YN, XN, half, hidden), BF),
            pltpu.VMEM((2, MATS, ZN, half, hidden), BF),
            pltpu.VMEM((2, MATS, ZN, half, hidden), BF),
            pltpu.VMEM((2, MATS, ZN, half, hidden), BF),
            pltpu.VMEM((2, MATS, ZN - 1, half, hidden), BF),
            pltpu.VMEM((2, MATS, half, hidden), F32),
            pltpu.VMEM((2, 4, hidden, windows), BF),
            pltpu.VMEM((2, 128, windows), BF),
            pltpu.VMEM((2, hidden, windows), BF),
            pltpu.VMEM((2, hidden, 128), F32),
            pltpu.VMEM((2, 4, windows, hidden), BF),
            pltpu.VMEM((3, windows, hidden), BF),
            pltpu.VMEM((windows, 128), F32),
            pltpu.VMEM((windows, 128), F32),
            pltpu.VMEM((windows, 128), BF),
            pltpu.VMEM((windows, 128), BF),
            pltpu.VMEM((8, 128), F32),
            pltpu.VMEM((128, hidden), F32),
            pltpu.VMEM((128, hidden), F32),
            pltpu.VMEM((128, 128), F32),
            pltpu.VMEM((windows, past), F32),
            pltpu.VMEM((span, windows), F32),
            pltpu.VMEM((span, windows), F32),
            pltpu.VMEM((2, span, 1, windows), F32),
            pltpu.VMEM((2, past, 1, windows), F32),
            pltpu.VMEM((half, hidden), F32),
            pltpu.VMEM((7 + ZN, 8, 128), F32),
            DMA((1,)),
            DMA((1,)),
            DMA((count, 7)),
            DMA((count, 7)),
            DMA((count, 4 + ZN - 1)),
            DMA((count, 4 + ZN - 1)),
            DMA((3,)),
            DMA((3,)),
            DMA((4,)),
            DMA((3 + ZN - 1,)),
            DMA((3 + ZN - 1,)),
        ],
        compiler_params=pltpu.CompilerParams(
            collective_id=0, has_side_effects=True, vmem_limit_bytes=64 * 1024 * 1024
        ),
        cost_estimate=pl.CostEstimate(flops=flops, bytes_accessed=8_000_000, transcendentals=8 * windows * hidden),
        name="train",
    )(segments, adjoint, extents.reshape(-1, 128), first, square, head, biases)


def update_kernel(past, span, prediction, sensitivity, grads, norm, *refs):
    masters, momenta, variances, outs = refs[0:4], refs[4:8], refs[8:12], refs[12:28]
    norm_out, prediction_out, sensitivity_out, pad, prediction_held, sensitivity_held, sems = refs[28:]
    arriving = [
        pltpu.make_async_copy(sensitivity, sensitivity_held, sems.at[0]),
        pltpu.make_async_copy(prediction, prediction_held, sems.at[1]),
    ]
    leaving = [
        pltpu.make_async_copy(sensitivity_held, sensitivity_out, sems.at[2]),
        pltpu.make_async_copy(prediction_held, prediction_out, sems.at[3]),
    ]
    for copy in arriving:
        copy.start()
    norm_out[...] = norm[0:1, 0:1]
    factor = 1.0 / jnp.maximum(norm[0:1, 0:1], 1.0)
    units = masters[3].shape[2]

    def rows(m, lane, width):
        return grads[m, :, :, lane : lane + width].reshape(units, width)

    forecast = rows(0, 128, 128)
    pad[...] = jnp.zeros_like(pad)
    outs[0][0] = rows(0, 0, 128)[:, 0:past]
    pad[0:units, :] = forecast
    outs[3][0] = pad[...].T[span : span + 4, 0:units]
    for m in range(5):
        outs[1][0, m] = rows(m + 1, 0, grads.shape[3])
    outs[2][0, :, 0:past] = rows(0, 256, 128)[:, 0:past]
    outs[2][0, :, past : past + span] = forecast[:, 0:span]
    for before, after in zip(arriving, leaving):
        before.wait()
        after.start()
    for n in range(4):
        master, gradient = masters[n][...], outs[n][...]
        new, moment, spread = adamw(master, gradient, momenta[n][...], variances[n][...], factor[None])
        outs[4 + n][...], outs[8 + n][...], outs[12 + n][...] = new, moment, spread
    for copy in leaving:
        copy.wait()


def update_call(prediction, sensitivity, grads, norm, state):
    vmem, hbm = pl.BlockSpec(memory_space=pltpu.VMEM), pl.BlockSpec(memory_space=pl.ANY)
    shapes = tuple(jax.ShapeDtypeStruct(a.shape, F32) for a in state[:4])
    passed = tuple(jax.ShapeDtypeStruct(a.shape, F32) for a in (prediction, sensitivity))
    return pl.pallas_call(
        functools.partial(update_kernel, sensitivity.shape[0], prediction.shape[0]),
        out_shape=4 * shapes + (jax.ShapeDtypeStruct((1, 1), F32),) + passed,
        in_specs=[hbm, hbm] + [vmem] * (2 + len(state)),
        out_specs=tuple([vmem] * 17 + [hbm, hbm]),
        scratch_shapes=[
            pltpu.VMEM((128, 128), F32),
            pltpu.VMEM(prediction.shape, F32),
            pltpu.VMEM(sensitivity.shape, F32),
            pltpu.SemaphoreType.DMA((4,)),
        ],
        name="update",
    )(prediction, sensitivity, grads, norm, *state)


def turned(arrays):
    return [a.transpose(0, 2, 1) if n % 4 == 0 else a for n, a in enumerate(arrays)]


def kernel_shards(plane, segments, extents, adjoint, *state):
    state = turned(state)
    results = train_call(plane, segments, extents, adjoint.T, *state[:4])
    *updated, norm, prediction, sensitivity = update_call(*results, state)
    by_window = (prediction.transpose(1, 2, 0), sensitivity.transpose(1, 2, 0))
    return (*by_window, norm.reshape(()), *turned(updated))


STATE_SPECS = (
    P("section", None, "dp"),
    P("section", None, "dp", None),
    P("section", "dp", None),
    P("section", None, "dp"),
)


def solution(mesh):
    in_specs = (P("dp", None), P("dp"), P("dp", None)) + 3 * STATE_SPECS
    out_specs = (P("section", "dp", None), P("section", "dp", None), P()) + 4 * STATE_SPECS
    plane = PLANES.get(mesh.shape["dp"])
    shards = plain_shards if plane is None else functools.partial(kernel_shards, plane)
    return jax.shard_map(shards, mesh=mesh, in_specs=in_specs, out_specs=out_specs, check_vma=False)
```

```python
import functools

import jax
import jax.numpy as jnp
from jax import lax
from jax.experimental import pallas as pl
from jax.experimental.pallas import tpu as pltpu
from jax.sharding import PartitionSpec as P

STEP = 10


def dot_nn(a, b):
    return jnp.dot(a, b, preferred_element_type=jnp.float32)


def dot_tn(a, b):
    return lax.dot_general(a, b, (((0,), (0,)), ((), ())), preferred_element_type=jnp.float32)


def dot_nt(a, b):
    return lax.dot_general(a, b, (((1,), (1,)), ((), ())), preferred_element_type=jnp.float32)


def unit_rows(first, square, head, biases):
    units = first.shape[1]
    return jnp.concatenate(
        [square.transpose(1, 0, 2).reshape(units, -1), first.T, head, biases.T], axis=1
    )


def from_unit_rows(rows, past, hidden, out):
    wide = 5 * hidden
    square = rows[:, :wide].reshape(-1, 5, hidden).transpose(1, 0, 2)
    first = rows[:, wide : wide + past].T
    head = rows[:, wide + past : wide + past + out]
    biases = rows[:, wide + past + out :].T
    return first, square, head, biases


def plain_forward(weights, resid):
    first, square, head, biases = weights
    past = resid.shape[1]
    acts, slopes = [resid.astype(jnp.bfloat16)], []
    for k in range(4):
        z = dot_nn(acts[-1], first if k == 0 else square[k - 1]) + biases[k].astype(jnp.float32)
        sig = jax.nn.sigmoid(z)
        acts.append((z * sig).astype(jnp.bfloat16))
        slopes.append(sig * (1.0 + z * (1.0 - sig)))
    theta_b = dot_nn(acts[4], square[3]).astype(jnp.bfloat16)
    theta_f = dot_nn(acts[4], square[4]).astype(jnp.bfloat16)
    backcast = dot_nn(theta_b, head[:, :past])
    part = dot_nn(theta_f, head[:, past:])
    return backcast, part, (acts, slopes, theta_b, theta_f)


def plain_backward(weights, saved, e, f):
    first, square, head, biases = weights
    acts, slopes, theta_b, theta_f = saved
    past = e.shape[1]
    head_grad = jnp.concatenate([dot_tn(theta_b, e), dot_tn(theta_f, f)], axis=1)
    u_b = dot_nt(e, head[:, :past]).astype(jnp.bfloat16)
    u_f = dot_nt(f, head[:, past:]).astype(jnp.bfloat16)
    squares = [None, None, None, dot_tn(acts[4], u_b), dot_tn(acts[4], u_f)]
    da = dot_nt(u_b, square[3]) + dot_nt(u_f, square[4])
    bias_grads = [None] * 4
    first_grad = None
    for k in (3, 2, 1, 0):
        dz = (da * slopes[k]).astype(jnp.bfloat16)
        bias_grads[k] = jnp.sum(dz, axis=0, dtype=jnp.float32)
        grad = dot_tn(acts[k], dz)
        if k == 0:
            first_grad = grad
        else:
            squares[k - 1] = grad
        da = dot_nt(dz, first if k == 0 else square[k - 1])
    return da, (first_grad, jnp.stack(squares), head_grad, jnp.stack(bias_grads))


def adamw(master, gradient, momentum, variance, factor):
    clipped = gradient * factor
    moment_new = 0.9 * momentum + 0.1 * clipped
    variance_new = 0.999 * variance + 0.001 * clipped * clipped
    ratio = moment_new / (1.0 - 0.9**STEP) / (jnp.sqrt(variance_new / (1.0 - 0.999**STEP)) + 1e-08)
    return master - 0.05 * (ratio + 0.01 * master), moment_new, variance_new


def plain_shards(segments, extents, adjoint, *state):
    masters, momenta, variances = state[:4], state[4:8], state[8:]
    core = lax.axis_index("section")
    past, span = segments.shape[1], adjoint.shape[1]
    windows = segments.shape[0] // 2
    hidden = masters[1].shape[3]
    mine = [
        lax.dynamic_slice_in_dim(v, core * windows, windows, 0) for v in (segments, extents, adjoint)
    ]
    seg, ext, adj = mine
    rows = unit_rows(*(m[0].astype(jnp.bfloat16) for m in masters))
    rows = lax.all_gather(rows, "dp", axis=0, tiled=True)
    rows = lax.all_gather(rows, "section", axis=0)
    blocks = [from_unit_rows(rows[b], past, hidden, past + span) for b in range(2)]
    mask = (
        lax.broadcasted_iota(jnp.int32, (windows, past), 1) >= past - ext[:, None]
    ).astype(jnp.float32)
    r0 = seg * mask
    backcast, part0, saved0 = plain_forward(blocks[0], r0)
    r1 = (r0 - backcast) * mask
    _, part1, saved1 = plain_forward(blocks[1], r1)
    forecast = part0.astype(jnp.bfloat16).astype(jnp.float32) + part1
    f = adj.astype(jnp.bfloat16)
    zero = jnp.zeros_like(r0)
    da1, grads1 = plain_backward(blocks[1], saved1, (-(zero * mask)).astype(jnp.bfloat16), f)
    dr1 = zero * mask + da1
    t = dr1.astype(jnp.bfloat16).astype(jnp.float32)
    da0, grads0 = plain_backward(blocks[0], saved0, (-(t * mask)).astype(jnp.bfloat16), f)
    dr0 = (t * mask + da0) * mask

    def by_section(first_block, second_block):
        mine, other = (
            jnp.where(core == 0, first_block, second_block),
            jnp.where(core == 0, second_block, first_block),
        )
        got = lax.ppermute(other, "section", [(0, 1), (1, 0)])
        return jnp.where(
            core == 0, jnp.concatenate([mine, got]), jnp.concatenate([got, mine])
        )[None]

    prediction = by_section(part0, forecast)
    sensitivity = by_section(dr0, dr1)
    packed = jnp.stack([unit_rows(*grads0), unit_rows(*grads1)])
    packed = lax.psum_scatter(packed, "section", scatter_dimension=0, tiled=False)
    packed = lax.psum_scatter(packed, "dp", scatter_dimension=0, tiled=True)
    norm = jnp.sqrt(lax.psum(jnp.sum(packed * packed), ("section", "dp")))
    factor = 1.0 / jnp.maximum(norm, 1.0)
    summed = [g[None] for g in from_unit_rows(packed, past, hidden, past + span)]
    updated = [adamw(*four, factor) for four in zip(masters, summed, momenta, variances)]
    return (
        prediction,
        sensitivity,
        norm,
        *summed,
        *(u[0] for u in updated),
        *(u[1] for u in updated),
        *(u[2] for u in updated),
    )


PLANES = {16: (4, 2, 2)}
MESH = pl.DeviceIdType.MESH
MATS = 6
CORE_SLOTS, DIAG_SLOTS, PLAIN_SLOTS, PAIR_SLOTS, Z_SLOTS = 4, 4, 6, 4, 4
BF, F32 = jnp.bfloat16, jnp.float32


def remote(src, dst, send_sem, recv_sem, device):
    return pltpu.make_async_remote_copy(
        src_ref=src, dst_ref=dst, send_sem=send_sem, recv_sem=recv_sem, device_id=device, device_id_type=MESH
    )


def train_kernel(
    sizes,
    seg_hbm, adj_hbm, ext, first, square, head, biases,
    pred_out, sens_out, grad_out, norm_out,
    wg, handed, gp, from_core, from_diag, from_plain, from_pair, from_z, total,
    act_t, in_t, theta_keep, head_acc, slope, work, resid, mask, f_ref, f_t, e_t, bias_t, bias_sum, pad,
    seg, adj, first_part, pred, sens, squares, norm_buf,
    own_send, own_recv, ag_send, ag_recv, rs_send, rs_recv, out_send, out_recv, local_sem, norm_send, norm_recv,
):
    ZN, YN, XN, windows, tile, past, span, hidden = sizes
    units = ZN * YN * XN
    core, dp = lax.axis_index("section"), lax.axis_index("dp")
    x, y, z = lax.rem(dp, XN), lax.rem(lax.div(dp, XN), YN), lax.div(dp, XN * YN)
    other, xo, yo = 1 - core, 1 - x, 1 - y
    near_y, near_x = y + core * (yo - y), xo + core * (x - xo)
    far_y, far_x = yo + core * (y - yo), x + core * (xo - x)

    def chip(zi, yi, xi):
        return (core, (zi * YN + yi) * XN + xi)

    sibling = (other, dp)
    z_peers = [lax.rem(z + step, ZN) for step in range(1, ZN)]

    row0 = core * windows
    loads = [
        pltpu.make_async_copy(seg_hbm.at[pl.ds(row0, windows), :], seg, local_sem.at[0]),
        pltpu.make_async_copy(adj_hbm.at[:, pl.ds(row0, windows)], adj, local_sem.at[1]),
    ]
    for load in loads:
        load.start()

    barrier = pltpu.get_barrier_semaphore()
    peers = [sibling, chip(z, y, xo), chip(z, yo, x)] + [chip(zi, y, x) for zi in z_peers]
    for peer in peers:
        pl.semaphore_signal(barrier, inc=1, device_id=peer, device_id_type=MESH)

    rows = hidden // units
    half_rows = rows // 2

    def put_own(m, value, lanes):
        halves = value.astype(BF).reshape(2, half_rows, -1)
        for h in range(2):
            pl.when(core == h)(functools.partial(put_half, m, halves[h], halves[1 - h], lanes))

    def put_half(m, kept, given, lanes):
        wg[core, m, z, y, x, core, :, lanes] = kept
        handed[m, :, lanes] = given

    pad[...] = jnp.zeros_like(pad)
    pad[0:rows, 0:past] = first[0] * 0.5
    put_own(0, pad[0:rows, :], slice(0, 128))
    pad[...] = jnp.zeros_like(pad)
    pad[span : span + 4, 0:rows] = biases[0] * 0.5
    bias_cols = pad[...].T[0:rows]
    pad[...] = jnp.zeros_like(pad)
    pad[0:rows, 0:span] = head[0, :, past : past + span]
    put_own(0, pad[0:rows, :] + bias_cols, slice(128, 256))
    pad[...] = jnp.zeros_like(pad)
    pad[0:rows, 0:past] = head[0, :, 0:past]
    put_own(0, pad[0:rows, :], slice(256, 384))
    for m in range(5):
        put_own(m + 1, square[0, m] * 0.5 if m < 3 else square[0, m], slice(0, hidden))
    pl.semaphore_wait(barrier, len(peers))

    handed[0, :, 384:512] = jnp.zeros((half_rows, 128), BF)
    own = remote(handed, wg.at[core, :, z, y, x, other], own_send.at[0], own_recv.at[0], sibling)
    own.start()

    def of(i):
        return lax.div(i, MATS), lax.rem(i, MATS)

    def z_copies(i, lanes):
        b, m = of(i)
        part = wg.at[b, m, z, y, x, core, :, lanes]
        return [
            remote(part, part, ag_send.at[i, s], ag_recv.at[i, s], chip(zi, y, x)) for s, zi in enumerate(z_peers)
        ]

    def column_copies(i, lanes):
        b, m = of(i)
        part = wg.at[b, m, :, y, x, core, :, lanes]
        return [
            remote(part, part, ag_send.at[i, 3], ag_recv.at[i, 3], chip(z, near_y, near_x)),
            remote(part, part, ag_send.at[i, 4], ag_recv.at[i, 4], chip(z, far_y, far_x)),
        ]

    def corner_copy(i, lanes):
        b, m = of(i)
        part = wg.at[b, m, :, near_y, near_x, core, :, lanes]
        return remote(part, part, ag_send.at[i, 5], ag_recv.at[i, 5], chip(z, far_y, far_x))

    def core_copy(i, lanes):
        b, m = of(i)
        part = wg.at[b, m, :, :, :, core, :, lanes]
        return remote(part, part, ag_send.at[i, 6], ag_recv.at[i, 6], sibling)

    def by_lanes(m, step):
        pl.when(m == 0)(lambda: step(slice(0, 384)))
        pl.when(m > 0)(lambda: step(slice(0, hidden)))

    def start_all(copies):
        for copy in copies:
            copy.start()

    for load in loads:
        load.wait()
    zeros_tile = jnp.zeros((tile, 128), F32)

    def prepare(t, carry):
        at = pl.ds(t * tile, tile)
        resid[at, :] = zeros_tile
        resid[at, 0:past] = seg[at, :]
        return carry

    def prepare_mask(g, carry):
        lengths = ext[pl.ds(core * (windows // 128) + g, 1), :]
        position = lax.broadcasted_iota(jnp.int32, (128, 128), 0)
        keep = jnp.where(position >= past - lengths, 1.0, 0.0).astype(F32).T
        at = pl.ds(pl.multiple_of(g * 128, 128), 128)
        pad[0:span, :] = adj[:, at]
        f_ref[at, :] = pad[...].T.astype(BF)
        f_t[:, at] = pad[...].astype(BF)
        mask[at, :] = keep.astype(BF)
        resid[at, :] = resid[at, :] * keep
        return carry

    tiles = windows // tile
    part_tile = windows // 2

    def matrix(b, m):
        return wg[b, m].reshape(hidden, hidden)

    def small(b, lane):
        return wg[b, 0, :, :, :, :, :, lane : lane + 128].reshape(hidden, 128)

    def store_layer(b, k, at, v, scale):
        p = 1.0 + jnp.tanh(v)
        a = v * p
        rate = p + a * (2.0 - p)
        slope[b, k, at, :] = (rate if scale is None else rate * scale).astype(BF)
        low = a.astype(BF)
        act_t[b, k, :, at] = low.T
        return low

    def layer_zero(b):
        bias_t[...] = small(b, 128).astype(F32).T

        def body(t, carry):
            at = pl.ds(pl.multiple_of(t * tile, tile), tile)
            a = resid[at, :].astype(BF)
            in_t[b, :, at] = a.T
            v = dot_nt(a, small(b, 0)) + bias_t[span : span + 1, :]
            work[0, at, :] = store_layer(b, 0, at, v, None)
            return carry

        lax.fori_loop(0, tiles, body, 0)

    def layer_next(b, k):
        source, target = lax.rem(k + 1, 2), lax.rem(k, 2)
        bias = bias_t[pl.ds(span + k, 1), :]
        scale = jnp.where(k == 3, 0.5, 1.0)

        def body(t, carry):
            at = pl.ds(pl.multiple_of(t * tile, tile), tile)
            v = dot_nn(work[source, at, :], matrix(b, k)) + bias
            work[target, at, :] = store_layer(b, k, at, v, scale)
            return carry

        lax.fori_loop(0, tiles, body, 0)

    def grid(value):
        return value.astype(BF).reshape(ZN, YN, XN, 2, half_rows, -1)

    def head_grad(acc, lane, b):
        gp[b, 0, :, :, :, :, :, lane : lane + 128] = grid(acc[...].T)

    def backcast_step(b):
        def body(t, carry):
            at = pl.ds(pl.multiple_of(t * part_tile, part_tile), part_tile)
            theta = dot_nn(work[1, at, :], matrix(b, 4)).astype(BF)

            @pl.when(b == 0)
            def _():
                theta_keep[at, :] = theta
                backcast = dot_nn(theta, small(b, 256))
                resid[at, :] = (resid[at, :] - backcast) * mask[at, :].astype(F32)

            @pl.when(b == 1)
            def _():
                head_acc[...] += dot_nn(e_t[:, at], theta)

            return carry

        head_acc[...] = jnp.zeros_like(head_acc)
        lax.fori_loop(0, windows // part_tile, body, 0)
        pl.when(b == 1)(lambda: head_grad(head_acc, 256, b))

    def put_rows(buf, b, at, value):
        for row in range(value.shape[0]):
            buf[b, row, :, at] = value[row : row + 1]

    def forecast_step(b):
        def body(t, carry):
            at = pl.ds(pl.multiple_of(t * part_tile, part_tile), part_tile)
            theta = dot_nn(work[1, at, :], matrix(b, 5)).astype(BF)
            head_acc[...] += dot_nn(f_t[:, at], theta)
            part = dot_nn(theta, small(b, 128)).T[0:span]

            @pl.when(b == 0)
            def _():
                first_part[:, at] = part
                put_rows(pred, 0, at, part)

            @pl.when(b == 1)
            def _():
                put_rows(pred, 1, at, first_part[:, at].astype(BF).astype(F32) + part)

            return carry

        head_acc[...] = jnp.zeros_like(head_acc)
        lax.fori_loop(0, windows // part_tile, body, 0)
        head_grad(head_acc, 128, b)

    count = 2 * MATS

    def delayed(lag, t, step):
        pl.when(jnp.logical_and(t >= lag, t < count + lag))(lambda: step(t - lag))

    def gather_line(i):
        by_lanes(of(i)[1], lambda lanes: start_all(z_copies(i, lanes)))

    def gather_columns(i):
        def step(lanes):
            for copy in z_copies(i, lanes):
                copy.wait_recv()
            start_all(column_copies(i, lanes))

        by_lanes(of(i)[1], step)

    def gather_corner(i):
        def step(lanes):
            column_copies(i, lanes)[0].wait_recv()
            corner_copy(i, lanes).start()

        by_lanes(of(i)[1], step)

    def gather_core(i):
        def step(lanes):
            column_copies(i, lanes)[1].wait_recv()
            corner_copy(i, lanes).wait_recv()
            core_copy(i, lanes).start()

        by_lanes(of(i)[1], step)

    def forward_unit(i):
        b, m = of(i)
        by_lanes(m, lambda lanes: core_copy(i, lanes).wait_recv())
        pl.when(m == 0)(lambda: layer_zero(b))
        pl.when(jnp.logical_and(m >= 1, m <= 3))(lambda: layer_next(b, m))
        pl.when(m == 4)(lambda: backcast_step(b))
        pl.when(m == 5)(lambda: forecast_step(b))

        @pl.when(m == jnp.where(b == 1, 3, 5))
        def _():
            pl.when(b == 1)(lambda: feed_back(b))
            feed_forward(b)
            lax.fori_loop(jnp.where(b == 1, 4, 5), MATS, lambda n, carry: (weight_grad(b, n), carry)[1], 0)

            @pl.when(b == 1)
            def _():
                scatter_start(0)
                scatter_start(1)

    def gather_step(t, carry):
        delayed(4, t, gather_core)
        delayed(2, t, gather_corner)
        delayed(0, t, gather_columns)
        pl.when(t + 4 < count)(lambda: gather_line(t + 4))
        delayed(5, t, forward_unit)
        return carry

    def out_copies(buf, out, s):
        at = pl.ds(row0, windows)
        return [
            pltpu.make_async_copy(buf.at[core], out.at[:, :, at], local_sem.at[2 + s]),
            remote(buf.at[other], out.at[:, :, at], out_send.at[s], out_recv.at[s], sibling),
        ]


    def back_of(j):
        b = jnp.where(jnp.logical_or(j <= 1, jnp.logical_and(j >= 3, j <= 6)), 1, 0)
        m = jnp.where(j <= 1, 4 + j, jnp.where(j == 2, 5, jnp.where(j <= 6, 6 - j, jnp.where(j == 7, 4, 11 - j))))
        return b, m

    def to_core(j, lanes):
        b, m = back_of(j)
        return remote(
            gp.at[b, m, :, :, :, other, :, lanes], from_core.at[lax.rem(j, CORE_SLOTS), :, :, :, :, lanes],
            rs_send.at[j, 0], rs_recv.at[j, 0], sibling,
        )

    def to_far(j, lanes):
        b, m = back_of(j)
        device = chip(z, far_y, far_x)
        return [
            remote(
                gp.at[b, m, :, yo, xo, core, :, lanes], from_diag.at[lax.rem(j, DIAG_SLOTS), :, :, lanes],
                rs_send.at[j, 1], rs_recv.at[j, 1], device,
            ),
            remote(
                gp.at[b, m, :, far_y, far_x, core, :, lanes], from_plain.at[lax.rem(j, PLAIN_SLOTS), :, :, lanes],
                rs_send.at[j, 2], rs_recv.at[j, 2], device,
            ),
        ]

    def to_near(j, lanes):
        b, m = back_of(j)
        return remote(
            gp.at[b, m, :, near_y, near_x, core, :, lanes], from_pair.at[lax.rem(j, PAIR_SLOTS), :, :, lanes],
            rs_send.at[j, 3], rs_recv.at[j, 3], chip(z, near_y, near_x),
        )

    def to_z(j, lanes):
        b, m = back_of(j)
        return [
            remote(
                gp.at[b, m, zi, y, x, core, :, lanes], from_z.at[lax.rem(j, Z_SLOTS), s, :, lanes],
                rs_send.at[j, 4 + s], rs_recv.at[j, 4 + s], chip(zi, y, x),
            )
            for s, zi in enumerate(z_peers)
        ]

    def scatter_start(j):
        by_lanes(back_of(j)[1], lambda lanes: to_core(j, lanes).start())

    def scatter_core(j):
        b, m = back_of(j)

        def step(lanes):
            to_core(j, lanes).wait_recv()
            part = gp[b, m, :, :, :, core, :, lanes] + from_core[lax.rem(j, CORE_SLOTS), :, :, :, :, lanes]
            gp[b, m, :, :, :, core, :, lanes] = part
            start_all(to_far(j, lanes))

        by_lanes(m, step)

    def scatter_diag(j):
        b, m = back_of(j)

        def step(lanes):
            to_far(j, lanes)[0].wait_recv()
            part = gp[b, m, :, near_y, near_x, core, :, lanes] + from_diag[lax.rem(j, DIAG_SLOTS), :, :, lanes]
            gp[b, m, :, near_y, near_x, core, :, lanes] = part
            to_near(j, lanes).start()

        by_lanes(m, step)

    def scatter_plane(j):
        b, m = back_of(j)

        def step(lanes):
            to_far(j, lanes)[1].wait_recv()
            to_near(j, lanes).wait_recv()
            value = gp[b, m, :, y, x, core, :, lanes].astype(F32)
            value = value + from_plain[lax.rem(j, PLAIN_SLOTS), :, :, lanes].astype(F32)
            value = value + from_pair[lax.rem(j, PAIR_SLOTS), :, :, lanes].astype(F32)
            gp[b, m, :, y, x, core, :, lanes] = value.astype(BF)
            start_all(to_z(j, lanes))

        by_lanes(m, step)

    def scatter_z(j):
        b, m = back_of(j)

        def step(lanes):
            for copy in to_z(j, lanes):
                copy.wait_recv()
            value = gp[b, m, z, y, x, core, :, lanes].astype(F32)
            for s in range(ZN - 1):
                value = value + from_z[lax.rem(j, Z_SLOTS), s, :, lanes].astype(F32)
            total[b, m, :, lanes] = value
            squares[:, lanes] = squares[:, lanes] + value * value

        by_lanes(m, step)

    def add_rows(value):
        return jnp.sum(value.reshape(-1, 8, hidden), axis=0)

    def put_bias(k, acc):
        bias_sum[pl.ds(span + k, 1), :] = jnp.sum(acc, axis=0, keepdims=True)

    def feed_back(b):
        def body(t, carry):
            at = pl.ds(pl.multiple_of(t * tile, tile), tile)

            @pl.when(b == 1)
            def _():
                resid[at, :] = jnp.zeros((tile, 128), F32)

            e = (-(resid[at, :] * mask[at, :].astype(F32))).astype(BF)
            e_t[:, at] = e.T
            work[0, at, :] = dot_nt(e, small(b, 256)).astype(BF)
            return carry

        lax.fori_loop(0, tiles, body, 0)

    def feed_forward(b):
        def body(t, carry):
            at = pl.ds(pl.multiple_of(t * tile, tile), tile)
            work[2, at, :] = dot_nt(f_ref[at, :], small(b, 128)).astype(BF)
            return carry

        lax.fori_loop(0, tiles, body, 0)

    def theta_step(b):
        def body(t, acc):
            at = pl.ds(pl.multiple_of(t * tile, tile), tile)
            da = dot_nt(work[0, at, :], matrix(b, 4)) + dot_nt(work[2, at, :], matrix(b, 5))
            dz = da * slope[b, 3, at, :].astype(F32)
            work[1, at, :] = dz.astype(BF)
            return acc + add_rows(dz)

        put_bias(3, lax.fori_loop(0, tiles, body, jnp.zeros((8, hidden), F32)))

    def layer_back(b, k):
        source, target = lax.rem(k + 1, 2), lax.rem(k, 2)

        def body(t, acc):
            at = pl.ds(pl.multiple_of(t * tile, tile), tile)
            dz = dot_nt(work[source, at, :], matrix(b, k + 1)) * slope[b, k, at, :].astype(F32)
            work[target, at, :] = dz.astype(BF)
            return acc + add_rows(dz)

        put_bias(k, lax.fori_loop(0, tiles, body, jnp.zeros((8, hidden), F32)))

    def weight_grad(b, m):
        layer = jnp.where(m >= 4, 3, m - 1)
        slot = jnp.where(m == 4, 0, jnp.where(m == 5, 2, lax.rem(m, 2)))
        gp[b, m] = grid(dot_nn(act_t[b, layer], work[slot]))

    def small_grads(b):
        gp[b, 0, :, :, :, :, :, 0:128] = grid(dot_nn(in_t[b], work[0]).T)
        gp[b, 0, :, :, :, :, :, 128:256] = gp[b, 0, :, :, :, :, :, 128:256] + grid(bias_sum[...].T)

        @pl.when(b == 0)
        def _():
            head_acc[...] = dot_nn(e_t[...], theta_keep[...])
            head_grad(head_acc, 256, b)


    def input_grad(b):
        def body(t, carry):
            at = pl.ds(pl.multiple_of(t * tile, tile), tile)
            keep = mask[at, :].astype(F32)
            dr = resid[at, :] * keep + 2.0 * dot_nn(work[0, at, :], small(b, 0))

            @pl.when(b == 1)
            def _():
                put_rows(sens, 1, at, dr.T[0:past])
                resid[at, :] = dr.astype(BF).astype(F32)

            @pl.when(b == 0)
            def _():
                put_rows(sens, 0, at, (dr * keep).T[0:past])

            return carry

        lax.fori_loop(0, tiles, body, 0)

    bias_sum[...] = jnp.zeros_like(bias_sum)
    squares[...] = jnp.zeros_like(squares)
    total[...] = jnp.zeros_like(total)

    def back_step(j, carry):
        b, m = back_of(j)
        live = jnp.logical_and(j >= 3, j < count)

        def on(test, step):
            pl.when(jnp.logical_and(live, test))(step)

        @pl.when(j == 7)
        def _():
            feed_back(b)
            feed_forward(b)

        on(m == 3, lambda: theta_step(b))
        on(m <= 2, lambda: layer_back(b, m))
        delayed(8, j, scatter_z)
        delayed(6, j, scatter_plane)
        delayed(4, j, scatter_diag)
        delayed(2, j, scatter_core)
        on(m >= 1, lambda: weight_grad(b, m))
        on(m == 0, lambda: small_grads(b))
        pl.when(jnp.logical_and(j >= 2, j < count))(lambda: scatter_start(j))
        on(m == 0, lambda: input_grad(b))
        pl.when(j == count - 1)(lambda: start_all(out_copies(sens, sens_out, 1)))
        return carry

    own.wait_recv()
    for i in range(4):
        gather_line(i)
    lax.fori_loop(0, tiles, prepare, 0)
    pad[...] = jnp.zeros_like(pad)
    lax.fori_loop(0, windows // 128, prepare_mask, 0)
    lax.fori_loop(0, count + 5, gather_step, 0)

    start_all(out_copies(pred, pred_out, 0))
    lax.fori_loop(0, count + 8, back_step, 0)

    grad_copy = remote(total.at[other], grad_out.at[:, core], out_send.at[2], out_recv.at[2], sibling)
    grad_copy.start()
    grad_out[:, core] = total[core]
    sq = squares[:, 0:128] + squares[:, 128:256] + squares[:, 256:384] + squares[:, 384:512]
    norm_buf[0] = sq[0:8] + sq[8:16]
    for step, device in enumerate([sibling, chip(z, y, xo), chip(z, yo, x)]):
        copy = remote(norm_buf.at[2 * step], norm_buf.at[2 * step + 1], norm_send.at[step], norm_recv.at[step], device)
        copy.start()
        copy.wait()
        norm_buf[2 * step + 2] = norm_buf[2 * step] + norm_buf[2 * step + 1]
    norm_buf[7 + z] = norm_buf[6]
    spread = [
        remote(norm_buf.at[6], norm_buf.at[7 + z], norm_send.at[3 + s], norm_recv.at[3 + s], chip(zi, y, x))
        for s, zi in enumerate(z_peers)
    ]
    start_all(spread)
    for copy in spread:
        copy.wait()
    everything = norm_buf[7]
    for zi in range(1, ZN):
        everything = everything + norm_buf[7 + zi]
    norm_out[...] = jnp.broadcast_to(jnp.sqrt(jnp.sum(everything, keepdims=True)), norm_out.shape)

    grad_copy.wait()
    for buf, out, s in ((pred, pred_out, 0), (sens, sens_out, 1)):
        for copy in out_copies(buf, out, s):
            copy.wait()
    own.wait_send()

    def drain(i, carry):
        def gathered(lanes):
            for copy in [*z_copies(i, lanes), *column_copies(i, lanes), corner_copy(i, lanes), core_copy(i, lanes)]:
                copy.wait_send()

        def scattered(lanes):
            for copy in [to_core(i, lanes), *to_far(i, lanes), to_near(i, lanes), *to_z(i, lanes)]:
                copy.wait_send()

        by_lanes(of(i)[1], gathered)
        by_lanes(back_of(i)[1], scattered)
        return carry

    lax.fori_loop(0, count, drain, 0)


def train_call(plane, segments, extents, adjoint, first, square, head, biases):
    ZN, YN, XN = plane
    past, span, hidden = segments.shape[1], adjoint.shape[0], square.shape[3]
    windows = segments.shape[0] // 2
    tile = windows
    half = hidden // (ZN * YN * XN) // 2
    sizes = (ZN, YN, XN, windows, tile, past, span, hidden)
    DMA = pltpu.SemaphoreType.DMA
    vmem = pl.BlockSpec(memory_space=pltpu.VMEM)
    hbm = pl.BlockSpec(memory_space=pl.ANY)
    count = 2 * MATS
    flops = 2 * 2 * 3 * windows * hidden * (6 * hidden + 2 * 128)
    return pl.pallas_call(
        functools.partial(train_kernel, sizes),
        out_shape=(
            jax.ShapeDtypeStruct((span, 1, 2 * windows), F32),
            jax.ShapeDtypeStruct((past, 1, 2 * windows), F32),
            jax.ShapeDtypeStruct((MATS, 2, half, hidden), F32),
            jax.ShapeDtypeStruct((8, 128), F32),
        ),
        in_specs=[hbm, hbm] + [vmem] * 5,
        out_specs=(hbm, hbm, vmem, vmem),
        scratch_shapes=[
            pltpu.VMEM((2, MATS, ZN, YN, XN, 2, half, hidden), BF),
            pltpu.VMEM((MATS, half, hidden), BF),
            pltpu.VMEM((2, MATS, ZN, YN, XN, 2, half, hidden), BF),
            pltpu.VMEM((CORE_SLOTS, ZN, YN, XN, half, hidden), BF),
            pltpu.VMEM((DIAG_SLOTS, ZN, half, hidden), BF),
            pltpu.VMEM((PLAIN_SLOTS, ZN, half, hidden), BF),
            pltpu.VMEM((PAIR_SLOTS, ZN, half, hidden), BF),
            pltpu.VMEM((Z_SLOTS, ZN - 1, half, hidden), BF),
            pltpu.VMEM((2, MATS, half, hidden), F32),
            pltpu.VMEM((2, 4, hidden, windows), BF),
            pltpu.VMEM((2, 128, windows), BF),
            pltpu.VMEM((windows, hidden), BF),
            pltpu.VMEM((128, hidden), F32),
            pltpu.VMEM((2, 4, windows, hidden), BF),
            pltpu.VMEM((3, windows, hidden), BF),
            pltpu.VMEM((windows, 128), F32),
            pltpu.VMEM((windows, 128), BF),
            pltpu.VMEM((windows, 128), BF),
            pltpu.VMEM((128, windows), BF),
            pltpu.VMEM((128, windows), BF),
            pltpu.VMEM((128, hidden), F32),
            pltpu.VMEM((128, hidden), F32),
            pltpu.VMEM((128, 128), F32),
            pltpu.VMEM((windows, past), F32),
            pltpu.VMEM((span, windows), F32),
            pltpu.VMEM((span, windows), F32),
            pltpu.VMEM((2, span, 1, windows), F32),
            pltpu.VMEM((2, past, 1, windows), F32),
            pltpu.VMEM((half, hidden), F32),
            pltpu.VMEM((7 + ZN, 8, 128), F32),
            DMA((1,)),
            DMA((1,)),
            DMA((count, 7)),
            DMA((count, 7)),
            DMA((count, 4 + ZN - 1)),
            DMA((count, 4 + ZN - 1)),
            DMA((3,)),
            DMA((3,)),
            DMA((4,)),
            DMA((3 + ZN - 1,)),
            DMA((3 + ZN - 1,)),
        ],
        compiler_params=pltpu.CompilerParams(
            collective_id=0, has_side_effects=True, vmem_limit_bytes=64 * 1024 * 1024
        ),
        cost_estimate=pl.CostEstimate(flops=flops, bytes_accessed=8_000_000, transcendentals=8 * windows * hidden),
        name="train",
    )(segments, adjoint, extents.reshape(-1, 128), first, square, head, biases)


def update_kernel(past, span, prediction, sensitivity, grads, norm, *refs):
    masters, momenta, variances, outs = refs[0:4], refs[4:8], refs[8:12], refs[12:28]
    norm_out, prediction_out, sensitivity_out, pad, prediction_held, sensitivity_held, sems = refs[28:]
    arriving = [
        pltpu.make_async_copy(sensitivity, sensitivity_held, sems.at[0]),
        pltpu.make_async_copy(prediction, prediction_held, sems.at[1]),
    ]
    leaving = [
        pltpu.make_async_copy(sensitivity_held, sensitivity_out, sems.at[2]),
        pltpu.make_async_copy(prediction_held, prediction_out, sems.at[3]),
    ]
    for copy in arriving:
        copy.start()
    norm_out[...] = norm[0:1, 0:1]
    factor = 1.0 / jnp.maximum(norm[0:1, 0:1], 1.0)
    units = masters[3].shape[2]

    def rows(m, lane, width):
        return grads[m, :, :, lane : lane + width].reshape(units, width)

    forecast = rows(0, 128, 128)
    pad[...] = jnp.zeros_like(pad)
    outs[0][0] = rows(0, 0, 128)[:, 0:past]
    pad[0:units, :] = forecast
    outs[3][0] = pad[...].T[span : span + 4, 0:units]
    for m in range(5):
        outs[1][0, m] = rows(m + 1, 0, grads.shape[3])
    outs[2][0, :, 0:past] = rows(0, 256, 128)[:, 0:past]
    outs[2][0, :, past : past + span] = forecast[:, 0:span]
    for before, after in zip(arriving, leaving):
        before.wait()
        after.start()
    for n in range(4):
        master, gradient = masters[n][...], outs[n][...]
        new, moment, spread = adamw(master, gradient, momenta[n][...], variances[n][...], factor[None])
        outs[4 + n][...], outs[8 + n][...], outs[12 + n][...] = new, moment, spread
    for copy in leaving:
        copy.wait()


def update_call(prediction, sensitivity, grads, norm, state):
    vmem, hbm = pl.BlockSpec(memory_space=pltpu.VMEM), pl.BlockSpec(memory_space=pl.ANY)
    shapes = tuple(jax.ShapeDtypeStruct(a.shape, F32) for a in state[:4])
    passed = tuple(jax.ShapeDtypeStruct(a.shape, F32) for a in (prediction, sensitivity))
    return pl.pallas_call(
        functools.partial(update_kernel, sensitivity.shape[0], prediction.shape[0]),
        out_shape=4 * shapes + (jax.ShapeDtypeStruct((1, 1), F32),) + passed,
        in_specs=[hbm, hbm] + [vmem] * (2 + len(state)),
        out_specs=tuple([vmem] * 17 + [hbm, hbm]),
        scratch_shapes=[
            pltpu.VMEM((128, 128), F32),
            pltpu.VMEM(prediction.shape, F32),
            pltpu.VMEM(sensitivity.shape, F32),
            pltpu.SemaphoreType.DMA((4,)),
        ],
        name="update",
    )(prediction, sensitivity, grads, norm, *state)


def turned(arrays):
    return [a.transpose(0, 2, 1) if n % 4 == 0 else a for n, a in enumerate(arrays)]


def kernel_shards(plane, segments, extents, adjoint, *state):
    state = turned(state)
    results = train_call(plane, segments, extents, adjoint.T, *state[:4])
    *updated, norm, prediction, sensitivity = update_call(*results, state)
    by_window = (prediction.transpose(1, 2, 0), sensitivity.transpose(1, 2, 0))
    return (*by_window, norm.reshape(()), *turned(updated))


STATE_SPECS = (
    P("section", None, "dp"),
    P("section", None, "dp", None),
    P("section", "dp", None),
    P("section", None, "dp"),
)


def solution(mesh):
    in_specs = (P("dp", None), P("dp"), P("dp", None)) + 3 * STATE_SPECS
    out_specs = (P("section", "dp", None), P("section", "dp", None), P()) + 4 * STATE_SPECS
    plane = PLANES.get(mesh.shape["dp"])
    shards = plain_shards if plane is None else functools.partial(kernel_shards, plane)
    return jax.shard_map(shards, mesh=mesh, in_specs=in_specs, out_specs=out_specs, check_vma=False)
```

```python
import functools

import jax
import jax.numpy as jnp
from jax import lax
from jax.experimental import pallas as pl
from jax.experimental.pallas import tpu as pltpu
from jax.sharding import PartitionSpec as P

STEP = 10


def dot_nn(a, b):
    return jnp.dot(a, b, preferred_element_type=jnp.float32)


def dot_tn(a, b):
    return lax.dot_general(a, b, (((0,), (0,)), ((), ())), preferred_element_type=jnp.float32)


def dot_nt(a, b):
    return lax.dot_general(a, b, (((1,), (1,)), ((), ())), preferred_element_type=jnp.float32)


def unit_rows(first, square, head, biases):
    units = first.shape[1]
    return jnp.concatenate(
        [square.transpose(1, 0, 2).reshape(units, -1), first.T, head, biases.T], axis=1
    )


def from_unit_rows(rows, past, hidden, out):
    wide = 5 * hidden
    square = rows[:, :wide].reshape(-1, 5, hidden).transpose(1, 0, 2)
    first = rows[:, wide : wide + past].T
    head = rows[:, wide + past : wide + past + out]
    biases = rows[:, wide + past + out :].T
    return first, square, head, biases


def plain_forward(weights, resid):
    first, square, head, biases = weights
    past = resid.shape[1]
    acts, slopes = [resid.astype(jnp.bfloat16)], []
    for k in range(4):
        z = dot_nn(acts[-1], first if k == 0 else square[k - 1]) + biases[k].astype(jnp.float32)
        sig = jax.nn.sigmoid(z)
        acts.append((z * sig).astype(jnp.bfloat16))
        slopes.append(sig * (1.0 + z * (1.0 - sig)))
    theta_b = dot_nn(acts[4], square[3]).astype(jnp.bfloat16)
    theta_f = dot_nn(acts[4], square[4]).astype(jnp.bfloat16)
    backcast = dot_nn(theta_b, head[:, :past])
    part = dot_nn(theta_f, head[:, past:])
    return backcast, part, (acts, slopes, theta_b, theta_f)


def plain_backward(weights, saved, e, f):
    first, square, head, biases = weights
    acts, slopes, theta_b, theta_f = saved
    past = e.shape[1]
    head_grad = jnp.concatenate([dot_tn(theta_b, e), dot_tn(theta_f, f)], axis=1)
    u_b = dot_nt(e, head[:, :past]).astype(jnp.bfloat16)
    u_f = dot_nt(f, head[:, past:]).astype(jnp.bfloat16)
    squares = [None, None, None, dot_tn(acts[4], u_b), dot_tn(acts[4], u_f)]
    da = dot_nt(u_b, square[3]) + dot_nt(u_f, square[4])
    bias_grads = [None] * 4
    first_grad = None
    for k in (3, 2, 1, 0):
        dz = (da * slopes[k]).astype(jnp.bfloat16)
        bias_grads[k] = jnp.sum(dz, axis=0, dtype=jnp.float32)
        grad = dot_tn(acts[k], dz)
        if k == 0:
            first_grad = grad
        else:
            squares[k - 1] = grad
        da = dot_nt(dz, first if k == 0 else square[k - 1])
    return da, (first_grad, jnp.stack(squares), head_grad, jnp.stack(bias_grads))


def adamw(master, gradient, momentum, variance, factor):
    clipped = gradient * factor
    moment_new = 0.9 * momentum + 0.1 * clipped
    variance_new = 0.999 * variance + 0.001 * clipped * clipped
    ratio = moment_new / (1.0 - 0.9**STEP) / (jnp.sqrt(variance_new / (1.0 - 0.999**STEP)) + 1e-08)
    return master - 0.05 * (ratio + 0.01 * master), moment_new, variance_new


def plain_shards(segments, extents, adjoint, *state):
    masters, momenta, variances = state[:4], state[4:8], state[8:]
    core = lax.axis_index("section")
    past, span = segments.shape[1], adjoint.shape[1]
    windows = segments.shape[0] // 2
    hidden = masters[1].shape[3]
    mine = [
        lax.dynamic_slice_in_dim(v, core * windows, windows, 0) for v in (segments, extents, adjoint)
    ]
    seg, ext, adj = mine
    rows = unit_rows(*(m[0].astype(jnp.bfloat16) for m in masters))
    rows = lax.all_gather(rows, "dp", axis=0, tiled=True)
    rows = lax.all_gather(rows, "section", axis=0)
    blocks = [from_unit_rows(rows[b], past, hidden, past + span) for b in range(2)]
    mask = (
        lax.broadcasted_iota(jnp.int32, (windows, past), 1) >= past - ext[:, None]
    ).astype(jnp.float32)
    r0 = seg * mask
    backcast, part0, saved0 = plain_forward(blocks[0], r0)
    r1 = (r0 - backcast) * mask
    _, part1, saved1 = plain_forward(blocks[1], r1)
    forecast = part0.astype(jnp.bfloat16).astype(jnp.float32) + part1
    f = adj.astype(jnp.bfloat16)
    zero = jnp.zeros_like(r0)
    da1, grads1 = plain_backward(blocks[1], saved1, (-(zero * mask)).astype(jnp.bfloat16), f)
    dr1 = zero * mask + da1
    t = dr1.astype(jnp.bfloat16).astype(jnp.float32)
    da0, grads0 = plain_backward(blocks[0], saved0, (-(t * mask)).astype(jnp.bfloat16), f)
    dr0 = (t * mask + da0) * mask

    def by_section(first_block, second_block):
        mine, other = (
            jnp.where(core == 0, first_block, second_block),
            jnp.where(core == 0, second_block, first_block),
        )
        got = lax.ppermute(other, "section", [(0, 1), (1, 0)])
        return jnp.where(
            core == 0, jnp.concatenate([mine, got]), jnp.concatenate([got, mine])
        )[None]

    prediction = by_section(part0, forecast)
    sensitivity = by_section(dr0, dr1)
    packed = jnp.stack([unit_rows(*grads0), unit_rows(*grads1)])
    packed = lax.psum_scatter(packed, "section", scatter_dimension=0, tiled=False)
    packed = lax.psum_scatter(packed, "dp", scatter_dimension=0, tiled=True)
    norm = jnp.sqrt(lax.psum(jnp.sum(packed * packed), ("section", "dp")))
    factor = 1.0 / jnp.maximum(norm, 1.0)
    summed = [g[None] for g in from_unit_rows(packed, past, hidden, past + span)]
    updated = [adamw(*four, factor) for four in zip(masters, summed, momenta, variances)]
    return (
        prediction,
        sensitivity,
        norm,
        *summed,
        *(u[0] for u in updated),
        *(u[1] for u in updated),
        *(u[2] for u in updated),
    )


PLANES = {16: (4, 2, 2)}
MESH = pl.DeviceIdType.MESH
MATS = 6
CORE_SLOTS, DIAG_SLOTS, PLAIN_SLOTS, PAIR_SLOTS, Z_SLOTS = 4, 4, 6, 4, 4
BF, F32 = jnp.bfloat16, jnp.float32


def remote(src, dst, send_sem, recv_sem, device):
    return pltpu.make_async_remote_copy(
        src_ref=src, dst_ref=dst, send_sem=send_sem, recv_sem=recv_sem, device_id=device, device_id_type=MESH
    )


def train_kernel(
    sizes,
    seg_hbm, adj_hbm, ext, first, square, head, biases,
    pred_out, sens_out, grad_out, norm_out,
    wg, handed, gp, from_core, from_diag, from_plain, from_pair, from_z, total,
    act_t, in_t, theta_keep, head_acc, slope, work, resid, mask, f_ref, f_t, e_t, bias_t, bias_sum, pad,
    seg, adj, first_part, pred, sens, squares, norm_buf,
    own_send, own_recv, ag_send, ag_recv, rs_send, rs_recv, out_send, out_recv, local_sem, norm_send, norm_recv,
):
    ZN, YN, XN, windows, tile, past, span, hidden = sizes
    units = ZN * YN * XN
    core, dp = lax.axis_index("section"), lax.axis_index("dp")
    x, y, z = lax.rem(dp, XN), lax.rem(lax.div(dp, XN), YN), lax.div(dp, XN * YN)
    other, xo, yo = 1 - core, 1 - x, 1 - y
    near_y, near_x = y + core * (yo - y), xo + core * (x - xo)
    far_y, far_x = yo + core * (y - yo), x + core * (xo - x)

    def chip(zi, yi, xi):
        return (core, (zi * YN + yi) * XN + xi)

    sibling = (other, dp)
    z_peers = [lax.rem(z + step, ZN) for step in range(1, ZN)]

    row0 = core * windows
    loads = [
        pltpu.make_async_copy(seg_hbm.at[pl.ds(row0, windows), :], seg, local_sem.at[0]),
        pltpu.make_async_copy(adj_hbm.at[:, pl.ds(row0, windows)], adj, local_sem.at[1]),
    ]
    for load in loads:
        load.start()

    barrier = pltpu.get_barrier_semaphore()
    peers = [sibling, chip(z, y, xo), chip(z, yo, x)] + [chip(zi, y, x) for zi in z_peers]
    for peer in peers:
        pl.semaphore_signal(barrier, inc=1, device_id=peer, device_id_type=MESH)

    rows = hidden // units
    half_rows = rows // 2

    def put_own(m, value, lanes):
        halves = value.astype(BF).reshape(2, half_rows, -1)
        for h in range(2):
            pl.when(core == h)(functools.partial(put_half, m, halves[h], halves[1 - h], lanes))

    def put_half(m, kept, given, lanes):
        wg[core, m, z, y, x, core, :, lanes] = kept
        handed[m, :, lanes] = given

    pad[...] = jnp.zeros_like(pad)
    pad[0:rows, 0:past] = first[0] * 0.5
    put_own(0, pad[0:rows, :], slice(0, 128))
    pad[...] = jnp.zeros_like(pad)
    pad[span : span + 4, 0:rows] = biases[0] * 0.5
    bias_cols = pad[...].T[0:rows]
    pad[...] = jnp.zeros_like(pad)
    pad[0:rows, 0:span] = head[0, :, past : past + span]
    put_own(0, pad[0:rows, :] + bias_cols, slice(128, 256))
    pad[...] = jnp.zeros_like(pad)
    pad[0:rows, 0:past] = head[0, :, 0:past]
    put_own(0, pad[0:rows, :], slice(256, 384))
    for m in range(5):
        put_own(m + 1, square[0, m] * 0.5 if m < 3 else square[0, m], slice(0, hidden))
    pl.semaphore_wait(barrier, len(peers))

    handed[0, :, 384:512] = jnp.zeros((half_rows, 128), BF)
    own = remote(handed, wg.at[core, :, z, y, x, other], own_send.at[0], own_recv.at[0], sibling)
    own.start()

    def of(i):
        return lax.div(i, MATS), lax.rem(i, MATS)

    def z_copies(i, lanes):
        b, m = of(i)
        part = wg.at[b, m, z, y, x, core, :, lanes]
        return [
            remote(part, part, ag_send.at[i, s], ag_recv.at[i, s], chip(zi, y, x)) for s, zi in enumerate(z_peers)
        ]

    def column_copies(i, lanes):
        b, m = of(i)
        part = wg.at[b, m, :, y, x, core, :, lanes]
        return [
            remote(part, part, ag_send.at[i, 3], ag_recv.at[i, 3], chip(z, near_y, near_x)),
            remote(part, part, ag_send.at[i, 4], ag_recv.at[i, 4], chip(z, far_y, far_x)),
        ]

    def corner_copy(i, lanes):
        b, m = of(i)
        part = wg.at[b, m, :, near_y, near_x, core, :, lanes]
        return remote(part, part, ag_send.at[i, 5], ag_recv.at[i, 5], chip(z, far_y, far_x))

    def core_copy(i, lanes):
        b, m = of(i)
        part = wg.at[b, m, :, :, :, core, :, lanes]
        return remote(part, part, ag_send.at[i, 6], ag_recv.at[i, 6], sibling)

    def by_lanes(m, step):
        pl.when(m == 0)(lambda: step(slice(0, 384)))
        pl.when(m > 0)(lambda: step(slice(0, hidden)))

    def start_all(copies):
        for copy in copies:
            copy.start()

    for load in loads:
        load.wait()
    zeros_tile = jnp.zeros((tile, 128), F32)

    def prepare(t, carry):
        at = pl.ds(t * tile, tile)
        resid[at, :] = zeros_tile
        resid[at, 0:past] = seg[at, :]
        return carry

    def prepare_mask(g, carry):
        lengths = ext[pl.ds(core * (windows // 128) + g, 1), :]
        position = lax.broadcasted_iota(jnp.int32, (128, 128), 0)
        keep = jnp.where(position >= past - lengths, 1.0, 0.0).astype(F32).T
        at = pl.ds(pl.multiple_of(g * 128, 128), 128)
        pad[0:span, :] = adj[:, at]
        f_ref[at, :] = pad[...].T.astype(BF)
        f_t[:, at] = pad[...].astype(BF)
        mask[at, :] = keep.astype(BF)
        resid[at, :] = resid[at, :] * keep
        return carry

    tiles = windows // tile
    part_tile = tile

    def matrix(b, m):
        return wg[b, m].reshape(hidden, hidden)

    def small(b, lane):
        return wg[b, 0, :, :, :, :, :, lane : lane + 128].reshape(hidden, 128)

    def store_layer(b, k, at, v, scale):
        p = 1.0 + jnp.tanh(v)
        a = v * p
        rate = p + a * (2.0 - p)
        slope[b, k, at, :] = (rate if scale is None else rate * scale).astype(BF)
        low = a.astype(BF)
        act_t[b, k, :, at] = low.T
        return low

    def layer_zero(b):
        bias_t[...] = small(b, 128).astype(F32).T

        def body(t, carry):
            at = pl.ds(pl.multiple_of(t * tile, tile), tile)
            a = resid[at, :].astype(BF)
            in_t[b, :, at] = a.T
            v = dot_nt(a, small(b, 0)) + bias_t[span : span + 1, :]
            work[0, at, :] = store_layer(b, 0, at, v, None)
            return carry

        lax.fori_loop(0, tiles, body, 0)

    def layer_next(b, k):
        source, target = lax.rem(k + 1, 2), lax.rem(k, 2)
        bias = bias_t[pl.ds(span + k, 1), :]
        scale = jnp.where(k == 3, 0.5, 1.0)

        def body(t, carry):
            at = pl.ds(pl.multiple_of(t * tile, tile), tile)
            v = dot_nn(work[source, at, :], matrix(b, k)) + bias
            work[target, at, :] = store_layer(b, k, at, v, scale)
            return carry

        lax.fori_loop(0, tiles, body, 0)

    def grid(value):
        return value.astype(BF).reshape(ZN, YN, XN, 2, half_rows, -1)

    def head_grad(acc, lane, b):
        gp[b, 0, :, :, :, :, :, lane : lane + 128] = grid(acc[...].T)

    def backcast_step(b):
        def body(t, carry):
            at = pl.ds(pl.multiple_of(t * part_tile, part_tile), part_tile)
            theta = dot_nn(work[1, at, :], matrix(b, 4)).astype(BF)

            @pl.when(b == 0)
            def _():
                theta_keep[at, :] = theta
                backcast = dot_nn(theta, small(b, 256))
                resid[at, :] = (resid[at, :] - backcast) * mask[at, :].astype(F32)

            @pl.when(b == 1)
            def _():
                head_acc[...] += dot_nn(e_t[:, at], theta)

            return carry

        head_acc[...] = jnp.zeros_like(head_acc)
        lax.fori_loop(0, windows // part_tile, body, 0)
        pl.when(b == 1)(lambda: head_grad(head_acc, 256, b))

    def put_rows(buf, b, at, value):
        for row in range(value.shape[0]):
            buf[b, row, :, at] = value[row : row + 1]

    def forecast_step(b):
        def body(t, carry):
            at = pl.ds(pl.multiple_of(t * part_tile, part_tile), part_tile)
            theta = dot_nn(work[1, at, :], matrix(b, 5)).astype(BF)
            head_acc[...] += dot_nn(f_t[:, at], theta)
            part = dot_nn(theta, small(b, 128)).T[0:span]

            @pl.when(b == 0)
            def _():
                first_part[:, at] = part
                put_rows(pred, 0, at, part)

            @pl.when(b == 1)
            def _():
                put_rows(pred, 1, at, first_part[:, at].astype(BF).astype(F32) + part)

            return carry

        head_acc[...] = jnp.zeros_like(head_acc)
        lax.fori_loop(0, windows // part_tile, body, 0)
        head_grad(head_acc, 128, b)

    count = 2 * MATS

    def delayed(lag, t, step):
        pl.when(jnp.logical_and(t >= lag, t < count + lag))(lambda: step(t - lag))

    def gather_line(i):
        by_lanes(of(i)[1], lambda lanes: start_all(z_copies(i, lanes)))

    def gather_columns(i):
        def step(lanes):
            for copy in z_copies(i, lanes):
                copy.wait_recv()
            start_all(column_copies(i, lanes))

        by_lanes(of(i)[1], step)

    def gather_corner(i):
        def step(lanes):
            column_copies(i, lanes)[0].wait_recv()
            corner_copy(i, lanes).start()

        by_lanes(of(i)[1], step)

    def gather_core(i):
        def step(lanes):
            column_copies(i, lanes)[1].wait_recv()
            corner_copy(i, lanes).wait_recv()
            core_copy(i, lanes).start()

        by_lanes(of(i)[1], step)

    def forward_unit(i):
        b, m = of(i)
        by_lanes(m, lambda lanes: core_copy(i, lanes).wait_recv())
        pl.when(m == 0)(lambda: layer_zero(b))
        pl.when(jnp.logical_and(m >= 1, m <= 3))(lambda: layer_next(b, m))
        pl.when(m == 4)(lambda: backcast_step(b))
        pl.when(m == 5)(lambda: forecast_step(b))

        @pl.when(m == jnp.where(b == 1, 3, 5))
        def _():
            pl.when(b == 1)(lambda: feed_back(b))
            feed_forward(b)
            lax.fori_loop(jnp.where(b == 1, 4, 5), MATS, lambda n, carry: (weight_grad(b, n), carry)[1], 0)

            @pl.when(b == 1)
            def _():
                scatter_start(0)
                scatter_start(1)

    def gather_step(t, carry):
        delayed(4, t, gather_core)
        delayed(2, t, gather_corner)
        delayed(0, t, gather_columns)
        pl.when(t + 4 < count)(lambda: gather_line(t + 4))
        delayed(5, t, forward_unit)
        return carry

    def out_copies(buf, out, s):
        at = pl.ds(row0, windows)
        return [
            pltpu.make_async_copy(buf.at[core], out.at[:, :, at], local_sem.at[2 + s]),
            remote(buf.at[other], out.at[:, :, at], out_send.at[s], out_recv.at[s], sibling),
        ]


    def back_of(j):
        b = jnp.where(jnp.logical_or(j <= 1, jnp.logical_and(j >= 3, j <= 6)), 1, 0)
        m = jnp.where(j <= 1, 4 + j, jnp.where(j == 2, 5, jnp.where(j <= 6, 6 - j, jnp.where(j == 7, 4, 11 - j))))
        return b, m

    def to_core(j, lanes):
        b, m = back_of(j)
        return remote(
            gp.at[b, m, :, :, :, other, :, lanes], from_core.at[lax.rem(j, CORE_SLOTS), :, :, :, :, lanes],
            rs_send.at[j, 0], rs_recv.at[j, 0], sibling,
        )

    def to_far(j, lanes):
        b, m = back_of(j)
        device = chip(z, far_y, far_x)
        return [
            remote(
                gp.at[b, m, :, yo, xo, core, :, lanes], from_diag.at[lax.rem(j, DIAG_SLOTS), :, :, lanes],
                rs_send.at[j, 1], rs_recv.at[j, 1], device,
            ),
            remote(
                gp.at[b, m, :, far_y, far_x, core, :, lanes], from_plain.at[lax.rem(j, PLAIN_SLOTS), :, :, lanes],
                rs_send.at[j, 2], rs_recv.at[j, 2], device,
            ),
        ]

    def to_near(j, lanes):
        b, m = back_of(j)
        return remote(
            gp.at[b, m, :, near_y, near_x, core, :, lanes], from_pair.at[lax.rem(j, PAIR_SLOTS), :, :, lanes],
            rs_send.at[j, 3], rs_recv.at[j, 3], chip(z, near_y, near_x),
        )

    def to_z(j, lanes):
        b, m = back_of(j)
        return [
            remote(
                gp.at[b, m, zi, y, x, core, :, lanes], from_z.at[lax.rem(j, Z_SLOTS), s, :, lanes],
                rs_send.at[j, 4 + s], rs_recv.at[j, 4 + s], chip(zi, y, x),
            )
            for s, zi in enumerate(z_peers)
        ]

    def scatter_start(j):
        by_lanes(back_of(j)[1], lambda lanes: to_core(j, lanes).start())

    def scatter_core(j):
        b, m = back_of(j)

        def step(lanes):
            to_core(j, lanes).wait_recv()
            part = gp[b, m, :, :, :, core, :, lanes] + from_core[lax.rem(j, CORE_SLOTS), :, :, :, :, lanes]
            gp[b, m, :, :, :, core, :, lanes] = part
            start_all(to_far(j, lanes))

        by_lanes(m, step)

    def scatter_diag(j):
        b, m = back_of(j)

        def step(lanes):
            to_far(j, lanes)[0].wait_recv()
            part = gp[b, m, :, near_y, near_x, core, :, lanes] + from_diag[lax.rem(j, DIAG_SLOTS), :, :, lanes]
            gp[b, m, :, near_y, near_x, core, :, lanes] = part
            to_near(j, lanes).start()

        by_lanes(m, step)

    def scatter_plane(j):
        b, m = back_of(j)

        def step(lanes):
            to_far(j, lanes)[1].wait_recv()
            to_near(j, lanes).wait_recv()
            value = gp[b, m, :, y, x, core, :, lanes].astype(F32)
            value = value + from_plain[lax.rem(j, PLAIN_SLOTS), :, :, lanes].astype(F32)
            value = value + from_pair[lax.rem(j, PAIR_SLOTS), :, :, lanes].astype(F32)
            gp[b, m, :, y, x, core, :, lanes] = value.astype(BF)
            start_all(to_z(j, lanes))

        by_lanes(m, step)

    def scatter_z(j):
        b, m = back_of(j)

        def step(lanes):
            for copy in to_z(j, lanes):
                copy.wait_recv()
            value = gp[b, m, z, y, x, core, :, lanes].astype(F32)
            for s in range(ZN - 1):
                value = value + from_z[lax.rem(j, Z_SLOTS), s, :, lanes].astype(F32)
            total[b, m, :, lanes] = value
            squares[:, lanes] = squares[:, lanes] + value * value

        by_lanes(m, step)

    def add_rows(value):
        return jnp.sum(value.reshape(-1, 8, hidden), axis=0)

    def put_bias(k, acc):
        bias_sum[pl.ds(span + k, 1), :] = jnp.sum(acc, axis=0, keepdims=True)

    def feed_back(b):
        def body(t, carry):
            at = pl.ds(pl.multiple_of(t * tile, tile), tile)

            @pl.when(b == 1)
            def _():
                resid[at, :] = jnp.zeros((tile, 128), F32)

            e = (-(resid[at, :] * mask[at, :].astype(F32))).astype(BF)
            e_t[:, at] = e.T
            work[0, at, :] = dot_nt(e, small(b, 256)).astype(BF)
            return carry

        lax.fori_loop(0, tiles, body, 0)

    def feed_forward(b):
        def body(t, carry):
            at = pl.ds(pl.multiple_of(t * tile, tile), tile)
            work[2, at, :] = dot_nt(f_ref[at, :], small(b, 128)).astype(BF)
            return carry

        lax.fori_loop(0, tiles, body, 0)

    def theta_step(b):
        def body(t, acc):
            at = pl.ds(pl.multiple_of(t * tile, tile), tile)
            da = dot_nt(work[0, at, :], matrix(b, 4)) + dot_nt(work[2, at, :], matrix(b, 5))
            dz = da * slope[b, 3, at, :].astype(F32)
            work[1, at, :] = dz.astype(BF)
            return acc + add_rows(dz)

        put_bias(3, lax.fori_loop(0, tiles, body, jnp.zeros((8, hidden), F32)))

    def layer_back(b, k):
        source, target = lax.rem(k + 1, 2), lax.rem(k, 2)

        def body(t, acc):
            at = pl.ds(pl.multiple_of(t * tile, tile), tile)
            dz = dot_nt(work[source, at, :], matrix(b, k + 1)) * slope[b, k, at, :].astype(F32)
            work[target, at, :] = dz.astype(BF)
            return acc + add_rows(dz)

        put_bias(k, lax.fori_loop(0, tiles, body, jnp.zeros((8, hidden), F32)))

    def weight_grad(b, m):
        layer = jnp.where(m >= 4, 3, m - 1)
        slot = jnp.where(m == 4, 0, jnp.where(m == 5, 2, lax.rem(m, 2)))
        gp[b, m] = grid(dot_nn(act_t[b, layer], work[slot]))

    def small_grads(b):
        gp[b, 0, :, :, :, :, :, 0:128] = grid(dot_nn(in_t[b], work[0]).T)
        gp[b, 0, :, :, :, :, :, 128:256] = gp[b, 0, :, :, :, :, :, 128:256] + grid(bias_sum[...].T)

        @pl.when(b == 0)
        def _():
            head_acc[...] = dot_nn(e_t[...], theta_keep[...])
            head_grad(head_acc, 256, b)


    def input_grad(b):
        def body(t, carry):
            at = pl.ds(pl.multiple_of(t * tile, tile), tile)
            keep = mask[at, :].astype(F32)
            dr = resid[at, :] * keep + 2.0 * dot_nn(work[0, at, :], small(b, 0))

            @pl.when(b == 1)
            def _():
                put_rows(sens, 1, at, dr.T[0:past])
                resid[at, :] = dr.astype(BF).astype(F32)

            @pl.when(b == 0)
            def _():
                put_rows(sens, 0, at, (dr * keep).T[0:past])

            return carry

        lax.fori_loop(0, tiles, body, 0)

    bias_sum[...] = jnp.zeros_like(bias_sum)
    squares[...] = jnp.zeros_like(squares)
    total[...] = jnp.zeros_like(total)

    def back_step(j, carry):
        b, m = back_of(j)
        live = jnp.logical_and(j >= 3, j < count)

        def on(test, step):
            pl.when(jnp.logical_and(live, test))(step)

        @pl.when(j == 7)
        def _():
            feed_back(b)
            feed_forward(b)

        on(m == 3, lambda: theta_step(b))
        on(m <= 2, lambda: layer_back(b, m))
        delayed(8, j, scatter_z)
        delayed(6, j, scatter_plane)
        delayed(4, j, scatter_diag)
        delayed(2, j, scatter_core)
        on(m >= 1, lambda: weight_grad(b, m))
        on(m == 0, lambda: small_grads(b))
        pl.when(jnp.logical_and(j >= 2, j < count))(lambda: scatter_start(j))
        on(m == 0, lambda: input_grad(b))
        pl.when(j == count - 1)(lambda: start_all(out_copies(sens, sens_out, 1)))
        return carry

    own.wait_recv()
    for i in range(4):
        gather_line(i)
    lax.fori_loop(0, tiles, prepare, 0)
    pad[...] = jnp.zeros_like(pad)
    lax.fori_loop(0, windows // 128, prepare_mask, 0)
    lax.fori_loop(0, count + 5, gather_step, 0)

    start_all(out_copies(pred, pred_out, 0))
    lax.fori_loop(0, count + 8, back_step, 0)

    grad_copy = remote(total.at[other], grad_out.at[:, core], out_send.at[2], out_recv.at[2], sibling)
    grad_copy.start()
    grad_out[:, core] = total[core]
    sq = squares[:, 0:128] + squares[:, 128:256] + squares[:, 256:384] + squares[:, 384:512]
    norm_buf[0] = sq[0:8] + sq[8:16]
    for step, device in enumerate([sibling, chip(z, y, xo), chip(z, yo, x)]):
        copy = remote(norm_buf.at[2 * step], norm_buf.at[2 * step + 1], norm_send.at[step], norm_recv.at[step], device)
        copy.start()
        copy.wait()
        norm_buf[2 * step + 2] = norm_buf[2 * step] + norm_buf[2 * step + 1]
    norm_buf[7 + z] = norm_buf[6]
    spread = [
        remote(norm_buf.at[6], norm_buf.at[7 + z], norm_send.at[3 + s], norm_recv.at[3 + s], chip(zi, y, x))
        for s, zi in enumerate(z_peers)
    ]
    start_all(spread)
    for copy in spread:
        copy.wait()
    everything = norm_buf[7]
    for zi in range(1, ZN):
        everything = everything + norm_buf[7 + zi]
    norm_out[...] = jnp.broadcast_to(jnp.sqrt(jnp.sum(everything, keepdims=True)), norm_out.shape)

    grad_copy.wait()
    for buf, out, s in ((pred, pred_out, 0), (sens, sens_out, 1)):
        for copy in out_copies(buf, out, s):
            copy.wait()
    own.wait_send()

    def drain(i, carry):
        def gathered(lanes):
            for copy in [*z_copies(i, lanes), *column_copies(i, lanes), corner_copy(i, lanes), core_copy(i, lanes)]:
                copy.wait_send()

        def scattered(lanes):
            for copy in [to_core(i, lanes), *to_far(i, lanes), to_near(i, lanes), *to_z(i, lanes)]:
                copy.wait_send()

        by_lanes(of(i)[1], gathered)
        by_lanes(back_of(i)[1], scattered)
        return carry

    lax.fori_loop(0, count, drain, 0)


def train_call(plane, segments, extents, adjoint, first, square, head, biases):
    ZN, YN, XN = plane
    past, span, hidden = segments.shape[1], adjoint.shape[0], square.shape[3]
    windows = segments.shape[0] // 2
    tile = windows // 3
    half = hidden // (ZN * YN * XN) // 2
    sizes = (ZN, YN, XN, windows, tile, past, span, hidden)
    DMA = pltpu.SemaphoreType.DMA
    vmem = pl.BlockSpec(memory_space=pltpu.VMEM)
    hbm = pl.BlockSpec(memory_space=pl.ANY)
    count = 2 * MATS
    flops = 2 * 2 * 3 * windows * hidden * (6 * hidden + 2 * 128)
    return pl.pallas_call(
        functools.partial(train_kernel, sizes),
        out_shape=(
            jax.ShapeDtypeStruct((span, 1, 2 * windows), F32),
            jax.ShapeDtypeStruct((past, 1, 2 * windows), F32),
            jax.ShapeDtypeStruct((MATS, 2, half, hidden), F32),
            jax.ShapeDtypeStruct((8, 128), F32),
        ),
        in_specs=[hbm, hbm] + [vmem] * 5,
        out_specs=(hbm, hbm, vmem, vmem),
        scratch_shapes=[
            pltpu.VMEM((2, MATS, ZN, YN, XN, 2, half, hidden), BF),
            pltpu.VMEM((MATS, half, hidden), BF),
            pltpu.VMEM((2, MATS, ZN, YN, XN, 2, half, hidden), BF),
            pltpu.VMEM((CORE_SLOTS, ZN, YN, XN, half, hidden), BF),
            pltpu.VMEM((DIAG_SLOTS, ZN, half, hidden), BF),
            pltpu.VMEM((PLAIN_SLOTS, ZN, half, hidden), BF),
            pltpu.VMEM((PAIR_SLOTS, ZN, half, hidden), BF),
            pltpu.VMEM((Z_SLOTS, ZN - 1, half, hidden), BF),
            pltpu.VMEM((2, MATS, half, hidden), F32),
            pltpu.VMEM((2, 4, hidden, windows), BF),
            pltpu.VMEM((2, 128, windows), BF),
            pltpu.VMEM((windows, hidden), BF),
            pltpu.VMEM((128, hidden), F32),
            pltpu.VMEM((2, 4, windows, hidden), BF),
            pltpu.VMEM((3, windows, hidden), BF),
            pltpu.VMEM((windows, 128), F32),
            pltpu.VMEM((windows, 128), BF),
            pltpu.VMEM((windows, 128), BF),
            pltpu.VMEM((128, windows), BF),
            pltpu.VMEM((128, windows), BF),
            pltpu.VMEM((128, hidden), F32),
            pltpu.VMEM((128, hidden), F32),
            pltpu.VMEM((128, 128), F32),
            pltpu.VMEM((windows, past), F32),
            pltpu.VMEM((span, windows), F32),
            pltpu.VMEM((span, windows), F32),
            pltpu.VMEM((2, span, 1, windows), F32),
            pltpu.VMEM((2, past, 1, windows), F32),
            pltpu.VMEM((half, hidden), F32),
            pltpu.VMEM((7 + ZN, 8, 128), F32),
            DMA((1,)),
            DMA((1,)),
            DMA((count, 7)),
            DMA((count, 7)),
            DMA((count, 4 + ZN - 1)),
            DMA((count, 4 + ZN - 1)),
            DMA((3,)),
            DMA((3,)),
            DMA((4,)),
            DMA((3 + ZN - 1,)),
            DMA((3 + ZN - 1,)),
        ],
        compiler_params=pltpu.CompilerParams(
            collective_id=0, has_side_effects=True, vmem_limit_bytes=64 * 1024 * 1024
        ),
        cost_estimate=pl.CostEstimate(flops=flops, bytes_accessed=8_000_000, transcendentals=8 * windows * hidden),
        name="train",
    )(segments, adjoint, extents.reshape(-1, 128), first, square, head, biases)


def update_kernel(past, span, prediction, sensitivity, grads, norm, *refs):
    masters, momenta, variances, outs = refs[0:4], refs[4:8], refs[8:12], refs[12:28]
    norm_out, prediction_out, sensitivity_out, pad, prediction_held, sensitivity_held, sems = refs[28:]
    arriving = [
        pltpu.make_async_copy(sensitivity, sensitivity_held, sems.at[0]),
        pltpu.make_async_copy(prediction, prediction_held, sems.at[1]),
    ]
    leaving = [
        pltpu.make_async_copy(sensitivity_held, sensitivity_out, sems.at[2]),
        pltpu.make_async_copy(prediction_held, prediction_out, sems.at[3]),
    ]
    for copy in arriving:
        copy.start()
    norm_out[...] = norm[0:1, 0:1]
    factor = 1.0 / jnp.maximum(norm[0:1, 0:1], 1.0)
    units = masters[3].shape[2]

    def rows(m, lane, width):
        return grads[m, :, :, lane : lane + width].reshape(units, width)

    forecast = rows(0, 128, 128)
    pad[...] = jnp.zeros_like(pad)
    outs[0][0] = rows(0, 0, 128)[:, 0:past]
    pad[0:units, :] = forecast
    outs[3][0] = pad[...].T[span : span + 4, 0:units]
    for m in range(5):
        outs[1][0, m] = rows(m + 1, 0, grads.shape[3])
    outs[2][0, :, 0:past] = rows(0, 256, 128)[:, 0:past]
    outs[2][0, :, past : past + span] = forecast[:, 0:span]
    for before, after in zip(arriving, leaving):
        before.wait()
        after.start()
    for n in range(4):
        master, gradient = masters[n][...], outs[n][...]
        new, moment, spread = adamw(master, gradient, momenta[n][...], variances[n][...], factor[None])
        outs[4 + n][...], outs[8 + n][...], outs[12 + n][...] = new, moment, spread
    for copy in leaving:
        copy.wait()


def update_call(prediction, sensitivity, grads, norm, state):
    vmem, hbm = pl.BlockSpec(memory_space=pltpu.VMEM), pl.BlockSpec(memory_space=pl.ANY)
    shapes = tuple(jax.ShapeDtypeStruct(a.shape, F32) for a in state[:4])
    passed = tuple(jax.ShapeDtypeStruct(a.shape, F32) for a in (prediction, sensitivity))
    return pl.pallas_call(
        functools.partial(update_kernel, sensitivity.shape[0], prediction.shape[0]),
        out_shape=4 * shapes + (jax.ShapeDtypeStruct((1, 1), F32),) + passed,
        in_specs=[hbm, hbm] + [vmem] * (2 + len(state)),
        out_specs=tuple([vmem] * 17 + [hbm, hbm]),
        scratch_shapes=[
            pltpu.VMEM((128, 128), F32),
            pltpu.VMEM(prediction.shape, F32),
            pltpu.VMEM(sensitivity.shape, F32),
            pltpu.SemaphoreType.DMA((4,)),
        ],
        name="update",
    )(prediction, sensitivity, grads, norm, *state)


def turned(arrays):
    return [a.transpose(0, 2, 1) if n % 4 == 0 else a for n, a in enumerate(arrays)]


def kernel_shards(plane, segments, extents, adjoint, *state):
    state = turned(state)
    results = train_call(plane, segments, extents, adjoint.T, *state[:4])
    *updated, norm, prediction, sensitivity = update_call(*results, state)
    by_window = (prediction.transpose(1, 2, 0), sensitivity.transpose(1, 2, 0))
    return (*by_window, norm.reshape(()), *turned(updated))


STATE_SPECS = (
    P("section", None, "dp"),
    P("section", None, "dp", None),
    P("section", "dp", None),
    P("section", None, "dp"),
)


def solution(mesh):
    in_specs = (P("dp", None), P("dp"), P("dp", None)) + 3 * STATE_SPECS
    out_specs = (P("section", "dp", None), P("section", "dp", None), P()) + 4 * STATE_SPECS
    plane = PLANES.get(mesh.shape["dp"])
    shards = plain_shards if plane is None else functools.partial(kernel_shards, plane)
    return jax.shard_map(shards, mesh=mesh, in_specs=in_specs, out_specs=out_specs, check_vma=False)
```

```python
import functools

import jax
import jax.numpy as jnp
from jax import lax
from jax.experimental import pallas as pl
from jax.experimental.pallas import tpu as pltpu
from jax.sharding import PartitionSpec as P

STEP = 10


def dot_nn(a, b):
    return jnp.dot(a, b, preferred_element_type=jnp.float32)


def dot_tn(a, b):
    return lax.dot_general(a, b, (((0,), (0,)), ((), ())), preferred_element_type=jnp.float32)


def dot_nt(a, b):
    return lax.dot_general(a, b, (((1,), (1,)), ((), ())), preferred_element_type=jnp.float32)


def unit_rows(first, square, head, biases):
    units = first.shape[1]
    return jnp.concatenate(
        [square.transpose(1, 0, 2).reshape(units, -1), first.T, head, biases.T], axis=1
    )


def from_unit_rows(rows, past, hidden, out):
    wide = 5 * hidden
    square = rows[:, :wide].reshape(-1, 5, hidden).transpose(1, 0, 2)
    first = rows[:, wide : wide + past].T
    head = rows[:, wide + past : wide + past + out]
    biases = rows[:, wide + past + out :].T
    return first, square, head, biases


def plain_forward(weights, resid):
    first, square, head, biases = weights
    past = resid.shape[1]
    acts, slopes = [resid.astype(jnp.bfloat16)], []
    for k in range(4):
        z = dot_nn(acts[-1], first if k == 0 else square[k - 1]) + biases[k].astype(jnp.float32)
        sig = jax.nn.sigmoid(z)
        acts.append((z * sig).astype(jnp.bfloat16))
        slopes.append(sig * (1.0 + z * (1.0 - sig)))
    theta_b = dot_nn(acts[4], square[3]).astype(jnp.bfloat16)
    theta_f = dot_nn(acts[4], square[4]).astype(jnp.bfloat16)
    backcast = dot_nn(theta_b, head[:, :past])
    part = dot_nn(theta_f, head[:, past:])
    return backcast, part, (acts, slopes, theta_b, theta_f)


def plain_backward(weights, saved, e, f):
    first, square, head, biases = weights
    acts, slopes, theta_b, theta_f = saved
    past = e.shape[1]
    head_grad = jnp.concatenate([dot_tn(theta_b, e), dot_tn(theta_f, f)], axis=1)
    u_b = dot_nt(e, head[:, :past]).astype(jnp.bfloat16)
    u_f = dot_nt(f, head[:, past:]).astype(jnp.bfloat16)
    squares = [None, None, None, dot_tn(acts[4], u_b), dot_tn(acts[4], u_f)]
    da = dot_nt(u_b, square[3]) + dot_nt(u_f, square[4])
    bias_grads = [None] * 4
    first_grad = None
    for k in (3, 2, 1, 0):
        dz = (da * slopes[k]).astype(jnp.bfloat16)
        bias_grads[k] = jnp.sum(dz, axis=0, dtype=jnp.float32)
        grad = dot_tn(acts[k], dz)
        if k == 0:
            first_grad = grad
        else:
            squares[k - 1] = grad
        da = dot_nt(dz, first if k == 0 else square[k - 1])
    return da, (first_grad, jnp.stack(squares), head_grad, jnp.stack(bias_grads))


def adamw(master, gradient, momentum, variance, factor):
    clipped = gradient * factor
    moment_new = 0.9 * momentum + 0.1 * clipped
    variance_new = 0.999 * variance + 0.001 * clipped * clipped
    ratio = moment_new / (1.0 - 0.9**STEP) / (jnp.sqrt(variance_new / (1.0 - 0.999**STEP)) + 1e-08)
    return master - 0.05 * (ratio + 0.01 * master), moment_new, variance_new


def plain_shards(segments, extents, adjoint, *state):
    masters, momenta, variances = state[:4], state[4:8], state[8:]
    core = lax.axis_index("section")
    past, span = segments.shape[1], adjoint.shape[1]
    windows = segments.shape[0] // 2
    hidden = masters[1].shape[3]
    mine = [
        lax.dynamic_slice_in_dim(v, core * windows, windows, 0) for v in (segments, extents, adjoint)
    ]
    seg, ext, adj = mine
    rows = unit_rows(*(m[0].astype(jnp.bfloat16) for m in masters))
    rows = lax.all_gather(rows, "dp", axis=0, tiled=True)
    rows = lax.all_gather(rows, "section", axis=0)
    blocks = [from_unit_rows(rows[b], past, hidden, past + span) for b in range(2)]
    mask = (
        lax.broadcasted_iota(jnp.int32, (windows, past), 1) >= past - ext[:, None]
    ).astype(jnp.float32)
    r0 = seg * mask
    backcast, part0, saved0 = plain_forward(blocks[0], r0)
    r1 = (r0 - backcast) * mask
    _, part1, saved1 = plain_forward(blocks[1], r1)
    forecast = part0.astype(jnp.bfloat16).astype(jnp.float32) + part1
    f = adj.astype(jnp.bfloat16)
    zero = jnp.zeros_like(r0)
    da1, grads1 = plain_backward(blocks[1], saved1, (-(zero * mask)).astype(jnp.bfloat16), f)
    dr1 = zero * mask + da1
    t = dr1.astype(jnp.bfloat16).astype(jnp.float32)
    da0, grads0 = plain_backward(blocks[0], saved0, (-(t * mask)).astype(jnp.bfloat16), f)
    dr0 = (t * mask + da0) * mask

    def by_section(first_block, second_block):
        mine, other = (
            jnp.where(core == 0, first_block, second_block),
            jnp.where(core == 0, second_block, first_block),
        )
        got = lax.ppermute(other, "section", [(0, 1), (1, 0)])
        return jnp.where(
            core == 0, jnp.concatenate([mine, got]), jnp.concatenate([got, mine])
        )[None]

    prediction = by_section(part0, forecast)
    sensitivity = by_section(dr0, dr1)
    packed = jnp.stack([unit_rows(*grads0), unit_rows(*grads1)])
    packed = lax.psum_scatter(packed, "section", scatter_dimension=0, tiled=False)
    packed = lax.psum_scatter(packed, "dp", scatter_dimension=0, tiled=True)
    norm = jnp.sqrt(lax.psum(jnp.sum(packed * packed), ("section", "dp")))
    factor = 1.0 / jnp.maximum(norm, 1.0)
    summed = [g[None] for g in from_unit_rows(packed, past, hidden, past + span)]
    updated = [adamw(*four, factor) for four in zip(masters, summed, momenta, variances)]
    return (
        prediction,
        sensitivity,
        norm,
        *summed,
        *(u[0] for u in updated),
        *(u[1] for u in updated),
        *(u[2] for u in updated),
    )


PLANES = {16: (4, 2, 2)}
MESH = pl.DeviceIdType.MESH
MATS = 6
CORE_SLOTS, DIAG_SLOTS, PLAIN_SLOTS, PAIR_SLOTS, Z_SLOTS = 4, 4, 6, 4, 4
BF, F32 = jnp.bfloat16, jnp.float32


def remote(src, dst, send_sem, recv_sem, device):
    return pltpu.make_async_remote_copy(
        src_ref=src, dst_ref=dst, send_sem=send_sem, recv_sem=recv_sem, device_id=device, device_id_type=MESH
    )


def train_kernel(
    sizes,
    seg_hbm, adj_hbm, ext, first, square, head, biases,
    pred_out, sens_out, grad_out, norm_out,
    wg, handed, gp, from_core, from_diag, from_plain, from_pair, from_z, total,
    act_t, in_t, theta_keep, head_acc, slope, work, resid, mask, f_t, e_t, turn, turn_small, bias, bias_acc, bias_grad, pad,
    seg, adj, first_part, pred, sens, squares, norm_buf,
    own_send, own_recv, ag_send, ag_recv, rs_send, rs_recv, out_send, out_recv, local_sem, norm_send, norm_recv,
):
    ZN, YN, XN, windows, chunk, past, span, hidden = sizes
    units = ZN * YN * XN
    core, dp = lax.axis_index("section"), lax.axis_index("dp")
    x, y, z = lax.rem(dp, XN), lax.rem(lax.div(dp, XN), YN), lax.div(dp, XN * YN)
    other, xo, yo = 1 - core, 1 - x, 1 - y
    near_y, near_x = y + core * (yo - y), xo + core * (x - xo)
    far_y, far_x = yo + core * (y - yo), x + core * (xo - x)

    def chip(zi, yi, xi):
        return (core, (zi * YN + yi) * XN + xi)

    sibling = (other, dp)
    z_peers = [lax.rem(z + step, ZN) for step in range(1, ZN)]

    row0 = core * windows
    loads = [
        pltpu.make_async_copy(seg_hbm.at[pl.ds(row0, windows), :], seg, local_sem.at[0]),
        pltpu.make_async_copy(adj_hbm.at[:, pl.ds(row0, windows)], adj, local_sem.at[1]),
    ]
    for load in loads:
        load.start()

    barrier = pltpu.get_barrier_semaphore()
    peers = [sibling, chip(z, y, xo), chip(z, yo, x)] + [chip(zi, y, x) for zi in z_peers]
    for peer in peers:
        pl.semaphore_signal(barrier, inc=1, device_id=peer, device_id_type=MESH)

    rows = hidden // units
    half_rows = rows // 2

    def put_own(m, value, lanes):
        halves = value.astype(BF).reshape(2, half_rows, -1)
        for h in range(2):
            pl.when(core == h)(functools.partial(put_half, m, halves[h], halves[1 - h], lanes))

    def put_half(m, kept, given, lanes):
        wg[core, m, z, y, x, core, :, lanes] = kept
        handed[m, :, lanes] = given

    pad[...] = jnp.zeros_like(pad)
    pad[0:rows, 0:past] = first[0] * 0.5
    put_own(0, pad[0:rows, :], slice(0, 128))
    pad[...] = jnp.zeros_like(pad)
    pad[span : span + 4, 0:rows] = biases[0] * 0.5
    bias_cols = pad[...].T[0:rows]
    pad[...] = jnp.zeros_like(pad)
    pad[0:rows, 0:span] = head[0, :, past : past + span]
    put_own(0, pad[0:rows, :] + bias_cols, slice(128, 256))
    pad[...] = jnp.zeros_like(pad)
    pad[0:rows, 0:past] = head[0, :, 0:past]
    put_own(0, pad[0:rows, :], slice(256, 384))
    for m in range(5):
        put_own(m + 1, square[0, m] * 0.5 if m < 3 else square[0, m], slice(0, hidden))
    pl.semaphore_wait(barrier, len(peers))

    handed[0, :, 384:512] = jnp.zeros((half_rows, 128), BF)
    own = remote(handed, wg.at[core, :, z, y, x, other], own_send.at[0], own_recv.at[0], sibling)
    own.start()

    def of(i):
        return lax.div(i, MATS), lax.rem(i, MATS)

    def z_copies(i, lanes):
        b, m = of(i)
        part = wg.at[b, m, z, y, x, core, :, lanes]
        return [
            remote(part, part, ag_send.at[i, s], ag_recv.at[i, s], chip(zi, y, x)) for s, zi in enumerate(z_peers)
        ]

    def column_copies(i, lanes):
        b, m = of(i)
        part = wg.at[b, m, :, y, x, core, :, lanes]
        return [
            remote(part, part, ag_send.at[i, 3], ag_recv.at[i, 3], chip(z, near_y, near_x)),
            remote(part, part, ag_send.at[i, 4], ag_recv.at[i, 4], chip(z, far_y, far_x)),
        ]

    def corner_copy(i, lanes):
        b, m = of(i)
        part = wg.at[b, m, :, near_y, near_x, core, :, lanes]
        return remote(part, part, ag_send.at[i, 5], ag_recv.at[i, 5], chip(z, far_y, far_x))

    def core_copy(i, lanes):
        b, m = of(i)
        part = wg.at[b, m, :, :, :, core, :, lanes]
        return remote(part, part, ag_send.at[i, 6], ag_recv.at[i, 6], sibling)

    def by_lanes(m, step):
        pl.when(m == 0)(lambda: step(slice(0, 384)))
        pl.when(m > 0)(lambda: step(slice(0, hidden)))

    def start_all(copies):
        for copy in copies:
            copy.start()

    for load in loads:
        load.wait()

    def prepare():
        resid[...] = jnp.zeros_like(resid)
        resid[0:span, :] = adj[...]
        f_t[...] = resid[...].astype(BF)
        pad[...] = jnp.zeros_like(pad)
        for g in range(windows // 128):
            at = slice(g * 128, (g + 1) * 128)
            lengths = ext[pl.ds(core * (windows // 128) + g, 1), :]
            position = lax.broadcasted_iota(jnp.int32, (128, 128), 0)
            keep = jnp.where(position >= past - lengths, 1.0, 0.0).astype(F32)
            pad[:, 0:past] = seg[at, :]
            mask[:, at] = keep.astype(BF)
            resid[:, at] = pad[...].T * keep

    def each_chunk(body):
        for t in range(windows // chunk):
            body(slice(t * chunk, (t + 1) * chunk))

    def matrix(b, m):
        return wg[b, m].reshape(hidden, hidden)

    def small(b, lane):
        return wg[b, 0, :, :, :, :, :, lane : lane + 128].reshape(hidden, 128)

    def wide(column):
        return jnp.concatenate([column] * (chunk // 128), axis=1)

    def store_layer(b, k, at, v, scale):
        p = 1.0 + jnp.tanh(v)
        a = v * p
        rate = p + a * (2.0 - p)
        slope[b, k, :, at] = (rate if scale is None else rate * scale).astype(BF)
        act_t[b, k, :, at] = a.astype(BF)

    def layer_zero(b):
        columns = small(b, 128).astype(F32)
        for k in range(4):
            bias[k] = jnp.broadcast_to(columns[:, span + k : span + k + 1], (hidden, 128))

        def body(at):
            a = resid[:, at].astype(BF)
            in_t[b, :, at] = a
            store_layer(b, 0, at, dot_nn(small(b, 0), a) + wide(bias[0]), None)

        each_chunk(body)

    def layer_next(b, k):
        scale = jnp.where(k == 3, 0.5, 1.0)
        turn[...] = matrix(b, k).T

        def body(at):
            store_layer(b, k, at, dot_nn(turn[...], act_t[b, k - 1, :, at]) + wide(bias[k]), scale)

        each_chunk(body)

    def grid(value):
        return value.astype(BF).reshape(ZN, YN, XN, 2, half_rows, -1)

    def put_head(b, lane):
        gp[b, 0, :, :, :, :, :, lane : lane + 128] = grid(head_acc[...])

    def backcast_step(b):
        turn[...] = matrix(b, 4).T
        turn_small[...] = small(b, 256).T
        head_acc[...] = jnp.zeros_like(head_acc)

        def body(at):
            theta = dot_nn(turn[...], act_t[b, 3, :, at]).astype(BF)

            @pl.when(b == 0)
            def _():
                theta_keep[:, at] = theta
                resid[:, at] = (resid[:, at] - dot_nn(turn_small[...], theta)) * mask[:, at].astype(F32)

            @pl.when(b == 1)
            def _():
                head_acc[...] += dot_nt(theta, e_t[:, at])

        each_chunk(body)
        pl.when(b == 1)(lambda: put_head(b, 256))

    def put_rows(buf, b, at, value):
        for row in range(value.shape[0]):
            buf[b, row, :, at] = value[row : row + 1]

    def forecast_step(b):
        turn[...] = matrix(b, 5).T
        turn_small[...] = small(b, 128).T
        head_acc[...] = jnp.zeros_like(head_acc)

        def body(at):
            theta = dot_nn(turn[...], act_t[b, 3, :, at]).astype(BF)
            head_acc[...] += dot_nt(theta, f_t[:, at])
            part = dot_nn(turn_small[...], theta)[0:span]

            @pl.when(b == 0)
            def _():
                first_part[:, at] = part
                put_rows(pred, 0, at, part)

            @pl.when(b == 1)
            def _():
                put_rows(pred, 1, at, first_part[:, at].astype(BF).astype(F32) + part)

        each_chunk(body)
        put_head(b, 128)

    count = 2 * MATS

    def delayed(lag, t, step):
        pl.when(jnp.logical_and(t >= lag, t < count + lag))(lambda: step(t - lag))

    def gather_line(i):
        by_lanes(of(i)[1], lambda lanes: start_all(z_copies(i, lanes)))

    def gather_columns(i):
        def step(lanes):
            for copy in z_copies(i, lanes):
                copy.wait_recv()
            start_all(column_copies(i, lanes))

        by_lanes(of(i)[1], step)

    def gather_corner(i):
        def step(lanes):
            column_copies(i, lanes)[0].wait_recv()
            corner_copy(i, lanes).start()

        by_lanes(of(i)[1], step)

    def gather_core(i):
        def step(lanes):
            column_copies(i, lanes)[1].wait_recv()
            corner_copy(i, lanes).wait_recv()
            core_copy(i, lanes).start()

        by_lanes(of(i)[1], step)

    def forward_unit(i):
        b, m = of(i)
        by_lanes(m, lambda lanes: core_copy(i, lanes).wait_recv())
        pl.when(m == 0)(lambda: layer_zero(b))
        pl.when(jnp.logical_and(m >= 1, m <= 3))(lambda: layer_next(b, m))
        pl.when(m == 4)(lambda: backcast_step(b))
        pl.when(m == 5)(lambda: forecast_step(b))

        @pl.when(m == jnp.where(b == 1, 3, 5))
        def _():
            pl.when(b == 1)(lambda: feed_back(b))
            feed_forward(b)
            lax.fori_loop(jnp.where(b == 1, 4, 5), MATS, lambda n, carry: (weight_grad(b, n), carry)[1], 0)

            @pl.when(b == 1)
            def _():
                scatter_start(0)
                scatter_start(1)

    def gather_step(t, carry):
        delayed(4, t, gather_core)
        delayed(2, t, gather_corner)
        delayed(0, t, gather_columns)
        pl.when(t + 4 < count)(lambda: gather_line(t + 4))
        delayed(5, t, forward_unit)
        return carry

    def out_copies(buf, out, s):
        at = pl.ds(row0, windows)
        return [
            pltpu.make_async_copy(buf.at[core], out.at[:, :, at], local_sem.at[2 + s]),
            remote(buf.at[other], out.at[:, :, at], out_send.at[s], out_recv.at[s], sibling),
        ]


    def back_of(j):
        b = jnp.where(jnp.logical_or(j <= 1, jnp.logical_and(j >= 3, j <= 6)), 1, 0)
        m = jnp.where(j <= 1, 4 + j, jnp.where(j == 2, 5, jnp.where(j <= 6, 6 - j, jnp.where(j == 7, 4, 11 - j))))
        return b, m

    def to_core(j, lanes):
        b, m = back_of(j)
        return remote(
            gp.at[b, m, :, :, :, other, :, lanes], from_core.at[lax.rem(j, CORE_SLOTS), :, :, :, :, lanes],
            rs_send.at[j, 0], rs_recv.at[j, 0], sibling,
        )

    def to_far(j, lanes):
        b, m = back_of(j)
        device = chip(z, far_y, far_x)
        return [
            remote(
                gp.at[b, m, :, yo, xo, core, :, lanes], from_diag.at[lax.rem(j, DIAG_SLOTS), :, :, lanes],
                rs_send.at[j, 1], rs_recv.at[j, 1], device,
            ),
            remote(
                gp.at[b, m, :, far_y, far_x, core, :, lanes], from_plain.at[lax.rem(j, PLAIN_SLOTS), :, :, lanes],
                rs_send.at[j, 2], rs_recv.at[j, 2], device,
            ),
        ]

    def to_near(j, lanes):
        b, m = back_of(j)
        return remote(
            gp.at[b, m, :, near_y, near_x, core, :, lanes], from_pair.at[lax.rem(j, PAIR_SLOTS), :, :, lanes],
            rs_send.at[j, 3], rs_recv.at[j, 3], chip(z, near_y, near_x),
        )

    def to_z(j, lanes):
        b, m = back_of(j)
        return [
            remote(
                gp.at[b, m, zi, y, x, core, :, lanes], from_z.at[lax.rem(j, Z_SLOTS), s, :, lanes],
                rs_send.at[j, 4 + s], rs_recv.at[j, 4 + s], chip(zi, y, x),
            )
            for s, zi in enumerate(z_peers)
        ]

    def scatter_start(j):
        by_lanes(back_of(j)[1], lambda lanes: to_core(j, lanes).start())

    def scatter_core(j):
        b, m = back_of(j)

        def step(lanes):
            to_core(j, lanes).wait_recv()
            part = gp[b, m, :, :, :, core, :, lanes] + from_core[lax.rem(j, CORE_SLOTS), :, :, :, :, lanes]
            gp[b, m, :, :, :, core, :, lanes] = part
            start_all(to_far(j, lanes))

        by_lanes(m, step)

    def scatter_diag(j):
        b, m = back_of(j)

        def step(lanes):
            to_far(j, lanes)[0].wait_recv()
            part = gp[b, m, :, near_y, near_x, core, :, lanes] + from_diag[lax.rem(j, DIAG_SLOTS), :, :, lanes]
            gp[b, m, :, near_y, near_x, core, :, lanes] = part
            to_near(j, lanes).start()

        by_lanes(m, step)

    def scatter_plane(j):
        b, m = back_of(j)

        def step(lanes):
            to_far(j, lanes)[1].wait_recv()
            to_near(j, lanes).wait_recv()
            value = gp[b, m, :, y, x, core, :, lanes].astype(F32)
            value = value + from_plain[lax.rem(j, PLAIN_SLOTS), :, :, lanes].astype(F32)
            value = value + from_pair[lax.rem(j, PAIR_SLOTS), :, :, lanes].astype(F32)
            gp[b, m, :, y, x, core, :, lanes] = value.astype(BF)
            start_all(to_z(j, lanes))

        by_lanes(m, step)

    def scatter_z(j):
        b, m = back_of(j)

        def step(lanes):
            for copy in to_z(j, lanes):
                copy.wait_recv()
            value = gp[b, m, z, y, x, core, :, lanes].astype(F32)
            for s in range(ZN - 1):
                value = value + from_z[lax.rem(j, Z_SLOTS), s, :, lanes].astype(F32)
            total[b, m, :, lanes] = value
            squares[:, lanes] = squares[:, lanes] + value * value

        by_lanes(m, step)

    def put_dz(b, k, slot, at, da):
        dz = da * slope[b, k, :, at].astype(F32)
        work[slot, :, at] = dz.astype(BF)
        bias_acc[...] += sum(dz[:, n : n + 128] for n in range(0, chunk, 128))

    def put_bias(k):
        lane = lax.broadcasted_iota(jnp.int32, (hidden, 128), 1)
        total_k = jnp.sum(bias_acc[...], axis=1, keepdims=True)
        bias_grad[...] = jnp.where(lane == span + k, total_k, bias_grad[...])

    def feed_back(b):
        def body(at):
            @pl.when(b == 1)
            def _():
                resid[:, at] = jnp.zeros((128, chunk), F32)

            e = (-(resid[:, at] * mask[:, at].astype(F32))).astype(BF)
            e_t[:, at] = e
            work[0, :, at] = dot_nn(small(b, 256), e).astype(BF)

        each_chunk(body)

    def feed_forward(b):
        def body(at):
            work[2, :, at] = dot_nn(small(b, 128), f_t[:, at]).astype(BF)

        each_chunk(body)

    def theta_step(b):
        bias_acc[...] = jnp.zeros_like(bias_acc)

        def body(at):
            da = dot_nn(matrix(b, 4), work[0, :, at]) + dot_nn(matrix(b, 5), work[2, :, at])
            put_dz(b, 3, 1, at, da)

        each_chunk(body)
        put_bias(3)

    def layer_back(b, k):
        source, target = lax.rem(k + 1, 2), lax.rem(k, 2)
        bias_acc[...] = jnp.zeros_like(bias_acc)
        each_chunk(lambda at: put_dz(b, k, target, at, dot_nn(matrix(b, k + 1), work[source, :, at])))
        put_bias(k)

    def weight_grad(b, m):
        layer = jnp.where(m >= 4, 3, m - 1)
        slot = jnp.where(m == 4, 0, jnp.where(m == 5, 2, lax.rem(m, 2)))
        gp[b, m] = grid(dot_nt(act_t[b, layer], work[slot]))

    def small_grads(b):
        gp[b, 0, :, :, :, :, :, 0:128] = grid(dot_nt(work[0], in_t[b]))
        gp[b, 0, :, :, :, :, :, 128:256] = gp[b, 0, :, :, :, :, :, 128:256] + grid(bias_grad[...])

        @pl.when(b == 0)
        def _():
            head_acc[...] = dot_nt(theta_keep[...], e_t[...])
            put_head(b, 256)

    def input_grad(b):
        turn_small[...] = small(b, 0).T

        def body(at):
            keep = mask[:, at].astype(F32)
            dr = resid[:, at] * keep + 2.0 * dot_nn(turn_small[...], work[0, :, at])

            @pl.when(b == 1)
            def _():
                put_rows(sens, 1, at, dr[0:past])
                resid[:, at] = dr.astype(BF).astype(F32)

            @pl.when(b == 0)
            def _():
                put_rows(sens, 0, at, (dr * keep)[0:past])

        each_chunk(body)

    bias_grad[...] = jnp.zeros_like(bias_grad)
    squares[...] = jnp.zeros_like(squares)
    total[...] = jnp.zeros_like(total)

    def back_step(j, carry):
        b, m = back_of(j)
        live = jnp.logical_and(j >= 3, j < count)

        def on(test, step):
            pl.when(jnp.logical_and(live, test))(step)

        @pl.when(j == 7)
        def _():
            feed_back(b)
            feed_forward(b)

        on(m == 3, lambda: theta_step(b))
        on(m <= 2, lambda: layer_back(b, m))
        delayed(8, j, scatter_z)
        delayed(6, j, scatter_plane)
        delayed(4, j, scatter_diag)
        delayed(2, j, scatter_core)
        on(m >= 1, lambda: weight_grad(b, m))
        on(m == 0, lambda: small_grads(b))
        pl.when(jnp.logical_and(j >= 2, j < count))(lambda: scatter_start(j))
        on(m == 0, lambda: input_grad(b))
        pl.when(j == count - 1)(lambda: start_all(out_copies(sens, sens_out, 1)))
        return carry

    own.wait_recv()
    for i in range(4):
        gather_line(i)
    prepare()
    lax.fori_loop(0, count + 5, gather_step, 0)

    start_all(out_copies(pred, pred_out, 0))
    lax.fori_loop(0, count + 8, back_step, 0)

    grad_copy = remote(total.at[other], grad_out.at[:, core], out_send.at[2], out_recv.at[2], sibling)
    grad_copy.start()
    grad_out[:, core] = total[core]
    sq = squares[:, 0:128] + squares[:, 128:256] + squares[:, 256:384] + squares[:, 384:512]
    norm_buf[0] = sq[0:8] + sq[8:16]
    for step, device in enumerate([sibling, chip(z, y, xo), chip(z, yo, x)]):
        copy = remote(norm_buf.at[2 * step], norm_buf.at[2 * step + 1], norm_send.at[step], norm_recv.at[step], device)
        copy.start()
        copy.wait()
        norm_buf[2 * step + 2] = norm_buf[2 * step] + norm_buf[2 * step + 1]
    norm_buf[7 + z] = norm_buf[6]
    spread = [
        remote(norm_buf.at[6], norm_buf.at[7 + z], norm_send.at[3 + s], norm_recv.at[3 + s], chip(zi, y, x))
        for s, zi in enumerate(z_peers)
    ]
    start_all(spread)
    for copy in spread:
        copy.wait()
    everything = norm_buf[7]
    for zi in range(1, ZN):
        everything = everything + norm_buf[7 + zi]
    norm_out[...] = jnp.broadcast_to(jnp.sqrt(jnp.sum(everything, keepdims=True)), norm_out.shape)

    grad_copy.wait()
    for buf, out, s in ((pred, pred_out, 0), (sens, sens_out, 1)):
        for copy in out_copies(buf, out, s):
            copy.wait()
    own.wait_send()

    def drain(i, carry):
        def gathered(lanes):
            for copy in [*z_copies(i, lanes), *column_copies(i, lanes), corner_copy(i, lanes), core_copy(i, lanes)]:
                copy.wait_send()

        def scattered(lanes):
            for copy in [to_core(i, lanes), *to_far(i, lanes), to_near(i, lanes), *to_z(i, lanes)]:
                copy.wait_send()

        by_lanes(of(i)[1], gathered)
        by_lanes(back_of(i)[1], scattered)
        return carry

    lax.fori_loop(0, count, drain, 0)


def train_call(plane, segments, extents, adjoint, first, square, head, biases):
    ZN, YN, XN = plane
    past, span, hidden = segments.shape[1], adjoint.shape[0], square.shape[3]
    windows = segments.shape[0] // 2
    chunk = 256
    half = hidden // (ZN * YN * XN) // 2
    sizes = (ZN, YN, XN, windows, chunk, past, span, hidden)
    DMA = pltpu.SemaphoreType.DMA
    vmem = pl.BlockSpec(memory_space=pltpu.VMEM)
    hbm = pl.BlockSpec(memory_space=pl.ANY)
    count = 2 * MATS
    flops = 2 * 2 * 3 * windows * hidden * (6 * hidden + 2 * 128)
    return pl.pallas_call(
        functools.partial(train_kernel, sizes),
        out_shape=(
            jax.ShapeDtypeStruct((span, 1, 2 * windows), F32),
            jax.ShapeDtypeStruct((past, 1, 2 * windows), F32),
            jax.ShapeDtypeStruct((MATS, 2, half, hidden), F32),
            jax.ShapeDtypeStruct((8, 128), F32),
        ),
        in_specs=[hbm, hbm] + [vmem] * 5,
        out_specs=(hbm, hbm, vmem, vmem),
        scratch_shapes=[
            pltpu.VMEM((2, MATS, ZN, YN, XN, 2, half, hidden), BF),
            pltpu.VMEM((MATS, half, hidden), BF),
            pltpu.VMEM((2, MATS, ZN, YN, XN, 2, half, hidden), BF),
            pltpu.VMEM((CORE_SLOTS, ZN, YN, XN, half, hidden), BF),
            pltpu.VMEM((DIAG_SLOTS, ZN, half, hidden), BF),
            pltpu.VMEM((PLAIN_SLOTS, ZN, half, hidden), BF),
            pltpu.VMEM((PAIR_SLOTS, ZN, half, hidden), BF),
            pltpu.VMEM((Z_SLOTS, ZN - 1, half, hidden), BF),
            pltpu.VMEM((2, MATS, half, hidden), F32),
            pltpu.VMEM((2, 4, hidden, windows), BF),
            pltpu.VMEM((2, 128, windows), BF),
            pltpu.VMEM((hidden, windows), BF),
            pltpu.VMEM((hidden, 128), F32),
            pltpu.VMEM((2, 4, hidden, windows), BF),
            pltpu.VMEM((3, hidden, windows), BF),
            pltpu.VMEM((128, windows), F32),
            pltpu.VMEM((128, windows), BF),
            pltpu.VMEM((128, windows), BF),
            pltpu.VMEM((128, windows), BF),
            pltpu.VMEM((hidden, hidden), BF),
            pltpu.VMEM((128, hidden), BF),
            pltpu.VMEM((4, hidden, 128), F32),
            pltpu.VMEM((hidden, 128), F32),
            pltpu.VMEM((hidden, 128), F32),
            pltpu.VMEM((128, 128), F32),
            pltpu.VMEM((windows, past), F32),
            pltpu.VMEM((span, windows), F32),
            pltpu.VMEM((span, windows), F32),
            pltpu.VMEM((2, span, 1, windows), F32),
            pltpu.VMEM((2, past, 1, windows), F32),
            pltpu.VMEM((half, hidden), F32),
            pltpu.VMEM((7 + ZN, 8, 128), F32),
            DMA((1,)),
            DMA((1,)),
            DMA((count, 7)),
            DMA((count, 7)),
            DMA((count, 4 + ZN - 1)),
            DMA((count, 4 + ZN - 1)),
            DMA((3,)),
            DMA((3,)),
            DMA((4,)),
            DMA((3 + ZN - 1,)),
            DMA((3 + ZN - 1,)),
        ],
        compiler_params=pltpu.CompilerParams(
            collective_id=0, has_side_effects=True, vmem_limit_bytes=64 * 1024 * 1024
        ),
        cost_estimate=pl.CostEstimate(flops=flops, bytes_accessed=8_000_000, transcendentals=8 * windows * hidden),
        name="train",
    )(segments, adjoint, extents.reshape(-1, 128), first, square, head, biases)


def update_kernel(past, span, prediction, sensitivity, grads, norm, *refs):
    masters, momenta, variances, outs = refs[0:4], refs[4:8], refs[8:12], refs[12:28]
    norm_out, prediction_out, sensitivity_out, pad, prediction_held, sensitivity_held, sems = refs[28:]
    arriving = [
        pltpu.make_async_copy(sensitivity, sensitivity_held, sems.at[0]),
        pltpu.make_async_copy(prediction, prediction_held, sems.at[1]),
    ]
    leaving = [
        pltpu.make_async_copy(sensitivity_held, sensitivity_out, sems.at[2]),
        pltpu.make_async_copy(prediction_held, prediction_out, sems.at[3]),
    ]
    for copy in arriving:
        copy.start()
    norm_out[...] = norm[0:1, 0:1]
    factor = 1.0 / jnp.maximum(norm[0:1, 0:1], 1.0)
    units = masters[3].shape[2]

    def rows(m, lane, width):
        return grads[m, :, :, lane : lane + width].reshape(units, width)

    forecast = rows(0, 128, 128)
    pad[...] = jnp.zeros_like(pad)
    outs[0][0] = rows(0, 0, 128)[:, 0:past]
    pad[0:units, :] = forecast
    outs[3][0] = pad[...].T[span : span + 4, 0:units]
    for m in range(5):
        outs[1][0, m] = rows(m + 1, 0, grads.shape[3])
    outs[2][0, :, 0:past] = rows(0, 256, 128)[:, 0:past]
    outs[2][0, :, past : past + span] = forecast[:, 0:span]
    for before, after in zip(arriving, leaving):
        before.wait()
        after.start()
    for n in range(4):
        master, gradient = masters[n][...], outs[n][...]
        new, moment, spread = adamw(master, gradient, momenta[n][...], variances[n][...], factor[None])
        outs[4 + n][...], outs[8 + n][...], outs[12 + n][...] = new, moment, spread
    for copy in leaving:
        copy.wait()


def update_call(prediction, sensitivity, grads, norm, state):
    vmem, hbm = pl.BlockSpec(memory_space=pltpu.VMEM), pl.BlockSpec(memory_space=pl.ANY)
    shapes = tuple(jax.ShapeDtypeStruct(a.shape, F32) for a in state[:4])
    passed = tuple(jax.ShapeDtypeStruct(a.shape, F32) for a in (prediction, sensitivity))
    return pl.pallas_call(
        functools.partial(update_kernel, sensitivity.shape[0], prediction.shape[0]),
        out_shape=4 * shapes + (jax.ShapeDtypeStruct((1, 1), F32),) + passed,
        in_specs=[hbm, hbm] + [vmem] * (2 + len(state)),
        out_specs=tuple([vmem] * 17 + [hbm, hbm]),
        scratch_shapes=[
            pltpu.VMEM((128, 128), F32),
            pltpu.VMEM(prediction.shape, F32),
            pltpu.VMEM(sensitivity.shape, F32),
            pltpu.SemaphoreType.DMA((4,)),
        ],
        name="update",
    )(prediction, sensitivity, grads, norm, *state)


def turned(arrays):
    return [a.transpose(0, 2, 1) if n % 4 == 0 else a for n, a in enumerate(arrays)]


def kernel_shards(plane, segments, extents, adjoint, *state):
    state = turned(state)
    results = train_call(plane, segments, extents, adjoint.T, *state[:4])
    *updated, norm, prediction, sensitivity = update_call(*results, state)
    by_window = (prediction.transpose(1, 2, 0), sensitivity.transpose(1, 2, 0))
    return (*by_window, norm.reshape(()), *turned(updated))


STATE_SPECS = (
    P("section", None, "dp"),
    P("section", None, "dp", None),
    P("section", "dp", None),
    P("section", None, "dp"),
)


def solution(mesh):
    in_specs = (P("dp", None), P("dp"), P("dp", None)) + 3 * STATE_SPECS
    out_specs = (P("section", "dp", None), P("section", "dp", None), P()) + 4 * STATE_SPECS
    plane = PLANES.get(mesh.shape["dp"])
    shards = plain_shards if plane is None else functools.partial(kernel_shards, plane)
    return jax.shard_map(shards, mesh=mesh, in_specs=in_specs, out_specs=out_specs, check_vma=False)
```

```python
import functools

import jax
import jax.numpy as jnp
from jax import lax
from jax.experimental import pallas as pl
from jax.experimental.pallas import tpu as pltpu
from jax.sharding import PartitionSpec as P

STEP = 10


def dot_nn(a, b):
    return jnp.dot(a, b, preferred_element_type=jnp.float32)


def dot_tn(a, b):
    return lax.dot_general(a, b, (((0,), (0,)), ((), ())), preferred_element_type=jnp.float32)


def dot_nt(a, b):
    return lax.dot_general(a, b, (((1,), (1,)), ((), ())), preferred_element_type=jnp.float32)


def unit_rows(first, square, head, biases):
    units = first.shape[1]
    return jnp.concatenate(
        [square.transpose(1, 0, 2).reshape(units, -1), first.T, head, biases.T], axis=1
    )


def from_unit_rows(rows, past, hidden, out):
    wide = 5 * hidden
    square = rows[:, :wide].reshape(-1, 5, hidden).transpose(1, 0, 2)
    first = rows[:, wide : wide + past].T
    head = rows[:, wide + past : wide + past + out]
    biases = rows[:, wide + past + out :].T
    return first, square, head, biases


def plain_forward(weights, resid):
    first, square, head, biases = weights
    past = resid.shape[1]
    acts, slopes = [resid.astype(jnp.bfloat16)], []
    for k in range(4):
        z = dot_nn(acts[-1], first if k == 0 else square[k - 1]) + biases[k].astype(jnp.float32)
        sig = jax.nn.sigmoid(z)
        acts.append((z * sig).astype(jnp.bfloat16))
        slopes.append(sig * (1.0 + z * (1.0 - sig)))
    theta_b = dot_nn(acts[4], square[3]).astype(jnp.bfloat16)
    theta_f = dot_nn(acts[4], square[4]).astype(jnp.bfloat16)
    backcast = dot_nn(theta_b, head[:, :past])
    part = dot_nn(theta_f, head[:, past:])
    return backcast, part, (acts, slopes, theta_b, theta_f)


def plain_backward(weights, saved, e, f):
    first, square, head, biases = weights
    acts, slopes, theta_b, theta_f = saved
    past = e.shape[1]
    head_grad = jnp.concatenate([dot_tn(theta_b, e), dot_tn(theta_f, f)], axis=1)
    u_b = dot_nt(e, head[:, :past]).astype(jnp.bfloat16)
    u_f = dot_nt(f, head[:, past:]).astype(jnp.bfloat16)
    squares = [None, None, None, dot_tn(acts[4], u_b), dot_tn(acts[4], u_f)]
    da = dot_nt(u_b, square[3]) + dot_nt(u_f, square[4])
    bias_grads = [None] * 4
    first_grad = None
    for k in (3, 2, 1, 0):
        dz = (da * slopes[k]).astype(jnp.bfloat16)
        bias_grads[k] = jnp.sum(dz, axis=0, dtype=jnp.float32)
        grad = dot_tn(acts[k], dz)
        if k == 0:
            first_grad = grad
        else:
            squares[k - 1] = grad
        da = dot_nt(dz, first if k == 0 else square[k - 1])
    return da, (first_grad, jnp.stack(squares), head_grad, jnp.stack(bias_grads))


def adamw(master, gradient, momentum, variance, factor):
    clipped = gradient * factor
    moment_new = 0.9 * momentum + 0.1 * clipped
    variance_new = 0.999 * variance + 0.001 * clipped * clipped
    ratio = moment_new / (1.0 - 0.9**STEP) / (jnp.sqrt(variance_new / (1.0 - 0.999**STEP)) + 1e-08)
    return master - 0.05 * (ratio + 0.01 * master), moment_new, variance_new


def plain_shards(segments, extents, adjoint, *state):
    masters, momenta, variances = state[:4], state[4:8], state[8:]
    core = lax.axis_index("section")
    past, span = segments.shape[1], adjoint.shape[1]
    windows = segments.shape[0] // 2
    hidden = masters[1].shape[3]
    mine = [
        lax.dynamic_slice_in_dim(v, core * windows, windows, 0) for v in (segments, extents, adjoint)
    ]
    seg, ext, adj = mine
    rows = unit_rows(*(m[0].astype(jnp.bfloat16) for m in masters))
    rows = lax.all_gather(rows, "dp", axis=0, tiled=True)
    rows = lax.all_gather(rows, "section", axis=0)
    blocks = [from_unit_rows(rows[b], past, hidden, past + span) for b in range(2)]
    mask = (
        lax.broadcasted_iota(jnp.int32, (windows, past), 1) >= past - ext[:, None]
    ).astype(jnp.float32)
    r0 = seg * mask
    backcast, part0, saved0 = plain_forward(blocks[0], r0)
    r1 = (r0 - backcast) * mask
    _, part1, saved1 = plain_forward(blocks[1], r1)
    forecast = part0.astype(jnp.bfloat16).astype(jnp.float32) + part1
    f = adj.astype(jnp.bfloat16)
    zero = jnp.zeros_like(r0)
    da1, grads1 = plain_backward(blocks[1], saved1, (-(zero * mask)).astype(jnp.bfloat16), f)
    dr1 = zero * mask + da1
    t = dr1.astype(jnp.bfloat16).astype(jnp.float32)
    da0, grads0 = plain_backward(blocks[0], saved0, (-(t * mask)).astype(jnp.bfloat16), f)
    dr0 = (t * mask + da0) * mask

    def by_section(first_block, second_block):
        mine, other = (
            jnp.where(core == 0, first_block, second_block),
            jnp.where(core == 0, second_block, first_block),
        )
        got = lax.ppermute(other, "section", [(0, 1), (1, 0)])
        return jnp.where(
            core == 0, jnp.concatenate([mine, got]), jnp.concatenate([got, mine])
        )[None]

    prediction = by_section(part0, forecast)
    sensitivity = by_section(dr0, dr1)
    packed = jnp.stack([unit_rows(*grads0), unit_rows(*grads1)])
    packed = lax.psum_scatter(packed, "section", scatter_dimension=0, tiled=False)
    packed = lax.psum_scatter(packed, "dp", scatter_dimension=0, tiled=True)
    norm = jnp.sqrt(lax.psum(jnp.sum(packed * packed), ("section", "dp")))
    factor = 1.0 / jnp.maximum(norm, 1.0)
    summed = [g[None] for g in from_unit_rows(packed, past, hidden, past + span)]
    updated = [adamw(*four, factor) for four in zip(masters, summed, momenta, variances)]
    return (
        prediction,
        sensitivity,
        norm,
        *summed,
        *(u[0] for u in updated),
        *(u[1] for u in updated),
        *(u[2] for u in updated),
    )


PLANES = {16: (4, 2, 2)}
MESH = pl.DeviceIdType.MESH
MATS = 6
CORE_SLOTS, DIAG_SLOTS, PLAIN_SLOTS, PAIR_SLOTS, Z_SLOTS = 4, 4, 6, 4, 4
BF, F32 = jnp.bfloat16, jnp.float32


def remote(src, dst, send_sem, recv_sem, device):
    return pltpu.make_async_remote_copy(
        src_ref=src, dst_ref=dst, send_sem=send_sem, recv_sem=recv_sem, device_id=device, device_id_type=MESH
    )


def train_kernel(
    sizes,
    seg_hbm, adj_hbm, ext, first, square, head, biases,
    pred_out, sens_out, grad_out, norm_out,
    wg, handed, gp, from_core, from_diag, from_plain, from_pair, from_z, total,
    act_t, in_t, theta_keep, head_acc, slope, work, resid, mask, f_ref, f_t, e_t, bias_t, bias_sum, pad,
    seg, adj, first_part, pred, sens, squares, norm_buf,
    own_send, own_recv, ag_send, ag_recv, rs_send, rs_recv, out_send, out_recv, local_sem, norm_send, norm_recv,
):
    ZN, YN, XN, windows, tile, past, span, hidden = sizes
    units = ZN * YN * XN
    core, dp = lax.axis_index("section"), lax.axis_index("dp")
    x, y, z = lax.rem(dp, XN), lax.rem(lax.div(dp, XN), YN), lax.div(dp, XN * YN)
    other, xo, yo = 1 - core, 1 - x, 1 - y
    near_y, near_x = y + core * (yo - y), xo + core * (x - xo)
    far_y, far_x = yo + core * (y - yo), x + core * (xo - x)

    def chip(zi, yi, xi):
        return (core, (zi * YN + yi) * XN + xi)

    sibling = (other, dp)
    z_peers = [lax.rem(z + step, ZN) for step in range(1, ZN)]

    row0 = core * windows
    loads = [
        pltpu.make_async_copy(seg_hbm.at[pl.ds(row0, windows), :], seg, local_sem.at[0]),
        pltpu.make_async_copy(adj_hbm.at[:, pl.ds(row0, windows)], adj, local_sem.at[1]),
    ]
    for load in loads:
        load.start()

    barrier = pltpu.get_barrier_semaphore()
    plane_peers = [
        (ci, (z * YN + yi) * XN + xi) for ci in (core, other) for yi in (y, yo) for xi in (x, xo)
    ][1:]
    peers = plane_peers + [chip(zi, y, x) for zi in z_peers]
    for peer in peers:
        pl.semaphore_signal(barrier, inc=1, device_id=peer, device_id_type=MESH)

    rows = hidden // units
    half_rows = rows // 2

    def put_own(m, value, lanes):
        halves = value.astype(BF).reshape(2, half_rows, -1)
        for h in range(2):
            pl.when(core == h)(functools.partial(put_half, m, halves[h], halves[1 - h], lanes))

    def put_half(m, kept, given, lanes):
        wg[core, m, z, y, x, core, :, lanes] = kept
        handed[m, :, lanes] = given

    pad[...] = jnp.zeros_like(pad)
    pad[0:rows, 0:past] = first[0] * 0.5
    put_own(0, pad[0:rows, :], slice(0, 128))
    pad[...] = jnp.zeros_like(pad)
    pad[span : span + 4, 0:rows] = biases[0] * 0.5
    bias_cols = pad[...].T[0:rows]
    pad[...] = jnp.zeros_like(pad)
    pad[0:rows, 0:span] = head[0, :, past : past + span]
    put_own(0, pad[0:rows, :] + bias_cols, slice(128, 256))
    pad[...] = jnp.zeros_like(pad)
    pad[0:rows, 0:past] = head[0, :, 0:past]
    put_own(0, pad[0:rows, :], slice(256, 384))
    for m in range(5):
        put_own(m + 1, square[0, m] * 0.5 if m < 3 else square[0, m], slice(0, hidden))
    pl.semaphore_wait(barrier, len(peers))

    handed[0, :, 384:512] = jnp.zeros((half_rows, 128), BF)
    own = remote(handed, wg.at[core, :, z, y, x, other], own_send.at[0], own_recv.at[0], sibling)
    own.start()

    def of(i):
        return lax.div(i, MATS), lax.rem(i, MATS)

    def sends(sems, kind, lanes):
        return sems.at[kind, 0 if lanes.stop == hidden else 1]

    def z_copies(i, lanes):
        b, m = of(i)
        part = wg.at[b, m, z, y, x, core, :, lanes]
        return [
            remote(part, part, sends(ag_send, 0, lanes), ag_recv.at[i, s], chip(zi, y, x)) for s, zi in enumerate(z_peers)
        ]

    def column_copies(i, lanes):
        b, m = of(i)
        part = wg.at[b, m, :, y, x, core, :, lanes]
        return [
            remote(part, part, sends(ag_send, 1, lanes), ag_recv.at[i, 3], chip(z, near_y, near_x)),
            remote(part, part, sends(ag_send, 1, lanes), ag_recv.at[i, 4], chip(z, far_y, far_x)),
        ]

    def corner_copy(i, lanes):
        b, m = of(i)
        part = wg.at[b, m, :, near_y, near_x, core, :, lanes]
        return remote(part, part, sends(ag_send, 2, lanes), ag_recv.at[i, 5], chip(z, far_y, far_x))

    def core_copy(i, lanes):
        b, m = of(i)
        part = wg.at[b, m, :, :, :, core, :, lanes]
        return remote(part, part, sends(ag_send, 3, lanes), ag_recv.at[i, 6], sibling)

    def by_lanes(m, step):
        pl.when(m == 0)(lambda: step(slice(0, 384)))
        pl.when(m > 0)(lambda: step(slice(0, hidden)))

    def start_all(copies):
        for copy in copies:
            copy.start()

    for load in loads:
        load.wait()
    zeros_tile = jnp.zeros((tile, 128), F32)

    def prepare(t, carry):
        at = pl.ds(t * tile, tile)
        resid[at, :] = zeros_tile
        resid[at, 0:past] = seg[at, :]
        return carry

    def prepare_mask(g, carry):
        lengths = ext[pl.ds(core * (windows // 128) + g, 1), :]
        position = lax.broadcasted_iota(jnp.int32, (128, 128), 0)
        keep = jnp.where(position >= past - lengths, 1.0, 0.0).astype(F32).T
        at = pl.ds(pl.multiple_of(g * 128, 128), 128)
        pad[0:span, :] = adj[:, at]
        f_ref[at, :] = pad[...].T.astype(BF)
        f_t[:, at] = pad[...].astype(BF)
        mask[at, :] = keep.astype(BF)
        resid[at, :] = resid[at, :] * keep
        return carry

    tiles = windows // tile
    part_tile = windows // 2

    def matrix(b, m):
        return wg[b, m].reshape(hidden, hidden)

    def small(b, lane):
        return wg[b, 0, :, :, :, :, :, lane : lane + 128].reshape(hidden, 128)

    def store_layer(b, k, at, v, scale):
        p = 1.0 + jnp.tanh(v)
        a = v * p
        rate = p + a * (2.0 - p)
        slope[b, k, at, :] = (rate if scale is None else rate * scale).astype(BF)
        low = a.astype(BF)
        act_t[b, k, :, at] = low.T
        return low

    def layer_zero(b):
        bias_t[...] = small(b, 128).astype(F32).T

        def body(t, carry):
            at = pl.ds(pl.multiple_of(t * tile, tile), tile)
            a = resid[at, :].astype(BF)
            in_t[b, :, at] = a.T
            v = dot_nt(a, small(b, 0)) + bias_t[span : span + 1, :]
            work[0, at, :] = store_layer(b, 0, at, v, None)
            return carry

        lax.fori_loop(0, tiles, body, 0)

    def layer_next(b, k):
        source, target = lax.rem(k + 1, 2), lax.rem(k, 2)
        bias = bias_t[pl.ds(span + k, 1), :]
        scale = jnp.where(k == 3, 0.5, 1.0)

        def body(t, carry):
            at = pl.ds(pl.multiple_of(t * tile, tile), tile)
            v = dot_nn(work[source, at, :], matrix(b, k)) + bias
            work[target, at, :] = store_layer(b, k, at, v, scale)
            return carry

        lax.fori_loop(0, tiles, body, 0)

    def grid(value):
        return value.astype(BF).reshape(ZN, YN, XN, 2, half_rows, -1)

    def head_grad(acc, lane, b):
        gp[b, 0, :, :, :, :, :, lane : lane + 128] = grid(acc[...].T)

    def backcast_step(b):
        def body(t, carry):
            at = pl.ds(pl.multiple_of(t * part_tile, part_tile), part_tile)
            theta = dot_nn(work[1, at, :], matrix(b, 4)).astype(BF)

            @pl.when(b == 0)
            def _():
                theta_keep[at, :] = theta
                backcast = dot_nn(theta, small(b, 256))
                resid[at, :] = (resid[at, :] - backcast) * mask[at, :].astype(F32)

            @pl.when(b == 1)
            def _():
                head_acc[...] += dot_nn(e_t[:, at], theta)

            return carry

        head_acc[...] = jnp.zeros_like(head_acc)
        lax.fori_loop(0, windows // part_tile, body, 0)
        pl.when(b == 1)(lambda: head_grad(head_acc, 256, b))

    def put_rows(buf, b, at, value):
        for row in range(value.shape[0]):
            buf[b, row, :, at] = value[row : row + 1]

    def forecast_step(b):
        def body(t, carry):
            at = pl.ds(pl.multiple_of(t * part_tile, part_tile), part_tile)
            theta = dot_nn(work[1, at, :], matrix(b, 5)).astype(BF)
            head_acc[...] += dot_nn(f_t[:, at], theta)
            part = dot_nn(theta, small(b, 128)).T[0:span]

            @pl.when(b == 0)
            def _():
                first_part[:, at] = part
                put_rows(pred, 0, at, part)

            @pl.when(b == 1)
            def _():
                put_rows(pred, 1, at, first_part[:, at].astype(BF).astype(F32) + part)

            return carry

        head_acc[...] = jnp.zeros_like(head_acc)
        lax.fori_loop(0, windows // part_tile, body, 0)
        head_grad(head_acc, 128, b)

    count = 2 * MATS

    def delayed(lag, t, step):
        pl.when(jnp.logical_and(t >= lag, t < count + lag))(lambda: step(t - lag))

    def gather_line(i):
        by_lanes(of(i)[1], lambda lanes: start_all(z_copies(i, lanes)))

    def gather_columns(i):
        def step(lanes):
            for copy in z_copies(i, lanes):
                copy.wait_recv()
            start_all(column_copies(i, lanes))

        by_lanes(of(i)[1], step)

    def gather_corner(i):
        def step(lanes):
            column_copies(i, lanes)[0].wait_recv()
            corner_copy(i, lanes).start()

        by_lanes(of(i)[1], step)

    def gather_core(i):
        def step(lanes):
            column_copies(i, lanes)[1].wait_recv()
            corner_copy(i, lanes).wait_recv()
            core_copy(i, lanes).start()

        by_lanes(of(i)[1], step)

    def forward_unit(i):
        b, m = of(i)
        by_lanes(m, lambda lanes: core_copy(i, lanes).wait_recv())
        pl.when(m == 0)(lambda: layer_zero(b))
        pl.when(jnp.logical_and(m >= 1, m <= 3))(lambda: layer_next(b, m))
        pl.when(m == 4)(lambda: backcast_step(b))
        pl.when(m == 5)(lambda: forecast_step(b))

        @pl.when(m == jnp.where(b == 1, 3, 5))
        def _():
            pl.when(b == 1)(lambda: feed(b))
            pl.when(b == 0)(lambda: feed_forward(b))
            lax.fori_loop(jnp.where(b == 1, 4, 5), MATS, lambda n, carry: (theta_grad(b, n), carry)[1], 0)

            @pl.when(b == 1)
            def _():
                scatter_start(0)
                scatter_start(1)

    def gather_step(t, carry):
        delayed(4, t, gather_core)
        delayed(2, t, gather_corner)
        delayed(0, t, gather_columns)
        pl.when(t + 4 < count)(lambda: gather_line(t + 4))
        delayed(5, t, forward_unit)
        return carry

    def out_copies(buf, out, s):
        at = pl.ds(row0, windows)
        return [
            pltpu.make_async_copy(buf.at[core], out.at[:, :, at], local_sem.at[2 + s]),
            remote(buf.at[other], out.at[:, :, at], out_send.at[s], out_recv.at[s], sibling),
        ]


    def back_of(j):
        b = jnp.where(jnp.logical_or(j <= 1, jnp.logical_and(j >= 3, j <= 6)), 1, 0)
        m = jnp.where(j <= 1, 4 + j, jnp.where(j == 2, 5, jnp.where(j <= 6, 6 - j, jnp.where(j == 7, 4, 11 - j))))
        return b, m

    def to_core(j, lanes):
        b, m = back_of(j)
        return remote(
            gp.at[b, m, :, :, :, other, :, lanes], from_core.at[lax.rem(j, CORE_SLOTS), :, :, :, :, lanes],
            sends(rs_send, 3, lanes), rs_recv.at[j, 0], sibling,
        )

    def to_far(j, lanes):
        b, m = back_of(j)
        device = chip(z, far_y, far_x)
        return [
            remote(
                gp.at[b, m, :, yo, xo, core, :, lanes], from_diag.at[lax.rem(j, DIAG_SLOTS), :, :, lanes],
                sends(rs_send, 1, lanes), rs_recv.at[j, 1], device,
            ),
            remote(
                gp.at[b, m, :, far_y, far_x, core, :, lanes], from_plain.at[lax.rem(j, PLAIN_SLOTS), :, :, lanes],
                sends(rs_send, 1, lanes), rs_recv.at[j, 2], device,
            ),
        ]

    def to_near(j, lanes):
        b, m = back_of(j)
        return remote(
            gp.at[b, m, :, near_y, near_x, core, :, lanes], from_pair.at[lax.rem(j, PAIR_SLOTS), :, :, lanes],
            sends(rs_send, 2, lanes), rs_recv.at[j, 3], chip(z, near_y, near_x),
        )

    def to_z(j, lanes):
        b, m = back_of(j)
        return [
            remote(
                gp.at[b, m, zi, y, x, core, :, lanes], from_z.at[lax.rem(j, Z_SLOTS), s, :, lanes],
                sends(rs_send, 0, lanes), rs_recv.at[j, 4 + s], chip(zi, y, x),
            )
            for s, zi in enumerate(z_peers)
        ]

    def scatter_start(j):
        by_lanes(back_of(j)[1], lambda lanes: to_core(j, lanes).start())

    def scatter_core(j):
        b, m = back_of(j)

        def step(lanes):
            to_core(j, lanes).wait_recv()
            part = gp[b, m, :, :, :, core, :, lanes] + from_core[lax.rem(j, CORE_SLOTS), :, :, :, :, lanes]
            gp[b, m, :, :, :, core, :, lanes] = part
            start_all(to_far(j, lanes))

        by_lanes(m, step)

    def scatter_diag(j):
        b, m = back_of(j)

        def step(lanes):
            to_far(j, lanes)[0].wait_recv()
            part = gp[b, m, :, near_y, near_x, core, :, lanes] + from_diag[lax.rem(j, DIAG_SLOTS), :, :, lanes]
            gp[b, m, :, near_y, near_x, core, :, lanes] = part
            to_near(j, lanes).start()

        by_lanes(m, step)

    def scatter_plane(j):
        b, m = back_of(j)

        def step(lanes):
            to_far(j, lanes)[1].wait_recv()
            to_near(j, lanes).wait_recv()
            value = gp[b, m, :, y, x, core, :, lanes].astype(F32)
            value = value + from_plain[lax.rem(j, PLAIN_SLOTS), :, :, lanes].astype(F32)
            value = value + from_pair[lax.rem(j, PAIR_SLOTS), :, :, lanes].astype(F32)
            gp[b, m, :, y, x, core, :, lanes] = value.astype(BF)
            start_all(to_z(j, lanes))

        by_lanes(m, step)

    def scatter_z(j):
        b, m = back_of(j)

        def step(lanes):
            for copy in to_z(j, lanes):
                copy.wait_recv()
            value = gp[b, m, z, y, x, core, :, lanes].astype(F32)
            for s in range(ZN - 1):
                value = value + from_z[lax.rem(j, Z_SLOTS), s, :, lanes].astype(F32)
            total[b, m, :, lanes] = value
            squares[:, lanes] = squares[:, lanes] + value * value

        by_lanes(m, step)

    def add_rows(value):
        return jnp.sum(value.reshape(-1, 8, hidden), axis=0)

    def put_bias(k, acc):
        bias_sum[pl.ds(span + k, 1), :] = jnp.sum(acc, axis=0, keepdims=True)

    def feed(b):
        pl.when(b == 1)(lambda: resid.__setitem__(..., jnp.zeros_like(resid)))
        e = (-(resid[...] * mask[...].astype(F32))).astype(BF)
        e_t[...] = e.T
        work[0] = dot_nt(e, small(b, 256)).astype(BF)
        work[2] = dot_nt(f_ref[...], small(b, 128)).astype(BF)

    def feed_forward(b):
        work[2] = dot_nt(f_ref[...], small(b, 128)).astype(BF)

    def put_dz(b, k, da):
        dz = da * slope[b, k].astype(F32)
        work[k % 2 if isinstance(k, int) else lax.rem(k, 2)] = dz.astype(BF)
        bias_sum[pl.ds(span + k, 1), :] = jnp.sum(add_rows(dz), axis=0, keepdims=True)

    def theta_step(b):
        put_dz(b, 3, dot_nt(work[0], matrix(b, 4)) + dot_nt(work[2], matrix(b, 5)))

    def layer_back(b, k):
        source = lax.rem(k, 2)
        gp[b, k] = grid(dot_nn(act_t[b, k - 1], work[source]))
        put_dz(b, k - 1, dot_nt(work[source], matrix(b, k)))

    def theta_grad(b, m):
        gp[b, m] = grid(dot_nn(act_t[b, 3], work[jnp.where(m == 4, 0, 2)]))

    def small_grads(b):
        gp[b, 0, :, :, :, :, :, 0:128] = grid(dot_nn(in_t[b], work[0]).T)
        gp[b, 0, :, :, :, :, :, 128:256] = gp[b, 0, :, :, :, :, :, 128:256] + grid(bias_sum[...].T)

        @pl.when(b == 0)
        def _():
            head_acc[...] = dot_nn(e_t[...], theta_keep[...])
            head_grad(head_acc, 256, b)


    def input_grad(b):
        for t in range(2):
            at = slice(t * windows // 2, (t + 1) * windows // 2)
            keep = mask[at, :].astype(F32)
            dr = resid[at, :] * keep + 2.0 * dot_nn(work[0, at, :], small(b, 0))

            @pl.when(b == 1)
            def _():
                put_rows(sens, 1, at, dr.T[0:past])
                resid[at, :] = dr.astype(BF).astype(F32)

            @pl.when(b == 0)
            def _():
                put_rows(sens, 0, at, (dr * keep).T[0:past])

    bias_sum[...] = jnp.zeros_like(bias_sum)
    squares[...] = jnp.zeros_like(squares)
    total[...] = jnp.zeros_like(total)

    def back_step(j, carry):
        b, m = back_of(j)
        live = jnp.logical_and(j >= 3, j < count)

        def on(test, step):
            pl.when(jnp.logical_and(live, test))(step)

        delayed(8, j, scatter_z)
        delayed(6, j, scatter_plane)
        delayed(4, j, scatter_diag)
        delayed(2, j, scatter_core)
        pl.when(j == 2)(lambda: theta_step(1))
        on(jnp.logical_and(m >= 1, m <= 3), lambda: layer_back(b, m))
        on(m == 0, lambda: small_grads(b))

        @pl.when(j == 7)
        def _():
            feed(b)
            theta_grad(b, 4)
            theta_step(b)

        pl.when(jnp.logical_and(j >= 2, j < count))(lambda: scatter_start(j))
        on(m == 0, lambda: input_grad(b))
        pl.when(j == count - 1)(lambda: start_all(out_copies(sens, sens_out, 1)))
        return carry

    own.wait_recv()
    for i in range(4):
        gather_line(i)
    lax.fori_loop(0, tiles, prepare, 0)
    pad[...] = jnp.zeros_like(pad)
    lax.fori_loop(0, windows // 128, prepare_mask, 0)
    lax.fori_loop(0, count + 5, gather_step, 0)

    start_all(out_copies(pred, pred_out, 0))
    lax.fori_loop(0, count + 8, back_step, 0)

    grad_copy = remote(total.at[other], grad_out.at[:, core], out_send.at[2], out_recv.at[2], sibling)
    grad_copy.start()
    grad_out[:, core] = total[core]
    sq = squares[:, 0:128] + squares[:, 128:256] + squares[:, 256:384] + squares[:, 384:512]
    place = (y * XN + x) * 2 + core
    norm_buf[place] = sq[0:8] + sq[8:16]

    def spread(sources, targets, first):
        copies = [
            remote(norm_buf.at[sources], norm_buf.at[sources], norm_send.at[first + s], norm_recv.at[first + s], device)
            for s, device in enumerate(targets)
        ]
        start_all(copies)
        for copy in copies:
            copy.wait()

    def add_up(slots):
        value = norm_buf[slots[0]]
        for slot in slots[1:]:
            value = value + norm_buf[slot]
        return value

    spread(place, plane_peers, 0)
    norm_buf[8 + z] = add_up(range(8))
    spread(8 + z, [chip(zi, y, x) for zi in z_peers], 7)
    everything = add_up(range(8, 8 + ZN))
    norm_out[...] = jnp.broadcast_to(jnp.sqrt(jnp.sum(everything, keepdims=True)), norm_out.shape)

    grad_copy.wait()
    for buf, out, s in ((pred, pred_out, 0), (sens, sens_out, 1)):
        for copy in out_copies(buf, out, s):
            copy.wait()
    own.wait_send()

    for mats, lanes in ((slice(1, MATS), slice(0, hidden)), (slice(0, 1), slice(0, 384))):
        sent = (
            wg.at[:, mats, 0 : ZN - 1, 0, 0, 0, :, lanes],
            wg.at[:, mats, :, :, 0, 0, :, lanes],
            wg.at[:, mats, :, 0, 0, 0, :, lanes],
            wg.at[:, mats, :, :, :, 0, :, lanes],
        )
        for sems in (ag_send, rs_send):
            for kind, ref in enumerate(sent):
                remote(ref, ref, sends(sems, kind, lanes), out_recv.at[0], sibling).wait_send()


def train_call(plane, segments, extents, adjoint, first, square, head, biases):
    ZN, YN, XN = plane
    past, span, hidden = segments.shape[1], adjoint.shape[0], square.shape[3]
    windows = segments.shape[0] // 2
    tile = windows
    half = hidden // (ZN * YN * XN) // 2
    sizes = (ZN, YN, XN, windows, tile, past, span, hidden)
    DMA = pltpu.SemaphoreType.DMA
    vmem = pl.BlockSpec(memory_space=pltpu.VMEM)
    hbm = pl.BlockSpec(memory_space=pl.ANY)
    count = 2 * MATS
    flops = 2 * 2 * 3 * windows * hidden * (6 * hidden + 2 * 128)
    return pl.pallas_call(
        functools.partial(train_kernel, sizes),
        out_shape=(
            jax.ShapeDtypeStruct((span, 1, 2 * windows), F32),
            jax.ShapeDtypeStruct((past, 1, 2 * windows), F32),
            jax.ShapeDtypeStruct((MATS, 2, half, hidden), F32),
            jax.ShapeDtypeStruct((8, 128), F32),
        ),
        in_specs=[hbm, hbm] + [vmem] * 5,
        out_specs=(hbm, hbm, vmem, vmem),
        scratch_shapes=[
            pltpu.VMEM((2, MATS, ZN, YN, XN, 2, half, hidden), BF),
            pltpu.VMEM((MATS, half, hidden), BF),
            pltpu.VMEM((2, MATS, ZN, YN, XN, 2, half, hidden), BF),
            pltpu.VMEM((CORE_SLOTS, ZN, YN, XN, half, hidden), BF),
            pltpu.VMEM((DIAG_SLOTS, ZN, half, hidden), BF),
            pltpu.VMEM((PLAIN_SLOTS, ZN, half, hidden), BF),
            pltpu.VMEM((PAIR_SLOTS, ZN, half, hidden), BF),
            pltpu.VMEM((Z_SLOTS, ZN - 1, half, hidden), BF),
            pltpu.VMEM((2, MATS, half, hidden), F32),
            pltpu.VMEM((2, 4, hidden, windows), BF),
            pltpu.VMEM((2, 128, windows), BF),
            pltpu.VMEM((windows, hidden), BF),
            pltpu.VMEM((128, hidden), F32),
            pltpu.VMEM((2, 4, windows, hidden), BF),
            pltpu.VMEM((3, windows, hidden), BF),
            pltpu.VMEM((windows, 128), F32),
            pltpu.VMEM((windows, 128), BF),
            pltpu.VMEM((windows, 128), BF),
            pltpu.VMEM((128, windows), BF),
            pltpu.VMEM((128, windows), BF),
            pltpu.VMEM((128, hidden), F32),
            pltpu.VMEM((128, hidden), F32),
            pltpu.VMEM((128, 128), F32),
            pltpu.VMEM((windows, past), F32),
            pltpu.VMEM((span, windows), F32),
            pltpu.VMEM((span, windows), F32),
            pltpu.VMEM((2, span, 1, windows), F32),
            pltpu.VMEM((2, past, 1, windows), F32),
            pltpu.VMEM((half, hidden), F32),
            pltpu.VMEM((8 + ZN, 8, 128), F32),
            DMA((1,)),
            DMA((1,)),
            DMA((4, 2)),
            DMA((count, 4 + ZN - 1)),
            DMA((4, 2)),
            DMA((count, 4 + ZN - 1)),
            DMA((3,)),
            DMA((3,)),
            DMA((4,)),
            DMA((7 + ZN - 1,)),
            DMA((7 + ZN - 1,)),
        ],
        compiler_params=pltpu.CompilerParams(
            collective_id=0, has_side_effects=True, vmem_limit_bytes=64 * 1024 * 1024
        ),
        cost_estimate=pl.CostEstimate(flops=flops, bytes_accessed=8_000_000, transcendentals=8 * windows * hidden),
        name="train",
    )(segments, adjoint, extents.reshape(-1, 128), first, square, head, biases)


def update_kernel(past, span, prediction, sensitivity, grads, norm, *refs):
    masters, momenta, variances, outs = refs[0:4], refs[4:8], refs[8:12], refs[12:28]
    norm_out, prediction_out, sensitivity_out, pad, prediction_held, sensitivity_held, sems = refs[28:]
    arriving = [
        pltpu.make_async_copy(sensitivity, sensitivity_held, sems.at[0]),
        pltpu.make_async_copy(prediction, prediction_held, sems.at[1]),
    ]
    leaving = [
        pltpu.make_async_copy(sensitivity_held, sensitivity_out, sems.at[2]),
        pltpu.make_async_copy(prediction_held, prediction_out, sems.at[3]),
    ]
    for copy in arriving:
        copy.start()
    norm_out[...] = norm[0:1, 0:1]
    factor = 1.0 / jnp.maximum(norm[0:1, 0:1], 1.0)
    units = masters[3].shape[2]

    def rows(m, lane, width):
        return grads[m, :, :, lane : lane + width].reshape(units, width)

    forecast = rows(0, 128, 128)
    pad[...] = jnp.zeros_like(pad)
    outs[0][0] = rows(0, 0, 128)[:, 0:past]
    pad[0:units, :] = forecast
    outs[3][0] = pad[...].T[span : span + 4, 0:units]
    for m in range(5):
        outs[1][0, m] = rows(m + 1, 0, grads.shape[3])
    outs[2][0, :, 0:past] = rows(0, 256, 128)[:, 0:past]
    outs[2][0, :, past : past + span] = forecast[:, 0:span]
    for before, after in zip(arriving, leaving):
        before.wait()
        after.start()
    for n in range(4):
        master, gradient = masters[n][...], outs[n][...]
        new, moment, spread = adamw(master, gradient, momenta[n][...], variances[n][...], factor[None])
        outs[4 + n][...], outs[8 + n][...], outs[12 + n][...] = new, moment, spread
    for copy in leaving:
        copy.wait()


def update_call(prediction, sensitivity, grads, norm, state):
    vmem, hbm = pl.BlockSpec(memory_space=pltpu.VMEM), pl.BlockSpec(memory_space=pl.ANY)
    shapes = tuple(jax.ShapeDtypeStruct(a.shape, F32) for a in state[:4])
    passed = tuple(jax.ShapeDtypeStruct(a.shape, F32) for a in (prediction, sensitivity))
    return pl.pallas_call(
        functools.partial(update_kernel, sensitivity.shape[0], prediction.shape[0]),
        out_shape=4 * shapes + (jax.ShapeDtypeStruct((1, 1), F32),) + passed,
        in_specs=[hbm, hbm] + [vmem] * (2 + len(state)),
        out_specs=tuple([vmem] * 17 + [hbm, hbm]),
        scratch_shapes=[
            pltpu.VMEM((128, 128), F32),
            pltpu.VMEM(prediction.shape, F32),
            pltpu.VMEM(sensitivity.shape, F32),
            pltpu.SemaphoreType.DMA((4,)),
        ],
        name="update",
    )(prediction, sensitivity, grads, norm, *state)


def turned(arrays):
    return [a.transpose(0, 2, 1) if n % 4 == 0 else a for n, a in enumerate(arrays)]


def kernel_shards(plane, segments, extents, adjoint, *state):
    state = turned(state)
    results = train_call(plane, segments, extents, adjoint.T, *state[:4])
    *updated, norm, prediction, sensitivity = update_call(*results, state)
    by_window = (prediction.transpose(1, 2, 0), sensitivity.transpose(1, 2, 0))
    return (*by_window, norm.reshape(()), *turned(updated))


STATE_SPECS = (
    P("section", None, "dp"),
    P("section", None, "dp", None),
    P("section", "dp", None),
    P("section", None, "dp"),
)


def solution(mesh):
    in_specs = (P("dp", None), P("dp"), P("dp", None)) + 3 * STATE_SPECS
    out_specs = (P("section", "dp", None), P("section", "dp", None), P()) + 4 * STATE_SPECS
    plane = PLANES.get(mesh.shape["dp"])
    shards = plain_shards if plane is None else functools.partial(kernel_shards, plane)
    return jax.shard_map(shards, mesh=mesh, in_specs=in_specs, out_specs=out_specs, check_vma=False)
```

```python
import functools

import jax
import jax.numpy as jnp
from jax import lax
from jax.experimental import pallas as pl
from jax.experimental.pallas import tpu as pltpu
from jax.sharding import PartitionSpec as P

STEP = 10


def dot_nn(a, b):
    return jnp.dot(a, b, preferred_element_type=jnp.float32)


def dot_tn(a, b):
    return lax.dot_general(a, b, (((0,), (0,)), ((), ())), preferred_element_type=jnp.float32)


def dot_nt(a, b):
    return lax.dot_general(a, b, (((1,), (1,)), ((), ())), preferred_element_type=jnp.float32)


def unit_rows(first, square, head, biases):
    units = first.shape[1]
    return jnp.concatenate(
        [square.transpose(1, 0, 2).reshape(units, -1), first.T, head, biases.T], axis=1
    )


def from_unit_rows(rows, past, hidden, out):
    wide = 5 * hidden
    square = rows[:, :wide].reshape(-1, 5, hidden).transpose(1, 0, 2)
    first = rows[:, wide : wide + past].T
    head = rows[:, wide + past : wide + past + out]
    biases = rows[:, wide + past + out :].T
    return first, square, head, biases


def plain_forward(weights, resid):
    first, square, head, biases = weights
    past = resid.shape[1]
    acts, slopes = [resid.astype(jnp.bfloat16)], []
    for k in range(4):
        z = dot_nn(acts[-1], first if k == 0 else square[k - 1]) + biases[k].astype(jnp.float32)
        sig = jax.nn.sigmoid(z)
        acts.append((z * sig).astype(jnp.bfloat16))
        slopes.append(sig * (1.0 + z * (1.0 - sig)))
    theta_b = dot_nn(acts[4], square[3]).astype(jnp.bfloat16)
    theta_f = dot_nn(acts[4], square[4]).astype(jnp.bfloat16)
    backcast = dot_nn(theta_b, head[:, :past])
    part = dot_nn(theta_f, head[:, past:])
    return backcast, part, (acts, slopes, theta_b, theta_f)


def plain_backward(weights, saved, e, f):
    first, square, head, biases = weights
    acts, slopes, theta_b, theta_f = saved
    past = e.shape[1]
    head_grad = jnp.concatenate([dot_tn(theta_b, e), dot_tn(theta_f, f)], axis=1)
    u_b = dot_nt(e, head[:, :past]).astype(jnp.bfloat16)
    u_f = dot_nt(f, head[:, past:]).astype(jnp.bfloat16)
    squares = [None, None, None, dot_tn(acts[4], u_b), dot_tn(acts[4], u_f)]
    da = dot_nt(u_b, square[3]) + dot_nt(u_f, square[4])
    bias_grads = [None] * 4
    first_grad = None
    for k in (3, 2, 1, 0):
        dz = (da * slopes[k]).astype(jnp.bfloat16)
        bias_grads[k] = jnp.sum(dz, axis=0, dtype=jnp.float32)
        grad = dot_tn(acts[k], dz)
        if k == 0:
            first_grad = grad
        else:
            squares[k - 1] = grad
        da = dot_nt(dz, first if k == 0 else square[k - 1])
    return da, (first_grad, jnp.stack(squares), head_grad, jnp.stack(bias_grads))


def adamw(master, gradient, momentum, variance, factor):
    clipped = gradient * factor
    moment_new = 0.9 * momentum + 0.1 * clipped
    variance_new = 0.999 * variance + 0.001 * clipped * clipped
    ratio = moment_new / (1.0 - 0.9**STEP) / (jnp.sqrt(variance_new / (1.0 - 0.999**STEP)) + 1e-08)
    return master - 0.05 * (ratio + 0.01 * master), moment_new, variance_new


def plain_shards(segments, extents, adjoint, *state):
    masters, momenta, variances = state[:4], state[4:8], state[8:]
    core = lax.axis_index("section")
    past, span = segments.shape[1], adjoint.shape[1]
    windows = segments.shape[0] // 2
    hidden = masters[1].shape[3]
    mine = [
        lax.dynamic_slice_in_dim(v, core * windows, windows, 0) for v in (segments, extents, adjoint)
    ]
    seg, ext, adj = mine
    rows = unit_rows(*(m[0].astype(jnp.bfloat16) for m in masters))
    rows = lax.all_gather(rows, "dp", axis=0, tiled=True)
    rows = lax.all_gather(rows, "section", axis=0)
    blocks = [from_unit_rows(rows[b], past, hidden, past + span) for b in range(2)]
    mask = (
        lax.broadcasted_iota(jnp.int32, (windows, past), 1) >= past - ext[:, None]
    ).astype(jnp.float32)
    r0 = seg * mask
    backcast, part0, saved0 = plain_forward(blocks[0], r0)
    r1 = (r0 - backcast) * mask
    _, part1, saved1 = plain_forward(blocks[1], r1)
    forecast = part0.astype(jnp.bfloat16).astype(jnp.float32) + part1
    f = adj.astype(jnp.bfloat16)
    zero = jnp.zeros_like(r0)
    da1, grads1 = plain_backward(blocks[1], saved1, (-(zero * mask)).astype(jnp.bfloat16), f)
    dr1 = zero * mask + da1
    t = dr1.astype(jnp.bfloat16).astype(jnp.float32)
    da0, grads0 = plain_backward(blocks[0], saved0, (-(t * mask)).astype(jnp.bfloat16), f)
    dr0 = (t * mask + da0) * mask

    def by_section(first_block, second_block):
        mine, other = (
            jnp.where(core == 0, first_block, second_block),
            jnp.where(core == 0, second_block, first_block),
        )
        got = lax.ppermute(other, "section", [(0, 1), (1, 0)])
        return jnp.where(
            core == 0, jnp.concatenate([mine, got]), jnp.concatenate([got, mine])
        )[None]

    prediction = by_section(part0, forecast)
    sensitivity = by_section(dr0, dr1)
    packed = jnp.stack([unit_rows(*grads0), unit_rows(*grads1)])
    packed = lax.psum_scatter(packed, "section", scatter_dimension=0, tiled=False)
    packed = lax.psum_scatter(packed, "dp", scatter_dimension=0, tiled=True)
    norm = jnp.sqrt(lax.psum(jnp.sum(packed * packed), ("section", "dp")))
    factor = 1.0 / jnp.maximum(norm, 1.0)
    summed = [g[None] for g in from_unit_rows(packed, past, hidden, past + span)]
    updated = [adamw(*four, factor) for four in zip(masters, summed, momenta, variances)]
    return (
        prediction,
        sensitivity,
        norm,
        *summed,
        *(u[0] for u in updated),
        *(u[1] for u in updated),
        *(u[2] for u in updated),
    )


PLANES = {16: (4, 2, 2)}
MESH = pl.DeviceIdType.MESH
MATS = 6
CORE_SLOTS, DIAG_SLOTS, PLAIN_SLOTS, PAIR_SLOTS, Z_SLOTS = 4, 4, 6, 4, 4
BF, F32 = jnp.bfloat16, jnp.float32


def remote(src, dst, send_sem, recv_sem, device):
    return pltpu.make_async_remote_copy(
        src_ref=src, dst_ref=dst, send_sem=send_sem, recv_sem=recv_sem, device_id=device, device_id_type=MESH
    )


def train_kernel(
    sizes,
    seg_hbm, adj_hbm, ext_hbm, first_hbm, square_hbm, head_hbm, biases_hbm,
    pred_out, sens_out, grad_out, norm_out,
    wg, handed, gp, from_core, from_diag, from_plain, from_pair, from_z, total,
    act_t, in_t, theta_keep, head_acc, slope, work, resid, mask, f_ref, f_t, e_t, bias_t, bias_sum, pad,
    seg, adj, ext, first, square, head, biases, first_part, part_t, pred, sens, squares, norm_buf,
    own_send, own_recv, ag_send, ag_recv, rs_send, rs_recv, out_send, out_recv, local_sem, norm_send, norm_recv,
):
    ZN, YN, XN, windows, tile, past, span, hidden = sizes
    units = ZN * YN * XN
    core, dp = lax.axis_index("section"), lax.axis_index("dp")
    x, y, z = lax.rem(dp, XN), lax.rem(lax.div(dp, XN), YN), lax.div(dp, XN * YN)
    other, xo, yo = 1 - core, 1 - x, 1 - y
    near_y, near_x = y + core * (yo - y), xo + core * (x - xo)
    far_y, far_x = yo + core * (y - yo), x + core * (xo - x)

    def chip(zi, yi, xi):
        return (core, (zi * YN + yi) * XN + xi)

    sibling = (other, dp)
    z_peers = [lax.rem(z + step, ZN) for step in range(1, ZN)]

    row0 = core * windows
    loads = [
        pltpu.make_async_copy(seg_hbm.at[pl.ds(row0, windows), :], seg, local_sem.at[0]),
        pltpu.make_async_copy(adj_hbm.at[:, pl.ds(row0, windows)], adj, local_sem.at[1]),
    ]
    small_loads = [
        pltpu.make_async_copy(source, target, local_sem.at[4 + n])
        for n, (source, target) in enumerate(
            [(square_hbm, square), (first_hbm, first), (head_hbm, head), (biases_hbm, biases), (ext_hbm, ext)]
        )
    ]
    for load in small_loads + loads:
        load.start()

    barrier = pltpu.get_barrier_semaphore()
    plane_peers = [
        (ci, (z * YN + yi) * XN + xi) for ci in (core, other) for yi in (y, yo) for xi in (x, xo)
    ][1:]
    peers = plane_peers + [chip(zi, y, x) for zi in z_peers]
    for peer in peers:
        pl.semaphore_signal(barrier, inc=1, device_id=peer, device_id_type=MESH)

    rows = hidden // units
    half_rows = rows // 2

    def put_own(m, value, lanes):
        halves = value.astype(BF).reshape(2, half_rows, -1)
        for h in range(2):
            pl.when(core == h)(functools.partial(put_half, m, halves[h], halves[1 - h], lanes))

    def put_half(m, kept, given, lanes):
        wg[core, m, z, y, x, core, :, lanes] = kept
        handed[m, :, lanes] = given

    for load in small_loads:
        load.wait()
    pad[...] = jnp.zeros_like(pad)
    pad[0:rows, 0:past] = first[0] * 0.5
    put_own(0, pad[0:rows, :], slice(0, 128))
    pad[...] = jnp.zeros_like(pad)
    pad[span : span + 4, 0:rows] = biases[0] * 0.5
    bias_cols = pad[...].T[0:rows]
    pad[...] = jnp.zeros_like(pad)
    pad[0:rows, 0:span] = head[0, :, past : past + span]
    put_own(0, pad[0:rows, :] + bias_cols, slice(128, 256))
    pad[...] = jnp.zeros_like(pad)
    pad[0:rows, 0:past] = head[0, :, 0:past]
    put_own(0, pad[0:rows, :], slice(256, 384))
    for m in range(5):
        put_own(m + 1, square[0, m] * 0.5 if m < 3 else square[0, m], slice(0, hidden))
    pl.semaphore_wait(barrier, len(peers))

    handed[0, :, 384:512] = jnp.zeros((half_rows, 128), BF)
    own = remote(handed, wg.at[core, :, z, y, x, other], own_send.at[0], own_recv.at[0], sibling)
    own.start()

    def of(i):
        return lax.div(i, MATS), lax.rem(i, MATS)

    def sends(sems, kind, lanes):
        return sems.at[kind, 0 if lanes.stop == hidden else 1]

    def z_copies(i, lanes):
        b, m = of(i)
        part = wg.at[b, m, z, y, x, core, :, lanes]
        return [
            remote(part, part, sends(ag_send, 0, lanes), ag_recv.at[i, s], chip(zi, y, x)) for s, zi in enumerate(z_peers)
        ]

    def column_copies(i, lanes):
        b, m = of(i)
        part = wg.at[b, m, :, y, x, core, :, lanes]
        return [
            remote(part, part, sends(ag_send, 1, lanes), ag_recv.at[i, 3], chip(z, near_y, near_x)),
            remote(part, part, sends(ag_send, 1, lanes), ag_recv.at[i, 4], chip(z, far_y, far_x)),
        ]

    def corner_copy(i, lanes):
        b, m = of(i)
        part = wg.at[b, m, :, near_y, near_x, core, :, lanes]
        return remote(part, part, sends(ag_send, 2, lanes), ag_recv.at[i, 5], chip(z, far_y, far_x))

    def core_copy(i, lanes):
        b, m = of(i)
        part = wg.at[b, m, :, :, :, core, :, lanes]
        return remote(part, part, sends(ag_send, 3, lanes), ag_recv.at[i, 6], sibling)

    def by_lanes(m, step):
        pl.when(m == 0)(lambda: step(slice(0, 384)))
        pl.when(m > 0)(lambda: step(slice(0, hidden)))

    def start_all(copies):
        for copy in copies:
            copy.start()

    for load in loads:
        load.wait()
    zeros_tile = jnp.zeros((tile, 128), F32)

    def prepare(t, carry):
        at = pl.ds(t * tile, tile)
        resid[at, :] = zeros_tile
        resid[at, 0:past] = seg[at, :]
        return carry

    def prepare_mask(g, carry):
        lengths = ext[pl.ds(core * (windows // 128) + g, 1), :]
        position = lax.broadcasted_iota(jnp.int32, (128, 128), 0)
        keep = jnp.where(position >= past - lengths, 1.0, 0.0).astype(F32).T
        at = pl.ds(pl.multiple_of(g * 128, 128), 128)
        pad[0:span, :] = adj[:, at]
        f_ref[at, :] = pad[...].T.astype(BF)
        f_t[:, at] = pad[...].astype(BF)
        mask[at, :] = keep.astype(BF)
        resid[at, :] = resid[at, :] * keep
        return carry

    tiles = windows // tile
    part_tile = windows // 2

    def matrix(b, m):
        return wg[b, m].reshape(hidden, hidden)

    def small(b, lane):
        return wg[b, 0, :, :, :, :, :, lane : lane + 128].reshape(hidden, 128)

    def store_layer(b, k, at, v):
        p = 1.0 + jnp.tanh(v)
        a = v * p
        rate = p + a * (2.0 - p)
        slope[b, k, at, :] = rate.astype(BF)
        low = a.astype(BF)
        act_t[b, k, :, at] = low.T
        return low

    def halves(body):
        for t in range(2):
            body(slice(t * windows // 2, (t + 1) * windows // 2))

    def layer_zero(b):
        bias_t[...] = small(b, 128).astype(F32).T

        def body(at):
            a = resid[at, :].astype(BF)
            in_t[b, :, at] = a.T
            work[0, at, :] = store_layer(b, 0, at, dot_nt(a, small(b, 0)) + bias_t[span : span + 1, :])

        halves(body)

    def layer_next(b, k):
        source, target = lax.rem(k + 1, 2), lax.rem(k, 2)
        v = dot_nn(work[source], matrix(b, k)) + bias_t[pl.ds(span + k, 1), :]
        work[target] = store_layer(b, k, slice(0, windows), v)

    def grid(value):
        return value.astype(BF).reshape(ZN, YN, XN, 2, half_rows, -1)

    def head_grad(acc, lane, b):
        gp[b, 0, :, :, :, :, :, lane : lane + 128] = grid(acc[...].T)

    def backcast_step(b):
        @pl.when(b == 0)
        def _():
            def body(at):
                theta = dot_nn(work[1, at, :], matrix(b, 4)).astype(BF)
                theta_keep[at, :] = theta
                resid[at, :] = (resid[at, :] - dot_nn(theta, small(b, 256))) * mask[at, :].astype(F32)

            halves(body)

        @pl.when(b == 1)
        def _():
            head_acc[...] = jnp.zeros_like(head_acc)

            def body(at):
                theta = dot_nn(work[1, at, :], matrix(b, 4)).astype(BF)
                head_acc[...] += dot_nn(e_t[:, at], theta)

            halves(body)
            head_grad(head_acc, 256, b)

    def put_rows(buf, b, at, value):
        for row in range(value.shape[0]):
            buf[b, row, :, at] = value[row : row + 1]

    def forecast_step(b):
        head_acc[...] = jnp.zeros_like(head_acc)

        def body(at):
            theta = dot_nn(work[1, at, :], matrix(b, 5)).astype(BF)
            head_acc[...] += dot_nn(f_t[:, at], theta)
            part_t[:, at] = dot_nn(theta, small(b, 128)).T[0:span]

        halves(body)
        head_grad(head_acc, 128, b)

        @pl.when(b == 0)
        def _():
            put_rows(pred, 0, slice(0, windows), part_t[...])
            first_part[...] = part_t[...]

        @pl.when(b == 1)
        def _():
            put_rows(pred, 1, slice(0, windows), first_part[...].astype(BF).astype(F32) + part_t[...])

    count = 2 * MATS

    def delayed(lag, t, step):
        pl.when(jnp.logical_and(t >= lag, t < count + lag))(lambda: step(t - lag))

    def gather_line(i):
        by_lanes(of(i)[1], lambda lanes: start_all(z_copies(i, lanes)))

    def gather_columns(i):
        def step(lanes):
            for copy in z_copies(i, lanes):
                copy.wait_recv()
            start_all(column_copies(i, lanes))

        by_lanes(of(i)[1], step)

    def gather_corner(i):
        def step(lanes):
            column_copies(i, lanes)[0].wait_recv()
            corner_copy(i, lanes).start()

        by_lanes(of(i)[1], step)

    def gather_core(i):
        def step(lanes):
            column_copies(i, lanes)[1].wait_recv()
            corner_copy(i, lanes).wait_recv()
            core_copy(i, lanes).start()

        by_lanes(of(i)[1], step)

    def forward_unit(i):
        b, m = of(i)
        by_lanes(m, lambda lanes: core_copy(i, lanes).wait_recv())
        pl.when(m == 0)(lambda: layer_zero(b))
        pl.when(jnp.logical_and(m >= 1, m <= 3))(lambda: layer_next(b, m))
        pl.when(m == 4)(lambda: backcast_step(b))
        pl.when(m == 5)(lambda: forecast_step(b))

        @pl.when(m == jnp.where(b == 1, 3, 5))
        def _():
            pl.when(b == 1)(lambda: feed(b))
            pl.when(b == 0)(lambda: feed_forward(b))
            lax.fori_loop(jnp.where(b == 1, 4, 5), MATS, lambda n, carry: (theta_grad(b, n), carry)[1], 0)

            @pl.when(b == 1)
            def _():
                scatter_start(0)
                scatter_start(1)

    def gather_step(t, carry):
        delayed(4, t, gather_core)
        delayed(2, t, gather_corner)
        delayed(0, t, gather_columns)
        pl.when(t + 4 < count)(lambda: gather_line(t + 4))
        delayed(5, t, forward_unit)
        return carry

    def out_copies(buf, out, s):
        at = pl.ds(row0, windows)
        return [
            pltpu.make_async_copy(buf.at[core], out.at[:, :, at], local_sem.at[2 + s]),
            remote(buf.at[other], out.at[:, :, at], out_send.at[s], out_recv.at[s], sibling),
        ]


    def back_of(j):
        b = jnp.where(jnp.logical_or(j <= 1, jnp.logical_and(j >= 3, j <= 6)), 1, 0)
        m = jnp.where(j <= 1, 4 + j, jnp.where(j == 2, 5, jnp.where(j <= 6, 6 - j, jnp.where(j == 7, 4, 11 - j))))
        return b, m

    def to_core(j, lanes):
        b, m = back_of(j)
        return remote(
            gp.at[b, m, :, :, :, other, :, lanes], from_core.at[lax.rem(j, CORE_SLOTS), :, :, :, :, lanes],
            sends(rs_send, 3, lanes), rs_recv.at[j, 0], sibling,
        )

    def to_far(j, lanes):
        b, m = back_of(j)
        device = chip(z, far_y, far_x)
        return [
            remote(
                gp.at[b, m, :, yo, xo, core, :, lanes], from_diag.at[lax.rem(j, DIAG_SLOTS), :, :, lanes],
                sends(rs_send, 1, lanes), rs_recv.at[j, 1], device,
            ),
            remote(
                gp.at[b, m, :, far_y, far_x, core, :, lanes], from_plain.at[lax.rem(j, PLAIN_SLOTS), :, :, lanes],
                sends(rs_send, 1, lanes), rs_recv.at[j, 2], device,
            ),
        ]

    def to_near(j, lanes):
        b, m = back_of(j)
        return remote(
            gp.at[b, m, :, near_y, near_x, core, :, lanes], from_pair.at[lax.rem(j, PAIR_SLOTS), :, :, lanes],
            sends(rs_send, 2, lanes), rs_recv.at[j, 3], chip(z, near_y, near_x),
        )

    def to_z(j, lanes):
        b, m = back_of(j)
        return [
            remote(
                gp.at[b, m, zi, y, x, core, :, lanes], from_z.at[lax.rem(j, Z_SLOTS), s, :, lanes],
                sends(rs_send, 0, lanes), rs_recv.at[j, 4 + s], chip(zi, y, x),
            )
            for s, zi in enumerate(z_peers)
        ]

    def scatter_start(j):
        by_lanes(back_of(j)[1], lambda lanes: to_core(j, lanes).start())

    def scatter_core(j):
        b, m = back_of(j)

        def step(lanes):
            to_core(j, lanes).wait_recv()
            part = gp[b, m, :, :, :, core, :, lanes] + from_core[lax.rem(j, CORE_SLOTS), :, :, :, :, lanes]
            gp[b, m, :, :, :, core, :, lanes] = part
            start_all(to_far(j, lanes))

        by_lanes(m, step)

    def scatter_diag(j):
        b, m = back_of(j)

        def step(lanes):
            to_far(j, lanes)[0].wait_recv()
            part = gp[b, m, :, near_y, near_x, core, :, lanes] + from_diag[lax.rem(j, DIAG_SLOTS), :, :, lanes]
            gp[b, m, :, near_y, near_x, core, :, lanes] = part
            to_near(j, lanes).start()

        by_lanes(m, step)

    def scatter_plane(j):
        b, m = back_of(j)

        def step(lanes):
            to_far(j, lanes)[1].wait_recv()
            to_near(j, lanes).wait_recv()
            value = gp[b, m, :, y, x, core, :, lanes].astype(F32)
            value = value + from_plain[lax.rem(j, PLAIN_SLOTS), :, :, lanes].astype(F32)
            value = value + from_pair[lax.rem(j, PAIR_SLOTS), :, :, lanes].astype(F32)
            gp[b, m, :, y, x, core, :, lanes] = value.astype(BF)
            start_all(to_z(j, lanes))

        by_lanes(m, step)

    def scatter_z(j):
        b, m = back_of(j)

        def step(lanes):
            for copy in to_z(j, lanes):
                copy.wait_recv()
            value = gp[b, m, z, y, x, core, :, lanes].astype(F32)
            for s in range(ZN - 1):
                value = value + from_z[lax.rem(j, Z_SLOTS), s, :, lanes].astype(F32)
            total[b, m, :, lanes] = value
            squares[:, lanes] = squares[:, lanes] + value * value

        by_lanes(m, step)

    def add_rows(value):
        return jnp.sum(value.reshape(-1, 8, hidden), axis=0)

    def put_bias(k, acc):
        bias_sum[pl.ds(span + k, 1), :] = jnp.sum(acc, axis=0, keepdims=True)

    def feed(b):
        pl.when(b == 1)(lambda: resid.__setitem__(..., jnp.zeros_like(resid)))
        e = (-(resid[...] * mask[...].astype(F32))).astype(BF)
        e_t[...] = e.T
        work[0] = dot_nt(e, small(b, 256)).astype(BF)
        work[2] = dot_nt(f_ref[...], small(b, 128)).astype(BF)

    def feed_forward(b):
        work[2] = dot_nt(f_ref[...], small(b, 128)).astype(BF)

    def put_dz(b, k, da):
        dz = da * slope[b, k].astype(F32)
        work[k % 2 if isinstance(k, int) else lax.rem(k, 2)] = dz.astype(BF)
        bias_sum[pl.ds(span + k, 1), :] = jnp.sum(add_rows(dz), axis=0, keepdims=True)

    def theta_step(b):
        put_dz(b, 3, 0.5 * (dot_nt(work[0], matrix(b, 4)) + dot_nt(work[2], matrix(b, 5))))

    def layer_back(b, k):
        source = lax.rem(k, 2)
        gp[b, k] = grid(dot_nn(act_t[b, k - 1], work[source]))
        put_dz(b, k - 1, dot_nt(work[source], matrix(b, k)))

    def theta_grad(b, m):
        gp[b, m] = grid(dot_nn(act_t[b, 3], work[jnp.where(m == 4, 0, 2)]))

    def small_grads(b):
        gp[b, 0, :, :, :, :, :, 0:128] = grid(dot_nn(in_t[b], work[0]).T)
        gp[b, 0, :, :, :, :, :, 128:256] = gp[b, 0, :, :, :, :, :, 128:256] + grid(bias_sum[...].T)

        @pl.when(b == 0)
        def _():
            head_acc[...] = dot_nn(e_t[...], theta_keep[...])
            head_grad(head_acc, 256, b)


    def input_grad(b):
        for t in range(2):
            at = slice(t * windows // 2, (t + 1) * windows // 2)
            keep = mask[at, :].astype(F32)
            dr = resid[at, :] * keep + 2.0 * dot_nn(work[0, at, :], small(b, 0))

            @pl.when(b == 1)
            def _():
                seg[at, :] = dr[:, 0:past]
                resid[at, :] = dr.astype(BF).astype(F32)

            @pl.when(b == 0)
            def _():
                put_rows(sens, 0, at, (dr * keep).T[0:past])

    def late_rows():
        for g in range(windows // 128):
            at = slice(g * 128, (g + 1) * 128)
            pad[:, 0:past] = seg[at, :]
            put_rows(sens, 1, at, pad[...].T[0:past])

    bias_sum[...] = jnp.zeros_like(bias_sum)
    squares[...] = jnp.zeros_like(squares)
    total[...] = jnp.zeros_like(total)

    def back_step(j, carry):
        b, m = back_of(j)
        live = jnp.logical_and(j >= 3, j < count)

        def on(test, step):
            pl.when(jnp.logical_and(live, test))(step)

        delayed(8, j, scatter_z)
        delayed(6, j, scatter_plane)
        delayed(4, j, scatter_diag)
        delayed(2, j, scatter_core)
        pl.when(j == 2)(lambda: theta_step(1))
        on(jnp.logical_and(m >= 1, m <= 3), lambda: layer_back(b, m))
        on(m == 0, lambda: small_grads(b))

        @pl.when(j == 7)
        def _():
            feed(b)
            theta_grad(b, 4)
            theta_step(b)

        pl.when(jnp.logical_and(j >= 2, j < count))(lambda: scatter_start(j))
        on(m == 0, lambda: input_grad(b))

        @pl.when(j == count)
        def _():
            late_rows()
            start_all(out_copies(sens, sens_out, 1))

        return carry

    own.wait_recv()
    for i in range(4):
        gather_line(i)
    lax.fori_loop(0, tiles, prepare, 0)
    pad[...] = jnp.zeros_like(pad)
    lax.fori_loop(0, windows // 128, prepare_mask, 0)
    lax.fori_loop(0, count + 5, gather_step, 0)

    start_all(out_copies(pred, pred_out, 0))
    lax.fori_loop(0, count + 8, back_step, 0)

    grad_copy = remote(total.at[other], grad_out.at[:, core], out_send.at[2], out_recv.at[2], sibling)
    grad_copy.start()
    grad_out[:, core] = total[core]
    sq = squares[:, 0:128] + squares[:, 128:256] + squares[:, 256:384] + squares[:, 384:512]
    place = (y * XN + x) * 2 + core
    norm_buf[place] = sq[0:8] + sq[8:16]

    def spread(sources, targets, first):
        copies = [
            remote(norm_buf.at[sources], norm_buf.at[sources], norm_send.at[first + s], norm_recv.at[first + s], device)
            for s, device in enumerate(targets)
        ]
        start_all(copies)
        for copy in copies:
            copy.wait()

    def add_up(slots):
        value = norm_buf[slots[0]]
        for slot in slots[1:]:
            value = value + norm_buf[slot]
        return value

    spread(place, plane_peers, 0)
    norm_buf[8 + z] = add_up(range(8))
    spread(8 + z, [chip(zi, y, x) for zi in z_peers], 7)
    everything = add_up(range(8, 8 + ZN))
    norm_out[...] = jnp.broadcast_to(jnp.sqrt(jnp.sum(everything, keepdims=True)), norm_out.shape)

    grad_copy.wait()
    for buf, out, s in ((pred, pred_out, 0), (sens, sens_out, 1)):
        for copy in out_copies(buf, out, s):
            copy.wait()
    own.wait_send()

    for mats, lanes in ((slice(1, MATS), slice(0, hidden)), (slice(0, 1), slice(0, 384))):
        sent = (
            wg.at[:, mats, 0 : ZN - 1, 0, 0, 0, :, lanes],
            wg.at[:, mats, :, :, 0, 0, :, lanes],
            wg.at[:, mats, :, 0, 0, 0, :, lanes],
            wg.at[:, mats, :, :, :, 0, :, lanes],
        )
        for sems in (ag_send, rs_send):
            for kind, ref in enumerate(sent):
                remote(ref, ref, sends(sems, kind, lanes), out_recv.at[0], sibling).wait_send()


def train_call(plane, segments, extents, adjoint, first, square, head, biases):
    ZN, YN, XN = plane
    past, span, hidden = segments.shape[1], adjoint.shape[0], square.shape[3]
    windows = segments.shape[0] // 2
    tile = windows
    half = hidden // (ZN * YN * XN) // 2
    sizes = (ZN, YN, XN, windows, tile, past, span, hidden)
    DMA = pltpu.SemaphoreType.DMA
    vmem = pl.BlockSpec(memory_space=pltpu.VMEM)
    hbm = pl.BlockSpec(memory_space=pl.ANY)
    count = 2 * MATS
    flops = 2 * 2 * 3 * windows * hidden * (6 * hidden + 2 * 128)
    lengths = extents.reshape(-1, 128)
    return pl.pallas_call(
        functools.partial(train_kernel, sizes),
        out_shape=(
            jax.ShapeDtypeStruct((span, 1, 2 * windows), F32),
            jax.ShapeDtypeStruct((past, 1, 2 * windows), F32),
            jax.ShapeDtypeStruct((MATS, 2, half, hidden), F32),
            jax.ShapeDtypeStruct((8, 128), F32),
        ),
        in_specs=[hbm] * 7,
        out_specs=(hbm, hbm, vmem, vmem),
        scratch_shapes=[
            pltpu.VMEM((2, MATS, ZN, YN, XN, 2, half, hidden), BF),
            pltpu.VMEM((MATS, half, hidden), BF),
            pltpu.VMEM((2, MATS, ZN, YN, XN, 2, half, hidden), BF),
            pltpu.VMEM((CORE_SLOTS, ZN, YN, XN, half, hidden), BF),
            pltpu.VMEM((DIAG_SLOTS, ZN, half, hidden), BF),
            pltpu.VMEM((PLAIN_SLOTS, ZN, half, hidden), BF),
            pltpu.VMEM((PAIR_SLOTS, ZN, half, hidden), BF),
            pltpu.VMEM((Z_SLOTS, ZN - 1, half, hidden), BF),
            pltpu.VMEM((2, MATS, half, hidden), F32),
            pltpu.VMEM((2, 4, hidden, windows), BF),
            pltpu.VMEM((2, 128, windows), BF),
            pltpu.VMEM((windows, hidden), BF),
            pltpu.VMEM((128, hidden), F32),
            pltpu.VMEM((2, 4, windows, hidden), BF),
            pltpu.VMEM((3, windows, hidden), BF),
            pltpu.VMEM((windows, 128), F32),
            pltpu.VMEM((windows, 128), BF),
            pltpu.VMEM((windows, 128), BF),
            pltpu.VMEM((128, windows), BF),
            pltpu.VMEM((128, windows), BF),
            pltpu.VMEM((128, hidden), F32),
            pltpu.VMEM((128, hidden), F32),
            pltpu.VMEM((128, 128), F32),
            pltpu.VMEM((windows, past), F32),
            pltpu.VMEM((span, windows), F32),
            *(pltpu.VMEM(a.shape, a.dtype) for a in (lengths, first, square, head, biases)),
            pltpu.VMEM((span, windows), F32),
            pltpu.VMEM((span, windows), F32),
            pltpu.VMEM((2, span, 1, windows), F32),
            pltpu.VMEM((2, past, 1, windows), F32),
            pltpu.VMEM((half, hidden), F32),
            pltpu.VMEM((8 + ZN, 8, 128), F32),
            DMA((1,)),
            DMA((1,)),
            DMA((4, 2)),
            DMA((count, 4 + ZN - 1)),
            DMA((4, 2)),
            DMA((count, 4 + ZN - 1)),
            DMA((3,)),
            DMA((3,)),
            DMA((9,)),
            DMA((7 + ZN - 1,)),
            DMA((7 + ZN - 1,)),
        ],
        compiler_params=pltpu.CompilerParams(
            collective_id=0, has_side_effects=True, vmem_limit_bytes=64 * 1024 * 1024
        ),
        cost_estimate=pl.CostEstimate(flops=flops, bytes_accessed=8_000_000, transcendentals=8 * windows * hidden),
        name="train",
    )(segments, adjoint, lengths, first, square, head, biases)


def update_kernel(past, span, *refs):
    sources, targets, norm_out = refs[0:16], refs[16:34], refs[34]
    held, results, pad, in_sem, out_sem = refs[35:51], refs[51:67], *refs[67:70]
    arriving = [pltpu.make_async_copy(source, ref, in_sem.at[n]) for n, (source, ref) in enumerate(zip(sources, held))]
    leaving = [
        pltpu.make_async_copy(ref, target, out_sem.at[n]) for n, (ref, target) in enumerate(zip(held[0:2] + results, targets))
    ]
    for copy in arriving:
        copy.start()
    grads, norm, masters, momenta, variances = held[2], held[3], held[4:8], held[8:12], held[12:16]
    units = masters[3].shape[2]

    def rows(m, lane, width):
        return grads[m, :, :, lane : lane + width].reshape(units, width)

    arriving[2].wait()
    arriving[3].wait()
    norm_out[...] = norm[0:1, 0:1]
    factor = 1.0 / jnp.maximum(norm[0:1, 0:1], 1.0)
    for m in range(5):
        results[1][0, m] = rows(m + 1, 0, grads.shape[3])
    results[0][0] = rows(0, 0, 128)[:, 0:past]
    forecast = rows(0, 128, 128)
    pad[...] = jnp.zeros_like(pad)
    pad[0:units, :] = forecast
    results[3][0] = pad[...].T[span : span + 4, 0:units]
    results[2][0, :, 0:past] = rows(0, 256, 128)[:, 0:past]
    results[2][0, :, past : past + span] = forecast[:, 0:span]
    for n in (0, 1):
        arriving[n].wait()
        leaving[n].start()
    for n in (1, 0, 2, 3):
        leaving[2 + n].start()
        for state in range(3):
            arriving[4 + 4 * state + n].wait()
        updated = adamw(masters[n][...], results[n][...], momenta[n][...], variances[n][...], factor[None])
        for kind, value in enumerate(updated):
            results[4 * (kind + 1) + n][...] = value
            leaving[2 + 4 * (kind + 1) + n].start()
    for copy in leaving:
        copy.wait()


def update_call(prediction, sensitivity, grads, norm, state):
    hbm = pl.BlockSpec(memory_space=pl.ANY)
    sources = (prediction, sensitivity, grads, norm, *state)
    targets = (prediction, sensitivity, *(4 * list(state[:4])))
    return pl.pallas_call(
        functools.partial(update_kernel, sensitivity.shape[0], prediction.shape[0]),
        out_shape=tuple(jax.ShapeDtypeStruct(a.shape, F32) for a in targets) + (jax.ShapeDtypeStruct((1, 1), F32),),
        in_specs=[hbm] * len(sources),
        out_specs=tuple([hbm] * len(targets) + [pl.BlockSpec(memory_space=pltpu.VMEM)]),
        scratch_shapes=[pltpu.VMEM(a.shape, F32) for a in sources]
        + [pltpu.VMEM(a.shape, F32) for a in targets[2:]]
        + [pltpu.VMEM((128, 128), F32), pltpu.SemaphoreType.DMA((len(sources),)), pltpu.SemaphoreType.DMA((len(targets),))],
        name="update",
    )(*sources)


def turned(arrays):
    return [a.transpose(0, 2, 1) if n % 4 == 0 else a for n, a in enumerate(arrays)]


def kernel_shards(plane, segments, extents, adjoint, *state):
    state = turned(state)
    results = train_call(plane, segments, extents, adjoint.T, *state[:4])
    prediction, sensitivity, *updated, norm = update_call(*results, state)
    by_window = (prediction.transpose(1, 2, 0), sensitivity.transpose(1, 2, 0))
    return (*by_window, norm.reshape(()), *turned(updated))


STATE_SPECS = (
    P("section", None, "dp"),
    P("section", None, "dp", None),
    P("section", "dp", None),
    P("section", None, "dp"),
)


def solution(mesh):
    in_specs = (P("dp", None), P("dp"), P("dp", None)) + 3 * STATE_SPECS
    out_specs = (P("section", "dp", None), P("section", "dp", None), P()) + 4 * STATE_SPECS
    plane = PLANES.get(mesh.shape["dp"])
    shards = plain_shards if plane is None else functools.partial(kernel_shards, plane)
    return jax.shard_map(shards, mesh=mesh, in_specs=in_specs, out_specs=out_specs, check_vma=False)
```

```python
import functools

import jax
import jax.numpy as jnp
from jax import lax
from jax.experimental import pallas as pl
from jax.experimental.pallas import tpu as pltpu
from jax.sharding import PartitionSpec as P

STEP = 10


def dot_nn(a, b):
    return jnp.dot(a, b, preferred_element_type=jnp.float32)


def dot_tn(a, b):
    return lax.dot_general(a, b, (((0,), (0,)), ((), ())), preferred_element_type=jnp.float32)


def dot_nt(a, b):
    return lax.dot_general(a, b, (((1,), (1,)), ((), ())), preferred_element_type=jnp.float32)


def unit_rows(first, square, head, biases):
    units = first.shape[1]
    return jnp.concatenate(
        [square.transpose(1, 0, 2).reshape(units, -1), first.T, head, biases.T], axis=1
    )


def from_unit_rows(rows, past, hidden, out):
    wide = 5 * hidden
    square = rows[:, :wide].reshape(-1, 5, hidden).transpose(1, 0, 2)
    first = rows[:, wide : wide + past].T
    head = rows[:, wide + past : wide + past + out]
    biases = rows[:, wide + past + out :].T
    return first, square, head, biases


def plain_forward(weights, resid):
    first, square, head, biases = weights
    past = resid.shape[1]
    acts, slopes = [resid.astype(jnp.bfloat16)], []
    for k in range(4):
        z = dot_nn(acts[-1], first if k == 0 else square[k - 1]) + biases[k].astype(jnp.float32)
        sig = jax.nn.sigmoid(z)
        acts.append((z * sig).astype(jnp.bfloat16))
        slopes.append(sig * (1.0 + z * (1.0 - sig)))
    theta_b = dot_nn(acts[4], square[3]).astype(jnp.bfloat16)
    theta_f = dot_nn(acts[4], square[4]).astype(jnp.bfloat16)
    backcast = dot_nn(theta_b, head[:, :past])
    part = dot_nn(theta_f, head[:, past:])
    return backcast, part, (acts, slopes, theta_b, theta_f)


def plain_backward(weights, saved, e, f):
    first, square, head, biases = weights
    acts, slopes, theta_b, theta_f = saved
    past = e.shape[1]
    head_grad = jnp.concatenate([dot_tn(theta_b, e), dot_tn(theta_f, f)], axis=1)
    u_b = dot_nt(e, head[:, :past]).astype(jnp.bfloat16)
    u_f = dot_nt(f, head[:, past:]).astype(jnp.bfloat16)
    squares = [None, None, None, dot_tn(acts[4], u_b), dot_tn(acts[4], u_f)]
    da = dot_nt(u_b, square[3]) + dot_nt(u_f, square[4])
    bias_grads = [None] * 4
    first_grad = None
    for k in (3, 2, 1, 0):
        dz = (da * slopes[k]).astype(jnp.bfloat16)
        bias_grads[k] = jnp.sum(dz, axis=0, dtype=jnp.float32)
        grad = dot_tn(acts[k], dz)
        if k == 0:
            first_grad = grad
        else:
            squares[k - 1] = grad
        da = dot_nt(dz, first if k == 0 else square[k - 1])
    return da, (first_grad, jnp.stack(squares), head_grad, jnp.stack(bias_grads))


def adamw(master, gradient, momentum, variance, factor):
    clipped = gradient * factor
    moment_new = 0.9 * momentum + 0.1 * clipped
    variance_new = 0.999 * variance + 0.001 * clipped * clipped
    ratio = moment_new / (1.0 - 0.9**STEP) / (jnp.sqrt(variance_new / (1.0 - 0.999**STEP)) + 1e-08)
    return master - 0.05 * (ratio + 0.01 * master), moment_new, variance_new


def plain_shards(segments, extents, adjoint, *state):
    masters, momenta, variances = state[:4], state[4:8], state[8:]
    core = lax.axis_index("section")
    past, span = segments.shape[1], adjoint.shape[1]
    windows = segments.shape[0] // 2
    hidden = masters[1].shape[3]
    mine = [
        lax.dynamic_slice_in_dim(v, core * windows, windows, 0) for v in (segments, extents, adjoint)
    ]
    seg, ext, adj = mine
    rows = unit_rows(*(m[0].astype(jnp.bfloat16) for m in masters))
    rows = lax.all_gather(rows, "dp", axis=0, tiled=True)
    rows = lax.all_gather(rows, "section", axis=0)
    blocks = [from_unit_rows(rows[b], past, hidden, past + span) for b in range(2)]
    mask = (
        lax.broadcasted_iota(jnp.int32, (windows, past), 1) >= past - ext[:, None]
    ).astype(jnp.float32)
    r0 = seg * mask
    backcast, part0, saved0 = plain_forward(blocks[0], r0)
    r1 = (r0 - backcast) * mask
    _, part1, saved1 = plain_forward(blocks[1], r1)
    forecast = part0.astype(jnp.bfloat16).astype(jnp.float32) + part1
    f = adj.astype(jnp.bfloat16)
    zero = jnp.zeros_like(r0)
    da1, grads1 = plain_backward(blocks[1], saved1, (-(zero * mask)).astype(jnp.bfloat16), f)
    dr1 = zero * mask + da1
    t = dr1.astype(jnp.bfloat16).astype(jnp.float32)
    da0, grads0 = plain_backward(blocks[0], saved0, (-(t * mask)).astype(jnp.bfloat16), f)
    dr0 = (t * mask + da0) * mask

    def by_section(first_block, second_block):
        mine, other = (
            jnp.where(core == 0, first_block, second_block),
            jnp.where(core == 0, second_block, first_block),
        )
        got = lax.ppermute(other, "section", [(0, 1), (1, 0)])
        return jnp.where(
            core == 0, jnp.concatenate([mine, got]), jnp.concatenate([got, mine])
        )[None]

    prediction = by_section(part0, forecast)
    sensitivity = by_section(dr0, dr1)
    packed = jnp.stack([unit_rows(*grads0), unit_rows(*grads1)])
    packed = lax.psum_scatter(packed, "section", scatter_dimension=0, tiled=False)
    packed = lax.psum_scatter(packed, "dp", scatter_dimension=0, tiled=True)
    norm = jnp.sqrt(lax.psum(jnp.sum(packed * packed), ("section", "dp")))
    factor = 1.0 / jnp.maximum(norm, 1.0)
    summed = [g[None] for g in from_unit_rows(packed, past, hidden, past + span)]
    updated = [adamw(*four, factor) for four in zip(masters, summed, momenta, variances)]
    return (
        prediction,
        sensitivity,
        norm,
        *summed,
        *(u[0] for u in updated),
        *(u[1] for u in updated),
        *(u[2] for u in updated),
    )


PLANES = {16: (4, 2, 2)}
MESH = pl.DeviceIdType.MESH
MATS = 6
LAG = 3
CORE_SLOTS, DIAG_SLOTS, PLAIN_SLOTS, PAIR_SLOTS, Z_SLOTS = 2 * LAG, 2 * LAG, 3 * LAG, 2 * LAG, 2 * LAG
EARLY = 3
BF, F32 = jnp.bfloat16, jnp.float32


def remote(src, dst, send_sem, recv_sem, device):
    return pltpu.make_async_remote_copy(
        src_ref=src, dst_ref=dst, send_sem=send_sem, recv_sem=recv_sem, device_id=device, device_id_type=MESH
    )


def train_kernel(
    sizes,
    seg_hbm, adj_hbm, ext_hbm, first_hbm, square_hbm, head_hbm, biases_hbm,
    pred_out, sens_out, grad_out, norm_out,
    wg, handed, gp, from_core, from_diag, from_plain, from_pair, from_z, total,
    act_t, in_t, theta_keep, head_acc, slope, work, resid, mask, f_ref, f_t, e_t, bias_t, bias_sum, pad,
    seg, adj, ext, first, square, head, biases, first_part, part_t, pred, sens, squares, norm_buf,
    own_send, own_recv, ag_send, ag_recv, rs_send, rs_recv, out_send, out_recv, local_sem, norm_send, norm_recv,
):
    ZN, YN, XN, windows, tile, past, span, hidden = sizes
    units = ZN * YN * XN
    core, dp = lax.axis_index("section"), lax.axis_index("dp")
    x, y, z = lax.rem(dp, XN), lax.rem(lax.div(dp, XN), YN), lax.div(dp, XN * YN)
    other, xo, yo = 1 - core, 1 - x, 1 - y
    near_y, near_x = y + core * (yo - y), xo + core * (x - xo)
    far_y, far_x = yo + core * (y - yo), x + core * (xo - x)

    def chip(zi, yi, xi):
        return (core, (zi * YN + yi) * XN + xi)

    sibling = (other, dp)
    z_peers = [lax.rem(z + step, ZN) for step in range(1, ZN)]

    row0 = core * windows
    loads = [
        pltpu.make_async_copy(seg_hbm.at[pl.ds(row0, windows), :], seg, local_sem.at[0]),
        pltpu.make_async_copy(adj_hbm.at[:, pl.ds(row0, windows)], adj, local_sem.at[1]),
    ]
    small_loads = [
        pltpu.make_async_copy(source, target, local_sem.at[4 + n])
        for n, (source, target) in enumerate(
            [(square_hbm, square), (first_hbm, first), (head_hbm, head), (biases_hbm, biases), (ext_hbm, ext)]
        )
    ]
    for load in small_loads + loads:
        load.start()

    barrier = pltpu.get_barrier_semaphore()
    plane_peers = [
        (ci, (z * YN + yi) * XN + xi) for ci in (core, other) for yi in (y, yo) for xi in (x, xo)
    ][1:]
    peers = plane_peers + [chip(zi, y, x) for zi in z_peers]
    for peer in peers:
        pl.semaphore_signal(barrier, inc=1, device_id=peer, device_id_type=MESH)

    rows = hidden // units
    half_rows = rows // 2

    def put_own(m, value, lanes):
        halves = value.astype(BF).reshape(2, half_rows, -1)
        for h in range(2):
            pl.when(core == h)(functools.partial(put_half, m, halves[h], halves[1 - h], lanes))

    def put_half(m, kept, given, lanes):
        wg[core, m, z, y, x, core, :, lanes] = kept
        handed[m, :, lanes] = given

    for load in small_loads:
        load.wait()
    pad[...] = jnp.zeros_like(pad)
    pad[0:rows, 0:past] = first[0] * 0.5
    put_own(0, pad[0:rows, :], slice(0, 128))
    pad[...] = jnp.zeros_like(pad)
    pad[span : span + 4, 0:rows] = biases[0] * 0.5
    bias_cols = pad[...].T[0:rows]
    pad[...] = jnp.zeros_like(pad)
    pad[0:rows, 0:span] = head[0, :, past : past + span]
    put_own(0, pad[0:rows, :] + bias_cols, slice(128, 256))
    pad[...] = jnp.zeros_like(pad)
    pad[0:rows, 0:past] = head[0, :, 0:past]
    put_own(0, pad[0:rows, :], slice(256, 384))
    for m in range(5):
        put_own(m + 1, square[0, m] * 0.5 if m < 3 else square[0, m], slice(0, hidden))
    pl.semaphore_wait(barrier, len(peers))

    handed[0, :, 384:512] = jnp.zeros((half_rows, 128), BF)
    own = remote(handed, wg.at[core, :, z, y, x, other], own_send.at[0], own_recv.at[0], sibling)
    own.start()

    def of(i):
        return lax.div(i, MATS), lax.rem(i, MATS)

    def sends(sems, kind, lanes):
        return sems.at[kind, 0 if lanes.stop == hidden else 1]

    def z_copies(i, lanes):
        b, m = of(i)
        part = wg.at[b, m, z, y, x, core, :, lanes]
        return [
            remote(part, part, sends(ag_send, 0, lanes), ag_recv.at[i, s], chip(zi, y, x)) for s, zi in enumerate(z_peers)
        ]

    def column_copies(i, lanes):
        b, m = of(i)
        part = wg.at[b, m, :, y, x, core, :, lanes]
        return [
            remote(part, part, sends(ag_send, 1, lanes), ag_recv.at[i, 3], chip(z, near_y, near_x)),
            remote(part, part, sends(ag_send, 1, lanes), ag_recv.at[i, 4], chip(z, far_y, far_x)),
        ]

    def corner_copy(i, lanes):
        b, m = of(i)
        part = wg.at[b, m, :, near_y, near_x, core, :, lanes]
        return remote(part, part, sends(ag_send, 2, lanes), ag_recv.at[i, 5], chip(z, far_y, far_x))

    def core_copy(i, lanes):
        b, m = of(i)
        part = wg.at[b, m, :, :, :, core, :, lanes]
        return remote(part, part, sends(ag_send, 3, lanes), ag_recv.at[i, 6], sibling)

    def by_lanes(m, step):
        pl.when(m == 0)(lambda: step(slice(0, 384)))
        pl.when(m > 0)(lambda: step(slice(0, hidden)))

    def start_all(copies):
        for copy in copies:
            copy.start()

    for load in loads:
        load.wait()
    zeros_tile = jnp.zeros((tile, 128), F32)

    def prepare(t, carry):
        at = pl.ds(t * tile, tile)
        resid[at, :] = zeros_tile
        resid[at, 0:past] = seg[at, :]
        return carry

    def prepare_mask(g, carry):
        lengths = ext[pl.ds(core * (windows // 128) + g, 1), :]
        position = lax.broadcasted_iota(jnp.int32, (128, 128), 0)
        keep = jnp.where(position >= past - lengths, 1.0, 0.0).astype(F32).T
        at = pl.ds(pl.multiple_of(g * 128, 128), 128)
        pad[0:span, :] = adj[:, at]
        f_ref[at, :] = pad[...].T.astype(BF)
        f_t[:, at] = pad[...].astype(BF)
        mask[at, :] = keep.astype(BF)
        resid[at, :] = resid[at, :] * keep
        return carry

    tiles = windows // tile
    part_tile = windows // 2

    def matrix(b, m):
        return wg[b, m].reshape(hidden, hidden)

    def small(b, lane):
        return wg[b, 0, :, :, :, :, :, lane : lane + 128].reshape(hidden, 128)

    def store_layer(b, k, at, v):
        p = 1.0 + jnp.tanh(v)
        a = v * p
        rate = p + a * (2.0 - p)
        slope[b, k, at, :] = rate.astype(BF)
        low = a.astype(BF)
        act_t[b, k, :, at] = low.T
        return low

    def halves(body):
        for t in range(2):
            body(slice(t * windows // 2, (t + 1) * windows // 2))

    def layer_zero(b):
        bias_t[...] = small(b, 128).astype(F32).T

        def body(at):
            a = resid[at, :].astype(BF)
            in_t[b, :, at] = a.T
            work[0, at, :] = store_layer(b, 0, at, dot_nt(a, small(b, 0)) + bias_t[span : span + 1, :])

        halves(body)

    def layer_next(b, k):
        source, target = lax.rem(k + 1, 2), lax.rem(k, 2)
        v = dot_nn(work[source], matrix(b, k)) + bias_t[pl.ds(span + k, 1), :]
        work[target] = store_layer(b, k, slice(0, windows), v)

    def grid(value):
        return value.astype(BF).reshape(ZN, YN, XN, 2, half_rows, -1)

    def head_grad(acc, lane, b):
        gp[b, 0, :, :, :, :, :, lane : lane + 128] = grid(acc[...].T)

    def backcast_step(b):
        @pl.when(b == 0)
        def _():
            def body(at):
                theta = dot_nn(work[1, at, :], matrix(b, 4)).astype(BF)
                theta_keep[at, :] = theta
                resid[at, :] = (resid[at, :] - dot_nn(theta, small(b, 256))) * mask[at, :].astype(F32)

            halves(body)

        @pl.when(b == 1)
        def _():
            head_acc[...] = jnp.zeros_like(head_acc)

            def body(at):
                theta = dot_nn(work[1, at, :], matrix(b, 4)).astype(BF)
                head_acc[...] += dot_nn(e_t[:, at], theta)

            halves(body)
            head_grad(head_acc, 256, b)

    def put_rows(buf, b, at, value):
        for row in range(value.shape[0]):
            buf[b, row, :, at] = value[row : row + 1]

    def forecast_step(b):
        head_acc[...] = jnp.zeros_like(head_acc)

        def body(at):
            theta = dot_nn(work[1, at, :], matrix(b, 5)).astype(BF)
            head_acc[...] += dot_nn(f_t[:, at], theta)
            part_t[:, at] = dot_nn(theta, small(b, 128)).T[0:span]

        halves(body)
        head_grad(head_acc, 128, b)

        @pl.when(b == 0)
        def _():
            put_rows(pred, 0, slice(0, windows), part_t[...])
            first_part[...] = part_t[...]

        @pl.when(b == 1)
        def _():
            put_rows(pred, 1, slice(0, windows), first_part[...].astype(BF).astype(F32) + part_t[...])

    count = 2 * MATS

    def delayed(lag, t, step):
        pl.when(jnp.logical_and(t >= lag, t < count + lag))(lambda: step(t - lag))

    def staged(stage, t, step):
        early = t - LAG * (stage - 1)
        pl.when(jnp.logical_and(early >= 0, early < EARLY))(lambda: step(early))
        late = t - LAG * stage
        pl.when(jnp.logical_and(late >= EARLY, late < count))(lambda: step(late))

    def gather_line(i):
        by_lanes(of(i)[1], lambda lanes: start_all(z_copies(i, lanes)))

    def gather_columns(i):
        def step(lanes):
            for copy in z_copies(i, lanes):
                copy.wait_recv()
            start_all(column_copies(i, lanes))

        by_lanes(of(i)[1], step)

    def gather_corner(i):
        def step(lanes):
            column_copies(i, lanes)[0].wait_recv()
            corner_copy(i, lanes).start()

        by_lanes(of(i)[1], step)

    def gather_core(i):
        def step(lanes):
            column_copies(i, lanes)[1].wait_recv()
            corner_copy(i, lanes).wait_recv()
            core_copy(i, lanes).start()

        by_lanes(of(i)[1], step)

    def forward_unit(i):
        b, m = of(i)
        by_lanes(m, lambda lanes: core_copy(i, lanes).wait_recv())
        pl.when(m == 0)(lambda: layer_zero(b))
        pl.when(jnp.logical_and(m >= 1, m <= 3))(lambda: layer_next(b, m))
        pl.when(m == 4)(lambda: backcast_step(b))
        pl.when(m == 5)(lambda: forecast_step(b))

        @pl.when(m == jnp.where(b == 1, 3, 5))
        def _():
            pl.when(b == 1)(lambda: feed(b))
            pl.when(b == 0)(lambda: feed_forward(b))
            lax.fori_loop(jnp.where(b == 1, 4, 5), MATS, lambda n, carry: (theta_grad(b, n), carry)[1], 0)

            @pl.when(b == 1)
            def _():
                scatter_start(0)
                scatter_start(1)

            pl.when(b == 0)(lambda: scatter_start(2))

    def gather_step(t, carry):
        delayed(2 * LAG, t, gather_core)
        delayed(LAG, t, gather_corner)
        delayed(0, t, gather_columns)
        pl.when(t + 4 < count)(lambda: gather_line(t + 4))
        delayed(2 * LAG + 2, t, forward_unit)
        return carry

    def out_copies(buf, out, s):
        at = pl.ds(row0, windows)
        return [
            pltpu.make_async_copy(buf.at[core], out.at[:, :, at], local_sem.at[2 + s]),
            remote(buf.at[other], out.at[:, :, at], out_send.at[s], out_recv.at[s], sibling),
        ]


    def back_of(j):
        b = jnp.where(jnp.logical_or(j <= 1, jnp.logical_and(j >= 3, j <= 6)), 1, 0)
        m = jnp.where(j <= 1, 4 + j, jnp.where(j == 2, 5, jnp.where(j <= 6, 6 - j, jnp.where(j == 7, 4, 11 - j))))
        return b, m

    def to_core(j, lanes):
        b, m = back_of(j)
        return remote(
            gp.at[b, m, :, :, :, other, :, lanes], from_core.at[lax.rem(j, CORE_SLOTS), :, :, :, :, lanes],
            sends(rs_send, 3, lanes), rs_recv.at[j, 0], sibling,
        )

    def to_far(j, lanes):
        b, m = back_of(j)
        device = chip(z, far_y, far_x)
        return [
            remote(
                gp.at[b, m, :, yo, xo, core, :, lanes], from_diag.at[lax.rem(j, DIAG_SLOTS), :, :, lanes],
                sends(rs_send, 1, lanes), rs_recv.at[j, 1], device,
            ),
            remote(
                gp.at[b, m, :, far_y, far_x, core, :, lanes], from_plain.at[lax.rem(j, PLAIN_SLOTS), :, :, lanes],
                sends(rs_send, 1, lanes), rs_recv.at[j, 2], device,
            ),
        ]

    def to_near(j, lanes):
        b, m = back_of(j)
        return remote(
            gp.at[b, m, :, near_y, near_x, core, :, lanes], from_pair.at[lax.rem(j, PAIR_SLOTS), :, :, lanes],
            sends(rs_send, 2, lanes), rs_recv.at[j, 3], chip(z, near_y, near_x),
        )

    def to_z(j, lanes):
        b, m = back_of(j)
        return [
            remote(
                gp.at[b, m, zi, y, x, core, :, lanes], from_z.at[lax.rem(j, Z_SLOTS), s, :, lanes],
                sends(rs_send, 0, lanes), rs_recv.at[j, 4 + s], chip(zi, y, x),
            )
            for s, zi in enumerate(z_peers)
        ]

    def scatter_start(j):
        by_lanes(back_of(j)[1], lambda lanes: to_core(j, lanes).start())

    def scatter_core(j):
        b, m = back_of(j)

        def step(lanes):
            to_core(j, lanes).wait_recv()
            part = gp[b, m, :, :, :, core, :, lanes] + from_core[lax.rem(j, CORE_SLOTS), :, :, :, :, lanes]
            gp[b, m, :, :, :, core, :, lanes] = part
            start_all(to_far(j, lanes))

        by_lanes(m, step)

    def scatter_diag(j):
        b, m = back_of(j)

        def step(lanes):
            to_far(j, lanes)[0].wait_recv()
            part = gp[b, m, :, near_y, near_x, core, :, lanes] + from_diag[lax.rem(j, DIAG_SLOTS), :, :, lanes]
            gp[b, m, :, near_y, near_x, core, :, lanes] = part
            to_near(j, lanes).start()

        by_lanes(m, step)

    def scatter_plane(j):
        b, m = back_of(j)

        def step(lanes):
            to_far(j, lanes)[1].wait_recv()
            to_near(j, lanes).wait_recv()
            value = gp[b, m, :, y, x, core, :, lanes].astype(F32)
            value = value + from_plain[lax.rem(j, PLAIN_SLOTS), :, :, lanes].astype(F32)
            value = value + from_pair[lax.rem(j, PAIR_SLOTS), :, :, lanes].astype(F32)
            gp[b, m, :, y, x, core, :, lanes] = value.astype(BF)
            start_all(to_z(j, lanes))

        by_lanes(m, step)

    def scatter_z(j):
        b, m = back_of(j)

        def step(lanes):
            for copy in to_z(j, lanes):
                copy.wait_recv()
            value = gp[b, m, z, y, x, core, :, lanes].astype(F32)
            for s in range(ZN - 1):
                value = value + from_z[lax.rem(j, Z_SLOTS), s, :, lanes].astype(F32)
            total[b, m, :, lanes] = value
            squares[:, lanes] = squares[:, lanes] + value * value

        by_lanes(m, step)

    def add_rows(value):
        return jnp.sum(value.reshape(-1, 8, hidden), axis=0)

    def put_bias(k, acc):
        bias_sum[pl.ds(span + k, 1), :] = jnp.sum(acc, axis=0, keepdims=True)

    def feed(b):
        pl.when(b == 1)(lambda: resid.__setitem__(..., jnp.zeros_like(resid)))
        e = (-(resid[...] * mask[...].astype(F32))).astype(BF)
        e_t[...] = e.T
        work[0] = dot_nt(e, small(b, 256)).astype(BF)
        work[2] = dot_nt(f_ref[...], small(b, 128)).astype(BF)

    def feed_forward(b):
        work[2] = dot_nt(f_ref[...], small(b, 128)).astype(BF)

    def put_dz(b, k, da):
        dz = da * slope[b, k].astype(F32)
        work[k % 2 if isinstance(k, int) else lax.rem(k, 2)] = dz.astype(BF)
        bias_sum[pl.ds(span + k, 1), :] = jnp.sum(add_rows(dz), axis=0, keepdims=True)

    def theta_step(b):
        put_dz(b, 3, 0.5 * (dot_nt(work[0], matrix(b, 4)) + dot_nt(work[2], matrix(b, 5))))

    def layer_back(b, k):
        source = lax.rem(k, 2)
        gp[b, k] = grid(dot_nn(act_t[b, k - 1], work[source]))
        put_dz(b, k - 1, dot_nt(work[source], matrix(b, k)))

    def theta_grad(b, m):
        gp[b, m] = grid(dot_nn(act_t[b, 3], work[jnp.where(m == 4, 0, 2)]))

    def small_grads(b):
        gp[b, 0, :, :, :, :, :, 0:128] = grid(dot_nn(in_t[b], work[0]).T)
        gp[b, 0, :, :, :, :, :, 128:256] = gp[b, 0, :, :, :, :, :, 128:256] + grid(bias_sum[...].T)

        @pl.when(b == 0)
        def _():
            head_acc[...] = dot_nn(e_t[...], theta_keep[...])
            head_grad(head_acc, 256, b)


    def input_grad(b):
        for t in range(2):
            at = slice(t * windows // 2, (t + 1) * windows // 2)
            keep = mask[at, :].astype(F32)
            dr = resid[at, :] * keep + 2.0 * dot_nn(work[0, at, :], small(b, 0))

            @pl.when(b == 1)
            def _():
                seg[at, :] = dr[:, 0:past]
                resid[at, :] = dr.astype(BF).astype(F32)

            @pl.when(b == 0)
            def _():
                put_rows(sens, 0, at, (dr * keep).T[0:past])

    def late_rows():
        for g in range(windows // 128):
            at = slice(g * 128, (g + 1) * 128)
            pad[:, 0:past] = seg[at, :]
            put_rows(sens, 1, at, pad[...].T[0:past])

    bias_sum[...] = jnp.zeros_like(bias_sum)
    squares[...] = jnp.zeros_like(squares)
    total[...] = jnp.zeros_like(total)

    def back_step(j, carry):
        b, m = back_of(j)
        live = jnp.logical_and(j >= 3, j < count)

        def on(test, step):
            pl.when(jnp.logical_and(live, test))(step)

        staged(4, j, scatter_z)
        staged(3, j, scatter_plane)
        staged(2, j, scatter_diag)
        staged(1, j, scatter_core)
        pl.when(j == 2)(lambda: theta_step(1))
        on(jnp.logical_and(m >= 1, m <= 3), lambda: layer_back(b, m))
        on(m == 0, lambda: small_grads(b))

        @pl.when(j == 7)
        def _():
            feed(b)
            theta_grad(b, 4)
            theta_step(b)

        pl.when(live)(lambda: scatter_start(j))
        on(m == 0, lambda: input_grad(b))

        @pl.when(j == count)
        def _():
            late_rows()
            start_all(out_copies(sens, sens_out, 1))

        return carry

    own.wait_recv()
    for i in range(4):
        gather_line(i)
    lax.fori_loop(0, tiles, prepare, 0)
    pad[...] = jnp.zeros_like(pad)
    lax.fori_loop(0, windows // 128, prepare_mask, 0)
    lax.fori_loop(0, count + 2 * LAG + 2, gather_step, 0)

    start_all(out_copies(pred, pred_out, 0))
    lax.fori_loop(0, count + 4 * LAG, back_step, 0)

    grad_copy = remote(total.at[other], grad_out.at[:, core], out_send.at[2], out_recv.at[2], sibling)
    grad_copy.start()
    grad_out[:, core] = total[core]
    sq = squares[:, 0:128] + squares[:, 128:256] + squares[:, 256:384] + squares[:, 384:512]
    place = (y * XN + x) * 2 + core
    norm_buf[place] = sq[0:8] + sq[8:16]

    def spread(sources, targets, first):
        copies = [
            remote(norm_buf.at[sources], norm_buf.at[sources], norm_send.at[first + s], norm_recv.at[first + s], device)
            for s, device in enumerate(targets)
        ]
        start_all(copies)
        for copy in copies:
            copy.wait()

    def add_up(slots):
        value = norm_buf[slots[0]]
        for slot in slots[1:]:
            value = value + norm_buf[slot]
        return value

    spread(place, plane_peers, 0)
    norm_buf[8 + z] = add_up(range(8))
    spread(8 + z, [chip(zi, y, x) for zi in z_peers], 7)
    everything = add_up(range(8, 8 + ZN))
    norm_out[...] = jnp.broadcast_to(jnp.sqrt(jnp.sum(everything, keepdims=True)), norm_out.shape)

    grad_copy.wait()
    for buf, out, s in ((pred, pred_out, 0), (sens, sens_out, 1)):
        for copy in out_copies(buf, out, s):
            copy.wait()
    own.wait_send()

    for mats, lanes in ((slice(1, MATS), slice(0, hidden)), (slice(0, 1), slice(0, 384))):
        sent = (
            wg.at[:, mats, 0 : ZN - 1, 0, 0, 0, :, lanes],
            wg.at[:, mats, :, :, 0, 0, :, lanes],
            wg.at[:, mats, :, 0, 0, 0, :, lanes],
            wg.at[:, mats, :, :, :, 0, :, lanes],
        )
        for sems in (ag_send, rs_send):
            for kind, ref in enumerate(sent):
                remote(ref, ref, sends(sems, kind, lanes), out_recv.at[0], sibling).wait_send()


def train_call(plane, segments, extents, adjoint, first, square, head, biases):
    ZN, YN, XN = plane
    past, span, hidden = segments.shape[1], adjoint.shape[0], square.shape[3]
    windows = segments.shape[0] // 2
    tile = windows
    half = hidden // (ZN * YN * XN) // 2
    sizes = (ZN, YN, XN, windows, tile, past, span, hidden)
    DMA = pltpu.SemaphoreType.DMA
    vmem = pl.BlockSpec(memory_space=pltpu.VMEM)
    hbm = pl.BlockSpec(memory_space=pl.ANY)
    count = 2 * MATS
    flops = 2 * 2 * 3 * windows * hidden * (6 * hidden + 2 * 128)
    lengths = extents.reshape(-1, 128)
    return pl.pallas_call(
        functools.partial(train_kernel, sizes),
        out_shape=(
            jax.ShapeDtypeStruct((span, 1, 2 * windows), F32),
            jax.ShapeDtypeStruct((past, 1, 2 * windows), F32),
            jax.ShapeDtypeStruct((MATS, 2, half, hidden), F32),
            jax.ShapeDtypeStruct((8, 128), F32),
        ),
        in_specs=[hbm] * 7,
        out_specs=(hbm, hbm, vmem, vmem),
        scratch_shapes=[
            pltpu.VMEM((2, MATS, ZN, YN, XN, 2, half, hidden), BF),
            pltpu.VMEM((MATS, half, hidden), BF),
            pltpu.VMEM((2, MATS, ZN, YN, XN, 2, half, hidden), BF),
            pltpu.VMEM((CORE_SLOTS, ZN, YN, XN, half, hidden), BF),
            pltpu.VMEM((DIAG_SLOTS, ZN, half, hidden), BF),
            pltpu.VMEM((PLAIN_SLOTS, ZN, half, hidden), BF),
            pltpu.VMEM((PAIR_SLOTS, ZN, half, hidden), BF),
            pltpu.VMEM((Z_SLOTS, ZN - 1, half, hidden), BF),
            pltpu.VMEM((2, MATS, half, hidden), F32),
            pltpu.VMEM((2, 4, hidden, windows), BF),
            pltpu.VMEM((2, 128, windows), BF),
            pltpu.VMEM((windows, hidden), BF),
            pltpu.VMEM((128, hidden), F32),
            pltpu.VMEM((2, 4, windows, hidden), BF),
            pltpu.VMEM((3, windows, hidden), BF),
            pltpu.VMEM((windows, 128), F32),
            pltpu.VMEM((windows, 128), BF),
            pltpu.VMEM((windows, 128), BF),
            pltpu.VMEM((128, windows), BF),
            pltpu.VMEM((128, windows), BF),
            pltpu.VMEM((128, hidden), F32),
            pltpu.VMEM((128, hidden), F32),
            pltpu.VMEM((128, 128), F32),
            pltpu.VMEM((windows, past), F32),
            pltpu.VMEM((span, windows), F32),
            *(pltpu.VMEM(a.shape, a.dtype) for a in (lengths, first, square, head, biases)),
            pltpu.VMEM((span, windows), F32),
            pltpu.VMEM((span, windows), F32),
            pltpu.VMEM((2, span, 1, windows), F32),
            pltpu.VMEM((2, past, 1, windows), F32),
            pltpu.VMEM((half, hidden), F32),
            pltpu.VMEM((8 + ZN, 8, 128), F32),
            DMA((1,)),
            DMA((1,)),
            DMA((4, 2)),
            DMA((count, 4 + ZN - 1)),
            DMA((4, 2)),
            DMA((count, 4 + ZN - 1)),
            DMA((3,)),
            DMA((3,)),
            DMA((9,)),
            DMA((7 + ZN - 1,)),
            DMA((7 + ZN - 1,)),
        ],
        compiler_params=pltpu.CompilerParams(
            collective_id=0, has_side_effects=True, vmem_limit_bytes=64 * 1024 * 1024
        ),
        cost_estimate=pl.CostEstimate(flops=flops, bytes_accessed=8_000_000, transcendentals=8 * windows * hidden),
        name="train",
    )(segments, adjoint, lengths, first, square, head, biases)


def update_kernel(past, span, *refs):
    sources, targets, norm_out = refs[0:16], refs[16:34], refs[34]
    held, results, pad, in_sem, out_sem = refs[35:51], refs[51:67], *refs[67:70]
    arriving = [pltpu.make_async_copy(source, ref, in_sem.at[n]) for n, (source, ref) in enumerate(zip(sources, held))]
    leaving = [
        pltpu.make_async_copy(ref, target, out_sem.at[n]) for n, (ref, target) in enumerate(zip(held[0:2] + results, targets))
    ]
    for copy in arriving:
        copy.start()
    grads, norm, masters, momenta, variances = held[2], held[3], held[4:8], held[8:12], held[12:16]
    units = masters[3].shape[2]

    def rows(m, lane, width):
        return grads[m, :, :, lane : lane + width].reshape(units, width)

    arriving[2].wait()
    arriving[3].wait()
    norm_out[...] = norm[0:1, 0:1]
    factor = 1.0 / jnp.maximum(norm[0:1, 0:1], 1.0)
    for m in range(5):
        results[1][0, m] = rows(m + 1, 0, grads.shape[3])
    results[0][0] = rows(0, 0, 128)[:, 0:past]
    forecast = rows(0, 128, 128)
    pad[...] = jnp.zeros_like(pad)
    pad[0:units, :] = forecast
    results[3][0] = pad[...].T[span : span + 4, 0:units]
    results[2][0, :, 0:past] = rows(0, 256, 128)[:, 0:past]
    results[2][0, :, past : past + span] = forecast[:, 0:span]
    for n in (0, 1):
        arriving[n].wait()
        leaving[n].start()
    for n in (1, 0, 2, 3):
        leaving[2 + n].start()
        for state in range(3):
            arriving[4 + 4 * state + n].wait()
        updated = adamw(masters[n][...], results[n][...], momenta[n][...], variances[n][...], factor[None])
        for kind, value in enumerate(updated):
            results[4 * (kind + 1) + n][...] = value
            leaving[2 + 4 * (kind + 1) + n].start()
    for copy in leaving:
        copy.wait()


def update_call(prediction, sensitivity, grads, norm, state):
    hbm = pl.BlockSpec(memory_space=pl.ANY)
    sources = (prediction, sensitivity, grads, norm, *state)
    targets = (prediction, sensitivity, *(4 * list(state[:4])))
    return pl.pallas_call(
        functools.partial(update_kernel, sensitivity.shape[0], prediction.shape[0]),
        out_shape=tuple(jax.ShapeDtypeStruct(a.shape, F32) for a in targets) + (jax.ShapeDtypeStruct((1, 1), F32),),
        in_specs=[hbm] * len(sources),
        out_specs=tuple([hbm] * len(targets) + [pl.BlockSpec(memory_space=pltpu.VMEM)]),
        scratch_shapes=[pltpu.VMEM(a.shape, F32) for a in sources]
        + [pltpu.VMEM(a.shape, F32) for a in targets[2:]]
        + [pltpu.VMEM((128, 128), F32), pltpu.SemaphoreType.DMA((len(sources),)), pltpu.SemaphoreType.DMA((len(targets),))],
        name="update",
    )(*sources)


def turned(arrays):
    return [a.transpose(0, 2, 1) if n % 4 == 0 else a for n, a in enumerate(arrays)]


def kernel_shards(plane, segments, extents, adjoint, *state):
    state = turned(state)
    results = train_call(plane, segments, extents, adjoint.T, *state[:4])
    prediction, sensitivity, *updated, norm = update_call(*results, state)
    by_window = (prediction.transpose(1, 2, 0), sensitivity.transpose(1, 2, 0))
    return (*by_window, norm.reshape(()), *turned(updated))


STATE_SPECS = (
    P("section", None, "dp"),
    P("section", None, "dp", None),
    P("section", "dp", None),
    P("section", None, "dp"),
)


def solution(mesh):
    in_specs = (P("dp", None), P("dp"), P("dp", None)) + 3 * STATE_SPECS
    out_specs = (P("section", "dp", None), P("section", "dp", None), P()) + 4 * STATE_SPECS
    plane = PLANES.get(mesh.shape["dp"])
    shards = plain_shards if plane is None else functools.partial(kernel_shards, plane)
    return jax.shard_map(shards, mesh=mesh, in_specs=in_specs, out_specs=out_specs, check_vma=False)
```

```python
import functools

import jax
import jax.numpy as jnp
from jax import lax
from jax.experimental import pallas as pl
from jax.experimental.pallas import tpu as pltpu
from jax.sharding import PartitionSpec as P

STEP = 10


def dot_nn(a, b):
    return jnp.dot(a, b, preferred_element_type=jnp.float32)


def dot_tn(a, b):
    return lax.dot_general(a, b, (((0,), (0,)), ((), ())), preferred_element_type=jnp.float32)


def dot_nt(a, b):
    return lax.dot_general(a, b, (((1,), (1,)), ((), ())), preferred_element_type=jnp.float32)


def unit_rows(first, square, head, biases):
    units = first.shape[1]
    return jnp.concatenate(
        [square.transpose(1, 0, 2).reshape(units, -1), first.T, head, biases.T], axis=1
    )


def from_unit_rows(rows, past, hidden, out):
    wide = 5 * hidden
    square = rows[:, :wide].reshape(-1, 5, hidden).transpose(1, 0, 2)
    first = rows[:, wide : wide + past].T
    head = rows[:, wide + past : wide + past + out]
    biases = rows[:, wide + past + out :].T
    return first, square, head, biases


def plain_forward(weights, resid):
    first, square, head, biases = weights
    past = resid.shape[1]
    acts, slopes = [resid.astype(jnp.bfloat16)], []
    for k in range(4):
        z = dot_nn(acts[-1], first if k == 0 else square[k - 1]) + biases[k].astype(jnp.float32)
        sig = jax.nn.sigmoid(z)
        acts.append((z * sig).astype(jnp.bfloat16))
        slopes.append(sig * (1.0 + z * (1.0 - sig)))
    theta_b = dot_nn(acts[4], square[3]).astype(jnp.bfloat16)
    theta_f = dot_nn(acts[4], square[4]).astype(jnp.bfloat16)
    backcast = dot_nn(theta_b, head[:, :past])
    part = dot_nn(theta_f, head[:, past:])
    return backcast, part, (acts, slopes, theta_b, theta_f)


def plain_backward(weights, saved, e, f):
    first, square, head, biases = weights
    acts, slopes, theta_b, theta_f = saved
    past = e.shape[1]
    head_grad = jnp.concatenate([dot_tn(theta_b, e), dot_tn(theta_f, f)], axis=1)
    u_b = dot_nt(e, head[:, :past]).astype(jnp.bfloat16)
    u_f = dot_nt(f, head[:, past:]).astype(jnp.bfloat16)
    squares = [None, None, None, dot_tn(acts[4], u_b), dot_tn(acts[4], u_f)]
    da = dot_nt(u_b, square[3]) + dot_nt(u_f, square[4])
    bias_grads = [None] * 4
    first_grad = None
    for k in (3, 2, 1, 0):
        dz = (da * slopes[k]).astype(jnp.bfloat16)
        bias_grads[k] = jnp.sum(dz, axis=0, dtype=jnp.float32)
        grad = dot_tn(acts[k], dz)
        if k == 0:
            first_grad = grad
        else:
            squares[k - 1] = grad
        da = dot_nt(dz, first if k == 0 else square[k - 1])
    return da, (first_grad, jnp.stack(squares), head_grad, jnp.stack(bias_grads))


def adamw(master, gradient, momentum, variance, factor):
    clipped = gradient * factor
    moment_new = 0.9 * momentum + 0.1 * clipped
    variance_new = 0.999 * variance + 0.001 * clipped * clipped
    ratio = moment_new / (1.0 - 0.9**STEP) / (jnp.sqrt(variance_new / (1.0 - 0.999**STEP)) + 1e-08)
    return master - 0.05 * (ratio + 0.01 * master), moment_new, variance_new


def plain_shards(segments, extents, adjoint, *state):
    masters, momenta, variances = state[:4], state[4:8], state[8:]
    core = lax.axis_index("section")
    past, span = segments.shape[1], adjoint.shape[1]
    windows = segments.shape[0] // 2
    hidden = masters[1].shape[3]
    mine = [
        lax.dynamic_slice_in_dim(v, core * windows, windows, 0) for v in (segments, extents, adjoint)
    ]
    seg, ext, adj = mine
    rows = unit_rows(*(m[0].astype(jnp.bfloat16) for m in masters))
    rows = lax.all_gather(rows, "dp", axis=0, tiled=True)
    rows = lax.all_gather(rows, "section", axis=0)
    blocks = [from_unit_rows(rows[b], past, hidden, past + span) for b in range(2)]
    mask = (
        lax.broadcasted_iota(jnp.int32, (windows, past), 1) >= past - ext[:, None]
    ).astype(jnp.float32)
    r0 = seg * mask
    backcast, part0, saved0 = plain_forward(blocks[0], r0)
    r1 = (r0 - backcast) * mask
    _, part1, saved1 = plain_forward(blocks[1], r1)
    forecast = part0.astype(jnp.bfloat16).astype(jnp.float32) + part1
    f = adj.astype(jnp.bfloat16)
    zero = jnp.zeros_like(r0)
    da1, grads1 = plain_backward(blocks[1], saved1, (-(zero * mask)).astype(jnp.bfloat16), f)
    dr1 = zero * mask + da1
    t = dr1.astype(jnp.bfloat16).astype(jnp.float32)
    da0, grads0 = plain_backward(blocks[0], saved0, (-(t * mask)).astype(jnp.bfloat16), f)
    dr0 = (t * mask + da0) * mask

    def by_section(first_block, second_block):
        mine, other = (
            jnp.where(core == 0, first_block, second_block),
            jnp.where(core == 0, second_block, first_block),
        )
        got = lax.ppermute(other, "section", [(0, 1), (1, 0)])
        return jnp.where(
            core == 0, jnp.concatenate([mine, got]), jnp.concatenate([got, mine])
        )[None]

    prediction = by_section(part0, forecast)
    sensitivity = by_section(dr0, dr1)
    packed = jnp.stack([unit_rows(*grads0), unit_rows(*grads1)])
    packed = lax.psum_scatter(packed, "section", scatter_dimension=0, tiled=False)
    packed = lax.psum_scatter(packed, "dp", scatter_dimension=0, tiled=True)
    norm = jnp.sqrt(lax.psum(jnp.sum(packed * packed), ("section", "dp")))
    factor = 1.0 / jnp.maximum(norm, 1.0)
    summed = [g[None] for g in from_unit_rows(packed, past, hidden, past + span)]
    updated = [adamw(*four, factor) for four in zip(masters, summed, momenta, variances)]
    return (
        prediction,
        sensitivity,
        norm,
        *summed,
        *(u[0] for u in updated),
        *(u[1] for u in updated),
        *(u[2] for u in updated),
    )


PLANES = {16: (4, 2, 2)}
MESH = pl.DeviceIdType.MESH
MATS = 6
CORE_SLOTS, DIAG_SLOTS, PLAIN_SLOTS, PAIR_SLOTS, Z_SLOTS = 4, 4, 4, 4, 4
EARLY = 3
BF, F32 = jnp.bfloat16, jnp.float32


def remote(src, dst, send_sem, recv_sem, device):
    return pltpu.make_async_remote_copy(
        src_ref=src, dst_ref=dst, send_sem=send_sem, recv_sem=recv_sem, device_id=device, device_id_type=MESH
    )


def train_kernel(
    sizes,
    seg_hbm, adj_hbm, ext_hbm, first_hbm, square_hbm, head_hbm, biases_hbm,
    pred_out, sens_out, grad_out, norm_out,
    wg, handed, gp, from_core, from_diag, from_plain, from_pair, from_z, total,
    act_t, in_t, theta_keep, head_acc, slope, work, resid, mask, f_ref, f_t, e_t, bias_t, bias_sum, pad,
    seg, adj, ext, first, square, head, biases, first_part, part_t, pred, sens, squares, norm_buf,
    own_send, own_recv, ag_send, ag_recv, rs_send, rs_recv, out_send, out_recv, local_sem, norm_send, norm_recv,
):
    ZN, YN, XN, windows, tile, past, span, hidden = sizes
    units = ZN * YN * XN
    core, dp = lax.axis_index("section"), lax.axis_index("dp")
    x, y, z = lax.rem(dp, XN), lax.rem(lax.div(dp, XN), YN), lax.div(dp, XN * YN)
    other, xo, yo = 1 - core, 1 - x, 1 - y
    near_y, near_x = y + core * (yo - y), xo + core * (x - xo)
    far_y, far_x = yo + core * (y - yo), x + core * (xo - x)

    def chip(zi, yi, xi):
        return (core, (zi * YN + yi) * XN + xi)

    sibling = (other, dp)
    z_peers = [lax.rem(z + step, ZN) for step in range(1, ZN)]

    row0 = core * windows
    loads = [
        pltpu.make_async_copy(seg_hbm.at[pl.ds(row0, windows), :], seg, local_sem.at[0]),
        pltpu.make_async_copy(adj_hbm.at[:, pl.ds(row0, windows)], adj, local_sem.at[1]),
    ]
    small_loads = [
        pltpu.make_async_copy(source, target, local_sem.at[4 + n])
        for n, (source, target) in enumerate(
            [(square_hbm, square), (first_hbm, first), (head_hbm, head), (biases_hbm, biases), (ext_hbm, ext)]
        )
    ]
    for load in small_loads + loads:
        load.start()

    barrier = pltpu.get_barrier_semaphore()
    plane_peers = [
        (ci, (z * YN + yi) * XN + xi) for ci in (core, other) for yi in (y, yo) for xi in (x, xo)
    ][1:]
    peers = plane_peers + [chip(zi, y, x) for zi in z_peers]
    for peer in peers:
        pl.semaphore_signal(barrier, inc=1, device_id=peer, device_id_type=MESH)

    rows = hidden // units
    half_rows = rows // 2

    def put_own(m, value, lanes):
        halves = value.astype(BF).reshape(2, half_rows, -1)
        for h in range(2):
            pl.when(core == h)(functools.partial(put_half, m, halves[h], halves[1 - h], lanes))

    def put_half(m, kept, given, lanes):
        wg[core, m, z, y, x, core, :, lanes] = kept
        handed[m, :, lanes] = given

    for load in small_loads:
        load.wait()
    pad[...] = jnp.zeros_like(pad)
    pad[0:rows, 0:past] = first[0] * 0.5
    put_own(0, pad[0:rows, :], slice(0, 128))
    pad[...] = jnp.zeros_like(pad)
    pad[span : span + 4, 0:rows] = biases[0] * 0.5
    bias_cols = pad[...].T[0:rows]
    pad[...] = jnp.zeros_like(pad)
    pad[0:rows, 0:span] = head[0, :, past : past + span]
    put_own(0, pad[0:rows, :] + bias_cols, slice(128, 256))
    pad[...] = jnp.zeros_like(pad)
    pad[0:rows, 0:past] = head[0, :, 0:past]
    put_own(0, pad[0:rows, :], slice(256, 384))
    pl.semaphore_wait(barrier, len(peers))

    def hand_over(m, lanes):
        return remote(
            handed.at[m, :, lanes], wg.at[core, m, z, y, x, other, :, lanes], own_send.at[m], own_recv.at[m], sibling
        )

    hand_over(0, slice(0, 384)).start()
    for m in range(1, MATS):
        put_own(m, square[0, m - 1] * 0.5 if m < 4 else square[0, m - 1], slice(0, hidden))
        hand_over(m, slice(0, hidden)).start()


    def of(i):
        return lax.div(i, MATS), lax.rem(i, MATS)

    def sends(sems, kind, lanes):
        return sems.at[kind, 0 if lanes.stop == hidden else 1]

    def z_copies(i, lanes):
        b, m = of(i)
        part = wg.at[b, m, z, y, x, core, :, lanes]
        return [
            remote(part, part, sends(ag_send, 0, lanes), ag_recv.at[i, s], chip(zi, y, x)) for s, zi in enumerate(z_peers)
        ]

    def column_copies(i, lanes):
        b, m = of(i)
        part = wg.at[b, m, :, y, x, core, :, lanes]
        return [
            remote(part, part, sends(ag_send, 1, lanes), ag_recv.at[i, 3], chip(z, near_y, near_x)),
            remote(part, part, sends(ag_send, 1, lanes), ag_recv.at[i, 4], chip(z, far_y, far_x)),
        ]

    def corner_copy(i, lanes):
        b, m = of(i)
        part = wg.at[b, m, :, near_y, near_x, core, :, lanes]
        return remote(part, part, sends(ag_send, 2, lanes), ag_recv.at[i, 5], chip(z, far_y, far_x))

    def core_copy(i, lanes):
        b, m = of(i)
        part = wg.at[b, m, :, :, :, core, :, lanes]
        return remote(part, part, sends(ag_send, 3, lanes), ag_recv.at[i, 6], sibling)

    def by_lanes(m, step):
        pl.when(m == 0)(lambda: step(slice(0, 384)))
        pl.when(m > 0)(lambda: step(slice(0, hidden)))

    def start_all(copies):
        for copy in copies:
            copy.start()

    for load in loads:
        load.wait()
    zeros_tile = jnp.zeros((tile, 128), F32)

    def prepare(t, carry):
        at = pl.ds(t * tile, tile)
        resid[at, :] = zeros_tile
        resid[at, 0:past] = seg[at, :]
        return carry

    def prepare_mask(g, carry):
        lengths = ext[pl.ds(core * (windows // 128) + g, 1), :]
        position = lax.broadcasted_iota(jnp.int32, (128, 128), 0)
        keep = jnp.where(position >= past - lengths, 1.0, 0.0).astype(F32).T
        at = pl.ds(pl.multiple_of(g * 128, 128), 128)
        pad[0:span, :] = adj[:, at]
        f_ref[at, :] = pad[...].T.astype(BF)
        f_t[:, at] = pad[...].astype(BF)
        mask[at, :] = keep.astype(BF)
        resid[at, :] = resid[at, :] * keep
        return carry

    tiles = windows // tile
    part_tile = windows // 2

    def matrix(b, m):
        return wg[b, m].reshape(hidden, hidden)

    def small(b, lane):
        return wg[b, 0, :, :, :, :, :, lane : lane + 128].reshape(hidden, 128)

    def store_layer(b, k, at, v):
        p = 1.0 + jnp.tanh(v)
        a = v * p
        rate = p + a * (2.0 - p)
        slope[b, k, at, :] = rate.astype(BF)
        low = a.astype(BF)
        act_t[b, k, :, at] = low.T
        return low

    def halves(body):
        for t in range(2):
            body(slice(t * windows // 2, (t + 1) * windows // 2))

    def layer_zero(b):
        bias_t[...] = small(b, 128).astype(F32).T

        def body(at):
            a = resid[at, :].astype(BF)
            in_t[b, :, at] = a.T
            work[0, at, :] = store_layer(b, 0, at, dot_nt(a, small(b, 0)) + bias_t[span : span + 1, :])

        halves(body)

    def layer_next(b, k):
        source, target = lax.rem(k + 1, 2), lax.rem(k, 2)
        v = dot_nn(work[source], matrix(b, k)) + bias_t[pl.ds(span + k, 1), :]
        work[target] = store_layer(b, k, slice(0, windows), v)

    def grid(value):
        return value.astype(BF).reshape(ZN, YN, XN, 2, half_rows, -1)

    def head_grad(acc, lane, b):
        gp[b, 0, :, :, :, :, :, lane : lane + 128] = grid(acc[...].T)

    def backcast_step(b):
        @pl.when(b == 0)
        def _():
            def body(at):
                theta = dot_nn(work[1, at, :], matrix(b, 4)).astype(BF)
                theta_keep[at, :] = theta
                resid[at, :] = (resid[at, :] - dot_nn(theta, small(b, 256))) * mask[at, :].astype(F32)

            halves(body)

        @pl.when(b == 1)
        def _():
            head_acc[...] = jnp.zeros_like(head_acc)

            def body(at):
                theta = dot_nn(work[1, at, :], matrix(b, 4)).astype(BF)
                head_acc[...] += dot_nn(e_t[:, at], theta)

            halves(body)
            head_grad(head_acc, 256, b)

    def put_rows(buf, b, at, value):
        for row in range(value.shape[0]):
            buf[b, row, :, at] = value[row : row + 1]

    def forecast_step(b):
        head_acc[...] = jnp.zeros_like(head_acc)

        def body(at):
            theta = dot_nn(work[1, at, :], matrix(b, 5)).astype(BF)
            head_acc[...] += dot_nn(f_t[:, at], theta)
            part_t[:, at] = dot_nn(theta, small(b, 128)).T[0:span]

        halves(body)
        head_grad(head_acc, 128, b)

        @pl.when(b == 0)
        def _():
            put_rows(pred, 0, slice(0, windows), part_t[...])
            first_part[...] = part_t[...]

        @pl.when(b == 1)
        def _():
            put_rows(pred, 1, slice(0, windows), first_part[...].astype(BF).astype(F32) + part_t[...])

    count = 2 * MATS

    def delayed(lag, t, step):
        pl.when(jnp.logical_and(t >= lag, t < count + lag))(lambda: step(t - lag))

    def staged(stage, t, step):
        @pl.when(t == EARLY - 2 + stage)
        def _():
            lax.fori_loop(0, EARLY, lambda u, carry: (step(u), carry)[1], 0)

        unit = t - stage
        pl.when(jnp.logical_and(unit >= EARLY, unit < count))(lambda: step(unit))

    def gather_line(i):
        b, m = of(i)

        def step(lanes):
            pl.when(b != core)(lambda: hand_over(m, lanes).wait_recv())
            start_all(z_copies(i, lanes))

        by_lanes(m, step)

    def gather_columns(i):
        def step(lanes):
            for copy in z_copies(i, lanes):
                copy.wait_recv()
            start_all(column_copies(i, lanes))

        by_lanes(of(i)[1], step)

    def gather_corner(i):
        def step(lanes):
            column_copies(i, lanes)[0].wait_recv()
            corner_copy(i, lanes).start()

        by_lanes(of(i)[1], step)

    def gather_core(i):
        def step(lanes):
            column_copies(i, lanes)[1].wait_recv()
            corner_copy(i, lanes).wait_recv()
            core_copy(i, lanes).start()

        by_lanes(of(i)[1], step)

    def forward_unit(i):
        b, m = of(i)
        by_lanes(m, lambda lanes: core_copy(i, lanes).wait_recv())
        pl.when(m == 0)(lambda: layer_zero(b))
        pl.when(jnp.logical_and(m >= 1, m <= 3))(lambda: layer_next(b, m))
        pl.when(m == 4)(lambda: backcast_step(b))
        pl.when(m == 5)(lambda: forecast_step(b))

        @pl.when(m == jnp.where(b == 1, 3, 5))
        def _():
            pl.when(b == 1)(lambda: feed(b))
            pl.when(b == 0)(lambda: feed_forward(b))
            lax.fori_loop(jnp.where(b == 1, 4, 5), MATS, lambda n, carry: (theta_grad(b, n), carry)[1], 0)

            @pl.when(b == 1)
            def _():
                scatter_start(0)
                scatter_start(1)

            pl.when(b == 0)(lambda: scatter_start(2))

    def gather_step(t, carry):
        delayed(4, t, gather_core)
        delayed(2, t, gather_corner)
        delayed(0, t, gather_columns)
        pl.when(t + 4 < count)(lambda: gather_line(t + 4))
        delayed(5, t, forward_unit)
        return carry

    def out_copies(buf, out, s):
        at = pl.ds(row0, windows)
        return [
            pltpu.make_async_copy(buf.at[core], out.at[:, :, at], local_sem.at[2 + s]),
            remote(buf.at[other], out.at[:, :, at], out_send.at[s], out_recv.at[s], sibling),
        ]


    def back_of(j):
        b = jnp.where(jnp.logical_or(j <= 1, jnp.logical_and(j >= 3, j <= 6)), 1, 0)
        m = jnp.where(j <= 1, 4 + j, jnp.where(j == 2, 5, jnp.where(j <= 6, 6 - j, jnp.where(j == 7, 4, 11 - j))))
        return b, m

    def to_core(j, lanes):
        b, m = back_of(j)
        return remote(
            gp.at[b, m, :, :, :, other, :, lanes], from_core.at[lax.rem(j, CORE_SLOTS), :, :, :, :, lanes],
            sends(rs_send, 3, lanes), rs_recv.at[j, 0], sibling,
        )

    def to_far(j, lanes):
        b, m = back_of(j)
        device = chip(z, far_y, far_x)
        return [
            remote(
                gp.at[b, m, :, yo, xo, core, :, lanes], from_diag.at[lax.rem(j, DIAG_SLOTS), :, :, lanes],
                sends(rs_send, 1, lanes), rs_recv.at[j, 1], device,
            ),
            remote(
                gp.at[b, m, :, far_y, far_x, core, :, lanes], from_plain.at[lax.rem(j, PLAIN_SLOTS), :, :, lanes],
                sends(rs_send, 1, lanes), rs_recv.at[j, 2], device,
            ),
        ]

    def to_near(j, lanes):
        b, m = back_of(j)
        return remote(
            gp.at[b, m, :, near_y, near_x, core, :, lanes], from_pair.at[lax.rem(j, PAIR_SLOTS), :, :, lanes],
            sends(rs_send, 2, lanes), rs_recv.at[j, 3], chip(z, near_y, near_x),
        )

    def to_z(j, lanes):
        b, m = back_of(j)
        return [
            remote(
                gp.at[b, m, zi, y, x, core, :, lanes], from_z.at[lax.rem(j, Z_SLOTS), s, :, lanes],
                sends(rs_send, 0, lanes), rs_recv.at[j, 4 + s], chip(zi, y, x),
            )
            for s, zi in enumerate(z_peers)
        ]

    def scatter_start(j):
        by_lanes(back_of(j)[1], lambda lanes: to_core(j, lanes).start())

    def scatter_core(j):
        b, m = back_of(j)

        def step(lanes):
            to_core(j, lanes).wait_recv()
            part = gp[b, m, :, :, :, core, :, lanes] + from_core[lax.rem(j, CORE_SLOTS), :, :, :, :, lanes]
            gp[b, m, :, :, :, core, :, lanes] = part
            start_all(to_far(j, lanes))

        by_lanes(m, step)

    def scatter_diag(j):
        b, m = back_of(j)

        def step(lanes):
            to_far(j, lanes)[0].wait_recv()
            part = gp[b, m, :, near_y, near_x, core, :, lanes] + from_diag[lax.rem(j, DIAG_SLOTS), :, :, lanes]
            gp[b, m, :, near_y, near_x, core, :, lanes] = part
            to_near(j, lanes).start()

        by_lanes(m, step)

    def scatter_plane(j):
        b, m = back_of(j)

        def step(lanes):
            to_far(j, lanes)[1].wait_recv()
            to_near(j, lanes).wait_recv()
            value = gp[b, m, :, y, x, core, :, lanes].astype(F32)
            value = value + from_plain[lax.rem(j, PLAIN_SLOTS), :, :, lanes].astype(F32)
            value = value + from_pair[lax.rem(j, PAIR_SLOTS), :, :, lanes].astype(F32)
            gp[b, m, :, y, x, core, :, lanes] = value.astype(BF)
            start_all(to_z(j, lanes))

        by_lanes(m, step)

    def scatter_z(j):
        b, m = back_of(j)

        def step(lanes):
            for copy in to_z(j, lanes):
                copy.wait_recv()
            value = gp[b, m, z, y, x, core, :, lanes].astype(F32)
            for s in range(ZN - 1):
                value = value + from_z[lax.rem(j, Z_SLOTS), s, :, lanes].astype(F32)
            total[b, m, :, lanes] = value
            squares[:, lanes] = squares[:, lanes] + value * value

        by_lanes(m, step)

    def add_rows(value):
        return jnp.sum(value.reshape(-1, 8, hidden), axis=0)

    def put_bias(k, acc):
        bias_sum[pl.ds(span + k, 1), :] = jnp.sum(acc, axis=0, keepdims=True)

    def feed(b):
        pl.when(b == 1)(lambda: resid.__setitem__(..., jnp.zeros_like(resid)))
        e = (-(resid[...] * mask[...].astype(F32))).astype(BF)
        e_t[...] = e.T
        work[0] = dot_nt(e, small(b, 256)).astype(BF)
        work[2] = dot_nt(f_ref[...], small(b, 128)).astype(BF)

    def feed_forward(b):
        work[2] = dot_nt(f_ref[...], small(b, 128)).astype(BF)

    def put_dz(b, k, da):
        dz = da * slope[b, k].astype(F32)
        work[k % 2 if isinstance(k, int) else lax.rem(k, 2)] = dz.astype(BF)
        bias_sum[pl.ds(span + k, 1), :] = jnp.sum(add_rows(dz), axis=0, keepdims=True)

    def theta_step(b):
        put_dz(b, 3, 0.5 * (dot_nt(work[0], matrix(b, 4)) + dot_nt(work[2], matrix(b, 5))))

    def layer_back(b, k):
        source = lax.rem(k, 2)
        gp[b, k] = grid(dot_nn(act_t[b, k - 1], work[source]))
        put_dz(b, k - 1, dot_nt(work[source], matrix(b, k)))

    def theta_grad(b, m):
        gp[b, m] = grid(dot_nn(act_t[b, 3], work[jnp.where(m == 4, 0, 2)]))

    def small_grads(b):
        gp[b, 0, :, :, :, :, :, 0:128] = grid(dot_nn(in_t[b], work[0]).T)
        gp[b, 0, :, :, :, :, :, 128:256] = gp[b, 0, :, :, :, :, :, 128:256] + grid(bias_sum[...].T)

        @pl.when(b == 0)
        def _():
            head_acc[...] = dot_nn(e_t[...], theta_keep[...])
            head_grad(head_acc, 256, b)


    def input_grad(b):
        for t in range(2):
            at = slice(t * windows // 2, (t + 1) * windows // 2)
            keep = mask[at, :].astype(F32)
            dr = resid[at, :] * keep + 2.0 * dot_nn(work[0, at, :], small(b, 0))

            @pl.when(b == 1)
            def _():
                seg[at, :] = dr[:, 0:past]
                resid[at, :] = dr.astype(BF).astype(F32)

            @pl.when(b == 0)
            def _():
                put_rows(sens, 0, at, (dr * keep).T[0:past])

    def late_rows():
        for g in range(windows // 128):
            at = slice(g * 128, (g + 1) * 128)
            pad[:, 0:past] = seg[at, :]
            put_rows(sens, 1, at, pad[...].T[0:past])

    bias_sum[...] = jnp.zeros_like(bias_sum)
    squares[...] = jnp.zeros_like(squares)
    total[...] = jnp.zeros_like(total)

    def back_step(j, carry):
        b, m = back_of(j)
        live = jnp.logical_and(j >= 3, j < count)

        def on(test, step):
            pl.when(jnp.logical_and(live, test))(step)

        pl.when(j == 2)(lambda: theta_step(1))
        on(jnp.logical_and(m >= 1, m <= 3), lambda: layer_back(b, m))
        on(m == 0, lambda: small_grads(b))

        @pl.when(j == 7)
        def _():
            feed(b)
            theta_grad(b, 4)
            theta_step(b)

        staged(4, j, scatter_z)
        staged(3, j, scatter_plane)
        staged(2, j, scatter_diag)
        staged(1, j, scatter_core)
        pl.when(live)(lambda: scatter_start(j))
        on(m == 0, lambda: input_grad(b))

        @pl.when(j == count)
        def _():
            late_rows()
            start_all(out_copies(sens, sens_out, 1))

        return carry

    for i in range(4):
        gather_line(i)
    lax.fori_loop(0, tiles, prepare, 0)
    pad[...] = jnp.zeros_like(pad)
    lax.fori_loop(0, windows // 128, prepare_mask, 0)
    lax.fori_loop(0, count + 5, gather_step, 0)

    start_all(out_copies(pred, pred_out, 0))
    lax.fori_loop(EARLY - 1, count + 4, back_step, 0)

    grad_copy = remote(total.at[other], grad_out.at[:, core], out_send.at[2], out_recv.at[2], sibling)
    grad_copy.start()
    grad_out[:, core] = total[core]
    sq = squares[:, 0:128] + squares[:, 128:256] + squares[:, 256:384] + squares[:, 384:512]
    place = (y * XN + x) * 2 + core
    norm_buf[place] = sq[0:8] + sq[8:16]

    def spread(sources, targets, first):
        copies = [
            remote(norm_buf.at[sources], norm_buf.at[sources], norm_send.at[first + s], norm_recv.at[first + s], device)
            for s, device in enumerate(targets)
        ]
        start_all(copies)
        for copy in copies:
            copy.wait()

    def add_up(slots):
        value = norm_buf[slots[0]]
        for slot in slots[1:]:
            value = value + norm_buf[slot]
        return value

    spread(place, plane_peers, 0)
    norm_buf[8 + z] = add_up(range(8))
    spread(8 + z, [chip(zi, y, x) for zi in z_peers], 7)
    everything = add_up(range(8, 8 + ZN))
    norm_out[...] = jnp.broadcast_to(jnp.sqrt(jnp.sum(everything, keepdims=True)), norm_out.shape)

    grad_copy.wait()
    for buf, out, s in ((pred, pred_out, 0), (sens, sens_out, 1)):
        for copy in out_copies(buf, out, s):
            copy.wait()
    for m in range(MATS):
        hand_over(m, slice(0, hidden if m else 384)).wait_send()

    for mats, lanes in ((slice(1, MATS), slice(0, hidden)), (slice(0, 1), slice(0, 384))):
        sent = (
            wg.at[:, mats, 0 : ZN - 1, 0, 0, 0, :, lanes],
            wg.at[:, mats, :, :, 0, 0, :, lanes],
            wg.at[:, mats, :, 0, 0, 0, :, lanes],
            wg.at[:, mats, :, :, :, 0, :, lanes],
        )
        for sems in (ag_send, rs_send):
            for kind, ref in enumerate(sent):
                remote(ref, ref, sends(sems, kind, lanes), out_recv.at[0], sibling).wait_send()


def train_call(plane, segments, extents, adjoint, first, square, head, biases):
    ZN, YN, XN = plane
    past, span, hidden = segments.shape[1], adjoint.shape[0], square.shape[3]
    windows = segments.shape[0] // 2
    tile = windows
    half = hidden // (ZN * YN * XN) // 2
    sizes = (ZN, YN, XN, windows, tile, past, span, hidden)
    DMA = pltpu.SemaphoreType.DMA
    vmem = pl.BlockSpec(memory_space=pltpu.VMEM)
    hbm = pl.BlockSpec(memory_space=pl.ANY)
    count = 2 * MATS
    flops = 2 * 2 * 3 * windows * hidden * (6 * hidden + 2 * 128)
    lengths = extents.reshape(-1, 128)
    return pl.pallas_call(
        functools.partial(train_kernel, sizes),
        out_shape=(
            jax.ShapeDtypeStruct((span, 1, 2 * windows), F32),
            jax.ShapeDtypeStruct((past, 1, 2 * windows), F32),
            jax.ShapeDtypeStruct((MATS, 2, half, hidden), F32),
            jax.ShapeDtypeStruct((8, 128), F32),
        ),
        in_specs=[hbm] * 7,
        out_specs=(hbm, hbm, vmem, vmem),
        scratch_shapes=[
            pltpu.VMEM((2, MATS, ZN, YN, XN, 2, half, hidden), BF),
            pltpu.VMEM((MATS, half, hidden), BF),
            pltpu.VMEM((2, MATS, ZN, YN, XN, 2, half, hidden), BF),
            pltpu.VMEM((CORE_SLOTS, ZN, YN, XN, half, hidden), BF),
            pltpu.VMEM((DIAG_SLOTS, ZN, half, hidden), BF),
            pltpu.VMEM((PLAIN_SLOTS, ZN, half, hidden), BF),
            pltpu.VMEM((PAIR_SLOTS, ZN, half, hidden), BF),
            pltpu.VMEM((Z_SLOTS, ZN - 1, half, hidden), BF),
            pltpu.VMEM((2, MATS, half, hidden), F32),
            pltpu.VMEM((2, 4, hidden, windows), BF),
            pltpu.VMEM((2, 128, windows), BF),
            pltpu.VMEM((windows, hidden), BF),
            pltpu.VMEM((128, hidden), F32),
            pltpu.VMEM((2, 4, windows, hidden), BF),
            pltpu.VMEM((3, windows, hidden), BF),
            pltpu.VMEM((windows, 128), F32),
            pltpu.VMEM((windows, 128), BF),
            pltpu.VMEM((windows, 128), BF),
            pltpu.VMEM((128, windows), BF),
            pltpu.VMEM((128, windows), BF),
            pltpu.VMEM((128, hidden), F32),
            pltpu.VMEM((128, hidden), F32),
            pltpu.VMEM((128, 128), F32),
            pltpu.VMEM((windows, past), F32),
            pltpu.VMEM((span, windows), F32),
            *(pltpu.VMEM(a.shape, a.dtype) for a in (lengths, first, square, head, biases)),
            pltpu.VMEM((span, windows), F32),
            pltpu.VMEM((span, windows), F32),
            pltpu.VMEM((2, span, 1, windows), F32),
            pltpu.VMEM((2, past, 1, windows), F32),
            pltpu.VMEM((half, hidden), F32),
            pltpu.VMEM((8 + ZN, 8, 128), F32),
            DMA((MATS,)),
            DMA((MATS,)),
            DMA((4, 2)),
            DMA((count, 4 + ZN - 1)),
            DMA((4, 2)),
            DMA((count, 4 + ZN - 1)),
            DMA((3,)),
            DMA((3,)),
            DMA((9,)),
            DMA((7 + ZN - 1,)),
            DMA((7 + ZN - 1,)),
        ],
        compiler_params=pltpu.CompilerParams(
            collective_id=0, has_side_effects=True, vmem_limit_bytes=64 * 1024 * 1024
        ),
        cost_estimate=pl.CostEstimate(flops=flops, bytes_accessed=8_000_000, transcendentals=8 * windows * hidden),
        name="train",
    )(segments, adjoint, lengths, first, square, head, biases)


def update_kernel(past, span, *refs):
    sources, targets, norm_out = refs[0:16], refs[16:34], refs[34]
    held, results, pad, in_sem, out_sem = refs[35:51], refs[51:67], *refs[67:70]
    arriving = [pltpu.make_async_copy(source, ref, in_sem.at[n]) for n, (source, ref) in enumerate(zip(sources, held))]
    leaving = [
        pltpu.make_async_copy(ref, target, out_sem.at[n]) for n, (ref, target) in enumerate(zip(held[0:2] + results, targets))
    ]
    for copy in arriving:
        copy.start()
    grads, norm, masters, momenta, variances = held[2], held[3], held[4:8], held[8:12], held[12:16]
    units = masters[3].shape[2]

    def rows(m, lane, width):
        return grads[m, :, :, lane : lane + width].reshape(units, width)

    arriving[2].wait()
    arriving[3].wait()
    norm_out[...] = norm[0:1, 0:1]
    factor = 1.0 / jnp.maximum(norm[0:1, 0:1], 1.0)
    for m in range(5):
        results[1][0, m] = rows(m + 1, 0, grads.shape[3])
    results[0][0] = rows(0, 0, 128)[:, 0:past]
    forecast = rows(0, 128, 128)
    pad[...] = jnp.zeros_like(pad)
    pad[0:units, :] = forecast
    results[3][0] = pad[...].T[span : span + 4, 0:units]
    results[2][0, :, 0:past] = rows(0, 256, 128)[:, 0:past]
    results[2][0, :, past : past + span] = forecast[:, 0:span]
    for n in (0, 1):
        arriving[n].wait()
        leaving[n].start()
    for n in (1, 0, 2, 3):
        leaving[2 + n].start()
        for state in range(3):
            arriving[4 + 4 * state + n].wait()
        updated = adamw(masters[n][...], results[n][...], momenta[n][...], variances[n][...], factor[None])
        for kind, value in enumerate(updated):
            results[4 * (kind + 1) + n][...] = value
            leaving[2 + 4 * (kind + 1) + n].start()
    for copy in leaving:
        copy.wait()


def update_call(prediction, sensitivity, grads, norm, state):
    hbm = pl.BlockSpec(memory_space=pl.ANY)
    sources = (prediction, sensitivity, grads, norm, *state)
    targets = (prediction, sensitivity, *(4 * list(state[:4])))
    return pl.pallas_call(
        functools.partial(update_kernel, sensitivity.shape[0], prediction.shape[0]),
        out_shape=tuple(jax.ShapeDtypeStruct(a.shape, F32) for a in targets) + (jax.ShapeDtypeStruct((1, 1), F32),),
        in_specs=[hbm] * len(sources),
        out_specs=tuple([hbm] * len(targets) + [pl.BlockSpec(memory_space=pltpu.VMEM)]),
        scratch_shapes=[pltpu.VMEM(a.shape, F32) for a in sources]
        + [pltpu.VMEM(a.shape, F32) for a in targets[2:]]
        + [pltpu.VMEM((128, 128), F32), pltpu.SemaphoreType.DMA((len(sources),)), pltpu.SemaphoreType.DMA((len(targets),))],
        name="update",
    )(*sources)


def turned(arrays):
    return [a.transpose(0, 2, 1) if n % 4 == 0 else a for n, a in enumerate(arrays)]


def kernel_shards(plane, segments, extents, adjoint, *state):
    state = turned(state)
    results = train_call(plane, segments, extents, adjoint.T, *state[:4])
    prediction, sensitivity, *updated, norm = update_call(*results, state)
    by_window = (prediction.transpose(1, 2, 0), sensitivity.transpose(1, 2, 0))
    return (*by_window, norm.reshape(()), *turned(updated))


STATE_SPECS = (
    P("section", None, "dp"),
    P("section", None, "dp", None),
    P("section", "dp", None),
    P("section", None, "dp"),
)


def solution(mesh):
    in_specs = (P("dp", None), P("dp"), P("dp", None)) + 3 * STATE_SPECS
    out_specs = (P("section", "dp", None), P("section", "dp", None), P()) + 4 * STATE_SPECS
    plane = PLANES.get(mesh.shape["dp"])
    shards = plain_shards if plane is None else functools.partial(kernel_shards, plane)
    return jax.shard_map(shards, mesh=mesh, in_specs=in_specs, out_specs=out_specs, check_vma=False)
```

```python
import functools

import jax
import jax.numpy as jnp
from jax import lax
from jax.experimental import pallas as pl
from jax.experimental.pallas import tpu as pltpu
from jax.sharding import PartitionSpec as P

STEP = 10


def dot_nn(a, b):
    return jnp.dot(a, b, preferred_element_type=jnp.float32)


def dot_tn(a, b):
    return lax.dot_general(a, b, (((0,), (0,)), ((), ())), preferred_element_type=jnp.float32)


def dot_nt(a, b):
    return lax.dot_general(a, b, (((1,), (1,)), ((), ())), preferred_element_type=jnp.float32)


def unit_rows(first, square, head, biases):
    units = first.shape[1]
    return jnp.concatenate(
        [square.transpose(1, 0, 2).reshape(units, -1), first.T, head, biases.T], axis=1
    )


def from_unit_rows(rows, past, hidden, out):
    wide = 5 * hidden
    square = rows[:, :wide].reshape(-1, 5, hidden).transpose(1, 0, 2)
    first = rows[:, wide : wide + past].T
    head = rows[:, wide + past : wide + past + out]
    biases = rows[:, wide + past + out :].T
    return first, square, head, biases


def plain_forward(weights, resid):
    first, square, head, biases = weights
    past = resid.shape[1]
    acts, slopes = [resid.astype(jnp.bfloat16)], []
    for k in range(4):
        z = dot_nn(acts[-1], first if k == 0 else square[k - 1]) + biases[k].astype(jnp.float32)
        sig = jax.nn.sigmoid(z)
        acts.append((z * sig).astype(jnp.bfloat16))
        slopes.append(sig * (1.0 + z * (1.0 - sig)))
    theta_b = dot_nn(acts[4], square[3]).astype(jnp.bfloat16)
    theta_f = dot_nn(acts[4], square[4]).astype(jnp.bfloat16)
    backcast = dot_nn(theta_b, head[:, :past])
    part = dot_nn(theta_f, head[:, past:])
    return backcast, part, (acts, slopes, theta_b, theta_f)


def plain_backward(weights, saved, e, f):
    first, square, head, biases = weights
    acts, slopes, theta_b, theta_f = saved
    past = e.shape[1]
    head_grad = jnp.concatenate([dot_tn(theta_b, e), dot_tn(theta_f, f)], axis=1)
    u_b = dot_nt(e, head[:, :past]).astype(jnp.bfloat16)
    u_f = dot_nt(f, head[:, past:]).astype(jnp.bfloat16)
    squares = [None, None, None, dot_tn(acts[4], u_b), dot_tn(acts[4], u_f)]
    da = dot_nt(u_b, square[3]) + dot_nt(u_f, square[4])
    bias_grads = [None] * 4
    first_grad = None
    for k in (3, 2, 1, 0):
        dz = (da * slopes[k]).astype(jnp.bfloat16)
        bias_grads[k] = jnp.sum(dz, axis=0, dtype=jnp.float32)
        grad = dot_tn(acts[k], dz)
        if k == 0:
            first_grad = grad
        else:
            squares[k - 1] = grad
        da = dot_nt(dz, first if k == 0 else square[k - 1])
    return da, (first_grad, jnp.stack(squares), head_grad, jnp.stack(bias_grads))


def adamw(master, gradient, momentum, variance, factor):
    clipped = gradient * factor
    moment_new = 0.9 * momentum + 0.1 * clipped
    variance_new = 0.999 * variance + 0.001 * clipped * clipped
    ratio = moment_new / (1.0 - 0.9**STEP) / (jnp.sqrt(variance_new / (1.0 - 0.999**STEP)) + 1e-08)
    return master - 0.05 * (ratio + 0.01 * master), moment_new, variance_new


def plain_shards(segments, extents, adjoint, *state):
    masters, momenta, variances = state[:4], state[4:8], state[8:]
    core = lax.axis_index("section")
    past, span = segments.shape[1], adjoint.shape[1]
    windows = segments.shape[0] // 2
    hidden = masters[1].shape[3]
    mine = [
        lax.dynamic_slice_in_dim(v, core * windows, windows, 0) for v in (segments, extents, adjoint)
    ]
    seg, ext, adj = mine
    rows = unit_rows(*(m[0].astype(jnp.bfloat16) for m in masters))
    rows = lax.all_gather(rows, "dp", axis=0, tiled=True)
    rows = lax.all_gather(rows, "section", axis=0)
    blocks = [from_unit_rows(rows[b], past, hidden, past + span) for b in range(2)]
    mask = (
        lax.broadcasted_iota(jnp.int32, (windows, past), 1) >= past - ext[:, None]
    ).astype(jnp.float32)
    r0 = seg * mask
    backcast, part0, saved0 = plain_forward(blocks[0], r0)
    r1 = (r0 - backcast) * mask
    _, part1, saved1 = plain_forward(blocks[1], r1)
    forecast = part0.astype(jnp.bfloat16).astype(jnp.float32) + part1
    f = adj.astype(jnp.bfloat16)
    zero = jnp.zeros_like(r0)
    da1, grads1 = plain_backward(blocks[1], saved1, (-(zero * mask)).astype(jnp.bfloat16), f)
    dr1 = zero * mask + da1
    t = dr1.astype(jnp.bfloat16).astype(jnp.float32)
    da0, grads0 = plain_backward(blocks[0], saved0, (-(t * mask)).astype(jnp.bfloat16), f)
    dr0 = (t * mask + da0) * mask

    def by_section(first_block, second_block):
        mine, other = (
            jnp.where(core == 0, first_block, second_block),
            jnp.where(core == 0, second_block, first_block),
        )
        got = lax.ppermute(other, "section", [(0, 1), (1, 0)])
        return jnp.where(
            core == 0, jnp.concatenate([mine, got]), jnp.concatenate([got, mine])
        )[None]

    prediction = by_section(part0, forecast)
    sensitivity = by_section(dr0, dr1)
    packed = jnp.stack([unit_rows(*grads0), unit_rows(*grads1)])
    packed = lax.psum_scatter(packed, "section", scatter_dimension=0, tiled=False)
    packed = lax.psum_scatter(packed, "dp", scatter_dimension=0, tiled=True)
    norm = jnp.sqrt(lax.psum(jnp.sum(packed * packed), ("section", "dp")))
    factor = 1.0 / jnp.maximum(norm, 1.0)
    summed = [g[None] for g in from_unit_rows(packed, past, hidden, past + span)]
    updated = [adamw(*four, factor) for four in zip(masters, summed, momenta, variances)]
    return (
        prediction,
        sensitivity,
        norm,
        *summed,
        *(u[0] for u in updated),
        *(u[1] for u in updated),
        *(u[2] for u in updated),
    )


PLANES = {16: (4, 2, 2)}
MESH = pl.DeviceIdType.MESH
MATS = 6
CORE_SLOTS, DIAG_SLOTS, PLAIN_SLOTS, PAIR_SLOTS = 4, 4, 6, 4
BF, F32 = jnp.bfloat16, jnp.float32


def remote(src, dst, send_sem, recv_sem, device):
    return pltpu.make_async_remote_copy(
        src_ref=src, dst_ref=dst, send_sem=send_sem, recv_sem=recv_sem, device_id=device, device_id_type=MESH
    )


def train_kernel(
    sizes,
    seg_hbm, adj_hbm, ext_hbm, first_hbm, square_hbm, head_hbm, biases_hbm,
    pred_out, sens_out, grad_out, norm_out,
    wg, handed, gp, from_core, from_diag, from_plain, from_pair, from_z, total,
    act_t, in_t, theta_keep, slope, work, resid, mask, f_ref, e_t, bias_t, bias_sum, pad,
    seg, adj, ext, first, square, head, biases, part_t, pred, sens, squares, norm_buf,
    own_send, own_recv, ag_send, ag_recv, rs_send, rs_recv, out_send, out_recv, local_sem, norm_send, norm_recv,
):
    ZN, YN, XN, windows, tile, past, span, hidden = sizes
    units = ZN * YN * XN
    core, dp = lax.axis_index("section"), lax.axis_index("dp")
    x, y, z = lax.rem(dp, XN), lax.rem(lax.div(dp, XN), YN), lax.div(dp, XN * YN)
    other, xo, yo = 1 - core, 1 - x, 1 - y
    near_y, near_x = y + core * (yo - y), xo + core * (x - xo)
    far_y, far_x = yo + core * (y - yo), x + core * (xo - x)

    def chip(zi, yi, xi):
        return (core, (zi * YN + yi) * XN + xi)

    sibling = (other, dp)
    z_peers = [lax.rem(z + step, ZN) for step in range(1, ZN)]

    row0 = core * windows
    loads = [
        pltpu.make_async_copy(seg_hbm.at[pl.ds(row0, windows), :], seg, local_sem.at[0]),
        pltpu.make_async_copy(adj_hbm.at[:, pl.ds(row0, windows)], adj, local_sem.at[1]),
    ]
    small_loads = [
        pltpu.make_async_copy(source, target, local_sem.at[4 + n])
        for n, (source, target) in enumerate(
            [(square_hbm, square), (first_hbm, first), (head_hbm, head), (biases_hbm, biases), (ext_hbm, ext)]
        )
    ]
    for load in small_loads + loads:
        load.start()

    barrier = pltpu.get_barrier_semaphore()
    plane_peers = [
        (ci, (z * YN + yi) * XN + xi) for ci in (core, other) for yi in (y, yo) for xi in (x, xo)
    ][1:]
    peers = plane_peers + [chip(zi, y, x) for zi in z_peers]
    for peer in peers:
        pl.semaphore_signal(barrier, inc=1, device_id=peer, device_id_type=MESH)

    rows = hidden // units
    half_rows = rows // 2

    def put_own(m, value, lanes):
        halves = value.astype(BF).reshape(2, half_rows, -1)
        for h in range(2):
            pl.when(core == h)(functools.partial(put_half, m, halves[h], halves[1 - h], lanes))

    def put_half(m, kept, given, lanes):
        wg[core, m, z, y, x, core, :, lanes] = kept
        handed[m, :, lanes] = given

    for load in small_loads:
        load.wait()
    pad[...] = jnp.zeros_like(pad)
    pad[0:rows, 0:past] = first[0] * 0.5
    put_own(0, pad[0:rows, :], slice(0, 128))
    pad[...] = jnp.zeros_like(pad)
    pad[span : span + 4, 0:rows] = biases[0] * 0.5
    bias_cols = pad[...].T[0:rows]
    pad[...] = jnp.zeros_like(pad)
    pad[0:rows, 0:span] = head[0, :, past : past + span]
    put_own(0, pad[0:rows, :] + bias_cols, slice(128, 256))
    pad[...] = jnp.zeros_like(pad)
    pad[0:rows, 0:past] = head[0, :, 0:past]
    put_own(0, pad[0:rows, :], slice(256, 384))
    pl.semaphore_wait(barrier, len(peers))

    def hand_over(m, lanes):
        return remote(
            handed.at[m, :, lanes], wg.at[core, m, z, y, x, other, :, lanes], own_send.at[m], own_recv.at[m], sibling
        )

    hand_over(0, slice(0, 384)).start()
    for m in range(1, MATS):
        put_own(m, square[0, m - 1] * 0.5 if m < 4 else square[0, m - 1], slice(0, hidden))
        hand_over(m, slice(0, hidden)).start()


    def of(i):
        b = jnp.where(jnp.logical_and(i >= 5, i <= 10), 1, 0)
        return b, jnp.where(i <= 4, i, jnp.where(i <= 10, i - 5, 5))

    def sends(sems, kind, lanes):
        return sems.at[kind, 0 if lanes.stop == hidden else 1]

    def z_copies(i, lanes):
        b, m = of(i)
        part = wg.at[b, m, z, y, x, core, :, lanes]
        return [
            remote(part, part, sends(ag_send, 0, lanes), ag_recv.at[i, s], chip(zi, y, x)) for s, zi in enumerate(z_peers)
        ]

    def column_copies(i, lanes):
        b, m = of(i)
        part = wg.at[b, m, :, y, x, core, :, lanes]
        return [
            remote(part, part, sends(ag_send, 1, lanes), ag_recv.at[i, 3], chip(z, near_y, near_x)),
            remote(part, part, sends(ag_send, 1, lanes), ag_recv.at[i, 4], chip(z, far_y, far_x)),
        ]

    def corner_copy(i, lanes):
        b, m = of(i)
        part = wg.at[b, m, :, near_y, near_x, core, :, lanes]
        return remote(part, part, sends(ag_send, 2, lanes), ag_recv.at[i, 5], chip(z, far_y, far_x))

    def core_copy(i, lanes):
        b, m = of(i)
        part = wg.at[b, m, :, :, :, core, :, lanes]
        return remote(part, part, sends(ag_send, 3, lanes), ag_recv.at[i, 6], sibling)

    def by_lanes(m, step):
        pl.when(m == 0)(lambda: step(slice(0, 384)))
        pl.when(m > 0)(lambda: step(slice(0, hidden)))

    def start_all(copies):
        for copy in copies:
            copy.start()

    for load in loads:
        load.wait()
    zeros_tile = jnp.zeros((tile, 128), F32)

    def prepare(t, carry):
        at = pl.ds(t * tile, tile)
        resid[at, :] = zeros_tile
        resid[at, 0:past] = seg[at, :]
        return carry

    def prepare_mask(g, carry):
        lengths = ext[pl.ds(core * (windows // 128) + g, 1), :]
        position = lax.broadcasted_iota(jnp.int32, (128, 128), 0)
        keep = jnp.where(position >= past - lengths, 1.0, 0.0).astype(F32).T
        at = pl.ds(pl.multiple_of(g * 128, 128), 128)
        pad[0:span, :] = adj[:, at]
        f_ref[at, :] = pad[...].T.astype(BF)
        mask[at, :] = keep.astype(BF)
        resid[at, :] = resid[at, :] * keep
        return carry

    tiles = windows // tile
    part_tile = windows // 2

    def matrix(b, m):
        return wg[b, m].reshape(hidden, hidden)

    def small(b, lane):
        return wg[b, 0, :, :, :, :, :, lane : lane + 128].reshape(hidden, 128)

    def store_layer(b, k, at, v):
        p = 1.0 + jnp.tanh(v)
        a = v * p
        rate = p + a * (2.0 - p)
        slope[b, k, at, :] = rate.astype(BF)
        low = a.astype(BF)
        act_t[b, k, :, at] = low.T
        return low

    def halves(body):
        for t in range(2):
            body(slice(t * windows // 2, (t + 1) * windows // 2))

    def layer_zero(b):
        bias_t[...] = small(b, 128).astype(F32).T

        def body(at):
            a = resid[at, :].astype(BF)
            in_t[b, :, at] = a.T
            work[0, at, :] = store_layer(b, 0, at, dot_nt(a, small(b, 0)) + bias_t[span : span + 1, :])

        halves(body)

    def layer_next(b, k):
        source, target = lax.rem(k + 1, 2), lax.rem(k, 2)
        v = dot_nn(work[source], matrix(b, k)) + bias_t[pl.ds(span + k, 1), :]
        work[target] = store_layer(b, k, slice(0, windows), v)

    def grid(value):
        return value.astype(BF).reshape(ZN, YN, XN, 2, half_rows, -1)

    def backcast_step():
        def body(at):
            theta = dot_nn(work[1, at, :], matrix(0, 4)).astype(BF)
            theta_keep[at, :] = theta
            resid[at, :] = (resid[at, :] - dot_nn(theta, small(0, 256))) * mask[at, :].astype(F32)

        halves(body)

    def put_rows(buf, b, at, value):
        for row in range(value.shape[0]):
            buf[b, row, :, at] = value[row : row + 1]

    def late_theta(b, m):
        theta_t = act_t.at[1, 0]
        theta_t[...] = dot_nn(matrix(b, m).T, act_t[b, 3]).astype(BF)

        @pl.when(m == 4)
        def _():
            gp[b, 0, :, :, :, :, :, 256:384] = grid(dot_nt(theta_t[...], e_t[b]))

        @pl.when(m == 5)
        def _():
            grad = grid(dot_nn(theta_t[...], f_ref[...]))
            gp[b, 0, :, :, :, :, :, 128:256] = gp[b, 0, :, :, :, :, :, 128:256] + grad
            part_t[b] = dot_nn(small(b, 128).T, theta_t[...])[0:span]

    def forecasts():
        put_rows(pred, 0, slice(0, windows), part_t[0])
        put_rows(pred, 1, slice(0, windows), part_t[0].astype(BF).astype(F32) + part_t[1])

    count = 2 * MATS

    def delayed(lag, t, step):
        pl.when(jnp.logical_and(t >= lag, t < count + lag))(lambda: step(t - lag))

    def staged(lag, t, step):
        early = t - lag + 1
        pl.when(jnp.logical_and(early >= 1, early <= 2))(lambda: step(early))
        unit = t - lag
        pl.when(jnp.logical_and(unit >= 3, unit < count))(lambda: step(unit))
        if lag == 6:
            pl.when(t == 3)(lambda: step(0))

    def gather_line(i):
        b, m = of(i)

        def step(lanes):
            pl.when(b != core)(lambda: hand_over(m, lanes).wait_recv())
            start_all(z_copies(i, lanes))

        by_lanes(m, step)

    def gather_columns(i):
        def step(lanes):
            for copy in z_copies(i, lanes):
                copy.wait_recv()
            start_all(column_copies(i, lanes))

        by_lanes(of(i)[1], step)

    def gather_corner(i):
        def step(lanes):
            column_copies(i, lanes)[0].wait_recv()
            corner_copy(i, lanes).start()

        by_lanes(of(i)[1], step)

    def gather_core(i):
        def step(lanes):
            column_copies(i, lanes)[1].wait_recv()
            corner_copy(i, lanes).wait_recv()
            core_copy(i, lanes).start()

        by_lanes(of(i)[1], step)

    def arrived(i):
        by_lanes(of(i)[1], lambda lanes: core_copy(i, lanes).wait_recv())

    def forward_unit(i):
        arrived(i)
        b, m = of(i)
        pl.when(m == 0)(lambda: layer_zero(b))
        pl.when(jnp.logical_and(m >= 1, m <= 3))(lambda: layer_next(b, m))
        pl.when(m == 4)(backcast_step)

        @pl.when(jnp.logical_or(i == 4, i == 8))
        def _():
            pl.when(b == 1)(lambda: feed(b))
            pl.when(b == 0)(lambda: feed_forward(b))
            lax.fori_loop(jnp.where(b == 1, 4, 5), MATS, lambda n, carry: (theta_grad(b, n), carry)[1], 0)
            pl.when(b == 0)(lambda: scatter_start(0))

            @pl.when(b == 1)
            def _():
                scatter_start(1)
                scatter_start(2)

    def gather_step(t, carry):
        pl.when(t == 12)(lambda: scatter_core(0))
        pl.when(t == 15)(lambda: scatter_diag(0))
        delayed(4, t, gather_core)
        delayed(2, t, gather_corner)
        delayed(0, t, gather_columns)
        pl.when(t + 4 < count)(lambda: gather_line(t + 4))
        pl.when(jnp.logical_and(t >= 5, t < 14))(lambda: forward_unit(t - 5))
        return carry

    def out_copies(buf, out, s):
        at = pl.ds(row0, windows)
        return [
            pltpu.make_async_copy(buf.at[core], out.at[:, :, at], local_sem.at[2 + s]),
            remote(buf.at[other], out.at[:, :, at], out_send.at[s], out_recv.at[s], sibling),
        ]


    def back_of(j):
        b = jnp.where(jnp.logical_or(jnp.logical_and(j >= 1, j <= 5), j == 10), 1, 0)
        early = jnp.where(j == 1, 4, jnp.where(j <= 2, 5, 6 - j))
        return b, jnp.where(j <= 5, early, jnp.where(j == 6, 4, jnp.where(j <= 9, 10 - j, 0)))

    def to_core(j, lanes):
        b, m = back_of(j)
        return remote(
            gp.at[b, m, :, :, :, other, :, lanes], from_core.at[lax.rem(j, CORE_SLOTS), :, :, :, :, lanes],
            sends(rs_send, 3, lanes), rs_recv.at[j, 0], sibling,
        )

    def to_far(j, lanes):
        b, m = back_of(j)
        device = chip(z, far_y, far_x)
        return [
            remote(
                gp.at[b, m, :, yo, xo, core, :, lanes], from_diag.at[lax.rem(j, DIAG_SLOTS), :, :, lanes],
                sends(rs_send, 1, lanes), rs_recv.at[j, 1], device,
            ),
            remote(
                gp.at[b, m, :, far_y, far_x, core, :, lanes], from_plain.at[lax.rem(j, PLAIN_SLOTS), :, :, lanes],
                sends(rs_send, 1, lanes), rs_recv.at[j, 2], device,
            ),
        ]

    def to_near(j, lanes):
        b, m = back_of(j)
        return remote(
            gp.at[b, m, :, near_y, near_x, core, :, lanes], from_pair.at[lax.rem(j, PAIR_SLOTS), :, :, lanes],
            sends(rs_send, 2, lanes), rs_recv.at[j, 3], chip(z, near_y, near_x),
        )

    def to_z(j, lanes):
        b, m = back_of(j)
        return [
            remote(
                gp.at[b, m, zi, y, x, core, :, lanes], from_z.at[j, s, :, lanes],
                sends(rs_send, 0, lanes), rs_recv.at[j, 4 + s], chip(zi, y, x),
            )
            for s, zi in enumerate(z_peers)
        ]

    def scatter_start(j):
        by_lanes(back_of(j)[1], lambda lanes: to_core(j, lanes).start())

    def scatter_core(j):
        b, m = back_of(j)

        def step(lanes):
            to_core(j, lanes).wait_recv()
            part = gp[b, m, :, :, :, core, :, lanes] + from_core[lax.rem(j, CORE_SLOTS), :, :, :, :, lanes]
            gp[b, m, :, :, :, core, :, lanes] = part
            start_all(to_far(j, lanes))

        by_lanes(m, step)

    def scatter_diag(j):
        b, m = back_of(j)

        def step(lanes):
            to_far(j, lanes)[0].wait_recv()
            part = gp[b, m, :, near_y, near_x, core, :, lanes] + from_diag[lax.rem(j, DIAG_SLOTS), :, :, lanes]
            gp[b, m, :, near_y, near_x, core, :, lanes] = part
            to_near(j, lanes).start()

        by_lanes(m, step)

    def scatter_plane(j):
        b, m = back_of(j)

        def step(lanes):
            to_far(j, lanes)[1].wait_recv()
            to_near(j, lanes).wait_recv()
            value = gp[b, m, :, y, x, core, :, lanes].astype(F32)
            value = value + from_plain[lax.rem(j, PLAIN_SLOTS), :, :, lanes].astype(F32)
            value = value + from_pair[lax.rem(j, PAIR_SLOTS), :, :, lanes].astype(F32)
            gp[b, m, :, y, x, core, :, lanes] = value.astype(BF)
            start_all(to_z(j, lanes))

        by_lanes(m, step)

    def scatter_z(j):
        b, m = back_of(j)

        def step(lanes):
            for copy in to_z(j, lanes):
                copy.wait_recv()
            value = gp[b, m, z, y, x, core, :, lanes].astype(F32)
            for s in range(ZN - 1):
                value = value + from_z[j, s, :, lanes].astype(F32)
            total[b, m, :, lanes] = value
            squares[:, lanes] = squares[:, lanes] + value * value

        by_lanes(m, step)

    def add_rows(value):
        return jnp.sum(value.reshape(-1, 8, hidden), axis=0)

    def put_bias(k, acc):
        bias_sum[pl.ds(span + k, 1), :] = jnp.sum(acc, axis=0, keepdims=True)

    def feed(b):
        pl.when(b == 1)(lambda: resid.__setitem__(..., jnp.zeros_like(resid)))
        e = (-(resid[...] * mask[...].astype(F32))).astype(BF)
        e_t[b] = e.T
        work[0] = dot_nt(e, small(b, 256)).astype(BF)
        work[2] = dot_nt(f_ref[...], small(b, 128)).astype(BF)

    def feed_forward(b):
        work[2] = dot_nt(f_ref[...], small(b, 128)).astype(BF)

    def put_dz(b, k, da):
        dz = da * slope[b, k].astype(F32)
        work[k % 2 if isinstance(k, int) else lax.rem(k, 2)] = dz.astype(BF)
        bias_sum[pl.ds(span + k, 1), :] = jnp.sum(add_rows(dz), axis=0, keepdims=True)

    def theta_step(b):
        put_dz(b, 3, 0.5 * (dot_nt(work[0], matrix(b, 4)) + dot_nt(work[2], matrix(b, 5))))

    def layer_back(b, k):
        source = lax.rem(k, 2)
        gp[b, k] = grid(dot_nn(act_t[b, k - 1], work[source]))
        put_dz(b, k - 1, dot_nt(work[source], matrix(b, k)))

    def theta_grad(b, m):
        gp[b, m] = grid(dot_nn(act_t[b, 3], work[jnp.where(m == 4, 0, 2)]))

    def first_grads(b):
        gp[b, 0, :, :, :, :, :, 0:128] = grid(dot_nn(in_t[b], work[0]).T)
        gp[b, 0, :, :, :, :, :, 128:256] = grid(bias_sum[...].T)
        pl.when(b == 0)(backcast_grad)

    def backcast_grad():
        gp[0, 0, :, :, :, :, :, 256:384] = grid(dot_nn(e_t[0], theta_keep[...]).T)

    def input_grad(b):
        for t in range(2):
            at = slice(t * windows // 2, (t + 1) * windows // 2)
            keep = mask[at, :].astype(F32)
            dr = resid[at, :] * keep + 2.0 * dot_nn(work[0, at, :], small(b, 0))

            @pl.when(b == 1)
            def _():
                seg[at, :] = dr[:, 0:past]
                resid[at, :] = dr.astype(BF).astype(F32)

            @pl.when(b == 0)
            def _():
                put_rows(sens, 0, at, (dr * keep).T[0:past])

    def late_rows():
        for g in range(windows // 128):
            at = slice(g * 128, (g + 1) * 128)
            pad[:, 0:past] = seg[at, :]
            put_rows(sens, 1, at, pad[...].T[0:past])

    bias_sum[...] = jnp.zeros_like(bias_sum)
    squares[...] = jnp.zeros_like(squares)
    total[...] = jnp.zeros_like(total)

    def back_step(j, carry):
        b, m = back_of(j)

        @pl.when(jnp.logical_and(j >= count, j < count + 4))
        def _():
            scatter_z(2 * (j - count))
            scatter_z(2 * (j - count) + 1)

        pl.when(j >= count + 4)(lambda: scatter_z(j - 8))
        staged(6, j, scatter_plane)
        staged(4, j, scatter_diag)
        staged(2, j, scatter_core)

        @pl.when(j == 2)
        def _():
            arrived(9)
            arrived(10)
            theta_step(1)

        pl.when(jnp.logical_and(m >= 1, m <= 3))(lambda: layer_back(b, m))

        @pl.when(jnp.logical_or(j == 6, j == count - 1))
        def _():
            block = jnp.where(j == 6, 1, 0)
            first_grads(block)
            pl.when(j == 6)(lambda: input_grad(1))

        @pl.when(j == 6)
        def _():
            feed(0)
            theta_grad(0, 4)

        @pl.when(jnp.logical_or(j == 10, j == 11))
        def _():
            lax.fori_loop(jnp.where(j == 10, 4, 5), MATS, lambda n, carry: (late_theta(b, n), carry)[1], 0)

        pl.when(jnp.logical_and(j >= 3, j < count))(lambda: scatter_start(j))

        @pl.when(j == 6)
        def _():
            arrived(11)
            theta_step(0)

        @pl.when(j == count - 1)
        def _():
            input_grad(0)
            forecasts()
            start_all(out_copies(pred, pred_out, 0))

        @pl.when(j == count)
        def _():
            late_rows()
            start_all(out_copies(sens, sens_out, 1))

        return carry

    for i in range(4):
        gather_line(i)
    lax.fori_loop(0, tiles, prepare, 0)
    pad[...] = jnp.zeros_like(pad)
    lax.fori_loop(0, windows // 128, prepare_mask, 0)
    lax.fori_loop(0, count + 4, gather_step, 0)

    lax.fori_loop(2, count + 8, back_step, 0)

    grad_copy = remote(total.at[other], grad_out.at[:, core], out_send.at[2], out_recv.at[2], sibling)
    grad_copy.start()
    grad_out[:, core] = total[core]
    sq = squares[:, 0:128] + squares[:, 128:256] + squares[:, 256:384] + squares[:, 384:512]
    place = (y * XN + x) * 2 + core
    norm_buf[place] = sq[0:8] + sq[8:16]

    def spread(sources, targets, first):
        copies = [
            remote(norm_buf.at[sources], norm_buf.at[sources], norm_send.at[first + s], norm_recv.at[first + s], device)
            for s, device in enumerate(targets)
        ]
        start_all(copies)
        for copy in copies:
            copy.wait()

    def add_up(slots):
        value = norm_buf[slots[0]]
        for slot in slots[1:]:
            value = value + norm_buf[slot]
        return value

    spread(place, plane_peers, 0)
    norm_buf[8 + z] = add_up(range(8))
    spread(8 + z, [chip(zi, y, x) for zi in z_peers], 7)
    everything = add_up(range(8, 8 + ZN))
    norm_out[...] = jnp.broadcast_to(jnp.sqrt(jnp.sum(everything, keepdims=True)), norm_out.shape)

    grad_copy.wait()
    for buf, out, s in ((pred, pred_out, 0), (sens, sens_out, 1)):
        for copy in out_copies(buf, out, s):
            copy.wait()
    for m in range(MATS):
        hand_over(m, slice(0, hidden if m else 384)).wait_send()

    for mats, lanes in ((slice(1, MATS), slice(0, hidden)), (slice(0, 1), slice(0, 384))):
        sent = (
            wg.at[:, mats, 0 : ZN - 1, 0, 0, 0, :, lanes],
            wg.at[:, mats, :, :, 0, 0, :, lanes],
            wg.at[:, mats, :, 0, 0, 0, :, lanes],
            wg.at[:, mats, :, :, :, 0, :, lanes],
        )
        for sems in (ag_send, rs_send):
            for kind, ref in enumerate(sent):
                remote(ref, ref, sends(sems, kind, lanes), out_recv.at[0], sibling).wait_send()


def train_call(plane, segments, extents, adjoint, first, square, head, biases):
    ZN, YN, XN = plane
    past, span, hidden = segments.shape[1], adjoint.shape[0], square.shape[3]
    windows = segments.shape[0] // 2
    tile = windows
    half = hidden // (ZN * YN * XN) // 2
    sizes = (ZN, YN, XN, windows, tile, past, span, hidden)
    DMA = pltpu.SemaphoreType.DMA
    vmem = pl.BlockSpec(memory_space=pltpu.VMEM)
    hbm = pl.BlockSpec(memory_space=pl.ANY)
    count = 2 * MATS
    flops = 2 * 2 * 3 * windows * hidden * (6 * hidden + 2 * 128)
    lengths = extents.reshape(-1, 128)
    return pl.pallas_call(
        functools.partial(train_kernel, sizes),
        out_shape=(
            jax.ShapeDtypeStruct((span, 1, 2 * windows), F32),
            jax.ShapeDtypeStruct((past, 1, 2 * windows), F32),
            jax.ShapeDtypeStruct((MATS, 2, half, hidden), F32),
            jax.ShapeDtypeStruct((8, 128), F32),
        ),
        in_specs=[hbm] * 7,
        out_specs=(hbm, hbm, vmem, vmem),
        scratch_shapes=[
            pltpu.VMEM((2, MATS, ZN, YN, XN, 2, half, hidden), BF),
            pltpu.VMEM((MATS, half, hidden), BF),
            pltpu.VMEM((2, MATS, ZN, YN, XN, 2, half, hidden), BF),
            pltpu.VMEM((CORE_SLOTS, ZN, YN, XN, half, hidden), BF),
            pltpu.VMEM((DIAG_SLOTS, ZN, half, hidden), BF),
            pltpu.VMEM((PLAIN_SLOTS, ZN, half, hidden), BF),
            pltpu.VMEM((PAIR_SLOTS, ZN, half, hidden), BF),
            pltpu.VMEM((count, ZN - 1, half, hidden), BF),
            pltpu.VMEM((2, MATS, half, hidden), F32),
            pltpu.VMEM((2, 4, hidden, windows), BF),
            pltpu.VMEM((2, 128, windows), BF),
            pltpu.VMEM((windows, hidden), BF),
            pltpu.VMEM((2, 4, windows, hidden), BF),
            pltpu.VMEM((3, windows, hidden), BF),
            pltpu.VMEM((windows, 128), F32),
            pltpu.VMEM((windows, 128), BF),
            pltpu.VMEM((windows, 128), BF),
            pltpu.VMEM((2, 128, windows), BF),
            pltpu.VMEM((128, hidden), F32),
            pltpu.VMEM((128, hidden), F32),
            pltpu.VMEM((128, 128), F32),
            pltpu.VMEM((windows, past), F32),
            pltpu.VMEM((span, windows), F32),
            *(pltpu.VMEM(a.shape, a.dtype) for a in (lengths, first, square, head, biases)),
            pltpu.VMEM((2, span, windows), F32),
            pltpu.VMEM((2, span, 1, windows), F32),
            pltpu.VMEM((2, past, 1, windows), F32),
            pltpu.VMEM((half, hidden), F32),
            pltpu.VMEM((8 + ZN, 8, 128), F32),
            DMA((MATS,)),
            DMA((MATS,)),
            DMA((4, 2)),
            DMA((count, 4 + ZN - 1)),
            DMA((4, 2)),
            DMA((count, 4 + ZN - 1)),
            DMA((3,)),
            DMA((3,)),
            DMA((9,)),
            DMA((7 + ZN - 1,)),
            DMA((7 + ZN - 1,)),
        ],
        compiler_params=pltpu.CompilerParams(
            collective_id=0, has_side_effects=True, vmem_limit_bytes=64 * 1024 * 1024
        ),
        cost_estimate=pl.CostEstimate(flops=flops, bytes_accessed=8_000_000, transcendentals=8 * windows * hidden),
        name="train",
    )(segments, adjoint, lengths, first, square, head, biases)


def update_kernel(past, span, *refs):
    sources, targets, norm_out = refs[0:16], refs[16:34], refs[34]
    held, results, pad, in_sem, out_sem = refs[35:51], refs[51:67], *refs[67:70]
    arriving = [pltpu.make_async_copy(source, ref, in_sem.at[n]) for n, (source, ref) in enumerate(zip(sources, held))]
    leaving = [
        pltpu.make_async_copy(ref, target, out_sem.at[n]) for n, (ref, target) in enumerate(zip(held[0:2] + results, targets))
    ]
    for copy in arriving:
        copy.start()
    grads, norm, masters, momenta, variances = held[2], held[3], held[4:8], held[8:12], held[12:16]
    units = masters[3].shape[2]

    def rows(m, lane, width):
        return grads[m, :, :, lane : lane + width].reshape(units, width)

    arriving[2].wait()
    arriving[3].wait()
    norm_out[...] = norm[0:1, 0:1]
    factor = 1.0 / jnp.maximum(norm[0:1, 0:1], 1.0)
    for m in range(5):
        results[1][0, m] = rows(m + 1, 0, grads.shape[3])
    results[0][0] = rows(0, 0, 128)[:, 0:past]
    forecast = rows(0, 128, 128)
    pad[...] = jnp.zeros_like(pad)
    pad[0:units, :] = forecast
    results[3][0] = pad[...].T[span : span + 4, 0:units]
    results[2][0, :, 0:past] = rows(0, 256, 128)[:, 0:past]
    results[2][0, :, past : past + span] = forecast[:, 0:span]
    for n in (0, 1):
        arriving[n].wait()
        leaving[n].start()
    for n in (1, 0, 2, 3):
        leaving[2 + n].start()
        for state in range(3):
            arriving[4 + 4 * state + n].wait()
        updated = adamw(masters[n][...], results[n][...], momenta[n][...], variances[n][...], factor[None])
        for kind, value in enumerate(updated):
            results[4 * (kind + 1) + n][...] = value
            leaving[2 + 4 * (kind + 1) + n].start()
    for copy in leaving:
        copy.wait()


def update_call(prediction, sensitivity, grads, norm, state):
    hbm = pl.BlockSpec(memory_space=pl.ANY)
    sources = (prediction, sensitivity, grads, norm, *state)
    targets = (prediction, sensitivity, *(4 * list(state[:4])))
    return pl.pallas_call(
        functools.partial(update_kernel, sensitivity.shape[0], prediction.shape[0]),
        out_shape=tuple(jax.ShapeDtypeStruct(a.shape, F32) for a in targets) + (jax.ShapeDtypeStruct((1, 1), F32),),
        in_specs=[hbm] * len(sources),
        out_specs=tuple([hbm] * len(targets) + [pl.BlockSpec(memory_space=pltpu.VMEM)]),
        scratch_shapes=[pltpu.VMEM(a.shape, F32) for a in sources]
        + [pltpu.VMEM(a.shape, F32) for a in targets[2:]]
        + [pltpu.VMEM((128, 128), F32), pltpu.SemaphoreType.DMA((len(sources),)), pltpu.SemaphoreType.DMA((len(targets),))],
        name="update",
    )(*sources)


def turned(arrays):
    return [a.transpose(0, 2, 1) if n % 4 == 0 else a for n, a in enumerate(arrays)]


def kernel_shards(plane, segments, extents, adjoint, *state):
    state = turned(state)
    results = train_call(plane, segments, extents, adjoint.T, *state[:4])
    prediction, sensitivity, *updated, norm = update_call(*results, state)
    by_window = (prediction.transpose(1, 2, 0), sensitivity.transpose(1, 2, 0))
    return (*by_window, norm.reshape(()), *turned(updated))


STATE_SPECS = (
    P("section", None, "dp"),
    P("section", None, "dp", None),
    P("section", "dp", None),
    P("section", None, "dp"),
)


def solution(mesh):
    in_specs = (P("dp", None), P("dp"), P("dp", None)) + 3 * STATE_SPECS
    out_specs = (P("section", "dp", None), P("section", "dp", None), P()) + 4 * STATE_SPECS
    plane = PLANES.get(mesh.shape["dp"])
    shards = plain_shards if plane is None else functools.partial(kernel_shards, plane)
    return jax.shard_map(shards, mesh=mesh, in_specs=in_specs, out_specs=out_specs, check_vma=False)
```

```python
import functools

import jax
import jax.numpy as jnp
from jax import lax
from jax.experimental import pallas as pl
from jax.experimental.pallas import tpu as pltpu
from jax.sharding import PartitionSpec as P

STEP = 10


def dot_nn(a, b):
    return jnp.dot(a, b, preferred_element_type=jnp.float32)


def dot_tn(a, b):
    return lax.dot_general(a, b, (((0,), (0,)), ((), ())), preferred_element_type=jnp.float32)


def dot_nt(a, b):
    return lax.dot_general(a, b, (((1,), (1,)), ((), ())), preferred_element_type=jnp.float32)


def unit_rows(first, square, head, biases):
    units = first.shape[1]
    return jnp.concatenate(
        [square.transpose(1, 0, 2).reshape(units, -1), first.T, head, biases.T], axis=1
    )


def from_unit_rows(rows, past, hidden, out):
    wide = 5 * hidden
    square = rows[:, :wide].reshape(-1, 5, hidden).transpose(1, 0, 2)
    first = rows[:, wide : wide + past].T
    head = rows[:, wide + past : wide + past + out]
    biases = rows[:, wide + past + out :].T
    return first, square, head, biases


def plain_forward(weights, resid):
    first, square, head, biases = weights
    past = resid.shape[1]
    acts, slopes = [resid.astype(jnp.bfloat16)], []
    for k in range(4):
        z = dot_nn(acts[-1], first if k == 0 else square[k - 1]) + biases[k].astype(jnp.float32)
        sig = jax.nn.sigmoid(z)
        acts.append((z * sig).astype(jnp.bfloat16))
        slopes.append(sig * (1.0 + z * (1.0 - sig)))
    theta_b = dot_nn(acts[4], square[3]).astype(jnp.bfloat16)
    theta_f = dot_nn(acts[4], square[4]).astype(jnp.bfloat16)
    backcast = dot_nn(theta_b, head[:, :past])
    part = dot_nn(theta_f, head[:, past:])
    return backcast, part, (acts, slopes, theta_b, theta_f)


def plain_backward(weights, saved, e, f):
    first, square, head, biases = weights
    acts, slopes, theta_b, theta_f = saved
    past = e.shape[1]
    head_grad = jnp.concatenate([dot_tn(theta_b, e), dot_tn(theta_f, f)], axis=1)
    u_b = dot_nt(e, head[:, :past]).astype(jnp.bfloat16)
    u_f = dot_nt(f, head[:, past:]).astype(jnp.bfloat16)
    squares = [None, None, None, dot_tn(acts[4], u_b), dot_tn(acts[4], u_f)]
    da = dot_nt(u_b, square[3]) + dot_nt(u_f, square[4])
    bias_grads = [None] * 4
    first_grad = None
    for k in (3, 2, 1, 0):
        dz = (da * slopes[k]).astype(jnp.bfloat16)
        bias_grads[k] = jnp.sum(dz, axis=0, dtype=jnp.float32)
        grad = dot_tn(acts[k], dz)
        if k == 0:
            first_grad = grad
        else:
            squares[k - 1] = grad
        da = dot_nt(dz, first if k == 0 else square[k - 1])
    return da, (first_grad, jnp.stack(squares), head_grad, jnp.stack(bias_grads))


def adamw(master, gradient, momentum, variance, factor):
    clipped = gradient * factor
    moment_new = 0.9 * momentum + 0.1 * clipped
    variance_new = 0.999 * variance + 0.001 * clipped * clipped
    ratio = moment_new / (1.0 - 0.9**STEP) / (jnp.sqrt(variance_new / (1.0 - 0.999**STEP)) + 1e-08)
    return master - 0.05 * (ratio + 0.01 * master), moment_new, variance_new


def plain_shards(segments, extents, adjoint, *state):
    masters, momenta, variances = state[:4], state[4:8], state[8:]
    core = lax.axis_index("section")
    past, span = segments.shape[1], adjoint.shape[1]
    windows = segments.shape[0] // 2
    hidden = masters[1].shape[3]
    mine = [
        lax.dynamic_slice_in_dim(v, core * windows, windows, 0) for v in (segments, extents, adjoint)
    ]
    seg, ext, adj = mine
    rows = unit_rows(*(m[0].astype(jnp.bfloat16) for m in masters))
    rows = lax.all_gather(rows, "dp", axis=0, tiled=True)
    rows = lax.all_gather(rows, "section", axis=0)
    blocks = [from_unit_rows(rows[b], past, hidden, past + span) for b in range(2)]
    mask = (
        lax.broadcasted_iota(jnp.int32, (windows, past), 1) >= past - ext[:, None]
    ).astype(jnp.float32)
    r0 = seg * mask
    backcast, part0, saved0 = plain_forward(blocks[0], r0)
    r1 = (r0 - backcast) * mask
    _, part1, saved1 = plain_forward(blocks[1], r1)
    forecast = part0.astype(jnp.bfloat16).astype(jnp.float32) + part1
    f = adj.astype(jnp.bfloat16)
    zero = jnp.zeros_like(r0)
    da1, grads1 = plain_backward(blocks[1], saved1, (-(zero * mask)).astype(jnp.bfloat16), f)
    dr1 = zero * mask + da1
    t = dr1.astype(jnp.bfloat16).astype(jnp.float32)
    da0, grads0 = plain_backward(blocks[0], saved0, (-(t * mask)).astype(jnp.bfloat16), f)
    dr0 = (t * mask + da0) * mask

    def by_section(first_block, second_block):
        mine, other = (
            jnp.where(core == 0, first_block, second_block),
            jnp.where(core == 0, second_block, first_block),
        )
        got = lax.ppermute(other, "section", [(0, 1), (1, 0)])
        return jnp.where(
            core == 0, jnp.concatenate([mine, got]), jnp.concatenate([got, mine])
        )[None]

    prediction = by_section(part0, forecast)
    sensitivity = by_section(dr0, dr1)
    packed = jnp.stack([unit_rows(*grads0), unit_rows(*grads1)])
    packed = lax.psum_scatter(packed, "section", scatter_dimension=0, tiled=False)
    packed = lax.psum_scatter(packed, "dp", scatter_dimension=0, tiled=True)
    norm = jnp.sqrt(lax.psum(jnp.sum(packed * packed), ("section", "dp")))
    factor = 1.0 / jnp.maximum(norm, 1.0)
    summed = [g[None] for g in from_unit_rows(packed, past, hidden, past + span)]
    updated = [adamw(*four, factor) for four in zip(masters, summed, momenta, variances)]
    return (
        prediction,
        sensitivity,
        norm,
        *summed,
        *(u[0] for u in updated),
        *(u[1] for u in updated),
        *(u[2] for u in updated),
    )


PLANES = {16: (4, 2, 2)}
MESH = pl.DeviceIdType.MESH
MATS = 6
CORE_SLOTS, DIAG_SLOTS, PLAIN_SLOTS, PAIR_SLOTS = 4, 4, 6, 4
BF, F32 = jnp.bfloat16, jnp.float32


ORDER = ((0, 5), (1, 4), (1, 5), (1, 3), (1, 2), (1, 1), (0, 4), (0, 3), (0, 2), (0, 1), (1, 0), (0, 0))


def remote(src, dst, send_sem, recv_sem, device):
    return pltpu.make_async_remote_copy(
        src_ref=src, dst_ref=dst, send_sem=send_sem, recv_sem=recv_sem, device_id=device, device_id_type=MESH
    )


def train_kernel(
    sizes,
    seg_hbm, adj_hbm, ext_hbm, first_hbm, square_hbm, head_hbm, biases_hbm,
    pred_out, sens_out, grad_out, norm_out,
    wg, handed, gp, from_core, from_diag, from_plain, from_pair, from_z, total,
    act_t, in_t, theta_keep, slope, work, resid, mask, f_ref, e_t, bias_t, bias_sum, pad,
    seg, adj, ext, first, square, head, biases, part_t, pred, sens, squares, norm_buf,
    own_send, own_recv, ag_send, ag_recv, rs_send, rs_recv, out_send, out_recv, local_sem, norm_send, norm_recv,
):
    ZN, YN, XN, windows, tile, past, span, hidden = sizes
    units = ZN * YN * XN
    core, dp = lax.axis_index("section"), lax.axis_index("dp")
    x, y, z = lax.rem(dp, XN), lax.rem(lax.div(dp, XN), YN), lax.div(dp, XN * YN)
    other, xo, yo = 1 - core, 1 - x, 1 - y
    near_y, near_x = y + core * (yo - y), xo + core * (x - xo)
    far_y, far_x = yo + core * (y - yo), x + core * (xo - x)

    def chip(zi, yi, xi):
        return (core, (zi * YN + yi) * XN + xi)

    sibling = (other, dp)
    z_peers = [lax.rem(z + step, ZN) for step in range(1, ZN)]

    row0 = core * windows
    loads = [
        pltpu.make_async_copy(seg_hbm.at[pl.ds(row0, windows), :], seg, local_sem.at[0]),
        pltpu.make_async_copy(adj_hbm.at[:, pl.ds(row0, windows)], adj, local_sem.at[1]),
    ]
    small_loads = [
        pltpu.make_async_copy(source, target, local_sem.at[4 + n])
        for n, (source, target) in enumerate(
            [(square_hbm, square), (first_hbm, first), (head_hbm, head), (biases_hbm, biases), (ext_hbm, ext)]
        )
    ]
    for load in small_loads + loads:
        load.start()

    barrier = pltpu.get_barrier_semaphore()
    plane_peers = [
        (ci, (z * YN + yi) * XN + xi) for ci in (core, other) for yi in (y, yo) for xi in (x, xo)
    ][1:]
    peers = plane_peers + [(ci, (zi * YN + y) * XN + x) for zi in z_peers for ci in (core, other)]
    for peer in peers:
        pl.semaphore_signal(barrier, inc=1, device_id=peer, device_id_type=MESH)

    rows = hidden // units
    half_rows = rows // 2

    def put_own(m, value, lanes):
        halves = value.astype(BF).reshape(2, half_rows, -1)
        for h in range(2):
            pl.when(core == h)(functools.partial(put_half, m, halves[h], halves[1 - h], lanes))

    def put_half(m, kept, given, lanes):
        wg[core, m, z, y, x, core, :, lanes] = kept
        handed[m, :, lanes] = given

    for load in small_loads:
        load.wait()
    pad[...] = jnp.zeros_like(pad)
    pad[0:rows, 0:past] = first[0] * 0.5
    put_own(0, pad[0:rows, :], slice(0, 128))
    pad[...] = jnp.zeros_like(pad)
    pad[span : span + 4, 0:rows] = biases[0] * 0.5
    bias_cols = pad[...].T[0:rows]
    pad[...] = jnp.zeros_like(pad)
    pad[0:rows, 0:span] = head[0, :, past : past + span]
    put_own(0, pad[0:rows, :] + bias_cols, slice(128, 256))
    pad[...] = jnp.zeros_like(pad)
    pad[0:rows, 0:past] = head[0, :, 0:past]
    put_own(0, pad[0:rows, :], slice(256, 384))
    pl.semaphore_wait(barrier, len(peers))

    def hand_over(m, lanes):
        return remote(
            handed.at[m, :, lanes], wg.at[core, m, z, y, x, other, :, lanes], own_send.at[m], own_recv.at[m], sibling
        )

    def pack(m):
        put_own(m, square[0, m - 1] * 0.5 if m < 4 else square[0, m - 1], slice(0, hidden))


    def of(i):
        b = jnp.where(jnp.logical_and(i >= 5, i <= 10), 1, 0)
        return b, jnp.where(i <= 4, i, jnp.where(i <= 10, i - 5, 5))

    def sends(sems, kind, lanes):
        return sems.at[kind, 0 if lanes.stop == hidden else 1]

    def z_copies(i, lanes):
        b, m = of(i)
        part = wg.at[b, m, z, y, x, core, :, lanes]
        return [
            remote(part, part, sends(ag_send, 0, lanes), ag_recv.at[i, s], chip(zi, y, x)) for s, zi in enumerate(z_peers)
        ]

    def line_copies(i, lanes):
        b, m = of(i)
        given = wg.at[b, m, z, y, x, other, :, lanes]
        return [
            remote(
                handed.at[m, :, lanes], given, sends(ag_send, 0, lanes), ag_recv.at[i, s], (other, (zi * YN + y) * XN + x)
            )
            for s, zi in enumerate(z_peers)
        ]

    def column_copies(i, lanes):
        b, m = of(i)
        part = wg.at[b, m, :, y, x, core, :, lanes]
        return [
            remote(part, part, sends(ag_send, 1, lanes), ag_recv.at[i, 3], chip(z, near_y, near_x)),
            remote(part, part, sends(ag_send, 1, lanes), ag_recv.at[i, 4], chip(z, far_y, far_x)),
        ]

    def corner_copy(i, lanes):
        b, m = of(i)
        part = wg.at[b, m, :, near_y, near_x, core, :, lanes]
        return remote(part, part, sends(ag_send, 2, lanes), ag_recv.at[i, 5], chip(z, far_y, far_x))

    def core_copy(i, lanes):
        b, m = of(i)
        part = wg.at[b, m, :, :, :, core, :, lanes]
        return remote(part, part, sends(ag_send, 3, lanes), ag_recv.at[i, 6], sibling)

    def by_lanes(m, step):
        if isinstance(m, int):
            step(slice(0, hidden if m else 384))
            return
        pl.when(m == 0)(lambda: step(slice(0, 384)))
        pl.when(m > 0)(lambda: step(slice(0, hidden)))

    def start_all(copies):
        for copy in copies:
            copy.start()

    zeros_tile = jnp.zeros((tile, 128), F32)

    def prepare(t, carry):
        at = pl.ds(t * tile, tile)
        resid[at, :] = zeros_tile
        resid[at, 0:past] = seg[at, :]
        return carry

    def prepare_mask(g, carry):
        lengths = ext[pl.ds(core * (windows // 128) + g, 1), :]
        position = lax.broadcasted_iota(jnp.int32, (128, 128), 0)
        keep = jnp.where(position >= past - lengths, 1.0, 0.0).astype(F32).T
        at = pl.ds(pl.multiple_of(g * 128, 128), 128)
        pad[0:span, :] = adj[:, at]
        f_ref[at, :] = pad[...].T.astype(BF)
        mask[at, :] = keep.astype(BF)
        resid[at, :] = resid[at, :] * keep
        return carry

    tiles = windows // tile
    part_tile = windows // 2

    def matrix(b, m):
        return wg[b, m].reshape(hidden, hidden)

    def small(b, lane):
        return wg[b, 0, :, :, :, :, :, lane : lane + 128].reshape(hidden, 128)

    def store_layer(b, k, at, v):
        p = 1.0 + jnp.tanh(v)
        a = v * p
        rate = p + a * (2.0 - p)
        slope[b, k, at, :] = rate.astype(BF)
        low = a.astype(BF)
        act_t[b, k, :, at] = low.T
        return low

    def halves(body):
        for t in range(2):
            body(slice(t * windows // 2, (t + 1) * windows // 2))

    def layer_zero(b):
        bias_t[...] = small(b, 128).astype(F32).T

        def body(at):
            a = resid[at, :].astype(BF)
            in_t[b, :, at] = a.T
            work[0, at, :] = store_layer(b, 0, at, dot_nt(a, small(b, 0)) + bias_t[span : span + 1, :])

        halves(body)

    def layer_next(b, k):
        source, target = lax.rem(k + 1, 2), lax.rem(k, 2)
        v = dot_nn(work[source], matrix(b, k)) + bias_t[pl.ds(span + k, 1), :]
        work[target] = store_layer(b, k, slice(0, windows), v)

    def grid(value):
        return value.astype(BF).reshape(ZN, YN, XN, 2, half_rows, -1)

    def backcast_step():
        def body(at):
            theta = dot_nn(work[1, at, :], matrix(0, 4)).astype(BF)
            theta_keep[at, :] = theta
            resid[at, :] = (resid[at, :] - dot_nn(theta, small(0, 256))) * mask[at, :].astype(F32)

        halves(body)

    def put_rows(buf, b, at, value):
        for row in range(value.shape[0]):
            buf[b, row, :, at] = value[row : row + 1]

    def late_theta(b, m):
        theta_t = act_t.at[1, 0]
        theta_t[...] = dot_nn(matrix(b, m).T, act_t[b, 3]).astype(BF)

        @pl.when(m == 4)
        def _():
            gp[b, 0, :, :, :, :, :, 256:384] = grid(dot_nt(theta_t[...], e_t[b]))

        @pl.when(m == 5)
        def _():
            grad = grid(dot_nn(theta_t[...], f_ref[...]))
            gp[b, 0, :, :, :, :, :, 128:256] = gp[b, 0, :, :, :, :, :, 128:256] + grad
            part_t[b] = dot_nn(small(b, 128).T, theta_t[...])[0:span]

    def forecasts():
        put_rows(pred, 0, slice(0, windows), part_t[0])
        put_rows(pred, 1, slice(0, windows), part_t[0].astype(BF).astype(F32) + part_t[1])

    count = 2 * MATS

    def delayed(lag, t, step):
        pl.when(jnp.logical_and(t >= lag, t < count + lag))(lambda: step(t - lag))

    def staged(lag, t, step):
        early = t - lag + 1
        pl.when(jnp.logical_and(early >= (2 if lag == 2 else 1), early <= 2))(lambda: step(early))
        unit = t - lag
        pl.when(jnp.logical_and(unit >= 3, unit < count))(lambda: step(unit))
        if lag == 6:
            pl.when(t == 3)(lambda: step(0))

    def gather_line(i):
        b, m = of(i)

        pl.when(b == core)(lambda: by_lanes(m, lambda lanes: start_all(line_copies(i, lanes) + z_copies(i, lanes))))

    def gather_columns(i):
        b, m = of(i)

        def step(lanes):
            pl.when(b != core)(lambda: hand_over(m, lanes).wait_recv())
            for copy in z_copies(i, lanes):
                copy.wait_recv()
            start_all(column_copies(i, lanes))

        by_lanes(m, step)

    def gather_corner(i):
        def step(lanes):
            column_copies(i, lanes)[0].wait_recv()
            corner_copy(i, lanes).start()

        by_lanes(of(i)[1], step)

    def gather_core(i):
        def step(lanes):
            column_copies(i, lanes)[1].wait_recv()
            corner_copy(i, lanes).wait_recv()
            core_copy(i, lanes).start()

        by_lanes(of(i)[1], step)

    def arrived(i):
        by_lanes(of(i)[1], lambda lanes: core_copy(i, lanes).wait_recv())

    def forward_unit(i):
        arrived(i)
        b, m = of(i)
        pl.when(m == 0)(lambda: layer_zero(b))
        pl.when(jnp.logical_and(m >= 1, m <= 3))(lambda: layer_next(b, m))
        pl.when(m == 4)(backcast_step)

        pl.when(i == 8)(lambda: gather_core(10))

        @pl.when(jnp.logical_or(i == 4, i == 8))
        def _():
            pl.when(b == 1)(lambda: feed(b))
            pl.when(b == 0)(lambda: feed_forward(b))
            lax.fori_loop(jnp.where(b == 1, 4, 5), MATS, lambda n, carry: (theta_grad(b, n), carry)[1], 0)
            pl.when(b == 0)(lambda: scatter_start(0))

            @pl.when(b == 1)
            def _():
                scatter_start(1)
                scatter_start(2)

    def gather_step(t, carry):
        pl.when(t == 12)(lambda: scatter_core(0))
        pl.when(t == 15)(lambda: scatter_diag(0))
        pl.when(jnp.logical_and(t >= 4, t != 14))(lambda: gather_core(t - 4))
        delayed(2, t, gather_corner)
        delayed(0, t, gather_columns)
        pl.when(t + 4 < count)(lambda: gather_line(t + 4))

        @pl.when(t == 0)
        def _():
            for load in loads:
                load.wait()
            lax.fori_loop(0, tiles, prepare, 0)
            pad[...] = jnp.zeros_like(pad)
            lax.fori_loop(0, windows // 128, prepare_mask, 0)

        pl.when(jnp.logical_and(t >= 5, t < 14))(lambda: forward_unit(t - 5))
        return carry

    def out_copies(buf, out, s):
        at = pl.ds(row0, windows)
        return [
            pltpu.make_async_copy(buf.at[core], out.at[:, :, at], local_sem.at[2 + s]),
            remote(buf.at[other], out.at[:, :, at], out_send.at[s], out_recv.at[s], sibling),
        ]


    def back_of(j):
        if isinstance(j, int):
            return ORDER[j]
        b = jnp.where(jnp.logical_or(jnp.logical_and(j >= 1, j <= 5), j == 10), 1, 0)
        early = jnp.where(j == 1, 4, jnp.where(j <= 2, 5, 6 - j))
        return b, jnp.where(j <= 5, early, jnp.where(j == 6, 4, jnp.where(j <= 9, 10 - j, 0)))

    def to_core(j, lanes):
        b, m = back_of(j)
        return remote(
            gp.at[b, m, :, :, :, other, :, lanes], from_core.at[lax.rem(j, CORE_SLOTS), :, :, :, :, lanes],
            sends(rs_send, 3, lanes), rs_recv.at[j, 0], sibling,
        )

    def to_far(j, lanes):
        b, m = back_of(j)
        device = chip(z, far_y, far_x)
        return [
            remote(
                gp.at[b, m, :, yo, xo, core, :, lanes], from_diag.at[lax.rem(j, DIAG_SLOTS), :, :, lanes],
                sends(rs_send, 1, lanes), rs_recv.at[j, 1], device,
            ),
            remote(
                gp.at[b, m, :, far_y, far_x, core, :, lanes], from_plain.at[lax.rem(j, PLAIN_SLOTS), :, :, lanes],
                sends(rs_send, 1, lanes), rs_recv.at[j, 2], device,
            ),
        ]

    def to_near(j, lanes):
        b, m = back_of(j)
        return remote(
            gp.at[b, m, :, near_y, near_x, core, :, lanes], from_pair.at[lax.rem(j, PAIR_SLOTS), :, :, lanes],
            sends(rs_send, 2, lanes), rs_recv.at[j, 3], chip(z, near_y, near_x),
        )

    def to_z(j, lanes):
        b, m = back_of(j)
        return [
            remote(
                gp.at[b, m, zi, y, x, core, :, lanes], from_z.at[j, s, :, lanes],
                sends(rs_send, 0, lanes), rs_recv.at[j, 4 + s], chip(zi, y, x),
            )
            for s, zi in enumerate(z_peers)
        ]

    def scatter_start(j):
        by_lanes(back_of(j)[1], lambda lanes: to_core(j, lanes).start())

    def scatter_core(j):
        b, m = back_of(j)

        def step(lanes):
            to_core(j, lanes).wait_recv()
            part = gp[b, m, :, :, :, core, :, lanes] + from_core[lax.rem(j, CORE_SLOTS), :, :, :, :, lanes]
            gp[b, m, :, :, :, core, :, lanes] = part
            start_all(to_far(j, lanes))

        by_lanes(m, step)

    def scatter_diag(j):
        b, m = back_of(j)

        def step(lanes):
            to_far(j, lanes)[0].wait_recv()
            part = gp[b, m, :, near_y, near_x, core, :, lanes] + from_diag[lax.rem(j, DIAG_SLOTS), :, :, lanes]
            gp[b, m, :, near_y, near_x, core, :, lanes] = part
            to_near(j, lanes).start()

        by_lanes(m, step)

    def scatter_plane(j):
        b, m = back_of(j)

        def step(lanes):
            to_far(j, lanes)[1].wait_recv()
            to_near(j, lanes).wait_recv()
            value = gp[b, m, :, y, x, core, :, lanes].astype(F32)
            value = value + from_plain[lax.rem(j, PLAIN_SLOTS), :, :, lanes].astype(F32)
            value = value + from_pair[lax.rem(j, PAIR_SLOTS), :, :, lanes].astype(F32)
            gp[b, m, :, y, x, core, :, lanes] = value.astype(BF)
            start_all(to_z(j, lanes))

        by_lanes(m, step)

    def scatter_z(j):
        b, m = back_of(j)

        def step(lanes):
            for copy in to_z(j, lanes):
                copy.wait_recv()
            value = gp[b, m, z, y, x, core, :, lanes].astype(F32)
            for s in range(ZN - 1):
                value = value + from_z[j, s, :, lanes].astype(F32)
            total[b, m, :, lanes] = value
            squares[:, lanes] = squares[:, lanes] + value * value

        by_lanes(m, step)

    def add_rows(value):
        return jnp.sum(value.reshape(-1, 8, hidden), axis=0)

    def put_bias(k, acc):
        bias_sum[pl.ds(span + k, 1), :] = jnp.sum(acc, axis=0, keepdims=True)

    def feed(b):
        pl.when(b == 1)(lambda: resid.__setitem__(..., jnp.zeros_like(resid)))
        e = (-(resid[...] * mask[...].astype(F32))).astype(BF)
        e_t[b] = e.T
        work[0] = dot_nt(e, small(b, 256)).astype(BF)
        work[2] = dot_nt(f_ref[...], small(b, 128)).astype(BF)

    def feed_forward(b):
        work[2] = dot_nt(f_ref[...], small(b, 128)).astype(BF)

    def put_dz(b, k, da):
        dz = da * slope[b, k].astype(F32)
        work[k % 2 if isinstance(k, int) else lax.rem(k, 2)] = dz.astype(BF)
        bias_sum[pl.ds(span + k, 1), :] = jnp.sum(add_rows(dz), axis=0, keepdims=True)

    def theta_step(b):
        put_dz(b, 3, 0.5 * (dot_nt(work[0], matrix(b, 4)) + dot_nt(work[2], matrix(b, 5))))

    def layer_back(b, k):
        source = lax.rem(k, 2)
        gp[b, k] = grid(dot_nn(act_t[b, k - 1], work[source]))
        put_dz(b, k - 1, dot_nt(work[source], matrix(b, k)))

    def theta_grad(b, m):
        gp[b, m] = grid(dot_nn(act_t[b, 3], work[jnp.where(m == 4, 0, 2)]))

    def first_grads(b):
        gp[b, 0, :, :, :, :, :, 0:128] = grid(dot_nn(in_t[b], work[0]).T)
        gp[b, 0, :, :, :, :, :, 128:256] = grid(bias_sum[...].T)
        pl.when(b == 0)(backcast_grad)

    def backcast_grad():
        gp[0, 0, :, :, :, :, :, 256:384] = grid(dot_nn(e_t[0], theta_keep[...]).T)

    def input_grad(b):
        for t in range(2):
            at = slice(t * windows // 2, (t + 1) * windows // 2)
            keep = mask[at, :].astype(F32)
            dr = resid[at, :] * keep + 2.0 * dot_nn(work[0, at, :], small(b, 0))

            @pl.when(b == 1)
            def _():
                seg[at, :] = dr[:, 0:past]
                resid[at, :] = dr.astype(BF).astype(F32)

            @pl.when(b == 0)
            def _():
                put_rows(sens, 0, at, (dr * keep).T[0:past])

    def late_rows():
        for g in range(windows // 128):
            at = slice(g * 128, (g + 1) * 128)
            pad[:, 0:past] = seg[at, :]
            put_rows(sens, 1, at, pad[...].T[0:past])

    bias_sum[...] = jnp.zeros_like(bias_sum)
    squares[...] = jnp.zeros_like(squares)
    total[...] = jnp.zeros_like(total)

    def back_step(j, carry):
        b, m = back_of(j)

        staged(6, j, scatter_plane)
        staged(4, j, scatter_diag)
        staged(2, j, scatter_core)

        @pl.when(j == 2)
        def _():
            arrived(9)
            arrived(10)
            theta_step(1)
            scatter_core(1)

        pl.when(jnp.logical_and(m >= 1, m <= 3))(lambda: layer_back(b, m))

        @pl.when(jnp.logical_or(j == 6, j == count - 1))
        def _():
            block = jnp.where(j == 6, 1, 0)
            first_grads(block)
            pl.when(j == 6)(lambda: input_grad(1))

        @pl.when(j == 6)
        def _():
            feed(0)
            theta_grad(0, 4)

        @pl.when(jnp.logical_or(j == 10, j == 11))
        def _():
            lax.fori_loop(jnp.where(j == 10, 4, 5), MATS, lambda n, carry: (late_theta(b, n), carry)[1], 0)

        pl.when(jnp.logical_and(j >= 3, j < count))(lambda: scatter_start(j))

        @pl.when(j == 6)
        def _():
            arrived(11)
            theta_step(0)

        return carry

    def last_steps():
        scatter_plane(6), scatter_diag(8), scatter_core(10)
        input_grad(0)
        forecasts()
        start_all(out_copies(pred, pred_out, 0))
        scatter_plane(7), scatter_diag(9), scatter_core(11)
        late_rows()
        start_all(out_copies(sens, sens_out, 1))
        scatter_z(0), scatter_z(1)
        scatter_plane(8), scatter_diag(10)
        scatter_z(2), scatter_z(3), scatter_z(4)
        scatter_plane(9), scatter_diag(11)
        scatter_plane(10)
        scatter_z(5), scatter_z(6)
        scatter_plane(11)
        for j in range(7, count):
            scatter_z(j)

    gather_line(0)
    hand_over(0, slice(0, 384)).start()
    for m in range(1, MATS):
        pack(m)
        if m < 4:
            gather_line(m)
        hand_over(m, slice(0, hidden)).start()
    lax.fori_loop(0, count + 4, gather_step, 0)

    lax.fori_loop(2, count, back_step, 0)
    last_steps()

    grad_copy = remote(total.at[other], grad_out.at[:, core], out_send.at[2], out_recv.at[2], sibling)
    grad_copy.start()
    grad_out[:, core] = total[core]
    sq = squares[:, 0:128] + squares[:, 128:256] + squares[:, 256:384] + squares[:, 384:512]
    place = (y * XN + x) * 2 + core
    norm_buf[place] = sq[0:8] + sq[8:16]

    def spread(sources, targets, first):
        copies = [
            remote(norm_buf.at[sources], norm_buf.at[sources], norm_send.at[first + s], norm_recv.at[first + s], device)
            for s, device in enumerate(targets)
        ]
        start_all(copies)
        for copy in copies:
            copy.wait()

    def add_up(slots):
        value = norm_buf[slots[0]]
        for slot in slots[1:]:
            value = value + norm_buf[slot]
        return value

    spread(place, plane_peers, 0)
    norm_buf[8 + z] = add_up(range(8))
    spread(8 + z, [chip(zi, y, x) for zi in z_peers], 7)
    everything = add_up(range(8, 8 + ZN))
    norm_out[...] = jnp.broadcast_to(jnp.sqrt(jnp.sum(everything, keepdims=True)), norm_out.shape)

    grad_copy.wait()
    for buf, out, s in ((pred, pred_out, 0), (sens, sens_out, 1)):
        for copy in out_copies(buf, out, s):
            copy.wait()
    for m in range(MATS):
        hand_over(m, slice(0, hidden if m else 384)).wait_send()

    for mats, lanes in ((slice(1, MATS), slice(0, hidden)), (slice(0, 1), slice(0, 384))):
        sent = (
            wg.at[:, mats, 0 : ZN - 1, 0, 0, 0, :, lanes],
            wg.at[:, mats, :, :, 0, 0, :, lanes],
            wg.at[:, mats, :, 0, 0, 0, :, lanes],
            wg.at[:, mats, :, :, :, 0, :, lanes],
        )
        for sems in (ag_send, rs_send):
            for kind, ref in enumerate(sent):
                remote(ref, ref, sends(sems, kind, lanes), out_recv.at[0], sibling).wait_send()


def train_call(plane, segments, extents, adjoint, first, square, head, biases):
    ZN, YN, XN = plane
    past, span, hidden = segments.shape[1], adjoint.shape[0], square.shape[3]
    windows = segments.shape[0] // 2
    tile = windows
    half = hidden // (ZN * YN * XN) // 2
    sizes = (ZN, YN, XN, windows, tile, past, span, hidden)
    DMA = pltpu.SemaphoreType.DMA
    vmem = pl.BlockSpec(memory_space=pltpu.VMEM)
    hbm = pl.BlockSpec(memory_space=pl.ANY)
    count = 2 * MATS
    flops = 2 * 2 * 3 * windows * hidden * (6 * hidden + 2 * 128)
    lengths = extents.reshape(-1, 128)
    return pl.pallas_call(
        functools.partial(train_kernel, sizes),
        out_shape=(
            jax.ShapeDtypeStruct((span, 1, 2 * windows), F32),
            jax.ShapeDtypeStruct((past, 1, 2 * windows), F32),
            jax.ShapeDtypeStruct((MATS, 2, half, hidden), F32),
            jax.ShapeDtypeStruct((8, 128), F32),
        ),
        in_specs=[hbm] * 7,
        out_specs=(hbm, hbm, vmem, vmem),
        scratch_shapes=[
            pltpu.VMEM((2, MATS, ZN, YN, XN, 2, half, hidden), BF),
            pltpu.VMEM((MATS, half, hidden), BF),
            pltpu.VMEM((2, MATS, ZN, YN, XN, 2, half, hidden), BF),
            pltpu.VMEM((CORE_SLOTS, ZN, YN, XN, half, hidden), BF),
            pltpu.VMEM((DIAG_SLOTS, ZN, half, hidden), BF),
            pltpu.VMEM((PLAIN_SLOTS, ZN, half, hidden), BF),
            pltpu.VMEM((PAIR_SLOTS, ZN, half, hidden), BF),
            pltpu.VMEM((count, ZN - 1, half, hidden), BF),
            pltpu.VMEM((2, MATS, half, hidden), F32),
            pltpu.VMEM((2, 4, hidden, windows), BF),
            pltpu.VMEM((2, 128, windows), BF),
            pltpu.VMEM((windows, hidden), BF),
            pltpu.VMEM((2, 4, windows, hidden), BF),
            pltpu.VMEM((3, windows, hidden), BF),
            pltpu.VMEM((windows, 128), F32),
            pltpu.VMEM((windows, 128), BF),
            pltpu.VMEM((windows, 128), BF),
            pltpu.VMEM((2, 128, windows), BF),
            pltpu.VMEM((128, hidden), F32),
            pltpu.VMEM((128, hidden), F32),
            pltpu.VMEM((128, 128), F32),
            pltpu.VMEM((windows, past), F32),
            pltpu.VMEM((span, windows), F32),
            *(pltpu.VMEM(a.shape, a.dtype) for a in (lengths, first, square, head, biases)),
            pltpu.VMEM((2, span, windows), F32),
            pltpu.VMEM((2, span, 1, windows), F32),
            pltpu.VMEM((2, past, 1, windows), F32),
            pltpu.VMEM((half, hidden), F32),
            pltpu.VMEM((8 + ZN, 8, 128), F32),
            DMA((MATS,)),
            DMA((MATS,)),
            DMA((4, 2)),
            DMA((count, 4 + ZN - 1)),
            DMA((4, 2)),
            DMA((count, 4 + ZN - 1)),
            DMA((3,)),
            DMA((3,)),
            DMA((9,)),
            DMA((7 + ZN - 1,)),
            DMA((7 + ZN - 1,)),
        ],
        compiler_params=pltpu.CompilerParams(
            collective_id=0, has_side_effects=True, vmem_limit_bytes=64 * 1024 * 1024
        ),
        cost_estimate=pl.CostEstimate(flops=flops, bytes_accessed=8_000_000, transcendentals=8 * windows * hidden),
        name="train",
    )(segments, adjoint, lengths, first, square, head, biases)


def update_kernel(past, span, *refs):
    sources, targets, norm_out = refs[0:16], refs[16:34], refs[34]
    held, results, pad, in_sem, out_sem = refs[35:51], refs[51:67], *refs[67:70]
    arriving = [pltpu.make_async_copy(source, ref, in_sem.at[n]) for n, (source, ref) in enumerate(zip(sources, held))]
    leaving = [
        pltpu.make_async_copy(ref, target, out_sem.at[n]) for n, (ref, target) in enumerate(zip(held[0:2] + results, targets))
    ]
    for copy in arriving:
        copy.start()
    grads, norm, masters, momenta, variances = held[2], held[3], held[4:8], held[8:12], held[12:16]
    units = masters[3].shape[2]

    def rows(m, lane, width):
        return grads[m, :, :, lane : lane + width].reshape(units, width)

    arriving[2].wait()
    arriving[3].wait()
    norm_out[...] = norm[0:1, 0:1]
    factor = 1.0 / jnp.maximum(norm[0:1, 0:1], 1.0)
    for m in range(5):
        results[1][0, m] = rows(m + 1, 0, grads.shape[3])
    results[0][0] = rows(0, 0, 128)[:, 0:past]
    forecast = rows(0, 128, 128)
    pad[...] = jnp.zeros_like(pad)
    pad[0:units, :] = forecast
    results[3][0] = pad[...].T[span : span + 4, 0:units]
    results[2][0, :, 0:past] = rows(0, 256, 128)[:, 0:past]
    results[2][0, :, past : past + span] = forecast[:, 0:span]
    for n in (0, 1):
        arriving[n].wait()
        leaving[n].start()
    for n in (1, 0, 2, 3):
        leaving[2 + n].start()
        for state in range(3):
            arriving[4 + 4 * state + n].wait()
        updated = adamw(masters[n][...], results[n][...], momenta[n][...], variances[n][...], factor[None])
        for kind, value in enumerate(updated):
            results[4 * (kind + 1) + n][...] = value
            leaving[2 + 4 * (kind + 1) + n].start()
    for copy in leaving:
        copy.wait()


def update_call(prediction, sensitivity, grads, norm, state):
    hbm = pl.BlockSpec(memory_space=pl.ANY)
    sources = (prediction, sensitivity, grads, norm, *state)
    targets = (prediction, sensitivity, *(4 * list(state[:4])))
    return pl.pallas_call(
        functools.partial(update_kernel, sensitivity.shape[0], prediction.shape[0]),
        out_shape=tuple(jax.ShapeDtypeStruct(a.shape, F32) for a in targets) + (jax.ShapeDtypeStruct((1, 1), F32),),
        in_specs=[hbm] * len(sources),
        out_specs=tuple([hbm] * len(targets) + [pl.BlockSpec(memory_space=pltpu.VMEM)]),
        scratch_shapes=[pltpu.VMEM(a.shape, F32) for a in sources]
        + [pltpu.VMEM(a.shape, F32) for a in targets[2:]]
        + [pltpu.VMEM((128, 128), F32), pltpu.SemaphoreType.DMA((len(sources),)), pltpu.SemaphoreType.DMA((len(targets),))],
        name="update",
    )(*sources)


def turned(arrays):
    return [a.transpose(0, 2, 1) if n % 4 == 0 else a for n, a in enumerate(arrays)]


def kernel_shards(plane, segments, extents, adjoint, *state):
    state = turned(state)
    results = train_call(plane, segments, extents, adjoint.T, *state[:4])
    prediction, sensitivity, *updated, norm = update_call(*results, state)
    by_window = (prediction.transpose(1, 2, 0), sensitivity.transpose(1, 2, 0))
    return (*by_window, norm.reshape(()), *turned(updated))


STATE_SPECS = (
    P("section", None, "dp"),
    P("section", None, "dp", None),
    P("section", "dp", None),
    P("section", None, "dp"),
)


def solution(mesh):
    in_specs = (P("dp", None), P("dp"), P("dp", None)) + 3 * STATE_SPECS
    out_specs = (P("section", "dp", None), P("section", "dp", None), P()) + 4 * STATE_SPECS
    plane = PLANES.get(mesh.shape["dp"])
    shards = plain_shards if plane is None else functools.partial(kernel_shards, plane)
    return jax.shard_map(shards, mesh=mesh, in_specs=in_specs, out_specs=out_specs, check_vma=False)
```

```python
import functools

import jax
import jax.numpy as jnp
from jax import lax
from jax.experimental import pallas as pl
from jax.experimental.pallas import tpu as pltpu
from jax.sharding import PartitionSpec as P

STEP = 10


def dot_nn(a, b):
    return jnp.dot(a, b, preferred_element_type=jnp.float32)


def dot_tn(a, b):
    return lax.dot_general(a, b, (((0,), (0,)), ((), ())), preferred_element_type=jnp.float32)


def dot_nt(a, b):
    return lax.dot_general(a, b, (((1,), (1,)), ((), ())), preferred_element_type=jnp.float32)


def unit_rows(first, square, head, biases):
    units = first.shape[1]
    return jnp.concatenate(
        [square.transpose(1, 0, 2).reshape(units, -1), first.T, head, biases.T], axis=1
    )


def from_unit_rows(rows, past, hidden, out):
    wide = 5 * hidden
    square = rows[:, :wide].reshape(-1, 5, hidden).transpose(1, 0, 2)
    first = rows[:, wide : wide + past].T
    head = rows[:, wide + past : wide + past + out]
    biases = rows[:, wide + past + out :].T
    return first, square, head, biases


def plain_forward(weights, resid):
    first, square, head, biases = weights
    past = resid.shape[1]
    acts, slopes = [resid.astype(jnp.bfloat16)], []
    for k in range(4):
        z = dot_nn(acts[-1], first if k == 0 else square[k - 1]) + biases[k].astype(jnp.float32)
        sig = jax.nn.sigmoid(z)
        acts.append((z * sig).astype(jnp.bfloat16))
        slopes.append(sig * (1.0 + z * (1.0 - sig)))
    theta_b = dot_nn(acts[4], square[3]).astype(jnp.bfloat16)
    theta_f = dot_nn(acts[4], square[4]).astype(jnp.bfloat16)
    backcast = dot_nn(theta_b, head[:, :past])
    part = dot_nn(theta_f, head[:, past:])
    return backcast, part, (acts, slopes, theta_b, theta_f)


def plain_backward(weights, saved, e, f):
    first, square, head, biases = weights
    acts, slopes, theta_b, theta_f = saved
    past = e.shape[1]
    head_grad = jnp.concatenate([dot_tn(theta_b, e), dot_tn(theta_f, f)], axis=1)
    u_b = dot_nt(e, head[:, :past]).astype(jnp.bfloat16)
    u_f = dot_nt(f, head[:, past:]).astype(jnp.bfloat16)
    squares = [None, None, None, dot_tn(acts[4], u_b), dot_tn(acts[4], u_f)]
    da = dot_nt(u_b, square[3]) + dot_nt(u_f, square[4])
    bias_grads = [None] * 4
    first_grad = None
    for k in (3, 2, 1, 0):
        dz = (da * slopes[k]).astype(jnp.bfloat16)
        bias_grads[k] = jnp.sum(dz, axis=0, dtype=jnp.float32)
        grad = dot_tn(acts[k], dz)
        if k == 0:
            first_grad = grad
        else:
            squares[k - 1] = grad
        da = dot_nt(dz, first if k == 0 else square[k - 1])
    return da, (first_grad, jnp.stack(squares), head_grad, jnp.stack(bias_grads))


def adamw(master, gradient, momentum, variance, factor):
    clipped = gradient * factor
    moment_new = 0.9 * momentum + 0.1 * clipped
    variance_new = 0.999 * variance + 0.001 * clipped * clipped
    ratio = moment_new / (1.0 - 0.9**STEP) / (jnp.sqrt(variance_new / (1.0 - 0.999**STEP)) + 1e-08)
    return master - 0.05 * (ratio + 0.01 * master), moment_new, variance_new


def plain_shards(segments, extents, adjoint, *state):
    masters, momenta, variances = state[:4], state[4:8], state[8:]
    core = lax.axis_index("section")
    past, span = segments.shape[1], adjoint.shape[1]
    windows = segments.shape[0] // 2
    hidden = masters[1].shape[3]
    mine = [
        lax.dynamic_slice_in_dim(v, core * windows, windows, 0) for v in (segments, extents, adjoint)
    ]
    seg, ext, adj = mine
    rows = unit_rows(*(m[0].astype(jnp.bfloat16) for m in masters))
    rows = lax.all_gather(rows, "dp", axis=0, tiled=True)
    rows = lax.all_gather(rows, "section", axis=0)
    blocks = [from_unit_rows(rows[b], past, hidden, past + span) for b in range(2)]
    mask = (
        lax.broadcasted_iota(jnp.int32, (windows, past), 1) >= past - ext[:, None]
    ).astype(jnp.float32)
    r0 = seg * mask
    backcast, part0, saved0 = plain_forward(blocks[0], r0)
    r1 = (r0 - backcast) * mask
    _, part1, saved1 = plain_forward(blocks[1], r1)
    forecast = part0.astype(jnp.bfloat16).astype(jnp.float32) + part1
    f = adj.astype(jnp.bfloat16)
    zero = jnp.zeros_like(r0)
    da1, grads1 = plain_backward(blocks[1], saved1, (-(zero * mask)).astype(jnp.bfloat16), f)
    dr1 = zero * mask + da1
    t = dr1.astype(jnp.bfloat16).astype(jnp.float32)
    da0, grads0 = plain_backward(blocks[0], saved0, (-(t * mask)).astype(jnp.bfloat16), f)
    dr0 = (t * mask + da0) * mask

    def by_section(first_block, second_block):
        mine, other = (
            jnp.where(core == 0, first_block, second_block),
            jnp.where(core == 0, second_block, first_block),
        )
        got = lax.ppermute(other, "section", [(0, 1), (1, 0)])
        return jnp.where(
            core == 0, jnp.concatenate([mine, got]), jnp.concatenate([got, mine])
        )[None]

    prediction = by_section(part0, forecast)
    sensitivity = by_section(dr0, dr1)
    packed = jnp.stack([unit_rows(*grads0), unit_rows(*grads1)])
    packed = lax.psum_scatter(packed, "section", scatter_dimension=0, tiled=False)
    packed = lax.psum_scatter(packed, "dp", scatter_dimension=0, tiled=True)
    norm = jnp.sqrt(lax.psum(jnp.sum(packed * packed), ("section", "dp")))
    factor = 1.0 / jnp.maximum(norm, 1.0)
    summed = [g[None] for g in from_unit_rows(packed, past, hidden, past + span)]
    updated = [adamw(*four, factor) for four in zip(masters, summed, momenta, variances)]
    return (
        prediction,
        sensitivity,
        norm,
        *summed,
        *(u[0] for u in updated),
        *(u[1] for u in updated),
        *(u[2] for u in updated),
    )


PLANES = {16: (4, 2, 2)}
MESH = pl.DeviceIdType.MESH
MATS = 6
CORE_SLOTS = 6
BF, F32 = jnp.bfloat16, jnp.float32
GATHER = ((0, 0), (0, 1), (0, 2), (0, 3), (0, 4), (1, 0), (1, 1), (1, 2), (1, 3), (1, 4), (1, 5), (0, 5))
STEPS = (
    (0, 0, 0, 0, 0, 1, 1, 1, 1, 1, 3, 1),
    (1, 1, 2, 3, 4, 4, 5, 7, 8, 11, 9, 13),
    (3, 3, 3, 5, 7, 8, 8, 9, 11, 13, 12, 17),
    (4, 4, 6, 8, 9, 10, 11, 12, 13, 16, 16, 21),
    (14, 19, 20, 22, 23, 23, 25, 26, 27, 28, 29, 31),
    (21, 21, 22, 24, 24, 25, 27, 28, 29, 30, 36, 37),
    (23, 25, 24, 26, 28, 27, 29, 30, 35, 37, 40, 41),
    (42, 44, 40, 43, 44, 44, 44, 41, 41, 44, 44, 44),
)
FIRST, LAST = 6, 30
ORDER = ((0, 5), (1, 4), (1, 5), (1, 3), (1, 2), (1, 1), (0, 4), (0, 3), (0, 2), (0, 1), (1, 0), (0, 0))


def remote(src, dst, send_sem, recv_sem, device):
    return pltpu.make_async_remote_copy(
        src_ref=src, dst_ref=dst, send_sem=send_sem, recv_sem=recv_sem, device_id=device, device_id_type=MESH
    )


def train_kernel(
    sizes,
    seg_hbm, adj_hbm, ext_hbm, first_hbm, square_hbm, head_hbm, biases_hbm,
    pred_out, sens_out, grad_out, norm_out,
    wg, handed, gp, from_core, from_diag, from_plain, from_pair, from_z, total,
    act_t, in_t, theta_keep, slope, work, resid, mask, f_ref, e_t, bias_t, bias_sum, pad,
    seg, adj, ext, first, square, head, biases, part_t, pred, sens, squares, norm_buf,
    own_send, own_recv, ag_send, ag_recv, rs_send, rs_recv, out_send, out_recv, local_sem, norm_send, norm_recv,
):
    ZN, YN, XN, windows, tile, past, span, hidden = sizes
    units = ZN * YN * XN
    core, dp = lax.axis_index("section"), lax.axis_index("dp")
    x, y, z = lax.rem(dp, XN), lax.rem(lax.div(dp, XN), YN), lax.div(dp, XN * YN)
    other, xo, yo = 1 - core, 1 - x, 1 - y
    near_y, near_x = y + core * (yo - y), xo + core * (x - xo)
    far_y, far_x = yo + core * (y - yo), x + core * (xo - x)

    def chip(zi, yi, xi):
        return (core, (zi * YN + yi) * XN + xi)

    sibling = (other, dp)
    z_peers = [lax.rem(z + step, ZN) for step in range(1, ZN)]

    row0 = core * windows
    loads = [
        pltpu.make_async_copy(seg_hbm.at[pl.ds(row0, windows), :], seg, local_sem.at[0]),
        pltpu.make_async_copy(adj_hbm.at[:, pl.ds(row0, windows)], adj, local_sem.at[1]),
    ]
    small_loads = [
        pltpu.make_async_copy(source, target, local_sem.at[4 + n])
        for n, (source, target) in enumerate(
            [(square_hbm, square), (first_hbm, first), (head_hbm, head), (biases_hbm, biases), (ext_hbm, ext)]
        )
    ]
    for load in small_loads + loads:
        load.start()

    barrier = pltpu.get_barrier_semaphore()
    plane_peers = [
        (ci, (z * YN + yi) * XN + xi) for ci in (core, other) for yi in (y, yo) for xi in (x, xo)
    ][1:]
    peers = plane_peers + [(ci, (zi * YN + y) * XN + x) for zi in z_peers for ci in (core, other)]
    for peer in peers:
        pl.semaphore_signal(barrier, inc=1, device_id=peer, device_id_type=MESH)

    rows = hidden // units
    half_rows = rows // 2

    def put_own(m, value, lanes):
        halves = value.astype(BF).reshape(2, half_rows, -1)
        for h in range(2):
            pl.when(core == h)(functools.partial(put_half, m, halves[h], halves[1 - h], lanes))

    def put_half(m, kept, given, lanes):
        wg[core, m, z, y, x, core, :, lanes] = kept
        handed[m, :, lanes] = given

    for load in small_loads:
        load.wait()
    pad[...] = jnp.zeros_like(pad)
    pad[0:rows, 0:past] = first[0] * 0.5
    put_own(0, pad[0:rows, :], slice(0, 128))
    pad[...] = jnp.zeros_like(pad)
    pad[span : span + 4, 0:rows] = biases[0] * 0.5
    bias_cols = pad[...].T[0:rows]
    pad[...] = jnp.zeros_like(pad)
    pad[0:rows, 0:span] = head[0, :, past : past + span]
    put_own(0, pad[0:rows, :] + bias_cols, slice(128, 256))
    pad[...] = jnp.zeros_like(pad)
    pad[0:rows, 0:past] = head[0, :, 0:past]
    put_own(0, pad[0:rows, :], slice(256, 384))
    pl.semaphore_wait(barrier, len(peers))

    def hand_over(m, lanes):
        return remote(
            handed.at[m, :, lanes], wg.at[core, m, z, y, x, other, :, lanes], own_send.at[m], own_recv.at[m], sibling
        )

    def pack(m):
        put_own(m, square[0, m - 1] * 0.5 if m < 4 else square[0, m - 1], slice(0, hidden))


    def of(i):
        if isinstance(i, int):
            return GATHER[i]
        b = jnp.where(jnp.logical_and(i >= 5, i <= 10), 1, 0)
        return b, jnp.where(i <= 4, i, jnp.where(i <= 10, i - 5, 5))

    def sends(sems, kind, lanes):
        return sems.at[kind, 0 if lanes.stop == hidden else 1]

    def z_copies(i, lanes):
        b, m = of(i)
        part = wg.at[b, m, z, y, x, core, :, lanes]
        return [
            remote(part, part, sends(ag_send, 0, lanes), ag_recv.at[i, s], chip(zi, y, x)) for s, zi in enumerate(z_peers)
        ]

    def line_copies(i, lanes):
        b, m = of(i)
        given = wg.at[b, m, z, y, x, other, :, lanes]
        return [
            remote(
                handed.at[m, :, lanes], given, sends(ag_send, 0, lanes), ag_recv.at[i, s], (other, (zi * YN + y) * XN + x)
            )
            for s, zi in enumerate(z_peers)
        ]

    def column_copies(i, lanes):
        b, m = of(i)
        part = wg.at[b, m, :, y, x, core, :, lanes]
        return [
            remote(part, part, sends(ag_send, 1, lanes), ag_recv.at[i, 3], chip(z, near_y, near_x)),
            remote(part, part, sends(ag_send, 1, lanes), ag_recv.at[i, 4], chip(z, far_y, far_x)),
        ]

    def corner_copy(i, lanes):
        b, m = of(i)
        part = wg.at[b, m, :, near_y, near_x, core, :, lanes]
        return remote(part, part, sends(ag_send, 2, lanes), ag_recv.at[i, 5], chip(z, far_y, far_x))

    def core_copy(i, lanes):
        b, m = of(i)
        part = wg.at[b, m, :, :, :, core, :, lanes]
        return remote(part, part, sends(ag_send, 3, lanes), ag_recv.at[i, 6], sibling)

    def by_lanes(m, step):
        if isinstance(m, int):
            step(slice(0, hidden if m else 384))
            return
        pl.when(m == 0)(lambda: step(slice(0, 384)))
        pl.when(m > 0)(lambda: step(slice(0, hidden)))

    def start_all(copies):
        for copy in copies:
            copy.start()

    zeros_tile = jnp.zeros((tile, 128), F32)

    def prepare(t, carry):
        at = pl.ds(t * tile, tile)
        resid[at, :] = zeros_tile
        resid[at, 0:past] = seg[at, :]
        return carry

    def prepare_mask(g, carry):
        lengths = ext[pl.ds(core * (windows // 128) + g, 1), :]
        position = lax.broadcasted_iota(jnp.int32, (128, 128), 0)
        keep = jnp.where(position >= past - lengths, 1.0, 0.0).astype(F32).T
        at = pl.ds(pl.multiple_of(g * 128, 128), 128)
        pad[0:span, :] = adj[:, at]
        f_ref[at, :] = pad[...].T.astype(BF)
        mask[at, :] = keep.astype(BF)
        resid[at, :] = resid[at, :] * keep
        return carry

    tiles = windows // tile
    part_tile = windows // 2

    def prepare_all():
        for load in loads:
            load.wait()
        lax.fori_loop(0, tiles, prepare, 0)
        pad[...] = jnp.zeros_like(pad)
        lax.fori_loop(0, windows // 128, prepare_mask, 0)

    def matrix(b, m):
        return wg[b, m].reshape(hidden, hidden)

    def small(b, lane):
        return wg[b, 0, :, :, :, :, :, lane : lane + 128].reshape(hidden, 128)

    def store_layer(b, k, at, v):
        p = 1.0 + jnp.tanh(v)
        a = v * p
        rate = p + a * (2.0 - p)
        slope[b, k, at, :] = rate.astype(BF)
        low = a.astype(BF)
        act_t[b, k, :, at] = low.T
        return low

    def halves(body):
        for t in range(2):
            body(slice(t * windows // 2, (t + 1) * windows // 2))

    def layer_zero(b):
        bias_t[...] = small(b, 128).astype(F32).T

        def body(at):
            a = resid[at, :].astype(BF)
            in_t[b, :, at] = a.T
            work[0, at, :] = store_layer(b, 0, at, dot_nt(a, small(b, 0)) + bias_t[span : span + 1, :])

        halves(body)

    def layer_next(b, k):
        source, target = lax.rem(k + 1, 2), lax.rem(k, 2)
        v = dot_nn(work[source], matrix(b, k)) + bias_t[pl.ds(span + k, 1), :]
        work[target] = store_layer(b, k, slice(0, windows), v)

    def grid(value):
        return value.astype(BF).reshape(ZN, YN, XN, 2, half_rows, -1)

    def backcast_step():
        def body(at):
            theta = dot_nn(work[1, at, :], matrix(0, 4)).astype(BF)
            theta_keep[at, :] = theta
            resid[at, :] = (resid[at, :] - dot_nn(theta, small(0, 256))) * mask[at, :].astype(F32)

        halves(body)

    def put_rows(buf, b, at, value):
        for row in range(value.shape[0]):
            buf[b, row, :, at] = value[row : row + 1]

    def late_theta(b, m):
        theta_t = act_t.at[1, 0]
        theta_t[...] = dot_nn(matrix(b, m).T, act_t[b, 3]).astype(BF)

        @pl.when(m == 4)
        def _():
            gp[b, 0, :, :, :, :, :, 256:384] = grid(dot_nt(theta_t[...], e_t[b]))

        @pl.when(m == 5)
        def _():
            grad = grid(dot_nn(theta_t[...], f_ref[...]))
            gp[b, 0, :, :, :, :, :, 128:256] = gp[b, 0, :, :, :, :, :, 128:256] + grad
            part_t[b] = dot_nn(small(b, 128).T, theta_t[...])[0:span]

    def forecasts():
        put_rows(pred, 0, slice(0, windows), part_t[0])
        put_rows(pred, 1, slice(0, windows), part_t[0].astype(BF).astype(F32) + part_t[1])

    count = 2 * MATS

    def gather_line(i):
        b, m = of(i)

        pl.when(b == core)(lambda: by_lanes(m, lambda lanes: start_all(line_copies(i, lanes) + z_copies(i, lanes))))

    def gather_columns(i):
        b, m = of(i)

        def step(lanes):
            pl.when(b != core)(lambda: hand_over(m, lanes).wait_recv())
            for copy in z_copies(i, lanes):
                copy.wait_recv()
            start_all(column_copies(i, lanes))

        by_lanes(m, step)

    def gather_corner(i):
        def step(lanes):
            column_copies(i, lanes)[0].wait_recv()
            corner_copy(i, lanes).start()

        by_lanes(of(i)[1], step)

    def gather_core(i):
        def step(lanes):
            column_copies(i, lanes)[1].wait_recv()
            corner_copy(i, lanes).wait_recv()
            core_copy(i, lanes).start()

        by_lanes(of(i)[1], step)

    def arrived(i):
        by_lanes(of(i)[1], lambda lanes: core_copy(i, lanes).wait_recv())

    def forward_unit(i):
        arrived(i)
        b, m = of(i)
        pl.when(m == 0)(lambda: layer_zero(b))
        pl.when(jnp.logical_and(m >= 1, m <= 3))(lambda: layer_next(b, m))
        pl.when(m == 4)(backcast_step)

    def out_copies(buf, out, s):
        at = pl.ds(row0, windows)
        return [
            pltpu.make_async_copy(buf.at[core], out.at[:, :, at], local_sem.at[2 + s]),
            remote(buf.at[other], out.at[:, :, at], out_send.at[s], out_recv.at[s], sibling),
        ]


    def back_of(j):
        if isinstance(j, int):
            return ORDER[j]
        b = jnp.where(jnp.logical_or(jnp.logical_and(j >= 1, j <= 5), j == 10), 1, 0)
        early = jnp.where(j == 1, 4, jnp.where(j <= 2, 5, 6 - j))
        return b, jnp.where(j <= 5, early, jnp.where(j == 6, 4, jnp.where(j <= 9, 10 - j, 0)))

    def to_core(j, lanes):
        b, m = back_of(j)
        return remote(
            gp.at[b, m, :, :, :, other, :, lanes], from_core.at[lax.rem(j, CORE_SLOTS), :, :, :, :, lanes],
            sends(rs_send, 3, lanes), rs_recv.at[j, 0], sibling,
        )

    def to_far(j, lanes):
        b, m = back_of(j)
        device = chip(z, far_y, far_x)
        return [
            remote(
                gp.at[b, m, :, yo, xo, core, :, lanes], from_diag.at[j, :, :, lanes],
                sends(rs_send, 1, lanes), rs_recv.at[j, 1], device,
            ),
            remote(
                gp.at[b, m, :, far_y, far_x, core, :, lanes], from_plain.at[j, :, :, lanes],
                sends(rs_send, 1, lanes), rs_recv.at[j, 2], device,
            ),
        ]

    def to_near(j, lanes):
        b, m = back_of(j)
        return remote(
            gp.at[b, m, :, near_y, near_x, core, :, lanes], from_pair.at[j, :, :, lanes],
            sends(rs_send, 2, lanes), rs_recv.at[j, 3], chip(z, near_y, near_x),
        )

    def to_z(j, lanes):
        b, m = back_of(j)
        return [
            remote(
                gp.at[b, m, zi, y, x, core, :, lanes], from_z.at[j, s, :, lanes],
                sends(rs_send, 0, lanes), rs_recv.at[j, 4 + s], chip(zi, y, x),
            )
            for s, zi in enumerate(z_peers)
        ]

    def scatter_start(j):
        by_lanes(back_of(j)[1], lambda lanes: to_core(j, lanes).start())

    def scatter_core(j):
        b, m = back_of(j)

        def step(lanes):
            to_core(j, lanes).wait_recv()
            part = gp[b, m, :, :, :, core, :, lanes] + from_core[lax.rem(j, CORE_SLOTS), :, :, :, :, lanes]
            gp[b, m, :, :, :, core, :, lanes] = part
            start_all(to_far(j, lanes))

        by_lanes(m, step)

    def scatter_diag(j):
        b, m = back_of(j)

        def step(lanes):
            to_far(j, lanes)[0].wait_recv()
            part = gp[b, m, :, near_y, near_x, core, :, lanes] + from_diag[j, :, :, lanes]
            gp[b, m, :, near_y, near_x, core, :, lanes] = part
            to_near(j, lanes).start()

        by_lanes(m, step)

    def scatter_plane(j):
        b, m = back_of(j)

        def step(lanes):
            to_far(j, lanes)[1].wait_recv()
            to_near(j, lanes).wait_recv()
            value = gp[b, m, :, y, x, core, :, lanes].astype(F32)
            value = value + from_plain[j, :, :, lanes].astype(F32)
            value = value + from_pair[j, :, :, lanes].astype(F32)
            gp[b, m, :, y, x, core, :, lanes] = value.astype(BF)
            start_all(to_z(j, lanes))

        by_lanes(m, step)

    def scatter_z(j):
        b, m = back_of(j)

        def step(lanes):
            for copy in to_z(j, lanes):
                copy.wait_recv()
            value = gp[b, m, z, y, x, core, :, lanes].astype(F32)
            for s in range(ZN - 1):
                value = value + from_z[j, s, :, lanes].astype(F32)
            total[b, m, :, lanes] = value
            squares[:, lanes] = squares[:, lanes] + value * value

        by_lanes(m, step)

    def add_rows(value):
        return jnp.sum(value.reshape(-1, 8, hidden), axis=0)

    def put_bias(k, acc):
        bias_sum[pl.ds(span + k, 1), :] = jnp.sum(acc, axis=0, keepdims=True)

    def feed(b):
        pl.when(b == 1)(lambda: resid.__setitem__(..., jnp.zeros_like(resid)))
        e = (-(resid[...] * mask[...].astype(F32))).astype(BF)
        e_t[b] = e.T
        work[0] = dot_nt(e, small(b, 256)).astype(BF)
        work[2] = dot_nt(f_ref[...], small(b, 128)).astype(BF)

    def feed_forward(b):
        work[2] = dot_nt(f_ref[...], small(b, 128)).astype(BF)

    def put_dz(b, k, da):
        dz = da * slope[b, k].astype(F32)
        work[k % 2 if isinstance(k, int) else lax.rem(k, 2)] = dz.astype(BF)
        bias_sum[pl.ds(span + k, 1), :] = jnp.sum(add_rows(dz), axis=0, keepdims=True)

    def theta_step(b):
        put_dz(b, 3, 0.5 * (dot_nt(work[0], matrix(b, 4)) + dot_nt(work[2], matrix(b, 5))))

    def layer_back(b, k):
        source = lax.rem(k, 2)
        gp[b, k] = grid(dot_nn(act_t[b, k - 1], work[source]))
        put_dz(b, k - 1, dot_nt(work[source], matrix(b, k)))

    def theta_grad(b, m):
        gp[b, m] = grid(dot_nn(act_t[b, 3], work[jnp.where(m == 4, 0, 2)]))

    def first_grads(b):
        gp[b, 0, :, :, :, :, :, 0:128] = grid(dot_nn(in_t[b], work[0]).T)
        gp[b, 0, :, :, :, :, :, 128:256] = grid(bias_sum[...].T)
        pl.when(b == 0)(backcast_grad)

    def backcast_grad():
        gp[0, 0, :, :, :, :, :, 256:384] = grid(dot_nn(e_t[0], theta_keep[...]).T)

    def input_grad(b):
        for t in range(2):
            at = slice(t * windows // 2, (t + 1) * windows // 2)
            keep = mask[at, :].astype(F32)
            dr = resid[at, :] * keep + 2.0 * dot_nn(work[0, at, :], small(b, 0))

            @pl.when(b == 1)
            def _():
                seg[at, :] = dr[:, 0:past]
                resid[at, :] = dr.astype(BF).astype(F32)

            @pl.when(b == 0)
            def _():
                put_rows(sens, 0, at, (dr * keep).T[0:past])

    def late_rows():
        for g in range(windows // 128):
            at = slice(g * 128, (g + 1) * 128)
            pad[:, 0:past] = seg[at, :]
            put_rows(sens, 1, at, pad[...].T[0:past])

    bias_sum[...] = jnp.zeros_like(bias_sum)
    squares[...] = jnp.zeros_like(squares)
    total[...] = jnp.zeros_like(total)

    moves = (
        gather_line, gather_columns, gather_corner, gather_core, scatter_core, scatter_diag, scatter_plane, scatter_z
    )

    def move(place):
        for stage in range(len(moves) - 1, -1, -1):
            for unit in range(count):
                if STEPS[stage][unit] == place:
                    moves[stage](unit)

    def any_of(t, *places):
        return functools.reduce(jnp.logical_or, [t == place for place in places])

    def between(t, low, high):
        return jnp.logical_and(t >= low, t <= high)

    def product(t, carry):
        for low in range(FIRST, LAST, 6):

            @pl.when(between(t, low, low + 5))
            def _():
                for place in range(low, low + 6):
                    pl.when(t == place)(functools.partial(move, place))

        forward = jnp.logical_or(t <= 10, between(t, 12, 15))
        pl.when(forward)(lambda: forward_unit(jnp.where(t <= 10, t - 6, t - 7)))

        pl.when(t == 11)(lambda: feed_forward(0))
        pl.when(any_of(t, 16, 23))(lambda: feed(jnp.where(t == 16, 1, 0)))
        theta_block = jnp.where(between(t, 16, 17), 1, 0)
        pl.when(any_of(t, 11, 16, 17, 23))(lambda: theta_grad(theta_block, jnp.where(any_of(t, 11, 17), 5, 4)))

        early = t <= 21
        layers = jnp.logical_or(between(t, 19, 21), between(t, 24, 26))
        pl.when(layers)(lambda: layer_back(jnp.where(early, 1, 0), jnp.where(early, 22 - t, 27 - t)))
        pl.when(any_of(t, 22, 28))(lambda: first_grads(jnp.where(t == 22, 1, 0)))

        @pl.when(any_of(t, 27, 28))
        def _():
            block = jnp.where(t == 27, 1, 0)
            lax.fori_loop(5 - block, MATS, lambda n, carry: (late_theta(block, n), carry)[1], 0)

        unit = jnp.where(t == 11, 0, jnp.where(t <= 17, t - 15, jnp.where(early, t - 16, t - 17)))
        ready = functools.reduce(
            jnp.logical_or, [t == 11, between(t, 16, 17), between(t, 19, 21), between(t, 23, 28)]
        )
        pl.when(ready)(lambda: scatter_start(unit))
        pl.when(any_of(t, 22, 29))(lambda: input_grad(jnp.where(t == 22, 1, 0)))

        @pl.when(t == 18)
        def _():
            arrived(9)
            arrived(10)

        pl.when(t == 23)(lambda: arrived(11))
        pl.when(any_of(t, 18, 23))(lambda: theta_step(jnp.where(t == 18, 1, 0)))
        return carry

    gather_line(0)
    hand_over(0, slice(0, 384)).start()
    for m in range(1, MATS):
        pack(m)
        hand_over(m, slice(0, hidden)).start()
        if STEPS[0][m] == 0:
            gather_line(m)
    for place in range(1, FIRST):
        move(place)
        if place == 1:
            prepare_all()
    lax.fori_loop(FIRST, LAST, product, 0)
    forecasts()
    start_all(out_copies(pred, pred_out, 0))
    move(LAST)
    late_rows()
    start_all(out_copies(sens, sens_out, 1))
    for place in range(LAST + 1, max(map(max, STEPS)) + 1):
        move(place)

    grad_copy = remote(total.at[other], grad_out.at[:, core], out_send.at[2], out_recv.at[2], sibling)
    grad_copy.start()
    grad_out[:, core] = total[core]
    sq = squares[:, 0:128] + squares[:, 128:256] + squares[:, 256:384] + squares[:, 384:512]
    place = (y * XN + x) * 2 + core
    norm_buf[place] = sq[0:8] + sq[8:16]

    def spread(sources, targets, first):
        copies = [
            remote(norm_buf.at[sources], norm_buf.at[sources], norm_send.at[first + s], norm_recv.at[first + s], device)
            for s, device in enumerate(targets)
        ]
        start_all(copies)
        for copy in copies:
            copy.wait()

    def add_up(slots):
        value = norm_buf[slots[0]]
        for slot in slots[1:]:
            value = value + norm_buf[slot]
        return value

    spread(place, plane_peers, 0)
    norm_buf[8 + z] = add_up(range(8))
    spread(8 + z, [chip(zi, y, x) for zi in z_peers], 7)
    everything = add_up(range(8, 8 + ZN))
    norm_out[...] = jnp.broadcast_to(jnp.sqrt(jnp.sum(everything, keepdims=True)), norm_out.shape)

    grad_copy.wait()
    for buf, out, s in ((pred, pred_out, 0), (sens, sens_out, 1)):
        for copy in out_copies(buf, out, s):
            copy.wait()
    for m in range(MATS):
        hand_over(m, slice(0, hidden if m else 384)).wait_send()

    for mats, lanes in ((slice(1, MATS), slice(0, hidden)), (slice(0, 1), slice(0, 384))):
        sent = (
            wg.at[:, mats, 0 : ZN - 1, 0, 0, 0, :, lanes],
            wg.at[:, mats, :, :, 0, 0, :, lanes],
            wg.at[:, mats, :, 0, 0, 0, :, lanes],
            wg.at[:, mats, :, :, :, 0, :, lanes],
        )
        for sems in (ag_send, rs_send):
            for kind, ref in enumerate(sent):
                remote(ref, ref, sends(sems, kind, lanes), out_recv.at[0], sibling).wait_send()


def train_call(plane, segments, extents, adjoint, first, square, head, biases):
    ZN, YN, XN = plane
    past, span, hidden = segments.shape[1], adjoint.shape[0], square.shape[3]
    windows = segments.shape[0] // 2
    tile = windows
    half = hidden // (ZN * YN * XN) // 2
    sizes = (ZN, YN, XN, windows, tile, past, span, hidden)
    DMA = pltpu.SemaphoreType.DMA
    vmem = pl.BlockSpec(memory_space=pltpu.VMEM)
    hbm = pl.BlockSpec(memory_space=pl.ANY)
    count = 2 * MATS
    flops = 2 * 2 * 3 * windows * hidden * (6 * hidden + 2 * 128)
    lengths = extents.reshape(-1, 128)
    return pl.pallas_call(
        functools.partial(train_kernel, sizes),
        out_shape=(
            jax.ShapeDtypeStruct((span, 1, 2 * windows), F32),
            jax.ShapeDtypeStruct((past, 1, 2 * windows), F32),
            jax.ShapeDtypeStruct((MATS, 2, half, hidden), F32),
            jax.ShapeDtypeStruct((8, 128), F32),
        ),
        in_specs=[hbm] * 7,
        out_specs=(hbm, hbm, vmem, vmem),
        scratch_shapes=[
            pltpu.VMEM((2, MATS, ZN, YN, XN, 2, half, hidden), BF),
            pltpu.VMEM((MATS, half, hidden), BF),
            pltpu.VMEM((2, MATS, ZN, YN, XN, 2, half, hidden), BF),
            pltpu.VMEM((CORE_SLOTS, ZN, YN, XN, half, hidden), BF),
            pltpu.VMEM((count, ZN, half, hidden), BF),
            pltpu.VMEM((count, ZN, half, hidden), BF),
            pltpu.VMEM((count, ZN, half, hidden), BF),
            pltpu.VMEM((count, ZN - 1, half, hidden), BF),
            pltpu.VMEM((2, MATS, half, hidden), F32),
            pltpu.VMEM((2, 4, hidden, windows), BF),
            pltpu.VMEM((2, 128, windows), BF),
            pltpu.VMEM((windows, hidden), BF),
            pltpu.VMEM((2, 4, windows, hidden), BF),
            pltpu.VMEM((3, windows, hidden), BF),
            pltpu.VMEM((windows, 128), F32),
            pltpu.VMEM((windows, 128), BF),
            pltpu.VMEM((windows, 128), BF),
            pltpu.VMEM((2, 128, windows), BF),
            pltpu.VMEM((128, hidden), F32),
            pltpu.VMEM((128, hidden), F32),
            pltpu.VMEM((128, 128), F32),
            pltpu.VMEM((windows, past), F32),
            pltpu.VMEM((span, windows), F32),
            *(pltpu.VMEM(a.shape, a.dtype) for a in (lengths, first, square, head, biases)),
            pltpu.VMEM((2, span, windows), F32),
            pltpu.VMEM((2, span, 1, windows), F32),
            pltpu.VMEM((2, past, 1, windows), F32),
            pltpu.VMEM((half, hidden), F32),
            pltpu.VMEM((8 + ZN, 8, 128), F32),
            DMA((MATS,)),
            DMA((MATS,)),
            DMA((4, 2)),
            DMA((count, 4 + ZN - 1)),
            DMA((4, 2)),
            DMA((count, 4 + ZN - 1)),
            DMA((3,)),
            DMA((3,)),
            DMA((9,)),
            DMA((7 + ZN - 1,)),
            DMA((7 + ZN - 1,)),
        ],
        compiler_params=pltpu.CompilerParams(
            collective_id=0, has_side_effects=True, vmem_limit_bytes=64 * 1024 * 1024
        ),
        cost_estimate=pl.CostEstimate(flops=flops, bytes_accessed=8_000_000, transcendentals=8 * windows * hidden),
        name="train",
    )(segments, adjoint, lengths, first, square, head, biases)


def update_kernel(past, span, *refs):
    sources, targets, norm_out = refs[0:16], refs[16:34], refs[34]
    held, results, pad, in_sem, out_sem = refs[35:51], refs[51:67], *refs[67:70]
    arriving = [pltpu.make_async_copy(source, ref, in_sem.at[n]) for n, (source, ref) in enumerate(zip(sources, held))]
    leaving = [
        pltpu.make_async_copy(ref, target, out_sem.at[n]) for n, (ref, target) in enumerate(zip(held[0:2] + results, targets))
    ]
    for copy in arriving:
        copy.start()
    grads, norm, masters, momenta, variances = held[2], held[3], held[4:8], held[8:12], held[12:16]
    units = masters[3].shape[2]

    def rows(m, lane, width):
        return grads[m, :, :, lane : lane + width].reshape(units, width)

    arriving[2].wait()
    arriving[3].wait()
    norm_out[...] = norm[0:1, 0:1]
    factor = 1.0 / jnp.maximum(norm[0:1, 0:1], 1.0)
    for m in range(5):
        results[1][0, m] = rows(m + 1, 0, grads.shape[3])
    results[0][0] = rows(0, 0, 128)[:, 0:past]
    forecast = rows(0, 128, 128)
    pad[...] = jnp.zeros_like(pad)
    pad[0:units, :] = forecast
    results[3][0] = pad[...].T[span : span + 4, 0:units]
    results[2][0, :, 0:past] = rows(0, 256, 128)[:, 0:past]
    results[2][0, :, past : past + span] = forecast[:, 0:span]
    for n in (0, 1):
        arriving[n].wait()
        leaving[n].start()
    for n in (1, 0, 2, 3):
        leaving[2 + n].start()
        for state in range(3):
            arriving[4 + 4 * state + n].wait()
        updated = adamw(masters[n][...], results[n][...], momenta[n][...], variances[n][...], factor[None])
        for kind, value in enumerate(updated):
            results[4 * (kind + 1) + n][...] = value
            leaving[2 + 4 * (kind + 1) + n].start()
    for copy in leaving:
        copy.wait()


def update_call(prediction, sensitivity, grads, norm, state):
    hbm = pl.BlockSpec(memory_space=pl.ANY)
    sources = (prediction, sensitivity, grads, norm, *state)
    targets = (prediction, sensitivity, *(4 * list(state[:4])))
    return pl.pallas_call(
        functools.partial(update_kernel, sensitivity.shape[0], prediction.shape[0]),
        out_shape=tuple(jax.ShapeDtypeStruct(a.shape, F32) for a in targets) + (jax.ShapeDtypeStruct((1, 1), F32),),
        in_specs=[hbm] * len(sources),
        out_specs=tuple([hbm] * len(targets) + [pl.BlockSpec(memory_space=pltpu.VMEM)]),
        scratch_shapes=[pltpu.VMEM(a.shape, F32) for a in sources]
        + [pltpu.VMEM(a.shape, F32) for a in targets[2:]]
        + [pltpu.VMEM((128, 128), F32), pltpu.SemaphoreType.DMA((len(sources),)), pltpu.SemaphoreType.DMA((len(targets),))],
        name="update",
    )(*sources)


def turned(arrays):
    return [a.transpose(0, 2, 1) if n % 4 == 0 else a for n, a in enumerate(arrays)]


def kernel_shards(plane, segments, extents, adjoint, *state):
    state = turned(state)
    results = train_call(plane, segments, extents, adjoint.T, *state[:4])
    prediction, sensitivity, *updated, norm = update_call(*results, state)
    by_window = (prediction.transpose(1, 2, 0), sensitivity.transpose(1, 2, 0))
    return (*by_window, norm.reshape(()), *turned(updated))


STATE_SPECS = (
    P("section", None, "dp"),
    P("section", None, "dp", None),
    P("section", "dp", None),
    P("section", None, "dp"),
)


def solution(mesh):
    in_specs = (P("dp", None), P("dp"), P("dp", None)) + 3 * STATE_SPECS
    out_specs = (P("section", "dp", None), P("section", "dp", None), P()) + 4 * STATE_SPECS
    plane = PLANES.get(mesh.shape["dp"])
    shards = plain_shards if plane is None else functools.partial(kernel_shards, plane)
    return jax.shard_map(shards, mesh=mesh, in_specs=in_specs, out_specs=out_specs, check_vma=False)
```

```python
import functools

import jax
import jax.numpy as jnp
from jax import lax
from jax.experimental import pallas as pl
from jax.experimental.pallas import tpu as pltpu
from jax.sharding import PartitionSpec as P

STEP = 10


def dot_nn(a, b):
    return jnp.dot(a, b, preferred_element_type=jnp.float32)


def dot_tn(a, b):
    return lax.dot_general(a, b, (((0,), (0,)), ((), ())), preferred_element_type=jnp.float32)


def dot_nt(a, b):
    return lax.dot_general(a, b, (((1,), (1,)), ((), ())), preferred_element_type=jnp.float32)


def unit_rows(first, square, head, biases):
    units = first.shape[1]
    return jnp.concatenate(
        [square.transpose(1, 0, 2).reshape(units, -1), first.T, head, biases.T], axis=1
    )


def from_unit_rows(rows, past, hidden, out):
    wide = 5 * hidden
    square = rows[:, :wide].reshape(-1, 5, hidden).transpose(1, 0, 2)
    first = rows[:, wide : wide + past].T
    head = rows[:, wide + past : wide + past + out]
    biases = rows[:, wide + past + out :].T
    return first, square, head, biases


def plain_forward(weights, resid):
    first, square, head, biases = weights
    past = resid.shape[1]
    acts, slopes = [resid.astype(jnp.bfloat16)], []
    for k in range(4):
        z = dot_nn(acts[-1], first if k == 0 else square[k - 1]) + biases[k].astype(jnp.float32)
        sig = jax.nn.sigmoid(z)
        acts.append((z * sig).astype(jnp.bfloat16))
        slopes.append(sig * (1.0 + z * (1.0 - sig)))
    theta_b = dot_nn(acts[4], square[3]).astype(jnp.bfloat16)
    theta_f = dot_nn(acts[4], square[4]).astype(jnp.bfloat16)
    backcast = dot_nn(theta_b, head[:, :past])
    part = dot_nn(theta_f, head[:, past:])
    return backcast, part, (acts, slopes, theta_b, theta_f)


def plain_backward(weights, saved, e, f):
    first, square, head, biases = weights
    acts, slopes, theta_b, theta_f = saved
    past = e.shape[1]
    head_grad = jnp.concatenate([dot_tn(theta_b, e), dot_tn(theta_f, f)], axis=1)
    u_b = dot_nt(e, head[:, :past]).astype(jnp.bfloat16)
    u_f = dot_nt(f, head[:, past:]).astype(jnp.bfloat16)
    squares = [None, None, None, dot_tn(acts[4], u_b), dot_tn(acts[4], u_f)]
    da = dot_nt(u_b, square[3]) + dot_nt(u_f, square[4])
    bias_grads = [None] * 4
    first_grad = None
    for k in (3, 2, 1, 0):
        dz = (da * slopes[k]).astype(jnp.bfloat16)
        bias_grads[k] = jnp.sum(dz, axis=0, dtype=jnp.float32)
        grad = dot_tn(acts[k], dz)
        if k == 0:
            first_grad = grad
        else:
            squares[k - 1] = grad
        da = dot_nt(dz, first if k == 0 else square[k - 1])
    return da, (first_grad, jnp.stack(squares), head_grad, jnp.stack(bias_grads))


def adamw(master, gradient, momentum, variance, factor):
    clipped = gradient * factor
    moment_new = 0.9 * momentum + 0.1 * clipped
    variance_new = 0.999 * variance + 0.001 * clipped * clipped
    ratio = moment_new / (1.0 - 0.9**STEP) / (jnp.sqrt(variance_new / (1.0 - 0.999**STEP)) + 1e-08)
    return master - 0.05 * (ratio + 0.01 * master), moment_new, variance_new


def plain_shards(segments, extents, adjoint, *state):
    masters, momenta, variances = state[:4], state[4:8], state[8:]
    core = lax.axis_index("section")
    past, span = segments.shape[1], adjoint.shape[1]
    windows = segments.shape[0] // 2
    hidden = masters[1].shape[3]
    mine = [
        lax.dynamic_slice_in_dim(v, core * windows, windows, 0) for v in (segments, extents, adjoint)
    ]
    seg, ext, adj = mine
    rows = unit_rows(*(m[0].astype(jnp.bfloat16) for m in masters))
    rows = lax.all_gather(rows, "dp", axis=0, tiled=True)
    rows = lax.all_gather(rows, "section", axis=0)
    blocks = [from_unit_rows(rows[b], past, hidden, past + span) for b in range(2)]
    mask = (
        lax.broadcasted_iota(jnp.int32, (windows, past), 1) >= past - ext[:, None]
    ).astype(jnp.float32)
    r0 = seg * mask
    backcast, part0, saved0 = plain_forward(blocks[0], r0)
    r1 = (r0 - backcast) * mask
    _, part1, saved1 = plain_forward(blocks[1], r1)
    forecast = part0.astype(jnp.bfloat16).astype(jnp.float32) + part1
    f = adj.astype(jnp.bfloat16)
    zero = jnp.zeros_like(r0)
    da1, grads1 = plain_backward(blocks[1], saved1, (-(zero * mask)).astype(jnp.bfloat16), f)
    dr1 = zero * mask + da1
    t = dr1.astype(jnp.bfloat16).astype(jnp.float32)
    da0, grads0 = plain_backward(blocks[0], saved0, (-(t * mask)).astype(jnp.bfloat16), f)
    dr0 = (t * mask + da0) * mask

    def by_section(first_block, second_block):
        mine, other = (
            jnp.where(core == 0, first_block, second_block),
            jnp.where(core == 0, second_block, first_block),
        )
        got = lax.ppermute(other, "section", [(0, 1), (1, 0)])
        return jnp.where(
            core == 0, jnp.concatenate([mine, got]), jnp.concatenate([got, mine])
        )[None]

    prediction = by_section(part0, forecast)
    sensitivity = by_section(dr0, dr1)
    packed = jnp.stack([unit_rows(*grads0), unit_rows(*grads1)])
    packed = lax.psum_scatter(packed, "section", scatter_dimension=0, tiled=False)
    packed = lax.psum_scatter(packed, "dp", scatter_dimension=0, tiled=True)
    norm = jnp.sqrt(lax.psum(jnp.sum(packed * packed), ("section", "dp")))
    factor = 1.0 / jnp.maximum(norm, 1.0)
    summed = [g[None] for g in from_unit_rows(packed, past, hidden, past + span)]
    updated = [adamw(*four, factor) for four in zip(masters, summed, momenta, variances)]
    return (
        prediction,
        sensitivity,
        norm,
        *summed,
        *(u[0] for u in updated),
        *(u[1] for u in updated),
        *(u[2] for u in updated),
    )


PLANES = {16: (4, 2, 2)}
MESH = pl.DeviceIdType.MESH
MATS = 6
CORE_SLOTS = 6
BF, F32 = jnp.bfloat16, jnp.float32
GATHER = ((0, 0), (0, 1), (0, 2), (0, 3), (0, 4), (1, 0), (1, 1), (1, 2), (1, 3), (1, 4), (1, 5), (0, 5))
STEPS = (
    (0, 0, 0, 1, 1, 1, 2, 3, 4, 6, 7, 8),
    (1, 1, 2, 3, 4, 4, 5, 7, 8, 11, 9, 13),
    (3, 3, 3, 5, 7, 8, 8, 9, 11, 13, 12, 17),
    (4, 4, 6, 8, 9, 10, 11, 12, 13, 16, 16, 21),
    (14, 19, 20, 22, 23, 23, 25, 26, 27, 28, 29, 31),
    (21, 21, 22, 24, 24, 25, 27, 28, 29, 30, 36, 37),
    (23, 25, 24, 26, 28, 27, 29, 30, 35, 37, 40, 41),
    (32, 32, 33, 33, 36, 38, 38, 41, 42, 43, 44, 44),
)
FIRST, LAST = 6, 30
ORDER = ((0, 5), (1, 4), (1, 5), (1, 3), (1, 2), (1, 1), (0, 4), (0, 3), (0, 2), (0, 1), (1, 0), (0, 0))


def remote(src, dst, send_sem, recv_sem, device):
    return pltpu.make_async_remote_copy(
        src_ref=src, dst_ref=dst, send_sem=send_sem, recv_sem=recv_sem, device_id=device, device_id_type=MESH
    )


def train_kernel(
    sizes,
    seg_hbm, adj_hbm, ext_hbm, first_hbm, square_hbm, head_hbm, biases_hbm,
    pred_out, sens_out, grad_out, norm_out,
    wg, handed, gp, from_core, from_diag, from_plain, from_pair, from_z, total,
    act_t, in_t, theta_keep, slope, work, resid, mask, f_ref, e_t, bias_t, bias_sum, pad,
    seg, adj, ext, first, square, head, biases, part_t, pred, sens, squares, norm_buf,
    own_send, own_recv, ag_send, ag_recv, rs_send, rs_recv, out_send, out_recv, local_sem, norm_send, norm_recv,
):
    ZN, YN, XN, windows, tile, past, span, hidden = sizes
    units = ZN * YN * XN
    core, dp = lax.axis_index("section"), lax.axis_index("dp")
    x, y, z = lax.rem(dp, XN), lax.rem(lax.div(dp, XN), YN), lax.div(dp, XN * YN)
    other, xo, yo = 1 - core, 1 - x, 1 - y
    near_y, near_x = y + core * (yo - y), xo + core * (x - xo)
    far_y, far_x = yo + core * (y - yo), x + core * (xo - x)

    def chip(zi, yi, xi):
        return (core, (zi * YN + yi) * XN + xi)

    sibling = (other, dp)
    z_peers = [lax.rem(z + step, ZN) for step in range(1, ZN)]

    row0 = core * windows
    loads = [
        pltpu.make_async_copy(seg_hbm.at[pl.ds(row0, windows), :], seg, local_sem.at[0]),
        pltpu.make_async_copy(adj_hbm.at[:, pl.ds(row0, windows)], adj, local_sem.at[1]),
    ]
    small_loads = [
        pltpu.make_async_copy(source, target, local_sem.at[4 + n])
        for n, (source, target) in enumerate(
            [(square_hbm, square), (first_hbm, first), (head_hbm, head), (biases_hbm, biases), (ext_hbm, ext)]
        )
    ]
    for load in small_loads + loads:
        load.start()

    barrier = pltpu.get_barrier_semaphore()
    plane_peers = [
        (ci, (z * YN + yi) * XN + xi) for ci in (core, other) for yi in (y, yo) for xi in (x, xo)
    ][1:]
    peers = plane_peers + [(ci, (zi * YN + y) * XN + x) for zi in z_peers for ci in (core, other)]
    for peer in peers:
        pl.semaphore_signal(barrier, inc=1, device_id=peer, device_id_type=MESH)

    rows = hidden // units
    half_rows = rows // 2

    def put_own(m, value, lanes):
        halves = value.astype(BF).reshape(2, half_rows, -1)
        for h in range(2):
            pl.when(core == h)(functools.partial(put_half, m, halves[h], halves[1 - h], lanes))

    def put_half(m, kept, given, lanes):
        wg[core, m, z, y, x, core, :, lanes] = kept
        handed[m, :, lanes] = given

    for load in small_loads:
        load.wait()
    pad[...] = jnp.zeros_like(pad)
    pad[0:rows, 0:past] = first[0] * 0.5
    put_own(0, pad[0:rows, :], slice(0, 128))
    pad[...] = jnp.zeros_like(pad)
    pad[span : span + 4, 0:rows] = biases[0] * 0.5
    bias_cols = pad[...].T[0:rows]
    pad[...] = jnp.zeros_like(pad)
    pad[0:rows, 0:span] = head[0, :, past : past + span]
    put_own(0, pad[0:rows, :] + bias_cols, slice(128, 256))
    pad[...] = jnp.zeros_like(pad)
    pad[0:rows, 0:past] = head[0, :, 0:past]
    put_own(0, pad[0:rows, :], slice(256, 384))
    pl.semaphore_wait(barrier, len(peers))

    def hand_over(m, lanes):
        return remote(
            handed.at[m, :, lanes], wg.at[core, m, z, y, x, other, :, lanes], own_send.at[m], own_recv.at[m], sibling
        )

    def pack(m):
        put_own(m, square[0, m - 1] * 0.5 if m < 4 else square[0, m - 1], slice(0, hidden))


    def of(i):
        if isinstance(i, int):
            return GATHER[i]
        b = jnp.where(jnp.logical_and(i >= 5, i <= 10), 1, 0)
        return b, jnp.where(i <= 4, i, jnp.where(i <= 10, i - 5, 5))

    def sends(sems, kind, lanes):
        return sems.at[kind, 0 if lanes.stop == hidden else 1]

    def z_copies(i, lanes):
        b, m = of(i)
        part = wg.at[b, m, z, y, x, core, :, lanes]
        return [
            remote(part, part, sends(ag_send, 0, lanes), ag_recv.at[i, s], chip(zi, y, x)) for s, zi in enumerate(z_peers)
        ]

    def line_copies(i, lanes):
        b, m = of(i)
        given = wg.at[b, m, z, y, x, other, :, lanes]
        return [
            remote(
                handed.at[m, :, lanes], given, sends(ag_send, 0, lanes), ag_recv.at[i, s], (other, (zi * YN + y) * XN + x)
            )
            for s, zi in enumerate(z_peers)
        ]

    def column_copies(i, lanes):
        b, m = of(i)
        part = wg.at[b, m, :, y, x, core, :, lanes]
        return [
            remote(part, part, sends(ag_send, 1, lanes), ag_recv.at[i, 3], chip(z, near_y, near_x)),
            remote(part, part, sends(ag_send, 1, lanes), ag_recv.at[i, 4], chip(z, far_y, far_x)),
        ]

    def corner_copy(i, lanes):
        b, m = of(i)
        part = wg.at[b, m, :, near_y, near_x, core, :, lanes]
        return remote(part, part, sends(ag_send, 2, lanes), ag_recv.at[i, 5], chip(z, far_y, far_x))

    def core_copy(i, lanes):
        b, m = of(i)
        part = wg.at[b, m, :, :, :, core, :, lanes]
        return remote(part, part, sends(ag_send, 3, lanes), ag_recv.at[i, 6], sibling)

    def by_lanes(m, step):
        if isinstance(m, int):
            step(slice(0, hidden if m else 384))
            return
        pl.when(m == 0)(lambda: step(slice(0, 384)))
        pl.when(m > 0)(lambda: step(slice(0, hidden)))

    def start_all(copies):
        for copy in copies:
            copy.start()

    zeros_tile = jnp.zeros((tile, 128), F32)

    def prepare(t, carry):
        at = pl.ds(t * tile, tile)
        resid[at, :] = zeros_tile
        resid[at, 0:past] = seg[at, :]
        return carry

    def prepare_mask(g, carry):
        lengths = ext[pl.ds(core * (windows // 128) + g, 1), :]
        position = lax.broadcasted_iota(jnp.int32, (128, 128), 0)
        keep = jnp.where(position >= past - lengths, 1.0, 0.0).astype(F32).T
        at = pl.ds(pl.multiple_of(g * 128, 128), 128)
        pad[0:span, :] = adj[:, at]
        f_ref[at, :] = pad[...].T.astype(BF)
        mask[at, :] = keep.astype(BF)
        resid[at, :] = resid[at, :] * keep
        return carry

    tiles = windows // tile
    part_tile = windows // 2

    def prepare_all():
        for load in loads:
            load.wait()
        lax.fori_loop(0, tiles, prepare, 0)
        pad[...] = jnp.zeros_like(pad)
        lax.fori_loop(0, windows // 128, prepare_mask, 0)

    def matrix(b, m):
        return wg[b, m].reshape(hidden, hidden)

    def small(b, lane):
        return wg[b, 0, :, :, :, :, :, lane : lane + 128].reshape(hidden, 128)

    def store_layer(b, k, at, v):
        p = 1.0 + jnp.tanh(v)
        a = v * p
        rate = p + a * (2.0 - p)
        slope[b, k, at, :] = rate.astype(BF)
        low = a.astype(BF)
        act_t[b, k, :, at] = low.T
        return low

    def halves(body):
        for t in range(2):
            body(slice(t * windows // 2, (t + 1) * windows // 2))

    def layer_zero(b):
        bias_t[...] = small(b, 128).astype(F32).T

        def body(at):
            a = resid[at, :].astype(BF)
            in_t[b, :, at] = a.T
            work[0, at, :] = store_layer(b, 0, at, dot_nt(a, small(b, 0)) + bias_t[span : span + 1, :])

        halves(body)

    def layer_next(b, k):
        source, target = lax.rem(k + 1, 2), lax.rem(k, 2)
        v = dot_nn(work[source], matrix(b, k)) + bias_t[pl.ds(span + k, 1), :]
        work[target] = store_layer(b, k, slice(0, windows), v)

    def grid(value):
        return value.astype(BF).reshape(ZN, YN, XN, 2, half_rows, -1)

    def backcast_step():
        def body(at):
            theta = dot_nn(work[1, at, :], matrix(0, 4)).astype(BF)
            theta_keep[at, :] = theta
            resid[at, :] = (resid[at, :] - dot_nn(theta, small(0, 256))) * mask[at, :].astype(F32)

        halves(body)

    def put_rows(buf, b, at, value):
        for row in range(value.shape[0]):
            buf[b, row, :, at] = value[row : row + 1]

    def late_theta(b, m):
        theta_t = act_t.at[1, 0]
        theta_t[...] = dot_nn(matrix(b, m).T, act_t[b, 3]).astype(BF)

        @pl.when(m == 4)
        def _():
            gp[b, 0, :, :, :, :, :, 256:384] = grid(dot_nt(theta_t[...], e_t[b]))

        @pl.when(m == 5)
        def _():
            grad = grid(dot_nn(theta_t[...], f_ref[...]))
            gp[b, 0, :, :, :, :, :, 128:256] = gp[b, 0, :, :, :, :, :, 128:256] + grad
            part_t[b] = dot_nn(small(b, 128).T, theta_t[...])[0:span]

    def forecasts():
        put_rows(pred, 0, slice(0, windows), part_t[0])
        put_rows(pred, 1, slice(0, windows), part_t[0].astype(BF).astype(F32) + part_t[1])

    count = 2 * MATS

    def gather_line(i):
        b, m = of(i)

        pl.when(b == core)(lambda: by_lanes(m, lambda lanes: start_all(line_copies(i, lanes) + z_copies(i, lanes))))

    def gather_columns(i):
        b, m = of(i)

        def step(lanes):
            pl.when(b != core)(lambda: hand_over(m, lanes).wait_recv())
            for copy in z_copies(i, lanes):
                copy.wait_recv()
            start_all(column_copies(i, lanes))

        by_lanes(m, step)

    def gather_corner(i):
        def step(lanes):
            column_copies(i, lanes)[0].wait_recv()
            corner_copy(i, lanes).start()

        by_lanes(of(i)[1], step)

    def gather_core(i):
        def step(lanes):
            column_copies(i, lanes)[1].wait_recv()
            corner_copy(i, lanes).wait_recv()
            core_copy(i, lanes).start()

        by_lanes(of(i)[1], step)

    def arrived(i):
        by_lanes(of(i)[1], lambda lanes: core_copy(i, lanes).wait_recv())

    def forward_unit(i):
        arrived(i)
        b, m = of(i)
        pl.when(m == 0)(lambda: layer_zero(b))
        pl.when(jnp.logical_and(m >= 1, m <= 3))(lambda: layer_next(b, m))
        pl.when(m == 4)(backcast_step)

    def out_copies(buf, out, s):
        at = pl.ds(row0, windows)
        return [
            pltpu.make_async_copy(buf.at[core], out.at[:, :, at], local_sem.at[2 + s]),
            remote(buf.at[other], out.at[:, :, at], out_send.at[s], out_recv.at[s], sibling),
        ]


    def back_of(j):
        if isinstance(j, int):
            return ORDER[j]
        b = jnp.where(jnp.logical_or(jnp.logical_and(j >= 1, j <= 5), j == 10), 1, 0)
        early = jnp.where(j == 1, 4, jnp.where(j <= 2, 5, 6 - j))
        return b, jnp.where(j <= 5, early, jnp.where(j == 6, 4, jnp.where(j <= 9, 10 - j, 0)))

    def to_core(j, lanes):
        b, m = back_of(j)
        return remote(
            gp.at[b, m, :, :, :, other, :, lanes], from_core.at[lax.rem(j, CORE_SLOTS), :, :, :, :, lanes],
            sends(rs_send, 3, lanes), rs_recv.at[j, 0], sibling,
        )

    def to_far(j, lanes):
        b, m = back_of(j)
        device = chip(z, far_y, far_x)
        return [
            remote(
                gp.at[b, m, :, yo, xo, core, :, lanes], from_diag.at[j, :, :, lanes],
                sends(rs_send, 1, lanes), rs_recv.at[j, 1], device,
            ),
            remote(
                gp.at[b, m, :, far_y, far_x, core, :, lanes], from_plain.at[j, :, :, lanes],
                sends(rs_send, 1, lanes), rs_recv.at[j, 2], device,
            ),
        ]

    def to_near(j, lanes):
        b, m = back_of(j)
        return remote(
            gp.at[b, m, :, near_y, near_x, core, :, lanes], from_pair.at[j, :, :, lanes],
            sends(rs_send, 2, lanes), rs_recv.at[j, 3], chip(z, near_y, near_x),
        )

    def to_z(j, lanes):
        b, m = back_of(j)
        return [
            remote(
                gp.at[b, m, zi, y, x, core, :, lanes], from_z.at[j, s, :, lanes],
                sends(rs_send, 0, lanes), rs_recv.at[j, 4 + s], chip(zi, y, x),
            )
            for s, zi in enumerate(z_peers)
        ]

    def scatter_start(j):
        by_lanes(back_of(j)[1], lambda lanes: to_core(j, lanes).start())

    def scatter_core(j):
        b, m = back_of(j)

        def step(lanes):
            to_core(j, lanes).wait_recv()
            part = gp[b, m, :, :, :, core, :, lanes] + from_core[lax.rem(j, CORE_SLOTS), :, :, :, :, lanes]
            gp[b, m, :, :, :, core, :, lanes] = part
            start_all(to_far(j, lanes))

        by_lanes(m, step)

    def scatter_diag(j):
        b, m = back_of(j)

        def step(lanes):
            to_far(j, lanes)[0].wait_recv()
            part = gp[b, m, :, near_y, near_x, core, :, lanes] + from_diag[j, :, :, lanes]
            gp[b, m, :, near_y, near_x, core, :, lanes] = part
            to_near(j, lanes).start()

        by_lanes(m, step)

    def scatter_plane(j):
        b, m = back_of(j)

        def step(lanes):
            to_far(j, lanes)[1].wait_recv()
            to_near(j, lanes).wait_recv()
            value = gp[b, m, :, y, x, core, :, lanes].astype(F32)
            value = value + from_plain[j, :, :, lanes].astype(F32)
            value = value + from_pair[j, :, :, lanes].astype(F32)
            gp[b, m, :, y, x, core, :, lanes] = value.astype(BF)
            start_all(to_z(j, lanes))

        by_lanes(m, step)

    def scatter_z(j):
        b, m = back_of(j)

        def step(lanes):
            for copy in to_z(j, lanes):
                copy.wait_recv()
            value = gp[b, m, z, y, x, core, :, lanes].astype(F32)
            for s in range(ZN - 1):
                value = value + from_z[j, s, :, lanes].astype(F32)
            total[b, m, :, lanes] = value
            squares[:, lanes] = squares[:, lanes] + value * value

        by_lanes(m, step)

    def add_rows(value):
        return jnp.sum(value.reshape(-1, 8, hidden), axis=0)

    def put_bias(k, acc):
        bias_sum[pl.ds(span + k, 1), :] = jnp.sum(acc, axis=0, keepdims=True)

    def feed(b):
        pl.when(b == 1)(lambda: resid.__setitem__(..., jnp.zeros_like(resid)))
        e = (-(resid[...] * mask[...].astype(F32))).astype(BF)
        e_t[b] = e.T
        work[0] = dot_nt(e, small(b, 256)).astype(BF)
        work[2] = dot_nt(f_ref[...], small(b, 128)).astype(BF)

    def feed_forward(b):
        work[2] = dot_nt(f_ref[...], small(b, 128)).astype(BF)

    def put_dz(b, k, da):
        dz = da * slope[b, k].astype(F32)
        work[k % 2 if isinstance(k, int) else lax.rem(k, 2)] = dz.astype(BF)
        bias_sum[pl.ds(span + k, 1), :] = jnp.sum(add_rows(dz), axis=0, keepdims=True)

    def theta_step(b):
        put_dz(b, 3, 0.5 * (dot_nt(work[0], matrix(b, 4)) + dot_nt(work[2], matrix(b, 5))))

    def layer_back(b, k):
        source = lax.rem(k, 2)
        gp[b, k] = grid(dot_nn(act_t[b, k - 1], work[source]))
        put_dz(b, k - 1, dot_nt(work[source], matrix(b, k)))

    def theta_grad(b, m):
        gp[b, m] = grid(dot_nn(act_t[b, 3], work[jnp.where(m == 4, 0, 2)]))

    def first_grads(b):
        gp[b, 0, :, :, :, :, :, 0:128] = grid(dot_nn(in_t[b], work[0]).T)
        gp[b, 0, :, :, :, :, :, 128:256] = grid(bias_sum[...].T)
        pl.when(b == 0)(backcast_grad)

    def backcast_grad():
        gp[0, 0, :, :, :, :, :, 256:384] = grid(dot_nn(e_t[0], theta_keep[...]).T)

    def input_grad(b):
        for t in range(2):
            at = slice(t * windows // 2, (t + 1) * windows // 2)
            keep = mask[at, :].astype(F32)
            dr = resid[at, :] * keep + 2.0 * dot_nn(work[0, at, :], small(b, 0))

            @pl.when(b == 1)
            def _():
                seg[at, :] = dr[:, 0:past]
                resid[at, :] = dr.astype(BF).astype(F32)

            @pl.when(b == 0)
            def _():
                put_rows(sens, 0, at, (dr * keep).T[0:past])

    def late_rows():
        for g in range(windows // 128):
            at = slice(g * 128, (g + 1) * 128)
            pad[:, 0:past] = seg[at, :]
            put_rows(sens, 1, at, pad[...].T[0:past])

    bias_sum[...] = jnp.zeros_like(bias_sum)
    squares[...] = jnp.zeros_like(squares)
    total[...] = jnp.zeros_like(total)

    moves = (
        gather_line, gather_columns, gather_corner, gather_core, scatter_core, scatter_diag, scatter_plane, scatter_z
    )

    def move(place):
        for stage in range(len(moves) - 1, -1, -1):
            for unit in range(count):
                if STEPS[stage][unit] == place:
                    moves[stage](unit)

    def any_of(t, *places):
        return functools.reduce(jnp.logical_or, [t == place for place in places])

    def between(t, low, high):
        return jnp.logical_and(t >= low, t <= high)

    def product(t, carry):
        for low in range(FIRST, LAST, 6):

            @pl.when(between(t, low, low + 5))
            def _():
                for place in range(low, low + 6):
                    pl.when(t == place)(functools.partial(move, place))

        forward = jnp.logical_or(t <= 10, between(t, 12, 15))
        pl.when(forward)(lambda: forward_unit(jnp.where(t <= 10, t - 6, t - 7)))

        pl.when(t == 11)(lambda: feed_forward(0))
        pl.when(any_of(t, 16, 23))(lambda: feed(jnp.where(t == 16, 1, 0)))
        theta_block = jnp.where(between(t, 16, 17), 1, 0)
        pl.when(any_of(t, 11, 16, 17, 23))(lambda: theta_grad(theta_block, jnp.where(any_of(t, 11, 17), 5, 4)))

        early = t <= 21
        layers = jnp.logical_or(between(t, 19, 21), between(t, 24, 26))
        pl.when(layers)(lambda: layer_back(jnp.where(early, 1, 0), jnp.where(early, 22 - t, 27 - t)))
        pl.when(any_of(t, 22, 28))(lambda: first_grads(jnp.where(t == 22, 1, 0)))

        @pl.when(any_of(t, 27, 28))
        def _():
            block = jnp.where(t == 27, 1, 0)
            lax.fori_loop(5 - block, MATS, lambda n, carry: (late_theta(block, n), carry)[1], 0)

        unit = jnp.where(t == 11, 0, jnp.where(t <= 17, t - 15, jnp.where(early, t - 16, t - 17)))
        ready = functools.reduce(
            jnp.logical_or, [t == 11, between(t, 16, 17), between(t, 19, 21), between(t, 23, 28)]
        )
        pl.when(ready)(lambda: scatter_start(unit))
        pl.when(any_of(t, 22, 29))(lambda: input_grad(jnp.where(t == 22, 1, 0)))

        @pl.when(t == 18)
        def _():
            arrived(9)
            arrived(10)

        pl.when(t == 23)(lambda: arrived(11))
        pl.when(any_of(t, 18, 23))(lambda: theta_step(jnp.where(t == 18, 1, 0)))
        return carry

    gather_line(0)
    hand_over(0, slice(0, 384)).start()
    for m in range(1, MATS):
        pack(m)
        hand_over(m, slice(0, hidden)).start()
        if STEPS[0][m] == 0:
            gather_line(m)
    for place in range(1, FIRST):
        move(place)
        if place == 1:
            prepare_all()
    lax.fori_loop(FIRST, LAST, product, 0)
    forecasts()
    start_all(out_copies(pred, pred_out, 0))
    move(LAST)
    move(LAST + 1)
    late_rows()
    start_all(out_copies(sens, sens_out, 1))
    for place in range(LAST + 2, max(map(max, STEPS)) + 1):
        move(place)

    grad_copy = remote(total.at[other], grad_out.at[:, core], out_send.at[2], out_recv.at[2], sibling)
    grad_copy.start()
    grad_out[:, core] = total[core]
    sq = squares[:, 0:128] + squares[:, 128:256] + squares[:, 256:384] + squares[:, 384:512]
    place = (y * XN + x) * 2 + core
    norm_buf[place] = sq[0:8] + sq[8:16]

    def spread(sources, targets, first):
        copies = [
            remote(norm_buf.at[sources], norm_buf.at[sources], norm_send.at[first + s], norm_recv.at[first + s], device)
            for s, device in enumerate(targets)
        ]
        start_all(copies)
        for copy in copies:
            copy.wait()

    def add_up(slots):
        value = norm_buf[slots[0]]
        for slot in slots[1:]:
            value = value + norm_buf[slot]
        return value

    spread(place, plane_peers, 0)
    norm_buf[8 + z] = add_up(range(8))
    spread(8 + z, [chip(zi, y, x) for zi in z_peers], 7)
    everything = add_up(range(8, 8 + ZN))
    norm_out[...] = jnp.broadcast_to(jnp.sqrt(jnp.sum(everything, keepdims=True)), norm_out.shape)

    grad_copy.wait()
    for buf, out, s in ((pred, pred_out, 0), (sens, sens_out, 1)):
        for copy in out_copies(buf, out, s):
            copy.wait()
    for m in range(MATS):
        hand_over(m, slice(0, hidden if m else 384)).wait_send()

    for mats, lanes in ((slice(1, MATS), slice(0, hidden)), (slice(0, 1), slice(0, 384))):
        sent = (
            wg.at[:, mats, 0 : ZN - 1, 0, 0, 0, :, lanes],
            wg.at[:, mats, :, :, 0, 0, :, lanes],
            wg.at[:, mats, :, 0, 0, 0, :, lanes],
            wg.at[:, mats, :, :, :, 0, :, lanes],
        )
        for sems in (ag_send, rs_send):
            for kind, ref in enumerate(sent):
                remote(ref, ref, sends(sems, kind, lanes), out_recv.at[0], sibling).wait_send()


def train_call(plane, segments, extents, adjoint, first, square, head, biases):
    ZN, YN, XN = plane
    past, span, hidden = segments.shape[1], adjoint.shape[0], square.shape[3]
    windows = segments.shape[0] // 2
    tile = windows
    half = hidden // (ZN * YN * XN) // 2
    sizes = (ZN, YN, XN, windows, tile, past, span, hidden)
    DMA = pltpu.SemaphoreType.DMA
    vmem = pl.BlockSpec(memory_space=pltpu.VMEM)
    hbm = pl.BlockSpec(memory_space=pl.ANY)
    count = 2 * MATS
    flops = 2 * 2 * 3 * windows * hidden * (6 * hidden + 2 * 128)
    lengths = extents.reshape(-1, 128)
    return pl.pallas_call(
        functools.partial(train_kernel, sizes),
        out_shape=(
            jax.ShapeDtypeStruct((span, 1, 2 * windows), F32),
            jax.ShapeDtypeStruct((past, 1, 2 * windows), F32),
            jax.ShapeDtypeStruct((MATS, 2, half, hidden), F32),
            jax.ShapeDtypeStruct((8, 128), F32),
        ),
        in_specs=[hbm] * 7,
        out_specs=(hbm, hbm, vmem, vmem),
        scratch_shapes=[
            pltpu.VMEM((2, MATS, ZN, YN, XN, 2, half, hidden), BF),
            pltpu.VMEM((MATS, half, hidden), BF),
            pltpu.VMEM((2, MATS, ZN, YN, XN, 2, half, hidden), BF),
            pltpu.VMEM((CORE_SLOTS, ZN, YN, XN, half, hidden), BF),
            pltpu.VMEM((count, ZN, half, hidden), BF),
            pltpu.VMEM((count, ZN, half, hidden), BF),
            pltpu.VMEM((count, ZN, half, hidden), BF),
            pltpu.VMEM((count, ZN - 1, half, hidden), BF),
            pltpu.VMEM((2, MATS, half, hidden), F32),
            pltpu.VMEM((2, 4, hidden, windows), BF),
            pltpu.VMEM((2, 128, windows), BF),
            pltpu.VMEM((windows, hidden), BF),
            pltpu.VMEM((2, 4, windows, hidden), BF),
            pltpu.VMEM((3, windows, hidden), BF),
            pltpu.VMEM((windows, 128), F32),
            pltpu.VMEM((windows, 128), BF),
            pltpu.VMEM((windows, 128), BF),
            pltpu.VMEM((2, 128, windows), BF),
            pltpu.VMEM((128, hidden), F32),
            pltpu.VMEM((128, hidden), F32),
            pltpu.VMEM((128, 128), F32),
            pltpu.VMEM((windows, past), F32),
            pltpu.VMEM((span, windows), F32),
            *(pltpu.VMEM(a.shape, a.dtype) for a in (lengths, first, square, head, biases)),
            pltpu.VMEM((2, span, windows), F32),
            pltpu.VMEM((2, span, 1, windows), F32),
            pltpu.VMEM((2, past, 1, windows), F32),
            pltpu.VMEM((half, hidden), F32),
            pltpu.VMEM((8 + ZN, 8, 128), F32),
            DMA((MATS,)),
            DMA((MATS,)),
            DMA((4, 2)),
            DMA((count, 4 + ZN - 1)),
            DMA((4, 2)),
            DMA((count, 4 + ZN - 1)),
            DMA((3,)),
            DMA((3,)),
            DMA((9,)),
            DMA((7 + ZN - 1,)),
            DMA((7 + ZN - 1,)),
        ],
        compiler_params=pltpu.CompilerParams(
            collective_id=0, has_side_effects=True, vmem_limit_bytes=64 * 1024 * 1024
        ),
        cost_estimate=pl.CostEstimate(flops=flops, bytes_accessed=8_000_000, transcendentals=8 * windows * hidden),
        name="train",
    )(segments, adjoint, lengths, first, square, head, biases)


def update_kernel(past, span, *refs):
    sources, targets, norm_out = refs[0:16], refs[16:34], refs[34]
    held, results, pad, in_sem, out_sem = refs[35:51], refs[51:67], *refs[67:70]
    arriving = [pltpu.make_async_copy(source, ref, in_sem.at[n]) for n, (source, ref) in enumerate(zip(sources, held))]
    leaving = [
        pltpu.make_async_copy(ref, target, out_sem.at[n]) for n, (ref, target) in enumerate(zip(held[0:2] + results, targets))
    ]
    for copy in arriving:
        copy.start()
    grads, norm, masters, momenta, variances = held[2], held[3], held[4:8], held[8:12], held[12:16]
    units = masters[3].shape[2]

    def rows(m, lane, width):
        return grads[m, :, :, lane : lane + width].reshape(units, width)

    arriving[2].wait()
    arriving[3].wait()
    norm_out[...] = norm[0:1, 0:1]
    factor = 1.0 / jnp.maximum(norm[0:1, 0:1], 1.0)
    for m in range(5):
        results[1][0, m] = rows(m + 1, 0, grads.shape[3])
    results[0][0] = rows(0, 0, 128)[:, 0:past]
    forecast = rows(0, 128, 128)
    pad[...] = jnp.zeros_like(pad)
    pad[0:units, :] = forecast
    results[3][0] = pad[...].T[span : span + 4, 0:units]
    results[2][0, :, 0:past] = rows(0, 256, 128)[:, 0:past]
    results[2][0, :, past : past + span] = forecast[:, 0:span]
    for n in (0, 1):
        arriving[n].wait()
        leaving[n].start()
    for n in (1, 0, 2, 3):
        leaving[2 + n].start()
        for state in range(3):
            arriving[4 + 4 * state + n].wait()
        updated = adamw(masters[n][...], results[n][...], momenta[n][...], variances[n][...], factor[None])
        for kind, value in enumerate(updated):
            results[4 * (kind + 1) + n][...] = value
            leaving[2 + 4 * (kind + 1) + n].start()
    for copy in leaving:
        copy.wait()


def update_call(prediction, sensitivity, grads, norm, state):
    hbm = pl.BlockSpec(memory_space=pl.ANY)
    sources = (prediction, sensitivity, grads, norm, *state)
    targets = (prediction, sensitivity, *(4 * list(state[:4])))
    return pl.pallas_call(
        functools.partial(update_kernel, sensitivity.shape[0], prediction.shape[0]),
        out_shape=tuple(jax.ShapeDtypeStruct(a.shape, F32) for a in targets) + (jax.ShapeDtypeStruct((1, 1), F32),),
        in_specs=[hbm] * len(sources),
        out_specs=tuple([hbm] * len(targets) + [pl.BlockSpec(memory_space=pltpu.VMEM)]),
        scratch_shapes=[pltpu.VMEM(a.shape, F32) for a in sources]
        + [pltpu.VMEM(a.shape, F32) for a in targets[2:]]
        + [pltpu.VMEM((128, 128), F32), pltpu.SemaphoreType.DMA((len(sources),)), pltpu.SemaphoreType.DMA((len(targets),))],
        name="update",
    )(*sources)


def turned(arrays):
    return [a.transpose(0, 2, 1) if n % 4 == 0 else a for n, a in enumerate(arrays)]


def kernel_shards(plane, segments, extents, adjoint, *state):
    state = turned(state)
    results = train_call(plane, segments, extents, adjoint.T, *state[:4])
    prediction, sensitivity, *updated, norm = update_call(*results, state)
    by_window = (prediction.transpose(1, 2, 0), sensitivity.transpose(1, 2, 0))
    return (*by_window, norm.reshape(()), *turned(updated))


STATE_SPECS = (
    P("section", None, "dp"),
    P("section", None, "dp", None),
    P("section", "dp", None),
    P("section", None, "dp"),
)


def solution(mesh):
    in_specs = (P("dp", None), P("dp"), P("dp", None)) + 3 * STATE_SPECS
    out_specs = (P("section", "dp", None), P("section", "dp", None), P()) + 4 * STATE_SPECS
    plane = PLANES.get(mesh.shape["dp"])
    shards = plain_shards if plane is None else functools.partial(kernel_shards, plane)
    return jax.shard_map(shards, mesh=mesh, in_specs=in_specs, out_specs=out_specs, check_vma=False)
```

```python
import functools

import jax
import jax.numpy as jnp
from jax import lax
from jax.experimental import pallas as pl
from jax.experimental.pallas import tpu as pltpu
from jax.sharding import PartitionSpec as P

STEP = 10


def dot_nn(a, b):
    return jnp.dot(a, b, preferred_element_type=jnp.float32)


def dot_tn(a, b):
    return lax.dot_general(a, b, (((0,), (0,)), ((), ())), preferred_element_type=jnp.float32)


def dot_nt(a, b):
    return lax.dot_general(a, b, (((1,), (1,)), ((), ())), preferred_element_type=jnp.float32)


def unit_rows(first, square, head, biases):
    units = first.shape[1]
    return jnp.concatenate(
        [square.transpose(1, 0, 2).reshape(units, -1), first.T, head, biases.T], axis=1
    )


def from_unit_rows(rows, past, hidden, out):
    wide = 5 * hidden
    square = rows[:, :wide].reshape(-1, 5, hidden).transpose(1, 0, 2)
    first = rows[:, wide : wide + past].T
    head = rows[:, wide + past : wide + past + out]
    biases = rows[:, wide + past + out :].T
    return first, square, head, biases


def plain_forward(weights, resid):
    first, square, head, biases = weights
    past = resid.shape[1]
    acts, slopes = [resid.astype(jnp.bfloat16)], []
    for k in range(4):
        z = dot_nn(acts[-1], first if k == 0 else square[k - 1]) + biases[k].astype(jnp.float32)
        sig = jax.nn.sigmoid(z)
        acts.append((z * sig).astype(jnp.bfloat16))
        slopes.append(sig * (1.0 + z * (1.0 - sig)))
    theta_b = dot_nn(acts[4], square[3]).astype(jnp.bfloat16)
    theta_f = dot_nn(acts[4], square[4]).astype(jnp.bfloat16)
    backcast = dot_nn(theta_b, head[:, :past])
    part = dot_nn(theta_f, head[:, past:])
    return backcast, part, (acts, slopes, theta_b, theta_f)


def plain_backward(weights, saved, e, f):
    first, square, head, biases = weights
    acts, slopes, theta_b, theta_f = saved
    past = e.shape[1]
    head_grad = jnp.concatenate([dot_tn(theta_b, e), dot_tn(theta_f, f)], axis=1)
    u_b = dot_nt(e, head[:, :past]).astype(jnp.bfloat16)
    u_f = dot_nt(f, head[:, past:]).astype(jnp.bfloat16)
    squares = [None, None, None, dot_tn(acts[4], u_b), dot_tn(acts[4], u_f)]
    da = dot_nt(u_b, square[3]) + dot_nt(u_f, square[4])
    bias_grads = [None] * 4
    first_grad = None
    for k in (3, 2, 1, 0):
        dz = (da * slopes[k]).astype(jnp.bfloat16)
        bias_grads[k] = jnp.sum(dz, axis=0, dtype=jnp.float32)
        grad = dot_tn(acts[k], dz)
        if k == 0:
            first_grad = grad
        else:
            squares[k - 1] = grad
        da = dot_nt(dz, first if k == 0 else square[k - 1])
    return da, (first_grad, jnp.stack(squares), head_grad, jnp.stack(bias_grads))


def adamw(master, gradient, momentum, variance, factor):
    clipped = gradient * factor
    moment_new = 0.9 * momentum + 0.1 * clipped
    variance_new = 0.999 * variance + 0.001 * clipped * clipped
    ratio = moment_new / (1.0 - 0.9**STEP) / (jnp.sqrt(variance_new / (1.0 - 0.999**STEP)) + 1e-08)
    return master - 0.05 * (ratio + 0.01 * master), moment_new, variance_new


def plain_shards(segments, extents, adjoint, *state):
    masters, momenta, variances = state[:4], state[4:8], state[8:]
    core = lax.axis_index("section")
    past, span = segments.shape[1], adjoint.shape[1]
    windows = segments.shape[0] // 2
    hidden = masters[1].shape[3]
    mine = [
        lax.dynamic_slice_in_dim(v, core * windows, windows, 0) for v in (segments, extents, adjoint)
    ]
    seg, ext, adj = mine
    rows = unit_rows(*(m[0].astype(jnp.bfloat16) for m in masters))
    rows = lax.all_gather(rows, "dp", axis=0, tiled=True)
    rows = lax.all_gather(rows, "section", axis=0)
    blocks = [from_unit_rows(rows[b], past, hidden, past + span) for b in range(2)]
    mask = (
        lax.broadcasted_iota(jnp.int32, (windows, past), 1) >= past - ext[:, None]
    ).astype(jnp.float32)
    r0 = seg * mask
    backcast, part0, saved0 = plain_forward(blocks[0], r0)
    r1 = (r0 - backcast) * mask
    _, part1, saved1 = plain_forward(blocks[1], r1)
    forecast = part0.astype(jnp.bfloat16).astype(jnp.float32) + part1
    f = adj.astype(jnp.bfloat16)
    zero = jnp.zeros_like(r0)
    da1, grads1 = plain_backward(blocks[1], saved1, (-(zero * mask)).astype(jnp.bfloat16), f)
    dr1 = zero * mask + da1
    t = dr1.astype(jnp.bfloat16).astype(jnp.float32)
    da0, grads0 = plain_backward(blocks[0], saved0, (-(t * mask)).astype(jnp.bfloat16), f)
    dr0 = (t * mask + da0) * mask

    def by_section(first_block, second_block):
        mine, other = (
            jnp.where(core == 0, first_block, second_block),
            jnp.where(core == 0, second_block, first_block),
        )
        got = lax.ppermute(other, "section", [(0, 1), (1, 0)])
        return jnp.where(
            core == 0, jnp.concatenate([mine, got]), jnp.concatenate([got, mine])
        )[None]

    prediction = by_section(part0, forecast)
    sensitivity = by_section(dr0, dr1)
    packed = jnp.stack([unit_rows(*grads0), unit_rows(*grads1)])
    packed = lax.psum_scatter(packed, "section", scatter_dimension=0, tiled=False)
    packed = lax.psum_scatter(packed, "dp", scatter_dimension=0, tiled=True)
    norm = jnp.sqrt(lax.psum(jnp.sum(packed * packed), ("section", "dp")))
    factor = 1.0 / jnp.maximum(norm, 1.0)
    summed = [g[None] for g in from_unit_rows(packed, past, hidden, past + span)]
    updated = [adamw(*four, factor) for four in zip(masters, summed, momenta, variances)]
    return (
        prediction,
        sensitivity,
        norm,
        *summed,
        *(u[0] for u in updated),
        *(u[1] for u in updated),
        *(u[2] for u in updated),
    )


PLANES = {16: (4, 2, 2)}
MESH = pl.DeviceIdType.MESH
MATS = 6
SLOTS = 3
BF, F32 = jnp.bfloat16, jnp.float32


def remote(src, dst, send_sem, recv_sem, device):
    return pltpu.make_async_remote_copy(
        src_ref=src, dst_ref=dst, send_sem=send_sem, recv_sem=recv_sem, device_id=device, device_id_type=MESH
    )


def train_kernel(
    sizes,
    seg_hbm, adj_hbm, ext_hbm, first_hbm, square_hbm, head_hbm, biases_hbm,
    pred_out, sens_out, grad_out, norm_out,
    wg, handed, gp, from_core, from_diag, from_plain, from_pair, from_z, total,
    act_t, in_t, theta_keep, slope, work, resid, mask, f_ref, e_t, bias_t, bias_sum, pad,
    seg, adj, ext, first, square, head, biases, part_t, pred, sens, squares, norm_buf,
    own_send, own_recv, ag_send, ag_recv, rs_send, rs_recv, out_send, out_recv, total_send, total_recv, local_sem, norm_send, norm_recv,
):
    ZN, YN, XN, windows, tile, past, span, hidden = sizes
    units = ZN * YN * XN
    core, dp = lax.axis_index("section"), lax.axis_index("dp")
    x, y, z = lax.rem(dp, XN), lax.rem(lax.div(dp, XN), YN), lax.div(dp, XN * YN)
    other, xo, yo = 1 - core, 1 - x, 1 - y
    near_y, near_x = y + core * (yo - y), xo + core * (x - xo)
    far_y, far_x = yo + core * (y - yo), x + core * (xo - x)

    def chip(zi, yi, xi):
        return (core, (zi * YN + yi) * XN + xi)

    sibling = (other, dp)
    z_peers = [lax.rem(z + step, ZN) for step in range(1, ZN)]

    row0 = core * windows
    loads = [
        pltpu.make_async_copy(seg_hbm.at[pl.ds(row0, windows), :], seg, local_sem.at[0]),
        pltpu.make_async_copy(adj_hbm.at[:, pl.ds(row0, windows)], adj, local_sem.at[1]),
    ]
    small_loads = [
        pltpu.make_async_copy(source, target, local_sem.at[4 + n])
        for n, (source, target) in enumerate(
            [(square_hbm, square), (first_hbm, first), (head_hbm, head), (biases_hbm, biases), (ext_hbm, ext)]
        )
    ]
    for load in small_loads + loads:
        load.start()

    barrier = pltpu.get_barrier_semaphore()
    plane_peers = [
        (ci, (z * YN + yi) * XN + xi) for ci in (core, other) for yi in (y, yo) for xi in (x, xo)
    ][1:]
    peers = plane_peers + [(ci, (zi * YN + y) * XN + x) for zi in z_peers for ci in (core, other)]
    for peer in peers:
        pl.semaphore_signal(barrier, inc=1, device_id=peer, device_id_type=MESH)

    rows = hidden // units

    def put_own(m, value, lanes):
        low = value.astype(BF)
        handed[m, :, lanes] = low
        if m % 2 == 0:
            wg[core, m, z, y, x, :, lanes] = low

    for load in small_loads:
        load.wait()
    pad[...] = jnp.zeros_like(pad)
    pad[0:rows, 0:past] = first[0] * 0.5
    put_own(0, pad[0:rows, :], slice(0, 128))
    pad[...] = jnp.zeros_like(pad)
    pad[span : span + 4, 0:rows] = biases[0] * 0.5
    bias_cols = pad[...].T[0:rows]
    pad[...] = jnp.zeros_like(pad)
    pad[0:rows, 0:span] = head[0, :, past : past + span]
    put_own(0, pad[0:rows, :] + bias_cols, slice(128, 256))
    pad[...] = jnp.zeros_like(pad)
    pad[0:rows, 0:past] = head[0, :, 0:past]
    put_own(0, pad[0:rows, :], slice(256, 384))
    pl.semaphore_wait(barrier, len(peers))

    def hand_over(m, lanes):
        return remote(handed.at[m, :, lanes], wg.at[core, m, z, y, x, :, lanes], own_send.at[m], own_recv.at[m], sibling)

    def pack(m):
        put_own(m, square[0, m - 1] * 0.5 if m < 4 else square[0, m - 1], slice(0, hidden))


    def of(i):
        b = jnp.where(jnp.logical_and(i >= 5, i <= 10), 1, 0)
        return b, jnp.where(i <= 4, i, jnp.where(i <= 10, i - 5, 5))

    def sends(sems, kind, lanes):
        return sems.at[kind, 0 if lanes.stop == hidden else 1]

    def z_copies(i, lanes):
        b, m = of(i)
        part = wg.at[b, m, z, y, x, :, lanes]
        return [
            remote(
                handed.at[m, :, lanes], part, sends(ag_send, 0, lanes), ag_recv.at[i, s],
                (lax.rem(i, 2), (zi * YN + y) * XN + x),
            )
            for s, zi in enumerate(z_peers)
        ]

    def column_copies(i, lanes):
        b, m = of(i)
        part = wg.at[b, m, :, y, x, :, lanes]
        return [
            remote(part, part, sends(ag_send, 1, lanes), ag_recv.at[i, 3], chip(z, near_y, near_x)),
            remote(part, part, sends(ag_send, 1, lanes), ag_recv.at[i, 4], chip(z, far_y, far_x)),
        ]

    def corner_copy(i, lanes):
        b, m = of(i)
        part = wg.at[b, m, :, near_y, near_x, :, lanes]
        return remote(part, part, sends(ag_send, 2, lanes), ag_recv.at[i, 5], chip(z, far_y, far_x))

    def core_copy(i, lanes):
        b, m = of(i)
        part = wg.at[b, m, :, :, :, :, lanes]
        return remote(part, part, sends(ag_send, 3, lanes), ag_recv.at[i, 6], sibling)

    def mine(i, step):
        pl.when(lax.rem(i, 2) == core)(lambda: step(i))

    def by_lanes(m, step):
        pl.when(m == 0)(lambda: step(slice(0, 384)))
        pl.when(m > 0)(lambda: step(slice(0, hidden)))

    def start_all(copies):
        for copy in copies:
            copy.start()

    zeros_tile = jnp.zeros((tile, 128), F32)

    def prepare(t, carry):
        at = pl.ds(t * tile, tile)
        resid[at, :] = zeros_tile
        resid[at, 0:past] = seg[at, :]
        return carry

    def prepare_mask(g, carry):
        lengths = ext[pl.ds(core * (windows // 128) + g, 1), :]
        position = lax.broadcasted_iota(jnp.int32, (128, 128), 0)
        keep = jnp.where(position >= past - lengths, 1.0, 0.0).astype(F32).T
        at = pl.ds(pl.multiple_of(g * 128, 128), 128)
        pad[0:span, :] = adj[:, at]
        f_ref[at, :] = pad[...].T.astype(BF)
        mask[at, :] = keep.astype(BF)
        resid[at, :] = resid[at, :] * keep
        return carry

    tiles = windows // tile
    part_tile = windows // 2

    def prepare_all():
        for load in loads:
            load.wait()
        lax.fori_loop(0, tiles, prepare, 0)
        pad[...] = jnp.zeros_like(pad)
        lax.fori_loop(0, windows // 128, prepare_mask, 0)

    def matrix(b, m):
        return wg[b, m].reshape(hidden, hidden)

    def small(b, lane):
        return wg[b, 0, :, :, :, :, lane : lane + 128].reshape(hidden, 128)

    def store_layer(b, k, at, v):
        p = 1.0 + jnp.tanh(v)
        a = v * p
        rate = p + a * (2.0 - p)
        slope[b, k, at, :] = rate.astype(BF)
        low = a.astype(BF)
        act_t[b, k, :, at] = low.T
        return low

    def halves(body):
        for t in range(2):
            body(slice(t * windows // 2, (t + 1) * windows // 2))

    def layer_zero(b):
        bias_t[...] = small(b, 128).astype(F32).T

        def body(at):
            a = resid[at, :].astype(BF)
            in_t[b, :, at] = a.T
            work[0, at, :] = store_layer(b, 0, at, dot_nt(a, small(b, 0)) + bias_t[span : span + 1, :])

        halves(body)

    def layer_next(b, k):
        source, target = lax.rem(k + 1, 2), lax.rem(k, 2)
        v = dot_nn(work[source], matrix(b, k)) + bias_t[pl.ds(span + k, 1), :]
        work[target] = store_layer(b, k, slice(0, windows), v)

    def grid(value):
        return value.astype(BF).reshape(ZN, YN, XN, rows, -1)

    def backcast_step():
        def body(at):
            theta = dot_nn(work[1, at, :], matrix(0, 4)).astype(BF)
            theta_keep[at, :] = theta
            resid[at, :] = (resid[at, :] - dot_nn(theta, small(0, 256))) * mask[at, :].astype(F32)

        halves(body)

    def put_rows(buf, b, at, value):
        for row in range(value.shape[0]):
            buf[b, row, :, at] = value[row : row + 1]

    def late_theta(b, m):
        theta_t = act_t.at[1, 0]
        theta_t[...] = dot_nn(matrix(b, m).T, act_t[b, 3]).astype(BF)

        @pl.when(m == 4)
        def _():
            gp[b, 0, :, :, :, :, 256:384] = grid(dot_nt(theta_t[...], e_t[b]))

        @pl.when(m == 5)
        def _():
            grad = grid(dot_nn(theta_t[...], f_ref[...]))
            gp[b, 0, :, :, :, :, 128:256] = gp[b, 0, :, :, :, :, 128:256] + grad
            part_t[b] = dot_nn(small(b, 128).T, theta_t[...])[0:span]

    def forecasts():
        put_rows(pred, 0, slice(0, windows), part_t[0])
        put_rows(pred, 1, slice(0, windows), part_t[0].astype(BF).astype(F32) + part_t[1])

    count = 2 * MATS

    def delayed(lag, t, step):
        pl.when(jnp.logical_and(t >= lag, t < count + lag))(lambda: step(t - lag))

    def staged(lag, t, step):
        early = t - lag + 1
        pl.when(jnp.logical_and(early >= (2 if lag == 2 else 1), early <= 2))(lambda: mine(early, step))
        unit = t - lag
        pl.when(jnp.logical_and(unit >= 3, unit < count))(lambda: mine(unit, step))
        if lag == 6:
            pl.when(t == 3)(lambda: mine(0, step))

    def gather_line(i):
        b, m = of(i)

        pl.when(b == core)(lambda: by_lanes(m, lambda lanes: start_all(z_copies(i, lanes))))

    def gather_columns(i):
        b, m = of(i)

        def step(lanes):
            pl.when(b != core)(lambda: hand_over(m, lanes).wait_recv())
            for copy in z_copies(i, lanes):
                copy.wait_recv()
            start_all(column_copies(i, lanes))

        by_lanes(m, step)

    def gather_corner(i):
        def step(lanes):
            column_copies(i, lanes)[0].wait_recv()
            corner_copy(i, lanes).start()

        by_lanes(of(i)[1], step)

    def gather_core(i):
        def step(lanes):
            column_copies(i, lanes)[1].wait_recv()
            corner_copy(i, lanes).wait_recv()
            core_copy(i, lanes).start()

        by_lanes(of(i)[1], step)

    def arrived(i):
        pl.when(lax.rem(i, 2) != core)(lambda: by_lanes(of(i)[1], lambda lanes: core_copy(i, lanes).wait_recv()))

    def forward_unit(i):
        arrived(i)
        b, m = of(i)
        pl.when(m == 0)(lambda: layer_zero(b))
        pl.when(jnp.logical_and(m >= 1, m <= 3))(lambda: layer_next(b, m))
        pl.when(m == 4)(backcast_step)

        pl.when(i == 8)(lambda: mine(10, gather_core))

        @pl.when(jnp.logical_or(i == 4, i == 8))
        def _():
            pl.when(b == 1)(lambda: feed(b))
            pl.when(b == 0)(lambda: feed_forward(b))
            lax.fori_loop(jnp.where(b == 1, 4, 5), MATS, lambda n, carry: (theta_grad(b, n), carry)[1], 0)
            pl.when(b == 0)(lambda: scatter_start(0))

            @pl.when(b == 1)
            def _():
                scatter_start(1)
                scatter_start(2)

    def gather_step(t, carry):
        pl.when(t == 12)(lambda: mine(0, scatter_core))
        pl.when(t == 15)(lambda: mine(0, scatter_diag))
        pl.when(jnp.logical_and(t >= 4, t != 14))(lambda: mine(t - 4, gather_core))
        delayed(2, t, lambda i: mine(i, gather_corner))
        delayed(0, t, lambda i: mine(i, gather_columns))
        pl.when(t + 4 < count)(lambda: gather_line(t + 4))
        pl.when(t == 0)(prepare_all)
        pl.when(jnp.logical_and(t >= 5, t < 14))(lambda: forward_unit(t - 5))
        return carry

    def out_copies(buf, out, s):
        at = pl.ds(row0, windows)
        return [
            pltpu.make_async_copy(buf.at[core], out.at[:, :, at], local_sem.at[2 + s]),
            remote(buf.at[other], out.at[:, :, at], out_send.at[s], out_recv.at[s], sibling),
        ]


    def back_of(j):
        b = jnp.where(jnp.logical_or(jnp.logical_and(j >= 1, j <= 5), j == 11), 1, 0)
        early = jnp.where(j == 1, 4, jnp.where(j <= 2, 5, 6 - j))
        return b, jnp.where(j <= 5, early, jnp.where(j == 6, 4, jnp.where(j <= 9, 10 - j, 0)))

    def slot_of(j):
        return lax.rem(lax.div(j, 2), SLOTS)

    def to_core(j, lanes):
        b, m = back_of(j)
        return remote(
            gp.at[b, m, :, :, :, :, lanes], from_core.at[slot_of(j), :, :, :, :, lanes],
            sends(rs_send, 3, lanes), rs_recv.at[j, 0], sibling,
        )

    def to_far(j, lanes):
        b, m = back_of(j)
        device = chip(z, far_y, far_x)
        return [
            remote(
                gp.at[b, m, :, yo, xo, :, lanes], from_diag.at[slot_of(j), :, :, lanes],
                sends(rs_send, 1, lanes), rs_recv.at[j, 1], device,
            ),
            remote(
                gp.at[b, m, :, far_y, far_x, :, lanes], from_plain.at[slot_of(j), :, :, lanes],
                sends(rs_send, 1, lanes), rs_recv.at[j, 2], device,
            ),
        ]

    def to_near(j, lanes):
        b, m = back_of(j)
        return remote(
            gp.at[b, m, :, near_y, near_x, :, lanes], from_pair.at[slot_of(j), :, :, lanes],
            sends(rs_send, 2, lanes), rs_recv.at[j, 3], chip(z, near_y, near_x),
        )

    def to_z(j, lanes):
        b, m = back_of(j)
        return [
            remote(
                gp.at[b, m, zi, y, x, :, lanes], from_z.at[lax.div(j, 2), s, :, lanes],
                sends(rs_send, 0, lanes), rs_recv.at[j, 4 + s], chip(zi, y, x),
            )
            for s, zi in enumerate(z_peers)
        ]

    def to_owner(m):
        return remote(total.at[m], grad_out.at[m], total_send.at[m], total_recv.at[m], sibling)

    def scatter_start(j):
        pl.when(lax.rem(j, 2) != core)(lambda: by_lanes(back_of(j)[1], lambda lanes: to_core(j, lanes).start()))

    def scatter_core(j):
        b, m = back_of(j)

        def step(lanes):
            to_core(j, lanes).wait_recv()
            gp[b, m, :, :, :, :, lanes] = gp[b, m, :, :, :, :, lanes] + from_core[slot_of(j), :, :, :, :, lanes]
            start_all(to_far(j, lanes))

        by_lanes(m, step)

    def scatter_diag(j):
        b, m = back_of(j)

        def step(lanes):
            to_far(j, lanes)[0].wait_recv()
            part = gp[b, m, :, near_y, near_x, :, lanes] + from_diag[slot_of(j), :, :, lanes]
            gp[b, m, :, near_y, near_x, :, lanes] = part
            to_near(j, lanes).start()

        by_lanes(m, step)

    def scatter_plane(j):
        b, m = back_of(j)

        def step(lanes):
            to_far(j, lanes)[1].wait_recv()
            to_near(j, lanes).wait_recv()
            value = gp[b, m, :, y, x, :, lanes].astype(F32)
            value = value + from_plain[slot_of(j), :, :, lanes].astype(F32)
            value = value + from_pair[slot_of(j), :, :, lanes].astype(F32)
            gp[b, m, :, y, x, :, lanes] = value.astype(BF)
            start_all(to_z(j, lanes))

        by_lanes(m, step)

    def scatter_z(j):
        b, m = back_of(j)

        def step(lanes):
            for copy in to_z(j, lanes):
                copy.wait_recv()
            value = gp[b, m, z, y, x, :, lanes].astype(F32)
            for s in range(ZN - 1):
                value = value + from_z[lax.div(j, 2), s, :, lanes].astype(F32)
            squares[:, lanes] = squares[:, lanes] + value * value

            @pl.when(b == core)
            def _():
                grad_out[m, :, lanes] = value

            @pl.when(b != core)
            def _():
                total[m, :, lanes] = value

        by_lanes(m, step)
        pl.when(b != core)(lambda: to_owner(m).start())

    def add_rows(value):
        return jnp.sum(value.reshape(-1, 8, hidden), axis=0)

    def put_bias(k, acc):
        bias_sum[pl.ds(span + k, 1), :] = jnp.sum(acc, axis=0, keepdims=True)

    def feed(b):
        pl.when(b == 1)(lambda: resid.__setitem__(..., jnp.zeros_like(resid)))
        e = (-(resid[...] * mask[...].astype(F32))).astype(BF)
        e_t[b] = e.T
        work[0] = dot_nt(e, small(b, 256)).astype(BF)
        work[2] = dot_nt(f_ref[...], small(b, 128)).astype(BF)

    def feed_forward(b):
        work[2] = dot_nt(f_ref[...], small(b, 128)).astype(BF)

    def put_dz(b, k, da):
        dz = da * slope[b, k].astype(F32)
        work[k % 2 if isinstance(k, int) else lax.rem(k, 2)] = dz.astype(BF)
        bias_sum[pl.ds(span + k, 1), :] = jnp.sum(add_rows(dz), axis=0, keepdims=True)

    def theta_step(b):
        put_dz(b, 3, 0.5 * (dot_nt(work[0], matrix(b, 4)) + dot_nt(work[2], matrix(b, 5))))

    def layer_back(b, k):
        source = lax.rem(k, 2)
        gp[b, k] = grid(dot_nn(act_t[b, k - 1], work[source]))
        put_dz(b, k - 1, dot_nt(work[source], matrix(b, k)))

    def theta_grad(b, m):
        gp[b, m] = grid(dot_nn(act_t[b, 3], work[jnp.where(m == 4, 0, 2)]))

    def first_grads(b):
        gp[b, 0, :, :, :, :, 0:128] = grid(dot_nn(in_t[b], work[0]).T)
        gp[b, 0, :, :, :, :, 128:256] = grid(bias_sum[...].T)
        pl.when(b == 0)(backcast_grad)

    def backcast_grad():
        gp[0, 0, :, :, :, :, 256:384] = grid(dot_nn(e_t[0], theta_keep[...]).T)

    def input_grad(b):
        for t in range(2):
            at = slice(t * windows // 2, (t + 1) * windows // 2)
            keep = mask[at, :].astype(F32)
            dr = resid[at, :] * keep + 2.0 * dot_nn(work[0, at, :], small(b, 0))

            @pl.when(b == 1)
            def _():
                seg[at, :] = dr[:, 0:past]
                resid[at, :] = dr.astype(BF).astype(F32)

            @pl.when(b == 0)
            def _():
                put_rows(sens, 0, at, (dr * keep).T[0:past])

    def late_rows():
        for g in range(windows // 128):
            at = slice(g * 128, (g + 1) * 128)
            pad[:, 0:past] = seg[at, :]
            put_rows(sens, 1, at, pad[...].T[0:past])

    bias_sum[...] = jnp.zeros_like(bias_sum)
    squares[...] = jnp.zeros_like(squares)

    def back_step(j, carry):
        b, m = back_of(j)

        staged(6, j, scatter_plane)
        staged(4, j, scatter_diag)
        staged(2, j, scatter_core)

        @pl.when(j == 2)
        def _():
            arrived(9)
            arrived(10)
            theta_step(1)
            mine(1, scatter_core)

        pl.when(jnp.logical_and(m >= 1, m <= 3))(lambda: layer_back(b, m))

        @pl.when(jnp.logical_or(j == 6, j == 10))
        def _():
            block = jnp.where(j == 6, 1, 0)
            first_grads(block)
            pl.when(j == 6)(lambda: input_grad(1))

        @pl.when(j == 6)
        def _():
            feed(0)
            theta_grad(0, 4)

        @pl.when(jnp.logical_or(j == 10, j == 11))
        def _():
            lax.fori_loop(jnp.where(j == 11, 4, 5), MATS, lambda n, carry: (late_theta(b, n), carry)[1], 0)

        pl.when(jnp.logical_and(j >= 3, j < count))(lambda: scatter_start(j))

        @pl.when(j == 6)
        def _():
            arrived(11)
            theta_step(0)

        @pl.when(j == count)
        def _():
            input_grad(0)
            forecasts()
            start_all(out_copies(pred, pred_out, 0))

        @pl.when(j == count + 1)
        def _():
            late_rows()
            start_all(out_copies(sens, sens_out, 1))

        pl.when(j >= count + 1)(lambda: scatter_z(2 * (j - count - 1) + core))
        return carry

    gather_line(0)
    for m in range(1, MATS):
        pack(m)
        if m < 4:
            gather_line(m)
        if m % 2:
            hand_over(m, slice(0, hidden)).start()
    lax.fori_loop(0, count + 4, gather_step, 0)
    lax.fori_loop(2, count + 7, back_step, 0)

    sq = squares[:, 0:128] + squares[:, 128:256] + squares[:, 256:384] + squares[:, 384:512]
    place = (y * XN + x) * 2 + core
    norm_buf[place] = sum(sq[n : n + 8] for n in range(0, rows, 8))

    def spread(sources, targets, first):
        copies = [
            remote(norm_buf.at[sources], norm_buf.at[sources], norm_send.at[first + s], norm_recv.at[first + s], device)
            for s, device in enumerate(targets)
        ]
        start_all(copies)
        for copy in copies:
            copy.wait()

    def add_up(slots):
        value = norm_buf[slots[0]]
        for slot in slots[1:]:
            value = value + norm_buf[slot]
        return value

    spread(place, plane_peers, 0)
    norm_buf[8 + z] = add_up(range(8))
    spread(8 + z, [chip(zi, y, x) for zi in z_peers], 7)
    everything = add_up(range(8, 8 + ZN))
    norm_out[...] = jnp.broadcast_to(jnp.sqrt(jnp.sum(everything, keepdims=True)), norm_out.shape)

    for block, matrices in ((0, (1, 3)), (1, (2, 5))):
        for m in matrices:
            pl.when(core == block)(to_owner(m).wait_recv)
            pl.when(core != block)(to_owner(m).wait_send)
    for buf, out, s in ((pred, pred_out, 0), (sens, sens_out, 1)):
        for copy in out_copies(buf, out, s):
            copy.wait()
    for m in range(1, MATS, 2):
        hand_over(m, slice(0, hidden)).wait_send()

    for mats, lanes in ((slice(1, MATS), slice(0, hidden)), (slice(0, 1), slice(0, 384))):
        sent = (
            wg.at[0, mats, 0 : ZN - 1, 0, 0, :, lanes],
            wg.at[0, mats, :, :, 0, :, lanes],
            wg.at[0, mats, :, 0, 0, :, lanes],
            wg.at[0, mats, :, :, :, :, lanes],
        )
        for sems in (ag_send, rs_send):
            for kind, ref in enumerate(sent):
                remote(ref, ref, sends(sems, kind, lanes), out_recv.at[0], sibling).wait_send()


def train_call(plane, segments, extents, adjoint, first, square, head, biases):
    ZN, YN, XN = plane
    past, span, hidden = segments.shape[1], adjoint.shape[0], square.shape[3]
    windows = segments.shape[0] // 2
    tile = windows
    rows = hidden // (ZN * YN * XN)
    sizes = (ZN, YN, XN, windows, tile, past, span, hidden)
    DMA = pltpu.SemaphoreType.DMA
    vmem = pl.BlockSpec(memory_space=pltpu.VMEM)
    hbm = pl.BlockSpec(memory_space=pl.ANY)
    count = 2 * MATS
    flops = 2 * 2 * 3 * windows * hidden * (6 * hidden + 2 * 128)
    lengths = extents.reshape(-1, 128)
    return pl.pallas_call(
        functools.partial(train_kernel, sizes),
        out_shape=(
            jax.ShapeDtypeStruct((span, 1, 2 * windows), F32),
            jax.ShapeDtypeStruct((past, 1, 2 * windows), F32),
            jax.ShapeDtypeStruct((MATS, rows, hidden), F32),
            jax.ShapeDtypeStruct((8, 128), F32),
        ),
        in_specs=[hbm] * 7,
        out_specs=(hbm, hbm, vmem, vmem),
        scratch_shapes=[
            pltpu.VMEM((2, MATS, ZN, YN, XN, rows, hidden), BF),
            pltpu.VMEM((MATS, rows, hidden), BF),
            pltpu.VMEM((2, MATS, ZN, YN, XN, rows, hidden), BF),
            pltpu.VMEM((SLOTS, ZN, YN, XN, rows, hidden), BF),
            pltpu.VMEM((SLOTS, ZN, rows, hidden), BF),
            pltpu.VMEM((SLOTS, ZN, rows, hidden), BF),
            pltpu.VMEM((SLOTS, ZN, rows, hidden), BF),
            pltpu.VMEM((MATS, ZN - 1, rows, hidden), BF),
            pltpu.VMEM((MATS, rows, hidden), F32),
            pltpu.VMEM((2, 4, hidden, windows), BF),
            pltpu.VMEM((2, 128, windows), BF),
            pltpu.VMEM((windows, hidden), BF),
            pltpu.VMEM((2, 4, windows, hidden), BF),
            pltpu.VMEM((3, windows, hidden), BF),
            pltpu.VMEM((windows, 128), F32),
            pltpu.VMEM((windows, 128), BF),
            pltpu.VMEM((windows, 128), BF),
            pltpu.VMEM((2, 128, windows), BF),
            pltpu.VMEM((128, hidden), F32),
            pltpu.VMEM((128, hidden), F32),
            pltpu.VMEM((128, 128), F32),
            pltpu.VMEM((windows, past), F32),
            pltpu.VMEM((span, windows), F32),
            *(pltpu.VMEM(a.shape, a.dtype) for a in (lengths, first, square, head, biases)),
            pltpu.VMEM((2, span, windows), F32),
            pltpu.VMEM((2, span, 1, windows), F32),
            pltpu.VMEM((2, past, 1, windows), F32),
            pltpu.VMEM((rows, hidden), F32),
            pltpu.VMEM((8 + ZN, 8, 128), F32),
            DMA((MATS,)),
            DMA((MATS,)),
            DMA((4, 2)),
            DMA((count, 4 + ZN - 1)),
            DMA((4, 2)),
            DMA((count, 4 + ZN - 1)),
            DMA((2,)),
            DMA((2,)),
            DMA((MATS,)),
            DMA((MATS,)),
            DMA((9,)),
            DMA((7 + ZN - 1,)),
            DMA((7 + ZN - 1,)),
        ],
        compiler_params=pltpu.CompilerParams(
            collective_id=0, has_side_effects=True, vmem_limit_bytes=64 * 1024 * 1024
        ),
        cost_estimate=pl.CostEstimate(flops=flops, bytes_accessed=8_000_000, transcendentals=8 * windows * hidden),
        name="train",
    )(segments, adjoint, lengths, first, square, head, biases)


def update_kernel(past, span, *refs):
    sources, targets, norm_out = refs[0:16], refs[16:34], refs[34]
    held, results, pad, in_sem, out_sem = refs[35:51], refs[51:67], *refs[67:70]
    arriving = [pltpu.make_async_copy(source, ref, in_sem.at[n]) for n, (source, ref) in enumerate(zip(sources, held))]
    leaving = [
        pltpu.make_async_copy(ref, target, out_sem.at[n]) for n, (ref, target) in enumerate(zip(held[0:2] + results, targets))
    ]
    for copy in arriving:
        copy.start()
    grads, norm, masters, momenta, variances = held[2], held[3], held[4:8], held[8:12], held[12:16]
    units = masters[3].shape[2]

    def rows(m, lane, width):
        return grads[m, :, lane : lane + width]

    arriving[2].wait()
    arriving[3].wait()
    norm_out[...] = norm[0:1, 0:1]
    factor = 1.0 / jnp.maximum(norm[0:1, 0:1], 1.0)
    for m in range(5):
        results[1][0, m] = rows(m + 1, 0, grads.shape[2])
    results[0][0] = rows(0, 0, 128)[:, 0:past]
    forecast = rows(0, 128, 128)
    pad[...] = jnp.zeros_like(pad)
    pad[0:units, :] = forecast
    results[3][0] = pad[...].T[span : span + 4, 0:units]
    results[2][0, :, 0:past] = rows(0, 256, 128)[:, 0:past]
    results[2][0, :, past : past + span] = forecast[:, 0:span]
    for n in (0, 1):
        arriving[n].wait()
        leaving[n].start()
    for n in (1, 0, 2, 3):
        leaving[2 + n].start()
        for state in range(3):
            arriving[4 + 4 * state + n].wait()
        updated = adamw(masters[n][...], results[n][...], momenta[n][...], variances[n][...], factor[None])
        for kind, value in enumerate(updated):
            results[4 * (kind + 1) + n][...] = value
            leaving[2 + 4 * (kind + 1) + n].start()
    for copy in leaving:
        copy.wait()


def update_call(prediction, sensitivity, grads, norm, state):
    hbm = pl.BlockSpec(memory_space=pl.ANY)
    sources = (prediction, sensitivity, grads, norm, *state)
    targets = (prediction, sensitivity, *(4 * list(state[:4])))
    return pl.pallas_call(
        functools.partial(update_kernel, sensitivity.shape[0], prediction.shape[0]),
        out_shape=tuple(jax.ShapeDtypeStruct(a.shape, F32) for a in targets) + (jax.ShapeDtypeStruct((1, 1), F32),),
        in_specs=[hbm] * len(sources),
        out_specs=tuple([hbm] * len(targets) + [pl.BlockSpec(memory_space=pltpu.VMEM)]),
        scratch_shapes=[pltpu.VMEM(a.shape, F32) for a in sources]
        + [pltpu.VMEM(a.shape, F32) for a in targets[2:]]
        + [pltpu.VMEM((128, 128), F32), pltpu.SemaphoreType.DMA((len(sources),)), pltpu.SemaphoreType.DMA((len(targets),))],
        name="update",
    )(*sources)


def turned(arrays):
    return [a.transpose(0, 2, 1) if n % 4 == 0 else a for n, a in enumerate(arrays)]


def kernel_shards(plane, segments, extents, adjoint, *state):
    state = turned(state)
    results = train_call(plane, segments, extents, adjoint.T, *state[:4])
    prediction, sensitivity, *updated, norm = update_call(*results, state)
    by_window = (prediction.transpose(1, 2, 0), sensitivity.transpose(1, 2, 0))
    return (*by_window, norm.reshape(()), *turned(updated))


STATE_SPECS = (
    P("section", None, "dp"),
    P("section", None, "dp", None),
    P("section", "dp", None),
    P("section", None, "dp"),
)


def solution(mesh):
    in_specs = (P("dp", None), P("dp"), P("dp", None)) + 3 * STATE_SPECS
    out_specs = (P("section", "dp", None), P("section", "dp", None), P()) + 4 * STATE_SPECS
    plane = PLANES.get(mesh.shape["dp"])
    shards = plain_shards if plane is None else functools.partial(kernel_shards, plane)
    return jax.shard_map(shards, mesh=mesh, in_specs=in_specs, out_specs=out_specs, check_vma=False)
```

```python
import functools

import jax
import jax.numpy as jnp
from jax import lax
from jax.experimental import pallas as pl
from jax.experimental.pallas import tpu as pltpu
from jax.sharding import PartitionSpec as P

STEP = 10


def dot_nn(a, b):
    return jnp.dot(a, b, preferred_element_type=jnp.float32)


def dot_tn(a, b):
    return lax.dot_general(a, b, (((0,), (0,)), ((), ())), preferred_element_type=jnp.float32)


def dot_nt(a, b):
    return lax.dot_general(a, b, (((1,), (1,)), ((), ())), preferred_element_type=jnp.float32)


def unit_rows(first, square, head, biases):
    units = first.shape[1]
    return jnp.concatenate(
        [square.transpose(1, 0, 2).reshape(units, -1), first.T, head, biases.T], axis=1
    )


def from_unit_rows(rows, past, hidden, out):
    wide = 5 * hidden
    square = rows[:, :wide].reshape(-1, 5, hidden).transpose(1, 0, 2)
    first = rows[:, wide : wide + past].T
    head = rows[:, wide + past : wide + past + out]
    biases = rows[:, wide + past + out :].T
    return first, square, head, biases


def plain_forward(weights, resid):
    first, square, head, biases = weights
    past = resid.shape[1]
    acts, slopes = [resid.astype(jnp.bfloat16)], []
    for k in range(4):
        z = dot_nn(acts[-1], first if k == 0 else square[k - 1]) + biases[k].astype(jnp.float32)
        sig = jax.nn.sigmoid(z)
        acts.append((z * sig).astype(jnp.bfloat16))
        slopes.append(sig * (1.0 + z * (1.0 - sig)))
    theta_b = dot_nn(acts[4], square[3]).astype(jnp.bfloat16)
    theta_f = dot_nn(acts[4], square[4]).astype(jnp.bfloat16)
    backcast = dot_nn(theta_b, head[:, :past])
    part = dot_nn(theta_f, head[:, past:])
    return backcast, part, (acts, slopes, theta_b, theta_f)


def plain_backward(weights, saved, e, f):
    first, square, head, biases = weights
    acts, slopes, theta_b, theta_f = saved
    past = e.shape[1]
    head_grad = jnp.concatenate([dot_tn(theta_b, e), dot_tn(theta_f, f)], axis=1)
    u_b = dot_nt(e, head[:, :past]).astype(jnp.bfloat16)
    u_f = dot_nt(f, head[:, past:]).astype(jnp.bfloat16)
    squares = [None, None, None, dot_tn(acts[4], u_b), dot_tn(acts[4], u_f)]
    da = dot_nt(u_b, square[3]) + dot_nt(u_f, square[4])
    bias_grads = [None] * 4
    first_grad = None
    for k in (3, 2, 1, 0):
        dz = (da * slopes[k]).astype(jnp.bfloat16)
        bias_grads[k] = jnp.sum(dz, axis=0, dtype=jnp.float32)
        grad = dot_tn(acts[k], dz)
        if k == 0:
            first_grad = grad
        else:
            squares[k - 1] = grad
        da = dot_nt(dz, first if k == 0 else square[k - 1])
    return da, (first_grad, jnp.stack(squares), head_grad, jnp.stack(bias_grads))


def adamw(master, gradient, momentum, variance, factor):
    clipped = gradient * factor
    moment_new = 0.9 * momentum + 0.1 * clipped
    variance_new = 0.999 * variance + 0.001 * clipped * clipped
    ratio = moment_new / (1.0 - 0.9**STEP) / (jnp.sqrt(variance_new / (1.0 - 0.999**STEP)) + 1e-08)
    return master - 0.05 * (ratio + 0.01 * master), moment_new, variance_new


def plain_shards(segments, extents, adjoint, *state):
    masters, momenta, variances = state[:4], state[4:8], state[8:]
    core = lax.axis_index("section")
    past, span = segments.shape[1], adjoint.shape[1]
    windows = segments.shape[0] // 2
    hidden = masters[1].shape[3]
    mine = [
        lax.dynamic_slice_in_dim(v, core * windows, windows, 0) for v in (segments, extents, adjoint)
    ]
    seg, ext, adj = mine
    rows = unit_rows(*(m[0].astype(jnp.bfloat16) for m in masters))
    rows = lax.all_gather(rows, "dp", axis=0, tiled=True)
    rows = lax.all_gather(rows, "section", axis=0)
    blocks = [from_unit_rows(rows[b], past, hidden, past + span) for b in range(2)]
    mask = (
        lax.broadcasted_iota(jnp.int32, (windows, past), 1) >= past - ext[:, None]
    ).astype(jnp.float32)
    r0 = seg * mask
    backcast, part0, saved0 = plain_forward(blocks[0], r0)
    r1 = (r0 - backcast) * mask
    _, part1, saved1 = plain_forward(blocks[1], r1)
    forecast = part0.astype(jnp.bfloat16).astype(jnp.float32) + part1
    f = adj.astype(jnp.bfloat16)
    zero = jnp.zeros_like(r0)
    da1, grads1 = plain_backward(blocks[1], saved1, (-(zero * mask)).astype(jnp.bfloat16), f)
    dr1 = zero * mask + da1
    t = dr1.astype(jnp.bfloat16).astype(jnp.float32)
    da0, grads0 = plain_backward(blocks[0], saved0, (-(t * mask)).astype(jnp.bfloat16), f)
    dr0 = (t * mask + da0) * mask

    def by_section(first_block, second_block):
        mine, other = (
            jnp.where(core == 0, first_block, second_block),
            jnp.where(core == 0, second_block, first_block),
        )
        got = lax.ppermute(other, "section", [(0, 1), (1, 0)])
        return jnp.where(
            core == 0, jnp.concatenate([mine, got]), jnp.concatenate([got, mine])
        )[None]

    prediction = by_section(part0, forecast)
    sensitivity = by_section(dr0, dr1)
    packed = jnp.stack([unit_rows(*grads0), unit_rows(*grads1)])
    packed = lax.psum_scatter(packed, "section", scatter_dimension=0, tiled=False)
    packed = lax.psum_scatter(packed, "dp", scatter_dimension=0, tiled=True)
    norm = jnp.sqrt(lax.psum(jnp.sum(packed * packed), ("section", "dp")))
    factor = 1.0 / jnp.maximum(norm, 1.0)
    summed = [g[None] for g in from_unit_rows(packed, past, hidden, past + span)]
    updated = [adamw(*four, factor) for four in zip(masters, summed, momenta, variances)]
    return (
        prediction,
        sensitivity,
        norm,
        *summed,
        *(u[0] for u in updated),
        *(u[1] for u in updated),
        *(u[2] for u in updated),
    )


PLANES = {16: (4, 2, 2)}
MESH = pl.DeviceIdType.MESH
MATS = 6
CORE_SLOTS, DIAG_SLOTS, PLAIN_SLOTS, PAIR_SLOTS = 4, 4, 6, 4
BF, F32 = jnp.bfloat16, jnp.float32


ORDER = ((0, 5), (1, 4), (1, 5), (1, 3), (1, 2), (1, 1), (0, 4), (0, 3), (0, 2), (0, 1), (1, 0), (0, 0))


def remote(src, dst, send_sem, recv_sem, device):
    return pltpu.make_async_remote_copy(
        src_ref=src, dst_ref=dst, send_sem=send_sem, recv_sem=recv_sem, device_id=device, device_id_type=MESH
    )


def train_kernel(
    sizes,
    seg_hbm, adj_hbm, ext_hbm, first_hbm, square_hbm, head_hbm, biases_hbm,
    pred_out, sens_out, grad_out, norm_out,
    wg, handed, gp, from_core, from_diag, from_plain, from_pair, from_z, total,
    act_t, in_t, theta_keep, slope, work, resid, mask, f_ref, e_t, bias_t, bias_sum, pad,
    seg, adj, ext, first, square, head, biases, part_t, pred, sens, squares, norm_buf,
    own_send, own_recv, ag_send, ag_recv, rs_send, rs_recv, out_send, out_recv, local_sem, norm_send, norm_recv,
):
    ZN, YN, XN, windows, tile, past, span, hidden = sizes
    units = ZN * YN * XN
    core, dp = lax.axis_index("section"), lax.axis_index("dp")
    x, y, z = lax.rem(dp, XN), lax.rem(lax.div(dp, XN), YN), lax.div(dp, XN * YN)
    other, xo, yo = 1 - core, 1 - x, 1 - y
    near_y, near_x = y + core * (yo - y), xo + core * (x - xo)
    far_y, far_x = yo + core * (y - yo), x + core * (xo - x)

    def chip(zi, yi, xi):
        return (core, (zi * YN + yi) * XN + xi)

    sibling = (other, dp)
    z_peers = [lax.rem(z + step, ZN) for step in range(1, ZN)]

    row0 = core * windows
    loads = [
        pltpu.make_async_copy(seg_hbm.at[pl.ds(row0, windows), :], seg, local_sem.at[0]),
        pltpu.make_async_copy(adj_hbm.at[:, pl.ds(row0, windows)], adj, local_sem.at[1]),
    ]
    small_loads = [
        pltpu.make_async_copy(source, target, local_sem.at[4 + n])
        for n, (source, target) in enumerate(
            [(square_hbm, square), (first_hbm, first), (head_hbm, head), (biases_hbm, biases), (ext_hbm, ext)]
        )
    ]
    for load in small_loads + loads:
        load.start()

    barrier = pltpu.get_barrier_semaphore()
    plane_peers = [
        (ci, (z * YN + yi) * XN + xi) for ci in (core, other) for yi in (y, yo) for xi in (x, xo)
    ][1:]
    peers = plane_peers + [(ci, (zi * YN + y) * XN + x) for zi in z_peers for ci in (core, other)]
    for peer in peers:
        pl.semaphore_signal(barrier, inc=1, device_id=peer, device_id_type=MESH)

    rows = hidden // units
    half_rows = rows // 2

    def put_own(m, value, lanes):
        halves = value.astype(BF).reshape(2, half_rows, -1)
        for h in range(2):
            pl.when(core == h)(functools.partial(put_half, m, halves[h], halves[1 - h], lanes))

    def put_half(m, kept, given, lanes):
        wg[core, m, z, y, x, core, :, lanes] = kept
        handed[m, :, lanes] = given

    for load in small_loads:
        load.wait()
    pad[...] = jnp.zeros_like(pad)
    pad[0:rows, 0:past] = first[0] * 0.5
    put_own(0, pad[0:rows, :], slice(0, 128))
    pad[...] = jnp.zeros_like(pad)
    pad[span : span + 4, 0:rows] = biases[0] * 0.5
    bias_cols = pad[...].T[0:rows]
    pad[...] = jnp.zeros_like(pad)
    pad[0:rows, 0:span] = head[0, :, past : past + span]
    put_own(0, pad[0:rows, :] + bias_cols, slice(128, 256))
    pad[...] = jnp.zeros_like(pad)
    pad[0:rows, 0:past] = head[0, :, 0:past]
    put_own(0, pad[0:rows, :], slice(256, 384))
    pl.semaphore_wait(barrier, len(peers))

    def hand_over(m, lanes):
        return remote(
            handed.at[m, :, lanes], wg.at[core, m, z, y, x, other, :, lanes], own_send.at[m], own_recv.at[m], sibling
        )

    def pack(m):
        put_own(m, square[0, m - 1] * 0.5 if m < 4 else square[0, m - 1], slice(0, hidden))


    def of(i):
        b = jnp.where(jnp.logical_and(i >= 5, i <= 10), 1, 0)
        return b, jnp.where(i <= 4, i, jnp.where(i <= 10, i - 5, 5))

    def sends(sems, kind, lanes):
        return sems.at[kind, 0 if lanes.stop == hidden else 1]

    def z_copies(i, lanes):
        b, m = of(i)
        part = wg.at[b, m, z, y, x, core, :, lanes]
        return [
            remote(part, part, sends(ag_send, 0, lanes), ag_recv.at[i, s], chip(zi, y, x)) for s, zi in enumerate(z_peers)
        ]

    def line_copies(i, lanes):
        b, m = of(i)
        given = wg.at[b, m, z, y, x, other, :, lanes]
        return [
            remote(
                handed.at[m, :, lanes], given, sends(ag_send, 0, lanes), ag_recv.at[i, s], (other, (zi * YN + y) * XN + x)
            )
            for s, zi in enumerate(z_peers)
        ]

    def column_copies(i, lanes):
        b, m = of(i)
        part = wg.at[b, m, :, y, x, core, :, lanes]
        return [
            remote(part, part, sends(ag_send, 1, lanes), ag_recv.at[i, 3], chip(z, near_y, near_x)),
            remote(part, part, sends(ag_send, 1, lanes), ag_recv.at[i, 4], chip(z, far_y, far_x)),
        ]

    def corner_copy(i, lanes):
        b, m = of(i)
        part = wg.at[b, m, :, near_y, near_x, core, :, lanes]
        return remote(part, part, sends(ag_send, 2, lanes), ag_recv.at[i, 5], chip(z, far_y, far_x))

    def core_copy(i, lanes):
        b, m = of(i)
        part = wg.at[b, m, :, :, :, core, :, lanes]
        return remote(part, part, sends(ag_send, 3, lanes), ag_recv.at[i, 6], sibling)

    def by_lanes(m, step):
        if isinstance(m, int):
            step(slice(0, hidden if m else 384))
            return
        pl.when(m == 0)(lambda: step(slice(0, 384)))
        pl.when(m > 0)(lambda: step(slice(0, hidden)))

    def start_all(copies):
        for copy in copies:
            copy.start()

    zeros_tile = jnp.zeros((tile, 128), F32)

    def prepare(t, carry):
        at = pl.ds(t * tile, tile)
        resid[at, :] = zeros_tile
        resid[at, 0:past] = seg[at, :]
        return carry

    def prepare_mask(g, carry):
        lengths = ext[pl.ds(core * (windows // 128) + g, 1), :]
        position = lax.broadcasted_iota(jnp.int32, (128, 128), 0)
        keep = jnp.where(position >= past - lengths, 1.0, 0.0).astype(F32).T
        at = pl.ds(pl.multiple_of(g * 128, 128), 128)
        pad[0:span, :] = adj[:, at]
        f_ref[at, :] = pad[...].T.astype(BF)
        mask[at, :] = keep.astype(BF)
        resid[at, :] = resid[at, :] * keep
        return carry

    tiles = windows // tile
    part_tile = windows // 2

    def matrix(b, m):
        return wg[b, m].reshape(hidden, hidden)

    def small(b, lane):
        return wg[b, 0, :, :, :, :, :, lane : lane + 128].reshape(hidden, 128)

    def store_layer(b, k, at, v):
        p = 1.0 + jnp.tanh(v)
        a = v * p
        rate = p + a * (2.0 - p)
        slope[b, k, at, :] = rate.astype(BF)
        low = a.astype(BF)
        act_t[b, k, :, at] = low.T
        return low

    def halves(body):
        for t in range(2):
            body(slice(t * windows // 2, (t + 1) * windows // 2))

    def layer_zero(b):
        bias_t[...] = small(b, 128).astype(F32).T

        def body(at):
            a = resid[at, :].astype(BF)
            in_t[b, :, at] = a.T
            work[0, at, :] = store_layer(b, 0, at, dot_nt(a, small(b, 0)) + bias_t[span : span + 1, :])

        halves(body)

    def layer_next(b, k):
        source, target = lax.rem(k + 1, 2), lax.rem(k, 2)
        v = dot_nn(work[source], matrix(b, k)) + bias_t[pl.ds(span + k, 1), :]
        work[target] = store_layer(b, k, slice(0, windows), v)

    def grid(value):
        return value.astype(BF).reshape(ZN, YN, XN, 2, half_rows, -1)

    def backcast_step():
        def body(at):
            theta = dot_nn(work[1, at, :], matrix(0, 4)).astype(BF)
            theta_keep[at, :] = theta
            resid[at, :] = (resid[at, :] - dot_nn(theta, small(0, 256))) * mask[at, :].astype(F32)

        halves(body)

    def put_rows(buf, b, at, value):
        for row in range(value.shape[0]):
            buf[b, row, :, at] = value[row : row + 1]

    def late_theta(b, m):
        theta_t = act_t.at[1, 0]
        theta_t[...] = dot_nn(matrix(b, m).T, act_t[b, 3]).astype(BF)

        @pl.when(m == 4)
        def _():
            gp[b, 0, :, :, :, :, :, 256:384] = grid(dot_nt(theta_t[...], e_t[b]))

        @pl.when(m == 5)
        def _():
            grad = grid(dot_nn(theta_t[...], f_ref[...]))
            gp[b, 0, :, :, :, :, :, 128:256] = gp[b, 0, :, :, :, :, :, 128:256] + grad
            part_t[b] = dot_nn(small(b, 128).T, theta_t[...])[0:span]

    def forecasts():
        put_rows(pred, 0, slice(0, windows), part_t[0])
        put_rows(pred, 1, slice(0, windows), part_t[0].astype(BF).astype(F32) + part_t[1])

    count = 2 * MATS

    def delayed(lag, t, step):
        pl.when(jnp.logical_and(t >= lag, t < count + lag))(lambda: step(t - lag))

    def staged(lag, t, step):
        early = t - lag + 1
        pl.when(jnp.logical_and(early >= (2 if lag == 2 else 1), early <= 2))(lambda: step(early))
        unit = t - lag
        pl.when(jnp.logical_and(unit >= 3, unit < count))(lambda: step(unit))
        if lag == 6:
            pl.when(t == 4)(lambda: step(0))

    def gather_line(i):
        b, m = of(i)

        pl.when(b == core)(lambda: by_lanes(m, lambda lanes: start_all(line_copies(i, lanes) + z_copies(i, lanes))))

    def gather_columns(i):
        b, m = of(i)

        def step(lanes):
            pl.when(b != core)(lambda: hand_over(m, lanes).wait_recv())
            for copy in z_copies(i, lanes):
                copy.wait_recv()
            start_all(column_copies(i, lanes))

        by_lanes(m, step)

    def gather_corner(i):
        def step(lanes):
            column_copies(i, lanes)[0].wait_recv()
            corner_copy(i, lanes).start()

        by_lanes(of(i)[1], step)

    def gather_core(i):
        def step(lanes):
            column_copies(i, lanes)[1].wait_recv()
            corner_copy(i, lanes).wait_recv()
            core_copy(i, lanes).start()

        by_lanes(of(i)[1], step)

    def arrived(i):
        by_lanes(of(i)[1], lambda lanes: core_copy(i, lanes).wait_recv())

    def forward_unit(i):
        arrived(i)
        b, m = of(i)
        pl.when(m == 0)(lambda: layer_zero(b))
        pl.when(jnp.logical_and(m >= 1, m <= 3))(lambda: layer_next(b, m))
        pl.when(m == 4)(backcast_step)

        @pl.when(jnp.logical_or(i == 4, i == 8))
        def _():
            pl.when(b == 1)(lambda: feed(b))
            pl.when(b == 0)(lambda: feed_forward(b))
            def one(n, carry):
                pl.when(jnp.logical_and(b == 1, n == 5))(lambda: gather_core(10))
                theta_grad(b, n)
                scatter_start(jnp.where(b == 0, 0, n - 3))
                return carry

            lax.fori_loop(jnp.where(b == 1, 4, 5), MATS, one, 0)

    def gather_step(t, carry):
        pl.when(t == 12)(lambda: scatter_core(0))
        pl.when(t == 15)(lambda: scatter_diag(0))
        pl.when(jnp.logical_and(t >= 4, t != 14))(lambda: gather_core(t - 4))
        delayed(2, t, gather_corner)
        delayed(0, t, gather_columns)
        pl.when(t + 4 < count)(lambda: gather_line(t + 4))

        @pl.when(t == 0)
        def _():
            for load in loads:
                load.wait()
            lax.fori_loop(0, tiles, prepare, 0)
            pad[...] = jnp.zeros_like(pad)
            lax.fori_loop(0, windows // 128, prepare_mask, 0)

        pl.when(jnp.logical_and(t >= 5, t < 14))(lambda: forward_unit(t - 5))
        return carry

    def out_copies(buf, out, s):
        at = pl.ds(row0, windows)
        return [
            pltpu.make_async_copy(buf.at[core], out.at[:, :, at], local_sem.at[2 + s]),
            remote(buf.at[other], out.at[:, :, at], out_send.at[s], out_recv.at[s], sibling),
        ]


    def back_of(j):
        if isinstance(j, int):
            return ORDER[j]
        b = jnp.where(jnp.logical_or(jnp.logical_and(j >= 1, j <= 5), j == 10), 1, 0)
        early = jnp.where(j == 1, 4, jnp.where(j <= 2, 5, 6 - j))
        return b, jnp.where(j <= 5, early, jnp.where(j == 6, 4, jnp.where(j <= 9, 10 - j, 0)))

    def to_core(j, lanes):
        b, m = back_of(j)
        return remote(
            gp.at[b, m, :, :, :, other, :, lanes], from_core.at[lax.rem(j, CORE_SLOTS), :, :, :, :, lanes],
            sends(rs_send, 3, lanes), rs_recv.at[j, 0], sibling,
        )

    def to_far(j, lanes):
        b, m = back_of(j)
        device = chip(z, far_y, far_x)
        return [
            remote(
                gp.at[b, m, :, yo, xo, core, :, lanes], from_diag.at[lax.rem(j, DIAG_SLOTS), :, :, lanes],
                sends(rs_send, 1, lanes), rs_recv.at[j, 1], device,
            ),
            remote(
                gp.at[b, m, :, far_y, far_x, core, :, lanes], from_plain.at[lax.rem(j, PLAIN_SLOTS), :, :, lanes],
                sends(rs_send, 1, lanes), rs_recv.at[j, 2], device,
            ),
        ]

    def to_near(j, lanes):
        b, m = back_of(j)
        return remote(
            gp.at[b, m, :, near_y, near_x, core, :, lanes], from_pair.at[lax.rem(j, PAIR_SLOTS), :, :, lanes],
            sends(rs_send, 2, lanes), rs_recv.at[j, 3], chip(z, near_y, near_x),
        )

    def to_z(j, lanes):
        b, m = back_of(j)
        return [
            remote(
                gp.at[b, m, zi, y, x, core, :, lanes], from_z.at[j, s, :, lanes],
                sends(rs_send, 0, lanes), rs_recv.at[j, 4 + s], chip(zi, y, x),
            )
            for s, zi in enumerate(z_peers)
        ]

    def scatter_start(j):
        by_lanes(back_of(j)[1], lambda lanes: to_core(j, lanes).start())

    def scatter_core(j):
        b, m = back_of(j)

        def step(lanes):
            to_core(j, lanes).wait_recv()
            part = gp[b, m, :, :, :, core, :, lanes] + from_core[lax.rem(j, CORE_SLOTS), :, :, :, :, lanes]
            gp[b, m, :, :, :, core, :, lanes] = part
            start_all(to_far(j, lanes))

        by_lanes(m, step)

    def scatter_diag(j):
        b, m = back_of(j)

        def step(lanes):
            to_far(j, lanes)[0].wait_recv()
            part = gp[b, m, :, near_y, near_x, core, :, lanes] + from_diag[lax.rem(j, DIAG_SLOTS), :, :, lanes]
            gp[b, m, :, near_y, near_x, core, :, lanes] = part
            to_near(j, lanes).start()

        by_lanes(m, step)

    def scatter_plane(j):
        b, m = back_of(j)

        def step(lanes):
            to_far(j, lanes)[1].wait_recv()
            to_near(j, lanes).wait_recv()
            value = gp[b, m, :, y, x, core, :, lanes].astype(F32)
            value = value + from_plain[lax.rem(j, PLAIN_SLOTS), :, :, lanes].astype(F32)
            value = value + from_pair[lax.rem(j, PAIR_SLOTS), :, :, lanes].astype(F32)
            gp[b, m, :, y, x, core, :, lanes] = value.astype(BF)
            start_all(to_z(j, lanes))

        by_lanes(m, step)

    def scatter_z(j):
        b, m = back_of(j)

        def step(lanes):
            for copy in to_z(j, lanes):
                copy.wait_recv()
            value = gp[b, m, z, y, x, core, :, lanes].astype(F32)
            for s in range(ZN - 1):
                value = value + from_z[j, s, :, lanes].astype(F32)
            total[b, m, :, lanes] = value
            squares[:, lanes] = squares[:, lanes] + value * value

        by_lanes(m, step)

    def add_rows(value):
        return jnp.sum(value.reshape(-1, 8, hidden), axis=0)

    def put_bias(k, acc):
        bias_sum[pl.ds(span + k, 1), :] = jnp.sum(acc, axis=0, keepdims=True)

    def feed(b):
        pl.when(b == 1)(lambda: resid.__setitem__(..., jnp.zeros_like(resid)))
        e = (-(resid[...] * mask[...].astype(F32))).astype(BF)
        e_t[b] = e.T
        work[0] = dot_nt(e, small(b, 256)).astype(BF)
        work[2] = dot_nt(f_ref[...], small(b, 128)).astype(BF)

    def feed_forward(b):
        work[2] = dot_nt(f_ref[...], small(b, 128)).astype(BF)

    def put_dz(b, k, da):
        dz = da * slope[b, k].astype(F32)
        work[k % 2 if isinstance(k, int) else lax.rem(k, 2)] = dz.astype(BF)
        bias_sum[pl.ds(span + k, 1), :] = jnp.sum(add_rows(dz), axis=0, keepdims=True)

    def theta_step(b):
        put_dz(b, 3, 0.5 * (dot_nt(work[0], matrix(b, 4)) + dot_nt(work[2], matrix(b, 5))))

    def layer_back(b, k):
        source = lax.rem(k, 2)
        gp[b, k] = grid(dot_nn(act_t[b, k - 1], work[source]))
        put_dz(b, k - 1, dot_nt(work[source], matrix(b, k)))

    def theta_grad(b, m):
        gp[b, m] = grid(dot_nn(act_t[b, 3], work[jnp.where(m == 4, 0, 2)]))

    def first_grads(b):
        gp[b, 0, :, :, :, :, :, 0:128] = grid(dot_nn(in_t[b], work[0]).T)
        gp[b, 0, :, :, :, :, :, 128:256] = grid(bias_sum[...].T)
        pl.when(b == 0)(backcast_grad)

    def backcast_grad():
        gp[0, 0, :, :, :, :, :, 256:384] = grid(dot_nn(e_t[0], theta_keep[...]).T)

    def input_grad(b):
        for t in range(2):
            at = slice(t * windows // 2, (t + 1) * windows // 2)
            keep = mask[at, :].astype(F32)
            dr = resid[at, :] * keep + 2.0 * dot_nn(work[0, at, :], small(b, 0))

            @pl.when(b == 1)
            def _():
                seg[at, :] = dr[:, 0:past]
                resid[at, :] = dr.astype(BF).astype(F32)

            @pl.when(b == 0)
            def _():
                put_rows(sens, 0, at, (dr * keep).T[0:past])

    def late_rows():
        for g in range(windows // 128):
            at = slice(g * 128, (g + 1) * 128)
            pad[:, 0:past] = seg[at, :]
            put_rows(sens, 1, at, pad[...].T[0:past])

    bias_sum[...] = jnp.zeros_like(bias_sum)
    squares[...] = jnp.zeros_like(squares)
    total[...] = jnp.zeros_like(total)

    def back_step(j, carry):
        b, m = back_of(j)

        staged(6, j, scatter_plane)
        staged(4, j, scatter_diag)
        staged(2, j, scatter_core)

        @pl.when(j == 2)
        def _():
            arrived(9)
            arrived(10)
            theta_step(1)
            scatter_core(1)

        pl.when(jnp.logical_and(m >= 1, m <= 3))(lambda: layer_back(b, m))

        @pl.when(jnp.logical_or(j == 6, j == count - 1))
        def _():
            block = jnp.where(j == 6, 1, 0)
            first_grads(block)
            pl.when(j == 6)(lambda: input_grad(1))

        @pl.when(j == 6)
        def _():
            feed(0)
            theta_grad(0, 4)

        @pl.when(jnp.logical_or(j == 10, j == 11))
        def _():
            lax.fori_loop(jnp.where(j == 10, 4, 5), MATS, lambda n, carry: (late_theta(b, n), carry)[1], 0)

        pl.when(jnp.logical_and(j >= 3, j < count))(lambda: scatter_start(j))

        @pl.when(j == 6)
        def _():
            arrived(11)
            theta_step(0)

        @pl.when(j == count)
        def _():
            input_grad(0)
            forecasts()
            start_all(out_copies(pred, pred_out, 0))

        @pl.when(j == count + 1)
        def _():
            late_rows()
            start_all(out_copies(sens, sens_out, 1))

        @pl.when(j >= count + 1)
        def _():
            scatter_z(2 * (j - count - 1))
            scatter_z(2 * (j - count - 1) + 1)

        return carry

    gather_line(0)
    hand_over(0, slice(0, 384)).start()
    for m in range(1, MATS):
        pack(m)
        if m < 4:
            gather_line(m)
        hand_over(m, slice(0, hidden)).start()
    lax.fori_loop(0, count + 4, gather_step, 0)

    lax.fori_loop(2, count + 7, back_step, 0)

    grad_copy = remote(total.at[other], grad_out.at[:, core], out_send.at[2], out_recv.at[2], sibling)
    grad_copy.start()
    grad_out[:, core] = total[core]
    sq = squares[:, 0:128] + squares[:, 128:256] + squares[:, 256:384] + squares[:, 384:512]
    place = (y * XN + x) * 2 + core
    norm_buf[place] = sq[0:8] + sq[8:16]

    def spread(sources, targets, first):
        copies = [
            remote(norm_buf.at[sources], norm_buf.at[sources], norm_send.at[first + s], norm_recv.at[first + s], device)
            for s, device in enumerate(targets)
        ]
        start_all(copies)
        for copy in copies:
            copy.wait()

    def add_up(slots):
        value = norm_buf[slots[0]]
        for slot in slots[1:]:
            value = value + norm_buf[slot]
        return value

    spread(place, plane_peers, 0)
    norm_buf[8 + z] = add_up(range(8))
    spread(8 + z, [chip(zi, y, x) for zi in z_peers], 7)
    everything = add_up(range(8, 8 + ZN))
    norm_out[...] = jnp.broadcast_to(jnp.sqrt(jnp.sum(everything, keepdims=True)), norm_out.shape)

    grad_copy.wait()
    for buf, out, s in ((pred, pred_out, 0), (sens, sens_out, 1)):
        for copy in out_copies(buf, out, s):
            copy.wait()
    for m in range(MATS):
        hand_over(m, slice(0, hidden if m else 384)).wait_send()

    for mats, lanes in ((slice(1, MATS), slice(0, hidden)), (slice(0, 1), slice(0, 384))):
        sent = (
            wg.at[:, mats, 0 : ZN - 1, 0, 0, 0, :, lanes],
            wg.at[:, mats, :, :, 0, 0, :, lanes],
            wg.at[:, mats, :, 0, 0, 0, :, lanes],
            wg.at[:, mats, :, :, :, 0, :, lanes],
        )
        for sems in (ag_send, rs_send):
            for kind, ref in enumerate(sent):
                remote(ref, ref, sends(sems, kind, lanes), out_recv.at[0], sibling).wait_send()


def train_call(plane, segments, extents, adjoint, first, square, head, biases):
    ZN, YN, XN = plane
    past, span, hidden = segments.shape[1], adjoint.shape[0], square.shape[3]
    windows = segments.shape[0] // 2
    tile = windows
    half = hidden // (ZN * YN * XN) // 2
    sizes = (ZN, YN, XN, windows, tile, past, span, hidden)
    DMA = pltpu.SemaphoreType.DMA
    vmem = pl.BlockSpec(memory_space=pltpu.VMEM)
    hbm = pl.BlockSpec(memory_space=pl.ANY)
    count = 2 * MATS
    flops = 2 * 2 * 3 * windows * hidden * (6 * hidden + 2 * 128)
    lengths = extents.reshape(-1, 128)
    return pl.pallas_call(
        functools.partial(train_kernel, sizes),
        out_shape=(
            jax.ShapeDtypeStruct((span, 1, 2 * windows), F32),
            jax.ShapeDtypeStruct((past, 1, 2 * windows), F32),
            jax.ShapeDtypeStruct((MATS, 2, half, hidden), F32),
            jax.ShapeDtypeStruct((8, 128), F32),
        ),
        in_specs=[hbm] * 7,
        out_specs=(hbm, hbm, vmem, vmem),
        scratch_shapes=[
            pltpu.VMEM((2, MATS, ZN, YN, XN, 2, half, hidden), BF),
            pltpu.VMEM((MATS, half, hidden), BF),
            pltpu.VMEM((2, MATS, ZN, YN, XN, 2, half, hidden), BF),
            pltpu.VMEM((CORE_SLOTS, ZN, YN, XN, half, hidden), BF),
            pltpu.VMEM((DIAG_SLOTS, ZN, half, hidden), BF),
            pltpu.VMEM((PLAIN_SLOTS, ZN, half, hidden), BF),
            pltpu.VMEM((PAIR_SLOTS, ZN, half, hidden), BF),
            pltpu.VMEM((count, ZN - 1, half, hidden), BF),
            pltpu.VMEM((2, MATS, half, hidden), F32),
            pltpu.VMEM((2, 4, hidden, windows), BF),
            pltpu.VMEM((2, 128, windows), BF),
            pltpu.VMEM((windows, hidden), BF),
            pltpu.VMEM((2, 4, windows, hidden), BF),
            pltpu.VMEM((3, windows, hidden), BF),
            pltpu.VMEM((windows, 128), F32),
            pltpu.VMEM((windows, 128), BF),
            pltpu.VMEM((windows, 128), BF),
            pltpu.VMEM((2, 128, windows), BF),
            pltpu.VMEM((128, hidden), F32),
            pltpu.VMEM((128, hidden), F32),
            pltpu.VMEM((128, 128), F32),
            pltpu.VMEM((windows, past), F32),
            pltpu.VMEM((span, windows), F32),
            *(pltpu.VMEM(a.shape, a.dtype) for a in (lengths, first, square, head, biases)),
            pltpu.VMEM((2, span, windows), F32),
            pltpu.VMEM((2, span, 1, windows), F32),
            pltpu.VMEM((2, past, 1, windows), F32),
            pltpu.VMEM((half, hidden), F32),
            pltpu.VMEM((8 + ZN, 8, 128), F32),
            DMA((MATS,)),
            DMA((MATS,)),
            DMA((4, 2)),
            DMA((count, 4 + ZN - 1)),
            DMA((4, 2)),
            DMA((count, 4 + ZN - 1)),
            DMA((3,)),
            DMA((3,)),
            DMA((9,)),
            DMA((7 + ZN - 1,)),
            DMA((7 + ZN - 1,)),
        ],
        compiler_params=pltpu.CompilerParams(
            collective_id=0, has_side_effects=True, vmem_limit_bytes=64 * 1024 * 1024
        ),
        cost_estimate=pl.CostEstimate(flops=flops, bytes_accessed=8_000_000, transcendentals=8 * windows * hidden),
        name="train",
    )(segments, adjoint, lengths, first, square, head, biases)


def update_kernel(past, span, *refs):
    sources, targets, norm_out = refs[0:16], refs[16:34], refs[34]
    held, results, pad, in_sem, out_sem = refs[35:51], refs[51:67], *refs[67:70]
    arriving = [pltpu.make_async_copy(source, ref, in_sem.at[n]) for n, (source, ref) in enumerate(zip(sources, held))]
    leaving = [
        pltpu.make_async_copy(ref, target, out_sem.at[n]) for n, (ref, target) in enumerate(zip(held[0:2] + results, targets))
    ]
    for n in (2, 3, 0, 5, 9, 13, 1, 4, 8, 12, 6, 10, 14, 7, 11, 15):
        arriving[n].start()
    grads, norm, masters, momenta, variances = held[2], held[3], held[4:8], held[8:12], held[12:16]
    units = masters[3].shape[2]

    def rows(m, lane, width):
        return grads[m, :, :, lane : lane + width].reshape(units, width)

    arriving[2].wait()
    arriving[3].wait()
    norm_out[...] = norm[0:1, 0:1]
    factor = 1.0 / jnp.maximum(norm[0:1, 0:1], 1.0)
    for m in range(5):
        results[1][0, m] = rows(m + 1, 0, grads.shape[3])
    results[0][0] = rows(0, 0, 128)[:, 0:past]
    forecast = rows(0, 128, 128)
    pad[...] = jnp.zeros_like(pad)
    pad[0:units, :] = forecast
    results[3][0] = pad[...].T[span : span + 4, 0:units]
    results[2][0, :, 0:past] = rows(0, 256, 128)[:, 0:past]
    results[2][0, :, past : past + span] = forecast[:, 0:span]
    for n in (0, 1):
        arriving[n].wait()
        leaving[n].start()
    for n in (1, 0, 2, 3):
        leaving[2 + n].start()
        for state in range(3):
            arriving[4 + 4 * state + n].wait()
        updated = adamw(masters[n][...], results[n][...], momenta[n][...], variances[n][...], factor[None])
        for kind, value in enumerate(updated):
            results[4 * (kind + 1) + n][...] = value
            leaving[2 + 4 * (kind + 1) + n].start()
    for copy in leaving:
        copy.wait()


def update_call(prediction, sensitivity, grads, norm, state):
    hbm = pl.BlockSpec(memory_space=pl.ANY)
    sources = (prediction, sensitivity, grads, norm, *state)
    targets = (prediction, sensitivity, *(4 * list(state[:4])))
    return pl.pallas_call(
        functools.partial(update_kernel, sensitivity.shape[0], prediction.shape[0]),
        out_shape=tuple(jax.ShapeDtypeStruct(a.shape, F32) for a in targets) + (jax.ShapeDtypeStruct((1, 1), F32),),
        in_specs=[hbm] * len(sources),
        out_specs=tuple([hbm] * len(targets) + [pl.BlockSpec(memory_space=pltpu.VMEM)]),
        scratch_shapes=[pltpu.VMEM(a.shape, F32) for a in sources]
        + [pltpu.VMEM(a.shape, F32) for a in targets[2:]]
        + [pltpu.VMEM((128, 128), F32), pltpu.SemaphoreType.DMA((len(sources),)), pltpu.SemaphoreType.DMA((len(targets),))],
        name="update",
    )(*sources)


def turned(arrays):
    return [a.transpose(0, 2, 1) if n % 4 == 0 else a for n, a in enumerate(arrays)]


def kernel_shards(plane, segments, extents, adjoint, *state):
    state = turned(state)
    results = train_call(plane, segments, extents, adjoint.T, *state[:4])
    prediction, sensitivity, *updated, norm = update_call(*results, state)
    by_window = (prediction.transpose(1, 2, 0), sensitivity.transpose(1, 2, 0))
    return (*by_window, norm.reshape(()), *turned(updated))


STATE_SPECS = (
    P("section", None, "dp"),
    P("section", None, "dp", None),
    P("section", "dp", None),
    P("section", None, "dp"),
)


def solution(mesh):
    in_specs = (P("dp", None), P("dp"), P("dp", None)) + 3 * STATE_SPECS
    out_specs = (P("section", "dp", None), P("section", "dp", None), P()) + 4 * STATE_SPECS
    plane = PLANES.get(mesh.shape["dp"])
    shards = plain_shards if plane is None else functools.partial(kernel_shards, plane)
    return jax.shard_map(shards, mesh=mesh, in_specs=in_specs, out_specs=out_specs, check_vma=False)
```

```python
import functools

import jax
import jax.numpy as jnp
from jax import lax
from jax.experimental import pallas as pl
from jax.experimental.pallas import tpu as pltpu
from jax.sharding import PartitionSpec as P

STEP = 10


def dot_nn(a, b):
    return jnp.dot(a, b, preferred_element_type=jnp.float32)


def dot_tn(a, b):
    return lax.dot_general(a, b, (((0,), (0,)), ((), ())), preferred_element_type=jnp.float32)


def dot_nt(a, b):
    return lax.dot_general(a, b, (((1,), (1,)), ((), ())), preferred_element_type=jnp.float32)


def unit_rows(first, square, head, biases):
    units = first.shape[1]
    return jnp.concatenate(
        [square.transpose(1, 0, 2).reshape(units, -1), first.T, head, biases.T], axis=1
    )


def from_unit_rows(rows, past, hidden, out):
    wide = 5 * hidden
    square = rows[:, :wide].reshape(-1, 5, hidden).transpose(1, 0, 2)
    first = rows[:, wide : wide + past].T
    head = rows[:, wide + past : wide + past + out]
    biases = rows[:, wide + past + out :].T
    return first, square, head, biases


def plain_forward(weights, resid):
    first, square, head, biases = weights
    past = resid.shape[1]
    acts, slopes = [resid.astype(jnp.bfloat16)], []
    for k in range(4):
        z = dot_nn(acts[-1], first if k == 0 else square[k - 1]) + biases[k].astype(jnp.float32)
        sig = jax.nn.sigmoid(z)
        acts.append((z * sig).astype(jnp.bfloat16))
        slopes.append(sig * (1.0 + z * (1.0 - sig)))
    theta_b = dot_nn(acts[4], square[3]).astype(jnp.bfloat16)
    theta_f = dot_nn(acts[4], square[4]).astype(jnp.bfloat16)
    backcast = dot_nn(theta_b, head[:, :past])
    part = dot_nn(theta_f, head[:, past:])
    return backcast, part, (acts, slopes, theta_b, theta_f)


def plain_backward(weights, saved, e, f):
    first, square, head, biases = weights
    acts, slopes, theta_b, theta_f = saved
    past = e.shape[1]
    head_grad = jnp.concatenate([dot_tn(theta_b, e), dot_tn(theta_f, f)], axis=1)
    u_b = dot_nt(e, head[:, :past]).astype(jnp.bfloat16)
    u_f = dot_nt(f, head[:, past:]).astype(jnp.bfloat16)
    squares = [None, None, None, dot_tn(acts[4], u_b), dot_tn(acts[4], u_f)]
    da = dot_nt(u_b, square[3]) + dot_nt(u_f, square[4])
    bias_grads = [None] * 4
    first_grad = None
    for k in (3, 2, 1, 0):
        dz = (da * slopes[k]).astype(jnp.bfloat16)
        bias_grads[k] = jnp.sum(dz, axis=0, dtype=jnp.float32)
        grad = dot_tn(acts[k], dz)
        if k == 0:
            first_grad = grad
        else:
            squares[k - 1] = grad
        da = dot_nt(dz, first if k == 0 else square[k - 1])
    return da, (first_grad, jnp.stack(squares), head_grad, jnp.stack(bias_grads))


def adamw(master, gradient, momentum, variance, factor):
    clipped = gradient * factor
    moment_new = 0.9 * momentum + 0.1 * clipped
    variance_new = 0.999 * variance + 0.001 * clipped * clipped
    ratio = moment_new / (1.0 - 0.9**STEP) / (jnp.sqrt(variance_new / (1.0 - 0.999**STEP)) + 1e-08)
    return master - 0.05 * (ratio + 0.01 * master), moment_new, variance_new


def plain_shards(segments, extents, adjoint, *state):
    masters, momenta, variances = state[:4], state[4:8], state[8:]
    core = lax.axis_index("section")
    past, span = segments.shape[1], adjoint.shape[1]
    windows = segments.shape[0] // 2
    hidden = masters[1].shape[3]
    mine = [
        lax.dynamic_slice_in_dim(v, core * windows, windows, 0) for v in (segments, extents, adjoint)
    ]
    seg, ext, adj = mine
    rows = unit_rows(*(m[0].astype(jnp.bfloat16) for m in masters))
    rows = lax.all_gather(rows, "dp", axis=0, tiled=True)
    rows = lax.all_gather(rows, "section", axis=0)
    blocks = [from_unit_rows(rows[b], past, hidden, past + span) for b in range(2)]
    mask = (
        lax.broadcasted_iota(jnp.int32, (windows, past), 1) >= past - ext[:, None]
    ).astype(jnp.float32)
    r0 = seg * mask
    backcast, part0, saved0 = plain_forward(blocks[0], r0)
    r1 = (r0 - backcast) * mask
    _, part1, saved1 = plain_forward(blocks[1], r1)
    forecast = part0.astype(jnp.bfloat16).astype(jnp.float32) + part1
    f = adj.astype(jnp.bfloat16)
    zero = jnp.zeros_like(r0)
    da1, grads1 = plain_backward(blocks[1], saved1, (-(zero * mask)).astype(jnp.bfloat16), f)
    dr1 = zero * mask + da1
    t = dr1.astype(jnp.bfloat16).astype(jnp.float32)
    da0, grads0 = plain_backward(blocks[0], saved0, (-(t * mask)).astype(jnp.bfloat16), f)
    dr0 = (t * mask + da0) * mask

    def by_section(first_block, second_block):
        mine, other = (
            jnp.where(core == 0, first_block, second_block),
            jnp.where(core == 0, second_block, first_block),
        )
        got = lax.ppermute(other, "section", [(0, 1), (1, 0)])
        return jnp.where(
            core == 0, jnp.concatenate([mine, got]), jnp.concatenate([got, mine])
        )[None]

    prediction = by_section(part0, forecast)
    sensitivity = by_section(dr0, dr1)
    packed = jnp.stack([unit_rows(*grads0), unit_rows(*grads1)])
    packed = lax.psum_scatter(packed, "section", scatter_dimension=0, tiled=False)
    packed = lax.psum_scatter(packed, "dp", scatter_dimension=0, tiled=True)
    norm = jnp.sqrt(lax.psum(jnp.sum(packed * packed), ("section", "dp")))
    factor = 1.0 / jnp.maximum(norm, 1.0)
    summed = [g[None] for g in from_unit_rows(packed, past, hidden, past + span)]
    updated = [adamw(*four, factor) for four in zip(masters, summed, momenta, variances)]
    return (
        prediction,
        sensitivity,
        norm,
        *summed,
        *(u[0] for u in updated),
        *(u[1] for u in updated),
        *(u[2] for u in updated),
    )


PLANES = {16: (4, 2, 2)}
MESH = pl.DeviceIdType.MESH
MATS = 6
CORE_SLOTS, DIAG_SLOTS, PLAIN_SLOTS, PAIR_SLOTS = 4, 4, 6, 4
BF, F32 = jnp.bfloat16, jnp.float32


ORDER = ((0, 5), (1, 4), (1, 5), (1, 3), (1, 2), (1, 1), (0, 4), (0, 3), (0, 2), (0, 1), (1, 0), (0, 0))


def remote(src, dst, send_sem, recv_sem, device):
    return pltpu.make_async_remote_copy(
        src_ref=src, dst_ref=dst, send_sem=send_sem, recv_sem=recv_sem, device_id=device, device_id_type=MESH
    )


def train_kernel(
    sizes,
    seg_hbm, adj_hbm, ext_hbm, first_hbm, square_hbm, head_hbm, biases_hbm,
    pred_out, sens_out, grad_out, norm_out,
    wg, handed, gp, from_core, from_diag, from_plain, from_pair, from_z, total,
    act_t, in_t, theta_keep, slope, work, resid, mask, f_ref, e_t, bias_t, bias_sum, pad,
    seg, adj, ext, first, square, head, biases, part_t, pred, sens, squares, norm_buf,
    own_send, own_recv, ag_send, ag_recv, rs_send, rs_recv, out_send, out_recv, local_sem, norm_send, norm_recv,
):
    ZN, YN, XN, windows, tile, past, span, hidden = sizes
    units = ZN * YN * XN
    core, dp = lax.axis_index("section"), lax.axis_index("dp")
    x, y, z = lax.rem(dp, XN), lax.rem(lax.div(dp, XN), YN), lax.div(dp, XN * YN)
    other, xo, yo = 1 - core, 1 - x, 1 - y
    near_y, near_x = y + core * (yo - y), xo + core * (x - xo)
    far_y, far_x = yo + core * (y - yo), x + core * (xo - x)

    def chip(zi, yi, xi):
        return (core, (zi * YN + yi) * XN + xi)

    sibling = (other, dp)
    z_peers = [lax.rem(z + step, ZN) for step in range(1, ZN)]

    row0 = core * windows
    loads = [
        pltpu.make_async_copy(seg_hbm.at[pl.ds(row0, windows), :], seg, local_sem.at[0]),
        pltpu.make_async_copy(adj_hbm.at[:, pl.ds(row0, windows)], adj, local_sem.at[1]),
    ]
    small_loads = [
        pltpu.make_async_copy(source, target, local_sem.at[4 + n])
        for n, (source, target) in enumerate(
            [(square_hbm, square), (first_hbm, first), (head_hbm, head), (biases_hbm, biases), (ext_hbm, ext)]
        )
    ]
    for load in small_loads + loads:
        load.start()

    barrier = pltpu.get_barrier_semaphore()
    plane_peers = [
        (ci, (z * YN + yi) * XN + xi) for ci in (core, other) for yi in (y, yo) for xi in (x, xo)
    ][1:]
    peers = plane_peers + [(ci, (zi * YN + y) * XN + x) for zi in z_peers for ci in (core, other)]
    for peer in peers:
        pl.semaphore_signal(barrier, inc=1, device_id=peer, device_id_type=MESH)

    rows = hidden // units
    half_rows = rows // 2

    def put_own(m, value, lanes):
        halves = value.astype(BF).reshape(2, half_rows, -1)
        for h in range(2):
            pl.when(core == h)(functools.partial(put_half, m, halves[h], halves[1 - h], lanes))

    def put_half(m, kept, given, lanes):
        wg[core, m, z, y, x, core, :, lanes] = kept
        handed[m, :, lanes] = given

    for load in small_loads:
        load.wait()
    pad[...] = jnp.zeros_like(pad)
    pad[0:rows, 0:past] = first[0] * 0.5
    put_own(0, pad[0:rows, :], slice(0, 128))
    pad[...] = jnp.zeros_like(pad)
    pad[span : span + 4, 0:rows] = biases[0] * 0.5
    bias_cols = pad[...].T[0:rows]
    pad[...] = jnp.zeros_like(pad)
    pad[0:rows, 0:span] = head[0, :, past : past + span]
    put_own(0, pad[0:rows, :] + bias_cols, slice(128, 256))
    pad[...] = jnp.zeros_like(pad)
    pad[0:rows, 0:past] = head[0, :, 0:past]
    put_own(0, pad[0:rows, :], slice(256, 384))
    pl.semaphore_wait(barrier, len(peers))

    def hand_over(m, lanes):
        return remote(
            handed.at[m, :, lanes], wg.at[core, m, z, y, x, other, :, lanes], own_send.at[m], own_recv.at[m], sibling
        )

    def pack(m):
        put_own(m, square[0, m - 1] * 0.5 if m < 4 else square[0, m - 1], slice(0, hidden))


    def of(i):
        b = jnp.where(jnp.logical_and(i >= 5, i <= 10), 1, 0)
        return b, jnp.where(i <= 4, i, jnp.where(i <= 10, i - 5, 5))

    def sends(sems, kind, lanes):
        return sems.at[kind, 0 if lanes.stop == hidden else 1]

    def z_copies(i, lanes):
        b, m = of(i)
        part = wg.at[b, m, z, y, x, core, :, lanes]
        return [
            remote(part, part, sends(ag_send, 0, lanes), ag_recv.at[i, s], chip(zi, y, x)) for s, zi in enumerate(z_peers)
        ]

    def line_copies(i, lanes):
        b, m = of(i)
        given = wg.at[b, m, z, y, x, other, :, lanes]
        return [
            remote(
                handed.at[m, :, lanes], given, sends(ag_send, 0, lanes), ag_recv.at[i, s], (other, (zi * YN + y) * XN + x)
            )
            for s, zi in enumerate(z_peers)
        ]

    def column_copies(i, lanes):
        b, m = of(i)
        part = wg.at[b, m, :, y, x, core, :, lanes]
        return [
            remote(part, part, sends(ag_send, 1, lanes), ag_recv.at[i, 3], chip(z, near_y, near_x)),
            remote(part, part, sends(ag_send, 1, lanes), ag_recv.at[i, 4], chip(z, far_y, far_x)),
        ]

    def corner_copy(i, lanes):
        b, m = of(i)
        part = wg.at[b, m, :, near_y, near_x, core, :, lanes]
        return remote(part, part, sends(ag_send, 2, lanes), ag_recv.at[i, 5], chip(z, far_y, far_x))

    def core_copy(i, lanes):
        b, m = of(i)
        part = wg.at[b, m, :, :, :, core, :, lanes]
        return remote(part, part, sends(ag_send, 3, lanes), ag_recv.at[i, 6], sibling)

    def by_lanes(m, step):
        if isinstance(m, int):
            step(slice(0, hidden if m else 384))
            return
        pl.when(m == 0)(lambda: step(slice(0, 384)))
        pl.when(m > 0)(lambda: step(slice(0, hidden)))

    def start_all(copies):
        for copy in copies:
            copy.start()

    zeros_tile = jnp.zeros((tile, 128), F32)

    def prepare(t, carry):
        at = pl.ds(t * tile, tile)
        resid[at, :] = zeros_tile
        resid[at, 0:past] = seg[at, :]
        return carry

    def prepare_mask(g, carry):
        lengths = ext[pl.ds(core * (windows // 128) + g, 1), :]
        position = lax.broadcasted_iota(jnp.int32, (128, 128), 0)
        keep = jnp.where(position >= past - lengths, 1.0, 0.0).astype(F32).T
        at = pl.ds(pl.multiple_of(g * 128, 128), 128)
        pad[0:span, :] = adj[:, at]
        f_ref[at, :] = pad[...].T.astype(BF)
        mask[at, :] = keep.astype(BF)
        resid[at, :] = resid[at, :] * keep
        return carry

    tiles = windows // tile
    part_tile = windows // 2

    def matrix(b, m):
        return wg[b, m].reshape(hidden, hidden)

    def small(b, lane):
        return wg[b, 0, :, :, :, :, :, lane : lane + 128].reshape(hidden, 128)

    def store_layer(b, k, at, v):
        p = 1.0 + jnp.tanh(v)
        a = v * p
        rate = p + a * (2.0 - p)
        slope[b, k, at, :] = rate.astype(BF)
        low = a.astype(BF)
        act_t[b, k, :, at] = low.T
        return low

    def halves(body):
        for t in range(2):
            body(slice(t * windows // 2, (t + 1) * windows // 2))

    def layer_zero(b):
        bias_t[...] = small(b, 128).astype(F32).T

        def body(at):
            a = resid[at, :].astype(BF)
            in_t[b, :, at] = a.T
            work[0, at, :] = store_layer(b, 0, at, dot_nt(a, small(b, 0)) + bias_t[span : span + 1, :])

        halves(body)

    def layer_next(b, k):
        source, target = lax.rem(k + 1, 2), lax.rem(k, 2)

        def body(at):
            v = dot_nn(work[source, at, :], matrix(b, k)) + bias_t[pl.ds(span + k, 1), :]
            work[target, at, :] = store_layer(b, k, at, v)

        halves(body)

    def grid(value):
        return value.astype(BF).reshape(ZN, YN, XN, 2, half_rows, -1)

    def backcast_step():
        def body(at):
            theta = dot_nn(work[1, at, :], matrix(0, 4)).astype(BF)
            theta_keep[at, :] = theta
            resid[at, :] = (resid[at, :] - dot_nn(theta, small(0, 256))) * mask[at, :].astype(F32)

        halves(body)

    def put_rows(buf, b, at, value):
        for row in range(value.shape[0]):
            buf[b, row, :, at] = value[row : row + 1]

    def late_theta(b, m):
        theta_t = act_t.at[1, 0]
        theta_t[...] = dot_nn(matrix(b, m).T, act_t[b, 3]).astype(BF)

        @pl.when(m == 4)
        def _():
            gp[b, 0, :, :, :, :, :, 256:384] = grid(dot_nt(theta_t[...], e_t[b]))

        @pl.when(m == 5)
        def _():
            grad = grid(dot_nn(theta_t[...], f_ref[...]))
            gp[b, 0, :, :, :, :, :, 128:256] = gp[b, 0, :, :, :, :, :, 128:256] + grad
            part_t[b] = dot_nn(small(b, 128).T, theta_t[...])[0:span]

    def forecasts():
        put_rows(pred, 0, slice(0, windows), part_t[0])
        put_rows(pred, 1, slice(0, windows), part_t[0].astype(BF).astype(F32) + part_t[1])

    count = 2 * MATS

    def delayed(lag, t, step):
        pl.when(jnp.logical_and(t >= lag, t < count + lag))(lambda: step(t - lag))

    def staged(lag, t, step):
        early = t - lag + 1
        pl.when(jnp.logical_and(early >= (2 if lag == 2 else 1), early <= 2))(lambda: step(early))
        unit = t - lag
        pl.when(jnp.logical_and(unit >= 3, unit < count))(lambda: step(unit))
        if lag == 6:
            pl.when(t == 4)(lambda: step(0))

    def gather_line(i):
        b, m = of(i)

        pl.when(b == core)(lambda: by_lanes(m, lambda lanes: start_all(line_copies(i, lanes) + z_copies(i, lanes))))

    def gather_columns(i):
        b, m = of(i)

        def step(lanes):
            pl.when(b != core)(lambda: hand_over(m, lanes).wait_recv())
            for copy in z_copies(i, lanes):
                copy.wait_recv()
            start_all(column_copies(i, lanes))

        by_lanes(m, step)

    def gather_corner(i):
        def step(lanes):
            column_copies(i, lanes)[0].wait_recv()
            corner_copy(i, lanes).start()

        by_lanes(of(i)[1], step)

    def gather_core(i):
        def step(lanes):
            column_copies(i, lanes)[1].wait_recv()
            corner_copy(i, lanes).wait_recv()
            core_copy(i, lanes).start()

        by_lanes(of(i)[1], step)

    def arrived(i):
        by_lanes(of(i)[1], lambda lanes: core_copy(i, lanes).wait_recv())

    def forward_unit(i):
        arrived(i)
        b, m = of(i)
        pl.when(m == 0)(lambda: layer_zero(b))
        pl.when(jnp.logical_and(m >= 1, m <= 3))(lambda: layer_next(b, m))
        pl.when(m == 4)(backcast_step)

        @pl.when(jnp.logical_or(i == 4, i == 8))
        def _():
            pl.when(b == 1)(lambda: feed(b))
            pl.when(b == 0)(lambda: feed_forward(b))
            def one(n, carry):
                pl.when(jnp.logical_and(b == 1, n == 5))(lambda: gather_core(10))
                theta_grad(b, n)
                scatter_start(jnp.where(b == 0, 0, n - 3))
                return carry

            lax.fori_loop(jnp.where(b == 1, 4, 5), MATS, one, 0)

    def gather_step(t, carry):
        pl.when(t == 12)(lambda: scatter_core(0))
        pl.when(t == 15)(lambda: scatter_diag(0))
        pl.when(jnp.logical_and(t >= 4, t != 14))(lambda: gather_core(t - 4))
        delayed(2, t, gather_corner)
        delayed(0, t, gather_columns)
        pl.when(t + 4 < count)(lambda: gather_line(t + 4))

        @pl.when(t == 0)
        def _():
            for load in loads:
                load.wait()
            lax.fori_loop(0, tiles, prepare, 0)
            pad[...] = jnp.zeros_like(pad)
            lax.fori_loop(0, windows // 128, prepare_mask, 0)

        pl.when(jnp.logical_and(t >= 5, t < 14))(lambda: forward_unit(t - 5))
        return carry

    def out_copies(buf, out, s):
        at = pl.ds(row0, windows)
        return [
            pltpu.make_async_copy(buf.at[core], out.at[:, :, at], local_sem.at[2 + s]),
            remote(buf.at[other], out.at[:, :, at], out_send.at[s], out_recv.at[s], sibling),
        ]


    def back_of(j):
        if isinstance(j, int):
            return ORDER[j]
        b = jnp.where(jnp.logical_or(jnp.logical_and(j >= 1, j <= 5), j == 10), 1, 0)
        early = jnp.where(j == 1, 4, jnp.where(j <= 2, 5, 6 - j))
        return b, jnp.where(j <= 5, early, jnp.where(j == 6, 4, jnp.where(j <= 9, 10 - j, 0)))

    def to_core(j, lanes):
        b, m = back_of(j)
        return remote(
            gp.at[b, m, :, :, :, other, :, lanes], from_core.at[lax.rem(j, CORE_SLOTS), :, :, :, :, lanes],
            sends(rs_send, 3, lanes), rs_recv.at[j, 0], sibling,
        )

    def to_far(j, lanes):
        b, m = back_of(j)
        device = chip(z, far_y, far_x)
        return [
            remote(
                gp.at[b, m, :, yo, xo, core, :, lanes], from_diag.at[lax.rem(j, DIAG_SLOTS), :, :, lanes],
                sends(rs_send, 1, lanes), rs_recv.at[j, 1], device,
            ),
            remote(
                gp.at[b, m, :, far_y, far_x, core, :, lanes], from_plain.at[lax.rem(j, PLAIN_SLOTS), :, :, lanes],
                sends(rs_send, 1, lanes), rs_recv.at[j, 2], device,
            ),
        ]

    def to_near(j, lanes):
        b, m = back_of(j)
        return remote(
            gp.at[b, m, :, near_y, near_x, core, :, lanes], from_pair.at[lax.rem(j, PAIR_SLOTS), :, :, lanes],
            sends(rs_send, 2, lanes), rs_recv.at[j, 3], chip(z, near_y, near_x),
        )

    def to_z(j, lanes):
        b, m = back_of(j)
        return [
            remote(
                gp.at[b, m, zi, y, x, core, :, lanes], from_z.at[j, s, :, lanes],
                sends(rs_send, 0, lanes), rs_recv.at[j, 4 + s], chip(zi, y, x),
            )
            for s, zi in enumerate(z_peers)
        ]

    def scatter_start(j):
        by_lanes(back_of(j)[1], lambda lanes: to_core(j, lanes).start())

    def scatter_core(j):
        b, m = back_of(j)

        def step(lanes):
            to_core(j, lanes).wait_recv()
            part = gp[b, m, :, :, :, core, :, lanes] + from_core[lax.rem(j, CORE_SLOTS), :, :, :, :, lanes]
            gp[b, m, :, :, :, core, :, lanes] = part
            start_all(to_far(j, lanes))

        by_lanes(m, step)

    def scatter_diag(j):
        b, m = back_of(j)

        def step(lanes):
            to_far(j, lanes)[0].wait_recv()
            part = gp[b, m, :, near_y, near_x, core, :, lanes] + from_diag[lax.rem(j, DIAG_SLOTS), :, :, lanes]
            gp[b, m, :, near_y, near_x, core, :, lanes] = part
            to_near(j, lanes).start()

        by_lanes(m, step)

    def scatter_plane(j):
        b, m = back_of(j)

        def step(lanes):
            to_far(j, lanes)[1].wait_recv()
            to_near(j, lanes).wait_recv()
            value = gp[b, m, :, y, x, core, :, lanes].astype(F32)
            value = value + from_plain[lax.rem(j, PLAIN_SLOTS), :, :, lanes].astype(F32)
            value = value + from_pair[lax.rem(j, PAIR_SLOTS), :, :, lanes].astype(F32)
            gp[b, m, :, y, x, core, :, lanes] = value.astype(BF)
            start_all(to_z(j, lanes))

        by_lanes(m, step)

    def scatter_z(j):
        b, m = back_of(j)

        def step(lanes):
            for copy in to_z(j, lanes):
                copy.wait_recv()
            value = gp[b, m, z, y, x, core, :, lanes].astype(F32)
            for s in range(ZN - 1):
                value = value + from_z[j, s, :, lanes].astype(F32)
            total[b, m, :, lanes] = value
            squares[:, lanes] = squares[:, lanes] + value * value

        by_lanes(m, step)

    def add_rows(value):
        return jnp.sum(value.reshape(-1, 8, hidden), axis=0)

    def put_bias(k, acc):
        bias_sum[pl.ds(span + k, 1), :] = jnp.sum(acc, axis=0, keepdims=True)

    def feed(b):
        pl.when(b == 1)(lambda: resid.__setitem__(..., jnp.zeros_like(resid)))
        e = (-(resid[...] * mask[...].astype(F32))).astype(BF)
        e_t[b] = e.T
        work[0] = dot_nt(e, small(b, 256)).astype(BF)
        work[2] = dot_nt(f_ref[...], small(b, 128)).astype(BF)

    def feed_forward(b):
        work[2] = dot_nt(f_ref[...], small(b, 128)).astype(BF)

    def put_dz(b, k, da):
        sums = []

        def body(at):
            dz = da(at) * slope[b, k, at, :].astype(F32)
            work[k % 2 if isinstance(k, int) else lax.rem(k, 2), at, :] = dz.astype(BF)
            sums.append(add_rows(dz))

        halves(body)
        bias_sum[pl.ds(span + k, 1), :] = jnp.sum(sums[0] + sums[1], axis=0, keepdims=True)

    def theta_step(b):
        put_dz(
            b, 3, lambda at: 0.5 * (dot_nt(work[0, at, :], matrix(b, 4)) + dot_nt(work[2, at, :], matrix(b, 5)))
        )

    def layer_back(b, k):
        source = lax.rem(k, 2)
        gp[b, k] = grid(dot_nn(act_t[b, k - 1], work[source]))
        put_dz(b, k - 1, lambda at: dot_nt(work[source, at, :], matrix(b, k)))

    def theta_grad(b, m):
        gp[b, m] = grid(dot_nn(act_t[b, 3], work[jnp.where(m == 4, 0, 2)]))

    def first_grads(b):
        gp[b, 0, :, :, :, :, :, 0:128] = grid(dot_nn(in_t[b], work[0]).T)
        gp[b, 0, :, :, :, :, :, 128:256] = grid(bias_sum[...].T)
        pl.when(b == 0)(backcast_grad)

    def backcast_grad():
        gp[0, 0, :, :, :, :, :, 256:384] = grid(dot_nn(e_t[0], theta_keep[...]).T)

    def input_grad(b):
        for t in range(2):
            at = slice(t * windows // 2, (t + 1) * windows // 2)
            keep = mask[at, :].astype(F32)
            dr = resid[at, :] * keep + 2.0 * dot_nn(work[0, at, :], small(b, 0))

            @pl.when(b == 1)
            def _():
                seg[at, :] = dr[:, 0:past]
                resid[at, :] = dr.astype(BF).astype(F32)

            @pl.when(b == 0)
            def _():
                put_rows(sens, 0, at, (dr * keep).T[0:past])

    def late_rows():
        for g in range(windows // 128):
            at = slice(g * 128, (g + 1) * 128)
            pad[:, 0:past] = seg[at, :]
            put_rows(sens, 1, at, pad[...].T[0:past])

    bias_sum[...] = jnp.zeros_like(bias_sum)
    squares[...] = jnp.zeros_like(squares)
    total[...] = jnp.zeros_like(total)

    def back_step(j, carry):
        b, m = back_of(j)

        staged(6, j, scatter_plane)
        staged(4, j, scatter_diag)
        staged(2, j, scatter_core)

        @pl.when(j == 2)
        def _():
            arrived(9)
            arrived(10)
            theta_step(1)
            scatter_core(1)

        pl.when(jnp.logical_and(m >= 1, m <= 3))(lambda: layer_back(b, m))

        @pl.when(jnp.logical_or(j == 6, j == count - 1))
        def _():
            block = jnp.where(j == 6, 1, 0)
            first_grads(block)
            pl.when(j == 6)(lambda: input_grad(1))

        @pl.when(j == 6)
        def _():
            feed(0)
            theta_grad(0, 4)

        @pl.when(jnp.logical_or(j == 10, j == 11))
        def _():
            lax.fori_loop(jnp.where(j == 10, 4, 5), MATS, lambda n, carry: (late_theta(b, n), carry)[1], 0)

        pl.when(jnp.logical_and(j >= 3, j < count))(lambda: scatter_start(j))

        @pl.when(j == 6)
        def _():
            arrived(11)
            theta_step(0)

        @pl.when(j == count)
        def _():
            input_grad(0)
            forecasts()
            start_all(out_copies(pred, pred_out, 0))

        @pl.when(j == count + 1)
        def _():
            late_rows()
            start_all(out_copies(sens, sens_out, 1))

        @pl.when(j >= count + 1)
        def _():
            scatter_z(2 * (j - count - 1))
            scatter_z(2 * (j - count - 1) + 1)

        return carry

    gather_line(0)
    hand_over(0, slice(0, 384)).start()
    for m in range(1, MATS):
        pack(m)
        if m < 4:
            gather_line(m)
        hand_over(m, slice(0, hidden)).start()
    lax.fori_loop(0, count + 4, gather_step, 0)

    lax.fori_loop(2, count + 7, back_step, 0)

    grad_copy = remote(total.at[other], grad_out.at[:, core], out_send.at[2], out_recv.at[2], sibling)
    grad_copy.start()
    grad_out[:, core] = total[core]
    sq = squares[:, 0:128] + squares[:, 128:256] + squares[:, 256:384] + squares[:, 384:512]
    place = (y * XN + x) * 2 + core
    norm_buf[place] = sq[0:8] + sq[8:16]

    def spread(sources, targets, first):
        copies = [
            remote(norm_buf.at[sources], norm_buf.at[sources], norm_send.at[first + s], norm_recv.at[first + s], device)
            for s, device in enumerate(targets)
        ]
        start_all(copies)
        for copy in copies:
            copy.wait()

    def add_up(slots):
        value = norm_buf[slots[0]]
        for slot in slots[1:]:
            value = value + norm_buf[slot]
        return value

    spread(place, plane_peers, 0)
    norm_buf[8 + z] = add_up(range(8))
    spread(8 + z, [chip(zi, y, x) for zi in z_peers], 7)
    everything = add_up(range(8, 8 + ZN))
    norm_out[...] = jnp.broadcast_to(jnp.sqrt(jnp.sum(everything, keepdims=True)), norm_out.shape)

    grad_copy.wait()
    for buf, out, s in ((pred, pred_out, 0), (sens, sens_out, 1)):
        for copy in out_copies(buf, out, s):
            copy.wait()
    for m in range(MATS):
        hand_over(m, slice(0, hidden if m else 384)).wait_send()

    for mats, lanes in ((slice(1, MATS), slice(0, hidden)), (slice(0, 1), slice(0, 384))):
        sent = (
            wg.at[:, mats, 0 : ZN - 1, 0, 0, 0, :, lanes],
            wg.at[:, mats, :, :, 0, 0, :, lanes],
            wg.at[:, mats, :, 0, 0, 0, :, lanes],
            wg.at[:, mats, :, :, :, 0, :, lanes],
        )
        for sems in (ag_send, rs_send):
            for kind, ref in enumerate(sent):
                remote(ref, ref, sends(sems, kind, lanes), out_recv.at[0], sibling).wait_send()


def train_call(plane, segments, extents, adjoint, first, square, head, biases):
    ZN, YN, XN = plane
    past, span, hidden = segments.shape[1], adjoint.shape[0], square.shape[3]
    windows = segments.shape[0] // 2
    tile = windows
    half = hidden // (ZN * YN * XN) // 2
    sizes = (ZN, YN, XN, windows, tile, past, span, hidden)
    DMA = pltpu.SemaphoreType.DMA
    vmem = pl.BlockSpec(memory_space=pltpu.VMEM)
    hbm = pl.BlockSpec(memory_space=pl.ANY)
    count = 2 * MATS
    flops = 2 * 2 * 3 * windows * hidden * (6 * hidden + 2 * 128)
    lengths = extents.reshape(-1, 128)
    return pl.pallas_call(
        functools.partial(train_kernel, sizes),
        out_shape=(
            jax.ShapeDtypeStruct((span, 1, 2 * windows), F32),
            jax.ShapeDtypeStruct((past, 1, 2 * windows), F32),
            jax.ShapeDtypeStruct((MATS, 2, half, hidden), F32),
            jax.ShapeDtypeStruct((8, 128), F32),
        ),
        in_specs=[hbm] * 7,
        out_specs=(hbm, hbm, vmem, vmem),
        scratch_shapes=[
            pltpu.VMEM((2, MATS, ZN, YN, XN, 2, half, hidden), BF),
            pltpu.VMEM((MATS, half, hidden), BF),
            pltpu.VMEM((2, MATS, ZN, YN, XN, 2, half, hidden), BF),
            pltpu.VMEM((CORE_SLOTS, ZN, YN, XN, half, hidden), BF),
            pltpu.VMEM((DIAG_SLOTS, ZN, half, hidden), BF),
            pltpu.VMEM((PLAIN_SLOTS, ZN, half, hidden), BF),
            pltpu.VMEM((PAIR_SLOTS, ZN, half, hidden), BF),
            pltpu.VMEM((count, ZN - 1, half, hidden), BF),
            pltpu.VMEM((2, MATS, half, hidden), F32),
            pltpu.VMEM((2, 4, hidden, windows), BF),
            pltpu.VMEM((2, 128, windows), BF),
            pltpu.VMEM((windows, hidden), BF),
            pltpu.VMEM((2, 4, windows, hidden), BF),
            pltpu.VMEM((3, windows, hidden), BF),
            pltpu.VMEM((windows, 128), F32),
            pltpu.VMEM((windows, 128), BF),
            pltpu.VMEM((windows, 128), BF),
            pltpu.VMEM((2, 128, windows), BF),
            pltpu.VMEM((128, hidden), F32),
            pltpu.VMEM((128, hidden), F32),
            pltpu.VMEM((128, 128), F32),
            pltpu.VMEM((windows, past), F32),
            pltpu.VMEM((span, windows), F32),
            *(pltpu.VMEM(a.shape, a.dtype) for a in (lengths, first, square, head, biases)),
            pltpu.VMEM((2, span, windows), F32),
            pltpu.VMEM((2, span, 1, windows), F32),
            pltpu.VMEM((2, past, 1, windows), F32),
            pltpu.VMEM((half, hidden), F32),
            pltpu.VMEM((8 + ZN, 8, 128), F32),
            DMA((MATS,)),
            DMA((MATS,)),
            DMA((4, 2)),
            DMA((count, 4 + ZN - 1)),
            DMA((4, 2)),
            DMA((count, 4 + ZN - 1)),
            DMA((3,)),
            DMA((3,)),
            DMA((9,)),
            DMA((7 + ZN - 1,)),
            DMA((7 + ZN - 1,)),
        ],
        compiler_params=pltpu.CompilerParams(
            collective_id=0, has_side_effects=True, vmem_limit_bytes=64 * 1024 * 1024
        ),
        cost_estimate=pl.CostEstimate(flops=flops, bytes_accessed=8_000_000, transcendentals=8 * windows * hidden),
        name="train",
    )(segments, adjoint, lengths, first, square, head, biases)


def update_kernel(past, span, *refs):
    sources, targets, norm_out = refs[0:16], refs[16:34], refs[34]
    held, results, pad, in_sem, out_sem = refs[35:51], refs[51:67], *refs[67:70]
    arriving = [pltpu.make_async_copy(source, ref, in_sem.at[n]) for n, (source, ref) in enumerate(zip(sources, held))]
    leaving = [
        pltpu.make_async_copy(ref, target, out_sem.at[n]) for n, (ref, target) in enumerate(zip(held[0:2] + results, targets))
    ]
    for n in (2, 3, 0, 5, 9, 13, 1, 4, 8, 12, 6, 10, 14, 7, 11, 15):
        arriving[n].start()
    grads, norm, masters, momenta, variances = held[2], held[3], held[4:8], held[8:12], held[12:16]
    units = masters[3].shape[2]

    def rows(m, lane, width):
        return grads[m, :, :, lane : lane + width].reshape(units, width)

    arriving[2].wait()
    arriving[3].wait()
    norm_out[...] = norm[0:1, 0:1]
    factor = 1.0 / jnp.maximum(norm[0:1, 0:1], 1.0)
    for m in range(5):
        results[1][0, m] = rows(m + 1, 0, grads.shape[3])
    results[0][0] = rows(0, 0, 128)[:, 0:past]
    forecast = rows(0, 128, 128)
    pad[...] = jnp.zeros_like(pad)
    pad[0:units, :] = forecast
    results[3][0] = pad[...].T[span : span + 4, 0:units]
    results[2][0, :, 0:past] = rows(0, 256, 128)[:, 0:past]
    results[2][0, :, past : past + span] = forecast[:, 0:span]
    for n in (0, 1):
        arriving[n].wait()
        leaving[n].start()
    for n in (1, 0, 2, 3):
        leaving[2 + n].start()
        for state in range(3):
            arriving[4 + 4 * state + n].wait()
        updated = adamw(masters[n][...], results[n][...], momenta[n][...], variances[n][...], factor[None])
        for kind, value in enumerate(updated):
            results[4 * (kind + 1) + n][...] = value
            leaving[2 + 4 * (kind + 1) + n].start()
    for copy in leaving:
        copy.wait()


def update_call(prediction, sensitivity, grads, norm, state):
    hbm = pl.BlockSpec(memory_space=pl.ANY)
    sources = (prediction, sensitivity, grads, norm, *state)
    targets = (prediction, sensitivity, *(4 * list(state[:4])))
    return pl.pallas_call(
        functools.partial(update_kernel, sensitivity.shape[0], prediction.shape[0]),
        out_shape=tuple(jax.ShapeDtypeStruct(a.shape, F32) for a in targets) + (jax.ShapeDtypeStruct((1, 1), F32),),
        in_specs=[hbm] * len(sources),
        out_specs=tuple([hbm] * len(targets) + [pl.BlockSpec(memory_space=pltpu.VMEM)]),
        scratch_shapes=[pltpu.VMEM(a.shape, F32) for a in sources]
        + [pltpu.VMEM(a.shape, F32) for a in targets[2:]]
        + [pltpu.VMEM((128, 128), F32), pltpu.SemaphoreType.DMA((len(sources),)), pltpu.SemaphoreType.DMA((len(targets),))],
        name="update",
    )(*sources)


def turned(arrays):
    return [a.transpose(0, 2, 1) if n % 4 == 0 else a for n, a in enumerate(arrays)]


def kernel_shards(plane, segments, extents, adjoint, *state):
    state = turned(state)
    results = train_call(plane, segments, extents, adjoint.T, *state[:4])
    prediction, sensitivity, *updated, norm = update_call(*results, state)
    by_window = (prediction.transpose(1, 2, 0), sensitivity.transpose(1, 2, 0))
    return (*by_window, norm.reshape(()), *turned(updated))


STATE_SPECS = (
    P("section", None, "dp"),
    P("section", None, "dp", None),
    P("section", "dp", None),
    P("section", None, "dp"),
)


def solution(mesh):
    in_specs = (P("dp", None), P("dp"), P("dp", None)) + 3 * STATE_SPECS
    out_specs = (P("section", "dp", None), P("section", "dp", None), P()) + 4 * STATE_SPECS
    plane = PLANES.get(mesh.shape["dp"])
    shards = plain_shards if plane is None else functools.partial(kernel_shards, plane)
    return jax.shard_map(shards, mesh=mesh, in_specs=in_specs, out_specs=out_specs, check_vma=False)
```

```python
import functools

import jax
import jax.numpy as jnp
from jax import lax
from jax.experimental import pallas as pl
from jax.experimental.pallas import tpu as pltpu
from jax.sharding import PartitionSpec as P

STEP = 10


def dot_nn(a, b):
    return jnp.dot(a, b, preferred_element_type=jnp.float32)


def dot_tn(a, b):
    return lax.dot_general(a, b, (((0,), (0,)), ((), ())), preferred_element_type=jnp.float32)


def dot_nt(a, b):
    return lax.dot_general(a, b, (((1,), (1,)), ((), ())), preferred_element_type=jnp.float32)


def unit_rows(first, square, head, biases):
    units = first.shape[1]
    return jnp.concatenate(
        [square.transpose(1, 0, 2).reshape(units, -1), first.T, head, biases.T], axis=1
    )


def from_unit_rows(rows, past, hidden, out):
    wide = 5 * hidden
    square = rows[:, :wide].reshape(-1, 5, hidden).transpose(1, 0, 2)
    first = rows[:, wide : wide + past].T
    head = rows[:, wide + past : wide + past + out]
    biases = rows[:, wide + past + out :].T
    return first, square, head, biases


def plain_forward(weights, resid):
    first, square, head, biases = weights
    past = resid.shape[1]
    acts, slopes = [resid.astype(jnp.bfloat16)], []
    for k in range(4):
        z = dot_nn(acts[-1], first if k == 0 else square[k - 1]) + biases[k].astype(jnp.float32)
        sig = jax.nn.sigmoid(z)
        acts.append((z * sig).astype(jnp.bfloat16))
        slopes.append(sig * (1.0 + z * (1.0 - sig)))
    theta_b = dot_nn(acts[4], square[3]).astype(jnp.bfloat16)
    theta_f = dot_nn(acts[4], square[4]).astype(jnp.bfloat16)
    backcast = dot_nn(theta_b, head[:, :past])
    part = dot_nn(theta_f, head[:, past:])
    return backcast, part, (acts, slopes, theta_b, theta_f)


def plain_backward(weights, saved, e, f):
    first, square, head, biases = weights
    acts, slopes, theta_b, theta_f = saved
    past = e.shape[1]
    head_grad = jnp.concatenate([dot_tn(theta_b, e), dot_tn(theta_f, f)], axis=1)
    u_b = dot_nt(e, head[:, :past]).astype(jnp.bfloat16)
    u_f = dot_nt(f, head[:, past:]).astype(jnp.bfloat16)
    squares = [None, None, None, dot_tn(acts[4], u_b), dot_tn(acts[4], u_f)]
    da = dot_nt(u_b, square[3]) + dot_nt(u_f, square[4])
    bias_grads = [None] * 4
    first_grad = None
    for k in (3, 2, 1, 0):
        dz = (da * slopes[k]).astype(jnp.bfloat16)
        bias_grads[k] = jnp.sum(dz, axis=0, dtype=jnp.float32)
        grad = dot_tn(acts[k], dz)
        if k == 0:
            first_grad = grad
        else:
            squares[k - 1] = grad
        da = dot_nt(dz, first if k == 0 else square[k - 1])
    return da, (first_grad, jnp.stack(squares), head_grad, jnp.stack(bias_grads))


def adamw(master, gradient, momentum, variance, factor):
    clipped = gradient * factor
    moment_new = 0.9 * momentum + 0.1 * clipped
    variance_new = 0.999 * variance + 0.001 * clipped * clipped
    ratio = moment_new / (1.0 - 0.9**STEP) / (jnp.sqrt(variance_new / (1.0 - 0.999**STEP)) + 1e-08)
    return master - 0.05 * (ratio + 0.01 * master), moment_new, variance_new


def plain_shards(segments, extents, adjoint, *state):
    masters, momenta, variances = state[:4], state[4:8], state[8:]
    core = lax.axis_index("section")
    past, span = segments.shape[1], adjoint.shape[1]
    windows = segments.shape[0] // 2
    hidden = masters[1].shape[3]
    mine = [
        lax.dynamic_slice_in_dim(v, core * windows, windows, 0) for v in (segments, extents, adjoint)
    ]
    seg, ext, adj = mine
    rows = unit_rows(*(m[0].astype(jnp.bfloat16) for m in masters))
    rows = lax.all_gather(rows, "dp", axis=0, tiled=True)
    rows = lax.all_gather(rows, "section", axis=0)
    blocks = [from_unit_rows(rows[b], past, hidden, past + span) for b in range(2)]
    mask = (
        lax.broadcasted_iota(jnp.int32, (windows, past), 1) >= past - ext[:, None]
    ).astype(jnp.float32)
    r0 = seg * mask
    backcast, part0, saved0 = plain_forward(blocks[0], r0)
    r1 = (r0 - backcast) * mask
    _, part1, saved1 = plain_forward(blocks[1], r1)
    forecast = part0.astype(jnp.bfloat16).astype(jnp.float32) + part1
    f = adj.astype(jnp.bfloat16)
    zero = jnp.zeros_like(r0)
    da1, grads1 = plain_backward(blocks[1], saved1, (-(zero * mask)).astype(jnp.bfloat16), f)
    dr1 = zero * mask + da1
    t = dr1.astype(jnp.bfloat16).astype(jnp.float32)
    da0, grads0 = plain_backward(blocks[0], saved0, (-(t * mask)).astype(jnp.bfloat16), f)
    dr0 = (t * mask + da0) * mask

    def by_section(first_block, second_block):
        mine, other = (
            jnp.where(core == 0, first_block, second_block),
            jnp.where(core == 0, second_block, first_block),
        )
        got = lax.ppermute(other, "section", [(0, 1), (1, 0)])
        return jnp.where(
            core == 0, jnp.concatenate([mine, got]), jnp.concatenate([got, mine])
        )[None]

    prediction = by_section(part0, forecast)
    sensitivity = by_section(dr0, dr1)
    packed = jnp.stack([unit_rows(*grads0), unit_rows(*grads1)])
    packed = lax.psum_scatter(packed, "section", scatter_dimension=0, tiled=False)
    packed = lax.psum_scatter(packed, "dp", scatter_dimension=0, tiled=True)
    norm = jnp.sqrt(lax.psum(jnp.sum(packed * packed), ("section", "dp")))
    factor = 1.0 / jnp.maximum(norm, 1.0)
    summed = [g[None] for g in from_unit_rows(packed, past, hidden, past + span)]
    updated = [adamw(*four, factor) for four in zip(masters, summed, momenta, variances)]
    return (
        prediction,
        sensitivity,
        norm,
        *summed,
        *(u[0] for u in updated),
        *(u[1] for u in updated),
        *(u[2] for u in updated),
    )


PLANES = {16: (4, 2, 2)}
MESH = pl.DeviceIdType.MESH
MATS = 6
CORE_SLOTS, DIAG_SLOTS, PLAIN_SLOTS, PAIR_SLOTS = 4, 4, 6, 4
BF, F32 = jnp.bfloat16, jnp.float32


ORDER = ((0, 5), (1, 4), (1, 5), (1, 3), (1, 2), (1, 1), (0, 4), (0, 3), (0, 2), (0, 1), (1, 0), (0, 0))


def remote(src, dst, send_sem, recv_sem, device):
    return pltpu.make_async_remote_copy(
        src_ref=src, dst_ref=dst, send_sem=send_sem, recv_sem=recv_sem, device_id=device, device_id_type=MESH
    )


def train_kernel(
    sizes,
    seg_hbm, adj_hbm, ext_hbm, first_hbm, square_hbm, head_hbm, biases_hbm,
    pred_out, sens_out, grad_out, norm_out,
    wg, handed, gp, from_core, from_diag, from_plain, from_pair, from_z, total,
    act_t, in_t, theta_keep, slope, work, resid, mask, f_ref, e_t, bias_t, bias_sum, pad,
    seg, adj, ext, first, square, head, biases, part_t, pred, sens, squares, norm_buf,
    own_send, own_recv, ag_send, ag_recv, rs_send, rs_recv, out_send, out_recv, local_sem, norm_send, norm_recv,
):
    ZN, YN, XN, windows, tile, past, span, hidden = sizes
    units = ZN * YN * XN
    core, dp = lax.axis_index("section"), lax.axis_index("dp")
    x, y, z = lax.rem(dp, XN), lax.rem(lax.div(dp, XN), YN), lax.div(dp, XN * YN)
    other, xo, yo = 1 - core, 1 - x, 1 - y
    near_y, near_x = y + core * (yo - y), xo + core * (x - xo)
    far_y, far_x = yo + core * (y - yo), x + core * (xo - x)

    def chip(zi, yi, xi):
        return (core, (zi * YN + yi) * XN + xi)

    sibling = (other, dp)
    z_peers = [lax.rem(z + step, ZN) for step in range(1, ZN)]

    row0 = core * windows
    loads = [
        pltpu.make_async_copy(seg_hbm.at[pl.ds(row0, windows), :], seg, local_sem.at[0]),
        pltpu.make_async_copy(adj_hbm.at[:, pl.ds(row0, windows)], adj, local_sem.at[1]),
    ]
    small_loads = [
        pltpu.make_async_copy(source, target, local_sem.at[4 + n])
        for n, (source, target) in enumerate(
            [(first_hbm, first), (head_hbm, head), (biases_hbm, biases), (square_hbm, square), (ext_hbm, ext)]
        )
    ]
    for load in small_loads:
        load.start()

    barrier = pltpu.get_barrier_semaphore()
    plane_peers = [
        (ci, (z * YN + yi) * XN + xi) for ci in (core, other) for yi in (y, yo) for xi in (x, xo)
    ][1:]
    peers = plane_peers + [(ci, (zi * YN + y) * XN + x) for zi in z_peers for ci in (core, other)]
    for peer in peers:
        pl.semaphore_signal(barrier, inc=1, device_id=peer, device_id_type=MESH)

    rows = hidden // units
    half_rows = rows // 2

    def put_own(m, value, lanes):
        halves = value.astype(BF).reshape(2, half_rows, -1)
        for h in range(2):
            pl.when(core == h)(functools.partial(put_half, m, halves[h], halves[1 - h], lanes))

    def put_half(m, kept, given, lanes):
        wg[core, m, z, y, x, core, :, lanes] = kept
        handed[m, :, lanes] = given

    for load in small_loads[:3]:
        load.wait()
    pad[...] = jnp.zeros_like(pad)
    pad[0:rows, 0:past] = first[0] * 0.5
    put_own(0, pad[0:rows, :], slice(0, 128))
    pad[...] = jnp.zeros_like(pad)
    pad[span : span + 4, 0:rows] = biases[0] * 0.5
    bias_cols = pad[...].T[0:rows]
    pad[...] = jnp.zeros_like(pad)
    pad[0:rows, 0:span] = head[0, :, past : past + span]
    put_own(0, pad[0:rows, :] + bias_cols, slice(128, 256))
    pad[...] = jnp.zeros_like(pad)
    pad[0:rows, 0:past] = head[0, :, 0:past]
    put_own(0, pad[0:rows, :], slice(256, 384))
    pl.semaphore_wait(barrier, len(peers))

    def hand_over(m, lanes):
        return remote(
            handed.at[m, :, lanes], wg.at[core, m, z, y, x, other, :, lanes], own_send.at[m], own_recv.at[m], sibling
        )

    def pack(m):
        put_own(m, square[0, m - 1] * 0.5 if m < 4 else square[0, m - 1], slice(0, hidden))


    def of(i):
        b = jnp.where(jnp.logical_and(i >= 5, i <= 10), 1, 0)
        return b, jnp.where(i <= 4, i, jnp.where(i <= 10, i - 5, 5))

    def sends(sems, kind, lanes):
        return sems.at[kind, 0 if lanes.stop == hidden else 1]

    def z_copies(i, lanes):
        b, m = of(i)
        part = wg.at[b, m, z, y, x, core, :, lanes]
        return [
            remote(part, part, sends(ag_send, 0, lanes), ag_recv.at[i, s], chip(zi, y, x)) for s, zi in enumerate(z_peers)
        ]

    def line_copies(i, lanes):
        b, m = of(i)
        given = wg.at[b, m, z, y, x, other, :, lanes]
        return [
            remote(
                handed.at[m, :, lanes], given, sends(ag_send, 0, lanes), ag_recv.at[i, s], (other, (zi * YN + y) * XN + x)
            )
            for s, zi in enumerate(z_peers)
        ]

    def column_copies(i, lanes):
        b, m = of(i)
        part = wg.at[b, m, :, y, x, core, :, lanes]
        return [
            remote(part, part, sends(ag_send, 1, lanes), ag_recv.at[i, 3], chip(z, near_y, near_x)),
            remote(part, part, sends(ag_send, 1, lanes), ag_recv.at[i, 4], chip(z, far_y, far_x)),
        ]

    def corner_copy(i, lanes):
        b, m = of(i)
        part = wg.at[b, m, :, near_y, near_x, core, :, lanes]
        return remote(part, part, sends(ag_send, 2, lanes), ag_recv.at[i, 5], chip(z, far_y, far_x))

    def core_copy(i, lanes):
        b, m = of(i)
        part = wg.at[b, m, :, :, :, core, :, lanes]
        return remote(part, part, sends(ag_send, 3, lanes), ag_recv.at[i, 6], sibling)

    def by_lanes(m, step):
        if isinstance(m, int):
            step(slice(0, hidden if m else 384))
            return
        pl.when(m == 0)(lambda: step(slice(0, 384)))
        pl.when(m > 0)(lambda: step(slice(0, hidden)))

    def start_all(copies):
        for copy in copies:
            copy.start()

    zeros_tile = jnp.zeros((tile, 128), F32)

    def prepare(t, carry):
        at = pl.ds(t * tile, tile)
        resid[at, :] = zeros_tile
        resid[at, 0:past] = seg[at, :]
        return carry

    def prepare_mask(g, carry):
        lengths = ext[pl.ds(core * (windows // 128) + g, 1), :]
        position = lax.broadcasted_iota(jnp.int32, (128, 128), 0)
        keep = jnp.where(position >= past - lengths, 1.0, 0.0).astype(F32).T
        at = pl.ds(pl.multiple_of(g * 128, 128), 128)
        pad[0:span, :] = adj[:, at]
        f_ref[at, :] = pad[...].T.astype(BF)
        mask[at, :] = keep.astype(BF)
        resid[at, :] = resid[at, :] * keep
        return carry

    tiles = windows // tile
    part_tile = windows // 2

    def matrix(b, m):
        return wg[b, m].reshape(hidden, hidden)

    def small(b, lane):
        return wg[b, 0, :, :, :, :, :, lane : lane + 128].reshape(hidden, 128)

    def store_layer(b, k, at, v):
        p = 1.0 + jnp.tanh(v)
        a = v * p
        rate = p + a * (2.0 - p)
        slope[b, k, at, :] = rate.astype(BF)
        low = a.astype(BF)
        act_t[b, k, :, at] = low.T
        return low

    def halves(body):
        for t in range(2):
            body(slice(t * windows // 2, (t + 1) * windows // 2))

    def layer_zero(b):
        bias_t[...] = small(b, 128).astype(F32).T

        def body(at):
            a = resid[at, :].astype(BF)
            in_t[b, :, at] = a.T
            work[0, at, :] = store_layer(b, 0, at, dot_nt(a, small(b, 0)) + bias_t[span : span + 1, :])

        halves(body)

    def layer_next(b, k):
        source, target = lax.rem(k + 1, 2), lax.rem(k, 2)

        def body(at):
            v = dot_nn(work[source, at, :], matrix(b, k)) + bias_t[pl.ds(span + k, 1), :]
            work[target, at, :] = store_layer(b, k, at, v)

        halves(body)

    def grid(value):
        return value.astype(BF).reshape(ZN, YN, XN, 2, half_rows, -1)

    def backcast_step():
        def body(at):
            theta = dot_nn(work[1, at, :], matrix(0, 4)).astype(BF)
            theta_keep[at, :] = theta
            resid[at, :] = (resid[at, :] - dot_nn(theta, small(0, 256))) * mask[at, :].astype(F32)

        halves(body)

    def put_rows(buf, b, at, value):
        for row in range(value.shape[0]):
            buf[b, row, :, at] = value[row : row + 1]

    def late_theta(b, m):
        theta_t = act_t.at[1, 0]
        theta_t[...] = dot_nn(matrix(b, m).T, act_t[b, 3]).astype(BF)

        @pl.when(m == 4)
        def _():
            gp[b, 0, :, :, :, :, :, 256:384] = grid(dot_nt(theta_t[...], e_t[b]))

        @pl.when(m == 5)
        def _():
            grad = grid(dot_nn(theta_t[...], f_ref[...]))
            gp[b, 0, :, :, :, :, :, 128:256] = gp[b, 0, :, :, :, :, :, 128:256] + grad
            part_t[b] = dot_nn(small(b, 128).T, theta_t[...])[0:span]

    def forecasts():
        put_rows(pred, 0, slice(0, windows), part_t[0])
        put_rows(pred, 1, slice(0, windows), part_t[0].astype(BF).astype(F32) + part_t[1])

    count = 2 * MATS

    def delayed(lag, t, step):
        pl.when(jnp.logical_and(t >= lag, t < count + lag))(lambda: step(t - lag))

    def staged(lag, t, step):
        early = t - lag + 1
        pl.when(jnp.logical_and(early >= (2 if lag == 2 else 1), early <= 2))(lambda: step(early))
        unit = t - lag
        pl.when(jnp.logical_and(unit >= 3, unit < count))(lambda: step(unit))
        if lag == 6:
            pl.when(t == 4)(lambda: step(0))

    def gather_line(i):
        b, m = of(i)

        pl.when(b == core)(lambda: by_lanes(m, lambda lanes: start_all(line_copies(i, lanes) + z_copies(i, lanes))))

    def gather_columns(i):
        b, m = of(i)

        def step(lanes):
            pl.when(b != core)(lambda: hand_over(m, lanes).wait_recv())
            for copy in z_copies(i, lanes):
                copy.wait_recv()
            start_all(column_copies(i, lanes))

        by_lanes(m, step)

    def gather_corner(i):
        def step(lanes):
            column_copies(i, lanes)[0].wait_recv()
            corner_copy(i, lanes).start()

        by_lanes(of(i)[1], step)

    def gather_core(i):
        def step(lanes):
            column_copies(i, lanes)[1].wait_recv()
            corner_copy(i, lanes).wait_recv()
            core_copy(i, lanes).start()

        by_lanes(of(i)[1], step)

    def arrived(i):
        by_lanes(of(i)[1], lambda lanes: core_copy(i, lanes).wait_recv())

    def forward_unit(i):
        arrived(i)
        b, m = of(i)
        pl.when(m == 0)(lambda: layer_zero(b))
        pl.when(jnp.logical_and(m >= 1, m <= 3))(lambda: layer_next(b, m))
        pl.when(m == 4)(backcast_step)

        @pl.when(jnp.logical_or(i == 4, i == 8))
        def _():
            pl.when(b == 1)(lambda: feed(b))
            pl.when(b == 0)(lambda: feed_forward(b))
            def one(n, carry):
                pl.when(jnp.logical_and(b == 1, n == 5))(lambda: gather_core(10))
                theta_grad(b, n)
                scatter_start(jnp.where(b == 0, 0, n - 3))
                return carry

            lax.fori_loop(jnp.where(b == 1, 4, 5), MATS, one, 0)

    def gather_step(t, carry):
        pl.when(t == 12)(lambda: scatter_core(0))
        pl.when(t == 15)(lambda: scatter_diag(0))
        pl.when(jnp.logical_and(t >= 4, t != 14))(lambda: gather_core(t - 4))
        delayed(2, t, gather_corner)
        delayed(0, t, gather_columns)
        pl.when(t + 4 < count)(lambda: gather_line(t + 4))

        pl.when(t == 0)(lambda: start_all(loads))

        @pl.when(t == 2)
        def _():
            for load in loads + small_loads[4:]:
                load.wait()
            lax.fori_loop(0, tiles, prepare, 0)
            pad[...] = jnp.zeros_like(pad)
            lax.fori_loop(0, windows // 128, prepare_mask, 0)

        pl.when(jnp.logical_and(t >= 5, t < 14))(lambda: forward_unit(t - 5))
        return carry

    def out_copies(buf, out, s):
        at = pl.ds(row0, windows)
        return [
            pltpu.make_async_copy(buf.at[core], out.at[:, :, at], local_sem.at[2 + s]),
            remote(buf.at[other], out.at[:, :, at], out_send.at[s], out_recv.at[s], sibling),
        ]


    def back_of(j):
        if isinstance(j, int):
            return ORDER[j]
        b = jnp.where(jnp.logical_or(jnp.logical_and(j >= 1, j <= 5), j == 10), 1, 0)
        early = jnp.where(j == 1, 4, jnp.where(j <= 2, 5, 6 - j))
        return b, jnp.where(j <= 5, early, jnp.where(j == 6, 4, jnp.where(j <= 9, 10 - j, 0)))

    def to_core(j, lanes):
        b, m = back_of(j)
        return remote(
            gp.at[b, m, :, :, :, other, :, lanes], from_core.at[lax.rem(j, CORE_SLOTS), :, :, :, :, lanes],
            sends(rs_send, 3, lanes), rs_recv.at[j, 0], sibling,
        )

    def to_far(j, lanes):
        b, m = back_of(j)
        device = chip(z, far_y, far_x)
        return [
            remote(
                gp.at[b, m, :, yo, xo, core, :, lanes], from_diag.at[lax.rem(j, DIAG_SLOTS), :, :, lanes],
                sends(rs_send, 1, lanes), rs_recv.at[j, 1], device,
            ),
            remote(
                gp.at[b, m, :, far_y, far_x, core, :, lanes], from_plain.at[lax.rem(j, PLAIN_SLOTS), :, :, lanes],
                sends(rs_send, 1, lanes), rs_recv.at[j, 2], device,
            ),
        ]

    def to_near(j, lanes):
        b, m = back_of(j)
        return remote(
            gp.at[b, m, :, near_y, near_x, core, :, lanes], from_pair.at[lax.rem(j, PAIR_SLOTS), :, :, lanes],
            sends(rs_send, 2, lanes), rs_recv.at[j, 3], chip(z, near_y, near_x),
        )

    def to_z(j, lanes):
        b, m = back_of(j)
        return [
            remote(
                gp.at[b, m, zi, y, x, core, :, lanes], from_z.at[j, s, :, lanes],
                sends(rs_send, 0, lanes), rs_recv.at[j, 4 + s], chip(zi, y, x),
            )
            for s, zi in enumerate(z_peers)
        ]

    def scatter_start(j):
        by_lanes(back_of(j)[1], lambda lanes: to_core(j, lanes).start())

    def scatter_core(j):
        b, m = back_of(j)

        def step(lanes):
            to_core(j, lanes).wait_recv()
            part = gp[b, m, :, :, :, core, :, lanes] + from_core[lax.rem(j, CORE_SLOTS), :, :, :, :, lanes]
            gp[b, m, :, :, :, core, :, lanes] = part
            start_all(to_far(j, lanes))

        by_lanes(m, step)

    def scatter_diag(j):
        b, m = back_of(j)

        def step(lanes):
            to_far(j, lanes)[0].wait_recv()
            part = gp[b, m, :, near_y, near_x, core, :, lanes] + from_diag[lax.rem(j, DIAG_SLOTS), :, :, lanes]
            gp[b, m, :, near_y, near_x, core, :, lanes] = part
            to_near(j, lanes).start()

        by_lanes(m, step)

    def scatter_plane(j):
        b, m = back_of(j)

        def step(lanes):
            to_far(j, lanes)[1].wait_recv()
            to_near(j, lanes).wait_recv()
            value = gp[b, m, :, y, x, core, :, lanes].astype(F32)
            value = value + from_plain[lax.rem(j, PLAIN_SLOTS), :, :, lanes].astype(F32)
            value = value + from_pair[lax.rem(j, PAIR_SLOTS), :, :, lanes].astype(F32)
            gp[b, m, :, y, x, core, :, lanes] = value.astype(BF)
            start_all(to_z(j, lanes))

        by_lanes(m, step)

    def scatter_z(j):
        b, m = back_of(j)

        def step(lanes):
            for copy in to_z(j, lanes):
                copy.wait_recv()
            value = gp[b, m, z, y, x, core, :, lanes].astype(F32)
            for s in range(ZN - 1):
                value = value + from_z[j, s, :, lanes].astype(F32)
            total[b, m, :, lanes] = value
            squares[:, lanes] = squares[:, lanes] + value * value

        by_lanes(m, step)

    def add_rows(value):
        return jnp.sum(value.reshape(-1, 8, hidden), axis=0)

    def put_bias(k, acc):
        bias_sum[pl.ds(span + k, 1), :] = jnp.sum(acc, axis=0, keepdims=True)

    def feed(b):
        pl.when(b == 1)(lambda: resid.__setitem__(..., jnp.zeros_like(resid)))
        e = (-(resid[...] * mask[...].astype(F32))).astype(BF)
        e_t[b] = e.T
        work[0] = dot_nt(e, small(b, 256)).astype(BF)
        work[2] = dot_nt(f_ref[...], small(b, 128)).astype(BF)

    def feed_forward(b):
        work[2] = dot_nt(f_ref[...], small(b, 128)).astype(BF)

    def put_dz(b, k, da):
        sums = []

        def body(at):
            dz = da(at) * slope[b, k, at, :].astype(F32)
            work[k % 2 if isinstance(k, int) else lax.rem(k, 2), at, :] = dz.astype(BF)
            sums.append(add_rows(dz))

        halves(body)
        bias_sum[pl.ds(span + k, 1), :] = jnp.sum(sums[0] + sums[1], axis=0, keepdims=True)

    def theta_step(b):
        put_dz(
            b, 3, lambda at: 0.5 * (dot_nt(work[0, at, :], matrix(b, 4)) + dot_nt(work[2, at, :], matrix(b, 5)))
        )

    def layer_back(b, k):
        source = lax.rem(k, 2)
        gp[b, k] = grid(dot_nn(act_t[b, k - 1], work[source]))
        put_dz(b, k - 1, lambda at: dot_nt(work[source, at, :], matrix(b, k)))

    def theta_grad(b, m):
        gp[b, m] = grid(dot_nn(act_t[b, 3], work[jnp.where(m == 4, 0, 2)]))

    def first_grads(b):
        gp[b, 0, :, :, :, :, :, 0:128] = grid(dot_nn(in_t[b], work[0]).T)
        gp[b, 0, :, :, :, :, :, 128:256] = grid(bias_sum[...].T)
        pl.when(b == 0)(backcast_grad)

    def backcast_grad():
        gp[0, 0, :, :, :, :, :, 256:384] = grid(dot_nn(e_t[0], theta_keep[...]).T)

    def input_grad(b):
        for t in range(2):
            at = slice(t * windows // 2, (t + 1) * windows // 2)
            keep = mask[at, :].astype(F32)
            dr = resid[at, :] * keep + 2.0 * dot_nn(work[0, at, :], small(b, 0))

            @pl.when(b == 1)
            def _():
                seg[at, :] = dr[:, 0:past]
                resid[at, :] = dr.astype(BF).astype(F32)

            @pl.when(b == 0)
            def _():
                put_rows(sens, 0, at, (dr * keep).T[0:past])

    def late_rows():
        for g in range(windows // 128):
            at = slice(g * 128, (g + 1) * 128)
            pad[:, 0:past] = seg[at, :]
            put_rows(sens, 1, at, pad[...].T[0:past])

    bias_sum[...] = jnp.zeros_like(bias_sum)
    squares[...] = jnp.zeros_like(squares)
    total[...] = jnp.zeros_like(total)

    def back_step(j, carry):
        b, m = back_of(j)

        staged(6, j, scatter_plane)
        staged(4, j, scatter_diag)
        staged(2, j, scatter_core)

        @pl.when(j == 2)
        def _():
            arrived(9)
            arrived(10)
            theta_step(1)
            scatter_core(1)

        pl.when(jnp.logical_and(m >= 1, m <= 3))(lambda: layer_back(b, m))

        @pl.when(jnp.logical_or(j == 6, j == count - 1))
        def _():
            block = jnp.where(j == 6, 1, 0)
            first_grads(block)
            pl.when(j == 6)(lambda: input_grad(1))

        @pl.when(j == 6)
        def _():
            feed(0)
            theta_grad(0, 4)

        @pl.when(jnp.logical_or(j == 10, j == 11))
        def _():
            lax.fori_loop(jnp.where(j == 10, 4, 5), MATS, lambda n, carry: (late_theta(b, n), carry)[1], 0)

        pl.when(jnp.logical_and(j >= 3, j < count))(lambda: scatter_start(j))

        @pl.when(j == 6)
        def _():
            arrived(11)
            theta_step(0)

        @pl.when(j == count)
        def _():
            input_grad(0)
            forecasts()

        @pl.when(j == count + 1)
        def _():
            late_rows()

        @pl.when(j == count + 5)
        def _():
            start_all(out_copies(sens, sens_out, 1) + out_copies(pred, pred_out, 0))

        @pl.when(j >= count + 1)
        def _():
            scatter_z(2 * (j - count - 1))
            scatter_z(2 * (j - count - 1) + 1)

        return carry

    gather_line(0)
    hand_over(0, slice(0, 384)).start()
    small_loads[3].wait()
    for m in range(1, MATS):
        pack(m)
        if m < 4:
            gather_line(m)
        hand_over(m, slice(0, hidden)).start()
    lax.fori_loop(0, count + 4, gather_step, 0)

    lax.fori_loop(2, count + 7, back_step, 0)

    grad_copy = remote(total.at[other], grad_out.at[:, core], out_send.at[2], out_recv.at[2], sibling)
    grad_copy.start()
    grad_out[:, core] = total[core]
    sq = squares[:, 0:128] + squares[:, 128:256] + squares[:, 256:384] + squares[:, 384:512]
    place = (y * XN + x) * 2 + core
    norm_buf[place] = sq[0:8] + sq[8:16]

    def spread(sources, targets, first):
        copies = [
            remote(norm_buf.at[sources], norm_buf.at[sources], norm_send.at[first + s], norm_recv.at[first + s], device)
            for s, device in enumerate(targets)
        ]
        start_all(copies)
        for copy in copies:
            copy.wait()

    def add_up(slots):
        value = norm_buf[slots[0]]
        for slot in slots[1:]:
            value = value + norm_buf[slot]
        return value

    spread(place, plane_peers, 0)
    norm_buf[8 + z] = add_up(range(8))
    spread(8 + z, [chip(zi, y, x) for zi in z_peers], 7)
    everything = add_up(range(8, 8 + ZN))
    norm_out[...] = jnp.broadcast_to(jnp.sqrt(jnp.sum(everything, keepdims=True)), norm_out.shape)

    grad_copy.wait()
    for buf, out, s in ((pred, pred_out, 0), (sens, sens_out, 1)):
        for copy in out_copies(buf, out, s):
            copy.wait()
    for m in range(MATS):
        hand_over(m, slice(0, hidden if m else 384)).wait_send()

    for mats, lanes in ((slice(1, MATS), slice(0, hidden)), (slice(0, 1), slice(0, 384))):
        sent = (
            wg.at[:, mats, 0 : ZN - 1, 0, 0, 0, :, lanes],
            wg.at[:, mats, :, :, 0, 0, :, lanes],
            wg.at[:, mats, :, 0, 0, 0, :, lanes],
            wg.at[:, mats, :, :, :, 0, :, lanes],
        )
        for sems in (ag_send, rs_send):
            for kind, ref in enumerate(sent):
                remote(ref, ref, sends(sems, kind, lanes), out_recv.at[0], sibling).wait_send()


def train_call(plane, segments, extents, adjoint, first, square, head, biases):
    ZN, YN, XN = plane
    past, span, hidden = segments.shape[1], adjoint.shape[0], square.shape[3]
    windows = segments.shape[0] // 2
    tile = windows
    half = hidden // (ZN * YN * XN) // 2
    sizes = (ZN, YN, XN, windows, tile, past, span, hidden)
    DMA = pltpu.SemaphoreType.DMA
    vmem = pl.BlockSpec(memory_space=pltpu.VMEM)
    hbm = pl.BlockSpec(memory_space=pl.ANY)
    count = 2 * MATS
    flops = 2 * 2 * 3 * windows * hidden * (6 * hidden + 2 * 128)
    lengths = extents.reshape(-1, 128)
    return pl.pallas_call(
        functools.partial(train_kernel, sizes),
        out_shape=(
            jax.ShapeDtypeStruct((span, 1, 2 * windows), F32),
            jax.ShapeDtypeStruct((past, 1, 2 * windows), F32),
            jax.ShapeDtypeStruct((MATS, 2, half, hidden), F32),
            jax.ShapeDtypeStruct((8, 128), F32),
        ),
        in_specs=[hbm] * 7,
        out_specs=(hbm, hbm, vmem, vmem),
        scratch_shapes=[
            pltpu.VMEM((2, MATS, ZN, YN, XN, 2, half, hidden), BF),
            pltpu.VMEM((MATS, half, hidden), BF),
            pltpu.VMEM((2, MATS, ZN, YN, XN, 2, half, hidden), BF),
            pltpu.VMEM((CORE_SLOTS, ZN, YN, XN, half, hidden), BF),
            pltpu.VMEM((DIAG_SLOTS, ZN, half, hidden), BF),
            pltpu.VMEM((PLAIN_SLOTS, ZN, half, hidden), BF),
            pltpu.VMEM((PAIR_SLOTS, ZN, half, hidden), BF),
            pltpu.VMEM((count, ZN - 1, half, hidden), BF),
            pltpu.VMEM((2, MATS, half, hidden), F32),
            pltpu.VMEM((2, 4, hidden, windows), BF),
            pltpu.VMEM((2, 128, windows), BF),
            pltpu.VMEM((windows, hidden), BF),
            pltpu.VMEM((2, 4, windows, hidden), BF),
            pltpu.VMEM((3, windows, hidden), BF),
            pltpu.VMEM((windows, 128), F32),
            pltpu.VMEM((windows, 128), BF),
            pltpu.VMEM((windows, 128), BF),
            pltpu.VMEM((2, 128, windows), BF),
            pltpu.VMEM((128, hidden), F32),
            pltpu.VMEM((128, hidden), F32),
            pltpu.VMEM((128, 128), F32),
            pltpu.VMEM((windows, past), F32),
            pltpu.VMEM((span, windows), F32),
            *(pltpu.VMEM(a.shape, a.dtype) for a in (lengths, first, square, head, biases)),
            pltpu.VMEM((2, span, windows), F32),
            pltpu.VMEM((2, span, 1, windows), F32),
            pltpu.VMEM((2, past, 1, windows), F32),
            pltpu.VMEM((half, hidden), F32),
            pltpu.VMEM((8 + ZN, 8, 128), F32),
            DMA((MATS,)),
            DMA((MATS,)),
            DMA((4, 2)),
            DMA((count, 4 + ZN - 1)),
            DMA((4, 2)),
            DMA((count, 4 + ZN - 1)),
            DMA((3,)),
            DMA((3,)),
            DMA((9,)),
            DMA((7 + ZN - 1,)),
            DMA((7 + ZN - 1,)),
        ],
        compiler_params=pltpu.CompilerParams(
            collective_id=0, has_side_effects=True, vmem_limit_bytes=64 * 1024 * 1024
        ),
        cost_estimate=pl.CostEstimate(flops=flops, bytes_accessed=8_000_000, transcendentals=8 * windows * hidden),
        name="train",
    )(segments, adjoint, lengths, first, square, head, biases)


def update_kernel(past, span, *refs):
    sources, targets, norm_out = refs[0:16], refs[16:34], refs[34]
    held, results, pad, in_sem, out_sem = refs[35:51], refs[51:67], *refs[67:70]
    arriving = [pltpu.make_async_copy(source, ref, in_sem.at[n]) for n, (source, ref) in enumerate(zip(sources, held))]
    leaving = [
        pltpu.make_async_copy(ref, target, out_sem.at[n]) for n, (ref, target) in enumerate(zip(held[0:2] + results, targets))
    ]
    for n in (2, 3, 0, 5, 9, 13, 1, 4, 8, 12, 6, 10, 14, 7, 11, 15):
        arriving[n].start()
    grads, norm, masters, momenta, variances = held[2], held[3], held[4:8], held[8:12], held[12:16]
    units = masters[3].shape[2]

    def rows(m, lane, width):
        return grads[m, :, :, lane : lane + width].reshape(units, width)

    arriving[2].wait()
    arriving[3].wait()
    norm_out[...] = norm[0:1, 0:1]
    factor = 1.0 / jnp.maximum(norm[0:1, 0:1], 1.0)
    for m in range(5):
        results[1][0, m] = rows(m + 1, 0, grads.shape[3])
    results[0][0] = rows(0, 0, 128)[:, 0:past]
    forecast = rows(0, 128, 128)
    pad[...] = jnp.zeros_like(pad)
    pad[0:units, :] = forecast
    results[3][0] = pad[...].T[span : span + 4, 0:units]
    results[2][0, :, 0:past] = rows(0, 256, 128)[:, 0:past]
    results[2][0, :, past : past + span] = forecast[:, 0:span]
    for n in (0, 1):
        arriving[n].wait()
        leaving[n].start()
    for n in (1, 0, 2, 3):
        leaving[2 + n].start()
        for state in range(3):
            arriving[4 + 4 * state + n].wait()
        updated = adamw(masters[n][...], results[n][...], momenta[n][...], variances[n][...], factor[None])
        for kind, value in enumerate(updated):
            results[4 * (kind + 1) + n][...] = value
            leaving[2 + 4 * (kind + 1) + n].start()
    for copy in leaving:
        copy.wait()


def update_call(prediction, sensitivity, grads, norm, state):
    hbm = pl.BlockSpec(memory_space=pl.ANY)
    sources = (prediction, sensitivity, grads, norm, *state)
    targets = (prediction, sensitivity, *(4 * list(state[:4])))
    return pl.pallas_call(
        functools.partial(update_kernel, sensitivity.shape[0], prediction.shape[0]),
        out_shape=tuple(jax.ShapeDtypeStruct(a.shape, F32) for a in targets) + (jax.ShapeDtypeStruct((1, 1), F32),),
        in_specs=[hbm] * len(sources),
        out_specs=tuple([hbm] * len(targets) + [pl.BlockSpec(memory_space=pltpu.VMEM)]),
        scratch_shapes=[pltpu.VMEM(a.shape, F32) for a in sources]
        + [pltpu.VMEM(a.shape, F32) for a in targets[2:]]
        + [pltpu.VMEM((128, 128), F32), pltpu.SemaphoreType.DMA((len(sources),)), pltpu.SemaphoreType.DMA((len(targets),))],
        name="update",
    )(*sources)


def turned(arrays):
    return [a.transpose(0, 2, 1) if n % 4 == 0 else a for n, a in enumerate(arrays)]


def kernel_shards(plane, segments, extents, adjoint, *state):
    state = turned(state)
    results = train_call(plane, segments, extents, adjoint.T, *state[:4])
    prediction, sensitivity, *updated, norm = update_call(*results, state)
    by_window = (prediction.transpose(1, 2, 0), sensitivity.transpose(1, 2, 0))
    return (*by_window, norm.reshape(()), *turned(updated))


STATE_SPECS = (
    P("section", None, "dp"),
    P("section", None, "dp", None),
    P("section", "dp", None),
    P("section", None, "dp"),
)


def solution(mesh):
    in_specs = (P("dp", None), P("dp"), P("dp", None)) + 3 * STATE_SPECS
    out_specs = (P("section", "dp", None), P("section", "dp", None), P()) + 4 * STATE_SPECS
    plane = PLANES.get(mesh.shape["dp"])
    shards = plain_shards if plane is None else functools.partial(kernel_shards, plane)
    return jax.shard_map(shards, mesh=mesh, in_specs=in_specs, out_specs=out_specs, check_vma=False)
```

```python
import functools

import jax
import jax.numpy as jnp
from jax import lax
from jax.experimental import pallas as pl
from jax.experimental.pallas import tpu as pltpu
from jax.sharding import PartitionSpec as P

STEP = 10


def dot_nn(a, b):
    return jnp.dot(a, b, preferred_element_type=jnp.float32)


def dot_tn(a, b):
    return lax.dot_general(a, b, (((0,), (0,)), ((), ())), preferred_element_type=jnp.float32)


def dot_nt(a, b):
    return lax.dot_general(a, b, (((1,), (1,)), ((), ())), preferred_element_type=jnp.float32)


def unit_rows(first, square, head, biases):
    units = first.shape[1]
    return jnp.concatenate(
        [square.transpose(1, 0, 2).reshape(units, -1), first.T, head, biases.T], axis=1
    )


def from_unit_rows(rows, past, hidden, out):
    wide = 5 * hidden
    square = rows[:, :wide].reshape(-1, 5, hidden).transpose(1, 0, 2)
    first = rows[:, wide : wide + past].T
    head = rows[:, wide + past : wide + past + out]
    biases = rows[:, wide + past + out :].T
    return first, square, head, biases


def plain_forward(weights, resid):
    first, square, head, biases = weights
    past = resid.shape[1]
    acts, slopes = [resid.astype(jnp.bfloat16)], []
    for k in range(4):
        z = dot_nn(acts[-1], first if k == 0 else square[k - 1]) + biases[k].astype(jnp.float32)
        sig = jax.nn.sigmoid(z)
        acts.append((z * sig).astype(jnp.bfloat16))
        slopes.append(sig * (1.0 + z * (1.0 - sig)))
    theta_b = dot_nn(acts[4], square[3]).astype(jnp.bfloat16)
    theta_f = dot_nn(acts[4], square[4]).astype(jnp.bfloat16)
    backcast = dot_nn(theta_b, head[:, :past])
    part = dot_nn(theta_f, head[:, past:])
    return backcast, part, (acts, slopes, theta_b, theta_f)


def plain_backward(weights, saved, e, f):
    first, square, head, biases = weights
    acts, slopes, theta_b, theta_f = saved
    past = e.shape[1]
    head_grad = jnp.concatenate([dot_tn(theta_b, e), dot_tn(theta_f, f)], axis=1)
    u_b = dot_nt(e, head[:, :past]).astype(jnp.bfloat16)
    u_f = dot_nt(f, head[:, past:]).astype(jnp.bfloat16)
    squares = [None, None, None, dot_tn(acts[4], u_b), dot_tn(acts[4], u_f)]
    da = dot_nt(u_b, square[3]) + dot_nt(u_f, square[4])
    bias_grads = [None] * 4
    first_grad = None
    for k in (3, 2, 1, 0):
        dz = (da * slopes[k]).astype(jnp.bfloat16)
        bias_grads[k] = jnp.sum(dz, axis=0, dtype=jnp.float32)
        grad = dot_tn(acts[k], dz)
        if k == 0:
            first_grad = grad
        else:
            squares[k - 1] = grad
        da = dot_nt(dz, first if k == 0 else square[k - 1])
    return da, (first_grad, jnp.stack(squares), head_grad, jnp.stack(bias_grads))


def adamw(master, gradient, momentum, variance, factor):
    clipped = gradient * factor
    moment_new = 0.9 * momentum + 0.1 * clipped
    variance_new = 0.999 * variance + 0.001 * clipped * clipped
    ratio = moment_new / (1.0 - 0.9**STEP) / (jnp.sqrt(variance_new / (1.0 - 0.999**STEP)) + 1e-08)
    return master - 0.05 * (ratio + 0.01 * master), moment_new, variance_new


def plain_shards(segments, extents, adjoint, *state):
    masters, momenta, variances = state[:4], state[4:8], state[8:]
    core = lax.axis_index("section")
    past, span = segments.shape[1], adjoint.shape[1]
    windows = segments.shape[0] // 2
    hidden = masters[1].shape[3]
    mine = [
        lax.dynamic_slice_in_dim(v, core * windows, windows, 0) for v in (segments, extents, adjoint)
    ]
    seg, ext, adj = mine
    rows = unit_rows(*(m[0].astype(jnp.bfloat16) for m in masters))
    rows = lax.all_gather(rows, "dp", axis=0, tiled=True)
    rows = lax.all_gather(rows, "section", axis=0)
    blocks = [from_unit_rows(rows[b], past, hidden, past + span) for b in range(2)]
    mask = (
        lax.broadcasted_iota(jnp.int32, (windows, past), 1) >= past - ext[:, None]
    ).astype(jnp.float32)
    r0 = seg * mask
    backcast, part0, saved0 = plain_forward(blocks[0], r0)
    r1 = (r0 - backcast) * mask
    _, part1, saved1 = plain_forward(blocks[1], r1)
    forecast = part0.astype(jnp.bfloat16).astype(jnp.float32) + part1
    f = adj.astype(jnp.bfloat16)
    zero = jnp.zeros_like(r0)
    da1, grads1 = plain_backward(blocks[1], saved1, (-(zero * mask)).astype(jnp.bfloat16), f)
    dr1 = zero * mask + da1
    t = dr1.astype(jnp.bfloat16).astype(jnp.float32)
    da0, grads0 = plain_backward(blocks[0], saved0, (-(t * mask)).astype(jnp.bfloat16), f)
    dr0 = (t * mask + da0) * mask

    def by_section(first_block, second_block):
        mine, other = (
            jnp.where(core == 0, first_block, second_block),
            jnp.where(core == 0, second_block, first_block),
        )
        got = lax.ppermute(other, "section", [(0, 1), (1, 0)])
        return jnp.where(
            core == 0, jnp.concatenate([mine, got]), jnp.concatenate([got, mine])
        )[None]

    prediction = by_section(part0, forecast)
    sensitivity = by_section(dr0, dr1)
    packed = jnp.stack([unit_rows(*grads0), unit_rows(*grads1)])
    packed = lax.psum_scatter(packed, "section", scatter_dimension=0, tiled=False)
    packed = lax.psum_scatter(packed, "dp", scatter_dimension=0, tiled=True)
    norm = jnp.sqrt(lax.psum(jnp.sum(packed * packed), ("section", "dp")))
    factor = 1.0 / jnp.maximum(norm, 1.0)
    summed = [g[None] for g in from_unit_rows(packed, past, hidden, past + span)]
    updated = [adamw(*four, factor) for four in zip(masters, summed, momenta, variances)]
    return (
        prediction,
        sensitivity,
        norm,
        *summed,
        *(u[0] for u in updated),
        *(u[1] for u in updated),
        *(u[2] for u in updated),
    )


PLANES = {16: (4, 2, 2)}
MESH = pl.DeviceIdType.MESH
MATS = 6
CORE_SLOTS, DIAG_SLOTS, PLAIN_SLOTS, PAIR_SLOTS = 4, 4, 6, 4
BF, F32 = jnp.bfloat16, jnp.float32


ORDER = ((0, 5), (1, 4), (1, 5), (1, 3), (1, 2), (1, 1), (0, 4), (0, 3), (0, 2), (0, 1), (1, 0), (0, 0))


def remote(src, dst, send_sem, recv_sem, device):
    return pltpu.make_async_remote_copy(
        src_ref=src, dst_ref=dst, send_sem=send_sem, recv_sem=recv_sem, device_id=device, device_id_type=MESH
    )


def train_kernel(
    sizes,
    seg_hbm, adj_hbm, ext_hbm, first_hbm, square_hbm, head_hbm, biases_hbm,
    pred_out, sens_out, grad_out, norm_out,
    wg, handed, gp, from_core, from_diag, from_plain, from_pair, from_z, total,
    act_t, in_t, theta_keep, slope, work, resid, mask, f_ref, e_t, bias_t, bias_sum, pad,
    seg, adj, ext, first, square, head, biases, part_t, pred, sens, squares, norm_buf,
    own_send, own_recv, ag_send, ag_recv, rs_send, rs_recv, out_send, out_recv, local_sem, norm_send, norm_recv,
):
    ZN, YN, XN, windows, tile, past, span, hidden = sizes
    units = ZN * YN * XN
    core, dp = lax.axis_index("section"), lax.axis_index("dp")
    x, y, z = lax.rem(dp, XN), lax.rem(lax.div(dp, XN), YN), lax.div(dp, XN * YN)
    other, xo, yo = 1 - core, 1 - x, 1 - y
    near_y, near_x = y + core * (yo - y), xo + core * (x - xo)
    far_y, far_x = yo + core * (y - yo), x + core * (xo - x)

    def chip(zi, yi, xi):
        return (core, (zi * YN + yi) * XN + xi)

    sibling = (other, dp)
    z_peers = [lax.rem(z + step, ZN) for step in range(1, ZN)]

    row0 = core * windows
    loads = [
        pltpu.make_async_copy(seg_hbm.at[pl.ds(row0, windows), :], seg, local_sem.at[0]),
        pltpu.make_async_copy(adj_hbm.at[:, pl.ds(row0, windows)], adj, local_sem.at[1]),
    ]
    small_loads = [
        pltpu.make_async_copy(source, target, local_sem.at[4 + n])
        for n, (source, target) in enumerate(
            [(first_hbm, first), (head_hbm, head), (biases_hbm, biases), (square_hbm, square), (ext_hbm, ext)]
        )
    ]
    for load in small_loads:
        load.start()

    barrier = pltpu.get_barrier_semaphore()
    plane_peers = [
        (ci, (z * YN + yi) * XN + xi) for ci in (core, other) for yi in (y, yo) for xi in (x, xo)
    ][1:]
    peers = plane_peers + [(ci, (zi * YN + y) * XN + x) for zi in z_peers for ci in (core, other)]
    for peer in peers:
        pl.semaphore_signal(barrier, inc=1, device_id=peer, device_id_type=MESH)

    rows = hidden // units
    half_rows = rows // 2

    def put_own(m, value, lanes):
        halves = value.astype(BF).reshape(2, half_rows, -1)
        for h in range(2):
            pl.when(core == h)(functools.partial(put_half, m, halves[h], halves[1 - h], lanes))

    def put_half(m, kept, given, lanes):
        wg[core, m, z, y, x, core, :, lanes] = kept
        handed[m, :, lanes] = given

    for load in small_loads[:3]:
        load.wait()
    pad[...] = jnp.zeros_like(pad)
    pad[0:rows, 0:past] = first[0] * 0.5
    put_own(0, pad[0:rows, :], slice(0, 128))
    pad[...] = jnp.zeros_like(pad)
    pad[span : span + 4, 0:rows] = biases[0] * 0.5
    bias_cols = pad[...].T[0:rows]
    pad[...] = jnp.zeros_like(pad)
    pad[0:rows, 0:span] = head[0, :, past : past + span]
    put_own(0, pad[0:rows, :] + bias_cols, slice(128, 256))
    pad[...] = jnp.zeros_like(pad)
    pad[0:rows, 0:past] = head[0, :, 0:past]
    put_own(0, pad[0:rows, :], slice(256, 384))
    pl.semaphore_wait(barrier, len(peers))

    def hand_over(m, lanes):
        return remote(
            handed.at[m, :, lanes], wg.at[core, m, z, y, x, other, :, lanes], own_send.at[m], own_recv.at[m], sibling
        )

    def pack(m):
        put_own(m, square[0, m - 1] * 0.5 if m < 4 else square[0, m - 1], slice(0, hidden))


    def of(i):
        b = jnp.where(jnp.logical_and(i >= 5, i <= 10), 1, 0)
        return b, jnp.where(i <= 4, i, jnp.where(i <= 10, i - 5, 5))

    def sends(sems, kind, lanes):
        return sems.at[kind, 0 if lanes.stop == hidden else 1]

    def z_copies(i, lanes):
        b, m = of(i)
        part = wg.at[b, m, z, y, x, core, :, lanes]
        return [
            remote(part, part, sends(ag_send, 0, lanes), ag_recv.at[i, s], chip(zi, y, x)) for s, zi in enumerate(z_peers)
        ]

    def line_copies(i, lanes):
        b, m = of(i)
        given = wg.at[b, m, z, y, x, other, :, lanes]
        return [
            remote(
                handed.at[m, :, lanes], given, sends(ag_send, 0, lanes), ag_recv.at[i, s], (other, (zi * YN + y) * XN + x)
            )
            for s, zi in enumerate(z_peers)
        ]

    def column_copies(i, lanes):
        b, m = of(i)
        part = wg.at[b, m, :, y, x, core, :, lanes]
        return [
            remote(part, part, sends(ag_send, 1, lanes), ag_recv.at[i, 3], chip(z, near_y, near_x)),
            remote(part, part, sends(ag_send, 1, lanes), ag_recv.at[i, 4], chip(z, far_y, far_x)),
        ]

    def corner_copy(i, lanes):
        b, m = of(i)
        part = wg.at[b, m, :, near_y, near_x, core, :, lanes]
        return remote(part, part, sends(ag_send, 2, lanes), ag_recv.at[i, 5], chip(z, far_y, far_x))

    def core_copy(i, lanes):
        b, m = of(i)
        part = wg.at[b, m, :, :, :, core, :, lanes]
        return remote(part, part, sends(ag_send, 3, lanes), ag_recv.at[i, 6], sibling)

    def by_lanes(m, step):
        if isinstance(m, int):
            step(slice(0, hidden if m else 384))
            return
        pl.when(m == 0)(lambda: step(slice(0, 384)))
        pl.when(m > 0)(lambda: step(slice(0, hidden)))

    def start_all(copies):
        for copy in copies:
            copy.start()

    zeros_tile = jnp.zeros((tile, 128), F32)

    def prepare(t, carry):
        at = pl.ds(t * tile, tile)
        resid[at, :] = zeros_tile
        resid[at, 0:past] = seg[at, :]
        return carry

    def prepare_mask(g, carry):
        lengths = ext[pl.ds(core * (windows // 128) + g, 1), :]
        position = lax.broadcasted_iota(jnp.int32, (128, 128), 0)
        keep = jnp.where(position >= past - lengths, 1.0, 0.0).astype(F32).T
        at = pl.ds(pl.multiple_of(g * 128, 128), 128)
        pad[0:span, :] = adj[:, at]
        f_ref[at, :] = pad[...].T.astype(BF)
        mask[at, :] = keep.astype(BF)
        resid[at, :] = resid[at, :] * keep
        return carry

    tiles = windows // tile
    part_tile = windows // 2

    def matrix(b, m):
        return wg[b, m].reshape(hidden, hidden)

    def small(b, lane):
        return wg[b, 0, :, :, :, :, :, lane : lane + 128].reshape(hidden, 128)

    def store_layer(b, k, at, v):
        p = 1.0 + jnp.tanh(v)
        a = v * p
        rate = p + a * (2.0 - p)
        slope[b, k, at, :] = rate.astype(BF)
        low = a.astype(BF)
        act_t[b, k, :, at] = low.T
        return low

    def halves(body):
        for t in range(2):
            body(slice(t * windows // 2, (t + 1) * windows // 2))

    def layer_zero(b):
        bias_t[...] = small(b, 128).astype(F32).T

        def body(at):
            a = resid[at, :].astype(BF)
            in_t[b, :, at] = a.T
            work[0, at, :] = store_layer(b, 0, at, dot_nt(a, small(b, 0)) + bias_t[span : span + 1, :])

        halves(body)

    def layer_next(b, k):
        source, target = lax.rem(k + 1, 2), lax.rem(k, 2)

        def body(at):
            v = dot_nn(work[source, at, :], matrix(b, k)) + bias_t[pl.ds(span + k, 1), :]
            work[target, at, :] = store_layer(b, k, at, v)

        halves(body)

    def grid(value):
        return value.astype(BF).reshape(ZN, YN, XN, 2, half_rows, -1)

    def backcast_step():
        def body(at):
            theta = dot_nn(work[1, at, :], matrix(0, 4)).astype(BF)
            theta_keep[at, :] = theta
            resid[at, :] = (resid[at, :] - dot_nn(theta, small(0, 256))) * mask[at, :].astype(F32)

        halves(body)

    def put_rows(buf, b, at, value):
        for row in range(value.shape[0]):
            buf[b, row, :, at] = value[row : row + 1]

    def late_theta(b, m):
        theta_t = act_t.at[1, 0]
        theta_t[...] = dot_nn(matrix(b, m).T, act_t[b, 3]).astype(BF)

        @pl.when(m == 4)
        def _():
            gp[b, 0, :, :, :, :, :, 256:384] = grid(dot_nt(theta_t[...], e_t[b]))

        @pl.when(m == 5)
        def _():
            grad = grid(dot_nn(theta_t[...], f_ref[...]))
            gp[b, 0, :, :, :, :, :, 128:256] = gp[b, 0, :, :, :, :, :, 128:256] + grad
            part_t[b] = dot_nn(small(b, 128).T, theta_t[...])[0:span]

    def forecasts():
        put_rows(pred, 0, slice(0, windows), part_t[0])
        put_rows(pred, 1, slice(0, windows), part_t[0].astype(BF).astype(F32) + part_t[1])

    count = 2 * MATS

    def delayed(lag, t, step):
        pl.when(jnp.logical_and(t >= lag, t < count + lag))(lambda: step(t - lag))

    def staged(lag, t, step):
        early = t - lag + (1 if lag == 2 else 0)
        pl.when(jnp.logical_and(early >= (2 if lag == 2 else 1), early <= 2))(lambda: step(early))
        place = t - lag
        formed = jnp.logical_and(jnp.logical_and(place >= 3, place <= count), place != 6)
        pl.when(formed)(lambda: step(jnp.where(place <= 5, place, place - 1)))
        if lag == 6:
            pl.when(t == 4)(lambda: step(0))

    def gather_line(i):
        b, m = of(i)

        pl.when(b == core)(lambda: by_lanes(m, lambda lanes: start_all(line_copies(i, lanes) + z_copies(i, lanes))))

    def gather_columns(i):
        b, m = of(i)

        def step(lanes):
            pl.when(b != core)(lambda: hand_over(m, lanes).wait_recv())
            for copy in z_copies(i, lanes):
                copy.wait_recv()
            start_all(column_copies(i, lanes))

        by_lanes(m, step)

    def gather_corner(i):
        def step(lanes):
            column_copies(i, lanes)[0].wait_recv()
            corner_copy(i, lanes).start()

        by_lanes(of(i)[1], step)

    def gather_core(i):
        def step(lanes):
            column_copies(i, lanes)[1].wait_recv()
            corner_copy(i, lanes).wait_recv()
            core_copy(i, lanes).start()

        by_lanes(of(i)[1], step)

    def arrived(i):
        by_lanes(of(i)[1], lambda lanes: core_copy(i, lanes).wait_recv())

    def forward_unit(i):
        arrived(i)
        b, m = of(i)
        pl.when(m == 0)(lambda: layer_zero(b))
        pl.when(jnp.logical_and(m >= 1, m <= 3))(lambda: layer_next(b, m))
        pl.when(m == 4)(backcast_step)

        @pl.when(jnp.logical_or(i == 4, i == 8))
        def _():
            pl.when(b == 1)(lambda: feed(b))
            pl.when(b == 0)(lambda: feed_forward(b))
            def one(n, carry):
                pl.when(jnp.logical_and(b == 1, n == 5))(lambda: gather_core(10))
                theta_grad(b, n)
                scatter_start(jnp.where(b == 0, 0, n - 3))
                return carry

            lax.fori_loop(jnp.where(b == 1, 4, 5), MATS, one, 0)

    def gather_step(t, carry):
        pl.when(t == 12)(lambda: scatter_core(0))
        pl.when(t == 15)(lambda: scatter_diag(0))
        pl.when(jnp.logical_and(t >= 4, t != 14))(lambda: gather_core(t - 4))
        delayed(2, t, gather_corner)
        delayed(0, t, gather_columns)
        pl.when(t + 4 < count)(lambda: gather_line(t + 4))

        pl.when(t == 0)(lambda: start_all(loads))

        @pl.when(t == 2)
        def _():
            for load in loads + small_loads[4:]:
                load.wait()
            lax.fori_loop(0, tiles, prepare, 0)
            pad[...] = jnp.zeros_like(pad)
            lax.fori_loop(0, windows // 128, prepare_mask, 0)

        pl.when(jnp.logical_and(t >= 5, t < 14))(lambda: forward_unit(t - 5))
        return carry

    def out_copies(buf, out, s):
        at = pl.ds(row0, windows)
        return [
            pltpu.make_async_copy(buf.at[core], out.at[:, :, at], local_sem.at[2 + s]),
            remote(buf.at[other], out.at[:, :, at], out_send.at[s], out_recv.at[s], sibling),
        ]


    def back_of(j):
        if isinstance(j, int):
            return ORDER[j]
        b = jnp.where(jnp.logical_or(jnp.logical_and(j >= 1, j <= 5), j == 10), 1, 0)
        early = jnp.where(j == 1, 4, jnp.where(j <= 2, 5, 6 - j))
        return b, jnp.where(j <= 5, early, jnp.where(j == 6, 4, jnp.where(j <= 9, 10 - j, 0)))

    def to_core(j, lanes):
        b, m = back_of(j)
        return remote(
            gp.at[b, m, :, :, :, other, :, lanes], from_core.at[lax.rem(j, CORE_SLOTS), :, :, :, :, lanes],
            sends(rs_send, 3, lanes), rs_recv.at[j, 0], sibling,
        )

    def to_far(j, lanes):
        b, m = back_of(j)
        device = chip(z, far_y, far_x)
        return [
            remote(
                gp.at[b, m, :, yo, xo, core, :, lanes], from_diag.at[lax.rem(j, DIAG_SLOTS), :, :, lanes],
                sends(rs_send, 1, lanes), rs_recv.at[j, 1], device,
            ),
            remote(
                gp.at[b, m, :, far_y, far_x, core, :, lanes], from_plain.at[lax.rem(j, PLAIN_SLOTS), :, :, lanes],
                sends(rs_send, 1, lanes), rs_recv.at[j, 2], device,
            ),
        ]

    def to_near(j, lanes):
        b, m = back_of(j)
        return remote(
            gp.at[b, m, :, near_y, near_x, core, :, lanes], from_pair.at[lax.rem(j, PAIR_SLOTS), :, :, lanes],
            sends(rs_send, 2, lanes), rs_recv.at[j, 3], chip(z, near_y, near_x),
        )

    def to_z(j, lanes):
        b, m = back_of(j)
        return [
            remote(
                gp.at[b, m, zi, y, x, core, :, lanes], from_z.at[j, s, :, lanes],
                sends(rs_send, 0, lanes), rs_recv.at[j, 4 + s], chip(zi, y, x),
            )
            for s, zi in enumerate(z_peers)
        ]

    def scatter_start(j):
        by_lanes(back_of(j)[1], lambda lanes: to_core(j, lanes).start())

    def scatter_core(j):
        b, m = back_of(j)

        def step(lanes):
            to_core(j, lanes).wait_recv()
            part = gp[b, m, :, :, :, core, :, lanes] + from_core[lax.rem(j, CORE_SLOTS), :, :, :, :, lanes]
            gp[b, m, :, :, :, core, :, lanes] = part
            start_all(to_far(j, lanes))

        by_lanes(m, step)

    def scatter_diag(j):
        b, m = back_of(j)

        def step(lanes):
            to_far(j, lanes)[0].wait_recv()
            part = gp[b, m, :, near_y, near_x, core, :, lanes] + from_diag[lax.rem(j, DIAG_SLOTS), :, :, lanes]
            gp[b, m, :, near_y, near_x, core, :, lanes] = part
            to_near(j, lanes).start()

        by_lanes(m, step)

    def scatter_plane(j):
        b, m = back_of(j)

        def step(lanes):
            to_far(j, lanes)[1].wait_recv()
            to_near(j, lanes).wait_recv()
            value = gp[b, m, :, y, x, core, :, lanes].astype(F32)
            value = value + from_plain[lax.rem(j, PLAIN_SLOTS), :, :, lanes].astype(F32)
            value = value + from_pair[lax.rem(j, PAIR_SLOTS), :, :, lanes].astype(F32)
            gp[b, m, :, y, x, core, :, lanes] = value.astype(BF)
            start_all(to_z(j, lanes))

        by_lanes(m, step)

    def scatter_z(j):
        b, m = back_of(j)

        def step(lanes):
            for copy in to_z(j, lanes):
                copy.wait_recv()
            value = gp[b, m, z, y, x, core, :, lanes].astype(F32)
            for s in range(ZN - 1):
                value = value + from_z[j, s, :, lanes].astype(F32)
            total[b, m, :, lanes] = value
            squares[:, lanes] = squares[:, lanes] + value * value

        by_lanes(m, step)

    def add_rows(value):
        return jnp.sum(value.reshape(-1, 8, hidden), axis=0)

    def put_bias(k, acc):
        bias_sum[pl.ds(span + k, 1), :] = jnp.sum(acc, axis=0, keepdims=True)

    def feed(b):
        pl.when(b == 1)(lambda: resid.__setitem__(..., jnp.zeros_like(resid)))
        e = (-(resid[...] * mask[...].astype(F32))).astype(BF)
        e_t[b] = e.T
        work[0] = dot_nt(e, small(b, 256)).astype(BF)
        work[2] = dot_nt(f_ref[...], small(b, 128)).astype(BF)

    def feed_forward(b):
        work[2] = dot_nt(f_ref[...], small(b, 128)).astype(BF)

    def put_dz(b, k, da):
        sums = []

        def body(at):
            dz = da(at) * slope[b, k, at, :].astype(F32)
            work[k % 2 if isinstance(k, int) else lax.rem(k, 2), at, :] = dz.astype(BF)
            sums.append(add_rows(dz))

        halves(body)
        bias_sum[pl.ds(span + k, 1), :] = jnp.sum(sums[0] + sums[1], axis=0, keepdims=True)

    def theta_step(b):
        put_dz(
            b, 3, lambda at: 0.5 * (dot_nt(work[0, at, :], matrix(b, 4)) + dot_nt(work[2, at, :], matrix(b, 5)))
        )

    def layer_back(b, k):
        source = lax.rem(k, 2)
        gp[b, k] = grid(dot_nn(act_t[b, k - 1], work[source]))
        put_dz(b, k - 1, lambda at: dot_nt(work[source, at, :], matrix(b, k)))

    def theta_grad(b, m):
        gp[b, m] = grid(dot_nn(act_t[b, 3], work[jnp.where(m == 4, 0, 2)]))

    def first_grads(b):
        gp[b, 0, :, :, :, :, :, 0:128] = grid(dot_nn(in_t[b], work[0]).T)
        gp[b, 0, :, :, :, :, :, 128:256] = grid(bias_sum[...].T)
        pl.when(b == 0)(backcast_grad)

    def backcast_grad():
        gp[0, 0, :, :, :, :, :, 256:384] = grid(dot_nn(e_t[0], theta_keep[...]).T)

    def input_grad(b):
        for t in range(2):
            at = slice(t * windows // 2, (t + 1) * windows // 2)
            keep = mask[at, :].astype(F32)
            dr = resid[at, :] * keep + 2.0 * dot_nn(work[0, at, :], small(b, 0))

            @pl.when(b == 1)
            def _():
                seg[at, :] = dr[:, 0:past]
                resid[at, :] = dr.astype(BF).astype(F32)

            @pl.when(b == 0)
            def _():
                put_rows(sens, 0, at, (dr * keep).T[0:past])

    def late_rows():
        for g in range(windows // 128):
            at = slice(g * 128, (g + 1) * 128)
            pad[:, 0:past] = seg[at, :]
            put_rows(sens, 1, at, pad[...].T[0:past])

    bias_sum[...] = jnp.zeros_like(bias_sum)
    squares[...] = jnp.zeros_like(squares)
    total[...] = jnp.zeros_like(total)

    def back_step(j, carry):
        unit = jnp.where(j <= 5, j, j - 1)
        b, m = back_of(unit)

        staged(6, j, scatter_plane)
        staged(4, j, scatter_diag)
        staged(2, j, scatter_core)

        @pl.when(j == 2)
        def _():
            arrived(9)
            arrived(10)
            theta_step(1)
            scatter_core(1)

        layer = jnp.logical_and(m >= 1, m <= 3)
        pl.when(jnp.logical_and(layer, j != 6))(lambda: layer_back(b, m))
        pl.when(jnp.logical_or(j == 6, j == count))(lambda: first_grads(jnp.where(j == 6, 1, 0)))
        pl.when(j == 6)(lambda: input_grad(1))

        @pl.when(j == 7)
        def _():
            feed(0)
            theta_grad(0, 4)

        @pl.when(jnp.logical_or(j == 11, j == count))
        def _():
            lax.fori_loop(jnp.where(j == 11, 4, 5), MATS, lambda n, carry: (late_theta(b, n), carry)[1], 0)

        formed = jnp.logical_and(jnp.logical_and(j >= 3, j <= count), j != 6)
        pl.when(formed)(lambda: scatter_start(unit))

        @pl.when(j == 7)
        def _():
            arrived(11)
            theta_step(0)

        @pl.when(j == count + 1)
        def _():
            input_grad(0)
            forecasts()

        pl.when(j == count + 2)(late_rows)

        @pl.when(j == count + 6)
        def _():
            start_all(out_copies(sens, sens_out, 1) + out_copies(pred, pred_out, 0))

        @pl.when(j >= count + 2)
        def _():
            scatter_z(2 * (j - count - 2))
            scatter_z(2 * (j - count - 2) + 1)

        return carry

    gather_line(0)
    hand_over(0, slice(0, 384)).start()
    small_loads[3].wait()
    for m in range(1, MATS):
        pack(m)
        if m < 4:
            gather_line(m)
        hand_over(m, slice(0, hidden)).start()
    lax.fori_loop(0, count + 4, gather_step, 0)

    lax.fori_loop(2, count + 8, back_step, 0)

    grad_copy = remote(total.at[other], grad_out.at[:, core], out_send.at[2], out_recv.at[2], sibling)
    grad_copy.start()
    grad_out[:, core] = total[core]
    sq = squares[:, 0:128] + squares[:, 128:256] + squares[:, 256:384] + squares[:, 384:512]
    place = (y * XN + x) * 2 + core
    norm_buf[place] = sq[0:8] + sq[8:16]

    def spread(sources, targets, first):
        copies = [
            remote(norm_buf.at[sources], norm_buf.at[sources], norm_send.at[first + s], norm_recv.at[first + s], device)
            for s, device in enumerate(targets)
        ]
        start_all(copies)
        for copy in copies:
            copy.wait()

    def add_up(slots):
        value = norm_buf[slots[0]]
        for slot in slots[1:]:
            value = value + norm_buf[slot]
        return value

    spread(place, plane_peers, 0)
    norm_buf[8 + z] = add_up(range(8))
    spread(8 + z, [chip(zi, y, x) for zi in z_peers], 7)
    everything = add_up(range(8, 8 + ZN))
    norm_out[...] = jnp.broadcast_to(jnp.sqrt(jnp.sum(everything, keepdims=True)), norm_out.shape)

    grad_copy.wait()
    for buf, out, s in ((pred, pred_out, 0), (sens, sens_out, 1)):
        for copy in out_copies(buf, out, s):
            copy.wait()
    for m in range(MATS):
        hand_over(m, slice(0, hidden if m else 384)).wait_send()

    for mats, lanes in ((slice(1, MATS), slice(0, hidden)), (slice(0, 1), slice(0, 384))):
        sent = (
            wg.at[:, mats, 0 : ZN - 1, 0, 0, 0, :, lanes],
            wg.at[:, mats, :, :, 0, 0, :, lanes],
            wg.at[:, mats, :, 0, 0, 0, :, lanes],
            wg.at[:, mats, :, :, :, 0, :, lanes],
        )
        for sems in (ag_send, rs_send):
            for kind, ref in enumerate(sent):
                remote(ref, ref, sends(sems, kind, lanes), out_recv.at[0], sibling).wait_send()


def train_call(plane, segments, extents, adjoint, first, square, head, biases):
    ZN, YN, XN = plane
    past, span, hidden = segments.shape[1], adjoint.shape[0], square.shape[3]
    windows = segments.shape[0] // 2
    tile = windows
    half = hidden // (ZN * YN * XN) // 2
    sizes = (ZN, YN, XN, windows, tile, past, span, hidden)
    DMA = pltpu.SemaphoreType.DMA
    vmem = pl.BlockSpec(memory_space=pltpu.VMEM)
    hbm = pl.BlockSpec(memory_space=pl.ANY)
    count = 2 * MATS
    flops = 2 * 2 * 3 * windows * hidden * (6 * hidden + 2 * 128)
    lengths = extents.reshape(-1, 128)
    return pl.pallas_call(
        functools.partial(train_kernel, sizes),
        out_shape=(
            jax.ShapeDtypeStruct((span, 1, 2 * windows), F32),
            jax.ShapeDtypeStruct((past, 1, 2 * windows), F32),
            jax.ShapeDtypeStruct((MATS, 2, half, hidden), F32),
            jax.ShapeDtypeStruct((8, 128), F32),
        ),
        in_specs=[hbm] * 7,
        out_specs=(hbm, hbm, vmem, vmem),
        scratch_shapes=[
            pltpu.VMEM((2, MATS, ZN, YN, XN, 2, half, hidden), BF),
            pltpu.VMEM((MATS, half, hidden), BF),
            pltpu.VMEM((2, MATS, ZN, YN, XN, 2, half, hidden), BF),
            pltpu.VMEM((CORE_SLOTS, ZN, YN, XN, half, hidden), BF),
            pltpu.VMEM((DIAG_SLOTS, ZN, half, hidden), BF),
            pltpu.VMEM((PLAIN_SLOTS, ZN, half, hidden), BF),
            pltpu.VMEM((PAIR_SLOTS, ZN, half, hidden), BF),
            pltpu.VMEM((count, ZN - 1, half, hidden), BF),
            pltpu.VMEM((2, MATS, half, hidden), F32),
            pltpu.VMEM((2, 4, hidden, windows), BF),
            pltpu.VMEM((2, 128, windows), BF),
            pltpu.VMEM((windows, hidden), BF),
            pltpu.VMEM((2, 4, windows, hidden), BF),
            pltpu.VMEM((3, windows, hidden), BF),
            pltpu.VMEM((windows, 128), F32),
            pltpu.VMEM((windows, 128), BF),
            pltpu.VMEM((windows, 128), BF),
            pltpu.VMEM((2, 128, windows), BF),
            pltpu.VMEM((128, hidden), F32),
            pltpu.VMEM((128, hidden), F32),
            pltpu.VMEM((128, 128), F32),
            pltpu.VMEM((windows, past), F32),
            pltpu.VMEM((span, windows), F32),
            *(pltpu.VMEM(a.shape, a.dtype) for a in (lengths, first, square, head, biases)),
            pltpu.VMEM((2, span, windows), F32),
            pltpu.VMEM((2, span, 1, windows), F32),
            pltpu.VMEM((2, past, 1, windows), F32),
            pltpu.VMEM((half, hidden), F32),
            pltpu.VMEM((8 + ZN, 8, 128), F32),
            DMA((MATS,)),
            DMA((MATS,)),
            DMA((4, 2)),
            DMA((count, 4 + ZN - 1)),
            DMA((4, 2)),
            DMA((count, 4 + ZN - 1)),
            DMA((3,)),
            DMA((3,)),
            DMA((9,)),
            DMA((7 + ZN - 1,)),
            DMA((7 + ZN - 1,)),
        ],
        compiler_params=pltpu.CompilerParams(
            collective_id=0, has_side_effects=True, vmem_limit_bytes=64 * 1024 * 1024
        ),
        cost_estimate=pl.CostEstimate(flops=flops, bytes_accessed=8_000_000, transcendentals=8 * windows * hidden),
        name="train",
    )(segments, adjoint, lengths, first, square, head, biases)


def update_kernel(past, span, *refs):
    sources, targets, norm_out = refs[0:16], refs[16:34], refs[34]
    held, results, pad, in_sem, out_sem = refs[35:51], refs[51:67], *refs[67:70]
    arriving = [pltpu.make_async_copy(source, ref, in_sem.at[n]) for n, (source, ref) in enumerate(zip(sources, held))]
    leaving = [
        pltpu.make_async_copy(ref, target, out_sem.at[n]) for n, (ref, target) in enumerate(zip(held[0:2] + results, targets))
    ]
    for n in (2, 3, 0, 5, 9, 13, 1, 4, 8, 12, 6, 10, 14, 7, 11, 15):
        arriving[n].start()
    grads, norm, masters, momenta, variances = held[2], held[3], held[4:8], held[8:12], held[12:16]
    units = masters[3].shape[2]

    def rows(m, lane, width):
        return grads[m, :, :, lane : lane + width].reshape(units, width)

    arriving[2].wait()
    arriving[3].wait()
    norm_out[...] = norm[0:1, 0:1]
    factor = 1.0 / jnp.maximum(norm[0:1, 0:1], 1.0)
    for m in range(5):
        results[1][0, m] = rows(m + 1, 0, grads.shape[3])
    results[0][0] = rows(0, 0, 128)[:, 0:past]
    forecast = rows(0, 128, 128)
    pad[...] = jnp.zeros_like(pad)
    pad[0:units, :] = forecast
    results[3][0] = pad[...].T[span : span + 4, 0:units]
    results[2][0, :, 0:past] = rows(0, 256, 128)[:, 0:past]
    results[2][0, :, past : past + span] = forecast[:, 0:span]
    for n in (0, 1):
        arriving[n].wait()
        leaving[n].start()
    for n in (1, 0, 2, 3):
        leaving[2 + n].start()
        for state in range(3):
            arriving[4 + 4 * state + n].wait()
        updated = adamw(masters[n][...], results[n][...], momenta[n][...], variances[n][...], factor[None])
        for kind, value in enumerate(updated):
            results[4 * (kind + 1) + n][...] = value
            leaving[2 + 4 * (kind + 1) + n].start()
    for copy in leaving:
        copy.wait()


def update_call(prediction, sensitivity, grads, norm, state):
    hbm = pl.BlockSpec(memory_space=pl.ANY)
    sources = (prediction, sensitivity, grads, norm, *state)
    targets = (prediction, sensitivity, *(4 * list(state[:4])))
    return pl.pallas_call(
        functools.partial(update_kernel, sensitivity.shape[0], prediction.shape[0]),
        out_shape=tuple(jax.ShapeDtypeStruct(a.shape, F32) for a in targets) + (jax.ShapeDtypeStruct((1, 1), F32),),
        in_specs=[hbm] * len(sources),
        out_specs=tuple([hbm] * len(targets) + [pl.BlockSpec(memory_space=pltpu.VMEM)]),
        scratch_shapes=[pltpu.VMEM(a.shape, F32) for a in sources]
        + [pltpu.VMEM(a.shape, F32) for a in targets[2:]]
        + [pltpu.VMEM((128, 128), F32), pltpu.SemaphoreType.DMA((len(sources),)), pltpu.SemaphoreType.DMA((len(targets),))],
        name="update",
    )(*sources)


def turned(arrays):
    return [a.transpose(0, 2, 1) if n % 4 == 0 else a for n, a in enumerate(arrays)]


def kernel_shards(plane, segments, extents, adjoint, *state):
    state = turned(state)
    results = train_call(plane, segments, extents, adjoint.T, *state[:4])
    prediction, sensitivity, *updated, norm = update_call(*results, state)
    by_window = (prediction.transpose(1, 2, 0), sensitivity.transpose(1, 2, 0))
    return (*by_window, norm.reshape(()), *turned(updated))


STATE_SPECS = (
    P("section", None, "dp"),
    P("section", None, "dp", None),
    P("section", "dp", None),
    P("section", None, "dp"),
)


def solution(mesh):
    in_specs = (P("dp", None), P("dp"), P("dp", None)) + 3 * STATE_SPECS
    out_specs = (P("section", "dp", None), P("section", "dp", None), P()) + 4 * STATE_SPECS
    plane = PLANES.get(mesh.shape["dp"])
    shards = plain_shards if plane is None else functools.partial(kernel_shards, plane)
    return jax.shard_map(shards, mesh=mesh, in_specs=in_specs, out_specs=out_specs, check_vma=False)
```

```python
import functools

import jax
import jax.numpy as jnp
from jax import lax
from jax.experimental import pallas as pl
from jax.experimental.pallas import tpu as pltpu
from jax.sharding import PartitionSpec as P

STEP = 10


def dot_nn(a, b):
    return jnp.dot(a, b, preferred_element_type=jnp.float32)


def dot_tn(a, b):
    return lax.dot_general(a, b, (((0,), (0,)), ((), ())), preferred_element_type=jnp.float32)


def dot_nt(a, b):
    return lax.dot_general(a, b, (((1,), (1,)), ((), ())), preferred_element_type=jnp.float32)


def unit_rows(first, square, head, biases):
    units = first.shape[1]
    return jnp.concatenate(
        [square.transpose(1, 0, 2).reshape(units, -1), first.T, head, biases.T], axis=1
    )


def from_unit_rows(rows, past, hidden, out):
    wide = 5 * hidden
    square = rows[:, :wide].reshape(-1, 5, hidden).transpose(1, 0, 2)
    first = rows[:, wide : wide + past].T
    head = rows[:, wide + past : wide + past + out]
    biases = rows[:, wide + past + out :].T
    return first, square, head, biases


def plain_forward(weights, resid):
    first, square, head, biases = weights
    past = resid.shape[1]
    acts, slopes = [resid.astype(jnp.bfloat16)], []
    for k in range(4):
        z = dot_nn(acts[-1], first if k == 0 else square[k - 1]) + biases[k].astype(jnp.float32)
        sig = jax.nn.sigmoid(z)
        acts.append((z * sig).astype(jnp.bfloat16))
        slopes.append(sig * (1.0 + z * (1.0 - sig)))
    theta_b = dot_nn(acts[4], square[3]).astype(jnp.bfloat16)
    theta_f = dot_nn(acts[4], square[4]).astype(jnp.bfloat16)
    backcast = dot_nn(theta_b, head[:, :past])
    part = dot_nn(theta_f, head[:, past:])
    return backcast, part, (acts, slopes, theta_b, theta_f)


def plain_backward(weights, saved, e, f):
    first, square, head, biases = weights
    acts, slopes, theta_b, theta_f = saved
    past = e.shape[1]
    head_grad = jnp.concatenate([dot_tn(theta_b, e), dot_tn(theta_f, f)], axis=1)
    u_b = dot_nt(e, head[:, :past]).astype(jnp.bfloat16)
    u_f = dot_nt(f, head[:, past:]).astype(jnp.bfloat16)
    squares = [None, None, None, dot_tn(acts[4], u_b), dot_tn(acts[4], u_f)]
    da = dot_nt(u_b, square[3]) + dot_nt(u_f, square[4])
    bias_grads = [None] * 4
    first_grad = None
    for k in (3, 2, 1, 0):
        dz = (da * slopes[k]).astype(jnp.bfloat16)
        bias_grads[k] = jnp.sum(dz, axis=0, dtype=jnp.float32)
        grad = dot_tn(acts[k], dz)
        if k == 0:
            first_grad = grad
        else:
            squares[k - 1] = grad
        da = dot_nt(dz, first if k == 0 else square[k - 1])
    return da, (first_grad, jnp.stack(squares), head_grad, jnp.stack(bias_grads))


def adamw(master, gradient, momentum, variance, factor):
    clipped = gradient * factor
    moment_new = 0.9 * momentum + 0.1 * clipped
    variance_new = 0.999 * variance + 0.001 * clipped * clipped
    ratio = moment_new / (1.0 - 0.9**STEP) / (jnp.sqrt(variance_new / (1.0 - 0.999**STEP)) + 1e-08)
    return master - 0.05 * (ratio + 0.01 * master), moment_new, variance_new


def plain_shards(segments, extents, adjoint, *state):
    masters, momenta, variances = state[:4], state[4:8], state[8:]
    core = lax.axis_index("section")
    past, span = segments.shape[1], adjoint.shape[1]
    windows = segments.shape[0] // 2
    hidden = masters[1].shape[3]
    mine = [
        lax.dynamic_slice_in_dim(v, core * windows, windows, 0) for v in (segments, extents, adjoint)
    ]
    seg, ext, adj = mine
    rows = unit_rows(*(m[0].astype(jnp.bfloat16) for m in masters))
    rows = lax.all_gather(rows, "dp", axis=0, tiled=True)
    rows = lax.all_gather(rows, "section", axis=0)
    blocks = [from_unit_rows(rows[b], past, hidden, past + span) for b in range(2)]
    mask = (
        lax.broadcasted_iota(jnp.int32, (windows, past), 1) >= past - ext[:, None]
    ).astype(jnp.float32)
    r0 = seg * mask
    backcast, part0, saved0 = plain_forward(blocks[0], r0)
    r1 = (r0 - backcast) * mask
    _, part1, saved1 = plain_forward(blocks[1], r1)
    forecast = part0.astype(jnp.bfloat16).astype(jnp.float32) + part1
    f = adj.astype(jnp.bfloat16)
    zero = jnp.zeros_like(r0)
    da1, grads1 = plain_backward(blocks[1], saved1, (-(zero * mask)).astype(jnp.bfloat16), f)
    dr1 = zero * mask + da1
    t = dr1.astype(jnp.bfloat16).astype(jnp.float32)
    da0, grads0 = plain_backward(blocks[0], saved0, (-(t * mask)).astype(jnp.bfloat16), f)
    dr0 = (t * mask + da0) * mask

    def by_section(first_block, second_block):
        mine, other = (
            jnp.where(core == 0, first_block, second_block),
            jnp.where(core == 0, second_block, first_block),
        )
        got = lax.ppermute(other, "section", [(0, 1), (1, 0)])
        return jnp.where(
            core == 0, jnp.concatenate([mine, got]), jnp.concatenate([got, mine])
        )[None]

    prediction = by_section(part0, forecast)
    sensitivity = by_section(dr0, dr1)
    packed = jnp.stack([unit_rows(*grads0), unit_rows(*grads1)])
    packed = lax.psum_scatter(packed, "section", scatter_dimension=0, tiled=False)
    packed = lax.psum_scatter(packed, "dp", scatter_dimension=0, tiled=True)
    norm = jnp.sqrt(lax.psum(jnp.sum(packed * packed), ("section", "dp")))
    factor = 1.0 / jnp.maximum(norm, 1.0)
    summed = [g[None] for g in from_unit_rows(packed, past, hidden, past + span)]
    updated = [adamw(*four, factor) for four in zip(masters, summed, momenta, variances)]
    return (
        prediction,
        sensitivity,
        norm,
        *summed,
        *(u[0] for u in updated),
        *(u[1] for u in updated),
        *(u[2] for u in updated),
    )


PLANES = {16: (4, 2, 2)}
MESH = pl.DeviceIdType.MESH
MATS = 6
CORE_SLOTS, DIAG_SLOTS, PLAIN_SLOTS, PAIR_SLOTS = 4, 4, 6, 4
BF, F32 = jnp.bfloat16, jnp.float32


ORDER = ((0, 5), (1, 4), (1, 5), (1, 3), (1, 2), (1, 1), (0, 4), (0, 3), (0, 2), (0, 1), (1, 0), (0, 0))


def remote(src, dst, send_sem, recv_sem, device):
    return pltpu.make_async_remote_copy(
        src_ref=src, dst_ref=dst, send_sem=send_sem, recv_sem=recv_sem, device_id=device, device_id_type=MESH
    )


def train_kernel(
    sizes,
    seg_hbm, adj_hbm, ext_hbm, first_hbm, square_hbm, head_hbm, biases_hbm,
    pred_out, sens_out, grad_out, norm_out,
    wg, handed, gp, from_core, from_diag, from_plain, from_pair, from_z, total,
    act_t, in_t, theta_keep, slope, work, resid, mask, f_ref, e_t, bias_t, bias_sum, pad,
    seg, adj, ext, first, square, head, biases, part_t, pred, sens, squares, norm_buf,
    own_send, own_recv, ag_send, ag_recv, rs_send, rs_recv, out_send, out_recv, local_sem, norm_send, norm_recv,
):
    ZN, YN, XN, windows, tile, past, span, hidden = sizes
    units = ZN * YN * XN
    core, dp = lax.axis_index("section"), lax.axis_index("dp")
    x, y, z = lax.rem(dp, XN), lax.rem(lax.div(dp, XN), YN), lax.div(dp, XN * YN)
    other, xo, yo = 1 - core, 1 - x, 1 - y
    near_y, near_x = y + core * (yo - y), xo + core * (x - xo)
    far_y, far_x = yo + core * (y - yo), x + core * (xo - x)

    def chip(zi, yi, xi):
        return (core, (zi * YN + yi) * XN + xi)

    sibling = (other, dp)
    z_peers = [lax.rem(z + step, ZN) for step in range(1, ZN)]

    row0 = core * windows
    loads = [
        pltpu.make_async_copy(seg_hbm.at[pl.ds(row0, windows), :], seg, local_sem.at[0]),
        pltpu.make_async_copy(adj_hbm.at[:, pl.ds(row0, windows)], adj, local_sem.at[1]),
    ]
    small_loads = [
        pltpu.make_async_copy(source, target, local_sem.at[4 + n])
        for n, (source, target) in enumerate(
            [(first_hbm, first), (head_hbm, head), (biases_hbm, biases), (square_hbm, square), (ext_hbm, ext)]
        )
    ]
    for load in small_loads:
        load.start()

    barrier = pltpu.get_barrier_semaphore()
    plane_peers = [
        (ci, (z * YN + yi) * XN + xi) for ci in (core, other) for yi in (y, yo) for xi in (x, xo)
    ][1:]
    peers = plane_peers + [(ci, (zi * YN + y) * XN + x) for zi in z_peers for ci in (core, other)]
    for peer in peers:
        pl.semaphore_signal(barrier, inc=1, device_id=peer, device_id_type=MESH)

    rows = hidden // units
    half_rows = rows // 2

    def put_own(m, value, lanes):
        halves = value.astype(BF).reshape(2, half_rows, -1)
        for h in range(2):
            pl.when(core == h)(functools.partial(put_half, m, halves[h], halves[1 - h], lanes))

    def put_half(m, kept, given, lanes):
        wg[core, m, z, y, x, core, :, lanes] = kept
        handed[m, :, lanes] = given

    for load in small_loads[:3]:
        load.wait()
    pad[...] = jnp.zeros_like(pad)
    pad[0:rows, 0:past] = first[0] * 0.5
    put_own(0, pad[0:rows, :], slice(0, 128))
    pad[...] = jnp.zeros_like(pad)
    pad[span : span + 4, 0:rows] = biases[0] * 0.5
    bias_cols = pad[...].T[0:rows]
    pad[...] = jnp.zeros_like(pad)
    pad[0:rows, 0:span] = head[0, :, past : past + span]
    put_own(0, pad[0:rows, :] + bias_cols, slice(128, 256))
    pad[...] = jnp.zeros_like(pad)
    pad[0:rows, 0:past] = head[0, :, 0:past]
    put_own(0, pad[0:rows, :], slice(256, 384))
    pl.semaphore_wait(barrier, len(peers))

    def hand_over(m, lanes):
        return remote(
            handed.at[m, :, lanes], wg.at[core, m, z, y, x, other, :, lanes], own_send.at[m], own_recv.at[m], sibling
        )

    def pack(m):
        put_own(m, square[0, m - 1] * 0.5 if m < 4 else square[0, m - 1], slice(0, hidden))


    def of(i):
        b = jnp.where(jnp.logical_and(i >= 5, i <= 10), 1, 0)
        return b, jnp.where(i <= 4, i, jnp.where(i <= 10, i - 5, 5))

    def sends(sems, kind, lanes):
        return sems.at[kind, 0 if lanes.stop == hidden else 1]

    def z_copies(i, lanes):
        b, m = of(i)
        part = wg.at[b, m, z, y, x, core, :, lanes]
        return [
            remote(part, part, sends(ag_send, 0, lanes), ag_recv.at[i, s], chip(zi, y, x)) for s, zi in enumerate(z_peers)
        ]

    def line_copies(i, lanes):
        b, m = of(i)
        given = wg.at[b, m, z, y, x, other, :, lanes]
        return [
            remote(
                handed.at[m, :, lanes], given, sends(ag_send, 0, lanes), ag_recv.at[i, s], (other, (zi * YN + y) * XN + x)
            )
            for s, zi in enumerate(z_peers)
        ]

    def column_copies(i, lanes):
        b, m = of(i)
        part = wg.at[b, m, :, y, x, core, :, lanes]
        return [
            remote(part, part, sends(ag_send, 1, lanes), ag_recv.at[i, 3], chip(z, near_y, near_x)),
            remote(part, part, sends(ag_send, 1, lanes), ag_recv.at[i, 4], chip(z, far_y, far_x)),
        ]

    def corner_copy(i, lanes):
        b, m = of(i)
        part = wg.at[b, m, :, near_y, near_x, core, :, lanes]
        return remote(part, part, sends(ag_send, 2, lanes), ag_recv.at[i, 5], chip(z, far_y, far_x))

    def core_copy(i, lanes):
        b, m = of(i)
        part = wg.at[b, m, :, :, :, core, :, lanes]
        return remote(part, part, sends(ag_send, 3, lanes), ag_recv.at[i, 6], sibling)

    def by_lanes(m, step):
        if isinstance(m, int):
            step(slice(0, hidden if m else 384))
            return
        pl.when(m == 0)(lambda: step(slice(0, 384)))
        pl.when(m > 0)(lambda: step(slice(0, hidden)))

    def start_all(copies):
        for copy in copies:
            copy.start()

    zeros_tile = jnp.zeros((tile, 128), F32)

    def prepare(t, carry):
        at = pl.ds(t * tile, tile)
        resid[at, :] = zeros_tile
        resid[at, 0:past] = seg[at, :]
        return carry

    def prepare_mask(g, carry):
        lengths = ext[pl.ds(core * (windows // 128) + g, 1), :]
        position = lax.broadcasted_iota(jnp.int32, (128, 128), 0)
        keep = jnp.where(position >= past - lengths, 1.0, 0.0).astype(F32).T
        at = pl.ds(pl.multiple_of(g * 128, 128), 128)
        pad[0:span, :] = adj[:, at]
        f_ref[at, :] = pad[...].T.astype(BF)
        mask[at, :] = keep.astype(BF)
        resid[at, :] = resid[at, :] * keep
        return carry

    tiles = windows // tile
    part_tile = windows // 2

    def matrix(b, m):
        return wg[b, m].reshape(hidden, hidden)

    def small(b, lane):
        return wg[b, 0, :, :, :, :, :, lane : lane + 128].reshape(hidden, 128)

    def store_layer(b, k, at, v):
        p = 2.0 / (1.0 + jnp.exp(-2.0 * v))
        a = v * p
        rate = p + a * (2.0 - p)
        slope[b, k, at, :] = rate.astype(BF)
        low = a.astype(BF)
        act_t[b, k, :, at] = low.T
        return low

    def halves(body):
        for t in range(2):
            body(slice(t * windows // 2, (t + 1) * windows // 2))

    def layer_zero(b):
        bias_t[...] = small(b, 128).astype(F32).T

        def body(at):
            a = resid[at, :].astype(BF)
            in_t[b, :, at] = a.T
            work[0, at, :] = store_layer(b, 0, at, dot_nt(a, small(b, 0)) + bias_t[span : span + 1, :])

        halves(body)

    def layer_next(b, k):
        source, target = lax.rem(k + 1, 2), lax.rem(k, 2)

        def body(at):
            v = dot_nn(work[source, at, :], matrix(b, k)) + bias_t[pl.ds(span + k, 1), :]
            work[target, at, :] = store_layer(b, k, at, v)

        halves(body)

    def grid(value):
        return value.astype(BF).reshape(ZN, YN, XN, 2, half_rows, -1)

    def backcast_step():
        def body(at):
            theta = dot_nn(work[1, at, :], matrix(0, 4)).astype(BF)
            theta_keep[at, :] = theta
            resid[at, :] = (resid[at, :] - dot_nn(theta, small(0, 256))) * mask[at, :].astype(F32)

        halves(body)

    def put_rows(buf, b, at, value):
        for row in range(value.shape[0]):
            buf[b, row, :, at] = value[row : row + 1]

    def late_theta(b, m):
        theta_t = act_t.at[1, 0]
        theta_t[...] = dot_nn(matrix(b, m).T, act_t[b, 3]).astype(BF)

        @pl.when(m == 4)
        def _():
            gp[b, 0, :, :, :, :, :, 256:384] = grid(dot_nt(theta_t[...], e_t[b]))

        @pl.when(m == 5)
        def _():
            grad = grid(dot_nn(theta_t[...], f_ref[...]))
            gp[b, 0, :, :, :, :, :, 128:256] = gp[b, 0, :, :, :, :, :, 128:256] + grad
            part_t[b] = dot_nn(small(b, 128).T, theta_t[...])[0:span]

    def forecasts():
        put_rows(pred, 0, slice(0, windows), part_t[0])
        put_rows(pred, 1, slice(0, windows), part_t[0].astype(BF).astype(F32) + part_t[1])

    count = 2 * MATS

    def delayed(lag, t, step):
        pl.when(jnp.logical_and(t >= lag, t < count + lag))(lambda: step(t - lag))

    def staged(lag, t, step):
        early = t - lag + 1
        pl.when(jnp.logical_and(early >= (2 if lag == 2 else 1), early <= 2))(lambda: step(early))
        unit = t - lag
        pl.when(jnp.logical_and(unit >= 3, unit < count))(lambda: step(unit))
        if lag == 6:
            pl.when(t == 4)(lambda: step(0))

    def gather_line(i):
        b, m = of(i)

        pl.when(b == core)(lambda: by_lanes(m, lambda lanes: start_all(line_copies(i, lanes) + z_copies(i, lanes))))

    def gather_columns(i):
        b, m = of(i)

        def step(lanes):
            pl.when(b != core)(lambda: hand_over(m, lanes).wait_recv())
            for copy in z_copies(i, lanes):
                copy.wait_recv()
            start_all(column_copies(i, lanes))

        by_lanes(m, step)

    def gather_corner(i):
        def step(lanes):
            column_copies(i, lanes)[0].wait_recv()
            corner_copy(i, lanes).start()

        by_lanes(of(i)[1], step)

    def gather_core(i):
        def step(lanes):
            column_copies(i, lanes)[1].wait_recv()
            corner_copy(i, lanes).wait_recv()
            core_copy(i, lanes).start()

        by_lanes(of(i)[1], step)

    def arrived(i):
        by_lanes(of(i)[1], lambda lanes: core_copy(i, lanes).wait_recv())

    def forward_unit(i):
        arrived(i)
        b, m = of(i)
        pl.when(m == 0)(lambda: layer_zero(b))
        pl.when(jnp.logical_and(m >= 1, m <= 3))(lambda: layer_next(b, m))
        pl.when(m == 4)(backcast_step)

        @pl.when(jnp.logical_or(i == 4, i == 8))
        def _():
            pl.when(b == 1)(lambda: feed(b))
            pl.when(b == 0)(lambda: feed_forward(b))
            def one(n, carry):
                pl.when(jnp.logical_and(b == 1, n == 5))(lambda: gather_core(10))
                theta_grad(b, n)
                scatter_start(jnp.where(b == 0, 0, n - 3))
                return carry

            lax.fori_loop(jnp.where(b == 1, 4, 5), MATS, one, 0)

    def gather_step(t, carry):
        pl.when(t == 12)(lambda: scatter_core(0))
        pl.when(t == 15)(lambda: scatter_diag(0))
        pl.when(jnp.logical_and(t >= 4, t != 14))(lambda: gather_core(t - 4))
        delayed(2, t, gather_corner)
        delayed(0, t, gather_columns)
        pl.when(t + 4 < count)(lambda: gather_line(t + 4))

        pl.when(t == 0)(lambda: start_all(loads))

        @pl.when(t == 2)
        def _():
            for load in loads + small_loads[4:]:
                load.wait()
            lax.fori_loop(0, tiles, prepare, 0)
            pad[...] = jnp.zeros_like(pad)
            lax.fori_loop(0, windows // 128, prepare_mask, 0)

        pl.when(jnp.logical_and(t >= 5, t < 14))(lambda: forward_unit(t - 5))
        return carry

    def out_copies(buf, out, s):
        at = pl.ds(row0, windows)
        return [
            pltpu.make_async_copy(buf.at[core], out.at[:, :, at], local_sem.at[2 + s]),
            remote(buf.at[other], out.at[:, :, at], out_send.at[s], out_recv.at[s], sibling),
        ]


    def back_of(j):
        if isinstance(j, int):
            return ORDER[j]
        b = jnp.where(jnp.logical_or(jnp.logical_and(j >= 1, j <= 5), j == 10), 1, 0)
        early = jnp.where(j == 1, 4, jnp.where(j <= 2, 5, 6 - j))
        return b, jnp.where(j <= 5, early, jnp.where(j == 6, 4, jnp.where(j <= 9, 10 - j, 0)))

    def to_core(j, lanes):
        b, m = back_of(j)
        return remote(
            gp.at[b, m, :, :, :, other, :, lanes], from_core.at[lax.rem(j, CORE_SLOTS), :, :, :, :, lanes],
            sends(rs_send, 3, lanes), rs_recv.at[j, 0], sibling,
        )

    def to_far(j, lanes):
        b, m = back_of(j)
        device = chip(z, far_y, far_x)
        return [
            remote(
                gp.at[b, m, :, yo, xo, core, :, lanes], from_diag.at[lax.rem(j, DIAG_SLOTS), :, :, lanes],
                sends(rs_send, 1, lanes), rs_recv.at[j, 1], device,
            ),
            remote(
                gp.at[b, m, :, far_y, far_x, core, :, lanes], from_plain.at[lax.rem(j, PLAIN_SLOTS), :, :, lanes],
                sends(rs_send, 1, lanes), rs_recv.at[j, 2], device,
            ),
        ]

    def to_near(j, lanes):
        b, m = back_of(j)
        return remote(
            gp.at[b, m, :, near_y, near_x, core, :, lanes], from_pair.at[lax.rem(j, PAIR_SLOTS), :, :, lanes],
            sends(rs_send, 2, lanes), rs_recv.at[j, 3], chip(z, near_y, near_x),
        )

    def to_z(j, lanes):
        b, m = back_of(j)
        return [
            remote(
                gp.at[b, m, zi, y, x, core, :, lanes], from_z.at[j, s, :, lanes],
                sends(rs_send, 0, lanes), rs_recv.at[j, 4 + s], chip(zi, y, x),
            )
            for s, zi in enumerate(z_peers)
        ]

    def scatter_start(j):
        by_lanes(back_of(j)[1], lambda lanes: to_core(j, lanes).start())

    def scatter_core(j):
        b, m = back_of(j)

        def step(lanes):
            to_core(j, lanes).wait_recv()
            part = gp[b, m, :, :, :, core, :, lanes] + from_core[lax.rem(j, CORE_SLOTS), :, :, :, :, lanes]
            gp[b, m, :, :, :, core, :, lanes] = part
            start_all(to_far(j, lanes))

        by_lanes(m, step)

    def scatter_diag(j):
        b, m = back_of(j)

        def step(lanes):
            to_far(j, lanes)[0].wait_recv()
            part = gp[b, m, :, near_y, near_x, core, :, lanes] + from_diag[lax.rem(j, DIAG_SLOTS), :, :, lanes]
            gp[b, m, :, near_y, near_x, core, :, lanes] = part
            to_near(j, lanes).start()

        by_lanes(m, step)

    def scatter_plane(j):
        b, m = back_of(j)

        def step(lanes):
            to_far(j, lanes)[1].wait_recv()
            to_near(j, lanes).wait_recv()
            value = gp[b, m, :, y, x, core, :, lanes].astype(F32)
            value = value + from_plain[lax.rem(j, PLAIN_SLOTS), :, :, lanes].astype(F32)
            value = value + from_pair[lax.rem(j, PAIR_SLOTS), :, :, lanes].astype(F32)
            gp[b, m, :, y, x, core, :, lanes] = value.astype(BF)
            start_all(to_z(j, lanes))

        by_lanes(m, step)

    def scatter_z(j):
        b, m = back_of(j)

        def step(lanes):
            for copy in to_z(j, lanes):
                copy.wait_recv()
            value = gp[b, m, z, y, x, core, :, lanes].astype(F32)
            for s in range(ZN - 1):
                value = value + from_z[j, s, :, lanes].astype(F32)
            total[b, m, :, lanes] = value
            squares[:, lanes] = squares[:, lanes] + value * value

        by_lanes(m, step)

    def add_rows(value):
        return jnp.sum(value.reshape(-1, 8, hidden), axis=0)

    def put_bias(k, acc):
        bias_sum[pl.ds(span + k, 1), :] = jnp.sum(acc, axis=0, keepdims=True)

    def feed(b):
        pl.when(b == 1)(lambda: resid.__setitem__(..., jnp.zeros_like(resid)))
        e = (-(resid[...] * mask[...].astype(F32))).astype(BF)
        e_t[b] = e.T
        work[0] = dot_nt(e, small(b, 256)).astype(BF)
        work[2] = dot_nt(f_ref[...], small(b, 128)).astype(BF)

    def feed_forward(b):
        work[2] = dot_nt(f_ref[...], small(b, 128)).astype(BF)

    def put_dz(b, k, da):
        sums = []

        def body(at):
            dz = da(at) * slope[b, k, at, :].astype(F32)
            work[k % 2 if isinstance(k, int) else lax.rem(k, 2), at, :] = dz.astype(BF)
            sums.append(add_rows(dz))

        halves(body)
        bias_sum[pl.ds(span + k, 1), :] = jnp.sum(sums[0] + sums[1], axis=0, keepdims=True)

    def theta_step(b):
        put_dz(
            b, 3, lambda at: 0.5 * (dot_nt(work[0, at, :], matrix(b, 4)) + dot_nt(work[2, at, :], matrix(b, 5)))
        )

    def layer_back(b, k):
        source = lax.rem(k, 2)
        gp[b, k] = grid(dot_nn(act_t[b, k - 1], work[source]))
        put_dz(b, k - 1, lambda at: dot_nt(work[source, at, :], matrix(b, k)))

    def theta_grad(b, m):
        gp[b, m] = grid(dot_nn(act_t[b, 3], work[jnp.where(m == 4, 0, 2)]))

    def first_grads(b):
        gp[b, 0, :, :, :, :, :, 0:128] = grid(dot_nn(in_t[b], work[0]).T)
        gp[b, 0, :, :, :, :, :, 128:256] = grid(bias_sum[...].T)
        pl.when(b == 0)(backcast_grad)

    def backcast_grad():
        gp[0, 0, :, :, :, :, :, 256:384] = grid(dot_nn(e_t[0], theta_keep[...]).T)

    def input_grad(b):
        for t in range(2):
            at = slice(t * windows // 2, (t + 1) * windows // 2)
            keep = mask[at, :].astype(F32)
            dr = resid[at, :] * keep + 2.0 * dot_nn(work[0, at, :], small(b, 0))

            @pl.when(b == 1)
            def _():
                seg[at, :] = dr[:, 0:past]
                resid[at, :] = dr.astype(BF).astype(F32)

            @pl.when(b == 0)
            def _():
                put_rows(sens, 0, at, (dr * keep).T[0:past])

    def late_rows():
        for g in range(windows // 128):
            at = slice(g * 128, (g + 1) * 128)
            pad[:, 0:past] = seg[at, :]
            put_rows(sens, 1, at, pad[...].T[0:past])

    bias_sum[...] = jnp.zeros_like(bias_sum)
    squares[...] = jnp.zeros_like(squares)
    total[...] = jnp.zeros_like(total)

    def back_step(j, carry):
        b, m = back_of(j)

        staged(6, j, scatter_plane)
        staged(4, j, scatter_diag)
        staged(2, j, scatter_core)

        @pl.when(j == 2)
        def _():
            arrived(9)
            arrived(10)
            theta_step(1)
            scatter_core(1)

        pl.when(jnp.logical_and(m >= 1, m <= 3))(lambda: layer_back(b, m))

        @pl.when(jnp.logical_or(j == 6, j == count - 1))
        def _():
            block = jnp.where(j == 6, 1, 0)
            first_grads(block)
            pl.when(j == 6)(lambda: input_grad(1))

        @pl.when(j == 6)
        def _():
            feed(0)
            theta_grad(0, 4)

        @pl.when(jnp.logical_or(j == 10, j == 11))
        def _():
            lax.fori_loop(jnp.where(j == 10, 4, 5), MATS, lambda n, carry: (late_theta(b, n), carry)[1], 0)

        pl.when(jnp.logical_and(j >= 3, j < count))(lambda: scatter_start(j))

        @pl.when(j == 6)
        def _():
            arrived(11)
            theta_step(0)

        @pl.when(j == count)
        def _():
            input_grad(0)
            forecasts()

        @pl.when(j == count + 1)
        def _():
            late_rows()

        @pl.when(j == count + 5)
        def _():
            start_all(out_copies(sens, sens_out, 1) + out_copies(pred, pred_out, 0))

        @pl.when(j >= count + 1)
        def _():
            scatter_z(2 * (j - count - 1))
            scatter_z(2 * (j - count - 1) + 1)

        return carry

    gather_line(0)
    hand_over(0, slice(0, 384)).start()
    small_loads[3].wait()
    for m in range(1, MATS):
        pack(m)
        if m < 4:
            gather_line(m)
        hand_over(m, slice(0, hidden)).start()
    lax.fori_loop(0, count + 4, gather_step, 0)

    lax.fori_loop(2, count + 7, back_step, 0)

    grad_copy = remote(total.at[other], grad_out.at[:, core], out_send.at[2], out_recv.at[2], sibling)
    grad_copy.start()
    grad_out[:, core] = total[core]
    sq = squares[:, 0:128] + squares[:, 128:256] + squares[:, 256:384] + squares[:, 384:512]
    place = (y * XN + x) * 2 + core
    norm_buf[place] = sq[0:8] + sq[8:16]

    def spread(sources, targets, first):
        copies = [
            remote(norm_buf.at[sources], norm_buf.at[sources], norm_send.at[first + s], norm_recv.at[first + s], device)
            for s, device in enumerate(targets)
        ]
        start_all(copies)
        for copy in copies:
            copy.wait()

    def add_up(slots):
        value = norm_buf[slots[0]]
        for slot in slots[1:]:
            value = value + norm_buf[slot]
        return value

    spread(place, plane_peers, 0)
    norm_buf[8 + z] = add_up(range(8))
    spread(8 + z, [chip(zi, y, x) for zi in z_peers], 7)
    everything = add_up(range(8, 8 + ZN))
    norm_out[...] = jnp.broadcast_to(jnp.sqrt(jnp.sum(everything, keepdims=True)), norm_out.shape)

    grad_copy.wait()
    for buf, out, s in ((pred, pred_out, 0), (sens, sens_out, 1)):
        for copy in out_copies(buf, out, s):
            copy.wait()
    for m in range(MATS):
        hand_over(m, slice(0, hidden if m else 384)).wait_send()

    for mats, lanes in ((slice(1, MATS), slice(0, hidden)), (slice(0, 1), slice(0, 384))):
        sent = (
            wg.at[:, mats, 0 : ZN - 1, 0, 0, 0, :, lanes],
            wg.at[:, mats, :, :, 0, 0, :, lanes],
            wg.at[:, mats, :, 0, 0, 0, :, lanes],
            wg.at[:, mats, :, :, :, 0, :, lanes],
        )
        for sems in (ag_send, rs_send):
            for kind, ref in enumerate(sent):
                remote(ref, ref, sends(sems, kind, lanes), out_recv.at[0], sibling).wait_send()


def train_call(plane, segments, extents, adjoint, first, square, head, biases):
    ZN, YN, XN = plane
    past, span, hidden = segments.shape[1], adjoint.shape[0], square.shape[3]
    windows = segments.shape[0] // 2
    tile = windows
    half = hidden // (ZN * YN * XN) // 2
    sizes = (ZN, YN, XN, windows, tile, past, span, hidden)
    DMA = pltpu.SemaphoreType.DMA
    vmem = pl.BlockSpec(memory_space=pltpu.VMEM)
    hbm = pl.BlockSpec(memory_space=pl.ANY)
    count = 2 * MATS
    flops = 2 * 2 * 3 * windows * hidden * (6 * hidden + 2 * 128)
    lengths = extents.reshape(-1, 128)
    return pl.pallas_call(
        functools.partial(train_kernel, sizes),
        out_shape=(
            jax.ShapeDtypeStruct((span, 1, 2 * windows), F32),
            jax.ShapeDtypeStruct((past, 1, 2 * windows), F32),
            jax.ShapeDtypeStruct((MATS, 2, half, hidden), F32),
            jax.ShapeDtypeStruct((8, 128), F32),
        ),
        in_specs=[hbm] * 7,
        out_specs=(hbm, hbm, vmem, vmem),
        scratch_shapes=[
            pltpu.VMEM((2, MATS, ZN, YN, XN, 2, half, hidden), BF),
            pltpu.VMEM((MATS, half, hidden), BF),
            pltpu.VMEM((2, MATS, ZN, YN, XN, 2, half, hidden), BF),
            pltpu.VMEM((CORE_SLOTS, ZN, YN, XN, half, hidden), BF),
            pltpu.VMEM((DIAG_SLOTS, ZN, half, hidden), BF),
            pltpu.VMEM((PLAIN_SLOTS, ZN, half, hidden), BF),
            pltpu.VMEM((PAIR_SLOTS, ZN, half, hidden), BF),
            pltpu.VMEM((count, ZN - 1, half, hidden), BF),
            pltpu.VMEM((2, MATS, half, hidden), F32),
            pltpu.VMEM((2, 4, hidden, windows), BF),
            pltpu.VMEM((2, 128, windows), BF),
            pltpu.VMEM((windows, hidden), BF),
            pltpu.VMEM((2, 4, windows, hidden), BF),
            pltpu.VMEM((3, windows, hidden), BF),
            pltpu.VMEM((windows, 128), F32),
            pltpu.VMEM((windows, 128), BF),
            pltpu.VMEM((windows, 128), BF),
            pltpu.VMEM((2, 128, windows), BF),
            pltpu.VMEM((128, hidden), F32),
            pltpu.VMEM((128, hidden), F32),
            pltpu.VMEM((128, 128), F32),
            pltpu.VMEM((windows, past), F32),
            pltpu.VMEM((span, windows), F32),
            *(pltpu.VMEM(a.shape, a.dtype) for a in (lengths, first, square, head, biases)),
            pltpu.VMEM((2, span, windows), F32),
            pltpu.VMEM((2, span, 1, windows), F32),
            pltpu.VMEM((2, past, 1, windows), F32),
            pltpu.VMEM((half, hidden), F32),
            pltpu.VMEM((8 + ZN, 8, 128), F32),
            DMA((MATS,)),
            DMA((MATS,)),
            DMA((4, 2)),
            DMA((count, 4 + ZN - 1)),
            DMA((4, 2)),
            DMA((count, 4 + ZN - 1)),
            DMA((3,)),
            DMA((3,)),
            DMA((9,)),
            DMA((7 + ZN - 1,)),
            DMA((7 + ZN - 1,)),
        ],
        compiler_params=pltpu.CompilerParams(
            collective_id=0, has_side_effects=True, vmem_limit_bytes=64 * 1024 * 1024
        ),
        cost_estimate=pl.CostEstimate(flops=flops, bytes_accessed=8_000_000, transcendentals=8 * windows * hidden),
        name="train",
    )(segments, adjoint, lengths, first, square, head, biases)


def update_kernel(past, span, *refs):
    sources, targets, norm_out = refs[0:16], refs[16:34], refs[34]
    held, results, pad, in_sem, out_sem = refs[35:51], refs[51:67], *refs[67:70]
    arriving = [pltpu.make_async_copy(source, ref, in_sem.at[n]) for n, (source, ref) in enumerate(zip(sources, held))]
    leaving = [
        pltpu.make_async_copy(ref, target, out_sem.at[n]) for n, (ref, target) in enumerate(zip(held[0:2] + results, targets))
    ]
    for n in (2, 3, 0, 5, 9, 13, 1, 4, 8, 12, 6, 10, 14, 7, 11, 15):
        arriving[n].start()
    grads, norm, masters, momenta, variances = held[2], held[3], held[4:8], held[8:12], held[12:16]
    units = masters[3].shape[2]

    def rows(m, lane, width):
        return grads[m, :, :, lane : lane + width].reshape(units, width)

    arriving[2].wait()
    arriving[3].wait()
    norm_out[...] = norm[0:1, 0:1]
    factor = 1.0 / jnp.maximum(norm[0:1, 0:1], 1.0)
    for m in range(5):
        results[1][0, m] = rows(m + 1, 0, grads.shape[3])
    results[0][0] = rows(0, 0, 128)[:, 0:past]
    forecast = rows(0, 128, 128)
    pad[...] = jnp.zeros_like(pad)
    pad[0:units, :] = forecast
    results[3][0] = pad[...].T[span : span + 4, 0:units]
    results[2][0, :, 0:past] = rows(0, 256, 128)[:, 0:past]
    results[2][0, :, past : past + span] = forecast[:, 0:span]
    for n in (0, 1):
        arriving[n].wait()
        leaving[n].start()
    for n in (1, 0, 2, 3):
        leaving[2 + n].start()
        for state in range(3):
            arriving[4 + 4 * state + n].wait()
        updated = adamw(masters[n][...], results[n][...], momenta[n][...], variances[n][...], factor[None])
        for kind, value in enumerate(updated):
            results[4 * (kind + 1) + n][...] = value
            leaving[2 + 4 * (kind + 1) + n].start()
    for copy in leaving:
        copy.wait()


def update_call(prediction, sensitivity, grads, norm, state):
    hbm = pl.BlockSpec(memory_space=pl.ANY)
    sources = (prediction, sensitivity, grads, norm, *state)
    targets = (prediction, sensitivity, *(4 * list(state[:4])))
    return pl.pallas_call(
        functools.partial(update_kernel, sensitivity.shape[0], prediction.shape[0]),
        out_shape=tuple(jax.ShapeDtypeStruct(a.shape, F32) for a in targets) + (jax.ShapeDtypeStruct((1, 1), F32),),
        in_specs=[hbm] * len(sources),
        out_specs=tuple([hbm] * len(targets) + [pl.BlockSpec(memory_space=pltpu.VMEM)]),
        scratch_shapes=[pltpu.VMEM(a.shape, F32) for a in sources]
        + [pltpu.VMEM(a.shape, F32) for a in targets[2:]]
        + [pltpu.VMEM((128, 128), F32), pltpu.SemaphoreType.DMA((len(sources),)), pltpu.SemaphoreType.DMA((len(targets),))],
        name="update",
    )(*sources)


def turned(arrays):
    return [a.transpose(0, 2, 1) if n % 4 == 0 else a for n, a in enumerate(arrays)]


def kernel_shards(plane, segments, extents, adjoint, *state):
    state = turned(state)
    results = train_call(plane, segments, extents, adjoint.T, *state[:4])
    prediction, sensitivity, *updated, norm = update_call(*results, state)
    by_window = (prediction.transpose(1, 2, 0), sensitivity.transpose(1, 2, 0))
    return (*by_window, norm.reshape(()), *turned(updated))


STATE_SPECS = (
    P("section", None, "dp"),
    P("section", None, "dp", None),
    P("section", "dp", None),
    P("section", None, "dp"),
)


def solution(mesh):
    in_specs = (P("dp", None), P("dp"), P("dp", None)) + 3 * STATE_SPECS
    out_specs = (P("section", "dp", None), P("section", "dp", None), P()) + 4 * STATE_SPECS
    plane = PLANES.get(mesh.shape["dp"])
    shards = plain_shards if plane is None else functools.partial(kernel_shards, plane)
    return jax.shard_map(shards, mesh=mesh, in_specs=in_specs, out_specs=out_specs, check_vma=False)
```

```python
import functools

import jax
import jax.numpy as jnp
from jax import lax
from jax.experimental import pallas as pl
from jax.experimental.pallas import tpu as pltpu
from jax.sharding import PartitionSpec as P

STEP = 10


def dot_nn(a, b):
    return jnp.dot(a, b, preferred_element_type=jnp.float32)


def dot_tn(a, b):
    return lax.dot_general(a, b, (((0,), (0,)), ((), ())), preferred_element_type=jnp.float32)


def dot_nt(a, b):
    return lax.dot_general(a, b, (((1,), (1,)), ((), ())), preferred_element_type=jnp.float32)


def unit_rows(first, square, head, biases):
    units = first.shape[1]
    return jnp.concatenate(
        [square.transpose(1, 0, 2).reshape(units, -1), first.T, head, biases.T], axis=1
    )


def from_unit_rows(rows, past, hidden, out):
    wide = 5 * hidden
    square = rows[:, :wide].reshape(-1, 5, hidden).transpose(1, 0, 2)
    first = rows[:, wide : wide + past].T
    head = rows[:, wide + past : wide + past + out]
    biases = rows[:, wide + past + out :].T
    return first, square, head, biases


def plain_forward(weights, resid):
    first, square, head, biases = weights
    past = resid.shape[1]
    acts, slopes = [resid.astype(jnp.bfloat16)], []
    for k in range(4):
        z = dot_nn(acts[-1], first if k == 0 else square[k - 1]) + biases[k].astype(jnp.float32)
        sig = jax.nn.sigmoid(z)
        acts.append((z * sig).astype(jnp.bfloat16))
        slopes.append(sig * (1.0 + z * (1.0 - sig)))
    theta_b = dot_nn(acts[4], square[3]).astype(jnp.bfloat16)
    theta_f = dot_nn(acts[4], square[4]).astype(jnp.bfloat16)
    backcast = dot_nn(theta_b, head[:, :past])
    part = dot_nn(theta_f, head[:, past:])
    return backcast, part, (acts, slopes, theta_b, theta_f)


def plain_backward(weights, saved, e, f):
    first, square, head, biases = weights
    acts, slopes, theta_b, theta_f = saved
    past = e.shape[1]
    head_grad = jnp.concatenate([dot_tn(theta_b, e), dot_tn(theta_f, f)], axis=1)
    u_b = dot_nt(e, head[:, :past]).astype(jnp.bfloat16)
    u_f = dot_nt(f, head[:, past:]).astype(jnp.bfloat16)
    squares = [None, None, None, dot_tn(acts[4], u_b), dot_tn(acts[4], u_f)]
    da = dot_nt(u_b, square[3]) + dot_nt(u_f, square[4])
    bias_grads = [None] * 4
    first_grad = None
    for k in (3, 2, 1, 0):
        dz = (da * slopes[k]).astype(jnp.bfloat16)
        bias_grads[k] = jnp.sum(dz, axis=0, dtype=jnp.float32)
        grad = dot_tn(acts[k], dz)
        if k == 0:
            first_grad = grad
        else:
            squares[k - 1] = grad
        da = dot_nt(dz, first if k == 0 else square[k - 1])
    return da, (first_grad, jnp.stack(squares), head_grad, jnp.stack(bias_grads))


def adamw(master, gradient, momentum, variance, factor):
    clipped = gradient * factor
    moment_new = 0.9 * momentum + 0.1 * clipped
    variance_new = 0.999 * variance + 0.001 * clipped * clipped
    ratio = moment_new / (1.0 - 0.9**STEP) / (jnp.sqrt(variance_new / (1.0 - 0.999**STEP)) + 1e-08)
    return master - 0.05 * (ratio + 0.01 * master), moment_new, variance_new


def plain_shards(segments, extents, adjoint, *state):
    masters, momenta, variances = state[:4], state[4:8], state[8:]
    core = lax.axis_index("section")
    past, span = segments.shape[1], adjoint.shape[1]
    windows = segments.shape[0] // 2
    hidden = masters[1].shape[3]
    mine = [
        lax.dynamic_slice_in_dim(v, core * windows, windows, 0) for v in (segments, extents, adjoint)
    ]
    seg, ext, adj = mine
    rows = unit_rows(*(m[0].astype(jnp.bfloat16) for m in masters))
    rows = lax.all_gather(rows, "dp", axis=0, tiled=True)
    rows = lax.all_gather(rows, "section", axis=0)
    blocks = [from_unit_rows(rows[b], past, hidden, past + span) for b in range(2)]
    mask = (
        lax.broadcasted_iota(jnp.int32, (windows, past), 1) >= past - ext[:, None]
    ).astype(jnp.float32)
    r0 = seg * mask
    backcast, part0, saved0 = plain_forward(blocks[0], r0)
    r1 = (r0 - backcast) * mask
    _, part1, saved1 = plain_forward(blocks[1], r1)
    forecast = part0.astype(jnp.bfloat16).astype(jnp.float32) + part1
    f = adj.astype(jnp.bfloat16)
    zero = jnp.zeros_like(r0)
    da1, grads1 = plain_backward(blocks[1], saved1, (-(zero * mask)).astype(jnp.bfloat16), f)
    dr1 = zero * mask + da1
    t = dr1.astype(jnp.bfloat16).astype(jnp.float32)
    da0, grads0 = plain_backward(blocks[0], saved0, (-(t * mask)).astype(jnp.bfloat16), f)
    dr0 = (t * mask + da0) * mask

    def by_section(first_block, second_block):
        mine, other = (
            jnp.where(core == 0, first_block, second_block),
            jnp.where(core == 0, second_block, first_block),
        )
        got = lax.ppermute(other, "section", [(0, 1), (1, 0)])
        return jnp.where(
            core == 0, jnp.concatenate([mine, got]), jnp.concatenate([got, mine])
        )[None]

    prediction = by_section(part0, forecast)
    sensitivity = by_section(dr0, dr1)
    packed = jnp.stack([unit_rows(*grads0), unit_rows(*grads1)])
    packed = lax.psum_scatter(packed, "section", scatter_dimension=0, tiled=False)
    packed = lax.psum_scatter(packed, "dp", scatter_dimension=0, tiled=True)
    norm = jnp.sqrt(lax.psum(jnp.sum(packed * packed), ("section", "dp")))
    factor = 1.0 / jnp.maximum(norm, 1.0)
    summed = [g[None] for g in from_unit_rows(packed, past, hidden, past + span)]
    updated = [adamw(*four, factor) for four in zip(masters, summed, momenta, variances)]
    return (
        prediction,
        sensitivity,
        norm,
        *summed,
        *(u[0] for u in updated),
        *(u[1] for u in updated),
        *(u[2] for u in updated),
    )


PLANES = {16: (4, 2, 2)}
MESH = pl.DeviceIdType.MESH
MATS = 6
CORE_SLOTS, DIAG_SLOTS, PLAIN_SLOTS, PAIR_SLOTS = 4, 4, 6, 4
BF, F32 = jnp.bfloat16, jnp.float32


ORDER = ((0, 5), (1, 4), (1, 5), (1, 3), (1, 2), (1, 1), (0, 4), (0, 3), (0, 2), (0, 1), (1, 0), (0, 0))


def remote(src, dst, send_sem, recv_sem, device):
    return pltpu.make_async_remote_copy(
        src_ref=src, dst_ref=dst, send_sem=send_sem, recv_sem=recv_sem, device_id=device, device_id_type=MESH
    )


def train_kernel(
    sizes,
    seg_hbm, adj_hbm, ext_hbm, first_hbm, square_hbm, head_hbm, biases_hbm,
    pred_out, sens_out, grad_out, norm_out,
    wg, handed, gp, from_core, from_diag, from_plain, from_pair, from_z, total,
    act_t, in_t, theta_keep, slope, work, resid, mask, f_ref, e_t, bias_t, bias_sum, pad,
    seg, adj, ext, first, square, head, biases, part_t, pred, sens, squares, norm_buf,
    own_send, own_recv, ag_send, ag_recv, rs_send, rs_recv, out_send, out_recv, local_sem, norm_send, norm_recv,
):
    ZN, YN, XN, windows, tile, past, span, hidden = sizes
    units = ZN * YN * XN
    core, dp = lax.axis_index("section"), lax.axis_index("dp")
    x, y, z = lax.rem(dp, XN), lax.rem(lax.div(dp, XN), YN), lax.div(dp, XN * YN)
    other, xo, yo = 1 - core, 1 - x, 1 - y
    near_y, near_x = y + core * (yo - y), xo + core * (x - xo)
    far_y, far_x = yo + core * (y - yo), x + core * (xo - x)

    def chip(zi, yi, xi):
        return (core, (zi * YN + yi) * XN + xi)

    sibling = (other, dp)
    z_peers = [lax.rem(z + step, ZN) for step in range(1, ZN)]

    row0 = core * windows
    loads = [
        pltpu.make_async_copy(seg_hbm.at[pl.ds(row0, windows), :], seg, local_sem.at[0]),
        pltpu.make_async_copy(adj_hbm.at[:, pl.ds(row0, windows)], adj, local_sem.at[1]),
    ]
    small_loads = [
        pltpu.make_async_copy(source, target, local_sem.at[4 + n])
        for n, (source, target) in enumerate(
            [(first_hbm, first), (head_hbm, head), (biases_hbm, biases), (square_hbm, square), (ext_hbm, ext)]
        )
    ]
    for load in small_loads:
        load.start()

    barrier = pltpu.get_barrier_semaphore()
    plane_peers = [
        (ci, (z * YN + yi) * XN + xi) for ci in (core, other) for yi in (y, yo) for xi in (x, xo)
    ][1:]
    peers = plane_peers + [(ci, (zi * YN + y) * XN + x) for zi in z_peers for ci in (core, other)]
    for peer in peers:
        pl.semaphore_signal(barrier, inc=1, device_id=peer, device_id_type=MESH)

    rows = hidden // units
    half_rows = rows // 2

    def put_own(m, value, lanes):
        halves = value.astype(BF).reshape(2, half_rows, -1)
        for h in range(2):
            pl.when(core == h)(functools.partial(put_half, m, halves[h], halves[1 - h], lanes))

    def put_half(m, kept, given, lanes):
        wg[core, m, z, y, x, core, :, lanes] = kept
        handed[m, :, lanes] = given

    for load in small_loads[:3]:
        load.wait()
    pad[...] = jnp.zeros_like(pad)
    pad[0:rows, 0:past] = first[0] * 0.5
    put_own(0, pad[0:rows, :], slice(0, 128))
    pad[...] = jnp.zeros_like(pad)
    pad[span : span + 4, 0:rows] = biases[0] * 0.5
    bias_cols = pad[...].T[0:rows]
    pad[...] = jnp.zeros_like(pad)
    pad[0:rows, 0:span] = head[0, :, past : past + span]
    put_own(0, pad[0:rows, :] + bias_cols, slice(128, 256))
    pad[...] = jnp.zeros_like(pad)
    pad[0:rows, 0:past] = head[0, :, 0:past]
    put_own(0, pad[0:rows, :], slice(256, 384))
    pl.semaphore_wait(barrier, len(peers))

    def hand_over(m, lanes):
        return remote(
            handed.at[m, :, lanes], wg.at[core, m, z, y, x, other, :, lanes], own_send.at[m], own_recv.at[m], sibling
        )

    def pack(m):
        put_own(m, square[0, m - 1] * 0.5 if m < 4 else square[0, m - 1], slice(0, hidden))


    def of(i):
        b = jnp.where(jnp.logical_and(i >= 5, i <= 10), 1, 0)
        return b, jnp.where(i <= 4, i, jnp.where(i <= 10, i - 5, 5))

    def sends(sems, kind, lanes):
        return sems.at[kind, 0 if lanes.stop == hidden else 1]

    def z_copies(i, lanes):
        b, m = of(i)
        part = wg.at[b, m, z, y, x, core, :, lanes]
        return [
            remote(part, part, sends(ag_send, 0, lanes), ag_recv.at[i, s], chip(zi, y, x)) for s, zi in enumerate(z_peers)
        ]

    def line_copies(i, lanes):
        b, m = of(i)
        given = wg.at[b, m, z, y, x, other, :, lanes]
        return [
            remote(
                handed.at[m, :, lanes], given, sends(ag_send, 0, lanes), ag_recv.at[i, s], (other, (zi * YN + y) * XN + x)
            )
            for s, zi in enumerate(z_peers)
        ]

    def column_copies(i, lanes):
        b, m = of(i)
        part = wg.at[b, m, :, y, x, core, :, lanes]
        return [
            remote(part, part, sends(ag_send, 1, lanes), ag_recv.at[i, 3], chip(z, near_y, near_x)),
            remote(part, part, sends(ag_send, 1, lanes), ag_recv.at[i, 4], chip(z, far_y, far_x)),
        ]

    def corner_copy(i, lanes):
        b, m = of(i)
        part = wg.at[b, m, :, near_y, near_x, core, :, lanes]
        return remote(part, part, sends(ag_send, 2, lanes), ag_recv.at[i, 5], chip(z, far_y, far_x))

    def core_copy(i, lanes):
        b, m = of(i)
        part = wg.at[b, m, :, :, :, core, :, lanes]
        return remote(part, part, sends(ag_send, 3, lanes), ag_recv.at[i, 6], sibling)

    def by_lanes(m, step):
        if isinstance(m, int):
            step(slice(0, hidden if m else 384))
            return
        pl.when(m == 0)(lambda: step(slice(0, 384)))
        pl.when(m > 0)(lambda: step(slice(0, hidden)))

    def start_all(copies):
        for copy in copies:
            copy.start()

    zeros_tile = jnp.zeros((tile, 128), F32)

    def prepare(t, carry):
        at = pl.ds(t * tile, tile)
        resid[at, :] = zeros_tile
        resid[at, 0:past] = seg[at, :]
        return carry

    def prepare_mask(g, carry):
        lengths = ext[pl.ds(core * (windows // 128) + g, 1), :]
        position = lax.broadcasted_iota(jnp.int32, (128, 128), 0)
        keep = jnp.where(position >= past - lengths, 1.0, 0.0).astype(F32).T
        at = pl.ds(pl.multiple_of(g * 128, 128), 128)
        pad[0:span, :] = adj[:, at]
        f_ref[at, :] = pad[...].T.astype(BF)
        mask[at, :] = keep.astype(BF)
        resid[at, :] = resid[at, :] * keep
        return carry

    tiles = windows // tile
    part_tile = windows // 2

    def matrix(b, m):
        return wg[b, m].reshape(hidden, hidden)

    def small(b, lane):
        return wg[b, 0, :, :, :, :, :, lane : lane + 128].reshape(hidden, 128)

    def store_layer(b, k, at, v):
        p = 1.0 + jnp.tanh(v)
        a = v * p
        rate = p + a * (2.0 - p)
        slope[b, k, at, :] = rate.astype(BF)
        low = a.astype(BF)
        act_t[b, k, :, at] = low.T
        return low

    def halves(body):
        for t in range(2):
            body(slice(t * windows // 2, (t + 1) * windows // 2))

    def layer_zero(b):
        bias_t[...] = small(b, 128).astype(F32).T

        def body(at):
            a = resid[at, :].astype(BF)
            in_t[b, :, at] = a.T
            work[0, at, :] = store_layer(b, 0, at, dot_nt(a, small(b, 0)) + bias_t[span : span + 1, :])

        halves(body)

    def layer_next(b, k):
        source, target = lax.rem(k + 1, 2), lax.rem(k, 2)

        def body(at):
            v = dot_nn(work[source, at, :], matrix(b, k)) + bias_t[pl.ds(span + k, 1), :]
            work[target, at, :] = store_layer(b, k, at, v)

        halves(body)

    def grid(value):
        return value.astype(BF).reshape(ZN, YN, XN, 2, half_rows, -1)

    def backcast_step():
        def body(at):
            theta = dot_nn(work[1, at, :], matrix(0, 4)).astype(BF)
            theta_keep[at, :] = theta
            resid[at, :] = (resid[at, :] - dot_nn(theta, small(0, 256))) * mask[at, :].astype(F32)

        halves(body)

    def put_rows(buf, b, at, value):
        for row in range(value.shape[0]):
            buf[b, row, :, at] = value[row : row + 1]

    def late_theta(b, m):
        theta_t = act_t.at[1, 0]
        theta_t[...] = dot_nn(matrix(b, m).T, act_t[b, 3]).astype(BF)

        @pl.when(m == 4)
        def _():
            gp[b, 0, :, :, :, :, :, 256:384] = grid(dot_nt(theta_t[...], e_t[b]))

        @pl.when(m == 5)
        def _():
            grad = grid(dot_nn(theta_t[...], f_ref[...]))
            gp[b, 0, :, :, :, :, :, 128:256] = gp[b, 0, :, :, :, :, :, 128:256] + grad
            part_t[b] = dot_nn(small(b, 128).T, theta_t[...])[0:span]

    def forecasts():
        put_rows(pred, 0, slice(0, windows), part_t[0])
        put_rows(pred, 1, slice(0, windows), part_t[0].astype(BF).astype(F32) + part_t[1])

    count = 2 * MATS

    def delayed(lag, t, step):
        pl.when(jnp.logical_and(t >= lag, t < count + lag))(lambda: step(t - lag))

    def staged(lag, t, step):
        early = t - lag + 1
        pl.when(jnp.logical_and(early >= (2 if lag == 2 else 1), early <= 2))(lambda: step(early))
        unit = t - lag
        pl.when(jnp.logical_and(unit >= 3, unit < count))(lambda: step(unit))
        if lag == 6:
            pl.when(t == 4)(lambda: step(0))

    def gather_line(i):
        b, m = of(i)

        pl.when(b == core)(lambda: by_lanes(m, lambda lanes: start_all(line_copies(i, lanes) + z_copies(i, lanes))))

    def gather_columns(i):
        b, m = of(i)

        def step(lanes):
            pl.when(b != core)(lambda: hand_over(m, lanes).wait_recv())
            for copy in z_copies(i, lanes):
                copy.wait_recv()
            start_all(column_copies(i, lanes))

        by_lanes(m, step)

    def gather_corner(i):
        def step(lanes):
            column_copies(i, lanes)[0].wait_recv()
            corner_copy(i, lanes).start()

        by_lanes(of(i)[1], step)

    def gather_core(i):
        def step(lanes):
            column_copies(i, lanes)[1].wait_recv()
            corner_copy(i, lanes).wait_recv()
            core_copy(i, lanes).start()

        by_lanes(of(i)[1], step)

    def arrived(i):
        by_lanes(of(i)[1], lambda lanes: core_copy(i, lanes).wait_recv())

    def forward_unit(i):
        arrived(i)
        b, m = of(i)
        pl.when(m == 0)(lambda: layer_zero(b))
        pl.when(jnp.logical_and(m >= 1, m <= 3))(lambda: layer_next(b, m))
        pl.when(m == 4)(backcast_step)

        @pl.when(jnp.logical_or(i == 4, i == 8))
        def _():
            pl.when(b == 1)(lambda: feed(b))
            pl.when(b == 0)(lambda: feed_forward(b))
            def one(n, carry):
                pl.when(jnp.logical_and(b == 1, n == 5))(lambda: gather_core(10))
                theta_grad(b, n)
                scatter_start(jnp.where(b == 0, 0, n - 3))
                return carry

            lax.fori_loop(jnp.where(b == 1, 4, 5), MATS, one, 0)

    def gather_step(t, carry):
        pl.when(t == 12)(lambda: scatter_core(0))
        pl.when(t == 15)(lambda: scatter_diag(0))
        pl.when(jnp.logical_and(t >= 4, t != 14))(lambda: gather_core(t - 4))
        delayed(2, t, gather_corner)
        delayed(0, t, gather_columns)
        pl.when(t + 4 < count)(lambda: gather_line(t + 4))

        pl.when(t == 0)(lambda: start_all(loads))

        @pl.when(t == 2)
        def _():
            for load in loads + small_loads[4:]:
                load.wait()
            lax.fori_loop(0, tiles, prepare, 0)
            pad[...] = jnp.zeros_like(pad)
            lax.fori_loop(0, windows // 128, prepare_mask, 0)

        pl.when(jnp.logical_and(t >= 5, t < 14))(lambda: forward_unit(t - 5))
        return carry

    def out_copies(buf, out, s):
        at = pl.ds(row0, windows)
        return [
            pltpu.make_async_copy(buf.at[core], out.at[:, :, at], local_sem.at[2 + s]),
            remote(buf.at[other], out.at[:, :, at], out_send.at[s], out_recv.at[s], sibling),
        ]


    def back_of(j):
        if isinstance(j, int):
            return ORDER[j]
        b = jnp.where(jnp.logical_or(jnp.logical_and(j >= 1, j <= 5), j == 10), 1, 0)
        early = jnp.where(j == 1, 4, jnp.where(j <= 2, 5, 6 - j))
        return b, jnp.where(j <= 5, early, jnp.where(j == 6, 4, jnp.where(j <= 9, 10 - j, 0)))

    def to_core(j, lanes):
        b, m = back_of(j)
        return remote(
            gp.at[b, m, :, :, :, other, :, lanes], from_core.at[lax.rem(j, CORE_SLOTS), :, :, :, :, lanes],
            sends(rs_send, 3, lanes), rs_recv.at[j, 0], sibling,
        )

    def to_far(j, lanes):
        b, m = back_of(j)
        device = chip(z, far_y, far_x)
        return [
            remote(
                gp.at[b, m, :, yo, xo, core, :, lanes], from_diag.at[lax.rem(j, DIAG_SLOTS), :, :, lanes],
                sends(rs_send, 1, lanes), rs_recv.at[j, 1], device,
            ),
            remote(
                gp.at[b, m, :, far_y, far_x, core, :, lanes], from_plain.at[lax.rem(j, PLAIN_SLOTS), :, :, lanes],
                sends(rs_send, 1, lanes), rs_recv.at[j, 2], device,
            ),
        ]

    def to_near(j, lanes):
        b, m = back_of(j)
        return remote(
            gp.at[b, m, :, near_y, near_x, core, :, lanes], from_pair.at[lax.rem(j, PAIR_SLOTS), :, :, lanes],
            sends(rs_send, 2, lanes), rs_recv.at[j, 3], chip(z, near_y, near_x),
        )

    def to_z(j, lanes):
        b, m = back_of(j)
        return [
            remote(
                gp.at[b, m, zi, y, x, core, :, lanes], from_z.at[j, s, :, lanes],
                sends(rs_send, 0, lanes), rs_recv.at[j, 4 + s], chip(zi, y, x),
            )
            for s, zi in enumerate(z_peers)
        ]

    def scatter_start(j):
        by_lanes(back_of(j)[1], lambda lanes: to_core(j, lanes).start())

    def scatter_core(j):
        b, m = back_of(j)

        def step(lanes):
            to_core(j, lanes).wait_recv()
            part = gp[b, m, :, :, :, core, :, lanes] + from_core[lax.rem(j, CORE_SLOTS), :, :, :, :, lanes]
            gp[b, m, :, :, :, core, :, lanes] = part
            start_all(to_far(j, lanes))

        by_lanes(m, step)

    def scatter_diag(j):
        b, m = back_of(j)

        def step(lanes):
            to_far(j, lanes)[0].wait_recv()
            part = gp[b, m, :, near_y, near_x, core, :, lanes] + from_diag[lax.rem(j, DIAG_SLOTS), :, :, lanes]
            gp[b, m, :, near_y, near_x, core, :, lanes] = part
            to_near(j, lanes).start()

        by_lanes(m, step)

    def scatter_plane(j):
        b, m = back_of(j)

        def step(lanes):
            to_far(j, lanes)[1].wait_recv()
            to_near(j, lanes).wait_recv()
            value = gp[b, m, :, y, x, core, :, lanes].astype(F32)
            value = value + from_plain[lax.rem(j, PLAIN_SLOTS), :, :, lanes].astype(F32)
            value = value + from_pair[lax.rem(j, PAIR_SLOTS), :, :, lanes].astype(F32)
            gp[b, m, :, y, x, core, :, lanes] = value.astype(BF)
            start_all(to_z(j, lanes))

        by_lanes(m, step)

    def scatter_z(j):
        b, m = back_of(j)

        def step(lanes):
            for copy in to_z(j, lanes):
                copy.wait_recv()
            value = gp[b, m, z, y, x, core, :, lanes].astype(F32)
            for s in range(ZN - 1):
                value = value + from_z[j, s, :, lanes].astype(F32)
            total[b, m, :, lanes] = value
            squares[:, lanes] = squares[:, lanes] + value * value

        by_lanes(m, step)

    def add_rows(value):
        return jnp.sum(value.reshape(-1, 8, hidden), axis=0)

    def put_bias(k, acc):
        bias_sum[pl.ds(span + k, 1), :] = jnp.sum(acc, axis=0, keepdims=True)

    def feed(b):
        pl.when(b == 1)(lambda: resid.__setitem__(..., jnp.zeros_like(resid)))
        e = (-(resid[...] * mask[...].astype(F32))).astype(BF)
        e_t[b] = e.T
        work[0] = dot_nt(e, small(b, 256)).astype(BF)
        work[2] = dot_nt(f_ref[...], small(b, 128)).astype(BF)

    def feed_forward(b):
        work[2] = dot_nt(f_ref[...], small(b, 128)).astype(BF)

    def put_dz(b, k, da):
        sums = []

        def body(at):
            dz = da(at) * slope[b, k, at, :].astype(F32)
            work[k % 2 if isinstance(k, int) else lax.rem(k, 2), at, :] = dz.astype(BF)
            sums.append(add_rows(dz))

        halves(body)
        bias_sum[pl.ds(span + k, 1), :] = jnp.sum(sums[0] + sums[1], axis=0, keepdims=True)

    def theta_step(b):
        put_dz(
            b, 3, lambda at: 0.5 * (dot_nt(work[0, at, :], matrix(b, 4)) + dot_nt(work[2, at, :], matrix(b, 5)))
        )

    def layer_back(b, k):
        source = lax.rem(k, 2)
        weight_grad(b, k, k - 1, source)
        put_dz(b, k - 1, lambda at: dot_nt(work[source, at, :], matrix(b, k)))

    def weight_grad(b, m, layer, slot):
        for n in range(0, hidden, 256):
            part = slice(n, n + 256)
            gp[b, m, :, :, :, :, :, part] = grid(dot_nn(act_t[b, layer], work[slot, :, part]))

    def theta_grad(b, m):
        weight_grad(b, m, 3, jnp.where(m == 4, 0, 2))

    def first_grads(b):
        gp[b, 0, :, :, :, :, :, 0:128] = grid(dot_nn(in_t[b], work[0]).T)
        gp[b, 0, :, :, :, :, :, 128:256] = grid(bias_sum[...].T)
        pl.when(b == 0)(backcast_grad)

    def backcast_grad():
        gp[0, 0, :, :, :, :, :, 256:384] = grid(dot_nn(e_t[0], theta_keep[...]).T)

    def input_grad(b):
        for t in range(2):
            at = slice(t * windows // 2, (t + 1) * windows // 2)
            keep = mask[at, :].astype(F32)
            dr = resid[at, :] * keep + 2.0 * dot_nn(work[0, at, :], small(b, 0))

            @pl.when(b == 1)
            def _():
                seg[at, :] = dr[:, 0:past]
                resid[at, :] = dr.astype(BF).astype(F32)

            @pl.when(b == 0)
            def _():
                put_rows(sens, 0, at, (dr * keep).T[0:past])

    def late_rows():
        for g in range(windows // 128):
            at = slice(g * 128, (g + 1) * 128)
            pad[:, 0:past] = seg[at, :]
            put_rows(sens, 1, at, pad[...].T[0:past])

    bias_sum[...] = jnp.zeros_like(bias_sum)
    squares[...] = jnp.zeros_like(squares)
    total[...] = jnp.zeros_like(total)

    def back_step(j, carry):
        b, m = back_of(j)

        staged(6, j, scatter_plane)
        staged(4, j, scatter_diag)
        staged(2, j, scatter_core)

        @pl.when(j == 2)
        def _():
            arrived(9)
            arrived(10)
            theta_step(1)
            scatter_core(1)

        pl.when(jnp.logical_and(m >= 1, m <= 3))(lambda: layer_back(b, m))

        @pl.when(jnp.logical_or(j == 6, j == count - 1))
        def _():
            block = jnp.where(j == 6, 1, 0)
            first_grads(block)
            pl.when(j == 6)(lambda: input_grad(1))

        @pl.when(j == 6)
        def _():
            feed(0)
            theta_grad(0, 4)

        @pl.when(jnp.logical_or(j == 10, j == 11))
        def _():
            lax.fori_loop(jnp.where(j == 10, 4, 5), MATS, lambda n, carry: (late_theta(b, n), carry)[1], 0)

        pl.when(jnp.logical_and(j >= 3, j < count))(lambda: scatter_start(j))

        @pl.when(j == 6)
        def _():
            arrived(11)
            theta_step(0)

        @pl.when(j == count)
        def _():
            input_grad(0)
            forecasts()

        @pl.when(j == count + 1)
        def _():
            late_rows()

        @pl.when(j == count + 5)
        def _():
            start_all(out_copies(sens, sens_out, 1) + out_copies(pred, pred_out, 0))

        @pl.when(j >= count + 1)
        def _():
            scatter_z(2 * (j - count - 1))
            scatter_z(2 * (j - count - 1) + 1)

        return carry

    gather_line(0)
    hand_over(0, slice(0, 384)).start()
    small_loads[3].wait()
    for m in range(1, MATS):
        pack(m)
        if m < 4:
            gather_line(m)
        hand_over(m, slice(0, hidden)).start()
    lax.fori_loop(0, count + 4, gather_step, 0)

    lax.fori_loop(2, count + 7, back_step, 0)

    grad_copy = remote(total.at[other], grad_out.at[:, core], out_send.at[2], out_recv.at[2], sibling)
    grad_copy.start()
    grad_out[:, core] = total[core]
    sq = squares[:, 0:128] + squares[:, 128:256] + squares[:, 256:384] + squares[:, 384:512]
    place = (y * XN + x) * 2 + core
    norm_buf[place] = sq[0:8] + sq[8:16]

    def spread(sources, targets, first):
        copies = [
            remote(norm_buf.at[sources], norm_buf.at[sources], norm_send.at[first + s], norm_recv.at[first + s], device)
            for s, device in enumerate(targets)
        ]
        start_all(copies)
        for copy in copies:
            copy.wait()

    def add_up(slots):
        value = norm_buf[slots[0]]
        for slot in slots[1:]:
            value = value + norm_buf[slot]
        return value

    spread(place, plane_peers, 0)
    norm_buf[8 + z] = add_up(range(8))
    spread(8 + z, [chip(zi, y, x) for zi in z_peers], 7)
    everything = add_up(range(8, 8 + ZN))
    norm_out[...] = jnp.broadcast_to(jnp.sqrt(jnp.sum(everything, keepdims=True)), norm_out.shape)

    grad_copy.wait()
    for buf, out, s in ((pred, pred_out, 0), (sens, sens_out, 1)):
        for copy in out_copies(buf, out, s):
            copy.wait()
    for m in range(MATS):
        hand_over(m, slice(0, hidden if m else 384)).wait_send()

    for mats, lanes in ((slice(1, MATS), slice(0, hidden)), (slice(0, 1), slice(0, 384))):
        sent = (
            wg.at[:, mats, 0 : ZN - 1, 0, 0, 0, :, lanes],
            wg.at[:, mats, :, :, 0, 0, :, lanes],
            wg.at[:, mats, :, 0, 0, 0, :, lanes],
            wg.at[:, mats, :, :, :, 0, :, lanes],
        )
        for sems in (ag_send, rs_send):
            for kind, ref in enumerate(sent):
                remote(ref, ref, sends(sems, kind, lanes), out_recv.at[0], sibling).wait_send()


def train_call(plane, segments, extents, adjoint, first, square, head, biases):
    ZN, YN, XN = plane
    past, span, hidden = segments.shape[1], adjoint.shape[0], square.shape[3]
    windows = segments.shape[0] // 2
    tile = windows
    half = hidden // (ZN * YN * XN) // 2
    sizes = (ZN, YN, XN, windows, tile, past, span, hidden)
    DMA = pltpu.SemaphoreType.DMA
    vmem = pl.BlockSpec(memory_space=pltpu.VMEM)
    hbm = pl.BlockSpec(memory_space=pl.ANY)
    count = 2 * MATS
    flops = 2 * 2 * 3 * windows * hidden * (6 * hidden + 2 * 128)
    lengths = extents.reshape(-1, 128)
    return pl.pallas_call(
        functools.partial(train_kernel, sizes),
        out_shape=(
            jax.ShapeDtypeStruct((span, 1, 2 * windows), F32),
            jax.ShapeDtypeStruct((past, 1, 2 * windows), F32),
            jax.ShapeDtypeStruct((MATS, 2, half, hidden), F32),
            jax.ShapeDtypeStruct((8, 128), F32),
        ),
        in_specs=[hbm] * 7,
        out_specs=(hbm, hbm, vmem, vmem),
        scratch_shapes=[
            pltpu.VMEM((2, MATS, ZN, YN, XN, 2, half, hidden), BF),
            pltpu.VMEM((MATS, half, hidden), BF),
            pltpu.VMEM((2, MATS, ZN, YN, XN, 2, half, hidden), BF),
            pltpu.VMEM((CORE_SLOTS, ZN, YN, XN, half, hidden), BF),
            pltpu.VMEM((DIAG_SLOTS, ZN, half, hidden), BF),
            pltpu.VMEM((PLAIN_SLOTS, ZN, half, hidden), BF),
            pltpu.VMEM((PAIR_SLOTS, ZN, half, hidden), BF),
            pltpu.VMEM((count, ZN - 1, half, hidden), BF),
            pltpu.VMEM((2, MATS, half, hidden), F32),
            pltpu.VMEM((2, 4, hidden, windows), BF),
            pltpu.VMEM((2, 128, windows), BF),
            pltpu.VMEM((windows, hidden), BF),
            pltpu.VMEM((2, 4, windows, hidden), BF),
            pltpu.VMEM((3, windows, hidden), BF),
            pltpu.VMEM((windows, 128), F32),
            pltpu.VMEM((windows, 128), BF),
            pltpu.VMEM((windows, 128), BF),
            pltpu.VMEM((2, 128, windows), BF),
            pltpu.VMEM((128, hidden), F32),
            pltpu.VMEM((128, hidden), F32),
            pltpu.VMEM((128, 128), F32),
            pltpu.VMEM((windows, past), F32),
            pltpu.VMEM((span, windows), F32),
            *(pltpu.VMEM(a.shape, a.dtype) for a in (lengths, first, square, head, biases)),
            pltpu.VMEM((2, span, windows), F32),
            pltpu.VMEM((2, span, 1, windows), F32),
            pltpu.VMEM((2, past, 1, windows), F32),
            pltpu.VMEM((half, hidden), F32),
            pltpu.VMEM((8 + ZN, 8, 128), F32),
            DMA((MATS,)),
            DMA((MATS,)),
            DMA((4, 2)),
            DMA((count, 4 + ZN - 1)),
            DMA((4, 2)),
            DMA((count, 4 + ZN - 1)),
            DMA((3,)),
            DMA((3,)),
            DMA((9,)),
            DMA((7 + ZN - 1,)),
            DMA((7 + ZN - 1,)),
        ],
        compiler_params=pltpu.CompilerParams(
            collective_id=0, has_side_effects=True, vmem_limit_bytes=64 * 1024 * 1024
        ),
        cost_estimate=pl.CostEstimate(flops=flops, bytes_accessed=8_000_000, transcendentals=8 * windows * hidden),
        name="train",
    )(segments, adjoint, lengths, first, square, head, biases)


def update_kernel(past, span, *refs):
    sources, targets, norm_out = refs[0:16], refs[16:34], refs[34]
    held, results, pad, in_sem, out_sem = refs[35:51], refs[51:67], *refs[67:70]
    arriving = [pltpu.make_async_copy(source, ref, in_sem.at[n]) for n, (source, ref) in enumerate(zip(sources, held))]
    leaving = [
        pltpu.make_async_copy(ref, target, out_sem.at[n]) for n, (ref, target) in enumerate(zip(held[0:2] + results, targets))
    ]
    for n in (2, 3, 0, 5, 9, 13, 1, 4, 8, 12, 6, 10, 14, 7, 11, 15):
        arriving[n].start()
    grads, norm, masters, momenta, variances = held[2], held[3], held[4:8], held[8:12], held[12:16]
    units = masters[3].shape[2]

    def rows(m, lane, width):
        return grads[m, :, :, lane : lane + width].reshape(units, width)

    arriving[2].wait()
    arriving[3].wait()
    norm_out[...] = norm[0:1, 0:1]
    factor = 1.0 / jnp.maximum(norm[0:1, 0:1], 1.0)
    for m in range(5):
        results[1][0, m] = rows(m + 1, 0, grads.shape[3])
    results[0][0] = rows(0, 0, 128)[:, 0:past]
    forecast = rows(0, 128, 128)
    pad[...] = jnp.zeros_like(pad)
    pad[0:units, :] = forecast
    results[3][0] = pad[...].T[span : span + 4, 0:units]
    results[2][0, :, 0:past] = rows(0, 256, 128)[:, 0:past]
    results[2][0, :, past : past + span] = forecast[:, 0:span]
    for n in (0, 1):
        arriving[n].wait()
        leaving[n].start()
    for n in (1, 0, 2, 3):
        leaving[2 + n].start()
        for state in range(3):
            arriving[4 + 4 * state + n].wait()
        updated = adamw(masters[n][...], results[n][...], momenta[n][...], variances[n][...], factor[None])
        for kind, value in enumerate(updated):
            results[4 * (kind + 1) + n][...] = value
            leaving[2 + 4 * (kind + 1) + n].start()
    for copy in leaving:
        copy.wait()


def update_call(prediction, sensitivity, grads, norm, state):
    hbm = pl.BlockSpec(memory_space=pl.ANY)
    sources = (prediction, sensitivity, grads, norm, *state)
    targets = (prediction, sensitivity, *(4 * list(state[:4])))
    return pl.pallas_call(
        functools.partial(update_kernel, sensitivity.shape[0], prediction.shape[0]),
        out_shape=tuple(jax.ShapeDtypeStruct(a.shape, F32) for a in targets) + (jax.ShapeDtypeStruct((1, 1), F32),),
        in_specs=[hbm] * len(sources),
        out_specs=tuple([hbm] * len(targets) + [pl.BlockSpec(memory_space=pltpu.VMEM)]),
        scratch_shapes=[pltpu.VMEM(a.shape, F32) for a in sources]
        + [pltpu.VMEM(a.shape, F32) for a in targets[2:]]
        + [pltpu.VMEM((128, 128), F32), pltpu.SemaphoreType.DMA((len(sources),)), pltpu.SemaphoreType.DMA((len(targets),))],
        name="update",
    )(*sources)


def turned(arrays):
    return [a.transpose(0, 2, 1) if n % 4 == 0 else a for n, a in enumerate(arrays)]


def kernel_shards(plane, segments, extents, adjoint, *state):
    state = turned(state)
    results = train_call(plane, segments, extents, adjoint.T, *state[:4])
    prediction, sensitivity, *updated, norm = update_call(*results, state)
    by_window = (prediction.transpose(1, 2, 0), sensitivity.transpose(1, 2, 0))
    return (*by_window, norm.reshape(()), *turned(updated))


STATE_SPECS = (
    P("section", None, "dp"),
    P("section", None, "dp", None),
    P("section", "dp", None),
    P("section", None, "dp"),
)


def solution(mesh):
    in_specs = (P("dp", None), P("dp"), P("dp", None)) + 3 * STATE_SPECS
    out_specs = (P("section", "dp", None), P("section", "dp", None), P()) + 4 * STATE_SPECS
    plane = PLANES.get(mesh.shape["dp"])
    shards = plain_shards if plane is None else functools.partial(kernel_shards, plane)
    return jax.shard_map(shards, mesh=mesh, in_specs=in_specs, out_specs=out_specs, check_vma=False)
```
